32 devices in a mesh: grp: 4 (over y, x), dp: 2 (over core), tp: 4 (over z).
Axes of the slice: x: 2, y: 2, z: 4, core: 2. Of those that a mesh axis runs over, the one named last changes fastest.
Arguments:
- inputs: bfloat16 [16384, 640], P(('grp', 'dp', 'tp')), may hold values from -6 to 6
- memory: bfloat16 [3, 16384, 640], P(None, ('grp', 'dp', 'tp')), may hold values from -6 to 6
- out_grad: bfloat16 [16384, 640], P(('grp', 'dp', 'tp')), may hold values from -6 to 6
- lengths: int32 [64], P(('grp', 'dp')), may hold values from 33 to 256
- src_lengths: int32 [64], P(('grp', 'dp')), may hold values from 33 to 256
- configs: int32 [4, 4], P('grp'), may hold values from 1 to 3072, as said below
- norm_gain: float32 [3, 640], replicated, may hold values from 0.5 to 1.5
- norm_bias: float32 [3, 640], replicated, may hold values from -3 to 3
- self_qkv: bfloat16 [640, 3, 640], P(None, None, 'tp'), may hold values from -0.25 to 0.25
- self_out: bfloat16 [640, 640], P('tp'), may hold values from -1 to 1
- cross_q: bfloat16 [640, 640], P(None, 'tp'), may hold values from -0.25 to 0.25
- cross_kv: bfloat16 [640, 2, 640], P(None, None, 'tp'), may hold values from -0.25 to 0.25
- cross_out: bfloat16 [640, 640], P('tp'), may hold values from -1 to 1
- ffn_in: bfloat16 [640, 3072], P(None, 'tp'), may hold values from -0.25 to 0.25
- ffn_in_bias: float32 [3072], P('tp'), may hold values from -3 to 3
- ffn_out: bfloat16 [3072, 640], P('tp'), may hold values from -0.21875 to 0.21875
- ffn_out_bias: float32 [640], replicated, may hold values from -3 to 3
Outputs:
- layer_out: float32 [16384, 640], P(('grp', 'dp', 'tp'))
- input_grad: float32 [16384, 640], P(('grp', 'dp', 'tp'))
- memory_grad: float32 [3, 16384, 640], P(None, ('grp', 'dp', 'tp'))
- norm_gain_grad: float32 [3, 640], replicated
- norm_bias_grad: float32 [3, 640], replicated
- self_qkv_grad: float32 [640, 3, 640], P(None, None, 'tp')
- self_out_grad: float32 [640, 640], P('tp')
- cross_q_grad: float32 [640, 640], P(None, 'tp')
- cross_kv_grad: float32 [640, 2, 640], P(None, None, 'tp')
- cross_out_grad: float32 [640, 640], P('tp')
- ffn_in_grad: float32 [640, 3072], P(None, 'tp')
- ffn_in_bias_grad: float32 [3072], P('tp')
- ffn_out_grad: float32 [3072, 640], P('tp')
- ffn_out_bias_grad: float32 [640], replicated
The draws below stay inside these ranges and needn't reach their ends.
Inputs may be any that keep to these rules, and one draw needn't show every extreme that they name: Row g of configs is group g's sub-net: width 4 * 128 or 640; heads 8 // 2 or 8; hidden units 3072 // 3, 2048 or 3072; encoder layers averaged 1 to 3. Some group has 3072 hidden units and some group averages one layer.
All inputs are finite; a program needn't handle non-finite values.
Results may differ from the reference program's by a relative error of at most 0.017.
Values may be sent and summed in bfloat16 or wider, within the bound.
A program may use at most 128 MiB of HBM per device.

```python
import jax
import jax.numpy as jnp
from jax import lax

D = 640
HEADS = 8
HD = 80
FF = 3072
LEN = 256
ENC_LAYERS = 3
SENTS = 64
TOKENS = 16384
GROUPS = 4
N_GRP = 4
N_DP = 2


def draw_configs(key, part):
    key = jax.random.fold_in(key, 7)
    streams = jax.random.split(key, 6)
    widths = jnp.where(jax.random.randint(streams[0], (GROUPS,), 0, 2) == 1, D, D * 4 // 5)
    heads = jnp.where(jax.random.randint(streams[1], (GROUPS,), 0, 2) == 1, HEADS, HEADS // 2)
    units = jax.random.randint(streams[2], (GROUPS,), 1, 4) * (FF // 3)
    depths = jax.random.randint(streams[3], (GROUPS,), 1, ENC_LAYERS + 1)
    widest = jax.random.randint(streams[4], (), 0, GROUPS)
    units = jnp.where(jnp.arange(GROUPS) == widest, FF, units)
    single = jax.random.randint(streams[5], (), 0, GROUPS)
    depths = jnp.where(jnp.arange(GROUPS) == single, 1, depths)
    return jnp.stack([widths, heads, units, depths], axis=1).astype(jnp.int32)


def set_ends(drawn, key, low, top_value):
    spot = [jax.random.randint(jax.random.fold_in(key, axis), (), 0, length) for axis, length in enumerate(drawn.shape)]
    longest = drawn.shape.index(max(drawn.shape))
    next_to = spot[:longest] + [(spot[longest] + 1) % drawn.shape[longest]] + spot[longest + 1:]
    return drawn.at[tuple(spot)].set(low).at[tuple(next_to)].set(top_value)


def levels(stream_key, dims, cuts, low, largest):
    loudness, own = 1.0, jax.random.fold_in(stream_key, 6)
    for position, shards_of in cuts:
        steps = jnp.exp(jax.random.uniform(jax.random.fold_in(own, position), (shards_of,), jnp.float32, low / len(cuts), largest / len(cuts)))
        loudness = loudness * jnp.repeat(steps, dims[position] // shards_of).reshape([-1 if axis == position else 1 for axis in range(len(dims))])
    return loudness


def scatter_about(key, shape, scale, limit, shards=(), held_as=jnp.bfloat16):
    level = levels(key, shape, shards, -0.22, 0.18) if shards else 1.0
    drawn = jax.random.normal(key, shape, jnp.float32) * scale * level
    return jnp.minimum(jnp.maximum(drawn, -limit), limit).astype(held_as)


def setup_inputs(seed: int = 0) -> dict:
    seeds = jax.random.split(jax.random.key(seed), 18)
    return {
        "inputs": scatter_about(seeds[0], (TOKENS, D), 1.0, 6.0, ((0, 32),)),
        "memory": scatter_about(seeds[1], (ENC_LAYERS, TOKENS, D), 1.0, 6.0, ((1, 32),)),
        "out_grad": scatter_about(seeds[2], (TOKENS, D), 1.0, 6.0, ((0, 32),)),
        "lengths": set_ends(jax.random.randint(seeds[3], (SENTS,), LEN // 8 + 1, LEN + 1), jax.random.fold_in(seeds[3], 1), LEN // 8 + 1, LEN).astype(jnp.int32),
        "src_lengths": set_ends(jax.random.randint(seeds[4], (SENTS,), LEN // 8 + 1, LEN + 1), jax.random.fold_in(seeds[4], 1), LEN // 8 + 1, LEN).astype(jnp.int32),
        "configs": draw_configs(jax.random.fold_in(seeds[17], 71), 0),
        "norm_gain": jnp.clip(1.0 + 0.1 * jax.random.normal(seeds[6], (3, D), jnp.float32), 0.5, 1.5),
        "norm_bias": scatter_about(seeds[7], (3, D), 0.3, 3.0, (), jnp.float32),
        "self_qkv": scatter_about(seeds[8], (D, 3, HEADS * HD), D ** -0.5, 0.25, ((2, 4),)),
        "self_out": scatter_about(seeds[9], (HEADS * HD, D), (HEADS * HD // 16) ** -0.5, 1.0, ((0, 4),)),
        "cross_q": scatter_about(seeds[10], (D, HEADS * HD), D ** -0.5, 0.25, ((1, 4),)),
        "cross_kv": scatter_about(seeds[11], (D, 2, HEADS * HD), D ** -0.5, 0.25, ((2, 4),)),
        "cross_out": scatter_about(seeds[12], (HEADS * HD, D), (HEADS * HD // 16) ** -0.5, 1.0, ((0, 4),)),
        "ffn_in": scatter_about(seeds[13], (D, FF), D ** -0.5, 0.25, ((1, 4),)),
        "ffn_in_bias": scatter_about(seeds[14], (FF,), 0.3, 3.0, ((0, 4),), jnp.float32),
        "ffn_out": scatter_about(seeds[15], (FF, D), (FF // 4) ** -0.5, 0.21875, ((0, 4),)),
        "ffn_out_bias": scatter_about(seeds[16], (D,), 0.3, 3.0, (), jnp.float32),
    }


EPSILON = 1e-05
NEGATIVE = -1e+30
HIGHEST = lax.Precision.HIGHEST

@jax.custom_vjp
def low(v):
    return lax.optimization_barrier(v.astype(jnp.bfloat16)).astype(jnp.float32)

@jax.custom_vjp
def low_back(v):
    return v

def low_keep(v):
    return (low(v), None)

def low_pass(kept, grad):
    return (grad,)

def back_keep(v):
    return (v, None)

def back_low(kept, grad):
    return (low(grad),)
low.defvjp(low_keep, low_pass)
low_back.defvjp(back_keep, back_low)

def layer_norm(rows, gain, shift, width_mask, width):
    mean = lax.optimization_barrier(jnp.sum(rows * width_mask, axis=-1, keepdims=True)) / width
    centred = (rows - mean) * width_mask
    spread = lax.optimization_barrier(jnp.sum(centred * centred, axis=-1, keepdims=True)) / width
    return (centred * lax.rsqrt(spread + EPSILON) * gain + shift) * width_mask

def attend(query, keys, values, allowed):
    scores = jnp.einsum('bqhc,bkhc->bhqk', query, keys, precision=HIGHEST) * HD ** (-0.5)
    scores = low_back(jnp.where(allowed[:, None], scores, NEGATIVE))
    weights = low(jax.nn.softmax(scores, axis=-1))
    return jnp.einsum('bhqk,bkhc->bqhc', weights, values, precision=HIGHEST)

def block_out(weights, rows, layers, lengths, src_lengths, config):
    gains, shifts, self_qkv, self_out, cross_q, cross_kv, cross_out, ffn_in, ffn_in_bias, ffn_out, ffn_out_bias = weights
    width = config[0]
    heads = config[1]
    units = config[2]
    depth = config[3]
    width_f = width.astype(jnp.float32)
    width_mask = (jnp.arange(D) < width).astype(jnp.float32)
    head_mask = (jnp.arange(HEADS * HD) < heads * HD).astype(jnp.float32)
    unit_mask = (jnp.arange(FF) < units).astype(jnp.float32)
    sentences = lengths.shape[0]
    place = jnp.arange(LEN)
    valid = (place[None, :] < lengths[:, None]).astype(jnp.float32).reshape(sentences * LEN, 1)
    keep = width_mask * valid
    causal = jnp.broadcast_to(place[:, None] >= place[None, :], (sentences, LEN, LEN))
    crossing = jnp.broadcast_to(place[None, None, :] < src_lengths[:, None, None], (sentences, LEN, LEN))

    def split(flat):
        return flat.reshape(sentences, LEN, HEADS, HD)

    def joined(shaped):
        return shaped.reshape(sentences * LEN, HEADS * HD)
    normed = low(layer_norm(rows, gains[0], shifts[0], width_mask, width_f))
    triple = low_back(low(jnp.einsum('rd,dkc->rkc', normed, self_qkv, precision=HIGHEST)))
    context = attend(split(triple[:, 0]), split(triple[:, 1]), split(triple[:, 2]), causal)
    context = low_back(low(joined(context) * head_mask))
    after_self = rows + low_back(jnp.dot(context, self_out, precision=HIGHEST)) * keep
    normed = low(layer_norm(after_self, gains[1], shifts[1], width_mask, width_f))
    query = low_back(low(jnp.dot(normed, cross_q, precision=HIGHEST)))
    chosen = (jnp.arange(ENC_LAYERS) >= ENC_LAYERS - depth).astype(jnp.float32)
    source = low(jnp.einsum('l,lrd->rd', chosen, layers, precision=HIGHEST) / depth.astype(jnp.float32) * width_mask)
    paired = low_back(low(jnp.einsum('rd,dkc->rkc', source, cross_kv, precision=HIGHEST)))
    context = attend(split(query), split(paired[:, 0]), split(paired[:, 1]), crossing)
    context = low_back(low(joined(context) * head_mask))
    after_cross = after_self + low_back(jnp.dot(context, cross_out, precision=HIGHEST)) * keep
    normed = low(layer_norm(after_cross, gains[2], shifts[2], width_mask, width_f))
    before = low_back(jnp.dot(normed, ffn_in, precision=HIGHEST) + ffn_in_bias)
    hidden = low(jax.nn.gelu(before, approximate=True) * unit_mask)
    return after_cross + (low_back(jnp.dot(hidden, ffn_out, precision=HIGHEST)) + ffn_out_bias) * keep

def forward(floats, integers):
    rows = floats[0]
    memory = floats[1]
    weights = floats[2:]
    lengths, src_lengths, configs = integers
    blocks = N_GRP * N_DP
    per_block = rows.shape[0] // blocks
    row_blocks = rows.reshape(blocks, per_block, D)
    memory_blocks = memory.reshape(ENC_LAYERS, blocks, per_block, D).transpose(1, 0, 2, 3)
    length_blocks = lengths.reshape(blocks, -1)
    source_blocks = src_lengths.reshape(blocks, -1)
    config_blocks = jnp.repeat(configs, N_DP, axis=0)

    def step(carried, pieces):
        return (carried, block_out(weights, pieces[0], pieces[1], pieces[2], pieces[3], pieces[4]))
    final_carry, outputs = lax.scan(jax.checkpoint(step), jnp.zeros((), jnp.float32), (row_blocks, memory_blocks, length_blocks, source_blocks, config_blocks))
    return outputs.reshape(rows.shape[0], D)

def reference(inputs, memory, out_grad, lengths, src_lengths, configs, norm_gain, norm_bias, self_qkv, self_out, cross_q, cross_kv, cross_out, ffn_in, ffn_in_bias, ffn_out, ffn_out_bias):
    floats = tuple((array.astype(jnp.float32) for array in (inputs, memory, norm_gain, norm_bias, self_qkv, self_out, cross_q, cross_kv, cross_out, ffn_in, ffn_in_bias, ffn_out, ffn_out_bias)))

    def apply(*arrays):
        return forward(arrays, (lengths, src_lengths, configs))
    layer_out, pullback = jax.vjp(apply, *floats)
    grads = pullback(out_grad.astype(jnp.float32))
    total = jnp.sum(lengths).astype(jnp.float32)
    return (layer_out, grads[0], grads[1], grads[2] / total, grads[3] / total, grads[4] / total, grads[5] / total, grads[6] / total, grads[7] / total, grads[8] / total, grads[9] / total, grads[10] / total, grads[11] / total, grads[12] / total)
```

```python
import jax
import jax.numpy as jnp
from jax import lax
from jax.sharding import PartitionSpec as P

HD = 80
LEN = 256
EPSILON = 1e-05
NEGATIVE = -1e30
SCALE = HD ** (-0.5)
F32 = jnp.float32
BF16 = jnp.bfloat16


def dot(left, right, left_axis, right_axis):
    return lax.dot_general(
        left, right, (((left_axis,), (right_axis,)), ((), ())), preferred_element_type=F32
    )


def norm_parts(rows, mask, width):
    mean = jnp.sum(rows * mask, axis=-1, keepdims=True) / width
    centred = (rows - mean) * mask
    rstd = lax.rsqrt(jnp.sum(centred * centred, axis=-1, keepdims=True) / width + EPSILON)
    return centred * rstd, rstd


def norm_forward(rows, gain, shift, mask, width):
    hat, _ = norm_parts(rows, mask, width)
    return (hat * gain + shift) * mask


def norm_backward(rows, gain, mask, width, upstream):
    hat, rstd = norm_parts(rows, mask, width)
    upstream = upstream * mask
    gain_term = jnp.sum(upstream * hat, axis=0)
    shift_term = jnp.sum(upstream, axis=0)
    scaled = upstream * gain
    first = jnp.sum(scaled, axis=-1, keepdims=True) / width
    second = jnp.sum(scaled * hat, axis=-1, keepdims=True) / width
    return (rstd * (scaled - first - hat * second)) * mask, gain_term, shift_term


def scores_of(query, keys, allowed):
    raw = jnp.einsum("bqhc,bkhc->bhqk", query, keys, preferred_element_type=F32) * SCALE
    return jnp.where(allowed[:, None], raw, NEGATIVE)


def attend_forward(query, keys, values, allowed):
    scores = scores_of(query, keys, allowed)
    highest = jnp.max(scores, axis=-1, keepdims=True)
    log_total = highest + jnp.log(jnp.sum(jnp.exp(scores - highest), axis=-1, keepdims=True))
    weights = jnp.exp(scores - log_total).astype(BF16)
    context = jnp.einsum("bhqk,bkhc->bqhc", weights, values, preferred_element_type=F32)
    return context, log_total


def attend_backward(query, keys, values, allowed, log_total, upstream):
    weights = jnp.exp(scores_of(query, keys, allowed) - log_total)
    low = weights.astype(BF16)
    value_grad = jnp.einsum("bhqk,bqhc->bkhc", low, upstream, preferred_element_type=F32)
    weight_grad = jnp.einsum("bqhc,bkhc->bhqk", upstream, values, preferred_element_type=F32)
    score_grad = weights * (weight_grad - jnp.sum(weight_grad * weights, axis=-1, keepdims=True))
    score_low = score_grad.astype(BF16)
    query_grad = jnp.einsum("bhqk,bkhc->bqhc", score_low, keys, preferred_element_type=F32) * SCALE
    key_grad = jnp.einsum("bhqk,bqhc->bkhc", score_low, query, preferred_element_type=F32) * SCALE
    return query_grad, key_grad, value_grad


def gather_whole(shard):
    parts = lax.axis_size("grp") * lax.axis_size("dp")
    share = shard.shape[0] // parts
    mine = lax.axis_index("grp") * lax.axis_size("dp") + lax.axis_index("dp")
    piece = lax.dynamic_slice_in_dim(shard, mine * share, share)
    column = lax.all_gather(piece, "tp", axis=0, tiled=False)
    whole = lax.all_gather(column, ("grp", "dp"), axis=1, tiled=False)
    return whole.reshape(whole.shape[0], shard.shape[0], shard.shape[1])


def reduce_whole(grads):
    low = grads.astype(BF16)
    piece = lax.psum_scatter(low, ("grp", "dp"), scatter_dimension=1, tiled=True)
    mine = lax.psum_scatter(piece, "tp", scatter_dimension=0, tiled=False)
    return lax.all_gather(mine, ("grp", "dp"), axis=0, tiled=True).astype(F32)


def per_device(
    inputs, memory, out_grad, lengths, src_lengths, configs, norm_gain, norm_bias,
    self_qkv, self_out, cross_q, cross_kv, cross_out, ffn_in, ffn_in_bias, ffn_out, ffn_out_bias,
):
    owned, model = inputs.shape
    layers = memory.shape[0]
    tp = lax.axis_size("tp")
    place_tp = lax.axis_index("tp")
    sentences = owned // LEN
    local = self_out.shape[0]
    pair = local // HD
    units_local = ffn_in.shape[1]
    width, heads, units, depth = (configs[0, i] for i in range(4))
    width_f = width.astype(F32)
    depth_f = depth.astype(F32)
    width_mask = (jnp.arange(model) < width).astype(F32)
    head_mask = (jnp.arange(tp * local) < heads * HD).astype(F32)
    unit_mask = (jnp.arange(tp * units_local) < units).astype(F32)
    place = jnp.arange(LEN)
    own_lengths = lax.dynamic_slice_in_dim(lengths, place_tp * sentences, sentences)
    own_source = lax.dynamic_slice_in_dim(src_lengths, place_tp * sentences, sentences)
    valid = (place[None, :] < own_lengths[:, None]).astype(F32).reshape(owned, 1)
    keep = width_mask * valid
    causal = jnp.broadcast_to(place[:, None] >= place[None, :], (sentences, LEN, LEN))
    crossing = jnp.broadcast_to(place[None, None, :] < own_source[:, None, None], (sentences, LEN, LEN))

    first = jnp.concatenate([self_qkv.transpose(1, 2, 0).reshape(3 * local, model), self_out], axis=0)
    second = jnp.concatenate(
        [cross_q.T, cross_kv.transpose(1, 2, 0).reshape(2 * local, model), cross_out], axis=0
    )
    first = gather_whole(first)
    second = gather_whole(second)
    third = gather_whole(ffn_in)
    fourth = gather_whole(ffn_out)
    bias_in = lax.all_gather(ffn_in_bias, "tp", axis=0, tiled=True)

    def part(block, start):
        return block[:, start * local:(start + 1) * local].reshape(tp * local, model)

    def split(flat):
        return flat.astype(BF16).reshape(sentences, LEN, tp * pair, HD)

    def joined(shaped):
        return shaped.reshape(owned, tp * local)

    wq, wk, wv, wo = (part(first, i) for i in range(4))
    xq, xk, xv, xo = (part(second, i) for i in range(4))
    w_up = third.transpose(1, 0, 2).reshape(model, tp * units_local)
    w_down = fourth.reshape(tp * units_local, model)

    rows = inputs.astype(F32)
    a1 = norm_forward(rows, norm_gain[0], norm_bias[0], width_mask, width_f).astype(BF16)
    q1, k1, v1 = split(dot(a1, wq, 1, 1)), split(dot(a1, wk, 1, 1)), split(dot(a1, wv, 1, 1))
    c1, t1 = attend_forward(q1, k1, v1, causal)
    c1 = (joined(c1) * head_mask).astype(BF16)
    h1 = rows + dot(c1, wo, 1, 0) * keep
    a2 = norm_forward(h1, norm_gain[1], norm_bias[1], width_mask, width_f).astype(BF16)
    chosen = (jnp.arange(layers) >= layers - depth).astype(F32)
    mixed = chosen[0] * memory[0].astype(F32)
    for level in range(1, layers):
        mixed = mixed + chosen[level] * memory[level].astype(F32)
    source = (mixed / depth_f * width_mask).astype(BF16)
    q2, k2, v2 = split(dot(a2, xq, 1, 1)), split(dot(source, xk, 1, 1)), split(dot(source, xv, 1, 1))
    c2, t2 = attend_forward(q2, k2, v2, crossing)
    c2 = (joined(c2) * head_mask).astype(BF16)
    h2 = h1 + dot(c2, xo, 1, 0) * keep
    a3 = norm_forward(h2, norm_gain[2], norm_bias[2], width_mask, width_f).astype(BF16)
    before = dot(a3, w_up, 1, 0) + bias_in

    def activate(values):
        return jax.nn.gelu(values, approximate=True) * unit_mask

    hidden, gelu_back = jax.vjp(activate, before)
    hidden = hidden.astype(BF16)
    layer_out = h2 + (dot(hidden, w_down, 1, 0) + ffn_out_bias) * keep

    upstream = out_grad.astype(F32)
    masked = upstream * keep
    bias_out_grad = jnp.sum(masked, axis=0)
    e3 = masked.astype(BF16)
    down_grad = dot(hidden, e3, 0, 0)
    du = gelu_back(dot(e3, w_down, 1, 1))[0].astype(BF16)
    up_grad = dot(a3, du, 0, 0)
    bias_in_grad = jnp.sum(du.astype(F32), axis=0)
    rows_c, gain_c, shift_c = norm_backward(h2, norm_gain[2], width_mask, width_f, dot(du, w_up, 1, 1))
    dh2 = upstream + rows_c
    e2 = (dh2 * keep).astype(BF16)
    xo_grad = dot(c2, e2, 0, 0)
    dc2 = (dot(e2, xo, 1, 1) * head_mask).astype(BF16)
    dq2, dk2, dv2 = attend_backward(q2, k2, v2, crossing, t2, split(dc2))
    dq2, dk2, dv2 = (joined(x).astype(BF16) for x in (dq2, dk2, dv2))
    xq_grad, xk_grad, xv_grad = dot(dq2, a2, 0, 0), dot(dk2, source, 0, 0), dot(dv2, source, 0, 0)
    source_grad = (dot(dk2, xk, 1, 0) + dot(dv2, xv, 1, 0)) * width_mask / depth_f
    memory_grad = chosen[:, None, None] * source_grad[None]
    rows_b, gain_b, shift_b = norm_backward(h1, norm_gain[1], width_mask, width_f, dot(dq2, xq, 1, 0))
    dh1 = dh2 + rows_b
    e1 = (dh1 * keep).astype(BF16)
    wo_grad = dot(c1, e1, 0, 0)
    dc1 = (dot(e1, wo, 1, 1) * head_mask).astype(BF16)
    dq1, dk1, dv1 = attend_backward(q1, k1, v1, causal, t1, split(dc1))
    dq1, dk1, dv1 = (joined(x).astype(BF16) for x in (dq1, dk1, dv1))
    wq_grad, wk_grad, wv_grad = dot(dq1, a1, 0, 0), dot(dk1, a1, 0, 0), dot(dv1, a1, 0, 0)
    rows_a, gain_a, shift_a = norm_backward(
        rows, norm_gain[0], width_mask, width_f, dot(dq1, wq, 1, 0) + dot(dk1, wk, 1, 0) + dot(dv1, wv, 1, 0)
    )
    input_grad = dh1 + rows_a

    def packed(*grads):
        return jnp.concatenate([g.reshape(tp, local, model) for g in grads], axis=1)

    fourth_grad = reduce_whole(down_grad.reshape(tp, units_local, model))
    third_grad = reduce_whole(up_grad.reshape(model, tp, units_local).transpose(1, 0, 2))
    second_grad = reduce_whole(packed(xq_grad, xk_grad, xv_grad, xo_grad))
    first_grad = reduce_whole(packed(wq_grad, wk_grad, wv_grad, wo_grad))
    small = jnp.concatenate(
        [gain_a, gain_b, gain_c, shift_a, shift_b, shift_c, bias_out_grad, bias_in_grad,
         jnp.broadcast_to(jnp.sum(own_lengths).astype(F32), (128,))]
    )
    small = lax.psum(small, ("grp", "dp", "tp"))
    inverse = 1.0 / small[-1]
    small = small * inverse
    gains = small[:3 * model].reshape(3, model)
    shifts = small[3 * model:6 * model].reshape(3, model)
    bias_out_grad = small[6 * model:7 * model]
    bias_in_grad = lax.dynamic_slice_in_dim(small, 7 * model + place_tp * units_local, units_local)
    first_grad, second_grad, third_grad, fourth_grad = (
        x * inverse for x in (first_grad, second_grad, third_grad, fourth_grad)
    )
    return (
        layer_out,
        input_grad,
        memory_grad,
        gains,
        shifts,
        first_grad[:3 * local].reshape(3, local, model).transpose(2, 0, 1),
        first_grad[3 * local:],
        second_grad[:local].T,
        second_grad[local:3 * local].reshape(2, local, model).transpose(2, 0, 1),
        second_grad[3 * local:],
        third_grad,
        bias_in_grad,
        fourth_grad,
        bias_out_grad,
    )


def solution(mesh):
    rows = P(("grp", "dp", "tp"), None)
    stack = P(None, ("grp", "dp", "tp"), None)
    weights = (
        P(None, None, "tp"), P("tp", None), P(None, "tp"), P(None, None, "tp"), P("tp", None),
        P(None, "tp"), P("tp"), P("tp", None), P(),
    )
    return jax.shard_map(
        per_device,
        mesh=mesh,
        in_specs=(rows, stack, rows, P(("grp", "dp")), P(("grp", "dp")), P("grp", None), P(), P()) + weights,
        out_specs=(rows, rows, stack, P(), P()) + weights,
        check_vma=False,
    )
```

```python
import functools

import jax
import jax.numpy as jnp
from jax import lax
from jax.experimental import pallas as pl
from jax.experimental.pallas import tpu as pltpu
from jax.sharding import PartitionSpec as P

HD = 80
LEN = 256
EPSILON = 1e-05
NEGATIVE = -1e30
SCALE = HD ** (-0.5)
F32 = jnp.float32
BF16 = jnp.bfloat16


def dot(left, right, left_axis, right_axis):
    return lax.dot_general(
        left, right, (((left_axis,), (right_axis,)), ((), ())), preferred_element_type=F32
    )


def norm_parts(rows, mask, width):
    mean = jnp.sum(rows * mask, axis=-1, keepdims=True) / width
    centred = (rows - mean) * mask
    rstd = lax.rsqrt(jnp.sum(centred * centred, axis=-1, keepdims=True) / width + EPSILON)
    return centred * rstd, rstd


def norm_forward(rows, gain, shift, mask, width):
    hat, _ = norm_parts(rows, mask, width)
    return (hat * gain + shift) * mask


def norm_backward(rows, gain, mask, width, upstream):
    hat, rstd = norm_parts(rows, mask, width)
    upstream = upstream * mask
    gain_term = jnp.sum(upstream * hat, axis=0)
    shift_term = jnp.sum(upstream, axis=0)
    scaled = upstream * gain
    first = jnp.sum(scaled, axis=-1, keepdims=True) / width
    second = jnp.sum(scaled * hat, axis=-1, keepdims=True) / width
    return (rstd * (scaled - first - hat * second)) * mask, gain_term, shift_term


def scores_of(query, keys, allowed):
    raw = jnp.einsum("bqhc,bkhc->bhqk", query, keys, preferred_element_type=F32) * SCALE
    return jnp.where(allowed[:, None], raw, NEGATIVE)


def attend_forward(query, keys, values, allowed):
    scores = scores_of(query, keys, allowed)
    highest = jnp.max(scores, axis=-1, keepdims=True)
    log_total = highest + jnp.log(jnp.sum(jnp.exp(scores - highest), axis=-1, keepdims=True))
    weights = jnp.exp(scores - log_total).astype(BF16)
    context = jnp.einsum("bhqk,bkhc->bqhc", weights, values, preferred_element_type=F32)
    return context, log_total


def attend_backward(query, keys, values, allowed, log_total, upstream):
    weights = jnp.exp(scores_of(query, keys, allowed) - log_total)
    low = weights.astype(BF16)
    value_grad = jnp.einsum("bhqk,bqhc->bkhc", low, upstream, preferred_element_type=F32)
    weight_grad = jnp.einsum("bqhc,bkhc->bhqk", upstream, values, preferred_element_type=F32)
    score_grad = weights * (weight_grad - jnp.sum(weight_grad * weights, axis=-1, keepdims=True))
    score_low = score_grad.astype(BF16)
    query_grad = jnp.einsum("bhqk,bkhc->bqhc", score_low, keys, preferred_element_type=F32) * SCALE
    key_grad = jnp.einsum("bhqk,bqhc->bkhc", score_low, query, preferred_element_type=F32) * SCALE
    return query_grad, key_grad, value_grad


MESH = pl.DeviceIdType.MESH


class Place:
    def __init__(self):
        self.tps = lax.axis_size("tp")
        self.extra = lax.axis_size("dp") // 2
        assert lax.axis_size("grp") == 4 and lax.axis_size("dp") % 2 == 0
        grp, dp, tp = (lax.axis_index(name) for name in ("grp", "dp", "tp"))
        core, low, high = dp % 2, grp % 2, grp // 2
        flip_low, flip_high = grp + 1 - 2 * low, grp + 2 - 4 * high
        self.grp, self.dp, self.tp, self.core = grp, dp, tp, core
        self.first_bit = (1 - core) * low + core * high
        self.second_bit = (1 - core) * high + core * low
        self.first = ((1 - core) * flip_low + core * flip_high, dp, tp)
        self.second = ((1 - core) * flip_high + core * flip_low, dp, tp)
        self.sibling = (grp, dp + 1 - 2 * core, tp)
        self.above = (grp, dp, tp + 1)
        self.below = (grp, dp, tp - 1)
        self.has_above = tp < self.tps - 1
        self.has_below = tp > 0

    def copy_of(self, step):
        return (self.grp, ((self.dp // 2 + step) % self.extra) * 2 + self.core, self.tp)

    def nth_block(self, k):
        size = self.tps
        upper = (2 * self.tp) // size
        lead = (1 - upper) * self.tp + upper * (size - 1 - self.tp)
        spot = k + (k + size - lead) // size
        return (1 - upper) * spot + upper * (size - 1 - spot)

    def barrier(self):
        sem = pltpu.get_barrier_semaphore()
        fixed = [self.first, self.second, self.sibling] + [self.copy_of(s) for s in range(1, self.extra)]
        for device in fixed:
            pl.semaphore_signal(sem, inc=1, device_id=device, device_id_type=MESH)
        for there, device in ((self.has_above, self.above), (self.has_below, self.below)):

            @pl.when(there)
            def _():
                pl.semaphore_signal(sem, inc=1, device_id=device, device_id_type=MESH)

        size = self.tps
        ends = (self.tp + size - 1) // size + (2 * size - 2 - self.tp) // size
        pl.semaphore_wait(sem, len(fixed) + ends)


def push(src, dst, send_sem, recv_sem, device):
    return pltpu.make_async_remote_copy(
        src_ref=src, dst_ref=dst, send_sem=send_sem, recv_sem=recv_sem, device_id=device, device_id_type=MESH
    )


def rows_of(ref, lead, start, count):
    return ref.at[lead, pl.ds(pl.multiple_of(start, 16), count)]


class Spread:
    def __init__(self, place, view, unit, sems):
        self.place, self.view, self.unit, self.sems = place, view, unit, sems

    def region(self, stage, mine=True):
        p, unit = self.place, self.unit
        if stage == 0:
            bit = p.second_bit if mine else 1 - p.second_bit
            return self.view(p.core * 4 * unit + (p.first_bit * 2 + bit) * unit, unit)
        if stage == 1:
            bit = p.first_bit if mine else 1 - p.first_bit
            return self.view(p.core * 4 * unit + bit * 2 * unit, 2 * unit)
        half = p.core if mine else 1 - p.core
        return self.view(half * 4 * unit, 4 * unit)

    def copy(self, stage, mine=True):
        part = self.region(stage, mine)
        device = (self.place.second, self.place.first, self.place.sibling)[stage]
        return push(part, part, self.sems(2 * stage), self.sems(2 * stage + 1), device)

    def send(self, stage):
        self.copy(stage).start()

    def receive(self, stage):
        self.copy(stage, mine=False).wait_recv()

    def finish(self):
        for stage in range(3):
            self.copy(stage).wait_send()


class Gather:
    KINDS = 9

    def __init__(self, place, buffers, sems):
        self.place, self.buffers, self.sems = place, buffers, sems
        self.unit = [ref.shape[1] // 8 for ref in buffers]
        self.others = place.tps - 1

    def own_rows(self, g, j):
        p, unit = self.place, self.unit[g]
        return rows_of(self.buffers[g], j, p.core * 4 * unit + (p.first_bit * 2 + p.second_bit) * unit, unit)

    def spread(self, g, j):
        return Spread(
            self.place,
            lambda start, count: rows_of(self.buffers[g], j, start, count),
            self.unit[g],
            lambda kind: self.sems.at[kind, g, j],
        )

    def up(self, g, j):
        part = self.own_rows(g, j)
        return push(part, part, self.sems.at[6, g, j], self.sems.at[8, g, j], self.place.above)

    def down(self, g, j):
        part = self.own_rows(g, j)
        return push(part, part, self.sems.at[7, g, j], self.sems.at[8, g, j], self.place.below)

    def relays(self, g, j):
        p = self.place
        return (
            (jnp.logical_and(j <= p.tp, p.has_above), self.up(g, j)),
            (jnp.logical_and(j >= p.tp, p.has_below), self.down(g, j)),
        )

    def start(self, g):
        for needed, copy in self.relays(g, self.place.tp):
            pl.when(needed)(copy.start)

    def step(self, g, k, stage):
        j = self.place.nth_block(k)
        spread = self.spread(g, j)
        if stage == 0:
            self.up(g, j).wait_recv()
            for needed, copy in self.relays(g, j):
                pl.when(needed)(copy.start)
        else:
            spread.receive(stage - 1)
        if stage < 3:
            spread.send(stage)

    def finish(self, g):
        def drain(j):
            for needed, copy in self.relays(g, j):
                pl.when(needed)(copy.wait_send)

        drain(self.place.tp)
        for k in range(self.others):
            j = self.place.nth_block(k)
            drain(j)
            self.spread(g, j).finish()


def gather_kernel(*refs):
    sources, buffers, sems, local = refs[:7], refs[7:11], refs[11], refs[12]
    place = Place()
    columns = sources[1].shape[0]
    mine = place.tp
    pieces = (
        ((0, 3 * columns), (3 * columns, columns)),
        ((0, columns), (columns, 2 * columns), (3 * columns, columns)),
        ((0, sources[5].shape[0]),),
        ((0, sources[6].shape[0]),),
    )
    fills, n = [], 0
    for g, parts in enumerate(pieces):
        fills.append([])
        for start, size in parts:
            copy = pltpu.make_async_copy(sources[n], buffers[g].at[mine, pl.ds(start, size)], local.at[n])
            copy.start()
            fills[g].append(copy)
            n += 1
    place.barrier()
    gather = Gather(place, buffers, sems)
    for g in range(4):
        for copy in fills[g]:
            copy.wait()
        gather.start(g)
    events = [(g, k) for g in range(4) for k in range(gather.others)]
    for tick in range(len(events) + 3):
        for stage in range(4):
            if 0 <= tick - stage < len(events):
                gather.step(*events[tick - stage], stage)
    for g in range(4):
        gather.finish(g)


def gather_weights(sources):
    tp = lax.axis_size("tp")
    columns, model = sources[1].shape
    shapes = [(tp, 4 * columns, model)] * 2 + [(tp,) + sources[5].shape, (tp,) + sources[6].shape]
    return pl.pallas_call(
        gather_kernel,
        out_shape=[jax.ShapeDtypeStruct(shape, BF16) for shape in shapes],
        in_specs=[pl.BlockSpec(memory_space=pl.ANY)] * 7,
        out_specs=[pl.BlockSpec(memory_space=pl.ANY)] * 4,
        scratch_shapes=[
            pltpu.SemaphoreType.DMA((Gather.KINDS, 4, tp)),
            pltpu.SemaphoreType.DMA((7,)),
        ],
        compiler_params=pltpu.CompilerParams(collective_id=1, has_side_effects=True),
        name="gather_weights",
    )(*sources)


class Reduce:
    KINDS = 18

    def __init__(self, place, grads, halves, firsts, seconds, lines, extras, totals, sems):
        self.place, self.grads, self.totals, self.sems = place, grads, totals, sems
        self.halves, self.firsts, self.seconds, self.lines, self.extras = halves, firsts, seconds, lines, extras
        self.unit = [ref.shape[1] // 8 for ref in grads]

    def sem(self, kind, g, j):
        return self.sems.at[kind, g, j]

    def region(self, g, j, stage, kept):
        p, unit = self.place, self.unit[g]
        if stage == 0:
            half = p.core if kept else 1 - p.core
            return rows_of(self.grads[g], j, half * 4 * unit, 4 * unit)
        if stage == 1:
            bit = p.first_bit if kept else 1 - p.first_bit
            return rows_of(self.grads[g], j, p.core * 4 * unit + bit * 2 * unit, 2 * unit)
        bit = p.second_bit if kept else 1 - p.second_bit
        return rows_of(self.grads[g], j, p.core * 4 * unit + (p.first_bit * 2 + bit) * unit, unit)

    def landing(self, g, j, stage):
        return (self.halves, self.firsts, self.seconds)[stage][g].at[j]

    def copy(self, g, j, stage):
        device = (self.place.sibling, self.place.first, self.place.second)[stage]
        return push(
            self.region(g, j, stage, False), self.landing(g, j, stage),
            self.sem(2 * stage, g, j), self.sem(2 * stage + 1, g, j), device,
        )

    def add(self, g, j, stage):
        self.copy(g, j, stage).wait_recv()
        kept = self.region(g, j, stage, True)
        kept[...] = kept[...] + self.landing(g, j, stage)[...]

    def step(self, g, j, stage):
        if stage > 0:
            self.add(g, j, stage - 1)
        if stage < 3:
            self.copy(g, j, stage).start()

    def piece(self, g, j):
        return self.region(g, j, 2, True)

    def hop(self, g, j, upward):
        p = self.place
        way = 0 if upward else 1
        return push(
            self.piece(g, j), self.lines[g].at[way, j],
            self.sem(6 + 2 * way, g, j), self.sem(7 + 2 * way, g, j), p.above if upward else p.below,
        )

    def travel(self, g, k):
        p = self.place
        for upward in (True, False):
            j = p.tps - 1 - k if upward else k
            has_source = p.has_below if upward else p.has_above
            involved = j >= p.tp if upward else j <= p.tp
            passes = j > p.tp if upward else j < p.tp

            @pl.when(jnp.logical_and(involved, has_source))
            def _():
                self.hop(g, j, upward).wait_recv()
                kept = self.piece(g, j)
                kept[...] = kept[...] + self.lines[g][0 if upward else 1, j]

            pl.when(passes)(self.hop(g, j, upward).start)

    def copies(self, g, step):
        p = self.place
        return push(
            self.piece(g, p.tp), self.extras[g].at[step], self.sem(16, g, step), self.sem(17, g, step), p.copy_of(step)
        )

    def among_copies(self, g):
        p = self.place
        if p.extra > 1:
            for step in range(1, p.extra):
                self.copies(g, step).start()
            total = self.piece(g, p.tp)[...].astype(F32)
            for step in range(1, p.extra):
                self.copies(g, step).wait()
                total = total + self.extras[g][step].astype(F32)
            self.piece(g, p.tp)[...] = total.astype(BF16)

    def spread(self, g):
        return Spread(
            self.place,
            lambda start, count: self.totals[g].at[pl.ds(pl.multiple_of(start, 16), count)],
            self.unit[g],
            lambda kind: self.sems.at[10 + kind, g, 0],
        )

    def settle(self, g):
        self.among_copies(g)
        self.spread(g).region(0)[...] = self.piece(g, self.place.tp)[...]
        self.spread(g).send(0)

    def share(self, g, stage):
        spread = self.spread(g)
        spread.receive(stage - 1)
        if stage < 3:
            spread.send(stage)

    def finish(self, g):
        p = self.place
        for j in range(p.tps):
            for stage in range(3):
                self.copy(g, j, stage).wait_send()
            pl.when(j > p.tp)(self.hop(g, j, True).wait_send)
            pl.when(j < p.tp)(self.hop(g, j, False).wait_send)
        self.spread(g).finish()


class SumSmall:
    SLOTS = 12

    def __init__(self, place, slots, sems):
        self.place, self.slots, self.sems = place, slots, sems

    def move(self, source, device):
        return push(
            self.slots.at[source], self.slots.at[source + 1], self.sems.at[source], self.sems.at[source + 1], device
        )

    def pair(self, stage):
        p = self.place
        return self.move(2 * stage, (p.sibling, p.first, p.second)[stage])

    def start(self, value):
        p = self.place
        for there, slot in ((p.has_below, 7), (p.has_above, 9)):

            @pl.when(jnp.logical_not(there))
            def _():
                self.slots[slot] = jnp.zeros_like(value)

        self.slots[0] = value
        self.pair(0).start()

    def exchange(self, stage):
        self.pair(stage).wait_recv()
        value = self.slots[2 * stage] + self.slots[2 * stage + 1]
        if stage < 2:
            self.slots[2 * stage + 2] = value
            self.pair(stage + 1).start()
        else:
            self.slots[10] = value

    def among_copies(self):
        p = self.place
        base = self.SLOTS
        for step in range(1, p.extra):
            self.copies(step).start()
        for step in range(1, p.extra):
            self.copies(step).wait()
        if p.extra > 1:
            total = self.slots[10]
            for step in range(1, p.extra):
                total = total + self.slots[base + step]
            self.slots[11] = total
        else:
            self.slots[11] = self.slots[10]

    def copies(self, step):
        base = self.SLOTS
        return push(
            self.slots.at[10], self.slots.at[base + step],
            self.sems.at[base + 2 * step], self.sems.at[base + 2 * step + 1], self.place.copy_of(step),
        )

    def line(self, upward):
        p = self.place
        source, target = (p.has_below, p.has_above) if upward else (p.has_above, p.has_below)
        slot = 6 if upward else 8
        pl.when(source)(self.move(slot, p.above if upward else p.below).wait_recv)

        @pl.when(target)
        def _():
            self.slots[slot] = self.slots[slot + 1] + self.slots[11]
            self.move(slot, p.above if upward else p.below).start()

    def total(self):
        return self.slots[11] + self.slots[7] + self.slots[9]

    def finish(self):
        p = self.place
        for stage in range(3):
            self.pair(stage).wait_send()
        pl.when(p.has_above)(self.move(6, p.above).wait_send)
        pl.when(p.has_below)(self.move(8, p.below).wait_send)


def run_plan(plan):
    for _, _, step in sorted(plan, key=lambda entry: entry[:2]):
        step()


def reduce_kernel(*refs):
    sources, small_in = refs[:4], refs[4]
    outs, small_out = refs[5:9], refs[9]
    grads, halves, firsts, seconds, lines, extras, totals = (refs[10 + 4 * i:14 + 4 * i] for i in range(7))
    slots, sems, small_sems, local = refs[38:]
    place = Place()
    loads = {}
    for g in (3, 2, 1, 0):
        for j in range(place.tps):
            loads[g, j] = pltpu.make_async_copy(sources[g].at[j], grads[g].at[j], local.at[g, j])
            loads[g, j].start()
    place.barrier()
    reduce = Reduce(place, grads, halves, firsts, seconds, lines, extras, totals, sems)
    small = SumSmall(place, slots, small_sems)
    plan = []

    def add(tick, order, step, *args):
        plan.append((tick, order, functools.partial(step, *args)))

    def begin(g, j):
        loads[g, j].wait()
        reduce.step(g, j, 0)

    n = place.tps
    stores = {}

    def store(g):
        stores[g] = pltpu.make_async_copy(totals[g], outs[g], local.at[g, n])
        stores[g].start()

    for i, g in enumerate((3, 2, 1, 0)):
        for j in range(n):
            e = i * n + j
            add(e, 0, begin, g, j)
            for stage in (1, 2, 3):
                add(e + stage, 90 - 10 * i - stage, reduce.step, g, j, stage)
        last = i * n + n + 2
        for k in range(n - 1):
            add(last + k, 99 - 10 * i - 4, reduce.travel, g, k)
        add(last + n - 1, 99 - 10 * i - 5, reduce.settle, g)
        for stage in (1, 2, 3):
            add(last + n - 1 + stage, 99 - 10 * i - 5 - stage, reduce.share, g, stage)
        add(last + n + 2, 99, store, g)
    add(0, 1, lambda: small.start(small_in[...]))
    for stage in range(3):
        add(stage + 1, 98, small.exchange, stage)
    add(4, 98, small.among_copies)
    add(5, 98, small.line, True)
    add(5, 98, small.line, False)
    run_plan(plan)
    small_out[...] = small.total()
    for g in range(4):
        reduce.finish(g)
        stores[g].wait()
    small.finish()


def reduce_gradients(grads, small):
    n, extra = lax.axis_size("tp"), lax.axis_size("dp") // 2
    shapes = [g.shape for g in grads]
    vm = lambda parts, dtype=BF16: [pltpu.VMEM(shape, dtype) for shape in parts]
    scratch = (
        vm(shapes)
        + vm((n, r // 2, c) for _, r, c in shapes)
        + vm((n, r // 4, c) for _, r, c in shapes)
        + vm((n, r // 8, c) for _, r, c in shapes)
        + vm((2, n, r // 8, c) for _, r, c in shapes)
        + vm((extra, r // 8, c) for _, r, c in shapes)
        + vm((r, c) for _, r, c in shapes)
        + vm([(SumSmall.SLOTS + extra,) + small.shape], F32)
        + [
            pltpu.SemaphoreType.DMA((Reduce.KINDS, 4, max(n, extra))),
            pltpu.SemaphoreType.DMA((SumSmall.SLOTS + 2 * extra,)),
            pltpu.SemaphoreType.DMA((4, n + 1)),
        ]
    )
    return pl.pallas_call(
        reduce_kernel,
        out_shape=[jax.ShapeDtypeStruct((r, c), BF16) for _, r, c in shapes] + [jax.ShapeDtypeStruct(small.shape, F32)],
        in_specs=[pl.BlockSpec(memory_space=pl.ANY)] * 4 + [pl.BlockSpec(memory_space=pltpu.VMEM)],
        out_specs=[pl.BlockSpec(memory_space=pl.ANY)] * 4 + [pl.BlockSpec(memory_space=pltpu.VMEM)],
        scratch_shapes=scratch,
        compiler_params=pltpu.CompilerParams(collective_id=2, has_side_effects=True, vmem_limit_bytes=60 * 2**20),
        name="reduce_gradients",
    )(*grads, small)


def per_device(
    inputs, memory, out_grad, lengths, src_lengths, configs, norm_gain, norm_bias,
    self_qkv, self_out, cross_q, cross_kv, cross_out, ffn_in, ffn_in_bias, ffn_out, ffn_out_bias,
):
    owned, model = inputs.shape
    layers = memory.shape[0]
    tp = lax.axis_size("tp")
    place_tp = lax.axis_index("tp")
    sentences = owned // LEN
    local = self_out.shape[0]
    pair = local // HD
    units_local = ffn_in.shape[1]
    width, heads, units, depth = (configs[0, i] for i in range(4))
    width_f = width.astype(F32)
    depth_f = depth.astype(F32)
    width_mask = (jnp.arange(model) < width).astype(F32)
    head_mask = (jnp.arange(tp * local) < heads * HD).astype(F32)
    unit_mask = (jnp.arange(tp * units_local) < units).astype(F32)
    place = jnp.arange(LEN)
    own_lengths = lax.dynamic_slice_in_dim(lengths, place_tp * sentences, sentences)
    own_source = lax.dynamic_slice_in_dim(src_lengths, place_tp * sentences, sentences)
    valid = (place[None, :] < own_lengths[:, None]).astype(F32).reshape(owned, 1)
    keep = width_mask * valid
    causal = jnp.broadcast_to(place[:, None] >= place[None, :], (sentences, LEN, LEN))
    crossing = jnp.broadcast_to(place[None, None, :] < own_source[:, None, None], (sentences, LEN, LEN))

    first, second, third, fourth = gather_weights(
        (
            self_qkv.transpose(1, 2, 0).reshape(3 * local, model),
            self_out,
            cross_q.T,
            cross_kv.transpose(1, 2, 0).reshape(2 * local, model),
            cross_out,
            ffn_in,
            ffn_out,
        )
    )
    bias_in = lax.all_gather(ffn_in_bias, "tp", axis=0, tiled=True)

    def part(block, start):
        return block[:, start * local:(start + 1) * local].reshape(tp * local, model)

    def split(flat):
        return flat.astype(BF16).reshape(sentences, LEN, tp * pair, HD)

    def joined(shaped):
        return shaped.reshape(owned, tp * local)

    wq, wk, wv, wo = (part(first, i) for i in range(4))
    xq, xk, xv, xo = (part(second, i) for i in range(4))
    w_up = third.transpose(1, 0, 2).reshape(model, tp * units_local)
    w_down = fourth.reshape(tp * units_local, model)

    rows = inputs.astype(F32)
    a1 = norm_forward(rows, norm_gain[0], norm_bias[0], width_mask, width_f).astype(BF16)
    q1, k1, v1 = split(dot(a1, wq, 1, 1)), split(dot(a1, wk, 1, 1)), split(dot(a1, wv, 1, 1))
    c1, t1 = attend_forward(q1, k1, v1, causal)
    c1 = (joined(c1) * head_mask).astype(BF16)
    h1 = rows + dot(c1, wo, 1, 0) * keep
    a2 = norm_forward(h1, norm_gain[1], norm_bias[1], width_mask, width_f).astype(BF16)
    chosen = (jnp.arange(layers) >= layers - depth).astype(F32)
    mixed = chosen[0] * memory[0].astype(F32)
    for level in range(1, layers):
        mixed = mixed + chosen[level] * memory[level].astype(F32)
    source = (mixed / depth_f * width_mask).astype(BF16)
    q2, k2, v2 = split(dot(a2, xq, 1, 1)), split(dot(source, xk, 1, 1)), split(dot(source, xv, 1, 1))
    c2, t2 = attend_forward(q2, k2, v2, crossing)
    c2 = (joined(c2) * head_mask).astype(BF16)
    h2 = h1 + dot(c2, xo, 1, 0) * keep
    a3 = norm_forward(h2, norm_gain[2], norm_bias[2], width_mask, width_f).astype(BF16)
    before = dot(a3, w_up, 1, 0) + bias_in

    def activate(values):
        return jax.nn.gelu(values, approximate=True) * unit_mask

    hidden, gelu_back = jax.vjp(activate, before)
    hidden = hidden.astype(BF16)
    layer_out = h2 + (dot(hidden, w_down, 1, 0) + ffn_out_bias) * keep

    upstream = out_grad.astype(F32)
    masked = upstream * keep
    bias_out_grad = jnp.sum(masked, axis=0)
    e3 = masked.astype(BF16)
    down_grad = dot(hidden, e3, 0, 0)
    du = gelu_back(dot(e3, w_down, 1, 1))[0].astype(BF16)
    up_grad = dot(a3, du, 0, 0)
    bias_in_grad = jnp.sum(du.astype(F32), axis=0)
    rows_c, gain_c, shift_c = norm_backward(h2, norm_gain[2], width_mask, width_f, dot(du, w_up, 1, 1))
    dh2 = upstream + rows_c
    e2 = (dh2 * keep).astype(BF16)
    xo_grad = dot(c2, e2, 0, 0)
    dc2 = (dot(e2, xo, 1, 1) * head_mask).astype(BF16)
    dq2, dk2, dv2 = attend_backward(q2, k2, v2, crossing, t2, split(dc2))
    dq2, dk2, dv2 = (joined(x).astype(BF16) for x in (dq2, dk2, dv2))
    xq_grad, xk_grad, xv_grad = dot(dq2, a2, 0, 0), dot(dk2, source, 0, 0), dot(dv2, source, 0, 0)
    source_grad = (dot(dk2, xk, 1, 0) + dot(dv2, xv, 1, 0)) * width_mask / depth_f
    memory_grad = chosen[:, None, None] * source_grad[None]
    rows_b, gain_b, shift_b = norm_backward(h1, norm_gain[1], width_mask, width_f, dot(dq2, xq, 1, 0))
    dh1 = dh2 + rows_b
    e1 = (dh1 * keep).astype(BF16)
    wo_grad = dot(c1, e1, 0, 0)
    dc1 = (dot(e1, wo, 1, 1) * head_mask).astype(BF16)
    dq1, dk1, dv1 = attend_backward(q1, k1, v1, causal, t1, split(dc1))
    dq1, dk1, dv1 = (joined(x).astype(BF16) for x in (dq1, dk1, dv1))
    wq_grad, wk_grad, wv_grad = dot(dq1, a1, 0, 0), dot(dk1, a1, 0, 0), dot(dv1, a1, 0, 0)
    rows_a, gain_a, shift_a = norm_backward(
        rows, norm_gain[0], width_mask, width_f, dot(dq1, wq, 1, 0) + dot(dk1, wk, 1, 0) + dot(dv1, wv, 1, 0)
    )
    input_grad = dh1 + rows_a

    def packed(*grads):
        return jnp.concatenate([g.reshape(tp, local, model) for g in grads], axis=1)

    small = jnp.zeros((16, units_local), F32)
    small = small.at[:3, :model].set(jnp.stack([gain_a, gain_b, gain_c]))
    small = small.at[3:6, :model].set(jnp.stack([shift_a, shift_b, shift_c]))
    small = small.at[6, :model].set(bias_out_grad)
    small = small.at[7].set(jnp.sum(own_lengths).astype(F32))
    small = small.at[8:8 + tp].set(bias_in_grad.reshape(tp, units_local))
    *grads, small = reduce_gradients(
        (
            packed(wq_grad, wk_grad, wv_grad, wo_grad).astype(BF16),
            packed(xq_grad, xk_grad, xv_grad, xo_grad).astype(BF16),
            up_grad.reshape(model, tp, units_local).transpose(1, 0, 2).astype(BF16),
            down_grad.reshape(tp, units_local, model).astype(BF16),
        ),
        small,
    )
    inverse = 1.0 / small[7, 0]
    small = small * inverse
    gains, shifts, bias_out_grad = small[:3, :model], small[3:6, :model], small[6, :model]
    bias_in_grad = lax.dynamic_slice_in_dim(small, 8 + place_tp, 1)[0]
    first_grad, second_grad, third_grad, fourth_grad = (x.astype(F32) * inverse for x in grads)
    return (
        layer_out,
        input_grad,
        memory_grad,
        gains,
        shifts,
        first_grad[:3 * local].reshape(3, local, model).transpose(2, 0, 1),
        first_grad[3 * local:],
        second_grad[:local].T,
        second_grad[local:3 * local].reshape(2, local, model).transpose(2, 0, 1),
        second_grad[3 * local:],
        third_grad,
        bias_in_grad,
        fourth_grad,
        bias_out_grad,
    )


def solution(mesh):
    rows = P(("grp", "dp", "tp"), None)
    stack = P(None, ("grp", "dp", "tp"), None)
    weights = (
        P(None, None, "tp"), P("tp", None), P(None, "tp"), P(None, None, "tp"), P("tp", None),
        P(None, "tp"), P("tp"), P("tp", None), P(),
    )
    return jax.shard_map(
        per_device,
        mesh=mesh,
        in_specs=(rows, stack, rows, P(("grp", "dp")), P(("grp", "dp")), P("grp", None), P(), P()) + weights,
        out_specs=(rows, rows, stack, P(), P()) + weights,
        check_vma=False,
    )
```

```python
import functools

import jax
import jax.numpy as jnp
from jax import lax
from jax.experimental import pallas as pl
from jax.experimental.pallas import tpu as pltpu
from jax.sharding import PartitionSpec as P

HD = 80
LEN = 256
EPSILON = 1e-05
NEGATIVE = -1e30
SCALE = HD ** (-0.5)
F32 = jnp.float32
BF16 = jnp.bfloat16


def dot(left, right, left_axis, right_axis):
    return lax.dot_general(
        left, right, (((left_axis,), (right_axis,)), ((), ())), preferred_element_type=F32
    )


def norm_parts(rows, mask, width):
    mean = jnp.sum(rows * mask, axis=-1, keepdims=True) / width
    centred = (rows - mean) * mask
    rstd = lax.rsqrt(jnp.sum(centred * centred, axis=-1, keepdims=True) / width + EPSILON)
    return centred * rstd, rstd


def norm_forward(rows, gain, shift, mask, width):
    hat, _ = norm_parts(rows, mask, width)
    return (hat * gain + shift) * mask


def norm_backward(rows, gain, mask, width, upstream):
    hat, rstd = norm_parts(rows, mask, width)
    upstream = upstream * mask
    gain_term = jnp.sum(upstream * hat, axis=0)
    shift_term = jnp.sum(upstream, axis=0)
    scaled = upstream * gain
    first = jnp.sum(scaled, axis=-1, keepdims=True) / width
    second = jnp.sum(scaled * hat, axis=-1, keepdims=True) / width
    return (rstd * (scaled - first - hat * second)) * mask, gain_term, shift_term


def scores_of(query, keys, allowed):
    raw = jnp.einsum("bqhc,bkhc->bhqk", query, keys, preferred_element_type=F32) * SCALE
    return jnp.where(allowed[:, None], raw, NEGATIVE)


def attend_forward(query, keys, values, allowed):
    scores = scores_of(query, keys, allowed)
    highest = jnp.max(scores, axis=-1, keepdims=True)
    log_total = highest + jnp.log(jnp.sum(jnp.exp(scores - highest), axis=-1, keepdims=True))
    weights = jnp.exp(scores - log_total).astype(BF16)
    context = jnp.einsum("bhqk,bkhc->bqhc", weights, values, preferred_element_type=F32)
    return context, log_total


def attend_backward(query, keys, values, allowed, log_total, upstream):
    weights = jnp.exp(scores_of(query, keys, allowed) - log_total)
    low = weights.astype(BF16)
    value_grad = jnp.einsum("bhqk,bqhc->bkhc", low, upstream, preferred_element_type=F32)
    weight_grad = jnp.einsum("bqhc,bkhc->bhqk", upstream, values, preferred_element_type=F32)
    score_grad = weights * (weight_grad - jnp.sum(weight_grad * weights, axis=-1, keepdims=True))
    score_low = score_grad.astype(BF16)
    query_grad = jnp.einsum("bhqk,bkhc->bqhc", score_low, keys, preferred_element_type=F32) * SCALE
    key_grad = jnp.einsum("bhqk,bqhc->bkhc", score_low, query, preferred_element_type=F32) * SCALE
    return query_grad, key_grad, value_grad


MESH = pl.DeviceIdType.MESH


class Place:
    def __init__(self):
        self.tps = lax.axis_size("tp")
        self.extra = lax.axis_size("dp") // 2
        assert lax.axis_size("grp") == 4 and lax.axis_size("dp") % 2 == 0
        grp, dp, tp = (lax.axis_index(name) for name in ("grp", "dp", "tp"))
        core, low, high = dp % 2, grp % 2, grp // 2
        flip_low, flip_high = grp + 1 - 2 * low, grp + 2 - 4 * high
        self.grp, self.dp, self.tp, self.core = grp, dp, tp, core
        self.first_bit = (1 - core) * low + core * high
        self.second_bit = (1 - core) * high + core * low
        self.first = ((1 - core) * flip_low + core * flip_high, dp, tp)
        self.second = ((1 - core) * flip_high + core * flip_low, dp, tp)
        self.sibling = (grp, dp + 1 - 2 * core, tp)
        self.above = (grp, dp, tp + 1)
        self.below = (grp, dp, tp - 1)
        self.has_above = tp < self.tps - 1
        self.has_below = tp > 0

    def copy_of(self, step):
        return (self.grp, ((self.dp // 2 + step) % self.extra) * 2 + self.core, self.tp)

    def nth_block(self, k):
        size = self.tps
        upper = (2 * self.tp) // size
        lead = (1 - upper) * self.tp + upper * (size - 1 - self.tp)
        spot = k + (k + size - lead) // size
        return (1 - upper) * spot + upper * (size - 1 - spot)

    def barrier(self):
        sem = pltpu.get_barrier_semaphore()
        fixed = [self.first, self.second, self.sibling] + [self.copy_of(s) for s in range(1, self.extra)]
        for device in fixed:
            pl.semaphore_signal(sem, inc=1, device_id=device, device_id_type=MESH)
        for there, device in ((self.has_above, self.above), (self.has_below, self.below)):

            @pl.when(there)
            def _():
                pl.semaphore_signal(sem, inc=1, device_id=device, device_id_type=MESH)

        size = self.tps
        ends = (self.tp + size - 1) // size + (2 * size - 2 - self.tp) // size
        pl.semaphore_wait(sem, len(fixed) + ends)


def push(src, dst, send_sem, recv_sem, device):
    return pltpu.make_async_remote_copy(
        src_ref=src, dst_ref=dst, send_sem=send_sem, recv_sem=recv_sem, device_id=device, device_id_type=MESH
    )


def rows_of(ref, lead, start, count):
    return ref.at[lead, pl.ds(pl.multiple_of(start, 16), count)]


class Spread:
    KINDS = 14

    def __init__(self, place, view, unit, sems):
        self.place, self.view, self.unit, self.sems = place, view, unit, sems
        f, s, c = place.first_bit, place.second_bit, place.core
        self.units = (f * 2 + s, f * 2 + 1 - s, (1 - f) * 2 + s, (1 - f) * 2 + 1 - s)
        self.theirs = (s * 2 + f, s * 2 + 1 - f, (1 - s) * 2 + f, (1 - s) * 2 + 1 - f)
        self.table = [
            (place.second, (c, self.units[0]), (c, self.units[1])),
            (place.first, (c, self.units[0]), (c, self.units[2])),
            (place.first, (c, self.units[1]), (c, self.units[3])),
        ] + [(place.sibling, (c, u), (1 - c, t)) for u, t in zip(self.units, self.theirs)]

    def region(self, spot):
        half, unit = spot
        return self.view((half * 4 + unit) * self.unit, self.unit)

    def own(self):
        return self.region((self.place.core, self.units[0]))

    def copy(self, n, lands=False):
        device, leaves, landing = self.table[n]
        part = self.region(landing if lands else leaves)
        return push(part, part, self.sems(2 * n), self.sems(2 * n + 1), device)

    WAITS = ((), (0,), (1, 2), (3, 4, 5, 6))
    SENDS = ((0, 1, 3), (2, 4), (5, 6), ())

    def step(self, stage):
        for n in self.WAITS[stage]:
            self.copy(n, lands=True).wait_recv()
        for n in self.SENDS[stage]:
            self.copy(n).start()

    def finish(self):
        for n in range(7):
            self.copy(n).wait_send()


class Gather:
    KINDS = Spread.KINDS + 3

    def __init__(self, place, buffers, sems):
        self.place, self.buffers, self.sems = place, buffers, sems
        self.unit = [ref.shape[1] // 8 for ref in buffers]
        self.others = place.tps - 1

    def spread(self, g, j):
        return Spread(
            self.place,
            lambda start, count: rows_of(self.buffers[g], j, start, count),
            self.unit[g],
            lambda kind: self.sems.at[kind, g, j],
        )

    def relays(self, g, j):
        p = self.place
        part = self.spread(g, j).own()
        sem = lambda n: self.sems.at[Spread.KINDS + n, g, j]
        return (
            (jnp.logical_and(j <= p.tp, p.has_above), push(part, part, sem(0), sem(2), p.above)),
            (jnp.logical_and(j >= p.tp, p.has_below), push(part, part, sem(1), sem(2), p.below)),
        )

    def start(self, g):
        for needed, copy in self.relays(g, self.place.tp):
            pl.when(needed)(copy.start)

    def step(self, g, k, stage):
        j = self.place.nth_block(k)
        if stage == 0:
            relays = self.relays(g, j)
            relays[0][1].wait_recv()
            for needed, copy in relays:
                pl.when(needed)(copy.start)
        self.spread(g, j).step(stage)

    def finish(self, g):
        def drain(j):
            for needed, copy in self.relays(g, j):
                pl.when(needed)(copy.wait_send)

        drain(self.place.tp)
        for k in range(self.others):
            j = self.place.nth_block(k)
            drain(j)
            self.spread(g, j).finish()


def gather_kernel(*refs):
    sources, outs, buffers, sems, local, out_sems = refs[:7], refs[7:11], refs[11:15], *refs[15:]
    place = Place()
    columns = sources[1].shape[0]
    mine = place.tp
    pieces = (
        ((0, 3 * columns), (3 * columns, columns)),
        ((0, columns), (columns, 2 * columns), (3 * columns, columns)),
        ((0, sources[5].shape[0]),),
        ((0, sources[6].shape[0]),),
    )
    fills, n = [], 0
    for g, parts in enumerate(pieces):
        fills.append([])
        for start, size in parts:
            copy = pltpu.make_async_copy(sources[n], buffers[g].at[mine, pl.ds(start, size)], local.at[n])
            copy.start()
            fills[g].append(copy)
            n += 1
    place.barrier()
    gather = Gather(place, buffers, sems)

    def store(g, j):
        return pltpu.make_async_copy(buffers[g].at[j], outs[g].at[j], out_sems.at[g, j])

    for g in range(4):
        for copy in fills[g]:
            copy.wait()
        gather.start(g)
        store(g, mine).start()
    events = [(g, k) for g in range(4) for k in range(gather.others)]
    for tick in range(len(events) + 3):
        for stage in range(4):
            if 0 <= tick - stage < len(events):
                g, k = events[tick - stage]
                gather.step(g, k, stage)
                if stage == 3:
                    store(g, place.nth_block(k)).start()
    for g in range(4):
        gather.finish(g)
        for j in range(place.tps):
            store(g, j).wait()


def gather_weights(sources):
    tp = lax.axis_size("tp")
    columns, model = sources[1].shape
    shapes = [(tp, 4 * columns, model)] * 2 + [(tp,) + sources[5].shape, (tp,) + sources[6].shape]
    return pl.pallas_call(
        gather_kernel,
        out_shape=[jax.ShapeDtypeStruct(shape, BF16) for shape in shapes],
        in_specs=[pl.BlockSpec(memory_space=pl.ANY)] * 7,
        out_specs=[pl.BlockSpec(memory_space=pl.ANY)] * 4,
        scratch_shapes=[pltpu.VMEM(shape, BF16) for shape in shapes] + [
            pltpu.SemaphoreType.DMA((Gather.KINDS, 4, tp)),
            pltpu.SemaphoreType.DMA((7,)),
            pltpu.SemaphoreType.DMA((4, tp)),
        ],
        compiler_params=pltpu.CompilerParams(collective_id=1, has_side_effects=True, vmem_limit_bytes=60 * 2**20),
        name="gather_weights",
    )(*sources)


class Reduce:
    KINDS = 14 + 4 + Spread.KINDS + 2

    def __init__(self, place, grads, halves, firsts, seconds, lines, extras, totals, sems):
        self.place, self.grads, self.totals, self.sems = place, grads, totals, sems
        self.halves, self.firsts, self.seconds, self.lines, self.extras = halves, firsts, seconds, lines, extras
        self.unit = [ref.shape[1] // 8 for ref in grads]

    def sem(self, kind, g, j):
        return self.sems.at[kind, g, j]

    def span(self, g, stage, kept):
        p, unit = self.place, self.unit[g]
        if stage == 0:
            return (p.core if kept else 1 - p.core) * 4 * unit, 4
        if stage == 1:
            return (p.core * 4 + (p.first_bit if kept else 1 - p.first_bit) * 2) * unit, 2
        bit = p.second_bit if kept else 1 - p.second_bit
        return (p.core * 4 + p.first_bit * 2 + bit) * unit, 1

    def region(self, g, j, stage, kept):
        start, units = self.span(g, stage, kept)
        return rows_of(self.grads[g], j, start, units * self.unit[g])

    def landing(self, g, j, stage):
        return (self.halves, self.firsts, self.seconds)[stage][g].at[j]

    def copies_of(self, g, j, stage):
        device = (self.place.sibling, self.place.first, self.place.second)[stage]
        start, units = self.span(g, stage, False)
        unit, base = self.unit[g], (0, 8, 12)[stage]
        return [
            push(
                rows_of(self.grads[g], j, start + u * unit, unit),
                self.landing(g, j, stage).at[pl.ds(u * unit, unit)],
                self.sem(base + 2 * u, g, j), self.sem(base + 2 * u + 1, g, j), device,
            )
            for u in range(units)
        ]

    def step(self, g, j, stage):
        if stage > 0:
            for copy in self.copies_of(g, j, stage - 1):
                copy.wait_recv()
            kept = self.region(g, j, stage - 1, True)
            kept[...] = kept[...] + self.landing(g, j, stage - 1)[...]
        if stage < 3:
            for copy in self.copies_of(g, j, stage):
                copy.start()

    def piece(self, g, j):
        return self.region(g, j, 2, True)

    def hop(self, g, j, upward):
        p = self.place
        way = 0 if upward else 1
        return push(
            self.piece(g, j), self.lines[g].at[way, j],
            self.sem(14 + 2 * way, g, j), self.sem(15 + 2 * way, g, j), p.above if upward else p.below,
        )

    def travel(self, g, k):
        p = self.place
        for upward in (True, False):
            j = p.tps - 1 - k if upward else k
            has_source = p.has_below if upward else p.has_above
            involved = j >= p.tp if upward else j <= p.tp
            passes = j > p.tp if upward else j < p.tp

            @pl.when(jnp.logical_and(involved, has_source))
            def _():
                self.hop(g, j, upward).wait_recv()
                kept = self.piece(g, j)
                kept[...] = kept[...] + self.lines[g][0 if upward else 1, j]

            pl.when(passes)(self.hop(g, j, upward).start)

    def copies(self, g, step):
        p = self.place
        return push(
            self.piece(g, p.tp), self.extras[g].at[step], self.sem(self.KINDS - 2, g, step), self.sem(self.KINDS - 1, g, step), p.copy_of(step)
        )

    def among_copies(self, g):
        p = self.place
        if p.extra > 1:
            for step in range(1, p.extra):
                self.copies(g, step).start()
            total = self.piece(g, p.tp)[...].astype(F32)
            for step in range(1, p.extra):
                self.copies(g, step).wait()
                total = total + self.extras[g][step].astype(F32)
            self.piece(g, p.tp)[...] = total.astype(BF16)

    def spread(self, g):
        return Spread(
            self.place,
            lambda start, count: self.totals[g].at[pl.ds(pl.multiple_of(start, 16), count)],
            self.unit[g],
            lambda kind: self.sems.at[18 + kind, g, 0],
        )

    def settle(self, g):
        self.among_copies(g)
        self.spread(g).own()[...] = self.piece(g, self.place.tp)[...]
        self.spread(g).step(0)

    def share(self, g, stage):
        self.spread(g).step(stage)

    def finish(self, g):
        p = self.place
        for j in range(p.tps):
            for stage in range(3):
                for copy in self.copies_of(g, j, stage):
                    copy.wait_send()
            pl.when(j > p.tp)(self.hop(g, j, True).wait_send)
            pl.when(j < p.tp)(self.hop(g, j, False).wait_send)
        self.spread(g).finish()


class SumSmall:
    SLOTS = 12

    def __init__(self, place, slots, sems):
        self.place, self.slots, self.sems = place, slots, sems

    def move(self, source, device):
        return push(
            self.slots.at[source], self.slots.at[source + 1], self.sems.at[source], self.sems.at[source + 1], device
        )

    def pair(self, stage):
        p = self.place
        return self.move(2 * stage, (p.sibling, p.first, p.second)[stage])

    def start(self, value):
        p = self.place
        for there, slot in ((p.has_below, 7), (p.has_above, 9)):

            @pl.when(jnp.logical_not(there))
            def _():
                self.slots[slot] = jnp.zeros_like(value)

        self.slots[0] = value
        self.pair(0).start()

    def exchange(self, stage):
        self.pair(stage).wait_recv()
        value = self.slots[2 * stage] + self.slots[2 * stage + 1]
        if stage < 2:
            self.slots[2 * stage + 2] = value
            self.pair(stage + 1).start()
        else:
            self.slots[10] = value

    def among_copies(self):
        p = self.place
        base = self.SLOTS
        for step in range(1, p.extra):
            self.copies(step).start()
        for step in range(1, p.extra):
            self.copies(step).wait()
        if p.extra > 1:
            total = self.slots[10]
            for step in range(1, p.extra):
                total = total + self.slots[base + step]
            self.slots[11] = total
        else:
            self.slots[11] = self.slots[10]

    def copies(self, step):
        base = self.SLOTS
        return push(
            self.slots.at[10], self.slots.at[base + step],
            self.sems.at[base + 2 * step], self.sems.at[base + 2 * step + 1], self.place.copy_of(step),
        )

    def line(self, upward):
        p = self.place
        source, target = (p.has_below, p.has_above) if upward else (p.has_above, p.has_below)
        slot = 6 if upward else 8
        pl.when(source)(self.move(slot, p.above if upward else p.below).wait_recv)

        @pl.when(target)
        def _():
            self.slots[slot] = self.slots[slot + 1] + self.slots[11]
            self.move(slot, p.above if upward else p.below).start()

    def total(self):
        return self.slots[11] + self.slots[7] + self.slots[9]

    def finish(self):
        p = self.place
        for stage in range(3):
            self.pair(stage).wait_send()
        pl.when(p.has_above)(self.move(6, p.above).wait_send)
        pl.when(p.has_below)(self.move(8, p.below).wait_send)


def run_plan(plan):
    for _, _, step in sorted(plan, key=lambda entry: entry[:2]):
        step()


def reduce_kernel(*refs):
    sources, small_in = refs[:4], refs[4]
    outs, small_out = refs[5:9], refs[9]
    grads, halves, firsts, seconds, lines, extras, totals = (refs[10 + 4 * i:14 + 4 * i] for i in range(7))
    slots, sems, small_sems, local = refs[38:]
    place = Place()
    loads = {}
    for g in (3, 2, 1, 0):
        for j in range(place.tps):
            loads[g, j] = pltpu.make_async_copy(sources[g].at[j], grads[g].at[j], local.at[g, j])
            loads[g, j].start()
    place.barrier()
    reduce = Reduce(place, grads, halves, firsts, seconds, lines, extras, totals, sems)
    small = SumSmall(place, slots, small_sems)
    plan = []

    def add(tick, order, step, *args):
        plan.append((tick, order, functools.partial(step, *args)))

    def begin(g, j):
        loads[g, j].wait()
        reduce.step(g, j, 0)

    n = place.tps
    stores = {}

    def store(g):
        stores[g] = pltpu.make_async_copy(totals[g], outs[g], local.at[g, n])
        stores[g].start()

    for i, g in enumerate((3, 2, 1, 0)):
        for j in range(n):
            e = i * n + j
            add(e, 0, begin, g, j)
            for stage in (1, 2, 3):
                add(e + stage, 90 - 10 * i - stage, reduce.step, g, j, stage)
        last = i * n + n + 2
        for k in range(n - 1):
            add(last + k, 99 - 10 * i - 4, reduce.travel, g, k)
        add(last + n - 1, 99 - 10 * i - 5, reduce.settle, g)
        for stage in (1, 2, 3):
            add(last + n - 1 + stage, 99 - 10 * i - 5 - stage, reduce.share, g, stage)
        add(last + n + 2, 99, store, g)
    add(0, 1, lambda: small.start(small_in[...]))
    for stage in range(3):
        add(stage + 1, 98, small.exchange, stage)
    add(4, 98, small.among_copies)
    add(5, 98, small.line, True)
    add(5, 98, small.line, False)
    run_plan(plan)
    small_out[...] = small.total()
    for g in range(4):
        reduce.finish(g)
        stores[g].wait()
    small.finish()


def reduce_gradients(grads, small):
    n, extra = lax.axis_size("tp"), lax.axis_size("dp") // 2
    shapes = [g.shape for g in grads]
    vm = lambda parts, dtype=BF16: [pltpu.VMEM(shape, dtype) for shape in parts]
    scratch = (
        vm(shapes)
        + vm((n, r // 2, c) for _, r, c in shapes)
        + vm((n, r // 4, c) for _, r, c in shapes)
        + vm((n, r // 8, c) for _, r, c in shapes)
        + vm((2, n, r // 8, c) for _, r, c in shapes)
        + vm((extra, r // 8, c) for _, r, c in shapes)
        + vm((r, c) for _, r, c in shapes)
        + vm([(SumSmall.SLOTS + extra,) + small.shape], F32)
        + [
            pltpu.SemaphoreType.DMA((Reduce.KINDS, 4, max(n, extra))),
            pltpu.SemaphoreType.DMA((SumSmall.SLOTS + 2 * extra,)),
            pltpu.SemaphoreType.DMA((4, n + 1)),
        ]
    )
    return pl.pallas_call(
        reduce_kernel,
        out_shape=[jax.ShapeDtypeStruct((r, c), BF16) for _, r, c in shapes] + [jax.ShapeDtypeStruct(small.shape, F32)],
        in_specs=[pl.BlockSpec(memory_space=pl.ANY)] * 4 + [pl.BlockSpec(memory_space=pltpu.VMEM)],
        out_specs=[pl.BlockSpec(memory_space=pl.ANY)] * 4 + [pl.BlockSpec(memory_space=pltpu.VMEM)],
        scratch_shapes=scratch,
        compiler_params=pltpu.CompilerParams(collective_id=2, has_side_effects=True, vmem_limit_bytes=60 * 2**20),
        name="reduce_gradients",
    )(*grads, small)


def per_device(
    inputs, memory, out_grad, lengths, src_lengths, configs, norm_gain, norm_bias,
    self_qkv, self_out, cross_q, cross_kv, cross_out, ffn_in, ffn_in_bias, ffn_out, ffn_out_bias,
):
    owned, model = inputs.shape
    layers = memory.shape[0]
    tp = lax.axis_size("tp")
    place_tp = lax.axis_index("tp")
    sentences = owned // LEN
    local = self_out.shape[0]
    pair = local // HD
    units_local = ffn_in.shape[1]
    width, heads, units, depth = (configs[0, i] for i in range(4))
    width_f = width.astype(F32)
    depth_f = depth.astype(F32)
    width_mask = (jnp.arange(model) < width).astype(F32)
    head_mask = (jnp.arange(tp * local) < heads * HD).astype(F32)
    unit_mask = (jnp.arange(tp * units_local) < units).astype(F32)
    place = jnp.arange(LEN)
    own_lengths = lax.dynamic_slice_in_dim(lengths, place_tp * sentences, sentences)
    own_source = lax.dynamic_slice_in_dim(src_lengths, place_tp * sentences, sentences)
    valid = (place[None, :] < own_lengths[:, None]).astype(F32).reshape(owned, 1)
    keep = width_mask * valid
    causal = jnp.broadcast_to(place[:, None] >= place[None, :], (sentences, LEN, LEN))
    crossing = jnp.broadcast_to(place[None, None, :] < own_source[:, None, None], (sentences, LEN, LEN))

    first, second, third, fourth = gather_weights(
        (
            self_qkv.transpose(1, 2, 0).reshape(3 * local, model),
            self_out,
            cross_q.T,
            cross_kv.transpose(1, 2, 0).reshape(2 * local, model),
            cross_out,
            ffn_in,
            ffn_out,
        )
    )
    bias_in = lax.all_gather(ffn_in_bias, "tp", axis=0, tiled=True)

    def part(block, start):
        return block[:, start * local:(start + 1) * local].reshape(tp * local, model)

    def split(flat):
        return flat.astype(BF16).reshape(sentences, LEN, tp * pair, HD)

    def joined(shaped):
        return shaped.reshape(owned, tp * local)

    wq, wk, wv, wo = (part(first, i) for i in range(4))
    xq, xk, xv, xo = (part(second, i) for i in range(4))
    w_up = third.transpose(1, 0, 2).reshape(model, tp * units_local)
    w_down = fourth.reshape(tp * units_local, model)

    rows = inputs.astype(F32)
    a1 = norm_forward(rows, norm_gain[0], norm_bias[0], width_mask, width_f).astype(BF16)
    q1, k1, v1 = split(dot(a1, wq, 1, 1)), split(dot(a1, wk, 1, 1)), split(dot(a1, wv, 1, 1))
    c1, t1 = attend_forward(q1, k1, v1, causal)
    c1 = (joined(c1) * head_mask).astype(BF16)
    h1 = rows + dot(c1, wo, 1, 0) * keep
    a2 = norm_forward(h1, norm_gain[1], norm_bias[1], width_mask, width_f).astype(BF16)
    chosen = (jnp.arange(layers) >= layers - depth).astype(F32)
    mixed = chosen[0] * memory[0].astype(F32)
    for level in range(1, layers):
        mixed = mixed + chosen[level] * memory[level].astype(F32)
    source = (mixed / depth_f * width_mask).astype(BF16)
    q2, k2, v2 = split(dot(a2, xq, 1, 1)), split(dot(source, xk, 1, 1)), split(dot(source, xv, 1, 1))
    c2, t2 = attend_forward(q2, k2, v2, crossing)
    c2 = (joined(c2) * head_mask).astype(BF16)
    h2 = h1 + dot(c2, xo, 1, 0) * keep
    a3 = norm_forward(h2, norm_gain[2], norm_bias[2], width_mask, width_f).astype(BF16)
    before = dot(a3, w_up, 1, 0) + bias_in

    def activate(values):
        return jax.nn.gelu(values, approximate=True) * unit_mask

    hidden, gelu_back = jax.vjp(activate, before)
    hidden = hidden.astype(BF16)
    layer_out = h2 + (dot(hidden, w_down, 1, 0) + ffn_out_bias) * keep

    upstream = out_grad.astype(F32)
    masked = upstream * keep
    bias_out_grad = jnp.sum(masked, axis=0)
    e3 = masked.astype(BF16)
    down_grad = dot(hidden, e3, 0, 0)
    du = gelu_back(dot(e3, w_down, 1, 1))[0].astype(BF16)
    up_grad = dot(a3, du, 0, 0)
    bias_in_grad = jnp.sum(du.astype(F32), axis=0)
    rows_c, gain_c, shift_c = norm_backward(h2, norm_gain[2], width_mask, width_f, dot(du, w_up, 1, 1))
    dh2 = upstream + rows_c
    e2 = (dh2 * keep).astype(BF16)
    xo_grad = dot(c2, e2, 0, 0)
    dc2 = (dot(e2, xo, 1, 1) * head_mask).astype(BF16)
    dq2, dk2, dv2 = attend_backward(q2, k2, v2, crossing, t2, split(dc2))
    dq2, dk2, dv2 = (joined(x).astype(BF16) for x in (dq2, dk2, dv2))
    xq_grad, xk_grad, xv_grad = dot(dq2, a2, 0, 0), dot(dk2, source, 0, 0), dot(dv2, source, 0, 0)
    source_grad = (dot(dk2, xk, 1, 0) + dot(dv2, xv, 1, 0)) * width_mask / depth_f
    memory_grad = chosen[:, None, None] * source_grad[None]
    rows_b, gain_b, shift_b = norm_backward(h1, norm_gain[1], width_mask, width_f, dot(dq2, xq, 1, 0))
    dh1 = dh2 + rows_b
    e1 = (dh1 * keep).astype(BF16)
    wo_grad = dot(c1, e1, 0, 0)
    dc1 = (dot(e1, wo, 1, 1) * head_mask).astype(BF16)
    dq1, dk1, dv1 = attend_backward(q1, k1, v1, causal, t1, split(dc1))
    dq1, dk1, dv1 = (joined(x).astype(BF16) for x in (dq1, dk1, dv1))
    wq_grad, wk_grad, wv_grad = dot(dq1, a1, 0, 0), dot(dk1, a1, 0, 0), dot(dv1, a1, 0, 0)
    rows_a, gain_a, shift_a = norm_backward(
        rows, norm_gain[0], width_mask, width_f, dot(dq1, wq, 1, 0) + dot(dk1, wk, 1, 0) + dot(dv1, wv, 1, 0)
    )
    input_grad = dh1 + rows_a

    def packed(*grads):
        return jnp.concatenate([g.reshape(tp, local, model) for g in grads], axis=1)

    small = jnp.zeros((16, units_local), F32)
    small = small.at[:3, :model].set(jnp.stack([gain_a, gain_b, gain_c]))
    small = small.at[3:6, :model].set(jnp.stack([shift_a, shift_b, shift_c]))
    small = small.at[6, :model].set(bias_out_grad)
    small = small.at[7].set(jnp.sum(own_lengths).astype(F32))
    small = small.at[8:8 + tp].set(bias_in_grad.reshape(tp, units_local))
    *grads, small = reduce_gradients(
        (
            packed(wq_grad, wk_grad, wv_grad, wo_grad).astype(BF16),
            packed(xq_grad, xk_grad, xv_grad, xo_grad).astype(BF16),
            up_grad.reshape(model, tp, units_local).transpose(1, 0, 2).astype(BF16),
            down_grad.reshape(tp, units_local, model).astype(BF16),
        ),
        small,
    )
    inverse = 1.0 / small[7, 0]
    small = small * inverse
    gains, shifts, bias_out_grad = small[:3, :model], small[3:6, :model], small[6, :model]
    bias_in_grad = lax.dynamic_slice_in_dim(small, 8 + place_tp, 1)[0]
    first_grad, second_grad, third_grad, fourth_grad = (x.astype(F32) * inverse for x in grads)
    return (
        layer_out,
        input_grad,
        memory_grad,
        gains,
        shifts,
        first_grad[:3 * local].reshape(3, local, model).transpose(2, 0, 1),
        first_grad[3 * local:],
        second_grad[:local].T,
        second_grad[local:3 * local].reshape(2, local, model).transpose(2, 0, 1),
        second_grad[3 * local:],
        third_grad,
        bias_in_grad,
        fourth_grad,
        bias_out_grad,
    )


def solution(mesh):
    rows = P(("grp", "dp", "tp"), None)
    stack = P(None, ("grp", "dp", "tp"), None)
    weights = (
        P(None, None, "tp"), P("tp", None), P(None, "tp"), P(None, None, "tp"), P("tp", None),
        P(None, "tp"), P("tp"), P("tp", None), P(),
    )
    return jax.shard_map(
        per_device,
        mesh=mesh,
        in_specs=(rows, stack, rows, P(("grp", "dp")), P(("grp", "dp")), P("grp", None), P(), P()) + weights,
        out_specs=(rows, rows, stack, P(), P()) + weights,
        check_vma=False,
    )
```

```python
import functools

import jax
import jax.numpy as jnp
from jax import lax
from jax.experimental import pallas as pl
from jax.experimental.pallas import tpu as pltpu
from jax.sharding import PartitionSpec as P

HD = 80
LEN = 256
EPSILON = 1e-05
NEGATIVE = -1e30
SCALE = HD ** (-0.5)
F32 = jnp.float32
BF16 = jnp.bfloat16


def dot(left, right, left_axis, right_axis):
    return lax.dot_general(
        left, right, (((left_axis,), (right_axis,)), ((), ())), preferred_element_type=F32
    )


def norm_parts(rows, mask, width):
    mean = jnp.sum(rows * mask, axis=-1, keepdims=True) / width
    centred = (rows - mean) * mask
    rstd = lax.rsqrt(jnp.sum(centred * centred, axis=-1, keepdims=True) / width + EPSILON)
    return centred * rstd, rstd


def norm_forward(rows, gain, shift, mask, width):
    hat, _ = norm_parts(rows, mask, width)
    return (hat * gain + shift) * mask


def norm_backward(rows, gain, mask, width, upstream):
    hat, rstd = norm_parts(rows, mask, width)
    upstream = upstream * mask
    gain_term = jnp.sum(upstream * hat, axis=0)
    shift_term = jnp.sum(upstream, axis=0)
    scaled = upstream * gain
    first = jnp.sum(scaled, axis=-1, keepdims=True) / width
    second = jnp.sum(scaled * hat, axis=-1, keepdims=True) / width
    return (rstd * (scaled - first - hat * second)) * mask, gain_term, shift_term


def scores_of(query, keys, allowed):
    raw = jnp.einsum("bqhc,bkhc->bhqk", query, keys, preferred_element_type=F32) * SCALE
    return jnp.where(allowed[:, None], raw, NEGATIVE)


def attend_forward(query, keys, values, allowed):
    scores = scores_of(query, keys, allowed)
    highest = jnp.max(scores, axis=-1, keepdims=True)
    log_total = highest + jnp.log(jnp.sum(jnp.exp(scores - highest), axis=-1, keepdims=True))
    weights = jnp.exp(scores - log_total).astype(BF16)
    context = jnp.einsum("bhqk,bkhc->bqhc", weights, values, preferred_element_type=F32)
    return context, log_total


def attend_backward(query, keys, values, allowed, log_total, upstream):
    weights = jnp.exp(scores_of(query, keys, allowed) - log_total)
    low = weights.astype(BF16)
    value_grad = jnp.einsum("bhqk,bqhc->bkhc", low, upstream, preferred_element_type=F32)
    weight_grad = jnp.einsum("bqhc,bkhc->bhqk", upstream, values, preferred_element_type=F32)
    score_grad = weights * (weight_grad - jnp.sum(weight_grad * weights, axis=-1, keepdims=True))
    score_low = score_grad.astype(BF16)
    query_grad = jnp.einsum("bhqk,bkhc->bqhc", score_low, keys, preferred_element_type=F32) * SCALE
    key_grad = jnp.einsum("bhqk,bqhc->bkhc", score_low, query, preferred_element_type=F32) * SCALE
    return query_grad, key_grad, value_grad


MESH = pl.DeviceIdType.MESH


class Place:
    def __init__(self):
        self.tps = lax.axis_size("tp")
        self.extra = lax.axis_size("dp") // 2
        assert lax.axis_size("grp") == 4 and lax.axis_size("dp") % 2 == 0
        grp, dp, tp = (lax.axis_index(name) for name in ("grp", "dp", "tp"))
        core, low, high = dp % 2, grp % 2, grp // 2
        flip_low, flip_high = grp + 1 - 2 * low, grp + 2 - 4 * high
        self.grp, self.dp, self.tp, self.core = grp, dp, tp, core
        self.first_bit = (1 - core) * low + core * high
        self.second_bit = (1 - core) * high + core * low
        self.first = ((1 - core) * flip_low + core * flip_high, dp, tp)
        self.second = ((1 - core) * flip_high + core * flip_low, dp, tp)
        self.sibling = (grp, dp + 1 - 2 * core, tp)
        self.above = (grp, dp, tp + 1)
        self.below = (grp, dp, tp - 1)
        self.has_above = tp < self.tps - 1
        self.has_below = tp > 0

    def copy_of(self, step):
        return (self.grp, ((self.dp // 2 + step) % self.extra) * 2 + self.core, self.tp)

    def nth_block(self, k):
        size = self.tps
        upper = (2 * self.tp) // size
        lead = (1 - upper) * self.tp + upper * (size - 1 - self.tp)
        spot = k + (k + size - lead) // size
        return (1 - upper) * spot + upper * (size - 1 - spot)

    def barrier(self):
        sem = pltpu.get_barrier_semaphore()
        fixed = [self.first, self.second, self.sibling] + [self.copy_of(s) for s in range(1, self.extra)]
        for device in fixed:
            pl.semaphore_signal(sem, inc=1, device_id=device, device_id_type=MESH)
        for there, device in ((self.has_above, self.above), (self.has_below, self.below)):

            @pl.when(there)
            def _():
                pl.semaphore_signal(sem, inc=1, device_id=device, device_id_type=MESH)

        size = self.tps
        ends = (self.tp + size - 1) // size + (2 * size - 2 - self.tp) // size
        pl.semaphore_wait(sem, len(fixed) + ends)


def push(src, dst, send_sem, recv_sem, device):
    return pltpu.make_async_remote_copy(
        src_ref=src, dst_ref=dst, send_sem=send_sem, recv_sem=recv_sem, device_id=device, device_id_type=MESH
    )


def rows_of(ref, lead, start, count):
    return ref.at[lead, pl.ds(pl.multiple_of(start, 16), count)]


def add_into(total, term):
    def step(i, carry):
        rows = pl.ds(pl.multiple_of(i * 16, 16), 16)
        total[rows] = total[rows] + term[rows]
        return carry

    lax.fori_loop(0, total.shape[0] // 16, step, 0)


def copy_into(total, term):

    def step(i, carry):
        rows = pl.ds(pl.multiple_of(i * 16, 16), 16)
        total[rows] = term[rows]
        return carry

    lax.fori_loop(0, total.shape[0] // 16, step, 0)


class Spread:
    KINDS = 14

    def __init__(self, place, view, unit, sems):
        self.place, self.view, self.unit, self.sems = place, view, unit, sems
        f, s, c = place.first_bit, place.second_bit, place.core
        self.units = (f * 2 + s, f * 2 + 1 - s, (1 - f) * 2 + s, (1 - f) * 2 + 1 - s)
        self.theirs = (s * 2 + f, s * 2 + 1 - f, (1 - s) * 2 + f, (1 - s) * 2 + 1 - f)
        self.table = [
            (place.second, (c, self.units[0]), (c, self.units[1])),
            (place.first, (c, self.units[0]), (c, self.units[2])),
            (place.first, (c, self.units[1]), (c, self.units[3])),
        ] + [(place.sibling, (c, u), (1 - c, t)) for u, t in zip(self.units, self.theirs)]

    def region(self, spot):
        half, unit = spot
        return self.view((half * 4 + unit) * self.unit, self.unit)

    def own(self):
        return self.region((self.place.core, self.units[0]))

    def copy(self, n, lands=False):
        device, leaves, landing = self.table[n]
        part = self.region(landing if lands else leaves)
        return push(part, part, self.sems(2 * n), self.sems(2 * n + 1), device)

    WAITS = ((), (0,), (1, 2), (3, 4, 5, 6))
    SENDS = ((0, 1, 3), (2, 4), (5, 6), ())

    def step(self, stage):
        for n in self.WAITS[stage]:
            self.copy(n, lands=True).wait_recv()
        for n in self.SENDS[stage]:
            self.copy(n).start()

    def finish(self):
        for n in range(7):
            self.copy(n).wait_send()


class Gather:
    KINDS = Spread.KINDS + 3

    def __init__(self, place, buffers, sems):
        self.place, self.buffers, self.sems = place, buffers, sems
        self.unit = [ref.shape[1] // 8 for ref in buffers]
        self.others = place.tps - 1

    def spread(self, g, j):
        return Spread(
            self.place,
            lambda start, count: rows_of(self.buffers[g], j, start, count),
            self.unit[g],
            lambda kind: self.sems.at[kind, g, j],
        )

    def relays(self, g, j):
        p = self.place
        part = self.spread(g, j).own()
        sem = lambda n: self.sems.at[Spread.KINDS + n, g, j]
        return (
            (jnp.logical_and(j <= p.tp, p.has_above), push(part, part, sem(0), sem(2), p.above)),
            (jnp.logical_and(j >= p.tp, p.has_below), push(part, part, sem(1), sem(2), p.below)),
        )

    def start(self, g):
        for needed, copy in self.relays(g, self.place.tp):
            pl.when(needed)(copy.start)

    def step(self, g, k, stage):
        j = self.place.nth_block(k)
        if stage == 0:
            relays = self.relays(g, j)
            relays[0][1].wait_recv()
            for needed, copy in relays:
                pl.when(needed)(copy.start)
        self.spread(g, j).step(stage)

    def finish(self, g):
        def drain(j):
            for needed, copy in self.relays(g, j):
                pl.when(needed)(copy.wait_send)

        drain(self.place.tp)
        for k in range(self.others):
            j = self.place.nth_block(k)
            drain(j)
            self.spread(g, j).finish()


def gather_kernel(*refs):
    sources, outs, buffers, sems, local, out_sems = refs[:7], refs[7:11], refs[11:15], *refs[15:]
    place = Place()
    columns = sources[1].shape[0]
    mine = place.tp
    pieces = (
        ((0, 3 * columns), (3 * columns, columns)),
        ((0, columns), (columns, 2 * columns), (3 * columns, columns)),
        ((0, sources[5].shape[0]),),
        ((0, sources[6].shape[0]),),
    )
    fills, n = [], 0
    for g, parts in enumerate(pieces):
        fills.append([])
        for start, size in parts:
            copy = pltpu.make_async_copy(sources[n], buffers[g].at[mine, pl.ds(start, size)], local.at[n])
            copy.start()
            fills[g].append(copy)
            n += 1
    place.barrier()
    gather = Gather(place, buffers, sems)

    def store(g, j):
        return pltpu.make_async_copy(buffers[g].at[j], outs[g].at[j], out_sems.at[g, j])

    for g in range(4):
        for copy in fills[g]:
            copy.wait()
        gather.start(g)
        store(g, mine).start()
    events = [(g, k) for g in range(4) for k in range(gather.others)]
    for tick in range(len(events) + 3):
        for stage in range(4):
            if 0 <= tick - stage < len(events):
                g, k = events[tick - stage]
                gather.step(g, k, stage)
                if stage == 3:
                    store(g, place.nth_block(k)).start()
    for g in range(4):
        gather.finish(g)
        for j in range(place.tps):
            store(g, j).wait()


def gather_weights(sources):
    tp = lax.axis_size("tp")
    columns, model = sources[1].shape
    shapes = [(tp, 4 * columns, model)] * 2 + [(tp,) + sources[5].shape, (tp,) + sources[6].shape]
    return pl.pallas_call(
        gather_kernel,
        out_shape=[jax.ShapeDtypeStruct(shape, BF16) for shape in shapes],
        in_specs=[pl.BlockSpec(memory_space=pl.ANY)] * 7,
        out_specs=[pl.BlockSpec(memory_space=pl.ANY)] * 4,
        scratch_shapes=[pltpu.VMEM(shape, BF16) for shape in shapes] + [
            pltpu.SemaphoreType.DMA((Gather.KINDS, 4, tp)),
            pltpu.SemaphoreType.DMA((7,)),
            pltpu.SemaphoreType.DMA((4, tp)),
        ],
        compiler_params=pltpu.CompilerParams(collective_id=1, has_side_effects=True, vmem_limit_bytes=60 * 2**20),
        name="gather_weights",
    )(*sources)


class Reduce:
    KINDS = 14 + 4 + Spread.KINDS + 2

    def __init__(self, place, grads, halves, firsts, seconds, lines, extras, totals, sems):
        self.place, self.grads, self.totals, self.sems = place, grads, totals, sems
        self.halves, self.firsts, self.seconds, self.lines, self.extras = halves, firsts, seconds, lines, extras
        self.unit = [ref.shape[1] // 8 for ref in grads]

    def sem(self, kind, g, j):
        return self.sems.at[kind, g, j]

    def span(self, g, stage, kept):
        p, unit = self.place, self.unit[g]
        if stage == 0:
            return (p.core if kept else 1 - p.core) * 4 * unit, 4
        if stage == 1:
            return (p.core * 4 + (p.first_bit if kept else 1 - p.first_bit) * 2) * unit, 2
        bit = p.second_bit if kept else 1 - p.second_bit
        return (p.core * 4 + p.first_bit * 2 + bit) * unit, 1

    def region(self, g, j, stage, kept):
        start, units = self.span(g, stage, kept)
        return rows_of(self.grads[g], j, start, units * self.unit[g])

    def landing(self, g, j, stage):
        return (self.halves, self.firsts, self.seconds)[stage][g].at[j]

    def copies_of(self, g, j, stage):
        device = (self.place.sibling, self.place.first, self.place.second)[stage]
        start, units = self.span(g, stage, False)
        unit, base = self.unit[g], (0, 8, 12)[stage]
        return [
            push(
                rows_of(self.grads[g], j, start + u * unit, unit),
                self.landing(g, j, stage).at[pl.ds(u * unit, unit)],
                self.sem(base + 2 * u, g, j), self.sem(base + 2 * u + 1, g, j), device,
            )
            for u in range(units)
        ]

    def step(self, g, j, stage):
        if stage > 0:
            for copy in self.copies_of(g, j, stage - 1):
                copy.wait_recv()
            add_into(self.region(g, j, stage - 1, True), self.landing(g, j, stage - 1))
        if stage < 3:
            for copy in self.copies_of(g, j, stage):
                copy.start()

    def piece(self, g, j):
        return self.region(g, j, 2, True)

    def hop(self, g, j, upward):
        p = self.place
        way = 0 if upward else 1
        return push(
            self.piece(g, j), self.lines[g].at[way, j],
            self.sem(14 + 2 * way, g, j), self.sem(15 + 2 * way, g, j), p.above if upward else p.below,
        )

    def travel(self, g, k):
        p = self.place
        for upward in (True, False):
            j = p.tps - 1 - k if upward else k
            has_source = p.has_below if upward else p.has_above
            involved = j >= p.tp if upward else j <= p.tp
            passes = j > p.tp if upward else j < p.tp

            @pl.when(jnp.logical_and(involved, has_source))
            def _():
                self.hop(g, j, upward).wait_recv()
                add_into(self.piece(g, j), self.lines[g].at[0 if upward else 1, j])

            pl.when(passes)(self.hop(g, j, upward).start)

    def copies(self, g, step):
        p = self.place
        return push(
            self.piece(g, p.tp), self.extras[g].at[step], self.sem(self.KINDS - 2, g, step), self.sem(self.KINDS - 1, g, step), p.copy_of(step)
        )

    def among_copies(self, g):
        p = self.place
        if p.extra > 1:
            for step in range(1, p.extra):
                self.copies(g, step).start()
            total = self.piece(g, p.tp)[...].astype(F32)
            for step in range(1, p.extra):
                self.copies(g, step).wait()
                total = total + self.extras[g][step].astype(F32)
            self.piece(g, p.tp)[...] = total.astype(BF16)

    def spread(self, g):
        return Spread(
            self.place,
            lambda start, count: self.totals[g].at[pl.ds(pl.multiple_of(start, 16), count)],
            self.unit[g],
            lambda kind: self.sems.at[18 + kind, g, 0],
        )

    def settle(self, g):
        self.among_copies(g)
        copy_into(self.spread(g).own(), self.piece(g, self.place.tp))
        self.spread(g).step(0)

    def share(self, g, stage):
        self.spread(g).step(stage)

    def finish(self, g):
        p = self.place
        for j in range(p.tps):
            for stage in range(3):
                for copy in self.copies_of(g, j, stage):
                    copy.wait_send()
            pl.when(j > p.tp)(self.hop(g, j, True).wait_send)
            pl.when(j < p.tp)(self.hop(g, j, False).wait_send)
        self.spread(g).finish()


class SumSmall:
    SLOTS = 12

    def __init__(self, place, slots, sems):
        self.place, self.slots, self.sems = place, slots, sems

    def move(self, source, device):
        return push(
            self.slots.at[source], self.slots.at[source + 1], self.sems.at[source], self.sems.at[source + 1], device
        )

    def pair(self, stage):
        p = self.place
        return self.move(2 * stage, (p.sibling, p.first, p.second)[stage])

    def start(self, value):
        p = self.place
        for there, slot in ((p.has_below, 7), (p.has_above, 9)):

            @pl.when(jnp.logical_not(there))
            def _():
                self.slots[slot] = jnp.zeros_like(value)

        self.slots[0] = value
        self.pair(0).start()

    def exchange(self, stage):
        self.pair(stage).wait_recv()
        value = self.slots[2 * stage] + self.slots[2 * stage + 1]
        if stage < 2:
            self.slots[2 * stage + 2] = value
            self.pair(stage + 1).start()
        else:
            self.slots[10] = value

    def among_copies(self):
        p = self.place
        base = self.SLOTS
        for step in range(1, p.extra):
            self.copies(step).start()
        for step in range(1, p.extra):
            self.copies(step).wait()
        if p.extra > 1:
            total = self.slots[10]
            for step in range(1, p.extra):
                total = total + self.slots[base + step]
            self.slots[11] = total
        else:
            self.slots[11] = self.slots[10]

    def copies(self, step):
        base = self.SLOTS
        return push(
            self.slots.at[10], self.slots.at[base + step],
            self.sems.at[base + 2 * step], self.sems.at[base + 2 * step + 1], self.place.copy_of(step),
        )

    def line(self, upward):
        p = self.place
        source, target = (p.has_below, p.has_above) if upward else (p.has_above, p.has_below)
        slot = 6 if upward else 8
        pl.when(source)(self.move(slot, p.above if upward else p.below).wait_recv)

        @pl.when(target)
        def _():
            self.slots[slot] = self.slots[slot + 1] + self.slots[11]
            self.move(slot, p.above if upward else p.below).start()

    def total(self):
        return self.slots[11] + self.slots[7] + self.slots[9]

    def finish(self):
        p = self.place
        for stage in range(3):
            self.pair(stage).wait_send()
        pl.when(p.has_above)(self.move(6, p.above).wait_send)
        pl.when(p.has_below)(self.move(8, p.below).wait_send)


def run_plan(plan):
    for _, _, step in sorted(plan, key=lambda entry: entry[:2]):
        step()


def reduce_kernel(*refs):
    sources, small_in = refs[:4], refs[4]
    outs, small_out = refs[5:9], refs[9]
    grads, halves, firsts, seconds, lines, extras, totals = (refs[10 + 4 * i:14 + 4 * i] for i in range(7))
    slots, sems, small_sems, local = refs[38:]
    place = Place()
    loads = {}
    for g in (3, 2, 1, 0):
        for j in range(place.tps):
            loads[g, j] = pltpu.make_async_copy(sources[g].at[j], grads[g].at[j], local.at[g, j])
            loads[g, j].start()
    place.barrier()
    reduce = Reduce(place, grads, halves, firsts, seconds, lines, extras, totals, sems)
    small = SumSmall(place, slots, small_sems)
    plan = []

    def add(tick, order, step, *args):
        plan.append((tick, order, functools.partial(step, *args)))

    def begin(g, j):
        loads[g, j].wait()
        reduce.step(g, j, 0)

    n = place.tps
    stores = {}

    def store(g):
        stores[g] = pltpu.make_async_copy(totals[g], outs[g], local.at[g, n])
        stores[g].start()

    for i, g in enumerate((3, 2, 1, 0)):
        for j in range(n):
            e = i * n + j
            add(e, 0, begin, g, j)
            for stage in (1, 2, 3):
                add(e + stage, 90 - 10 * i - stage, reduce.step, g, j, stage)
        last = i * n + n + 2
        for k in range(n - 1):
            add(last + k, 99 - 10 * i - 4, reduce.travel, g, k)
        add(last + n - 1, 99 - 10 * i - 5, reduce.settle, g)
        for stage in (1, 2, 3):
            add(last + n - 1 + stage, 99 - 10 * i - 5 - stage, reduce.share, g, stage)
        add(last + n + 2, 99, store, g)
    add(0, 1, lambda: small.start(small_in[...]))
    for stage in range(3):
        add(stage + 1, 98, small.exchange, stage)
    add(4, 98, small.among_copies)
    add(5, 98, small.line, True)
    add(5, 98, small.line, False)
    run_plan(plan)
    small_out[...] = small.total()
    for g in range(4):
        reduce.finish(g)
        stores[g].wait()
    small.finish()


def reduce_gradients(grads, small):
    n, extra = lax.axis_size("tp"), lax.axis_size("dp") // 2
    shapes = [g.shape for g in grads]
    vm = lambda parts, dtype=BF16: [pltpu.VMEM(shape, dtype) for shape in parts]
    scratch = (
        vm(shapes)
        + vm((n, r // 2, c) for _, r, c in shapes)
        + vm((n, r // 4, c) for _, r, c in shapes)
        + vm((n, r // 8, c) for _, r, c in shapes)
        + vm((2, n, r // 8, c) for _, r, c in shapes)
        + vm((extra, r // 8, c) for _, r, c in shapes)
        + vm((r, c) for _, r, c in shapes)
        + vm([(SumSmall.SLOTS + extra,) + small.shape], F32)
        + [
            pltpu.SemaphoreType.DMA((Reduce.KINDS, 4, max(n, extra))),
            pltpu.SemaphoreType.DMA((SumSmall.SLOTS + 2 * extra,)),
            pltpu.SemaphoreType.DMA((4, n + 1)),
        ]
    )
    return pl.pallas_call(
        reduce_kernel,
        out_shape=[jax.ShapeDtypeStruct((r, c), BF16) for _, r, c in shapes] + [jax.ShapeDtypeStruct(small.shape, F32)],
        in_specs=[pl.BlockSpec(memory_space=pl.ANY)] * 4 + [pl.BlockSpec(memory_space=pltpu.VMEM)],
        out_specs=[pl.BlockSpec(memory_space=pl.ANY)] * 4 + [pl.BlockSpec(memory_space=pltpu.VMEM)],
        scratch_shapes=scratch,
        compiler_params=pltpu.CompilerParams(collective_id=2, has_side_effects=True, vmem_limit_bytes=60 * 2**20),
        name="reduce_gradients",
    )(*grads, small)


def per_device(
    inputs, memory, out_grad, lengths, src_lengths, configs, norm_gain, norm_bias,
    self_qkv, self_out, cross_q, cross_kv, cross_out, ffn_in, ffn_in_bias, ffn_out, ffn_out_bias,
):
    owned, model = inputs.shape
    layers = memory.shape[0]
    tp = lax.axis_size("tp")
    place_tp = lax.axis_index("tp")
    sentences = owned // LEN
    local = self_out.shape[0]
    pair = local // HD
    units_local = ffn_in.shape[1]
    width, heads, units, depth = (configs[0, i] for i in range(4))
    width_f = width.astype(F32)
    depth_f = depth.astype(F32)
    width_mask = (jnp.arange(model) < width).astype(F32)
    head_mask = (jnp.arange(tp * local) < heads * HD).astype(F32)
    unit_mask = (jnp.arange(tp * units_local) < units).astype(F32)
    place = jnp.arange(LEN)
    own_lengths = lax.dynamic_slice_in_dim(lengths, place_tp * sentences, sentences)
    own_source = lax.dynamic_slice_in_dim(src_lengths, place_tp * sentences, sentences)
    valid = (place[None, :] < own_lengths[:, None]).astype(F32).reshape(owned, 1)
    keep = width_mask * valid
    causal = jnp.broadcast_to(place[:, None] >= place[None, :], (sentences, LEN, LEN))
    crossing = jnp.broadcast_to(place[None, None, :] < own_source[:, None, None], (sentences, LEN, LEN))

    first, second, third, fourth = gather_weights(
        (
            self_qkv.transpose(1, 2, 0).reshape(3 * local, model),
            self_out,
            cross_q.T,
            cross_kv.transpose(1, 2, 0).reshape(2 * local, model),
            cross_out,
            ffn_in,
            ffn_out,
        )
    )
    bias_in = lax.all_gather(ffn_in_bias, "tp", axis=0, tiled=True)

    def part(block, start):
        return block[:, start * local:(start + 1) * local].reshape(tp * local, model)

    def split(flat):
        return flat.astype(BF16).reshape(sentences, LEN, tp * pair, HD)

    def joined(shaped):
        return shaped.reshape(owned, tp * local)

    wq, wk, wv, wo = (part(first, i) for i in range(4))
    xq, xk, xv, xo = (part(second, i) for i in range(4))
    w_up = third.transpose(1, 0, 2).reshape(model, tp * units_local)
    w_down = fourth.reshape(tp * units_local, model)

    rows = inputs.astype(F32)
    a1 = norm_forward(rows, norm_gain[0], norm_bias[0], width_mask, width_f).astype(BF16)
    q1, k1, v1 = split(dot(a1, wq, 1, 1)), split(dot(a1, wk, 1, 1)), split(dot(a1, wv, 1, 1))
    c1, t1 = attend_forward(q1, k1, v1, causal)
    c1 = (joined(c1) * head_mask).astype(BF16)
    h1 = rows + dot(c1, wo, 1, 0) * keep
    a2 = norm_forward(h1, norm_gain[1], norm_bias[1], width_mask, width_f).astype(BF16)
    chosen = (jnp.arange(layers) >= layers - depth).astype(F32)
    mixed = chosen[0] * memory[0].astype(F32)
    for level in range(1, layers):
        mixed = mixed + chosen[level] * memory[level].astype(F32)
    source = (mixed / depth_f * width_mask).astype(BF16)
    q2, k2, v2 = split(dot(a2, xq, 1, 1)), split(dot(source, xk, 1, 1)), split(dot(source, xv, 1, 1))
    c2, t2 = attend_forward(q2, k2, v2, crossing)
    c2 = (joined(c2) * head_mask).astype(BF16)
    h2 = h1 + dot(c2, xo, 1, 0) * keep
    a3 = norm_forward(h2, norm_gain[2], norm_bias[2], width_mask, width_f).astype(BF16)
    before = dot(a3, w_up, 1, 0) + bias_in

    def activate(values):
        return jax.nn.gelu(values, approximate=True) * unit_mask

    hidden, gelu_back = jax.vjp(activate, before)
    hidden = hidden.astype(BF16)
    layer_out = h2 + (dot(hidden, w_down, 1, 0) + ffn_out_bias) * keep

    upstream = out_grad.astype(F32)
    masked = upstream * keep
    bias_out_grad = jnp.sum(masked, axis=0)
    e3 = masked.astype(BF16)
    down_grad = dot(hidden, e3, 0, 0)
    du = gelu_back(dot(e3, w_down, 1, 1))[0].astype(BF16)
    up_grad = dot(a3, du, 0, 0)
    bias_in_grad = jnp.sum(du.astype(F32), axis=0)
    rows_c, gain_c, shift_c = norm_backward(h2, norm_gain[2], width_mask, width_f, dot(du, w_up, 1, 1))
    dh2 = upstream + rows_c
    e2 = (dh2 * keep).astype(BF16)
    xo_grad = dot(c2, e2, 0, 0)
    dc2 = (dot(e2, xo, 1, 1) * head_mask).astype(BF16)
    dq2, dk2, dv2 = attend_backward(q2, k2, v2, crossing, t2, split(dc2))
    dq2, dk2, dv2 = (joined(x).astype(BF16) for x in (dq2, dk2, dv2))
    xq_grad, xk_grad, xv_grad = dot(dq2, a2, 0, 0), dot(dk2, source, 0, 0), dot(dv2, source, 0, 0)
    source_grad = (dot(dk2, xk, 1, 0) + dot(dv2, xv, 1, 0)) * width_mask / depth_f
    memory_grad = chosen[:, None, None] * source_grad[None]
    rows_b, gain_b, shift_b = norm_backward(h1, norm_gain[1], width_mask, width_f, dot(dq2, xq, 1, 0))
    dh1 = dh2 + rows_b
    e1 = (dh1 * keep).astype(BF16)
    wo_grad = dot(c1, e1, 0, 0)
    dc1 = (dot(e1, wo, 1, 1) * head_mask).astype(BF16)
    dq1, dk1, dv1 = attend_backward(q1, k1, v1, causal, t1, split(dc1))
    dq1, dk1, dv1 = (joined(x).astype(BF16) for x in (dq1, dk1, dv1))
    wq_grad, wk_grad, wv_grad = dot(dq1, a1, 0, 0), dot(dk1, a1, 0, 0), dot(dv1, a1, 0, 0)
    rows_a, gain_a, shift_a = norm_backward(
        rows, norm_gain[0], width_mask, width_f, dot(dq1, wq, 1, 0) + dot(dk1, wk, 1, 0) + dot(dv1, wv, 1, 0)
    )
    input_grad = dh1 + rows_a

    def packed(*grads):
        return jnp.concatenate([g.reshape(tp, local, model) for g in grads], axis=1)

    small = jnp.zeros((16, units_local), F32)
    small = small.at[:3, :model].set(jnp.stack([gain_a, gain_b, gain_c]))
    small = small.at[3:6, :model].set(jnp.stack([shift_a, shift_b, shift_c]))
    small = small.at[6, :model].set(bias_out_grad)
    small = small.at[7].set(jnp.sum(own_lengths).astype(F32))
    small = small.at[8:8 + tp].set(bias_in_grad.reshape(tp, units_local))
    *grads, small = reduce_gradients(
        (
            packed(wq_grad, wk_grad, wv_grad, wo_grad).astype(BF16),
            packed(xq_grad, xk_grad, xv_grad, xo_grad).astype(BF16),
            up_grad.reshape(model, tp, units_local).transpose(1, 0, 2).astype(BF16),
            down_grad.reshape(tp, units_local, model).astype(BF16),
        ),
        small,
    )
    inverse = 1.0 / small[7, 0]
    small = small * inverse
    gains, shifts, bias_out_grad = small[:3, :model], small[3:6, :model], small[6, :model]
    bias_in_grad = lax.dynamic_slice_in_dim(small, 8 + place_tp, 1)[0]
    first_grad, second_grad, third_grad, fourth_grad = (x.astype(F32) * inverse for x in grads)
    return (
        layer_out,
        input_grad,
        memory_grad,
        gains,
        shifts,
        first_grad[:3 * local].reshape(3, local, model).transpose(2, 0, 1),
        first_grad[3 * local:],
        second_grad[:local].T,
        second_grad[local:3 * local].reshape(2, local, model).transpose(2, 0, 1),
        second_grad[3 * local:],
        third_grad,
        bias_in_grad,
        fourth_grad,
        bias_out_grad,
    )


def solution(mesh):
    rows = P(("grp", "dp", "tp"), None)
    stack = P(None, ("grp", "dp", "tp"), None)
    weights = (
        P(None, None, "tp"), P("tp", None), P(None, "tp"), P(None, None, "tp"), P("tp", None),
        P(None, "tp"), P("tp"), P("tp", None), P(),
    )
    return jax.shard_map(
        per_device,
        mesh=mesh,
        in_specs=(rows, stack, rows, P(("grp", "dp")), P(("grp", "dp")), P("grp", None), P(), P()) + weights,
        out_specs=(rows, rows, stack, P(), P()) + weights,
        check_vma=False,
    )
```

```python
import functools

import jax
import jax.numpy as jnp
from jax import lax
from jax.experimental import pallas as pl
from jax.experimental.pallas import tpu as pltpu
from jax.sharding import PartitionSpec as P

HD = 80
LEN = 256
EPSILON = 1e-05
NEGATIVE = -1e30
SCALE = HD ** (-0.5)
F32 = jnp.float32
BF16 = jnp.bfloat16


MESH = pl.DeviceIdType.MESH


class Place:
    def __init__(self):
        self.tps = lax.axis_size("tp")
        self.extra = lax.axis_size("dp") // 2
        assert lax.axis_size("grp") == 4 and lax.axis_size("dp") % 2 == 0
        grp, dp, tp = (lax.axis_index(name) for name in ("grp", "dp", "tp"))
        core, low, high = dp % 2, grp % 2, grp // 2
        flip_low, flip_high = grp + 1 - 2 * low, grp + 2 - 4 * high
        self.grp, self.dp, self.tp, self.core = grp, dp, tp, core
        self.first_bit = (1 - core) * low + core * high
        self.second_bit = (1 - core) * high + core * low
        self.first = ((1 - core) * flip_low + core * flip_high, dp, tp)
        self.second = ((1 - core) * flip_high + core * flip_low, dp, tp)
        self.sibling = (grp, dp + 1 - 2 * core, tp)
        self.above = (grp, dp, tp + 1)
        self.below = (grp, dp, tp - 1)
        self.has_above = tp < self.tps - 1
        self.has_below = tp > 0

    def copy_of(self, step):
        return (self.grp, ((self.dp // 2 + step) % self.extra) * 2 + self.core, self.tp)

    def nth_block(self, k):
        size = self.tps
        upper = (2 * self.tp) // size
        lead = (1 - upper) * self.tp + upper * (size - 1 - self.tp)
        spot = k + (k + size - lead) // size
        return (1 - upper) * spot + upper * (size - 1 - spot)

    def barrier(self):
        sem = pltpu.get_barrier_semaphore()
        fixed = [self.first, self.second, self.sibling] + [self.copy_of(s) for s in range(1, self.extra)]
        for device in fixed:
            pl.semaphore_signal(sem, inc=1, device_id=device, device_id_type=MESH)
        for there, device in ((self.has_above, self.above), (self.has_below, self.below)):

            @pl.when(there)
            def _():
                pl.semaphore_signal(sem, inc=1, device_id=device, device_id_type=MESH)

        size = self.tps
        ends = (self.tp + size - 1) // size + (2 * size - 2 - self.tp) // size
        pl.semaphore_wait(sem, len(fixed) + ends)


def push(src, dst, send_sem, recv_sem, device):
    return pltpu.make_async_remote_copy(
        src_ref=src, dst_ref=dst, send_sem=send_sem, recv_sem=recv_sem, device_id=device, device_id_type=MESH
    )


def rows_of(ref, lead, start, count):
    return ref.at[lead, pl.ds(pl.multiple_of(start, 16), count)]


def add_into(total, term):
    def step(i, carry):
        rows = pl.ds(pl.multiple_of(i * 16, 16), 16)
        total[rows] = total[rows] + term[rows]
        return carry

    lax.fori_loop(0, total.shape[0] // 16, step, 0)


def copy_into(total, term):

    def step(i, carry):
        rows = pl.ds(pl.multiple_of(i * 16, 16), 16)
        total[rows] = term[rows]
        return carry

    lax.fori_loop(0, total.shape[0] // 16, step, 0)


class Spread:
    KINDS = 14

    def __init__(self, place, view, unit, sems):
        self.place, self.view, self.unit, self.sems = place, view, unit, sems
        f, s, c = place.first_bit, place.second_bit, place.core
        self.units = (f * 2 + s, f * 2 + 1 - s, (1 - f) * 2 + s, (1 - f) * 2 + 1 - s)
        self.theirs = (s * 2 + f, s * 2 + 1 - f, (1 - s) * 2 + f, (1 - s) * 2 + 1 - f)
        self.table = [
            (place.second, (c, self.units[0]), (c, self.units[1])),
            (place.first, (c, self.units[0]), (c, self.units[2])),
            (place.first, (c, self.units[1]), (c, self.units[3])),
        ] + [(place.sibling, (c, u), (1 - c, t)) for u, t in zip(self.units, self.theirs)]

    def region(self, spot):
        half, unit = spot
        return self.view((half * 4 + unit) * self.unit, self.unit)

    def own(self):
        return self.region((self.place.core, self.units[0]))

    def copy(self, n, lands=False):
        device, leaves, landing = self.table[n]
        part = self.region(landing if lands else leaves)
        return push(part, part, self.sems(2 * n), self.sems(2 * n + 1), device)

    WAITS = ((), (0,), (1, 2), (3, 4, 5, 6))
    SENDS = ((0, 1, 3), (2, 4), (5, 6), ())

    def step(self, stage):
        for n in self.WAITS[stage]:
            self.copy(n, lands=True).wait_recv()
        for n in self.SENDS[stage]:
            self.copy(n).start()

    def finish(self):
        for n in range(7):
            self.copy(n).wait_send()


class Gather:
    KINDS = Spread.KINDS + 3

    def __init__(self, place, buffers, sems):
        self.place, self.buffers, self.sems = place, buffers, sems
        self.unit = [ref.shape[1] // 8 for ref in buffers]
        self.others = place.tps - 1

    def spread(self, g, j):
        return Spread(
            self.place,
            lambda start, count: rows_of(self.buffers[g], j, start, count),
            self.unit[g],
            lambda kind: self.sems.at[kind, g, j],
        )

    def relays(self, g, j):
        p = self.place
        part = self.spread(g, j).own()
        sem = lambda n: self.sems.at[Spread.KINDS + n, g, j]
        return (
            (jnp.logical_and(j <= p.tp, p.has_above), push(part, part, sem(0), sem(2), p.above)),
            (jnp.logical_and(j >= p.tp, p.has_below), push(part, part, sem(1), sem(2), p.below)),
        )

    def start(self, g):
        for needed, copy in self.relays(g, self.place.tp):
            pl.when(needed)(copy.start)

    def step(self, g, k, stage):
        j = self.place.nth_block(k)
        if stage == 0:
            relays = self.relays(g, j)
            relays[0][1].wait_recv()
            for needed, copy in relays:
                pl.when(needed)(copy.start)
        self.spread(g, j).step(stage)

    def drain(self, g, j):
        for needed, copy in self.relays(g, j):
            pl.when(needed)(copy.wait_send)

        @pl.when(j != self.place.tp)
        def _():
            self.spread(g, j).finish()


class Line:
    def __init__(self, place, buffer, sems):
        self.place, self.buffer, self.sems = place, buffer, sems

    def relays(self, j):
        p = self.place
        part = self.buffer.at[j]
        return (
            (jnp.logical_and(j <= p.tp, p.has_above), push(part, part, self.sems.at[0, j], self.sems.at[2, j], p.above)),
            (jnp.logical_and(j >= p.tp, p.has_below), push(part, part, self.sems.at[1, j], self.sems.at[2, j], p.below)),
        )

    def start(self):
        for needed, copy in self.relays(self.place.tp):
            pl.when(needed)(copy.start)

    def step(self, k):
        j = self.place.nth_block(k)
        relays = self.relays(j)
        relays[0][1].wait_recv()
        for needed, copy in relays:
            pl.when(needed)(copy.start)

    def finish(self):
        for j in range(self.place.tps):
            for needed, copy in self.relays(j):
                pl.when(needed)(copy.wait_send)


class Reduce:
    KINDS = 14 + 4 + Spread.KINDS + 2

    def __init__(self, place, grads, halves, firsts, seconds, lines, extras, totals, sems):
        self.place, self.grads, self.totals, self.sems = place, grads, totals, sems
        self.halves, self.firsts, self.seconds, self.lines, self.extras = halves, firsts, seconds, lines, extras
        self.unit = [ref.shape[1] // 8 for ref in grads]

    def sem(self, kind, g, j):
        return self.sems.at[kind, g, j]

    def span(self, g, stage, kept):
        p, unit = self.place, self.unit[g]
        if stage == 0:
            return (p.core if kept else 1 - p.core) * 4 * unit, 4
        if stage == 1:
            return (p.core * 4 + (p.first_bit if kept else 1 - p.first_bit) * 2) * unit, 2
        bit = p.second_bit if kept else 1 - p.second_bit
        return (p.core * 4 + p.first_bit * 2 + bit) * unit, 1

    def region(self, g, j, stage, kept):
        start, units = self.span(g, stage, kept)
        return rows_of(self.grads[g], j, start, units * self.unit[g])

    def landing(self, g, j, stage):
        return (self.halves, self.firsts, self.seconds)[stage][g].at[j]

    def copies_of(self, g, j, stage):
        device = (self.place.sibling, self.place.first, self.place.second)[stage]
        start, units = self.span(g, stage, False)
        unit, base = self.unit[g], (0, 8, 12)[stage]
        return [
            push(
                rows_of(self.grads[g], j, start + u * unit, unit),
                self.landing(g, j, stage).at[pl.ds(u * unit, unit)],
                self.sem(base + 2 * u, g, j), self.sem(base + 2 * u + 1, g, j), device,
            )
            for u in range(units)
        ]

    def step(self, g, j, stage):
        if stage > 0:
            for copy in self.copies_of(g, j, stage - 1):
                copy.wait_recv()
            add_into(self.region(g, j, stage - 1, True), self.landing(g, j, stage - 1))
        if stage < 3:
            for copy in self.copies_of(g, j, stage):
                copy.start()

    def piece(self, g, j):
        return self.region(g, j, 2, True)

    def hop(self, g, j, upward):
        p = self.place
        way = 0 if upward else 1
        return push(
            self.piece(g, j), self.lines[g].at[way, j],
            self.sem(14 + 2 * way, g, j), self.sem(15 + 2 * way, g, j), p.above if upward else p.below,
        )

    def travel(self, g, k):
        p = self.place
        for upward in (True, False):
            j = p.tps - 1 - k if upward else k
            has_source = p.has_below if upward else p.has_above
            involved = j >= p.tp if upward else j <= p.tp
            passes = j > p.tp if upward else j < p.tp

            @pl.when(jnp.logical_and(involved, has_source))
            def _():
                self.hop(g, j, upward).wait_recv()
                add_into(self.piece(g, j), self.lines[g].at[0 if upward else 1, j])

            pl.when(passes)(self.hop(g, j, upward).start)

    def copies(self, g, step):
        p = self.place
        return push(
            self.piece(g, p.tp), self.extras[g].at[step], self.sem(self.KINDS - 2, g, step), self.sem(self.KINDS - 1, g, step), p.copy_of(step)
        )

    def among_copies(self, g):
        p = self.place
        if p.extra > 1:
            for step in range(1, p.extra):
                self.copies(g, step).start()
            total = self.piece(g, p.tp)[...].astype(F32)
            for step in range(1, p.extra):
                self.copies(g, step).wait()
                total = total + self.extras[g][step].astype(F32)
            self.piece(g, p.tp)[...] = total.astype(BF16)

    def spread(self, g):
        return Spread(
            self.place,
            lambda start, count: self.totals[g].at[pl.ds(pl.multiple_of(start, 16), count)],
            self.unit[g],
            lambda kind: self.sems.at[18 + kind, g, 0],
        )

    def settle(self, g):
        self.among_copies(g)
        copy_into(self.spread(g).own(), self.piece(g, self.place.tp))
        self.spread(g).step(0)

    def share(self, g, stage):
        self.spread(g).step(stage)

    def finish(self, g):
        p = self.place
        for j in range(p.tps):
            for stage in range(3):
                for copy in self.copies_of(g, j, stage):
                    copy.wait_send()
            pl.when(j > p.tp)(self.hop(g, j, True).wait_send)
            pl.when(j < p.tp)(self.hop(g, j, False).wait_send)
        self.spread(g).finish()


class SumSmall:
    SLOTS = 12

    def __init__(self, place, slots, sems):
        self.place, self.slots, self.sems = place, slots, sems

    def move(self, source, device):
        return push(
            self.slots.at[source], self.slots.at[source + 1], self.sems.at[source], self.sems.at[source + 1], device
        )

    def pair(self, stage):
        p = self.place
        return self.move(2 * stage, (p.sibling, p.first, p.second)[stage])

    def start(self):
        p = self.place
        for there, slot in ((p.has_below, 7), (p.has_above, 9)):

            @pl.when(jnp.logical_not(there))
            def _():
                self.slots[slot] = jnp.zeros(self.slots.shape[1:], F32)

        self.pair(0).start()

    def exchange(self, stage):
        self.pair(stage).wait_recv()
        value = self.slots[2 * stage] + self.slots[2 * stage + 1]
        if stage < 2:
            self.slots[2 * stage + 2] = value
            self.pair(stage + 1).start()
        else:
            self.slots[10] = value

    def among_copies(self):
        p = self.place
        base = self.SLOTS
        for step in range(1, p.extra):
            self.copies(step).start()
        for step in range(1, p.extra):
            self.copies(step).wait()
        if p.extra > 1:
            total = self.slots[10]
            for step in range(1, p.extra):
                total = total + self.slots[base + step]
            self.slots[11] = total
        else:
            self.slots[11] = self.slots[10]

    def copies(self, step):
        base = self.SLOTS
        return push(
            self.slots.at[10], self.slots.at[base + step],
            self.sems.at[base + 2 * step], self.sems.at[base + 2 * step + 1], self.place.copy_of(step),
        )

    def line(self, k):
        p = self.place
        last = p.tps - 1
        for slot, turn, device in ((6, k, p.above), (8, last - k, p.below)):

            @pl.when(p.tp == turn)
            def _():
                if k > 0:
                    self.move(slot, device).wait_recv()
                if k < last:
                    self.slots[slot] = self.slots[slot + 1] + self.slots[11]
                    self.move(slot, device).start()

    def total(self):
        return self.slots[11] + self.slots[7] + self.slots[9]

    def finish(self):
        p = self.place
        for stage in range(3):
            self.pair(stage).wait_send()
        pl.when(p.has_above)(self.move(6, p.above).wait_send)
        pl.when(p.has_below)(self.move(8, p.below).wait_send)


def dot_nn(left, right):
    return lax.dot_general(left, right, (((1,), (0,)), ((), ())), preferred_element_type=F32)


def dot_nt(left, right):
    return lax.dot_general(left, right, (((1,), (1,)), ((), ())), preferred_element_type=F32)


def dot_tn(left, right):
    return lax.dot_general(left, right, (((0,), (0,)), ((), ())), preferred_element_type=F32)


def column(axis, shape):
    return lax.broadcasted_iota(jnp.int32, shape, axis)


def each(count, step):

    def run(i, carry):
        step(i)
        return carry

    lax.fori_loop(0, count, run, 0)


CHUNK = 64
CUBE = 0.044715
ROOT = 0.7978845608028654


def layer_kernel(names, *refs):
    r = dict(zip(names, refs))
    place = Place()
    n = place.tps
    x, model = r["x"], r["x"].shape[1]
    owned = x.shape[0]
    sentences = owned // LEN
    local = r["q1"].shape[2]
    heads_here = local // HD
    units = r["hidden"].shape[1]
    layers = r["memory"].shape[0]
    weights = [r["w%d" % i] for i in range(4)]
    lengths, sources, configs = r["lengths"], r["src_lengths"], r["configs"]
    width, heads, hidden_units, depth = (configs[0, i] for i in range(4))
    inv_width = 1.0 / jnp.full((1, 1), width.astype(F32))
    inv_depth = 1.0 / jnp.full((1, 1), depth.astype(F32))
    width_mask = (column(1, (1, model)) < width).astype(F32)

    local_sem = r["local_sems"]
    spots = (
        (0, 0, 3 * local), (0, 3 * local, local),
        (1, 0, local), (1, local, 2 * local), (1, 3 * local, local),
        (2, 0, weights[2].shape[1]), (3, 0, weights[3].shape[1]),
    )
    fills = [
        (g, pltpu.make_async_copy(r["in%d" % i], weights[g].at[place.tp, pl.ds(start, size)], local_sem.at[i]))
        for i, (g, start, size) in enumerate(spots)
    ]
    loads = [
        pltpu.make_async_copy(r[name + "_in"], r[name], local_sem.at[7 + i])
        for i, name in enumerate(("x", "memory", "upstream"))
    ]
    for _, copy in fills[:2]:
        copy.start()
    loads[0].start()
    for _, copy in fills[2:]:
        copy.start()
    loads[1].start()
    loads[2].start()
    r["bias"][place.tp] = jnp.broadcast_to(r["bias_in"][...], r["bias"].shape[1:])
    place.barrier()

    gather = Gather(place, weights, r["gather_sems"])
    bias = Line(place, r["bias"], r["bias_sems"])
    for g in range(4):
        for group, copy in fills:
            if group == g:
                copy.wait()
        gather.start(g)
        if g == 0:
            bias.start()
    order = [(g, k) for g in (0, 1) for k in range(n - 1)] + [(g, k) for k in range(n - 1) for g in (2, 3)]

    def g_tick(tick):
        for stage in range(4):
            if 0 <= tick - stage < len(order):
                gather.step(*order[tick - stage], stage)

    def block(k):
        later = (k + n - 1) // n
        return (1 - later) * place.tp + later * place.nth_block(k - 1)

    def hooks(table, k, b):
        for (kk, bb), steps in table.items():

            @pl.when(jnp.logical_and(k == kk, b == bb))
            def _():
                for step in steps:
                    step()

    def chunk(i):
        return pl.ds(pl.multiple_of(i * CHUNK, CHUNK), CHUNK)

    def keep_of(i):
        per = LEN // CHUNK
        spot = column(0, (CHUNK, 1)) + (i % per) * CHUNK
        return (spot < lengths[place.tp * sentences + i // per]).astype(F32) * width_mask

    def norm_parts(rows):
        mean = jnp.sum(rows * width_mask, axis=-1, keepdims=True) * inv_width
        centred = (rows - mean) * width_mask
        spread = jnp.sum(centred * centred, axis=-1, keepdims=True) * inv_width
        rstd = lax.rsqrt(spread + EPSILON)
        return centred * rstd, rstd

    def norm(rows, which):
        hat, _ = norm_parts(rows)
        return ((hat * r["gains"][which:which + 1] + r["shifts"][which:which + 1]) * width_mask).astype(BF16)

    def fold(values):
        return jnp.sum(values.reshape(values.shape[0] // 8, 8, values.shape[1]), axis=0)

    def norm_backward(rows, which, upstream):
        hat, rstd = norm_parts(rows)
        upstream = upstream * width_mask
        sums = r["norm_sums"]
        sums[which] = sums[which] + fold(upstream * hat)
        sums[3 + which] = sums[3 + which] + fold(upstream)
        scaled = upstream * r["gains"][which:which + 1]
        first = jnp.sum(scaled, axis=-1, keepdims=True) * inv_width
        second = jnp.sum(scaled * hat, axis=-1, keepdims=True) * inv_width
        return (rstd * (scaled - first - hat * second)) * width_mask

    chunks = owned // CHUNK
    acc, da, dh = r["acc"], r["da"], r["dh"]
    zeros = jnp.zeros((CHUNK, model), F32)
    r["norm_sums"][...] = jnp.zeros(r["norm_sums"].shape, F32)
    r["bias_sums"][...] = jnp.zeros(r["bias_sums"].shape, F32)

    def head_lanes(h):
        lane = column(1, (1, local))
        return jnp.logical_and(lane >= h * HD, lane < (h + 1) * HD)

    def of_head(values, h):
        return jnp.where(head_lanes(h), values, jnp.zeros_like(values))

    def head_mask(j):
        return (column(1, (1, local)) + j * local < heads * HD).astype(F32)

    def causal(b):
        return column(0, (LEN, LEN)) >= column(1, (LEN, LEN))

    def crossing(b):
        return column(1, (LEN, LEN)) < sources[place.tp * sentences + b]

    def weights_of(query, keys, allowed):
        scores = jnp.where(allowed, dot_nt(query, keys) * SCALE, NEGATIVE)
        raised = jnp.exp(scores - jnp.max(scores, axis=-1, keepdims=True))
        return raised * (1.0 / jnp.sum(raised, axis=-1, keepdims=True))

    def sentence(b):
        return pl.ds(pl.multiple_of(b * LEN, LEN), LEN)

    def attend(k, table, w, names, query_rows, key_rows, allowed):
        q, kk, v, c = (r[name] for name in names)
        j = block(k)

        def one(b):
            hooks(table, k, b)
            rows = sentence(b)
            query = dot_nt(query_rows[rows], w[j, :local]).astype(BF16)
            keys = dot_nt(key_rows[rows], w[j, local:2 * local]).astype(BF16)
            values = dot_nt(key_rows[rows], w[j, 2 * local:3 * local]).astype(BF16)
            q[j, rows] = query
            kk[j, rows] = keys
            v[j, rows] = values
            context = jnp.zeros((LEN, local), F32)
            for h in range(heads_here):
                p = weights_of(of_head(query, h), keys, allowed(b)).astype(BF16)
                context = context + dot_nn(p, of_head(values, h))
            context = (context * head_mask(j)).astype(BF16)
            c[j, rows] = context
            acc[rows] = acc[rows] + dot_nn(context, w[j, 3 * local:])

        each(sentences, one)

    def attend_backward(k, table, g, names, query_rows, key_rows, allowed, both):
        w = weights[g]
        q, kk, v, c = (r[name] for name in names)
        j = block(k)
        e = r["e"]

        def one(b):
            hooks(table, k, b)
            rows = sentence(b)
            query, keys, values = q[j, rows], kk[j, rows], v[j, rows]
            dc = (dot_nt(e[rows], w[j, 3 * local:]) * head_mask(j)).astype(BF16)
            dq = jnp.zeros((LEN, local), F32)
            dk = jnp.zeros((LEN, local), F32)
            dv = jnp.zeros((LEN, local), F32)
            for h in range(heads_here):
                query_h, dc_h = of_head(query, h), of_head(dc, h)
                p = weights_of(query_h, keys, allowed(b))
                dv = dv + dot_tn(p.astype(BF16), dc_h)
                dp = dot_nt(dc_h, values)
                ds = (p * (dp - jnp.sum(dp * p, axis=-1, keepdims=True))).astype(BF16)
                dq = dq + dot_nn(ds, of_head(keys, h))
                dk = dk + dot_tn(ds, query_h)
            dq, dk, dv = (dq * SCALE).astype(BF16), (dk * SCALE).astype(BF16), dv.astype(BF16)
            q[j, rows] = dq
            kk[j, rows] = dk
            v[j, rows] = dv
            from_query = dot_nn(dq, w[j, :local])
            from_keys = dot_nn(dk, w[j, local:2 * local]) + dot_nn(dv, w[j, 2 * local:3 * local])
            if both:
                da[rows] = da[rows] + (from_query + from_keys)
            else:
                da[rows] = da[rows] + from_query
                r["dm"][rows] = r["dm"][rows] + from_keys

        each(sentences, one)
        gather.drain(g, j)
        w[j, :local] = dot_tn(q[j], query_rows[...]).astype(BF16)
        w[j, local:2 * local] = dot_tn(kk[j], key_rows[...]).astype(BF16)
        w[j, 2 * local:3 * local] = dot_tn(v[j], key_rows[...]).astype(BF16)
        w[j, 3 * local:] = dot_tn(c[j], e[...]).astype(BF16)

    def feed(k, table):
        j = block(k)
        w_up, w_down = weights[2], weights[3]
        unit_mask = (column(1, (1, units)) + j * units < hidden_units).astype(F32)

        def one(b):
            hooks(table, k, b)
            rows = sentence(b)
            before = dot_nn(r["a3"][rows], w_up[j]) + r["bias"][j, 0:1]
            square = before * before
            bent = jnp.tanh(ROOT * before * (1.0 + CUBE * square))
            half = 0.5 * (1.0 + bent)
            g = (before * half * unit_mask).astype(BF16)
            slope = (half + 0.5 * before * (1.0 - bent * bent) * (ROOT + 3.0 * CUBE * ROOT * square)) * unit_mask
            r["hidden"][rows] = g
            acc[rows] = acc[rows] + dot_nn(g, w_down[j])
            du = (dot_nt(r["e"][rows], w_down[j]) * slope).astype(BF16)
            r["dhidden"][rows] = du
            r["bias_sums"][j] = r["bias_sums"][j] + fold(du.astype(F32))
            da[rows] = da[rows] + dot_nt(du, w_up[j])

        each(sentences, one)
        gather.drain(2, j)
        gather.drain(3, j)

        def down(i):
            part = pl.ds(pl.multiple_of(i * 128, 128), 128)
            w_down[j, part] = dot_tn(r["hidden"][:, part], r["e"][...]).astype(BF16)

        def up(i):
            part = pl.ds(pl.multiple_of(i * 128, 128), 128)
            w_up[j, part] = dot_tn(r["a3"][:, part], r["dhidden"][...]).astype(BF16)

        each(units // 128, down)
        each(model // 128, up)

    loads[0].wait()

    def begin(i):
        rows = chunk(i)
        r["a1"][rows] = norm(x[rows].astype(F32), 0)
        acc[rows] = zeros
        da[rows] = zeros
        r["dm"][rows] = zeros

    each(chunks, begin)
    g_tick(0)
    loads[1].wait()

    def mix(i):
        rows = chunk(i)
        total = jnp.zeros((CHUNK, model), F32)
        for level in range(layers):
            chosen = (jnp.full((1, 1), depth) >= layers - level).astype(F32)
            total = total + chosen * r["memory"][level, rows].astype(F32)
        r["m"][rows] = (total * inv_depth * width_mask).astype(BF16)

    each(chunks, mix)
    loads[2].wait()
    r["out_sums"][...] = jnp.zeros(r["out_sums"].shape, F32)

    def grad_in(i):
        rows = chunk(i)
        masked = r["upstream"][rows].astype(F32) * keep_of(i)
        r["out_sums"][...] = r["out_sums"][...] + fold(masked)
        r["e"][rows] = masked.astype(BF16)

    each(chunks, grad_in)

    def ticks(*numbers):
        return [functools.partial(g_tick, i) for i in numbers]

    first_names, second_names = ("q1", "k1", "v1", "c1"), ("q2", "k2", "v2", "c2")
    others = n - 1
    assert n == 4
    table = {
        (0, 1): ticks(1),
        (1, 0): ticks(2, 3) + [functools.partial(bias.step, 0)],
        (2, 0): ticks(4) + [functools.partial(bias.step, 1)],
        (3, 0): ticks(5) + [functools.partial(bias.step, 2)],
    }
    each(n, lambda k: attend(k, table, weights[0], first_names, r["a1"], r["a1"], causal))

    def after_self(i):
        rows = chunk(i)
        h = x[rows].astype(F32) + acc[rows] * keep_of(i)
        r["h1"][rows] = h
        r["a2"][rows] = norm(h, 1)
        acc[rows] = zeros

    each(chunks, after_self)
    table2 = {(k, 0): ticks(6 + k) for k in range(n)}
    each(n, lambda k: attend(k, table2, weights[1], second_names, r["a2"], r["m"], crossing))

    def after_cross(i):
        rows = chunk(i)
        h = r["h1"][rows] + acc[rows] * keep_of(i)
        r["h2"][rows] = h
        r["a3"][rows] = norm(h, 2)
        acc[rows] = zeros

    each(chunks, after_cross)

    reduce = Reduce(
        place, weights, *([r["%s%d" % (name, i)] for i in range(4)] for name in
                          ("half", "first", "second", "line", "extra", "total")), r["reduce_sems"],
    )
    plan = {}

    def add(tick, order, step, *args):
        plan.setdefault(tick, []).append((order, len(plan.get(tick, ())), functools.partial(step, *args)))

    def r_tick(tick):
        for _, _, step in sorted(plan.get(tick, ()), key=lambda entry: entry[:2]):
            step()

    def store(g):
        return pltpu.make_async_copy(r["total%d" % g], r["out%d" % g], local_sem.at[10 + g])

    starts = {3: [2 * k + 1 for k in range(n)], 2: [2 * k + 1 for k in range(n)]}
    starts[1] = [10 + 2 * k for k in range(n)]
    starts[0] = [19 + 2 * k for k in range(n)]
    for late, g in enumerate((3, 2, 1, 0)):
        for k, tick in enumerate(starts[g]):
            for stage in range(4):
                add(tick + stage, stage, reduce.step, g, block(k), stage)
        last = starts[g][-1] + 3
        for k in range(n - 1):
            add(last + 1 + k, 10 - late, reduce.travel, g, k)
        add(last + n, 20 - late, reduce.settle, g)
        for stage in (1, 2, 3):
            add(last + n + stage, 30 + stage - late, reduce.share, g, stage)
        add(last + n + 3, 50, lambda g=g: store(g).start())

    def reduce_ticks(*numbers):
        return [functools.partial(r_tick, i) for i in numbers]

    def at_end(k, numbers):
        for kk, number in enumerate(numbers):

            @pl.when(k == kk)
            def _():
                r_tick(number)

    table3 = {(0, 0): ticks(10), (0, 1): ticks(11), (1, 1): ticks(12) + reduce_ticks(2),
              (2, 1): ticks(13) + reduce_ticks(4), (3, 0): ticks(14), (3, 1): reduce_ticks(6)}

    def feed_step(k):
        feed(k, table3)
        at_end(k, [2 * i + 1 for i in range(n)])

    each(n, feed_step)
    r_tick(8)
    out_copy = pltpu.make_async_copy(acc, r["layer_out"], local_sem.at[14])

    def after_feed(i):
        rows = chunk(i)
        keep = keep_of(i)
        acc[rows] = r["h2"][rows] + (acc[rows] + r["bias_out"][...]) * keep
        down = r["upstream"][rows].astype(F32) + norm_backward(r["h2"][rows], 2, da[rows])
        dh[rows] = down
        r["e"][rows] = (down * keep).astype(BF16)
        da[rows] = zeros

    each(chunks, after_feed)
    out_copy.start()
    table4 = {(k, 1): reduce_ticks(9 + 2 * k) for k in range(n)}

    def cross_step(k):
        attend_backward(k, table4, 1, second_names, r["a2"], r["m"], crossing, False)
        at_end(k, [10 + 2 * i for i in range(n)])

    each(n, cross_step)
    memory_copy = pltpu.make_async_copy(r["dm"], r["memory_out"], local_sem.at[15])
    memory_copy.start()

    def before_cross(i):
        rows = chunk(i)
        down = dh[rows] + norm_backward(r["h1"][rows], 1, da[rows])
        dh[rows] = down
        r["e"][rows] = (down * keep_of(i)).astype(BF16)
        da[rows] = zeros

    each(chunks, before_cross)
    r_tick(17)
    table5 = {(k, 1): reduce_ticks(18 + 2 * k) for k in range(n)}

    def self_step(k):
        attend_backward(k, table5, 0, first_names, r["a1"], r["a1"], causal, True)
        at_end(k, [19 + 2 * i for i in range(n)])

    each(n, self_step)

    def before_self(i):
        rows = chunk(i)
        dh[rows] = dh[rows] + norm_backward(x[rows].astype(F32), 0, da[rows])

    each(chunks, before_self)
    grad_copy = pltpu.make_async_copy(dh, r["input_grad"], local_sem.at[16])
    grad_copy.start()

    small = SumSmall(place, r["slots"], r["small_sems"])

    def small_start():
        own = r["slots"].at[0]
        own[...] = jnp.zeros(own.shape, F32)
        for i in range(6):
            own[i:i + 1, :model] = jnp.sum(r["norm_sums"][i], axis=0, keepdims=True)
        own[6:7, :model] = jnp.sum(r["out_sums"][...], axis=0, keepdims=True)
        tokens = lengths[place.tp * sentences]
        for b in range(1, sentences):
            tokens = tokens + lengths[place.tp * sentences + b]
        own[7:8] = jnp.full((1, own.shape[1]), tokens.astype(F32))
        for i in range(n):
            own[8 + i:9 + i] = jnp.sum(r["bias_sums"][i], axis=0, keepdims=True)
        small.start()

    add(26, 5, small_start)
    for stage in range(3):
        add(27 + stage, 5, small.exchange, stage)
    add(30, 4, small.among_copies)
    for k in range(n):
        add(30 + k, 5, small.line, k)
    final = max(plan)
    for tick in range(26, final + 1):
        r_tick(tick)
    r["small_out"][...] = small.total()
    bias.finish()
    for copy in (out_copy, memory_copy, grad_copy):
        copy.wait()
    for g in range(4):
        reduce.finish(g)
        store(g).wait()
    small.finish()


def run_layer(args, weights):
    lengths, src_lengths, configs, gains, shifts, bias_in, bias_out, x, memory, upstream = args
    n, extra = lax.axis_size("tp"), lax.axis_size("dp") // 2
    owned, model = x.shape
    local, units = weights[1].shape[0], bias_in.shape[1]
    small = (16, units)
    assert n <= 8 and units >= model
    shapes = [(n, 4 * local, model)] * 2 + [(n,) + weights[5].shape, (n,) + weights[6].shape]
    scratch = {}

    def vmem(name, shape, dtype=BF16):
        scratch[name] = pltpu.VMEM(shape, dtype)

    def dma(name, *shape):
        scratch[name] = pltpu.SemaphoreType.DMA(shape)

    for i, shape in enumerate(shapes):
        vmem("w%d" % i, shape)
    vmem("bias", (n, 8, units), F32)
    vmem("x", x.shape)
    vmem("memory", memory.shape)
    vmem("upstream", upstream.shape)
    for name in ("a1", "a2", "a3", "m", "e"):
        vmem(name, (owned, model))
    for name in ("h1", "h2", "dh", "acc", "da", "dm"):
        vmem(name, (owned, model), F32)
    for name in ("q1", "k1", "v1", "c1", "q2", "k2", "v2", "c2"):
        vmem(name, (n, owned, local))
    vmem("hidden", (owned, units))
    vmem("dhidden", (owned, units))
    vmem("bias_sums", (n, 8, units), F32)
    vmem("norm_sums", (6, 8, model), F32)
    vmem("out_sums", (8, model), F32)
    for i, (_, rows, columns) in enumerate(shapes):
        vmem("half%d" % i, (n, rows // 2, columns))
        vmem("first%d" % i, (n, rows // 4, columns))
        vmem("second%d" % i, (n, rows // 8, columns))
        vmem("line%d" % i, (2, n, rows // 8, columns))
        vmem("extra%d" % i, (extra, rows // 8, columns))
        vmem("total%d" % i, (rows, columns))
    vmem("slots", (SumSmall.SLOTS + extra,) + small, F32)
    dma("gather_sems", Gather.KINDS, 4, n)
    dma("bias_sems", 3, n)
    dma("reduce_sems", Reduce.KINDS, 4, max(n, extra))
    dma("small_sems", SumSmall.SLOTS + 2 * extra)
    dma("local_sems", 17)
    outs = {
        "layer_out": (x.shape, F32), "input_grad": (x.shape, F32), "memory_out": (x.shape, F32),
        "out0": (shapes[0][1:], BF16), "out1": (shapes[1][1:], BF16), "out2": (shapes[2][1:], BF16), "out3": (shapes[3][1:], BF16),
        "small_out": (small, F32),
    }
    names = ["lengths", "src_lengths", "configs", "gains", "shifts", "bias_in", "bias_out", "x_in", "memory_in", "upstream_in"]
    names += ["in%d" % i for i in range(7)] + list(outs) + list(scratch)
    smem, vm, hbm = (pl.BlockSpec(memory_space=space) for space in (pltpu.SMEM, pltpu.VMEM, pl.ANY))
    flops = 6 * owned * model * (8 * n * local + 2 * n * units)
    return pl.pallas_call(
        functools.partial(layer_kernel, names),
        out_shape=[jax.ShapeDtypeStruct(*out) for out in outs.values()],
        in_specs=[smem] * 3 + [vm] * 4 + [hbm] * 10,
        out_specs=[hbm] * 7 + [vm],
        scratch_shapes=list(scratch.values()),
        compiler_params=pltpu.CompilerParams(collective_id=1, has_side_effects=True, vmem_limit_bytes=64 * 2**20),
        cost_estimate=pl.CostEstimate(flops=flops, bytes_accessed=40 * 2**20, transcendentals=0),
        name="layer",
    )(*args, *weights)


def per_device(
    inputs, memory, out_grad, lengths, src_lengths, configs, norm_gain, norm_bias,
    self_qkv, self_out, cross_q, cross_kv, cross_out, ffn_in, ffn_in_bias, ffn_out, ffn_out_bias,
):
    model = inputs.shape[1]
    layers = memory.shape[0]
    local = self_out.shape[0]
    units = ffn_in.shape[1]
    layer_out, input_grad, source_grad, first, second, third, fourth, small = run_layer(
        (lengths, src_lengths, configs, norm_gain, norm_bias, ffn_in_bias.reshape(1, units),
         ffn_out_bias.reshape(1, model), inputs, memory, out_grad),
        (self_qkv.transpose(1, 2, 0).reshape(3 * local, model), self_out, cross_q.T,
         cross_kv.transpose(1, 2, 0).reshape(2 * local, model), cross_out, ffn_in, ffn_out),
    )
    width_mask = (jnp.arange(model) < configs[0, 0]).astype(F32)
    chosen = (jnp.arange(layers) >= layers - configs[0, 3]).astype(F32) / configs[0, 3].astype(F32)
    memory_grad = chosen[:, None, None] * (source_grad * width_mask)[None]
    inverse = 1.0 / small[7, 0]
    small = small * inverse
    first, second, third, fourth = (block.astype(F32) * inverse for block in (first, second, third, fourth))
    return (
        layer_out,
        input_grad,
        memory_grad,
        small[:3, :model],
        small[3:6, :model],
        first[:3 * local].reshape(3, local, model).transpose(2, 0, 1),
        first[3 * local:],
        second[:local].T,
        second[local:3 * local].reshape(2, local, model).transpose(2, 0, 1),
        second[3 * local:],
        third,
        lax.dynamic_slice_in_dim(small, 8 + lax.axis_index("tp"), 1)[0],
        fourth,
        small[6, :model],
    )


def solution(mesh):
    rows = P(("grp", "dp", "tp"), None)
    stack = P(None, ("grp", "dp", "tp"), None)
    weights = (
        P(None, None, "tp"), P("tp", None), P(None, "tp"), P(None, None, "tp"), P("tp", None),
        P(None, "tp"), P("tp"), P("tp", None), P(),
    )
    return jax.shard_map(
        per_device,
        mesh=mesh,
        in_specs=(rows, stack, rows, P(("grp", "dp")), P(("grp", "dp")), P("grp", None), P(), P()) + weights,
        out_specs=(rows, rows, stack, P(), P()) + weights,
        check_vma=False,
    )
```

```python
import functools

import jax
import jax.numpy as jnp
from jax import lax
from jax.experimental import pallas as pl
from jax.experimental.pallas import tpu as pltpu
from jax.sharding import PartitionSpec as P

HD = 80
LEN = 256
EPSILON = 1e-05
NEGATIVE = -1e30
SCALE = HD ** (-0.5)
LOG2E = 1.4426950408889634
F32 = jnp.float32
BF16 = jnp.bfloat16


MESH = pl.DeviceIdType.MESH


class Place:
    def __init__(self):
        self.tps = lax.axis_size("tp")
        self.extra = lax.axis_size("dp") // 2
        assert lax.axis_size("grp") == 4 and lax.axis_size("dp") % 2 == 0
        grp, dp, tp = (lax.axis_index(name) for name in ("grp", "dp", "tp"))
        core, low, high = dp % 2, grp % 2, grp // 2
        flip_low, flip_high = grp + 1 - 2 * low, grp + 2 - 4 * high
        self.grp, self.dp, self.tp, self.core = grp, dp, tp, core
        self.first_bit = (1 - core) * low + core * high
        self.second_bit = (1 - core) * high + core * low
        self.first = ((1 - core) * flip_low + core * flip_high, dp, tp)
        self.second = ((1 - core) * flip_high + core * flip_low, dp, tp)
        self.sibling = (grp, dp + 1 - 2 * core, tp)
        self.above = (grp, dp, tp + 1)
        self.below = (grp, dp, tp - 1)
        self.has_above = tp < self.tps - 1
        self.has_below = tp > 0

    def copy_of(self, step):
        return (self.grp, ((self.dp // 2 + step) % self.extra) * 2 + self.core, self.tp)

    def nth_block(self, k):
        size = self.tps
        upper = (2 * self.tp) // size
        lead = (1 - upper) * self.tp + upper * (size - 1 - self.tp)
        spot = k + (k + size - lead) // size
        return (1 - upper) * spot + upper * (size - 1 - spot)

    def barrier(self):
        sem = pltpu.get_barrier_semaphore()
        fixed = [self.first, self.second, self.sibling] + [self.copy_of(s) for s in range(1, self.extra)]
        for device in fixed:
            pl.semaphore_signal(sem, inc=1, device_id=device, device_id_type=MESH)
        for there, device in ((self.has_above, self.above), (self.has_below, self.below)):

            @pl.when(there)
            def _():
                pl.semaphore_signal(sem, inc=1, device_id=device, device_id_type=MESH)

        size = self.tps
        ends = (self.tp + size - 1) // size + (2 * size - 2 - self.tp) // size
        pl.semaphore_wait(sem, len(fixed) + ends)


def push(src, dst, send_sem, recv_sem, device):
    return pltpu.make_async_remote_copy(
        src_ref=src, dst_ref=dst, send_sem=send_sem, recv_sem=recv_sem, device_id=device, device_id_type=MESH
    )


def rows_of(ref, lead, start, count):
    return ref.at[lead, pl.ds(pl.multiple_of(start, 16), count)]


def add_into(total, term):
    def step(i, carry):
        rows = pl.ds(pl.multiple_of(i * 16, 16), 16)
        total[rows] = total[rows] + term[rows]
        return carry

    lax.fori_loop(0, total.shape[0] // 16, step, 0)


def copy_into(total, term):

    def step(i, carry):
        rows = pl.ds(pl.multiple_of(i * 16, 16), 16)
        total[rows] = term[rows]
        return carry

    lax.fori_loop(0, total.shape[0] // 16, step, 0)


class Spread:
    KINDS = 14

    def __init__(self, place, view, unit, sems):
        self.place, self.view, self.unit, self.sems = place, view, unit, sems
        f, s, c = place.first_bit, place.second_bit, place.core
        self.units = (f * 2 + s, f * 2 + 1 - s, (1 - f) * 2 + s, (1 - f) * 2 + 1 - s)
        self.theirs = (s * 2 + f, s * 2 + 1 - f, (1 - s) * 2 + f, (1 - s) * 2 + 1 - f)
        self.table = [
            (place.second, (c, self.units[0]), (c, self.units[1])),
            (place.first, (c, self.units[0]), (c, self.units[2])),
            (place.first, (c, self.units[1]), (c, self.units[3])),
        ] + [(place.sibling, (c, u), (1 - c, t)) for u, t in zip(self.units, self.theirs)]

    def region(self, spot):
        half, unit = spot
        return self.view((half * 4 + unit) * self.unit, self.unit)

    def own(self):
        return self.region((self.place.core, self.units[0]))

    def copy(self, n, lands=False):
        device, leaves, landing = self.table[n]
        part = self.region(landing if lands else leaves)
        return push(part, part, self.sems(2 * n), self.sems(2 * n + 1), device)

    WAITS = ((), (0,), (1, 2), (3, 4, 5, 6))
    SENDS = ((0, 1, 3), (2, 4), (5, 6), ())

    def step(self, stage):
        for n in self.WAITS[stage]:
            self.copy(n, lands=True).wait_recv()
        for n in self.SENDS[stage]:
            self.copy(n).start()

    def finish(self):
        for n in range(7):
            self.copy(n).wait_send()


class Gather:
    KINDS = Spread.KINDS + 3

    def __init__(self, place, buffers, sems):
        self.place, self.buffers, self.sems = place, buffers, sems
        self.unit = [ref.shape[1] // 8 for ref in buffers]
        self.others = place.tps - 1

    def spread(self, g, j):
        return Spread(
            self.place,
            lambda start, count: rows_of(self.buffers[g], j, start, count),
            self.unit[g],
            lambda kind: self.sems.at[kind, g, j],
        )

    def relays(self, g, j):
        p = self.place
        part = self.spread(g, j).own()
        sem = lambda n: self.sems.at[Spread.KINDS + n, g, j]
        return (
            (jnp.logical_and(j <= p.tp, p.has_above), push(part, part, sem(0), sem(2), p.above)),
            (jnp.logical_and(j >= p.tp, p.has_below), push(part, part, sem(1), sem(2), p.below)),
        )

    def start(self, g):
        for needed, copy in self.relays(g, self.place.tp):
            pl.when(needed)(copy.start)

    def step(self, g, k, stage):
        j = self.place.nth_block(k)
        if stage == 0:
            relays = self.relays(g, j)
            relays[0][1].wait_recv()
            for needed, copy in relays:
                pl.when(needed)(copy.start)
        self.spread(g, j).step(stage)

    def drain(self, g, j):
        for needed, copy in self.relays(g, j):
            pl.when(needed)(copy.wait_send)

        @pl.when(j != self.place.tp)
        def _():
            self.spread(g, j).finish()


class Line:
    def __init__(self, place, buffer, sems):
        self.place, self.buffer, self.sems = place, buffer, sems

    def relays(self, j):
        p = self.place
        part = self.buffer.at[j]
        return (
            (jnp.logical_and(j <= p.tp, p.has_above), push(part, part, self.sems.at[0, j], self.sems.at[2, j], p.above)),
            (jnp.logical_and(j >= p.tp, p.has_below), push(part, part, self.sems.at[1, j], self.sems.at[2, j], p.below)),
        )

    def start(self):
        for needed, copy in self.relays(self.place.tp):
            pl.when(needed)(copy.start)

    def step(self, k):
        j = self.place.nth_block(k)
        relays = self.relays(j)
        relays[0][1].wait_recv()
        for needed, copy in relays:
            pl.when(needed)(copy.start)

    def finish(self):
        for j in range(self.place.tps):
            for needed, copy in self.relays(j):
                pl.when(needed)(copy.wait_send)


class Reduce:
    KINDS = 14 + 4 + Spread.KINDS + 2

    def __init__(self, place, grads, halves, firsts, seconds, lines, extras, totals, sems):
        self.place, self.grads, self.totals, self.sems = place, grads, totals, sems
        self.halves, self.firsts, self.seconds, self.lines, self.extras = halves, firsts, seconds, lines, extras
        self.unit = [ref.shape[1] // 8 for ref in grads]

    def sem(self, kind, g, j):
        return self.sems.at[kind, g, j]

    def span(self, g, stage, kept):
        p, unit = self.place, self.unit[g]
        if stage == 0:
            return (p.core if kept else 1 - p.core) * 4 * unit, 4
        if stage == 1:
            return (p.core * 4 + (p.first_bit if kept else 1 - p.first_bit) * 2) * unit, 2
        bit = p.second_bit if kept else 1 - p.second_bit
        return (p.core * 4 + p.first_bit * 2 + bit) * unit, 1

    def region(self, g, j, stage, kept):
        start, units = self.span(g, stage, kept)
        return rows_of(self.grads[g], j, start, units * self.unit[g])

    def landing(self, g, j, stage):
        return (self.halves, self.firsts, self.seconds)[stage][g].at[j]

    def copies_of(self, g, j, stage):
        device = (self.place.sibling, self.place.first, self.place.second)[stage]
        start, units = self.span(g, stage, False)
        unit, base = self.unit[g], (0, 8, 12)[stage]
        return [
            push(
                rows_of(self.grads[g], j, start + u * unit, unit),
                self.landing(g, j, stage).at[pl.ds(u * unit, unit)],
                self.sem(base + 2 * u, g, j), self.sem(base + 2 * u + 1, g, j), device,
            )
            for u in range(units)
        ]

    def step(self, g, j, stage):
        if stage > 0:
            for copy in self.copies_of(g, j, stage - 1):
                copy.wait_recv()
            add_into(self.region(g, j, stage - 1, True), self.landing(g, j, stage - 1))
        if stage < 3:
            for copy in self.copies_of(g, j, stage):
                copy.start()

    def piece(self, g, j):
        return self.region(g, j, 2, True)

    def line_slot(self, g, j, upward, target):
        size = self.place.tps
        if upward:
            return self.lines[g].at[j]
        gap = j - target
        own = 1 - (gap * gap + size * size - 1) // (size * size)
        return self.lines[g].at[j + own * (size - j)]

    def hop(self, g, j, upward, lands=False):
        p = self.place
        way = 0 if upward else 1
        target = p.tp if lands else (p.tp + 1 if upward else p.tp - 1)
        return push(
            self.piece(g, j), self.line_slot(g, j, upward, target),
            self.sem(14 + 2 * way, g, j), self.sem(15 + 2 * way, g, j), p.above if upward else p.below,
        )

    def travel(self, g, k):
        p = self.place
        for upward in (True, False):
            j = p.tps - 1 - k if upward else k
            has_source = p.has_below if upward else p.has_above
            involved = j >= p.tp if upward else j <= p.tp
            passes = j > p.tp if upward else j < p.tp

            @pl.when(jnp.logical_and(involved, has_source))
            def _():
                self.hop(g, j, upward, lands=True).wait_recv()
                add_into(self.piece(g, j), self.line_slot(g, j, upward, p.tp))

            pl.when(passes)(self.hop(g, j, upward).start)

    def copies(self, g, step):
        p = self.place
        return push(
            self.piece(g, p.tp), self.extras[g].at[step], self.sem(self.KINDS - 2, g, step), self.sem(self.KINDS - 1, g, step), p.copy_of(step)
        )

    def among_copies(self, g):
        p = self.place
        if p.extra > 1:
            for step in range(1, p.extra):
                self.copies(g, step).start()
            total = self.piece(g, p.tp)[...].astype(F32)
            for step in range(1, p.extra):
                self.copies(g, step).wait()
                total = total + self.extras[g][step].astype(F32)
            self.piece(g, p.tp)[...] = total.astype(BF16)

    def spread(self, g):
        return Spread(
            self.place,
            lambda start, count: self.totals[g].at[pl.ds(pl.multiple_of(start, 16), count)],
            self.unit[g],
            lambda kind: self.sems.at[18 + kind, g, 0],
        )

    def settle(self, g):
        self.among_copies(g)
        copy_into(self.spread(g).own(), self.piece(g, self.place.tp))
        self.spread(g).step(0)

    def share(self, g, stage):
        self.spread(g).step(stage)

    def finish(self, g):
        p = self.place
        for j in range(p.tps):
            for stage in range(3):
                for copy in self.copies_of(g, j, stage):
                    copy.wait_send()
            pl.when(j > p.tp)(self.hop(g, j, True).wait_send)
            pl.when(j < p.tp)(self.hop(g, j, False).wait_send)
        self.spread(g).finish()


class SumSmall:
    SLOTS = 12

    def __init__(self, place, slots, sems):
        self.place, self.slots, self.sems = place, slots, sems

    def move(self, source, device):
        return push(
            self.slots.at[source], self.slots.at[source + 1], self.sems.at[source], self.sems.at[source + 1], device
        )

    def pair(self, stage):
        p = self.place
        return self.move(2 * stage, (p.sibling, p.first, p.second)[stage])

    def start(self):
        p = self.place
        for there, slot in ((p.has_below, 7), (p.has_above, 9)):

            @pl.when(jnp.logical_not(there))
            def _():
                self.slots[slot] = jnp.zeros(self.slots.shape[1:], F32)

        self.pair(0).start()

    def exchange(self, stage):
        self.pair(stage).wait_recv()
        value = self.slots[2 * stage] + self.slots[2 * stage + 1]
        if stage < 2:
            self.slots[2 * stage + 2] = value
            self.pair(stage + 1).start()
        else:
            self.slots[10] = value

    def among_copies(self):
        p = self.place
        base = self.SLOTS
        for step in range(1, p.extra):
            self.copies(step).start()
        for step in range(1, p.extra):
            self.copies(step).wait()
        if p.extra > 1:
            total = self.slots[10]
            for step in range(1, p.extra):
                total = total + self.slots[base + step]
            self.slots[11] = total
        else:
            self.slots[11] = self.slots[10]

    def copies(self, step):
        base = self.SLOTS
        return push(
            self.slots.at[10], self.slots.at[base + step],
            self.sems.at[base + 2 * step], self.sems.at[base + 2 * step + 1], self.place.copy_of(step),
        )

    def line(self, k):
        p = self.place
        last = p.tps - 1
        for slot, turn, device in ((6, k, p.above), (8, last - k, p.below)):

            @pl.when(p.tp == turn)
            def _():
                if k > 0:
                    self.move(slot, device).wait_recv()
                if k < last:
                    self.slots[slot] = self.slots[slot + 1] + self.slots[11]
                    self.move(slot, device).start()

    def total(self):
        return self.slots[11] + self.slots[7] + self.slots[9]

    def finish(self):
        p = self.place
        for stage in range(3):
            self.pair(stage).wait_send()
        pl.when(p.has_above)(self.move(6, p.above).wait_send)
        pl.when(p.has_below)(self.move(8, p.below).wait_send)


def dot_nn(left, right):
    return lax.dot_general(left, right, (((1,), (0,)), ((), ())), preferred_element_type=F32)


def dot_nt(left, right):
    return lax.dot_general(left, right, (((1,), (1,)), ((), ())), preferred_element_type=F32)


def dot_tn(left, right):
    return lax.dot_general(left, right, (((0,), (0,)), ((), ())), preferred_element_type=F32)


def column(axis, shape):
    return lax.broadcasted_iota(jnp.int32, shape, axis)


def each(count, step):

    def run(i, carry):
        step(i)
        return carry

    lax.fori_loop(0, count, run, 0)


CHUNK = 64
CUBE = 0.044715
ROOT = 0.7978845608028654


def layer_kernel(names, *refs):
    r = dict(zip(names, refs))
    r["a2"], r["a3"], r["e"] = (r["memory"].at[i] for i in range(3))
    place = Place()
    n = place.tps
    x, model = r["x"], r["x"].shape[1]
    owned = x.shape[0]
    sentences = owned // LEN
    local = r["c1"].shape[1]
    heads_here = local // HD
    units = r["hidden"].shape[1]
    layers = r["memory"].shape[0]
    weights = [r["w%d" % i] for i in range(4)]
    lengths, sources, configs = r["lengths"], r["src_lengths"], r["configs"]
    width, heads, hidden_units, depth = (configs[0, i] for i in range(4))
    inv_width = 1.0 / jnp.full((1, 1), width.astype(F32))
    inv_depth = 1.0 / jnp.full((1, 1), depth.astype(F32))
    width_mask = (column(1, (1, model)) < width).astype(F32)

    local_sem = r["local_sems"]
    spots = (
        (0, 0, 3 * local), (0, 3 * local, local),
        (1, 0, local), (1, local, 2 * local), (1, 3 * local, local),
        (2, 0, weights[2].shape[1]), (3, 0, weights[3].shape[1]),
    )
    fills = [
        (g, pltpu.make_async_copy(r["in%d" % i], weights[g].at[place.tp, pl.ds(start, size)], local_sem.at[i]))
        for i, (g, start, size) in enumerate(spots)
    ]
    loads = [
        pltpu.make_async_copy(r[name + "_in"], r[name], local_sem.at[7 + i])
        for i, name in enumerate(("x", "memory", "upstream"))
    ]
    for _, copy in fills[:2]:
        copy.start()
    loads[0].start()
    for _, copy in fills[2:]:
        copy.start()
    loads[1].start()
    loads[2].start()
    r["bias"][place.tp] = jnp.broadcast_to(r["bias_in"][...], r["bias"].shape[1:])
    place.barrier()

    gather = Gather(place, weights, r["gather_sems"])
    bias = Line(place, r["bias"], r["bias_sems"])
    for g in range(4):
        for group, copy in fills:
            if group == g:
                copy.wait()
        gather.start(g)
        if g == 0:
            bias.start()
    order = [(g, k) for g in (0, 1) for k in range(n - 1)] + [(g, k) for k in range(n - 1) for g in (2, 3)]

    def g_tick(tick):
        for stage in range(4):
            if 0 <= tick - stage < len(order):
                gather.step(*order[tick - stage], stage)

    def block(k):
        later = (k + n - 1) // n
        return (1 - later) * place.tp + later * place.nth_block(k - 1)

    def hooks(table, k, b):
        for (kk, bb), steps in table.items():

            @pl.when(jnp.logical_and(k == kk, b == bb))
            def _():
                for step in steps:
                    step()

    def chunk(i):
        return pl.ds(pl.multiple_of(i * CHUNK, CHUNK), CHUNK)

    def keep_of(i):
        per = LEN // CHUNK
        spot = column(0, (CHUNK, 1)) + (i % per) * CHUNK
        return (spot < lengths[place.tp * sentences + i // per]).astype(F32) * width_mask

    def norm_parts(rows):
        mean = jnp.sum(rows * width_mask, axis=-1, keepdims=True) * inv_width
        centred = (rows - mean) * width_mask
        spread = jnp.sum(centred * centred, axis=-1, keepdims=True) * inv_width
        rstd = lax.rsqrt(spread + EPSILON)
        return centred * rstd, rstd

    def norm(rows, which):
        hat, _ = norm_parts(rows)
        return ((hat * r["gains"][which:which + 1] + r["shifts"][which:which + 1]) * width_mask).astype(BF16)

    def fold(values):
        return jnp.sum(values.reshape(values.shape[0] // 8, 8, values.shape[1]), axis=0)

    def norm_backward(rows, which, upstream):
        hat, rstd = norm_parts(rows)
        upstream = upstream * width_mask
        sums = r["norm_sums"]
        sums[which] = sums[which] + fold(upstream * hat)
        sums[3 + which] = sums[3 + which] + fold(upstream)
        scaled = upstream * r["gains"][which:which + 1]
        first = jnp.sum(scaled, axis=-1, keepdims=True) * inv_width
        second = jnp.sum(scaled * hat, axis=-1, keepdims=True) * inv_width
        return (rstd * (scaled - first - hat * second)) * width_mask

    chunks = owned // CHUNK
    acc, da, dh = r["acc"], r["da"], r["dh"]
    zeros = jnp.zeros((CHUNK, model), F32)
    r["norm_sums"][...] = jnp.zeros(r["norm_sums"].shape, F32)
    r["bias_sums"][...] = jnp.zeros(r["bias_sums"].shape, F32)

    def sentence(b):
        return pl.ds(pl.multiple_of(b * LEN, LEN), LEN)

    def head_keep(j, h):
        return jnp.where(j * heads_here + h < heads, 1.0, 0.0).astype(F32)

    def causal(b):
        return jnp.where(column(0, (LEN, LEN)) <= column(1, (LEN, LEN)), 0.0, NEGATIVE).astype(F32)

    def crossing(b):
        there = column(0, (LEN, 1)) < sources[place.tp * sentences + b]
        return jnp.where(there, 0.0, NEGATIVE).astype(F32)

    def bands(h):
        return [pl.ds(i * local + h * HD, HD) for i in range(3)]

    def lanes(b):
        return pl.ds(b * LEN, LEN)

    pairs = [(b, h) for b in range(sentences) for h in range(heads_here)]

    def attend(k, table, g, suffix, query_rows, key_rows, barred):
        w, t, c, p = weights[g], r["t" + suffix], r["c" + suffix], r["p" + suffix]
        j = block(k)
        hooks(table, k, 0)
        if query_rows is key_rows:
            t[j] = dot_nt(w[j, :3 * local], query_rows[...]).astype(BF16)
        else:
            t[j, :local] = dot_nt(w[j, :local], query_rows[...]).astype(BF16)
            t[j, local:] = dot_nt(w[j, local:3 * local], key_rows[...]).astype(BF16)
        for b, h in pairs:
            query, keys, values = (t[j, band, lanes(b)] for band in bands(h))
            scores = dot_tn(keys, query) + barred(b)
            raised = jnp.exp2((scores - jnp.max(scores, axis=0, keepdims=True)) * (SCALE * LOG2E))
            shares = (raised * (1.0 / jnp.sum(raised, axis=0, keepdims=True))).astype(BF16)
            p[j, b * heads_here + h] = shares
            c[j, pl.ds(h * HD, HD), lanes(b)] = (dot_nn(values, shares) * head_keep(j, h)).astype(BF16)
        hooks(table, k, 1)
        for b in range(sentences):
            rows = sentence(b)
            acc[rows] = acc[rows] + dot_tn(c[j, :, lanes(b)], w[j, 3 * local:])

    def attend_backward(k, table, g, suffix, query_rows, key_rows):
        w, t, c, p = weights[g], r["t" + suffix], r["c" + suffix], r["p" + suffix]
        j = block(k)
        e, dt, dc = r["e"], r["dt"], r["dc"]
        dc_all = dot_nt(w[j, 3 * local:], e[...])
        for h in range(heads_here):
            dc[h * HD:(h + 1) * HD] = (dc_all[h * HD:(h + 1) * HD] * head_keep(j, h)).astype(BF16)
        for b, h in pairs:
            (query, keys, values), (dq, dk, dv) = (t[j, band, lanes(b)] for band in bands(h)), bands(h)
            dc_h = dc[h * HD:(h + 1) * HD, lanes(b)]
            shares = p[j, b * heads_here + h]
            wide = shares.astype(F32)
            dp = dot_tn(values, dc_h)
            ds = (wide * (dp - jnp.sum(dp * wide, axis=0, keepdims=True))).astype(BF16)
            dt[dv, lanes(b)] = dot_nt(dc_h, shares).astype(BF16)
            dt[dq, lanes(b)] = (dot_nn(keys, ds) * SCALE).astype(BF16)
            dt[dk, lanes(b)] = (dot_nt(query, ds) * SCALE).astype(BF16)
        hooks(table, k, 1)
        gather.drain(g, j)
        own = query_rows is key_rows
        for b in range(sentences):
            rows = sentence(b)
            if own:
                da[rows] = da[rows] + dot_tn(dt[:, lanes(b)], w[j, :3 * local])
            else:
                da[rows] = da[rows] + dot_tn(dt[:local, lanes(b)], w[j, :local])
                r["dm"][rows] = r["dm"][rows] + dot_tn(dt[local:, lanes(b)], w[j, local:3 * local])
        if own:
            w[j, :3 * local] = dot_nn(dt[...], query_rows[...]).astype(BF16)
        else:
            w[j, :local] = dot_nn(dt[:local], query_rows[...]).astype(BF16)
            w[j, local:3 * local] = dot_nn(dt[local:], key_rows[...]).astype(BF16)
        w[j, 3 * local:] = dot_nn(c[j], e[...]).astype(BF16)

    def feed(k, table):
        j = block(k)
        w_up, w_down = weights[2], weights[3]
        unit_mask = (column(1, (1, units)) + j * units < hidden_units).astype(F32)

        def one(b):
            hooks(table, k, b)
            rows = sentence(b)
            before = dot_nn(r["a3"][rows], w_up[j]) + r["bias"][j, 0:1]
            square = before * before
            bent = jnp.tanh(ROOT * before * (1.0 + CUBE * square))
            half = 0.5 * (1.0 + bent)
            g = (before * half * unit_mask).astype(BF16)
            slope = (half + 0.5 * before * (1.0 - bent * bent) * (ROOT + 3.0 * CUBE * ROOT * square)) * unit_mask
            r["hidden"][rows] = g
            acc[rows] = acc[rows] + dot_nn(g, w_down[j])
            du = (dot_nt(r["e"][rows], w_down[j]) * slope).astype(BF16)
            r["dhidden"][rows] = du
            r["bias_sums"][j] = r["bias_sums"][j] + fold(du.astype(F32))
            da[rows] = da[rows] + dot_nt(du, w_up[j])

        each(sentences, one)
        gather.drain(2, j)
        gather.drain(3, j)

        def down(i):
            part = pl.ds(pl.multiple_of(i * 128, 128), 128)
            w_down[j, part] = dot_tn(r["hidden"][:, part], r["e"][...]).astype(BF16)

        def up(i):
            part = pl.ds(pl.multiple_of(i * 128, 128), 128)
            w_up[j, part] = dot_tn(r["a3"][:, part], r["dhidden"][...]).astype(BF16)

        each(units // 128, down)
        each(model // 128, up)

    loads[0].wait()

    def begin(i):
        rows = chunk(i)
        r["a1"][rows] = norm(x[rows].astype(F32), 0)
        acc[rows] = zeros
        da[rows] = zeros
        r["dm"][rows] = zeros

    each(chunks, begin)
    g_tick(0)
    loads[1].wait()

    def mix(i):
        rows = chunk(i)
        total = jnp.zeros((CHUNK, model), F32)
        for level in range(layers):
            chosen = (jnp.full((1, 1), depth) >= layers - level).astype(F32)
            total = total + chosen * r["memory"][level, rows].astype(F32)
        r["m"][rows] = (total * inv_depth * width_mask).astype(BF16)

    each(chunks, mix)
    loads[2].wait()
    r["out_sums"][...] = jnp.zeros(r["out_sums"].shape, F32)

    def grad_in(i):
        rows = chunk(i)
        masked = r["upstream"][rows].astype(F32) * keep_of(i)
        r["out_sums"][...] = r["out_sums"][...] + fold(masked)
        r["e"][rows] = masked.astype(BF16)

    each(chunks, grad_in)

    def ticks(*numbers):
        return [functools.partial(g_tick, i) for i in numbers]

    others = n - 1
    assert n == 4
    table = {
        (0, 1): ticks(1),
        (1, 0): ticks(2, 3) + [functools.partial(bias.step, 0)],
        (2, 0): ticks(4) + [functools.partial(bias.step, 1)],
        (3, 0): ticks(5) + [functools.partial(bias.step, 2)],
    }
    each(n, lambda k: attend(k, table, 0, "1", r["a1"], r["a1"], causal))

    def after_self(i):
        rows = chunk(i)
        h = x[rows].astype(F32) + acc[rows] * keep_of(i)
        r["h1"][rows] = h
        r["a2"][rows] = norm(h, 1)
        acc[rows] = zeros

    each(chunks, after_self)
    table2 = {(k, 0): ticks(6 + k) for k in range(n)}
    each(n, lambda k: attend(k, table2, 1, "2", r["a2"], r["m"], crossing))

    def after_cross(i):
        rows = chunk(i)
        h = r["h1"][rows] + acc[rows] * keep_of(i)
        r["h2"][rows] = h
        r["a3"][rows] = norm(h, 2)
        acc[rows] = zeros

    each(chunks, after_cross)

    reduce = Reduce(
        place, weights, *([r["%s%d" % (name, i)] for i in range(4)] for name in
                          ("half", "first", "second", "line", "extra", "total")), r["reduce_sems"],
    )
    plan = {}

    def add(tick, order, step, *args):
        plan.setdefault(tick, []).append((order, len(plan.get(tick, ())), functools.partial(step, *args)))

    def r_tick(tick):
        for _, _, step in sorted(plan.get(tick, ()), key=lambda entry: entry[:2]):
            step()

    def store(g):
        return pltpu.make_async_copy(r["total%d" % g], r["out%d" % g], local_sem.at[10 + g])

    starts = {3: [2 * k + 1 for k in range(n)], 2: [2 * k + 1 for k in range(n)]}
    starts[1] = [10 + 2 * k for k in range(n)]
    starts[0] = [19 + 2 * k for k in range(n)]
    for late, g in enumerate((3, 2, 1, 0)):
        for k, tick in enumerate(starts[g]):
            for stage in range(4):
                add(tick + stage, stage, reduce.step, g, block(k), stage)
        last = starts[g][-1] + 3
        for k in range(n - 1):
            add(last + 1 + k, 10 - late, reduce.travel, g, k)
        add(last + n, 20 - late, reduce.settle, g)
        for stage in (1, 2, 3):
            add(last + n + stage, 30 + stage - late, reduce.share, g, stage)
        add(last + n + 3, 50, lambda g=g: store(g).start())

    def reduce_ticks(*numbers):
        return [functools.partial(r_tick, i) for i in numbers]

    def at_end(k, numbers):
        for kk, number in enumerate(numbers):

            @pl.when(k == kk)
            def _():
                r_tick(number)

    table3 = {(0, 0): ticks(10), (0, 1): ticks(11), (1, 1): ticks(12) + reduce_ticks(2),
              (2, 1): ticks(13) + reduce_ticks(4), (3, 0): ticks(14), (3, 1): reduce_ticks(6)}

    def feed_step(k):
        feed(k, table3)
        at_end(k, [2 * i + 1 for i in range(n)])

    each(n, feed_step)
    r_tick(8)
    out_copy = pltpu.make_async_copy(acc, r["layer_out"], local_sem.at[14])

    def after_feed(i):
        rows = chunk(i)
        keep = keep_of(i)
        acc[rows] = r["h2"][rows] + (acc[rows] + r["bias_out"][...]) * keep
        down = r["upstream"][rows].astype(F32) + norm_backward(r["h2"][rows], 2, da[rows])
        dh[rows] = down
        r["e"][rows] = (down * keep).astype(BF16)
        da[rows] = zeros

    each(chunks, after_feed)
    out_copy.start()
    table4 = {(k, 1): reduce_ticks(9 + 2 * k) for k in range(n)}

    def cross_step(k):
        attend_backward(k, table4, 1, "2", r["a2"], r["m"])
        at_end(k, [10 + 2 * i for i in range(n)])

    each(n, cross_step)
    memory_copy = pltpu.make_async_copy(r["dm"], r["memory_out"], local_sem.at[15])
    memory_copy.start()

    def before_cross(i):
        rows = chunk(i)
        down = dh[rows] + norm_backward(r["h1"][rows], 1, da[rows])
        dh[rows] = down
        r["e"][rows] = (down * keep_of(i)).astype(BF16)
        da[rows] = zeros

    each(chunks, before_cross)
    r_tick(17)
    table5 = {(k, 1): reduce_ticks(18 + 2 * k) for k in range(n)}

    def self_step(k):
        attend_backward(k, table5, 0, "1", r["a1"], r["a1"])
        at_end(k, [19 + 2 * i for i in range(n)])

    each(n, self_step)

    def before_self(i):
        rows = chunk(i)
        dh[rows] = dh[rows] + norm_backward(x[rows].astype(F32), 0, da[rows])

    each(chunks, before_self)
    grad_copy = pltpu.make_async_copy(dh, r["input_grad"], local_sem.at[16])
    grad_copy.start()

    small = SumSmall(place, r["slots"], r["small_sems"])

    def small_start():
        own = r["slots"].at[0]
        own[...] = jnp.zeros(own.shape, F32)
        for i in range(6):
            own[i:i + 1, :model] = jnp.sum(r["norm_sums"][i], axis=0, keepdims=True)
        own[6:7, :model] = jnp.sum(r["out_sums"][...], axis=0, keepdims=True)
        tokens = lengths[place.tp * sentences]
        for b in range(1, sentences):
            tokens = tokens + lengths[place.tp * sentences + b]
        own[7:8] = jnp.full((1, own.shape[1]), tokens.astype(F32))
        for i in range(n):
            own[8 + i:9 + i] = jnp.sum(r["bias_sums"][i], axis=0, keepdims=True)
        small.start()

    add(26, 5, small_start)
    for stage in range(3):
        add(27 + stage, 5, small.exchange, stage)
    add(30, 4, small.among_copies)
    for k in range(n):
        add(30 + k, 5, small.line, k)
    final = max(plan)
    for tick in range(26, final + 1):
        r_tick(tick)
    r["small_out"][...] = small.total()
    bias.finish()
    for copy in (out_copy, memory_copy, grad_copy):
        copy.wait()
    for g in range(4):
        reduce.finish(g)
        store(g).wait()
    small.finish()


def run_layer(args, weights):
    lengths, src_lengths, configs, gains, shifts, bias_in, bias_out, x, memory, upstream = args
    n, extra = lax.axis_size("tp"), lax.axis_size("dp") // 2
    owned, model = x.shape
    local, units = weights[1].shape[0], bias_in.shape[1]
    small = (16, units)
    assert n <= 8 and units >= model
    shapes = [(n, 4 * local, model)] * 2 + [(n,) + weights[5].shape, (n,) + weights[6].shape]
    scratch = {}

    def vmem(name, shape, dtype=BF16):
        scratch[name] = pltpu.VMEM(shape, dtype)

    def dma(name, *shape):
        scratch[name] = pltpu.SemaphoreType.DMA(shape)

    for i, shape in enumerate(shapes):
        vmem("w%d" % i, shape)
    vmem("bias", (n, 8, units), F32)
    vmem("x", x.shape)
    vmem("memory", memory.shape)
    vmem("upstream", upstream.shape)
    assert memory.shape[0] >= 3
    for name in ("a1", "m"):
        vmem(name, (owned, model))
    for name in ("h1", "h2", "dh", "acc", "da", "dm"):
        vmem(name, (owned, model), F32)
    for suffix in ("1", "2"):
        vmem("t" + suffix, (n, 3 * local, owned))
        vmem("c" + suffix, (n, local, owned))
        vmem("p" + suffix, (n, owned // LEN * (local // HD), LEN, LEN))
    vmem("dt", (3 * local, owned))
    vmem("dc", (local, owned))
    vmem("hidden", (owned, units))
    vmem("dhidden", (owned, units))
    vmem("bias_sums", (n, 8, units), F32)
    vmem("norm_sums", (6, 8, model), F32)
    vmem("out_sums", (8, model), F32)
    for i, (_, rows, columns) in enumerate(shapes):
        vmem("half%d" % i, (n, rows // 2, columns))
        vmem("first%d" % i, (n, rows // 4, columns))
        vmem("second%d" % i, (n, rows // 8, columns))
        vmem("line%d" % i, (n + 1, rows // 8, columns))
        vmem("extra%d" % i, (extra, rows // 8, columns))
        vmem("total%d" % i, (rows, columns))
    vmem("slots", (SumSmall.SLOTS + extra,) + small, F32)
    dma("gather_sems", Gather.KINDS, 4, n)
    dma("bias_sems", 3, n)
    dma("reduce_sems", Reduce.KINDS, 4, max(n, extra))
    dma("small_sems", SumSmall.SLOTS + 2 * extra)
    dma("local_sems", 17)
    outs = {
        "layer_out": (x.shape, F32), "input_grad": (x.shape, F32), "memory_out": (x.shape, F32),
        "out0": (shapes[0][1:], BF16), "out1": (shapes[1][1:], BF16), "out2": (shapes[2][1:], BF16), "out3": (shapes[3][1:], BF16),
        "small_out": (small, F32),
    }
    names = ["lengths", "src_lengths", "configs", "gains", "shifts", "bias_in", "bias_out", "x_in", "memory_in", "upstream_in"]
    names += ["in%d" % i for i in range(7)] + list(outs) + list(scratch)
    smem, vm, hbm = (pl.BlockSpec(memory_space=space) for space in (pltpu.SMEM, pltpu.VMEM, pl.ANY))
    flops = 6 * owned * model * (8 * n * local + 2 * n * units)
    return pl.pallas_call(
        functools.partial(layer_kernel, names),
        out_shape=[jax.ShapeDtypeStruct(*out) for out in outs.values()],
        in_specs=[smem] * 3 + [vm] * 4 + [hbm] * 10,
        out_specs=[hbm] * 7 + [vm],
        scratch_shapes=list(scratch.values()),
        compiler_params=pltpu.CompilerParams(collective_id=1, has_side_effects=True, vmem_limit_bytes=64 * 2**20),
        cost_estimate=pl.CostEstimate(flops=flops, bytes_accessed=40 * 2**20, transcendentals=0),
        name="layer",
    )(*args, *weights)


def per_device(
    inputs, memory, out_grad, lengths, src_lengths, configs, norm_gain, norm_bias,
    self_qkv, self_out, cross_q, cross_kv, cross_out, ffn_in, ffn_in_bias, ffn_out, ffn_out_bias,
):
    model = inputs.shape[1]
    layers = memory.shape[0]
    local = self_out.shape[0]
    units = ffn_in.shape[1]
    layer_out, input_grad, source_grad, first, second, third, fourth, small = run_layer(
        (lengths, src_lengths, configs, norm_gain, norm_bias, ffn_in_bias.reshape(1, units),
         ffn_out_bias.reshape(1, model), inputs, memory, out_grad),
        (self_qkv.transpose(1, 2, 0).reshape(3 * local, model), self_out, cross_q.T,
         cross_kv.transpose(1, 2, 0).reshape(2 * local, model), cross_out, ffn_in, ffn_out),
    )
    width_mask = (jnp.arange(model) < configs[0, 0]).astype(F32)
    chosen = (jnp.arange(layers) >= layers - configs[0, 3]).astype(F32) / configs[0, 3].astype(F32)
    memory_grad = chosen[:, None, None] * (source_grad * width_mask)[None]
    inverse = 1.0 / small[7, 0]
    small = small * inverse
    first, second, third, fourth = (block.astype(F32) * inverse for block in (first, second, third, fourth))
    return (
        layer_out,
        input_grad,
        memory_grad,
        small[:3, :model],
        small[3:6, :model],
        first[:3 * local].reshape(3, local, model).transpose(2, 0, 1),
        first[3 * local:],
        second[:local].T,
        second[local:3 * local].reshape(2, local, model).transpose(2, 0, 1),
        second[3 * local:],
        third,
        lax.dynamic_slice_in_dim(small, 8 + lax.axis_index("tp"), 1)[0],
        fourth,
        small[6, :model],
    )


def solution(mesh):
    rows = P(("grp", "dp", "tp"), None)
    stack = P(None, ("grp", "dp", "tp"), None)
    weights = (
        P(None, None, "tp"), P("tp", None), P(None, "tp"), P(None, None, "tp"), P("tp", None),
        P(None, "tp"), P("tp"), P("tp", None), P(),
    )
    return jax.shard_map(
        per_device,
        mesh=mesh,
        in_specs=(rows, stack, rows, P(("grp", "dp")), P(("grp", "dp")), P("grp", None), P(), P()) + weights,
        out_specs=(rows, rows, stack, P(), P()) + weights,
        check_vma=False,
    )
```

```python
import functools

import jax
import jax.numpy as jnp
from jax import lax
from jax.experimental import pallas as pl
from jax.experimental.pallas import tpu as pltpu
from jax.sharding import PartitionSpec as P

HD = 80
LEN = 256
EPSILON = 1e-05
NEGATIVE = -1e30
SCALE = HD ** (-0.5)
LOG2E = 1.4426950408889634
F32 = jnp.float32
BF16 = jnp.bfloat16


MESH = pl.DeviceIdType.MESH


class Place:
    def __init__(self):
        self.tps = lax.axis_size("tp")
        self.extra = lax.axis_size("dp") // 2
        assert lax.axis_size("grp") == 4 and lax.axis_size("dp") % 2 == 0
        grp, dp, tp = (lax.axis_index(name) for name in ("grp", "dp", "tp"))
        core, low, high = dp % 2, grp % 2, grp // 2
        flip_low, flip_high = grp + 1 - 2 * low, grp + 2 - 4 * high
        self.grp, self.dp, self.tp, self.core = grp, dp, tp, core
        self.first_bit = (1 - core) * low + core * high
        self.second_bit = (1 - core) * high + core * low
        self.first = ((1 - core) * flip_low + core * flip_high, dp, tp)
        self.second = ((1 - core) * flip_high + core * flip_low, dp, tp)
        self.sibling = (grp, dp + 1 - 2 * core, tp)
        self.above = (grp, dp, tp + 1)
        self.below = (grp, dp, tp - 1)
        self.has_above = tp < self.tps - 1
        self.has_below = tp > 0

    def copy_of(self, step):
        return (self.grp, ((self.dp // 2 + step) % self.extra) * 2 + self.core, self.tp)

    def nth_block(self, k):
        size = self.tps
        upper = (2 * self.tp) // size
        lead = (1 - upper) * self.tp + upper * (size - 1 - self.tp)
        spot = k + (k + size - lead) // size
        return (1 - upper) * spot + upper * (size - 1 - spot)

    def barrier(self):
        sem = pltpu.get_barrier_semaphore()
        fixed = [self.first, self.second, self.sibling] + [self.copy_of(s) for s in range(1, self.extra)]
        for device in fixed:
            pl.semaphore_signal(sem, inc=1, device_id=device, device_id_type=MESH)
        for there, device in ((self.has_above, self.above), (self.has_below, self.below)):

            @pl.when(there)
            def _():
                pl.semaphore_signal(sem, inc=1, device_id=device, device_id_type=MESH)

        size = self.tps
        ends = (self.tp + size - 1) // size + (2 * size - 2 - self.tp) // size
        pl.semaphore_wait(sem, len(fixed) + ends)


def push(src, dst, send_sem, recv_sem, device):
    return pltpu.make_async_remote_copy(
        src_ref=src, dst_ref=dst, send_sem=send_sem, recv_sem=recv_sem, device_id=device, device_id_type=MESH
    )


def rows_of(ref, lead, start, count):
    return ref.at[lead, pl.ds(pl.multiple_of(start, 16), count)]


def add_into(total, term):
    def step(i, carry):
        rows = pl.ds(pl.multiple_of(i * 16, 16), 16)
        total[rows] = total[rows] + term[rows]
        return carry

    lax.fori_loop(0, total.shape[0] // 16, step, 0)


def copy_into(total, term):

    def step(i, carry):
        rows = pl.ds(pl.multiple_of(i * 16, 16), 16)
        total[rows] = term[rows]
        return carry

    lax.fori_loop(0, total.shape[0] // 16, step, 0)


class Spread:
    KINDS = 14

    def __init__(self, place, view, unit, sems):
        self.place, self.view, self.unit, self.sems = place, view, unit, sems
        f, s, c = place.first_bit, place.second_bit, place.core
        self.units = (f * 2 + s, f * 2 + 1 - s, (1 - f) * 2 + s, (1 - f) * 2 + 1 - s)
        self.theirs = (s * 2 + f, s * 2 + 1 - f, (1 - s) * 2 + f, (1 - s) * 2 + 1 - f)
        self.table = [
            (place.second, (c, self.units[0]), (c, self.units[1])),
            (place.first, (c, self.units[0]), (c, self.units[2])),
            (place.first, (c, self.units[1]), (c, self.units[3])),
        ] + [(place.sibling, (c, u), (1 - c, t)) for u, t in zip(self.units, self.theirs)]

    def region(self, spot):
        half, unit = spot
        return self.view((half * 4 + unit) * self.unit, self.unit)

    def own(self):
        return self.region((self.place.core, self.units[0]))

    def copy(self, n, lands=False):
        device, leaves, landing = self.table[n]
        part = self.region(landing if lands else leaves)
        return push(part, part, self.sems(2 * n), self.sems(2 * n + 1), device)

    WAITS = ((), (0,), (1, 2), (3, 4, 5, 6))
    SENDS = ((0, 1, 3), (2, 4), (5, 6), ())

    def step(self, stage):
        for n in self.WAITS[stage]:
            self.copy(n, lands=True).wait_recv()
        for n in self.SENDS[stage]:
            self.copy(n).start()

    def finish(self):
        for n in range(7):
            self.copy(n).wait_send()


class Gather:
    KINDS = Spread.KINDS + 3

    def __init__(self, place, buffers, sems):
        self.place, self.buffers, self.sems = place, buffers, sems
        self.unit = [ref.shape[1] // 8 for ref in buffers]
        self.others = place.tps - 1

    def spread(self, g, j):
        return Spread(
            self.place,
            lambda start, count: rows_of(self.buffers[g], j, start, count),
            self.unit[g],
            lambda kind: self.sems.at[kind, g, j],
        )

    def relays(self, g, j):
        p = self.place
        part = self.spread(g, j).own()
        sem = lambda n: self.sems.at[Spread.KINDS + n, g, j]
        return (
            (jnp.logical_and(j <= p.tp, p.has_above), push(part, part, sem(0), sem(2), p.above)),
            (jnp.logical_and(j >= p.tp, p.has_below), push(part, part, sem(1), sem(2), p.below)),
        )

    def start(self, g):
        for needed, copy in self.relays(g, self.place.tp):
            pl.when(needed)(copy.start)

    def step(self, g, k, stage):
        j = self.place.nth_block(k)
        if stage == 0:
            relays = self.relays(g, j)
            relays[0][1].wait_recv()
            for needed, copy in relays:
                pl.when(needed)(copy.start)
        self.spread(g, j).step(stage)

    def drain(self, g, j):
        for needed, copy in self.relays(g, j):
            pl.when(needed)(copy.wait_send)

        @pl.when(j != self.place.tp)
        def _():
            self.spread(g, j).finish()


class Line:
    def __init__(self, place, buffer, sems):
        self.place, self.buffer, self.sems = place, buffer, sems

    def relays(self, j):
        p = self.place
        part = self.buffer.at[j]
        return (
            (jnp.logical_and(j <= p.tp, p.has_above), push(part, part, self.sems.at[0, j], self.sems.at[2, j], p.above)),
            (jnp.logical_and(j >= p.tp, p.has_below), push(part, part, self.sems.at[1, j], self.sems.at[2, j], p.below)),
        )

    def start(self):
        for needed, copy in self.relays(self.place.tp):
            pl.when(needed)(copy.start)

    def step(self, k):
        j = self.place.nth_block(k)
        relays = self.relays(j)
        relays[0][1].wait_recv()
        for needed, copy in relays:
            pl.when(needed)(copy.start)

    def finish(self):
        for j in range(self.place.tps):
            for needed, copy in self.relays(j):
                pl.when(needed)(copy.wait_send)


class Reduce:
    KINDS = 14 + 4 + Spread.KINDS + 2

    def __init__(self, place, grads, halves, firsts, seconds, lines, extras, totals, sems):
        self.place, self.grads, self.totals, self.sems = place, grads, totals, sems
        self.halves, self.firsts, self.seconds, self.lines, self.extras = halves, firsts, seconds, lines, extras
        self.unit = [ref.shape[1] // 8 for ref in grads]

    def sem(self, kind, g, j):
        return self.sems.at[kind, g, j]

    def span(self, g, stage, kept):
        p, unit = self.place, self.unit[g]
        if stage == 0:
            return (p.core if kept else 1 - p.core) * 4 * unit, 4
        if stage == 1:
            return (p.core * 4 + (p.first_bit if kept else 1 - p.first_bit) * 2) * unit, 2
        bit = p.second_bit if kept else 1 - p.second_bit
        return (p.core * 4 + p.first_bit * 2 + bit) * unit, 1

    def region(self, g, j, stage, kept):
        start, units = self.span(g, stage, kept)
        return rows_of(self.grads[g], j, start, units * self.unit[g])

    def landing(self, g, j, stage):
        return (self.halves, self.firsts, self.seconds)[stage][g].at[j]

    def copies_of(self, g, j, stage):
        device = (self.place.sibling, self.place.first, self.place.second)[stage]
        start, units = self.span(g, stage, False)
        unit, base = self.unit[g], (0, 8, 12)[stage]
        return [
            push(
                rows_of(self.grads[g], j, start + u * unit, unit),
                self.landing(g, j, stage).at[pl.ds(u * unit, unit)],
                self.sem(base + 2 * u, g, j), self.sem(base + 2 * u + 1, g, j), device,
            )
            for u in range(units)
        ]

    def step(self, g, j, stage):
        if stage > 0:
            for copy in self.copies_of(g, j, stage - 1):
                copy.wait_recv()
            add_into(self.region(g, j, stage - 1, True), self.landing(g, j, stage - 1))
        if stage < 3:
            for copy in self.copies_of(g, j, stage):
                copy.start()

    def piece(self, g, j):
        return self.region(g, j, 2, True)

    def line_slot(self, g, j, upward, target):
        size = self.place.tps
        if upward:
            return self.lines[g].at[j]
        gap = j - target
        own = 1 - (gap * gap + size * size - 1) // (size * size)
        return self.lines[g].at[j + own * (size - j)]

    def hop(self, g, j, upward, lands=False):
        p = self.place
        way = 0 if upward else 1
        target = p.tp if lands else (p.tp + 1 if upward else p.tp - 1)
        return push(
            self.piece(g, j), self.line_slot(g, j, upward, target),
            self.sem(14 + 2 * way, g, j), self.sem(15 + 2 * way, g, j), p.above if upward else p.below,
        )

    def travel(self, g, step):
        p = self.place
        last = p.tps - 1
        for upward in (True, False):
            turn = p.tp if upward else last - p.tp
            j = p.tp + last - step if upward else p.tp - last + step

            @pl.when(jnp.logical_and(turn <= step, turn > 0))
            def _():
                self.hop(g, j, upward, lands=True).wait_recv()
                add_into(self.piece(g, j), self.line_slot(g, j, upward, p.tp))

            if step < last:
                pl.when(turn <= step)(self.hop(g, j, upward).start)

    def copies(self, g, step):
        p = self.place
        return push(
            self.piece(g, p.tp), self.extras[g].at[step], self.sem(self.KINDS - 2, g, step), self.sem(self.KINDS - 1, g, step), p.copy_of(step)
        )

    def among_copies(self, g):
        p = self.place
        if p.extra > 1:
            for step in range(1, p.extra):
                self.copies(g, step).start()
            total = self.piece(g, p.tp)[...].astype(F32)
            for step in range(1, p.extra):
                self.copies(g, step).wait()
                total = total + self.extras[g][step].astype(F32)
            self.piece(g, p.tp)[...] = total.astype(BF16)

    def spread(self, g):
        return Spread(
            self.place,
            lambda start, count: self.totals[g].at[pl.ds(pl.multiple_of(start, 16), count)],
            self.unit[g],
            lambda kind: self.sems.at[18 + kind, g, 0],
        )

    def settle(self, g):
        self.among_copies(g)
        copy_into(self.spread(g).own(), self.piece(g, self.place.tp))
        self.spread(g).step(0)

    def share(self, g, stage):
        self.spread(g).step(stage)

    def finish(self, g):
        p = self.place
        for j in range(p.tps):
            for stage in range(3):
                for copy in self.copies_of(g, j, stage):
                    copy.wait_send()
            pl.when(j > p.tp)(self.hop(g, j, True).wait_send)
            pl.when(j < p.tp)(self.hop(g, j, False).wait_send)
        self.spread(g).finish()


class SumSmall:
    SLOTS = 12

    def __init__(self, place, slots, sems):
        self.place, self.slots, self.sems = place, slots, sems

    def move(self, source, device):
        return push(
            self.slots.at[source], self.slots.at[source + 1], self.sems.at[source], self.sems.at[source + 1], device
        )

    def pair(self, stage):
        p = self.place
        return self.move(2 * stage, (p.sibling, p.first, p.second)[stage])

    def start(self):
        p = self.place
        for there, slot in ((p.has_below, 7), (p.has_above, 9)):

            @pl.when(jnp.logical_not(there))
            def _():
                self.slots[slot] = jnp.zeros(self.slots.shape[1:], F32)

        self.pair(0).start()

    def exchange(self, stage):
        self.pair(stage).wait_recv()
        value = self.slots[2 * stage] + self.slots[2 * stage + 1]
        if stage < 2:
            self.slots[2 * stage + 2] = value
            self.pair(stage + 1).start()
        else:
            self.slots[10] = value

    def among_copies(self):
        p = self.place
        base = self.SLOTS
        for step in range(1, p.extra):
            self.copies(step).start()
        for step in range(1, p.extra):
            self.copies(step).wait()
        if p.extra > 1:
            total = self.slots[10]
            for step in range(1, p.extra):
                total = total + self.slots[base + step]
            self.slots[11] = total
        else:
            self.slots[11] = self.slots[10]

    def copies(self, step):
        base = self.SLOTS
        return push(
            self.slots.at[10], self.slots.at[base + step],
            self.sems.at[base + 2 * step], self.sems.at[base + 2 * step + 1], self.place.copy_of(step),
        )

    def line(self, k):
        p = self.place
        last = p.tps - 1
        for slot, turn, device in ((6, k, p.above), (8, last - k, p.below)):

            @pl.when(p.tp == turn)
            def _():
                if k > 0:
                    self.move(slot, device).wait_recv()
                if k < last:
                    self.slots[slot] = self.slots[slot + 1] + self.slots[11]
                    self.move(slot, device).start()

    def total(self):
        return self.slots[11] + self.slots[7] + self.slots[9]

    def finish(self):
        p = self.place
        for stage in range(3):
            self.pair(stage).wait_send()
        pl.when(p.has_above)(self.move(6, p.above).wait_send)
        pl.when(p.has_below)(self.move(8, p.below).wait_send)


def dot_nn(left, right):
    return lax.dot_general(left, right, (((1,), (0,)), ((), ())), preferred_element_type=F32)


def dot_nt(left, right):
    return lax.dot_general(left, right, (((1,), (1,)), ((), ())), preferred_element_type=F32)


def dot_tn(left, right):
    return lax.dot_general(left, right, (((0,), (0,)), ((), ())), preferred_element_type=F32)


def column(axis, shape):
    return lax.broadcasted_iota(jnp.int32, shape, axis)


def each(count, step):

    def run(i, carry):
        step(i)
        return carry

    lax.fori_loop(0, count, run, 0)


CHUNK = 64
CUBE = 0.044715
ROOT = 0.7978845608028654


def layer_kernel(names, *refs):
    r = dict(zip(names, refs))
    r["a2"], r["a3"], r["e"] = (r["memory"].at[i] for i in range(3))
    place = Place()
    n = place.tps
    x, model = r["x"], r["x"].shape[1]
    owned = x.shape[0]
    sentences = owned // LEN
    local = r["c1"].shape[1]
    heads_here = local // HD
    units = r["hidden"].shape[1]
    layers = r["memory"].shape[0]
    weights = [r["w%d" % i] for i in range(4)]
    lengths, sources, configs = r["lengths"], r["src_lengths"], r["configs"]
    width, heads, hidden_units, depth = (configs[0, i] for i in range(4))
    inv_width = 1.0 / jnp.full((1, 1), width.astype(F32))
    inv_depth = 1.0 / jnp.full((1, 1), depth.astype(F32))
    width_mask = (column(1, (1, model)) < width).astype(F32)

    local_sem = r["local_sems"]
    spots = (
        (0, 0, 3 * local), (0, 3 * local, local),
        (1, 0, local), (1, local, 2 * local), (1, 3 * local, local),
        (2, 0, weights[2].shape[1]), (3, 0, weights[3].shape[1]),
    )
    fills = [
        (g, pltpu.make_async_copy(r["in%d" % i], weights[g].at[place.tp, pl.ds(start, size)], local_sem.at[i]))
        for i, (g, start, size) in enumerate(spots)
    ]
    loads = [
        pltpu.make_async_copy(r[name + "_in"], r[name], local_sem.at[7 + i])
        for i, name in enumerate(("x", "memory", "upstream"))
    ]
    for _, copy in fills[:2]:
        copy.start()
    loads[0].start()
    for _, copy in fills[2:]:
        copy.start()
    loads[1].start()
    loads[2].start()
    r["bias"][place.tp] = jnp.broadcast_to(r["bias_in"][...], r["bias"].shape[1:])
    place.barrier()

    gather = Gather(place, weights, r["gather_sems"])
    bias = Line(place, r["bias"], r["bias_sems"])
    for g in range(4):
        for group, copy in fills:
            if group == g:
                copy.wait()
        gather.start(g)
        if g == 0:
            bias.start()
    order = [(g, k) for g in (0, 1) for k in range(n - 1)] + [(g, k) for k in range(n - 1) for g in (2, 3)]

    def g_tick(tick):
        for stage in range(4):
            if 0 <= tick - stage < len(order):
                gather.step(*order[tick - stage], stage)

    def block(k):
        later = (k + n - 1) // n
        return (1 - later) * place.tp + later * place.nth_block(k - 1)

    def hooks(table, k, b):
        for (kk, bb), steps in table.items():

            @pl.when(jnp.logical_and(k == kk, b == bb))
            def _():
                for step in steps:
                    step()

    def chunk(i):
        return pl.ds(pl.multiple_of(i * CHUNK, CHUNK), CHUNK)

    def keep_of(i):
        per = LEN // CHUNK
        spot = column(0, (CHUNK, 1)) + (i % per) * CHUNK
        return (spot < lengths[place.tp * sentences + i // per]).astype(F32) * width_mask

    def norm_parts(rows):
        mean = jnp.sum(rows * width_mask, axis=-1, keepdims=True) * inv_width
        centred = (rows - mean) * width_mask
        spread = jnp.sum(centred * centred, axis=-1, keepdims=True) * inv_width
        rstd = lax.rsqrt(spread + EPSILON)
        return centred * rstd, rstd

    def norm(rows, which):
        hat, _ = norm_parts(rows)
        return ((hat * r["gains"][which:which + 1] + r["shifts"][which:which + 1]) * width_mask).astype(BF16)

    def fold(values):
        return jnp.sum(values.reshape(values.shape[0] // 8, 8, values.shape[1]), axis=0)

    def norm_backward(rows, which, upstream):
        hat, rstd = norm_parts(rows)
        upstream = upstream * width_mask
        sums = r["norm_sums"]
        sums[which] = sums[which] + fold(upstream * hat)
        sums[3 + which] = sums[3 + which] + fold(upstream)
        scaled = upstream * r["gains"][which:which + 1]
        first = jnp.sum(scaled, axis=-1, keepdims=True) * inv_width
        second = jnp.sum(scaled * hat, axis=-1, keepdims=True) * inv_width
        return (rstd * (scaled - first - hat * second)) * width_mask

    chunks = owned // CHUNK
    acc, da, dh = r["acc"], r["da"], r["dh"]
    zeros = jnp.zeros((CHUNK, model), F32)
    r["norm_sums"][...] = jnp.zeros(r["norm_sums"].shape, F32)
    r["bias_sums"][...] = jnp.zeros(r["bias_sums"].shape, F32)

    def sentence(b):
        return pl.ds(pl.multiple_of(b * LEN, LEN), LEN)

    def head_keep(j, h):
        return jnp.where(j * heads_here + h < heads, 1.0, 0.0).astype(F32)

    def causal(b):
        return jnp.where(column(0, (LEN, LEN)) <= column(1, (LEN, LEN)), 0.0, NEGATIVE).astype(F32)

    def crossing(b):
        there = column(0, (LEN, 1)) < sources[place.tp * sentences + b]
        return jnp.where(there, 0.0, NEGATIVE).astype(F32)

    def bands(h):
        return [pl.ds(i * local + h * HD, HD) for i in range(3)]

    def lanes(b):
        return pl.ds(b * LEN, LEN)

    pairs = [(b, h) for b in range(sentences) for h in range(heads_here)]

    def attend(k, table, g, suffix, query_rows, key_rows, barred):
        w, t, c, p = weights[g], r["t" + suffix], r["c" + suffix], r["p" + suffix]
        j = block(k)
        hooks(table, k, 0)
        if query_rows is key_rows:
            t[j] = dot_nt(w[j, :3 * local], query_rows[...]).astype(BF16)
        else:
            t[j, :local] = dot_nt(w[j, :local], query_rows[...]).astype(BF16)
            t[j, local:] = dot_nt(w[j, local:3 * local], key_rows[...]).astype(BF16)
        for b, h in pairs:
            query, keys, values = (t[j, band, lanes(b)] for band in bands(h))
            scores = dot_tn(keys, query) + barred(b)
            raised = jnp.exp2((scores - jnp.max(scores, axis=0, keepdims=True)) * (SCALE * LOG2E))
            shares = (raised * (1.0 / jnp.sum(raised, axis=0, keepdims=True))).astype(BF16)
            p[j, b * heads_here + h] = shares
            c[j, pl.ds(h * HD, HD), lanes(b)] = (dot_nn(values, shares) * head_keep(j, h)).astype(BF16)
        hooks(table, k, 1)
        for b in range(sentences):
            rows = sentence(b)
            acc[rows] = acc[rows] + dot_tn(c[j, :, lanes(b)], w[j, 3 * local:])

    def attend_backward(k, table, g, suffix, query_rows, key_rows):
        w, t, c, p = weights[g], r["t" + suffix], r["c" + suffix], r["p" + suffix]
        j = block(k)
        e, dt, dc = r["e"], r["dt"], r["dc"]
        dc_all = dot_nt(w[j, 3 * local:], e[...])
        for h in range(heads_here):
            dc[h * HD:(h + 1) * HD] = (dc_all[h * HD:(h + 1) * HD] * head_keep(j, h)).astype(BF16)
        for b, h in pairs:
            (query, keys, values), (dq, dk, dv) = (t[j, band, lanes(b)] for band in bands(h)), bands(h)
            dc_h = dc[h * HD:(h + 1) * HD, lanes(b)]
            shares = p[j, b * heads_here + h]
            wide = shares.astype(F32)
            dp = dot_tn(values, dc_h)
            ds = (wide * (dp - jnp.sum(dp * wide, axis=0, keepdims=True))).astype(BF16)
            dt[dv, lanes(b)] = dot_nt(dc_h, shares).astype(BF16)
            dt[dq, lanes(b)] = (dot_nn(keys, ds) * SCALE).astype(BF16)
            dt[dk, lanes(b)] = (dot_nt(query, ds) * SCALE).astype(BF16)
        hooks(table, k, 1)
        gather.drain(g, j)
        own = query_rows is key_rows
        for b in range(sentences):
            rows = sentence(b)
            if own:
                da[rows] = da[rows] + dot_tn(dt[:, lanes(b)], w[j, :3 * local])
            else:
                da[rows] = da[rows] + dot_tn(dt[:local, lanes(b)], w[j, :local])
                r["dm"][rows] = r["dm"][rows] + dot_tn(dt[local:, lanes(b)], w[j, local:3 * local])
        if own:
            w[j, :3 * local] = dot_nn(dt[...], query_rows[...]).astype(BF16)
        else:
            w[j, :local] = dot_nn(dt[:local], query_rows[...]).astype(BF16)
            w[j, local:3 * local] = dot_nn(dt[local:], key_rows[...]).astype(BF16)
        w[j, 3 * local:] = dot_nn(c[j], e[...]).astype(BF16)

    def feed(k, table):
        j = block(k)
        w_up, w_down = weights[2], weights[3]
        unit_mask = (column(1, (1, units)) + j * units < hidden_units).astype(F32)

        def one(b):
            hooks(table, k, b)
            rows = sentence(b)
            before = dot_nn(r["a3"][rows], w_up[j]) + r["bias"][j, 0:1]
            square = before * before
            bent = jnp.tanh(ROOT * before * (1.0 + CUBE * square))
            half = 0.5 * (1.0 + bent)
            g = (before * half * unit_mask).astype(BF16)
            slope = (half + 0.5 * before * (1.0 - bent * bent) * (ROOT + 3.0 * CUBE * ROOT * square)) * unit_mask
            r["hidden"][rows] = g
            acc[rows] = acc[rows] + dot_nn(g, w_down[j])
            du = (dot_nt(r["e"][rows], w_down[j]) * slope).astype(BF16)
            r["dhidden"][rows] = du
            r["bias_sums"][j] = r["bias_sums"][j] + fold(du.astype(F32))
            da[rows] = da[rows] + dot_nt(du, w_up[j])

        each(sentences, one)
        gather.drain(2, j)
        gather.drain(3, j)

        def down(i):
            part = pl.ds(pl.multiple_of(i * 128, 128), 128)
            w_down[j, part] = dot_tn(r["hidden"][:, part], r["e"][...]).astype(BF16)

        def up(i):
            part = pl.ds(pl.multiple_of(i * 128, 128), 128)
            w_up[j, part] = dot_tn(r["a3"][:, part], r["dhidden"][...]).astype(BF16)

        each(units // 128, down)
        each(model // 128, up)

    loads[0].wait()

    def begin(i):
        rows = chunk(i)
        r["a1"][rows] = norm(x[rows].astype(F32), 0)
        acc[rows] = zeros
        da[rows] = zeros
        r["dm"][rows] = zeros

    each(chunks, begin)
    g_tick(0)
    loads[1].wait()

    def mix(i):
        rows = chunk(i)
        total = jnp.zeros((CHUNK, model), F32)
        for level in range(layers):
            chosen = (jnp.full((1, 1), depth) >= layers - level).astype(F32)
            total = total + chosen * r["memory"][level, rows].astype(F32)
        r["m"][rows] = (total * inv_depth * width_mask).astype(BF16)

    each(chunks, mix)
    loads[2].wait()
    r["out_sums"][...] = jnp.zeros(r["out_sums"].shape, F32)

    def grad_in(i):
        rows = chunk(i)
        masked = r["upstream"][rows].astype(F32) * keep_of(i)
        r["out_sums"][...] = r["out_sums"][...] + fold(masked)
        r["e"][rows] = masked.astype(BF16)

    each(chunks, grad_in)

    def ticks(*numbers):
        return [functools.partial(g_tick, i) for i in numbers]

    others = n - 1
    assert n == 4
    table = {
        (0, 1): ticks(1),
        (1, 0): ticks(2, 3) + [functools.partial(bias.step, 0)],
        (2, 0): ticks(4) + [functools.partial(bias.step, 1)],
        (3, 0): ticks(5) + [functools.partial(bias.step, 2)],
    }
    each(n, lambda k: attend(k, table, 0, "1", r["a1"], r["a1"], causal))

    def after_self(i):
        rows = chunk(i)
        h = x[rows].astype(F32) + acc[rows] * keep_of(i)
        r["h1"][rows] = h
        r["a2"][rows] = norm(h, 1)
        acc[rows] = zeros

    each(chunks, after_self)
    table2 = {(k, 0): ticks(6 + k) for k in range(n)}
    each(n, lambda k: attend(k, table2, 1, "2", r["a2"], r["m"], crossing))

    def after_cross(i):
        rows = chunk(i)
        h = r["h1"][rows] + acc[rows] * keep_of(i)
        r["h2"][rows] = h
        r["a3"][rows] = norm(h, 2)
        acc[rows] = zeros

    each(chunks, after_cross)

    reduce = Reduce(
        place, weights, *([r["%s%d" % (name, i)] for i in range(4)] for name in
                          ("half", "first", "second", "line", "extra", "total")), r["reduce_sems"],
    )
    plan = {}

    def add(tick, order, step, *args):
        plan.setdefault(tick, []).append((order, len(plan.get(tick, ())), functools.partial(step, *args)))

    def r_tick(tick):
        for _, _, step in sorted(plan.get(tick, ()), key=lambda entry: entry[:2]):
            step()

    def store(g):
        return pltpu.make_async_copy(r["total%d" % g], r["out%d" % g], local_sem.at[10 + g])

    starts = {3: [2 * k + 1 for k in range(n)], 2: [2 * k + 1 for k in range(n)]}
    starts[1] = [10 + 2 * k for k in range(n)]
    starts[0] = [19 + 2 * k for k in range(n)]
    for late, g in enumerate((3, 2, 1, 0)):
        for k, tick in enumerate(starts[g]):
            for stage in range(4):
                add(tick + stage, stage, reduce.step, g, block(k), stage)
        last = starts[g][-1] + 3
        for k in range(n):
            add(last + k, 10 - late, reduce.travel, g, k)
        add(last + n, 20 - late, reduce.settle, g)
        for stage in (1, 2, 3):
            add(last + n + stage, 30 + stage - late, reduce.share, g, stage)
        add(last + n + 3, 50, lambda g=g: store(g).start())

    def reduce_ticks(*numbers):
        return [functools.partial(r_tick, i) for i in numbers]

    def at_end(k, numbers):
        for kk, number in enumerate(numbers):

            @pl.when(k == kk)
            def _():
                r_tick(number)

    table3 = {(0, 0): ticks(10), (0, 1): ticks(11), (1, 1): ticks(12) + reduce_ticks(2),
              (2, 1): ticks(13) + reduce_ticks(4), (3, 0): ticks(14), (3, 1): reduce_ticks(6)}

    def feed_step(k):
        feed(k, table3)
        at_end(k, [2 * i + 1 for i in range(n)])

    each(n, feed_step)
    r_tick(8)
    out_copy = pltpu.make_async_copy(acc, r["layer_out"], local_sem.at[14])

    def after_feed(i):
        rows = chunk(i)
        keep = keep_of(i)
        acc[rows] = r["h2"][rows] + (acc[rows] + r["bias_out"][...]) * keep
        down = r["upstream"][rows].astype(F32) + norm_backward(r["h2"][rows], 2, da[rows])
        dh[rows] = down
        r["e"][rows] = (down * keep).astype(BF16)
        da[rows] = zeros

    each(chunks, after_feed)
    out_copy.start()
    table4 = {(k, 1): reduce_ticks(9 + 2 * k) for k in range(n)}

    def cross_step(k):
        attend_backward(k, table4, 1, "2", r["a2"], r["m"])
        at_end(k, [10 + 2 * i for i in range(n)])

    each(n, cross_step)
    memory_copy = pltpu.make_async_copy(r["dm"], r["memory_out"], local_sem.at[15])
    memory_copy.start()

    def before_cross(i):
        rows = chunk(i)
        down = dh[rows] + norm_backward(r["h1"][rows], 1, da[rows])
        dh[rows] = down
        r["e"][rows] = (down * keep_of(i)).astype(BF16)
        da[rows] = zeros

    each(chunks, before_cross)
    r_tick(17)
    table5 = {(k, 1): reduce_ticks(18 + 2 * k) for k in range(n)}

    def self_step(k):
        attend_backward(k, table5, 0, "1", r["a1"], r["a1"])
        at_end(k, [19 + 2 * i for i in range(n)])

    each(n, self_step)

    def before_self(i):
        rows = chunk(i)
        dh[rows] = dh[rows] + norm_backward(x[rows].astype(F32), 0, da[rows])

    each(chunks, before_self)
    grad_copy = pltpu.make_async_copy(dh, r["input_grad"], local_sem.at[16])
    grad_copy.start()

    small = SumSmall(place, r["slots"], r["small_sems"])

    def small_start():
        own = r["slots"].at[0]
        own[...] = jnp.zeros(own.shape, F32)
        for i in range(6):
            own[i:i + 1, :model] = jnp.sum(r["norm_sums"][i], axis=0, keepdims=True)
        own[6:7, :model] = jnp.sum(r["out_sums"][...], axis=0, keepdims=True)
        tokens = lengths[place.tp * sentences]
        for b in range(1, sentences):
            tokens = tokens + lengths[place.tp * sentences + b]
        own[7:8] = jnp.full((1, own.shape[1]), tokens.astype(F32))
        for i in range(n):
            own[8 + i:9 + i] = jnp.sum(r["bias_sums"][i], axis=0, keepdims=True)
        small.start()

    add(26, 5, small_start)
    for stage in range(3):
        add(27 + stage, 5, small.exchange, stage)
    add(30, 4, small.among_copies)
    for k in range(n):
        add(30 + k, 5, small.line, k)
    final = max(plan)
    for tick in range(26, final + 1):
        r_tick(tick)
    r["small_out"][...] = small.total()
    bias.finish()
    for copy in (out_copy, memory_copy, grad_copy):
        copy.wait()
    for g in range(4):
        reduce.finish(g)
        store(g).wait()
    small.finish()


def run_layer(args, weights):
    lengths, src_lengths, configs, gains, shifts, bias_in, bias_out, x, memory, upstream = args
    n, extra = lax.axis_size("tp"), lax.axis_size("dp") // 2
    owned, model = x.shape
    local, units = weights[1].shape[0], bias_in.shape[1]
    small = (16, units)
    assert n <= 8 and units >= model
    shapes = [(n, 4 * local, model)] * 2 + [(n,) + weights[5].shape, (n,) + weights[6].shape]
    scratch = {}

    def vmem(name, shape, dtype=BF16):
        scratch[name] = pltpu.VMEM(shape, dtype)

    def dma(name, *shape):
        scratch[name] = pltpu.SemaphoreType.DMA(shape)

    for i, shape in enumerate(shapes):
        vmem("w%d" % i, shape)
    vmem("bias", (n, 8, units), F32)
    vmem("x", x.shape)
    vmem("memory", memory.shape)
    vmem("upstream", upstream.shape)
    assert memory.shape[0] >= 3
    for name in ("a1", "m"):
        vmem(name, (owned, model))
    for name in ("h1", "h2", "dh", "acc", "da", "dm"):
        vmem(name, (owned, model), F32)
    for suffix in ("1", "2"):
        vmem("t" + suffix, (n, 3 * local, owned))
        vmem("c" + suffix, (n, local, owned))
        vmem("p" + suffix, (n, owned // LEN * (local // HD), LEN, LEN))
    vmem("dt", (3 * local, owned))
    vmem("dc", (local, owned))
    vmem("hidden", (owned, units))
    vmem("dhidden", (owned, units))
    vmem("bias_sums", (n, 8, units), F32)
    vmem("norm_sums", (6, 8, model), F32)
    vmem("out_sums", (8, model), F32)
    for i, (_, rows, columns) in enumerate(shapes):
        vmem("half%d" % i, (n, rows // 2, columns))
        vmem("first%d" % i, (n, rows // 4, columns))
        vmem("second%d" % i, (n, rows // 8, columns))
        vmem("line%d" % i, (n + 1, rows // 8, columns))
        vmem("extra%d" % i, (extra, rows // 8, columns))
        vmem("total%d" % i, (rows, columns))
    vmem("slots", (SumSmall.SLOTS + extra,) + small, F32)
    dma("gather_sems", Gather.KINDS, 4, n)
    dma("bias_sems", 3, n)
    dma("reduce_sems", Reduce.KINDS, 4, max(n, extra))
    dma("small_sems", SumSmall.SLOTS + 2 * extra)
    dma("local_sems", 17)
    outs = {
        "layer_out": (x.shape, F32), "input_grad": (x.shape, F32), "memory_out": (x.shape, F32),
        "out0": (shapes[0][1:], BF16), "out1": (shapes[1][1:], BF16), "out2": (shapes[2][1:], BF16), "out3": (shapes[3][1:], BF16),
        "small_out": (small, F32),
    }
    names = ["lengths", "src_lengths", "configs", "gains", "shifts", "bias_in", "bias_out", "x_in", "memory_in", "upstream_in"]
    names += ["in%d" % i for i in range(7)] + list(outs) + list(scratch)
    smem, vm, hbm = (pl.BlockSpec(memory_space=space) for space in (pltpu.SMEM, pltpu.VMEM, pl.ANY))
    flops = 6 * owned * model * (8 * n * local + 2 * n * units)
    return pl.pallas_call(
        functools.partial(layer_kernel, names),
        out_shape=[jax.ShapeDtypeStruct(*out) for out in outs.values()],
        in_specs=[smem] * 3 + [vm] * 4 + [hbm] * 10,
        out_specs=[hbm] * 7 + [vm],
        scratch_shapes=list(scratch.values()),
        compiler_params=pltpu.CompilerParams(collective_id=1, has_side_effects=True, vmem_limit_bytes=64 * 2**20),
        cost_estimate=pl.CostEstimate(flops=flops, bytes_accessed=40 * 2**20, transcendentals=0),
        name="layer",
    )(*args, *weights)


def per_device(
    inputs, memory, out_grad, lengths, src_lengths, configs, norm_gain, norm_bias,
    self_qkv, self_out, cross_q, cross_kv, cross_out, ffn_in, ffn_in_bias, ffn_out, ffn_out_bias,
):
    model = inputs.shape[1]
    layers = memory.shape[0]
    local = self_out.shape[0]
    units = ffn_in.shape[1]
    layer_out, input_grad, source_grad, first, second, third, fourth, small = run_layer(
        (lengths, src_lengths, configs, norm_gain, norm_bias, ffn_in_bias.reshape(1, units),
         ffn_out_bias.reshape(1, model), inputs, memory, out_grad),
        (self_qkv.transpose(1, 2, 0).reshape(3 * local, model), self_out, cross_q.T,
         cross_kv.transpose(1, 2, 0).reshape(2 * local, model), cross_out, ffn_in, ffn_out),
    )
    width_mask = (jnp.arange(model) < configs[0, 0]).astype(F32)
    chosen = (jnp.arange(layers) >= layers - configs[0, 3]).astype(F32) / configs[0, 3].astype(F32)
    memory_grad = chosen[:, None, None] * (source_grad * width_mask)[None]
    inverse = 1.0 / small[7, 0]
    small = small * inverse
    first, second, third, fourth = (block.astype(F32) * inverse for block in (first, second, third, fourth))
    return (
        layer_out,
        input_grad,
        memory_grad,
        small[:3, :model],
        small[3:6, :model],
        first[:3 * local].reshape(3, local, model).transpose(2, 0, 1),
        first[3 * local:],
        second[:local].T,
        second[local:3 * local].reshape(2, local, model).transpose(2, 0, 1),
        second[3 * local:],
        third,
        lax.dynamic_slice_in_dim(small, 8 + lax.axis_index("tp"), 1)[0],
        fourth,
        small[6, :model],
    )


def solution(mesh):
    rows = P(("grp", "dp", "tp"), None)
    stack = P(None, ("grp", "dp", "tp"), None)
    weights = (
        P(None, None, "tp"), P("tp", None), P(None, "tp"), P(None, None, "tp"), P("tp", None),
        P(None, "tp"), P("tp"), P("tp", None), P(),
    )
    return jax.shard_map(
        per_device,
        mesh=mesh,
        in_specs=(rows, stack, rows, P(("grp", "dp")), P(("grp", "dp")), P("grp", None), P(), P()) + weights,
        out_specs=(rows, rows, stack, P(), P()) + weights,
        check_vma=False,
    )
```

```python
import functools
import types

import jax
import jax.numpy as jnp
from jax import lax
from jax.experimental import pallas as pl
from jax.experimental.pallas import tpu as pltpu
from jax.sharding import PartitionSpec as P

HD = 80
LEN = 256
EPSILON = 1e-05
NEGATIVE = -1e30
SCALE = HD ** (-0.5)
LOG2E = 1.4426950408889634
F32 = jnp.float32
BF16 = jnp.bfloat16


MESH = pl.DeviceIdType.MESH


class Place:
    def __init__(self):
        self.tps = lax.axis_size("tp")
        self.extra = lax.axis_size("dp") // 2
        assert lax.axis_size("grp") == 4 and lax.axis_size("dp") % 2 == 0
        grp, dp, tp = (lax.axis_index(name) for name in ("grp", "dp", "tp"))
        core, low, high = dp % 2, grp % 2, grp // 2
        flip_low, flip_high = grp + 1 - 2 * low, grp + 2 - 4 * high
        self.grp, self.dp, self.tp, self.core = grp, dp, tp, core
        self.first_bit = (1 - core) * low + core * high
        self.second_bit = (1 - core) * high + core * low
        self.first = ((1 - core) * flip_low + core * flip_high, dp, tp)
        self.second = ((1 - core) * flip_high + core * flip_low, dp, tp)
        self.across = (3 - grp, dp, tp)
        self.sibling = (grp, dp + 1 - 2 * core, tp)
        self.above = (grp, dp, tp + 1)
        self.below = (grp, dp, tp - 1)
        self.has_above = tp < self.tps - 1
        self.has_below = tp > 0

    def copy_of(self, step):
        return (self.grp, ((self.dp // 2 + step) % self.extra) * 2 + self.core, self.tp)

    def nth_block(self, k):
        size = self.tps
        upper = (2 * self.tp) // size
        lead = (1 - upper) * self.tp + upper * (size - 1 - self.tp)
        spot = k + (k + size - lead) // size
        return (1 - upper) * spot + upper * (size - 1 - spot)

    def along(self, tp):
        return (self.grp, self.dp, tp)

    def barrier(self):
        sem = pltpu.get_barrier_semaphore()
        partners = [self.first, self.second, self.across, self.sibling]
        partners += [self.along((self.tp + step) % self.tps) for step in range(1, self.tps)]
        partners += [self.copy_of(step) for step in range(1, self.extra)]
        for device in partners:
            pl.semaphore_signal(sem, inc=1, device_id=device, device_id_type=MESH)
        pl.semaphore_wait(sem, len(partners))


def push(src, dst, send_sem, recv_sem, device):
    return pltpu.make_async_remote_copy(
        src_ref=src, dst_ref=dst, send_sem=send_sem, recv_sem=recv_sem, device_id=device, device_id_type=MESH
    )


def rows_of(ref, lead, start, count):
    return ref.at[lead, pl.ds(pl.multiple_of(start, 16), count)]


def add_units(total, term, unit):
    def step(i, carry):
        rows = pl.ds(pl.multiple_of(i * unit, 16), unit)
        total[rows] = total[rows] + term[rows]
        return carry

    lax.fori_loop(0, total.shape[0] // unit, step, 0)


class Spread:
    KINDS = 14

    def __init__(self, place, view, unit, sems, direct=False):
        self.place, self.view, self.unit, self.sems = place, view, unit, sems
        f, s, c = place.first_bit, place.second_bit, place.core
        self.units = (f * 2 + s, f * 2 + 1 - s, (1 - f) * 2 + s, (1 - f) * 2 + 1 - s)
        self.theirs = (s * 2 + f, s * 2 + 1 - f, (1 - s) * 2 + f, (1 - s) * 2 + 1 - f)
        self.table = [
            (place.second, (c, self.units[0]), (c, self.units[1])),
            (place.first, (c, self.units[0]), (c, self.units[2])),
            (place.across if direct else place.first, (c, self.units[0 if direct else 1]), (c, self.units[3])),
        ] + [(place.sibling, (c, u), (1 - c, t)) for u, t in zip(self.units, self.theirs)]
        if direct:
            self.waits = ((), (0, 1, 2), (3, 4, 5, 6))
            self.sends = ((0, 1, 2, 3), (4, 5, 6), ())
        else:
            self.waits = ((), (0,), (1, 2), (3, 4, 5, 6))
            self.sends = ((0, 1, 3), (2, 4), (5, 6), ())

    def region(self, spot):
        half, unit = spot
        return self.view((half * 4 + unit) * self.unit, self.unit)

    def own(self):
        return self.region((self.place.core, self.units[0]))

    def copy(self, n, lands=False):
        device, leaves, landing = self.table[n]
        part = self.region(landing if lands else leaves)
        return push(part, part, self.sems(2 * n), self.sems(2 * n + 1), device)

    def step(self, stage):
        for n in self.waits[stage]:
            self.copy(n, lands=True).wait_recv()
        for n in self.sends[stage]:
            self.copy(n).start()

    def finish(self):
        for n in range(7):
            self.copy(n).wait_send()


class Gather:
    KINDS = Spread.KINDS + 3

    def __init__(self, place, buffers, sems):
        self.place, self.buffers, self.sems = place, buffers, sems
        self.unit = [ref.shape[1] // 8 for ref in buffers]
        self.others = place.tps - 1

    def spread(self, g, j):
        return Spread(
            self.place,
            lambda start, count: rows_of(self.buffers[g], j, start, count),
            self.unit[g],
            lambda kind: self.sems.at[kind, g, j],
        )

    def relays(self, g, j):
        p = self.place
        part = self.spread(g, j).own()
        sem = lambda n: self.sems.at[Spread.KINDS + n, g, j]
        return (
            (jnp.logical_and(j <= p.tp, p.has_above), push(part, part, sem(0), sem(2), p.above)),
            (jnp.logical_and(j >= p.tp, p.has_below), push(part, part, sem(1), sem(2), p.below)),
        )

    def start(self, g):
        for needed, copy in self.relays(g, self.place.tp):
            pl.when(needed)(copy.start)

    def step(self, g, k, stage):
        j = self.place.nth_block(k)
        if stage == 0:
            relays = self.relays(g, j)
            relays[0][1].wait_recv()
            for needed, copy in relays:
                pl.when(needed)(copy.start)
        self.spread(g, j).step(stage)

    def drain(self, g, j):
        for needed, copy in self.relays(g, j):
            pl.when(needed)(copy.wait_send)

        @pl.when(j != self.place.tp)
        def _():
            self.spread(g, j).finish()


class Line:
    def __init__(self, place, buffer, sems):
        self.place, self.buffer, self.sems = place, buffer, sems

    def relays(self, j):
        p = self.place
        part = self.buffer.at[j]
        return (
            (jnp.logical_and(j <= p.tp, p.has_above), push(part, part, self.sems.at[0, j], self.sems.at[2, j], p.above)),
            (jnp.logical_and(j >= p.tp, p.has_below), push(part, part, self.sems.at[1, j], self.sems.at[2, j], p.below)),
        )

    def start(self):
        for needed, copy in self.relays(self.place.tp):
            pl.when(needed)(copy.start)

    def step(self, k):
        j = self.place.nth_block(k)
        relays = self.relays(j)
        relays[0][1].wait_recv()
        for needed, copy in relays:
            pl.when(needed)(copy.start)

    def finish(self):
        for j in range(self.place.tps):
            for needed, copy in self.relays(j):
                pl.when(needed)(copy.wait_send)


class Reduce:
    KINDS = 8 + 6 + 2 + Spread.KINDS + 2

    def __init__(self, place, grads, halves, planes, lines, extras, totals, sems):
        self.place, self.grads, self.totals, self.sems = place, grads, totals, sems
        self.halves, self.planes, self.lines, self.extras = halves, planes, lines, extras
        self.unit = [ref.shape[1] // 8 for ref in grads]

    def sem(self, kind, g, j):
        return self.sems.at[kind, g, j]

    def rows(self, g, j, half, unit, count=1):
        size = self.unit[g]
        return rows_of(self.grads[g], j, (half * 4 + unit) * size, count * size)

    def to_sibling(self, g, j):
        p = self.place
        return [push(self.rows(g, j, 1 - p.core, 0, 4), self.halves[g].at[j], self.sem(0, g, j), self.sem(1, g, j), p.sibling)]

    def in_plane(self, g, j):
        p = self.place
        f, s = p.first_bit, p.second_bit
        goals = ((p.second, f * 2 + 1 - s), (p.first, (1 - f) * 2 + s), (p.across, (1 - f) * 2 + 1 - s))
        return [
            push(
                self.rows(g, j, p.core, u), self.planes[g].at[j, i],
                self.sem(8 + 2 * i, g, j), self.sem(9 + 2 * i, g, j), device,
            )
            for i, (device, u) in enumerate(goals)
        ]

    def piece(self, g, j):
        p = self.place
        return self.rows(g, j, p.core, p.first_bit * 2 + p.second_bit)

    def along(self, g, j):
        p = self.place
        return push(self.piece(g, j), self.lines[g].at[p.tp], self.sem(14, g, j), self.sem(15, g, p.tp), p.along(j))

    def from_place(self, g, j):
        p = self.place
        return push(self.piece(g, j), self.lines[g].at[j], self.sem(14, g, j), self.sem(15, g, j), p.along(j))

    def step(self, g, j, stage):
        p = self.place
        if stage == 0:
            for copy in self.to_sibling(g, j):
                copy.start()
        if stage == 1:
            for copy in self.to_sibling(g, j):
                copy.wait_recv()
            add_units(self.rows(g, j, p.core, 0, 4), self.halves[g].at[j], self.unit[g])
            for copy in self.in_plane(g, j):
                copy.start()
        if stage == 2:
            for copy in self.in_plane(g, j):
                copy.wait_recv()
            a, b, c = (self.planes[g][j, i].astype(F32) for i in range(3))
            piece = self.piece(g, j)
            piece[...] = ((piece[...].astype(F32) + a) + (b + c)).astype(BF16)
            pl.when(j != p.tp)(self.along(g, j).start)

    def spread(self, g):
        return Spread(
            self.place,
            lambda start, count: self.totals[g].at[pl.ds(pl.multiple_of(start, 16), count)],
            self.unit[g],
            lambda kind: self.sems.at[16 + kind, g, 0],
            direct=True,
        )

    def copies(self, g, step):
        p = self.place
        base = self.KINDS - 2
        return push(
            self.piece(g, p.tp), self.extras[g].at[step], self.sem(base, g, step), self.sem(base + 1, g, step), p.copy_of(step)
        )

    def settle(self, g):
        p = self.place
        piece = self.piece(g, p.tp)
        total = piece[...].astype(F32)
        for k in range(p.tps - 1):
            j = p.nth_block(k)
            self.from_place(g, j).wait_recv()
            total = total + self.lines[g][j].astype(F32)
        if p.extra > 1:
            piece[...] = total.astype(BF16)
            for step in range(1, p.extra):
                self.copies(g, step).start()
            for step in range(1, p.extra):
                self.copies(g, step).wait()
                total = total + self.extras[g][step].astype(F32)
        own = self.spread(g).own()
        own[...] = total.astype(BF16)
        self.spread(g).step(0)

    def share(self, g, stage):
        self.spread(g).step(stage)

    def finish(self, g):
        p = self.place
        for j in range(p.tps):
            for copy in self.to_sibling(g, j) + self.in_plane(g, j):
                copy.wait_send()
            pl.when(j != p.tp)(self.along(g, j).wait_send)
        self.spread(g).finish()


class SumSmall:
    @staticmethod
    def slots(tps, extra):
        return 8 + tps + extra

    def __init__(self, place, slots, sems):
        self.place, self.slots_ref, self.sems = place, slots, sems

    def move(self, source, target, device, kind):
        slots = self.slots_ref
        return push(slots.at[source], slots.at[target], self.sems.at[0, kind], self.sems.at[1, target], device)

    def in_plane(self):
        p = self.place
        return [self.move(2, 3 + i, device, 3 + i) for i, device in enumerate((p.second, p.first, p.across))]

    def copies(self):
        p = self.place
        return [self.move(6, 8 + p.tps + s, p.copy_of(s), 8 + p.tps + s) for s in range(1, p.extra)]

    def along(self, k, lands=False):
        p = self.place
        j = p.nth_block(k)
        return self.move(7, 8 + (j if lands else p.tp), p.along(j), 8 + j)

    def start(self):
        self.move(0, 1, self.place.sibling, 1).start()

    def exchange(self, stage):
        p, slots = self.place, self.slots_ref
        if stage == 0:
            self.move(0, 1, p.sibling, 1).wait_recv()
            slots[2] = slots[0] + slots[1]
            for copy in self.in_plane():
                copy.start()
        else:
            for copy in self.in_plane():
                copy.wait_recv()
            slots[6] = (slots[2] + slots[3]) + (slots[4] + slots[5])
            for copy in self.copies():
                copy.start()
            total = slots[6]
            for s, copy in enumerate(self.copies()):
                copy.wait_recv()
                total = total + slots[9 + p.tps + s]
            slots[7] = total
            for k in range(p.tps - 1):
                self.along(k).start()

    def total(self):
        p, slots = self.place, self.slots_ref
        value = slots[7]
        for k in range(p.tps - 1):
            self.along(k, lands=True).wait_recv()
            value = value + slots[8 + p.nth_block(k)]
        return value

    def finish(self):
        p = self.place
        self.move(0, 1, p.sibling, 1).wait_send()
        for copy in self.in_plane() + self.copies():
            copy.wait_send()
        for k in range(p.tps - 1):
            self.along(k).wait_send()


def dot_nn(left, right):
    return lax.dot_general(left, right, (((1,), (0,)), ((), ())), preferred_element_type=F32)


def dot_nt(left, right):
    return lax.dot_general(left, right, (((1,), (1,)), ((), ())), preferred_element_type=F32)


def dot_tn(left, right):
    return lax.dot_general(left, right, (((0,), (0,)), ((), ())), preferred_element_type=F32)


def column(axis, shape):
    return lax.broadcasted_iota(jnp.int32, shape, axis)


def each(count, step):

    def run(i, carry):
        step(i)
        return carry

    lax.fori_loop(0, count, run, 0)


CHUNK = 128
CUBE = 0.044715
ROOT = 0.7978845608028654


def layer_kernel(r):
    r.a2, r.a3, r.e = (r.memory.at[i] for i in range(3))
    place = Place()
    n = place.tps
    x, model = r.x, r.x.shape[1]
    owned = x.shape[0]
    sentences = owned // LEN
    local = r.c[0].shape[1]
    heads_here = local // HD
    units = r.hidden.shape[1]
    layers = r.memory.shape[0]
    weights = r.w
    lengths, sources, configs = r.lengths, r.src_lengths, r.configs
    width, heads, hidden_units, depth = (configs[0, i] for i in range(4))
    inv_width = 1.0 / jnp.full((1, 1), width.astype(F32))
    inv_depth = 1.0 / jnp.full((1, 1), depth.astype(F32))
    width_mask = (column(1, (1, model)) < width).astype(F32)

    local_sem = r.local_sems
    spots = (
        (0, 0, 3 * local), (0, 3 * local, local),
        (1, 0, local), (1, local, 2 * local), (1, 3 * local, local),
        (2, 0, weights[2].shape[1]), (3, 0, weights[3].shape[1]),
    )
    fills = [
        (g, pltpu.make_async_copy(r.shards[i], weights[g].at[place.tp, pl.ds(start, size)], local_sem.at[i]))
        for i, (g, start, size) in enumerate(spots)
    ]
    loads = [
        pltpu.make_async_copy(source, target, local_sem.at[7 + i])
        for i, (source, target) in enumerate(((r.x_in, r.x), (r.memory_in, r.memory), (r.upstream_in, r.upstream)))
    ]
    for _, copy in fills[:2]:
        copy.start()
    loads[0].start()
    for _, copy in fills[2:]:
        copy.start()
    loads[1].start()
    loads[2].start()
    r.bias[place.tp] = jnp.broadcast_to(r.bias_in[...].reshape(1, units), r.bias.shape[1:])
    place.barrier()

    gather = Gather(place, weights, r.gather_sems)
    bias = Line(place, r.bias, r.bias_sems)
    for g in range(4):
        for group, copy in fills:
            if group == g:
                copy.wait()
        gather.start(g)
        if g == 0:
            bias.start()
    order = [(g, k) for g in (0, 1) for k in range(n - 1)] + [(g, k) for k in range(n - 1) for g in (2, 3)]

    def g_tick(tick):
        for stage in range(4):
            if 0 <= tick - stage < len(order):
                gather.step(*order[tick - stage], stage)

    def block(k):
        later = (k + n - 1) // n
        return (1 - later) * place.tp + later * place.nth_block(k - 1)

    def block_last(k):
        own = k // (n - 1)
        return own * place.tp + (1 - own) * place.nth_block(k)

    def hooks(table, k, b):
        for (kk, bb), steps in table.items():

            @pl.when(jnp.logical_and(k == kk, b == bb))
            def _():
                for step in steps:
                    step()

    def chunk(i):
        return pl.ds(pl.multiple_of(i * CHUNK, CHUNK), CHUNK)

    def keep_of(i):
        per = LEN // CHUNK
        spot = column(0, (CHUNK, 1)) + (i % per) * CHUNK
        return (spot < lengths[place.tp * sentences + i // per]).astype(F32) * width_mask

    def norm_parts(rows):
        mean = jnp.sum(rows * width_mask, axis=-1, keepdims=True) * inv_width
        centred = (rows - mean) * width_mask
        spread = jnp.sum(centred * centred, axis=-1, keepdims=True) * inv_width
        rstd = lax.rsqrt(spread + EPSILON)
        return centred * rstd, rstd

    def norm(rows, which):
        hat, _ = norm_parts(rows)
        return ((hat * r.gains[which:which + 1] + r.shifts[which:which + 1]) * width_mask).astype(BF16)

    def fold(values):
        return jnp.sum(values.reshape(values.shape[0] // 8, 8, values.shape[1]), axis=0)

    def norm_backward(rows, which, upstream):
        hat, rstd = norm_parts(rows)
        upstream = upstream * width_mask
        sums = r.norm_sums
        sums[which] = sums[which] + fold(upstream * hat)
        sums[3 + which] = sums[3 + which] + fold(upstream)
        scaled = upstream * r.gains[which:which + 1]
        first = jnp.sum(scaled, axis=-1, keepdims=True) * inv_width
        second = jnp.sum(scaled * hat, axis=-1, keepdims=True) * inv_width
        return (rstd * (scaled - first - hat * second)) * width_mask

    chunks = owned // CHUNK
    acc, da, dh = r.acc, r.da, r.dh
    zeros = jnp.zeros((CHUNK, model), F32)
    r.norm_sums[...] = jnp.zeros(r.norm_sums.shape, F32)
    r.bias_sums[...] = jnp.zeros(r.bias_sums.shape, F32)

    def sentence(b):
        return pl.ds(pl.multiple_of(b * LEN, LEN), LEN)

    def head_keep(j, h):
        return jnp.where(j * heads_here + h < heads, 1.0, 0.0).astype(F32)

    def causal(b):
        return jnp.where(column(0, (LEN, LEN)) <= column(1, (LEN, LEN)), 0.0, NEGATIVE).astype(F32)

    def crossing(b):
        there = column(0, (LEN, 1)) < sources[place.tp * sentences + b]
        return jnp.where(there, 0.0, NEGATIVE).astype(F32)

    def bands(h):
        return [pl.ds(i * local + h * HD, HD) for i in range(3)]

    def lanes(b):
        return pl.ds(b * LEN, LEN)

    pairs = [(b, h) for b in range(sentences) for h in range(heads_here)]

    def attend(k, table, g, query_rows, key_rows, barred):
        w, t, c, p = weights[g], r.t[g], r.c[g], r.p[g]
        j = block(k)
        hooks(table, k, 0)
        if query_rows is key_rows:
            t[j] = dot_nt(w[j, :3 * local], query_rows[...]).astype(BF16)
        else:
            t[j, :local] = dot_nt(w[j, :local], query_rows[...]).astype(BF16)
            t[j, local:] = dot_nt(w[j, local:3 * local], key_rows[...]).astype(BF16)
        heads_of = [[t[j, band, lanes(b)] for band in bands(h)] for b, h in pairs]
        scores = [dot_tn(keys, query) for query, keys, _ in heads_of]
        shares = []
        for (b, h), score in zip(pairs, scores):
            score = score + barred(b)
            raised = jnp.exp2((score - jnp.max(score, axis=0, keepdims=True)) * (SCALE * LOG2E))
            shares.append((raised * (1.0 / jnp.sum(raised, axis=0, keepdims=True))).astype(BF16))
            p[j, b * heads_here + h] = shares[-1]
        for (b, h), (_, _, values), share in zip(pairs, heads_of, shares):
            c[j, pl.ds(h * HD, HD), lanes(b)] = (dot_nn(values, share) * head_keep(j, h)).astype(BF16)
        hooks(table, k, 1)
        acc[...] = acc[...] + dot_tn(c[j], w[j, 3 * local:])

    def attend_backward(k, table, g, query_rows, key_rows):
        w, t, c, p = weights[g], r.t[g], r.c[g], r.p[g]
        j = block_last(k)
        e, dt, dc = r.e, r.dt, r.dc
        dc_all = dot_nt(w[j, 3 * local:], e[...])
        for h in range(heads_here):
            dc[h * HD:(h + 1) * HD] = (dc_all[h * HD:(h + 1) * HD] * head_keep(j, h)).astype(BF16)
        heads_of = [[t[j, band, lanes(b)] for band in bands(h)] for b, h in pairs]
        dc_of = [dc[h * HD:(h + 1) * HD, lanes(b)] for b, h in pairs]
        dp_of = [dot_tn(values, dc_h) for (_, _, values), dc_h in zip(heads_of, dc_of)]
        ds_of = []
        for (b, h), dp in zip(pairs, dp_of):
            wide = p[j, b * heads_here + h].astype(F32)
            ds_of.append((wide * (dp - jnp.sum(dp * wide, axis=0, keepdims=True))).astype(BF16))
        for (b, h), (query, keys, _), dc_h, ds in zip(pairs, heads_of, dc_of, ds_of):
            dq, dk, dv = bands(h)
            dt[dv, lanes(b)] = dot_nt(dc_h, p[j, b * heads_here + h]).astype(BF16)
            dt[dq, lanes(b)] = (dot_nn(keys, ds) * SCALE).astype(BF16)
            dt[dk, lanes(b)] = (dot_nt(query, ds) * SCALE).astype(BF16)
        hooks(table, k, 1)
        gather.drain(g, j)
        own = query_rows is key_rows
        if own:
            da[...] = da[...] + dot_tn(dt[...], w[j, :3 * local])
        else:
            da[...] = da[...] + dot_tn(dt[:local], w[j, :local])
            r.dm[...] = r.dm[...] + dot_tn(dt[local:], w[j, local:3 * local])
        if own:
            w[j, :3 * local] = dot_nn(dt[...], query_rows[...]).astype(BF16)
        else:
            w[j, :local] = dot_nn(dt[:local], query_rows[...]).astype(BF16)
            w[j, local:3 * local] = dot_nn(dt[local:], key_rows[...]).astype(BF16)
        w[j, 3 * local:] = dot_nn(c[j], e[...]).astype(BF16)

    def feed(k, table):
        j = block(k)
        w_up, w_down = weights[2], weights[3]
        unit_mask = (column(1, (1, units)) + j * units < hidden_units).astype(F32)
        hooks(table, k, 0)

        def products(b):
            rows = sentence(b)
            return dot_nn(r.a3[rows], w_up[j]) + r.bias[j, 0:1], dot_nt(r.e[rows], w_down[j])

        def bend(b, before, down):
            rows = sentence(b)
            square = before * before
            bent = jnp.tanh(before * (ROOT + ROOT * CUBE * square))
            half = 0.5 * (1.0 + bent) * unit_mask
            r.hidden[rows] = (before * half).astype(BF16)
            slope = half + (half * before) * ((1.0 - bent) * (ROOT + 3.0 * CUBE * ROOT * square))
            du = (down * slope).astype(BF16)
            r.dhidden[rows] = du
            r.bias_sums[j] = r.bias_sums[j] + fold(du.astype(F32))

        found = [products(b) for b in range(sentences)]
        for b in range(sentences):
            bend(b, *found[b])
        for b in range(sentences):
            rows = sentence(b)
            acc[rows] = acc[rows] + dot_nn(r.hidden[rows], w_down[j])
            da[rows] = da[rows] + dot_nt(r.dhidden[rows], w_up[j])
        hooks(table, k, 1)
        gather.drain(2, j)
        gather.drain(3, j)
        w_down[j] = dot_tn(r.hidden[...], r.e[...]).astype(BF16)
        w_up[j] = dot_nn(r.a3t[...], r.dhidden[...]).astype(BF16)

    loads[0].wait()

    def begin(i):
        rows = chunk(i)
        r.a1[rows] = norm(x[rows].astype(F32), 0)
        acc[rows] = zeros
        da[rows] = zeros
        r.dm[rows] = zeros

    each(chunks, begin)
    g_tick(0)
    loads[1].wait()

    def mix(i):
        rows = chunk(i)
        total = jnp.zeros((CHUNK, model), F32)
        for level in range(layers):
            chosen = (jnp.full((1, 1), depth) >= layers - level).astype(F32)
            total = total + chosen * r.memory[level, rows].astype(F32)
        r.m[rows] = (total * inv_depth * width_mask).astype(BF16)

    each(chunks, mix)
    loads[2].wait()
    r.out_sums[...] = jnp.zeros(r.out_sums.shape, F32)

    def grad_in(i):
        rows = chunk(i)
        masked = r.upstream[rows].astype(F32) * keep_of(i)
        r.out_sums[...] = r.out_sums[...] + fold(masked)
        r.e[rows] = masked.astype(BF16)

    each(chunks, grad_in)

    def ticks(*numbers):
        return [functools.partial(g_tick, i) for i in numbers]

    others = n - 1
    assert n == 4
    table = {
        (0, 1): ticks(1),
        (1, 0): ticks(2, 3) + [functools.partial(bias.step, 0)],
        (2, 0): ticks(4) + [functools.partial(bias.step, 1)],
        (3, 0): ticks(5) + [functools.partial(bias.step, 2)],
    }
    each(n, lambda k: attend(k, table, 0, r.a1, r.a1, causal))

    def after_self(i):
        rows = chunk(i)
        h = x[rows].astype(F32) + acc[rows] * keep_of(i)
        r.h1[rows] = h
        r.a2[rows] = norm(h, 1)
        acc[rows] = zeros

    each(chunks, after_self)
    table2 = {(k, 0): ticks(6 + k) for k in range(n)}
    each(n, lambda k: attend(k, table2, 1, r.a2, r.m, crossing))

    def after_cross(i):
        rows = chunk(i)
        h = r.h1[rows] + acc[rows] * keep_of(i)
        r.h2[rows] = h
        r.a3[rows] = norm(h, 2)
        acc[rows] = zeros

    each(chunks, after_cross)
    r.a3t[...] = r.a3[...].T

    reduce = Reduce(
        place, weights, r.half, r.plane, r.line, r.extra, r.total, r.reduce_sems
    )
    plan = {}

    def add(tick, order, step, *args):
        plan.setdefault(tick, []).append((order, len(plan.get(tick, ())), functools.partial(step, *args)))

    def r_tick(tick):
        for _, _, step in sorted(plan.get(tick, ()), key=lambda entry: entry[:2]):
            step()

    def store(g):
        return pltpu.make_async_copy(r.total[g], r.blocks[g], local_sem.at[10 + g])

    starts = {3: [2 * k + 1 for k in range(n)], 2: [2 * k + 1 for k in range(n)]}
    starts[1] = [10 + 2 * k for k in range(n)]
    starts[0] = [19 + 2 * k for k in range(n)]
    for late, g in enumerate((3, 2, 1, 0)):
        for k, tick in enumerate(starts[g]):
            j = block(k) if g > 1 else block_last(k)
            for stage in range(3):
                add(tick + stage, stage, reduce.step, g, j, stage)
        last = starts[g][-1] + (3 if g > 1 else 2)
        add(last, 20 - late, reduce.settle, g)
        for stage in (1, 2):
            add(last + stage, 30 + stage - late, reduce.share, g, stage)
        add(last + 2, 50, lambda g=g: store(g).start())

    def reduce_ticks(*numbers):
        return [functools.partial(r_tick, i) for i in numbers]

    def at_end(k, numbers):
        for kk, number in enumerate(numbers):

            @pl.when(k == kk)
            def _():
                r_tick(number)

    table3 = {(0, 0): ticks(10), (0, 1): ticks(11), (1, 1): ticks(12) + reduce_ticks(2),
              (2, 1): ticks(13) + reduce_ticks(4), (3, 0): ticks(14), (3, 1): reduce_ticks(6)}

    def feed_step(k):
        feed(k, table3)
        at_end(k, [2 * i + 1 for i in range(n)])

    each(n, feed_step)
    r_tick(8)
    out_copy = pltpu.make_async_copy(acc, r.layer_out, local_sem.at[14])

    def after_feed(i):
        rows = chunk(i)
        keep = keep_of(i)
        acc[rows] = r.h2[rows] + (acc[rows] + r.bias_out[...].reshape(1, model)) * keep
        down = r.upstream[rows].astype(F32) + norm_backward(r.h2[rows], 2, da[rows])
        dh[rows] = down
        r.e[rows] = (down * keep).astype(BF16)
        da[rows] = zeros

    each(chunks, after_feed)
    out_copy.start()
    table4 = {(k, 1): reduce_ticks(9 + 2 * k) for k in range(n)}

    def cross_step(k):
        attend_backward(k, table4, 1, r.a2, r.m)
        at_end(k, [10 + 2 * i for i in range(n)])

    each(n, cross_step)
    memory_copy = pltpu.make_async_copy(r.dm, r.memory_out, local_sem.at[15])
    memory_copy.start()

    def before_cross(i):
        rows = chunk(i)
        down = dh[rows] + norm_backward(r.h1[rows], 1, da[rows])
        dh[rows] = down
        r.e[rows] = (down * keep_of(i)).astype(BF16)
        da[rows] = zeros

    each(chunks, before_cross)
    r_tick(17)
    table5 = {(k, 1): reduce_ticks(18 + 2 * k) for k in range(n)}

    def self_step(k):
        attend_backward(k, table5, 0, r.a1, r.a1)
        at_end(k, [19 + 2 * i for i in range(n)])

    each(n, self_step)

    def before_self(i):
        rows = chunk(i)
        dh[rows] = dh[rows] + norm_backward(x[rows].astype(F32), 0, da[rows])

    each(chunks, before_self)
    grad_copy = pltpu.make_async_copy(dh, r.input_grad, local_sem.at[16])
    grad_copy.start()

    small = SumSmall(place, r.slots, r.small_sems)

    def small_start():
        own = r.slots.at[0]
        own[...] = jnp.zeros(own.shape, F32)
        for i in range(6):
            own[i:i + 1, :model] = jnp.sum(r.norm_sums[i], axis=0, keepdims=True)
        own[6:7, :model] = jnp.sum(r.out_sums[...], axis=0, keepdims=True)
        tokens = lengths[place.tp * sentences]
        for b in range(1, sentences):
            tokens = tokens + lengths[place.tp * sentences + b]
        own[7:8] = jnp.full((1, own.shape[1]), tokens.astype(F32))
        for i in range(n):
            own[8 + i:9 + i] = jnp.sum(r.bias_sums[i], axis=0, keepdims=True)
        small.start()

    add(26, 5, small_start)
    for stage in range(2):
        add(27 + stage, 5, small.exchange, stage)
    final = max(plan)
    for tick in range(26, final + 1):
        r_tick(tick)
    r.small_out[...] = small.total()
    bias.finish()
    for copy in (out_copy, memory_copy, grad_copy):
        copy.wait()
    for g in range(4):
        reduce.finish(g)
        store(g).wait()
    small.finish()


def call(kernel, name, ins, outs, scratch, spaces, **options):
    trees = (ins, outs, scratch)
    structure = jax.tree_util.tree_structure(trees)

    def body(*refs):
        groups = jax.tree_util.tree_unflatten(structure, refs)
        kernel(types.SimpleNamespace(**groups[0], **groups[1], **groups[2]))

    def specs(group):
        return [
            pl.BlockSpec(memory_space=spaces.get(key, pltpu.VMEM))
            for key in sorted(group) for _ in jax.tree_util.tree_leaves(group[key])
        ]

    leaves = jax.tree_util.tree_leaves
    values = pl.pallas_call(
        body,
        out_shape=leaves(outs),
        in_specs=specs(ins),
        out_specs=specs(outs),
        scratch_shapes=leaves(scratch),
        compiler_params=pltpu.CompilerParams(**options),
        name=name,
    )(*leaves(ins))
    return types.SimpleNamespace(**jax.tree_util.tree_unflatten(jax.tree_util.tree_structure(outs), values))


def run_layer(ins):
    n, extra = lax.axis_size("tp"), lax.axis_size("dp") // 2
    owned, model = ins["x_in"].shape
    memory, shards = ins["memory_in"], ins["shards"]
    local, units = shards[1].shape[0], ins["bias_in"].shape[0]
    small = (16, units)
    assert n <= 8 and units >= model and memory.shape[0] >= 3
    shapes = [(n, 4 * local, model)] * 2 + [(n,) + shards[5].shape, (n,) + shards[6].shape]
    small_slots = SumSmall.slots(n, extra)

    def vmem(*shape):
        return pltpu.VMEM(shape, BF16)

    def wide(*shape):
        return pltpu.VMEM(shape, F32)

    def eighths(*lead, parts=1):
        return [vmem(*lead, rows * parts // 8, columns) for _, rows, columns in shapes]

    dma = pltpu.SemaphoreType.DMA
    scratch = dict(
        w=[vmem(*shape) for shape in shapes],
        bias=wide(n, 8, units),
        x=vmem(owned, model),
        memory=vmem(*memory.shape),
        upstream=vmem(owned, model),
        a1=vmem(owned, model),
        m=vmem(owned, model),
        h1=wide(owned, model),
        h2=wide(owned, model),
        dh=wide(owned, model),
        acc=wide(owned, model),
        da=wide(owned, model),
        dm=wide(owned, model),
        t=[vmem(n, 3 * local, owned)] * 2,
        c=[vmem(n, local, owned)] * 2,
        p=[vmem(n, owned // LEN * (local // HD), LEN, LEN)] * 2,
        dt=vmem(3 * local, owned),
        dc=vmem(local, owned),
        a3t=vmem(model, owned),
        hidden=vmem(owned, units),
        dhidden=vmem(owned, units),
        bias_sums=wide(n, 8, units),
        norm_sums=wide(6, 8, model),
        out_sums=wide(8, model),
        half=eighths(n, parts=4),
        plane=eighths(n, 3),
        line=eighths(n),
        extra=eighths(extra),
        total=eighths(parts=8),
        slots=wide(small_slots, *small),
        gather_sems=dma((Gather.KINDS, 4, n)),
        bias_sems=dma((3, n)),
        reduce_sems=dma((Reduce.KINDS, 4, max(n, extra))),
        small_sems=dma((2, small_slots)),
        local_sems=dma((17,)),
    )
    rows = jax.ShapeDtypeStruct((owned, model), F32)
    outs = dict(
        layer_out=rows, input_grad=rows, memory_out=rows, small_out=jax.ShapeDtypeStruct(small, F32),
        blocks=[jax.ShapeDtypeStruct(shape[1:], BF16) for shape in shapes],
    )
    smem, hbm = pltpu.SMEM, pl.ANY
    spaces = dict(
        lengths=smem, src_lengths=smem, configs=smem, x_in=hbm, memory_in=hbm, upstream_in=hbm, shards=hbm,
        layer_out=hbm, input_grad=hbm, memory_out=hbm, blocks=hbm,
    )
    return call(
        layer_kernel, "layer", ins, outs, scratch, spaces,
        collective_id=1, has_side_effects=True, vmem_limit_bytes=64 * 2**20,
    )


def finish_kernel(r):
    small, configs, sems = r.small, r.configs, r.sems
    model = r.gain_grad.shape[1]
    layers = r.memory_grad.shape[0]
    place = lax.axis_index("tp")
    local = r.grads[1].shape[0]
    parts = (
        (0, 0, 3 * local), (0, 3 * local, local),
        (1, 0, local), (1, local, 2 * local), (1, 3 * local, local),
        (2, 0, r.block[2].shape[0]), (3, 0, r.block[3].shape[0]),
    )
    loads = [pltpu.make_async_copy(r.blocks[g], r.block[g], sems.at[g]) for g in range(4)]
    rows = [
        pltpu.make_async_copy(source, target, sems.at[4 + i])
        for i, (source, target) in enumerate(((r.layer_in, r.layer), (r.grad_in, r.grad), (r.source_in, r.source)))
    ]
    outs = [pltpu.make_async_copy(r.layer, r.layer_out, sems.at[7]), pltpu.make_async_copy(r.grad, r.input_grad, sems.at[8])]
    for copy in rows[2:] + loads + rows[:2]:
        copy.start()
    inverse = 1.0 / small[7:8, :1]
    r.gain_grad[...] = small[:3, :model] * inverse
    r.shift_grad[...] = small[3:6, :model] * inverse
    r.bias_out_grad[...] = (small[6:7, :model] * inverse).reshape(model)
    r.bias_in_grad[...] = (small[pl.ds(8 + place, 1)] * inverse).reshape(small.shape[1])
    width, depth = configs[0, 0], configs[0, 3]
    factor = (column(1, (1, model)) < width).astype(F32) / jnp.full((1, 1), depth.astype(F32))
    rows[2].wait()

    def spread(i):
        part = pl.ds(pl.multiple_of(i * 64, 64), 64)
        value = r.source[part] * factor
        for level in range(layers):
            chosen = (jnp.full((1, 1), depth) >= layers - level).astype(F32)
            r.memories[level, part] = value * chosen

    each(r.source.shape[0] // 64, spread)
    outs.append(pltpu.make_async_copy(r.memories, r.memory_grad, sems.at[9]))
    outs[2].start()
    for i, (g, start, count) in enumerate(parts):
        if start == 0:
            loads[g].wait()

        def scale(at):
            here = pl.ds(pl.multiple_of(at * 32, 32), 32)
            there = pl.ds(pl.multiple_of(start + at * 32, 32), 32)
            r.wide[g][there] = r.block[g][there].astype(F32) * inverse

        each(count // 32, scale)
        outs.append(pltpu.make_async_copy(r.wide[g].at[pl.ds(start, count)], r.grads[i], sems.at[10 + i]))
        outs[-1].start()
    for i in range(2):
        rows[i].wait()
        outs[i].start()
    for copy in outs:
        copy.wait()


def run_finish(ins, layers):
    blocks, small = ins["blocks"], ins["small"]
    rows = ins["layer_in"].shape
    local, units = blocks[0].shape[0] // 4, small.shape[1]

    def shape(*dims):
        return jax.ShapeDtypeStruct(dims, F32)

    counts = (3 * local, local, local, 2 * local, local)
    outs = dict(
        layer_out=shape(*rows), input_grad=shape(*rows), memory_grad=shape(layers, *rows),
        gain_grad=shape(3, rows[1]), shift_grad=shape(3, rows[1]), bias_in_grad=shape(units), bias_out_grad=shape(rows[1]),
        grads=[shape(count, rows[1]) for count in counts] + [shape(*blocks[2].shape), shape(*blocks[3].shape)],
    )
    scratch = dict(
        layer=pltpu.VMEM(rows, F32), grad=pltpu.VMEM(rows, F32), source=pltpu.VMEM(rows, F32),
        memories=pltpu.VMEM((layers,) + rows, F32),
        block=[pltpu.VMEM(block.shape, BF16) for block in blocks],
        wide=[pltpu.VMEM(block.shape, F32) for block in blocks],
        sems=pltpu.SemaphoreType.DMA((17,)),
    )
    hbm = pl.ANY
    spaces = dict(
        configs=pltpu.SMEM, layer_in=hbm, grad_in=hbm, source_in=hbm, blocks=hbm,
        layer_out=hbm, input_grad=hbm, memory_grad=hbm, grads=hbm,
    )
    return call(finish_kernel, "finish", ins, outs, scratch, spaces, vmem_limit_bytes=60 * 2**20)


def per_device(
    inputs, memory, out_grad, lengths, src_lengths, configs, norm_gain, norm_bias,
    self_qkv, self_out, cross_q, cross_kv, cross_out, ffn_in, ffn_in_bias, ffn_out, ffn_out_bias,
):
    model = inputs.shape[1]
    layers = memory.shape[0]
    local = self_out.shape[0]
    done = run_layer(dict(
        lengths=lengths, src_lengths=src_lengths, configs=configs, gains=norm_gain, shifts=norm_bias,
        bias_in=ffn_in_bias, bias_out=ffn_out_bias, x_in=inputs, memory_in=memory, upstream_in=out_grad,
        shards=[
            self_qkv.transpose(1, 2, 0).reshape(3 * local, model), self_out, cross_q.T,
            cross_kv.transpose(1, 2, 0).reshape(2 * local, model), cross_out, ffn_in, ffn_out,
        ],
    ))
    out = run_finish(dict(
        configs=configs, small=done.small_out, layer_in=done.layer_out, grad_in=done.input_grad,
        source_in=done.memory_out, blocks=done.blocks,
    ), layers)
    grads = out.grads
    return (
        out.layer_out,
        out.input_grad,
        out.memory_grad,
        out.gain_grad,
        out.shift_grad,
        grads[0].reshape(3, local, model).transpose(2, 0, 1),
        grads[1],
        grads[2].T,
        grads[3].reshape(2, local, model).transpose(2, 0, 1),
        grads[4],
        grads[5],
        out.bias_in_grad,
        grads[6],
        out.bias_out_grad,
    )


def solution(mesh):
    rows = P(("grp", "dp", "tp"), None)
    stack = P(None, ("grp", "dp", "tp"), None)
    weights = (
        P(None, None, "tp"), P("tp", None), P(None, "tp"), P(None, None, "tp"), P("tp", None),
        P(None, "tp"), P("tp"), P("tp", None), P(),
    )
    return jax.shard_map(
        per_device,
        mesh=mesh,
        in_specs=(rows, stack, rows, P(("grp", "dp")), P(("grp", "dp")), P("grp", None), P(), P()) + weights,
        out_specs=(rows, rows, stack, P(), P()) + weights,
        check_vma=False,
    )
```

```python
import functools
import types

import jax
import jax.numpy as jnp
from jax import lax
from jax.experimental import pallas as pl
from jax.experimental.pallas import tpu as pltpu
from jax.sharding import PartitionSpec as P

HD = 80
LEN = 256
EPSILON = 1e-05
NEGATIVE = -1e30
SCALE = HD ** (-0.5)
LOG2E = 1.4426950408889634
F32 = jnp.float32
BF16 = jnp.bfloat16


MESH = pl.DeviceIdType.MESH


class Place:
    def __init__(self):
        self.tps = lax.axis_size("tp")
        self.extra = lax.axis_size("dp") // 2
        assert lax.axis_size("grp") == 4 and lax.axis_size("dp") % 2 == 0
        grp, dp, tp = (lax.axis_index(name) for name in ("grp", "dp", "tp"))
        core, low, high = dp % 2, grp % 2, grp // 2
        flip_low, flip_high = grp + 1 - 2 * low, grp + 2 - 4 * high
        self.grp, self.dp, self.tp, self.core = grp, dp, tp, core
        self.first_bit = (1 - core) * low + core * high
        self.second_bit = (1 - core) * high + core * low
        self.first = ((1 - core) * flip_low + core * flip_high, dp, tp)
        self.second = ((1 - core) * flip_high + core * flip_low, dp, tp)
        self.across = (3 - grp, dp, tp)
        self.sibling = (grp, dp + 1 - 2 * core, tp)
        self.above = (grp, dp, tp + 1)
        self.below = (grp, dp, tp - 1)
        self.has_above = tp < self.tps - 1
        self.has_below = tp > 0

    def copy_of(self, step):
        return (self.grp, ((self.dp // 2 + step) % self.extra) * 2 + self.core, self.tp)

    def nth_block(self, k):
        size = self.tps
        upper = (2 * self.tp) // size
        lead = (1 - upper) * self.tp + upper * (size - 1 - self.tp)
        spot = k + (k + size - lead) // size
        return (1 - upper) * spot + upper * (size - 1 - spot)

    def along(self, tp):
        return (self.grp, self.dp, tp)

    def barrier(self):
        sem = pltpu.get_barrier_semaphore()
        partners = [self.first, self.second, self.across, self.sibling]
        partners += [self.along((self.tp + step) % self.tps) for step in range(1, self.tps)]
        partners += [self.copy_of(step) for step in range(1, self.extra)]
        for device in partners:
            pl.semaphore_signal(sem, inc=1, device_id=device, device_id_type=MESH)
        pl.semaphore_wait(sem, len(partners))


def push(src, dst, send_sem, recv_sem, device):
    return pltpu.make_async_remote_copy(
        src_ref=src, dst_ref=dst, send_sem=send_sem, recv_sem=recv_sem, device_id=device, device_id_type=MESH
    )


def rows_of(ref, lead, start, count):
    return ref.at[lead, pl.ds(pl.multiple_of(start, 16), count)]


def add_units(total, term, unit):
    def step(i, carry):
        rows = pl.ds(pl.multiple_of(i * unit, 16), unit)
        total[rows] = total[rows] + term[rows]
        return carry

    lax.fori_loop(0, total.shape[0] // unit, step, 0)


class Spread:
    KINDS = 14

    def __init__(self, place, view, unit, sems, direct=False):
        self.place, self.view, self.unit, self.sems = place, view, unit, sems
        f, s, c = place.first_bit, place.second_bit, place.core
        self.units = (f * 2 + s, f * 2 + 1 - s, (1 - f) * 2 + s, (1 - f) * 2 + 1 - s)
        self.theirs = (s * 2 + f, s * 2 + 1 - f, (1 - s) * 2 + f, (1 - s) * 2 + 1 - f)
        self.table = [
            (place.second, (c, self.units[0]), (c, self.units[1])),
            (place.first, (c, self.units[0]), (c, self.units[2])),
            (place.across if direct else place.first, (c, self.units[0 if direct else 1]), (c, self.units[3])),
        ] + [(place.sibling, (c, u), (1 - c, t)) for u, t in zip(self.units, self.theirs)]
        if direct:
            self.waits = ((), (0, 1, 2), (3, 4, 5, 6))
            self.sends = ((0, 1, 2, 3), (4, 5, 6), ())
        else:
            self.waits = ((), (0,), (1, 2), (3, 4, 5, 6))
            self.sends = ((0, 1, 3), (2, 4), (5, 6), ())

    def region(self, spot):
        half, unit = spot
        return self.view((half * 4 + unit) * self.unit, self.unit)

    def own(self):
        return self.region((self.place.core, self.units[0]))

    def copy(self, n, lands=False):
        device, leaves, landing = self.table[n]
        part = self.region(landing if lands else leaves)
        return push(part, part, self.sems(2 * n), self.sems(2 * n + 1), device)

    def step(self, stage):
        for n in self.waits[stage]:
            self.copy(n, lands=True).wait_recv()
        for n in self.sends[stage]:
            self.copy(n).start()

    def finish(self):
        for n in range(7):
            self.copy(n).wait_send()


class Gather:
    KINDS = Spread.KINDS + 3

    def __init__(self, place, buffers, sems):
        self.place, self.buffers, self.sems = place, buffers, sems
        self.unit = [ref.shape[1] // 8 for ref in buffers]
        self.others = place.tps - 1

    def spread(self, g, j):
        return Spread(
            self.place,
            lambda start, count: rows_of(self.buffers[g], j, start, count),
            self.unit[g],
            lambda kind: self.sems.at[kind, g, j],
        )

    def relays(self, g, j):
        p = self.place
        part = self.spread(g, j).own()
        sem = lambda n: self.sems.at[Spread.KINDS + n, g, j]
        return (
            (jnp.logical_and(j <= p.tp, p.has_above), push(part, part, sem(0), sem(2), p.above)),
            (jnp.logical_and(j >= p.tp, p.has_below), push(part, part, sem(1), sem(2), p.below)),
        )

    def start(self, g):
        for needed, copy in self.relays(g, self.place.tp):
            pl.when(needed)(copy.start)

    def step(self, g, k, stage):
        j = self.place.nth_block(k)
        if stage == 0:
            relays = self.relays(g, j)
            relays[0][1].wait_recv()
            for needed, copy in relays:
                pl.when(needed)(copy.start)
        self.spread(g, j).step(stage)

    def drain(self, g, j):
        for needed, copy in self.relays(g, j):
            pl.when(needed)(copy.wait_send)

        @pl.when(j != self.place.tp)
        def _():
            self.spread(g, j).finish()


class Line:
    def __init__(self, place, buffer, sems):
        self.place, self.buffer, self.sems = place, buffer, sems

    def relays(self, j):
        p = self.place
        part = self.buffer.at[j]
        return (
            (jnp.logical_and(j <= p.tp, p.has_above), push(part, part, self.sems.at[0, j], self.sems.at[2, j], p.above)),
            (jnp.logical_and(j >= p.tp, p.has_below), push(part, part, self.sems.at[1, j], self.sems.at[2, j], p.below)),
        )

    def start(self):
        for needed, copy in self.relays(self.place.tp):
            pl.when(needed)(copy.start)

    def step(self, k):
        j = self.place.nth_block(k)
        relays = self.relays(j)
        relays[0][1].wait_recv()
        for needed, copy in relays:
            pl.when(needed)(copy.start)

    def finish(self):
        for j in range(self.place.tps):
            for needed, copy in self.relays(j):
                pl.when(needed)(copy.wait_send)


class Reduce:
    KINDS = 8 + 6 + 2 + Spread.KINDS + 2

    def __init__(self, place, grads, halves, planes, lines, extras, totals, sems):
        self.place, self.grads, self.totals, self.sems = place, grads, totals, sems
        self.halves, self.planes, self.lines, self.extras = halves, planes, lines, extras
        self.unit = [ref.shape[1] // 8 for ref in grads]

    def sem(self, kind, g, j):
        return self.sems.at[kind, g, j]

    def rows(self, g, j, half, unit, count=1):
        size = self.unit[g]
        return rows_of(self.grads[g], j, (half * 4 + unit) * size, count * size)

    def to_sibling(self, g, j):
        p = self.place
        return [push(self.rows(g, j, 1 - p.core, 0, 4), self.halves[g].at[j], self.sem(0, g, j), self.sem(1, g, j), p.sibling)]

    def in_plane(self, g, j):
        p = self.place
        f, s = p.first_bit, p.second_bit
        goals = ((p.second, f * 2 + 1 - s), (p.first, (1 - f) * 2 + s), (p.across, (1 - f) * 2 + 1 - s))
        return [
            push(
                self.rows(g, j, p.core, u), self.planes[g].at[j, i],
                self.sem(8 + 2 * i, g, j), self.sem(9 + 2 * i, g, j), device,
            )
            for i, (device, u) in enumerate(goals)
        ]

    def piece(self, g, j):
        p = self.place
        return self.rows(g, j, p.core, p.first_bit * 2 + p.second_bit)

    def along(self, g, j):
        p = self.place
        return push(self.piece(g, j), self.lines[g].at[p.tp], self.sem(14, g, j), self.sem(15, g, p.tp), p.along(j))

    def from_place(self, g, j):
        p = self.place
        return push(self.piece(g, j), self.lines[g].at[j], self.sem(14, g, j), self.sem(15, g, j), p.along(j))

    def step(self, g, j, stage):
        p = self.place
        if stage == 0:
            for copy in self.to_sibling(g, j):
                copy.start()
        if stage == 1:
            for copy in self.to_sibling(g, j):
                copy.wait_recv()
            add_units(self.rows(g, j, p.core, 0, 4), self.halves[g].at[j], self.unit[g])
            for copy in self.in_plane(g, j):
                copy.start()
        if stage == 2:
            for copy in self.in_plane(g, j):
                copy.wait_recv()
            a, b, c = (self.planes[g][j, i].astype(F32) for i in range(3))
            piece = self.piece(g, j)
            piece[...] = ((piece[...].astype(F32) + a) + (b + c)).astype(BF16)
            pl.when(j != p.tp)(self.along(g, j).start)

    def spread(self, g):
        return Spread(
            self.place,
            lambda start, count: self.totals[g].at[pl.ds(pl.multiple_of(start, 16), count)],
            self.unit[g],
            lambda kind: self.sems.at[16 + kind, g, 0],
            direct=True,
        )

    def copies(self, g, step):
        p = self.place
        base = self.KINDS - 2
        return push(
            self.piece(g, p.tp), self.extras[g].at[step], self.sem(base, g, step), self.sem(base + 1, g, step), p.copy_of(step)
        )

    def settle(self, g):
        p = self.place
        piece = self.piece(g, p.tp)
        total = piece[...].astype(F32)
        for k in range(p.tps - 1):
            j = p.nth_block(k)
            self.from_place(g, j).wait_recv()
            total = total + self.lines[g][j].astype(F32)
        if p.extra > 1:
            piece[...] = total.astype(BF16)
            for step in range(1, p.extra):
                self.copies(g, step).start()
            for step in range(1, p.extra):
                self.copies(g, step).wait()
                total = total + self.extras[g][step].astype(F32)
        own = self.spread(g).own()
        own[...] = total.astype(BF16)
        self.spread(g).step(0)

    def share(self, g, stage):
        self.spread(g).step(stage)

    def finish(self, g):
        p = self.place
        for j in range(p.tps):
            for copy in self.to_sibling(g, j) + self.in_plane(g, j):
                copy.wait_send()
            pl.when(j != p.tp)(self.along(g, j).wait_send)
        self.spread(g).finish()


class SumSmall:
    @staticmethod
    def slots(tps, extra):
        return 8 + tps + extra

    def __init__(self, place, slots, sems):
        self.place, self.slots_ref, self.sems = place, slots, sems

    def move(self, source, target, device, kind):
        slots = self.slots_ref
        return push(slots.at[source], slots.at[target], self.sems.at[0, kind], self.sems.at[1, target], device)

    def in_plane(self):
        p = self.place
        return [self.move(2, 3 + i, device, 3 + i) for i, device in enumerate((p.second, p.first, p.across))]

    def copies(self):
        p = self.place
        return [self.move(6, 8 + p.tps + s, p.copy_of(s), 8 + p.tps + s) for s in range(1, p.extra)]

    def along(self, k, lands=False):
        p = self.place
        j = p.nth_block(k)
        return self.move(7, 8 + (j if lands else p.tp), p.along(j), 8 + j)

    def start(self):
        self.move(0, 1, self.place.sibling, 1).start()

    def exchange(self, stage):
        p, slots = self.place, self.slots_ref
        if stage == 0:
            self.move(0, 1, p.sibling, 1).wait_recv()
            slots[2] = slots[0] + slots[1]
            for copy in self.in_plane():
                copy.start()
        else:
            for copy in self.in_plane():
                copy.wait_recv()
            slots[6] = (slots[2] + slots[3]) + (slots[4] + slots[5])
            for copy in self.copies():
                copy.start()
            total = slots[6]
            for s, copy in enumerate(self.copies()):
                copy.wait_recv()
                total = total + slots[9 + p.tps + s]
            slots[7] = total
            for k in range(p.tps - 1):
                self.along(k).start()

    def total(self):
        p, slots = self.place, self.slots_ref
        value = slots[7]
        for k in range(p.tps - 1):
            self.along(k, lands=True).wait_recv()
            value = value + slots[8 + p.nth_block(k)]
        return value

    def finish(self):
        p = self.place
        self.move(0, 1, p.sibling, 1).wait_send()
        for copy in self.in_plane() + self.copies():
            copy.wait_send()
        for k in range(p.tps - 1):
            self.along(k).wait_send()


def dot_nn(left, right):
    return lax.dot_general(left, right, (((1,), (0,)), ((), ())), preferred_element_type=F32)


def dot_nt(left, right):
    return lax.dot_general(left, right, (((1,), (1,)), ((), ())), preferred_element_type=F32)


def dot_tn(left, right):
    return lax.dot_general(left, right, (((0,), (0,)), ((), ())), preferred_element_type=F32)


def column(axis, shape):
    return lax.broadcasted_iota(jnp.int32, shape, axis)


def each(count, step):

    def run(i, carry):
        step(i)
        return carry

    lax.fori_loop(0, count, run, 0)


CHUNK = 32
CUBE = 0.044715
ROOT = 0.7978845608028654


def layer_kernel(r):
    r.a2, r.a3, r.e = (r.memory.at[i] for i in range(3))
    columns = pl.ds(0, r.x.shape[1])
    r.dh, r.dm = r.before.at[:, columns], r.down.at[:, columns]
    place = Place()
    n = place.tps
    x, model = r.x, r.x.shape[1]
    owned = x.shape[0]
    sentences = owned // LEN
    local = r.c[0].shape[1]
    heads_here = local // HD
    units = r.hidden.shape[1]
    layers = r.memory.shape[0]
    weights = r.w
    lengths, sources, configs = r.lengths, r.src_lengths, r.configs
    width, heads, hidden_units, depth = (configs[0, i] for i in range(4))
    inv_width = 1.0 / jnp.full((1, 1), width.astype(F32))
    inv_depth = 1.0 / jnp.full((1, 1), depth.astype(F32))
    width_mask = (column(1, (1, model)) < width).astype(F32)

    local_sem = r.local_sems
    spots = (
        (0, 0, 3 * local), (0, 3 * local, local),
        (1, 0, local), (1, local, 2 * local), (1, 3 * local, local),
        (2, 0, weights[2].shape[1]), (3, 0, weights[3].shape[1]),
    )
    fills = [
        (g, pltpu.make_async_copy(r.shards[i], weights[g].at[place.tp, pl.ds(start, size)], local_sem.at[i]))
        for i, (g, start, size) in enumerate(spots)
    ]
    loads = [
        pltpu.make_async_copy(source, target, local_sem.at[7 + i])
        for i, (source, target) in enumerate(((r.x_in, r.x), (r.memory_in, r.memory), (r.upstream_in, r.upstream)))
    ]
    for _, copy in fills[:2]:
        copy.start()
    loads[0].start()
    for _, copy in fills[2:]:
        copy.start()
    loads[1].start()
    loads[2].start()
    r.bias[place.tp] = jnp.broadcast_to(r.bias_in[...].reshape(1, units), r.bias.shape[1:])
    place.barrier()

    gather = Gather(place, weights, r.gather_sems)
    bias = Line(place, r.bias, r.bias_sems)
    for g in range(4):
        for group, copy in fills:
            if group == g:
                copy.wait()
        gather.start(g)
        if g == 0:
            bias.start()
    order = [(g, k) for g in (0, 1) for k in range(n - 1)] + [(g, k) for k in range(n - 1) for g in (2, 3)]

    def g_tick(tick):
        for stage in range(4):
            if 0 <= tick - stage < len(order):
                gather.step(*order[tick - stage], stage)

    def block(k):
        later = (k + n - 1) // n
        return (1 - later) * place.tp + later * place.nth_block(k - 1)

    def block_last(k):
        own = k // (n - 1)
        return own * place.tp + (1 - own) * place.nth_block(k)

    def hooks(table, k, b):
        for (kk, bb), steps in table.items():

            @pl.when(jnp.logical_and(k == kk, b == bb))
            def _():
                for step in steps:
                    step()

    def chunk(i):
        return pl.ds(pl.multiple_of(i * CHUNK, CHUNK), CHUNK)

    def keep_of(i):
        per = LEN // CHUNK
        spot = column(0, (CHUNK, 1)) + (i % per) * CHUNK
        return (spot < lengths[place.tp * sentences + i // per]).astype(F32) * width_mask

    def norm_parts(rows):
        mean = jnp.sum(rows * width_mask, axis=-1, keepdims=True) * inv_width
        centred = (rows - mean) * width_mask
        spread = jnp.sum(centred * centred, axis=-1, keepdims=True) * inv_width
        rstd = lax.rsqrt(spread + EPSILON)
        return centred * rstd, rstd

    def norm(rows, which):
        hat, _ = norm_parts(rows)
        return ((hat * r.gains[which:which + 1] + r.shifts[which:which + 1]) * width_mask).astype(BF16)

    def fold(values):
        return jnp.sum(values.reshape(values.shape[0] // 8, 8, values.shape[1]), axis=0)

    def norm_backward(rows, which, upstream):
        hat, rstd = norm_parts(rows)
        upstream = upstream * width_mask
        sums = r.norm_sums
        sums[which] = sums[which] + fold(upstream * hat)
        sums[3 + which] = sums[3 + which] + fold(upstream)
        scaled = upstream * r.gains[which:which + 1]
        first = jnp.sum(scaled, axis=-1, keepdims=True) * inv_width
        second = jnp.sum(scaled * hat, axis=-1, keepdims=True) * inv_width
        return (rstd * (scaled - first - hat * second)) * width_mask

    chunks = owned // CHUNK

    def each_chunk(step):

        def two(i):
            step(2 * i)
            step(2 * i + 1)

        each(chunks // 2, two)

    acc, da, dh = r.acc, r.da, r.dh
    zeros = jnp.zeros((CHUNK, model), F32)
    r.norm_sums[...] = jnp.zeros(r.norm_sums.shape, F32)
    r.bias_sums[...] = jnp.zeros(r.bias_sums.shape, F32)

    def sentence(b):
        return pl.ds(pl.multiple_of(b * LEN, LEN), LEN)

    def head_keep(j, h):
        return jnp.where(j * heads_here + h < heads, 1.0, 0.0).astype(F32)

    def causal(b, start):
        return column(0, (LEN, 128)) <= column(1, (LEN, 128)) + start

    def crossing(b, start):
        return column(0, (LEN, 1)) < sources[place.tp * sentences + b]

    def bands(h):
        return [pl.ds(i * local + h * HD, HD) for i in range(3)]

    def lanes(b):
        return pl.ds(b * LEN, LEN)

    pairs = [(b, h) for b in range(sentences) for h in range(heads_here)]

    quarters = [(i, b, h, start) for i, (b, h) in enumerate(pairs) for start in range(0, LEN, 128)]

    def attend(k, table, g, allowed):
        w, t, c, p = weights[g], r.t[g], r.c[g], r.p[g]
        j = block(k)
        hooks(table, k, 0)
        if g == 0:
            t[j] = dot_nn(w[j, :3 * local], r.flip[0][...]).astype(BF16)
        else:
            t[j, :local] = dot_nn(w[j, :local], r.flip[0][...]).astype(BF16)
            t[j, local:] = dot_nn(w[j, local:3 * local], r.flip[1][...]).astype(BF16)
        heads_of = [[t[j, band, lanes(b)] for band in bands(h)] for b, h in pairs]
        for i, (query, keys, _) in enumerate(heads_of):
            r.scores[i] = dot_tn(keys, query)
        for i, b, h, start in quarters:
            part = pl.ds(start, 128)
            score = jnp.where(allowed(b, start), r.scores[i, :, part], NEGATIVE)
            raised = jnp.exp2((score - jnp.max(score, axis=0, keepdims=True)) * (SCALE * LOG2E))
            p[j, i, :, part] = (raised * (1.0 / jnp.sum(raised, axis=0, keepdims=True))).astype(BF16)
        for i, (b, h) in enumerate(pairs):
            c[j, pl.ds(h * HD, HD), lanes(b)] = (dot_nn(heads_of[i][2], p[j, i]) * head_keep(j, h)).astype(BF16)
        hooks(table, k, 1)
        acc[...] = acc[...] + dot_tn(c[j], w[j, 3 * local:])

    def attend_backward(k, table, g, query_rows, key_rows):
        w, t, c, p = weights[g], r.t[g], r.c[g], r.p[g]
        j = block_last(k)
        e, dt, dc = r.e, r.dt, r.dc
        dc_all = dot_nn(w[j, 3 * local:], r.flip[0][...])
        for h in range(heads_here):
            dc[h * HD:(h + 1) * HD] = (dc_all[h * HD:(h + 1) * HD] * head_keep(j, h)).astype(BF16)
        heads_of = [[t[j, band, lanes(b)] for band in bands(h)] for b, h in pairs]
        dc_of = [dc[h * HD:(h + 1) * HD, lanes(b)] for b, h in pairs]
        for i, (_, _, values) in enumerate(heads_of):
            r.scores[i] = dot_tn(values, dc_of[i])
        for i, b, h, start in quarters:
            part = pl.ds(start, 128)
            dp, wide = r.scores[i, :, part], p[j, i, :, part].astype(F32)
            r.ds[i, :, part] = (wide * (dp - jnp.sum(dp * wide, axis=0, keepdims=True))).astype(BF16)
        for i, (b, h) in enumerate(pairs):
            (query, keys, _), (dq, dk, dv) = heads_of[i], bands(h)
            dt[dv, lanes(b)] = dot_nt(dc_of[i], p[j, i]).astype(BF16)
            dt[dq, lanes(b)] = (dot_nn(keys, r.ds[i]) * SCALE).astype(BF16)
            dt[dk, lanes(b)] = (dot_nt(query, r.ds[i]) * SCALE).astype(BF16)
        hooks(table, k, 1)
        gather.drain(g, j)
        if g == 0:
            da[...] = da[...] + dot_tn(dt[...], w[j, :3 * local])
            w[j, :3 * local] = dot_nn(dt[...], query_rows[...]).astype(BF16)
        else:
            da[...] = da[...] + dot_tn(dt[:local], w[j, :local])
            r.dm[...] = r.dm[...] + dot_tn(dt[local:], w[j, local:3 * local])
            w[j, :local] = dot_nn(dt[:local], query_rows[...]).astype(BF16)
            w[j, local:3 * local] = dot_nn(dt[local:], key_rows[...]).astype(BF16)
        w[j, 3 * local:] = dot_nn(c[j], e[...]).astype(BF16)

    def feed(k, table):
        j = block(k)
        w_up, w_down = weights[2], weights[3]
        hooks(table, k, 0)
        r.before[...] = dot_nn(r.a3[...], w_up[j]) + r.bias[j, 0:1]
        r.down[...] = dot_nt(r.e[...], w_down[j])
        step_lanes = units // 2

        def bend(i):
            rows = pl.ds(pl.multiple_of(i * 16, 16), 16)
            for start in range(0, units, step_lanes):
                part = pl.ds(start, step_lanes)
                unit = column(1, (1, step_lanes)) + (j * units + start)
                kept = jnp.where(unit < hidden_units, 0.5, 0.0)
                before = r.before[rows, part]
                square = before * before
                bent = jnp.tanh(before * (ROOT + ROOT * CUBE * square))
                half = kept + kept * bent
                through = before * half
                r.hidden[rows, part] = through.astype(BF16)
                slope = half + (through - through * bent) * (ROOT + 3.0 * CUBE * ROOT * square)
                du = (r.down[rows, part] * slope).astype(BF16)
                r.dhidden[rows, part] = du
                r.bias_sums[j, :, part] = r.bias_sums[j, :, part] + fold(du.astype(F32))

        each(owned // 16, bend)
        hooks(table, k, 1)
        acc[...] = acc[...] + dot_nn(r.hidden[...], w_down[j])
        da[...] = da[...] + dot_nt(r.dhidden[...], w_up[j])
        gather.drain(2, j)
        gather.drain(3, j)
        w_down[j] = dot_tn(r.hidden[...], r.e[...]).astype(BF16)
        w_up[j] = dot_nn(r.flip[0][...], r.dhidden[...]).astype(BF16)

    loads[0].wait()

    def begin(i):
        rows = chunk(i)
        r.a1[rows] = norm(x[rows].astype(F32), 0)
        acc[rows] = zeros
        da[rows] = zeros

    each_chunk(begin)
    r.flip[0][...] = r.a1[...].T
    g_tick(0)
    loads[1].wait()

    def mix(i):
        rows = chunk(i)
        total = jnp.zeros((CHUNK, model), F32)
        for level in range(layers):
            chosen = (jnp.full((1, 1), depth) >= layers - level).astype(F32)
            total = total + chosen * r.memory[level, rows].astype(F32)
        r.m[rows] = (total * inv_depth * width_mask).astype(BF16)

    each_chunk(mix)
    r.flip[1][...] = r.m[...].T
    loads[2].wait()
    r.out_sums[...] = jnp.zeros(r.out_sums.shape, F32)

    def grad_in(i):
        rows = chunk(i)
        masked = r.upstream[rows].astype(F32) * keep_of(i)
        r.out_sums[...] = r.out_sums[...] + fold(masked)
        r.e[rows] = masked.astype(BF16)

    each_chunk(grad_in)

    def ticks(*numbers):
        return [functools.partial(g_tick, i) for i in numbers]

    others = n - 1
    assert n == 4
    table = {
        (0, 1): ticks(1),
        (1, 0): ticks(2, 3) + [functools.partial(bias.step, 0)],
        (2, 0): ticks(4) + [functools.partial(bias.step, 1)],
        (3, 0): ticks(5) + [functools.partial(bias.step, 2)],
    }
    each(n, lambda k: attend(k, table, 0, causal))

    def after_self(i):
        rows = chunk(i)
        h = x[rows].astype(F32) + acc[rows] * keep_of(i)
        r.h1[rows] = h
        r.a2[rows] = norm(h, 1)
        acc[rows] = zeros

    each_chunk(after_self)
    r.flip[0][...] = r.a2[...].T
    table2 = {(k, 0): ticks(6 + k) for k in range(n)}
    each(n, lambda k: attend(k, table2, 1, crossing))

    def after_cross(i):
        rows = chunk(i)
        h = r.h1[rows] + acc[rows] * keep_of(i)
        r.h2[rows] = h
        r.a3[rows] = norm(h, 2)
        acc[rows] = zeros

    each_chunk(after_cross)
    r.flip[0][...] = r.a3[...].T

    reduce = Reduce(
        place, weights, r.half, r.plane, r.line, r.extra, r.total, r.reduce_sems
    )
    plan = {}

    def add(tick, order, step, *args):
        plan.setdefault(tick, []).append((order, len(plan.get(tick, ())), functools.partial(step, *args)))

    def r_tick(tick):
        for _, _, step in sorted(plan.get(tick, ()), key=lambda entry: entry[:2]):
            step()

    def store(g):
        return pltpu.make_async_copy(r.total[g], r.blocks[g], local_sem.at[10 + g])

    starts = {3: [2 * k + 1 for k in range(n)], 2: [2 * k + 1 for k in range(n)]}
    starts[1] = [10 + 2 * k for k in range(n)]
    starts[0] = [19 + 2 * k for k in range(n)]
    for late, g in enumerate((3, 2, 1, 0)):
        for k, tick in enumerate(starts[g]):
            j = block(k) if g > 1 else block_last(k)
            for stage in range(3):
                add(tick + stage, stage, reduce.step, g, j, stage)
        last = starts[g][-1] + (3 if g > 1 else 2)
        add(last, 20 - late, reduce.settle, g)
        for stage in (1, 2):
            add(last + stage, 30 + stage - late, reduce.share, g, stage)
        add(last + 2, 50, lambda g=g: store(g).start())

    def reduce_ticks(*numbers):
        return [functools.partial(r_tick, i) for i in numbers]

    def at_end(k, numbers):
        for kk, number in enumerate(numbers):

            @pl.when(k == kk)
            def _():
                r_tick(number)

    table3 = {(0, 0): ticks(10), (0, 1): ticks(11), (1, 1): ticks(12) + reduce_ticks(2),
              (2, 1): ticks(13) + reduce_ticks(4), (3, 0): ticks(14), (3, 1): reduce_ticks(6)}

    def feed_step(k):
        feed(k, table3)
        at_end(k, [2 * i + 1 for i in range(n)])

    each(n, feed_step)
    r_tick(8)
    out_copy = pltpu.make_async_copy(acc, r.layer_out, local_sem.at[14])

    def after_feed(i):
        rows = chunk(i)
        keep = keep_of(i)
        acc[rows] = r.h2[rows] + (acc[rows] + r.bias_out[...].reshape(1, model)) * keep
        down = r.upstream[rows].astype(F32) + norm_backward(r.h2[rows], 2, da[rows])
        dh[rows] = down
        r.e[rows] = (down * keep).astype(BF16)
        da[rows] = zeros
        r.dm[rows] = zeros

    each_chunk(after_feed)
    r.flip[0][...] = r.e[...].T
    out_copy.start()
    table4 = {(k, 1): reduce_ticks(9 + 2 * k) for k in range(n)}

    def cross_step(k):
        attend_backward(k, table4, 1, r.a2, r.m)
        at_end(k, [10 + 2 * i for i in range(n)])

    each(n, cross_step)
    memory_copy = pltpu.make_async_copy(r.dm, r.memory_out, local_sem.at[15])
    memory_copy.start()

    def before_cross(i):
        rows = chunk(i)
        down = dh[rows] + norm_backward(r.h1[rows], 1, da[rows])
        dh[rows] = down
        r.e[rows] = (down * keep_of(i)).astype(BF16)
        da[rows] = zeros

    each_chunk(before_cross)
    r.flip[0][...] = r.e[...].T
    r_tick(17)
    table5 = {(k, 1): reduce_ticks(18 + 2 * k) for k in range(n)}

    def self_step(k):
        attend_backward(k, table5, 0, r.a1, r.a1)
        at_end(k, [19 + 2 * i for i in range(n)])

    each(n, self_step)

    def before_self(i):
        rows = chunk(i)
        dh[rows] = dh[rows] + norm_backward(x[rows].astype(F32), 0, da[rows])

    each_chunk(before_self)
    grad_copy = pltpu.make_async_copy(dh, r.input_grad, local_sem.at[16])
    grad_copy.start()

    small = SumSmall(place, r.slots, r.small_sems)

    def small_start():
        own = r.slots.at[0]
        own[...] = jnp.zeros(own.shape, F32)
        for i in range(6):
            own[i:i + 1, :model] = jnp.sum(r.norm_sums[i], axis=0, keepdims=True)
        own[6:7, :model] = jnp.sum(r.out_sums[...], axis=0, keepdims=True)
        tokens = lengths[place.tp * sentences]
        for b in range(1, sentences):
            tokens = tokens + lengths[place.tp * sentences + b]
        own[7:8] = jnp.full((1, own.shape[1]), tokens.astype(F32))
        for i in range(n):
            own[8 + i:9 + i] = jnp.sum(r.bias_sums[i], axis=0, keepdims=True)
        small.start()

    add(26, 5, small_start)
    for stage in range(2):
        add(27 + stage, 5, small.exchange, stage)
    final = max(plan)
    for tick in range(26, final + 1):
        r_tick(tick)
    r.small_out[...] = small.total()
    bias.finish()
    for copy in (out_copy, memory_copy, grad_copy):
        copy.wait()
    for g in range(4):
        reduce.finish(g)
        store(g).wait()
    small.finish()


def call(kernel, name, ins, outs, scratch, spaces, **options):
    trees = (ins, outs, scratch)
    structure = jax.tree_util.tree_structure(trees)

    def body(*refs):
        groups = jax.tree_util.tree_unflatten(structure, refs)
        kernel(types.SimpleNamespace(**groups[0], **groups[1], **groups[2]))

    def specs(group):
        return [
            pl.BlockSpec(memory_space=spaces.get(key, pltpu.VMEM))
            for key in sorted(group) for _ in jax.tree_util.tree_leaves(group[key])
        ]

    leaves = jax.tree_util.tree_leaves
    values = pl.pallas_call(
        body,
        out_shape=leaves(outs),
        in_specs=specs(ins),
        out_specs=specs(outs),
        scratch_shapes=leaves(scratch),
        compiler_params=pltpu.CompilerParams(**options),
        name=name,
    )(*leaves(ins))
    return types.SimpleNamespace(**jax.tree_util.tree_unflatten(jax.tree_util.tree_structure(outs), values))


def run_layer(ins):
    n, extra = lax.axis_size("tp"), lax.axis_size("dp") // 2
    owned, model = ins["x_in"].shape
    memory, shards = ins["memory_in"], ins["shards"]
    local, units = shards[1].shape[0], ins["bias_in"].shape[0]
    small = (16, units)
    assert n <= 8 and units >= model and memory.shape[0] >= 3
    shapes = [(n, 4 * local, model)] * 2 + [(n,) + shards[5].shape, (n,) + shards[6].shape]
    small_slots = SumSmall.slots(n, extra)

    def vmem(*shape):
        return pltpu.VMEM(shape, BF16)

    def wide(*shape):
        return pltpu.VMEM(shape, F32)

    def eighths(*lead, parts=1):
        return [vmem(*lead, rows * parts // 8, columns) for _, rows, columns in shapes]

    dma = pltpu.SemaphoreType.DMA
    scratch = dict(
        w=[vmem(*shape) for shape in shapes],
        bias=wide(n, 8, units),
        x=vmem(owned, model),
        memory=vmem(*memory.shape),
        upstream=vmem(owned, model),
        a1=vmem(owned, model),
        m=vmem(owned, model),
        h1=wide(owned, model),
        h2=wide(owned, model),
        acc=wide(owned, model),
        da=wide(owned, model),
        t=[vmem(n, 3 * local, owned)] * 2,
        c=[vmem(n, local, owned)] * 2,
        p=[vmem(n, owned // LEN * (local // HD), LEN, LEN)] * 2,
        dt=vmem(3 * local, owned),
        dc=vmem(local, owned),
        flip=[vmem(model, owned)] * 2,
        scores=wide(owned // LEN * (local // HD), LEN, LEN),
        ds=vmem(owned // LEN * (local // HD), LEN, LEN),
        before=wide(owned, units),
        down=wide(owned, units),
        hidden=vmem(owned, units),
        dhidden=vmem(owned, units),
        bias_sums=wide(n, 8, units),
        norm_sums=wide(6, 8, model),
        out_sums=wide(8, model),
        half=eighths(n, parts=4),
        plane=eighths(n, 3),
        line=eighths(n),
        extra=eighths(extra),
        total=eighths(parts=8),
        slots=wide(small_slots, *small),
        gather_sems=dma((Gather.KINDS, 4, n)),
        bias_sems=dma((3, n)),
        reduce_sems=dma((Reduce.KINDS, 4, max(n, extra))),
        small_sems=dma((2, small_slots)),
        local_sems=dma((17,)),
    )
    rows = jax.ShapeDtypeStruct((owned, model), F32)
    outs = dict(
        layer_out=rows, input_grad=rows, memory_out=rows, small_out=jax.ShapeDtypeStruct(small, F32),
        blocks=[jax.ShapeDtypeStruct(shape[1:], BF16) for shape in shapes],
    )
    smem, hbm = pltpu.SMEM, pl.ANY
    spaces = dict(
        lengths=smem, src_lengths=smem, configs=smem, x_in=hbm, memory_in=hbm, upstream_in=hbm, shards=hbm,
        layer_out=hbm, input_grad=hbm, memory_out=hbm, blocks=hbm,
    )
    return call(
        layer_kernel, "layer", ins, outs, scratch, spaces,
        collective_id=1, has_side_effects=True, vmem_limit_bytes=64 * 2**20,
    )


def finish_kernel(r):
    small, configs, sems = r.small, r.configs, r.sems
    model = r.gain_grad.shape[1]
    layers = r.memory_grad.shape[0]
    place = lax.axis_index("tp")
    local = r.grads[1].shape[0]
    parts = (
        (0, 0, 3 * local), (0, 3 * local, local),
        (1, 0, local), (1, local, 2 * local), (1, 3 * local, local),
        (2, 0, r.block[2].shape[0]), (3, 0, r.block[3].shape[0]),
    )
    loads = [pltpu.make_async_copy(r.blocks[g], r.block[g], sems.at[g]) for g in range(4)]
    rows = [
        pltpu.make_async_copy(source, target, sems.at[4 + i])
        for i, (source, target) in enumerate(((r.layer_in, r.layer), (r.grad_in, r.grad), (r.source_in, r.source)))
    ]
    outs = [pltpu.make_async_copy(r.layer, r.layer_out, sems.at[7]), pltpu.make_async_copy(r.grad, r.input_grad, sems.at[8])]
    for copy in rows[2:] + loads + rows[:2]:
        copy.start()
    inverse = 1.0 / small[7:8, :1]
    r.gain_grad[...] = small[:3, :model] * inverse
    r.shift_grad[...] = small[3:6, :model] * inverse
    r.bias_out_grad[...] = (small[6:7, :model] * inverse).reshape(model)
    r.bias_in_grad[...] = (small[pl.ds(8 + place, 1)] * inverse).reshape(small.shape[1])
    width, depth = configs[0, 0], configs[0, 3]
    factor = (column(1, (1, model)) < width).astype(F32) / jnp.full((1, 1), depth.astype(F32))
    rows[2].wait()

    def spread(i):
        part = pl.ds(pl.multiple_of(i * 64, 64), 64)
        value = r.source[part] * factor
        for level in range(layers):
            chosen = (jnp.full((1, 1), depth) >= layers - level).astype(F32)
            r.memories[level, part] = value * chosen

    each(r.source.shape[0] // 64, spread)
    outs.append(pltpu.make_async_copy(r.memories, r.memory_grad, sems.at[9]))
    outs[2].start()
    for i, (g, start, count) in enumerate(parts):
        if start == 0:
            loads[g].wait()

        def scale(at):
            here = pl.ds(pl.multiple_of(at * 32, 32), 32)
            there = pl.ds(pl.multiple_of(start + at * 32, 32), 32)
            r.wide[g][there] = r.block[g][there].astype(F32) * inverse

        each(count // 32, scale)
        outs.append(pltpu.make_async_copy(r.wide[g].at[pl.ds(start, count)], r.grads[i], sems.at[10 + i]))
        outs[-1].start()
    for i in range(2):
        rows[i].wait()
        outs[i].start()
    for copy in outs:
        copy.wait()


def run_finish(ins, layers):
    blocks, small = ins["blocks"], ins["small"]
    rows = ins["layer_in"].shape
    local, units = blocks[0].shape[0] // 4, small.shape[1]

    def shape(*dims):
        return jax.ShapeDtypeStruct(dims, F32)

    counts = (3 * local, local, local, 2 * local, local)
    outs = dict(
        layer_out=shape(*rows), input_grad=shape(*rows), memory_grad=shape(layers, *rows),
        gain_grad=shape(3, rows[1]), shift_grad=shape(3, rows[1]), bias_in_grad=shape(units), bias_out_grad=shape(rows[1]),
        grads=[shape(count, rows[1]) for count in counts] + [shape(*blocks[2].shape), shape(*blocks[3].shape)],
    )
    scratch = dict(
        layer=pltpu.VMEM(rows, F32), grad=pltpu.VMEM(rows, F32), source=pltpu.VMEM(rows, F32),
        memories=pltpu.VMEM((layers,) + rows, F32),
        block=[pltpu.VMEM(block.shape, BF16) for block in blocks],
        wide=[pltpu.VMEM(block.shape, F32) for block in blocks],
        sems=pltpu.SemaphoreType.DMA((17,)),
    )
    hbm = pl.ANY
    spaces = dict(
        configs=pltpu.SMEM, layer_in=hbm, grad_in=hbm, source_in=hbm, blocks=hbm,
        layer_out=hbm, input_grad=hbm, memory_grad=hbm, grads=hbm,
    )
    return call(finish_kernel, "finish", ins, outs, scratch, spaces, vmem_limit_bytes=60 * 2**20)


def per_device(
    inputs, memory, out_grad, lengths, src_lengths, configs, norm_gain, norm_bias,
    self_qkv, self_out, cross_q, cross_kv, cross_out, ffn_in, ffn_in_bias, ffn_out, ffn_out_bias,
):
    model = inputs.shape[1]
    layers = memory.shape[0]
    local = self_out.shape[0]
    done = run_layer(dict(
        lengths=lengths, src_lengths=src_lengths, configs=configs, gains=norm_gain, shifts=norm_bias,
        bias_in=ffn_in_bias, bias_out=ffn_out_bias, x_in=inputs, memory_in=memory, upstream_in=out_grad,
        shards=[
            self_qkv.transpose(1, 2, 0).reshape(3 * local, model), self_out, cross_q.T,
            cross_kv.transpose(1, 2, 0).reshape(2 * local, model), cross_out, ffn_in, ffn_out,
        ],
    ))
    out = run_finish(dict(
        configs=configs, small=done.small_out, layer_in=done.layer_out, grad_in=done.input_grad,
        source_in=done.memory_out, blocks=done.blocks,
    ), layers)
    grads = out.grads
    return (
        out.layer_out,
        out.input_grad,
        out.memory_grad,
        out.gain_grad,
        out.shift_grad,
        grads[0].reshape(3, local, model).transpose(2, 0, 1),
        grads[1],
        grads[2].T,
        grads[3].reshape(2, local, model).transpose(2, 0, 1),
        grads[4],
        grads[5],
        out.bias_in_grad,
        grads[6],
        out.bias_out_grad,
    )


def solution(mesh):
    rows = P(("grp", "dp", "tp"), None)
    stack = P(None, ("grp", "dp", "tp"), None)
    weights = (
        P(None, None, "tp"), P("tp", None), P(None, "tp"), P(None, None, "tp"), P("tp", None),
        P(None, "tp"), P("tp"), P("tp", None), P(),
    )
    return jax.shard_map(
        per_device,
        mesh=mesh,
        in_specs=(rows, stack, rows, P(("grp", "dp")), P(("grp", "dp")), P("grp", None), P(), P()) + weights,
        out_specs=(rows, rows, stack, P(), P()) + weights,
        check_vma=False,
    )
```

```python
import functools
import types

import jax
import jax.numpy as jnp
from jax import lax
from jax.experimental import pallas as pl
from jax.experimental.pallas import tpu as pltpu
from jax.sharding import PartitionSpec as P

HD = 80
LEN = 256
EPSILON = 1e-05
NEGATIVE = -1e30
SCALE = HD ** (-0.5)
LOG2E = 1.4426950408889634
F32 = jnp.float32
BF16 = jnp.bfloat16


MESH = pl.DeviceIdType.MESH


class Place:
    def __init__(self):
        self.tps = lax.axis_size("tp")
        self.extra = lax.axis_size("dp") // 2
        assert lax.axis_size("grp") == 4 and lax.axis_size("dp") % 2 == 0
        grp, dp, tp = (lax.axis_index(name) for name in ("grp", "dp", "tp"))
        core, low, high = dp % 2, grp % 2, grp // 2
        flip_low, flip_high = grp + 1 - 2 * low, grp + 2 - 4 * high
        self.grp, self.dp, self.tp, self.core = grp, dp, tp, core
        self.first_bit = (1 - core) * low + core * high
        self.second_bit = (1 - core) * high + core * low
        self.first = ((1 - core) * flip_low + core * flip_high, dp, tp)
        self.second = ((1 - core) * flip_high + core * flip_low, dp, tp)
        self.across = (3 - grp, dp, tp)
        self.sibling = (grp, dp + 1 - 2 * core, tp)
        self.above = (grp, dp, tp + 1)
        self.below = (grp, dp, tp - 1)
        self.has_above = tp < self.tps - 1
        self.has_below = tp > 0

    def copy_of(self, step):
        return (self.grp, ((self.dp // 2 + step) % self.extra) * 2 + self.core, self.tp)

    def nth_block(self, k):
        size = self.tps
        upper = (2 * self.tp) // size
        lead = (1 - upper) * self.tp + upper * (size - 1 - self.tp)
        spot = k + (k + size - lead) // size
        return (1 - upper) * spot + upper * (size - 1 - spot)

    def along(self, tp):
        return (self.grp, self.dp, tp)

    def barrier(self):
        sem = pltpu.get_barrier_semaphore()
        partners = [self.first, self.second, self.across, self.sibling]
        partners += [self.along((self.tp + step) % self.tps) for step in range(1, self.tps)]
        partners += [self.copy_of(step) for step in range(1, self.extra)]
        for device in partners:
            pl.semaphore_signal(sem, inc=1, device_id=device, device_id_type=MESH)
        pl.semaphore_wait(sem, len(partners))


def push(src, dst, send_sem, recv_sem, device):
    return pltpu.make_async_remote_copy(
        src_ref=src, dst_ref=dst, send_sem=send_sem, recv_sem=recv_sem, device_id=device, device_id_type=MESH
    )


def rows_of(ref, lead, start, count):
    return ref.at[lead, pl.ds(pl.multiple_of(start, 16), count)]


def add_units(total, term, unit):
    def step(i, carry):
        rows = pl.ds(pl.multiple_of(i * unit, 16), unit)
        total[rows] = total[rows] + term[rows]
        return carry

    lax.fori_loop(0, total.shape[0] // unit, step, 0)


class Spread:
    KINDS = 14

    def __init__(self, place, view, unit, sems, direct=False):
        self.place, self.view, self.unit, self.sems = place, view, unit, sems
        f, s, c = place.first_bit, place.second_bit, place.core
        self.units = (f * 2 + s, f * 2 + 1 - s, (1 - f) * 2 + s, (1 - f) * 2 + 1 - s)
        self.theirs = (s * 2 + f, s * 2 + 1 - f, (1 - s) * 2 + f, (1 - s) * 2 + 1 - f)
        self.table = [
            (place.second, (c, self.units[0]), (c, self.units[1])),
            (place.first, (c, self.units[0]), (c, self.units[2])),
            (place.across if direct else place.first, (c, self.units[0 if direct else 1]), (c, self.units[3])),
        ] + [(place.sibling, (c, u), (1 - c, t)) for u, t in zip(self.units, self.theirs)]
        if direct:
            self.waits = ((), (0, 1, 2), (3, 4, 5, 6))
            self.sends = ((0, 1, 2, 3), (4, 5, 6), ())
        else:
            self.waits = ((), (0,), (1, 2), (3, 4, 5, 6))
            self.sends = ((0, 1, 3), (2, 4), (5, 6), ())

    def region(self, spot):
        half, unit = spot
        return self.view((half * 4 + unit) * self.unit, self.unit)

    def own(self):
        return self.region((self.place.core, self.units[0]))

    def copy(self, n, lands=False):
        device, leaves, landing = self.table[n]
        part = self.region(landing if lands else leaves)
        return push(part, part, self.sems(2 * n), self.sems(2 * n + 1), device)

    def step(self, stage):
        for n in self.waits[stage]:
            self.copy(n, lands=True).wait_recv()
        for n in self.sends[stage]:
            self.copy(n).start()

    def finish(self):
        for n in range(7):
            self.copy(n).wait_send()


class Gather:
    KINDS = Spread.KINDS + 3

    def __init__(self, place, buffers, sems):
        self.place, self.buffers, self.sems = place, buffers, sems
        self.unit = [ref.shape[1] // 8 for ref in buffers]
        self.others = place.tps - 1

    def spread(self, g, j):
        return Spread(
            self.place,
            lambda start, count: rows_of(self.buffers[g], j, start, count),
            self.unit[g],
            lambda kind: self.sems.at[kind, g, j],
        )

    def relays(self, g, j):
        p = self.place
        part = self.spread(g, j).own()
        sem = lambda n: self.sems.at[Spread.KINDS + n, g, j]
        return (
            (jnp.logical_and(j <= p.tp, p.has_above), push(part, part, sem(0), sem(2), p.above)),
            (jnp.logical_and(j >= p.tp, p.has_below), push(part, part, sem(1), sem(2), p.below)),
        )

    def start(self, g):
        for needed, copy in self.relays(g, self.place.tp):
            pl.when(needed)(copy.start)

    def step(self, g, k, stage):
        j = self.place.nth_block(k)
        if stage == 0:
            relays = self.relays(g, j)
            relays[0][1].wait_recv()
            for needed, copy in relays:
                pl.when(needed)(copy.start)
        self.spread(g, j).step(stage)

    def drain(self, g, j):
        for needed, copy in self.relays(g, j):
            pl.when(needed)(copy.wait_send)

        @pl.when(j != self.place.tp)
        def _():
            self.spread(g, j).finish()


class Line:
    def __init__(self, place, buffer, sems):
        self.place, self.buffer, self.sems = place, buffer, sems

    def relays(self, j):
        p = self.place
        part = self.buffer.at[j]
        return (
            (jnp.logical_and(j <= p.tp, p.has_above), push(part, part, self.sems.at[0, j], self.sems.at[2, j], p.above)),
            (jnp.logical_and(j >= p.tp, p.has_below), push(part, part, self.sems.at[1, j], self.sems.at[2, j], p.below)),
        )

    def start(self):
        for needed, copy in self.relays(self.place.tp):
            pl.when(needed)(copy.start)

    def step(self, k):
        j = self.place.nth_block(k)
        relays = self.relays(j)
        relays[0][1].wait_recv()
        for needed, copy in relays:
            pl.when(needed)(copy.start)

    def finish(self):
        for j in range(self.place.tps):
            for needed, copy in self.relays(j):
                pl.when(needed)(copy.wait_send)


class Reduce:
    KINDS = 8 + 6 + 2 + Spread.KINDS + 2

    def __init__(self, place, grads, halves, planes, lines, extras, totals, sems, halving):
        self.place, self.grads, self.totals, self.sems, self.halving = place, grads, totals, sems, halving
        self.halves, self.planes, self.lines, self.extras = halves, planes, lines, extras
        self.unit = [ref.shape[1] // 8 for ref in grads]

    def sem(self, kind, g, j):
        return self.sems.at[kind, g, j]

    def rows(self, g, j, half, unit, count=1):
        size = self.unit[g]
        return rows_of(self.grads[g], j, (half * 4 + unit) * size, count * size)

    def to_sibling(self, g, j):
        p = self.place
        return [push(self.rows(g, j, 1 - p.core, 0, 4), self.halves[g].at[j], self.sem(0, g, j), self.sem(1, g, j), p.sibling)]

    def in_plane(self, g, j):
        p = self.place
        f, s = p.first_bit, p.second_bit
        goals = ((p.second, f * 2 + 1 - s), (p.first, (1 - f) * 2 + s), (p.across, (1 - f) * 2 + 1 - s))
        return [self.plane_copy(g, j, i, device, u) for i, (device, u) in enumerate(goals)]

    def by_halves(self, g, j):
        p = self.place
        f, s = p.first_bit, p.second_bit
        goals = ((p.first, (1 - f) * 2), (p.first, (1 - f) * 2 + 1), (p.second, f * 2 + 1 - s))
        return [self.plane_copy(g, j, i, device, u) for i, (device, u) in enumerate(goals)]

    def plane_copy(self, g, j, i, device, unit):
        return push(
            self.rows(g, j, self.place.core, unit), self.planes[g].at[j, i],
            self.sem(8 + 2 * i, g, j), self.sem(9 + 2 * i, g, j), device,
        )

    def piece(self, g, j):
        p = self.place
        return self.rows(g, j, p.core, p.first_bit * 2 + p.second_bit)

    def along(self, g, j):
        p = self.place
        return push(self.piece(g, j), self.lines[g].at[p.tp], self.sem(14, g, j), self.sem(15, g, p.tp), p.along(j))

    def from_place(self, g, j):
        p = self.place
        return push(self.piece(g, j), self.lines[g].at[j], self.sem(14, g, j), self.sem(15, g, j), p.along(j))

    def step(self, g, j, stage):
        p = self.place
        if stage == 0:
            for copy in self.to_sibling(g, j):
                copy.start()
        if stage == 1:
            for copy in self.to_sibling(g, j):
                copy.wait_recv()
            add_units(self.rows(g, j, p.core, 0, 4), self.halves[g].at[j], self.unit[g])
            for copy in self.by_halves(g, j)[:2] if self.halving[g] else self.in_plane(g, j):
                copy.start()
        if stage == 2 and self.halving[g]:
            copies = self.by_halves(g, j)
            for i in range(2):
                copies[i].wait_recv()
                add_units(self.rows(g, j, p.core, p.first_bit * 2 + i), self.planes[g].at[j, i], self.unit[g])
            copies[2].start()
        elif stage == 2:
            for copy in self.in_plane(g, j):
                copy.wait_recv()
            a, b, c = (self.planes[g][j, i].astype(F32) for i in range(3))
            piece = self.piece(g, j)
            piece[...] = ((piece[...].astype(F32) + a) + (b + c)).astype(BF16)
            pl.when(j != p.tp)(self.along(g, j).start)
        if stage == 3:
            self.by_halves(g, j)[2].wait_recv()
            add_units(self.piece(g, j), self.planes[g].at[j, 2], self.unit[g])
            pl.when(j != p.tp)(self.along(g, j).start)

    def spread(self, g):
        return Spread(
            self.place,
            lambda start, count: self.totals[g].at[pl.ds(pl.multiple_of(start, 16), count)],
            self.unit[g],
            lambda kind: self.sems.at[16 + kind, g, 0],
            direct=not self.halving[g],
        )

    def copies(self, g, step):
        p = self.place
        base = self.KINDS - 2
        return push(
            self.piece(g, p.tp), self.extras[g].at[step], self.sem(base, g, step), self.sem(base + 1, g, step), p.copy_of(step)
        )

    def settle(self, g):
        p = self.place
        piece = self.piece(g, p.tp)
        total = piece[...].astype(F32)
        for k in range(p.tps - 1):
            j = p.nth_block(k)
            self.from_place(g, j).wait_recv()
            total = total + self.lines[g][j].astype(F32)
        if p.extra > 1:
            piece[...] = total.astype(BF16)
            for step in range(1, p.extra):
                self.copies(g, step).start()
            for step in range(1, p.extra):
                self.copies(g, step).wait()
                total = total + self.extras[g][step].astype(F32)
        own = self.spread(g).own()
        own[...] = total.astype(BF16)
        self.spread(g).step(0)

    def share(self, g, stage):
        self.spread(g).step(stage)

    def finish(self, g):
        p = self.place
        for j in range(p.tps):
            for copy in self.to_sibling(g, j) + (self.by_halves(g, j) if self.halving[g] else self.in_plane(g, j)):
                copy.wait_send()
            pl.when(j != p.tp)(self.along(g, j).wait_send)
        self.spread(g).finish()


class SumSmall:
    @staticmethod
    def slots(tps, extra):
        return 8 + tps + extra

    def __init__(self, place, slots, sems):
        self.place, self.slots_ref, self.sems = place, slots, sems

    def move(self, source, target, device, kind):
        slots = self.slots_ref
        return push(slots.at[source], slots.at[target], self.sems.at[0, kind], self.sems.at[1, target], device)

    def in_plane(self):
        p = self.place
        return [self.move(2, 3 + i, device, 3 + i) for i, device in enumerate((p.second, p.first, p.across))]

    def copies(self):
        p = self.place
        return [self.move(6, 8 + p.tps + s, p.copy_of(s), 8 + p.tps + s) for s in range(1, p.extra)]

    def along(self, k, lands=False):
        p = self.place
        j = p.nth_block(k)
        return self.move(7, 8 + (j if lands else p.tp), p.along(j), 8 + j)

    def start(self):
        self.move(0, 1, self.place.sibling, 1).start()

    def exchange(self, stage):
        p, slots = self.place, self.slots_ref
        if stage == 0:
            self.move(0, 1, p.sibling, 1).wait_recv()
            slots[2] = slots[0] + slots[1]
            for copy in self.in_plane():
                copy.start()
        else:
            for copy in self.in_plane():
                copy.wait_recv()
            slots[6] = (slots[2] + slots[3]) + (slots[4] + slots[5])
            for copy in self.copies():
                copy.start()
            total = slots[6]
            for s, copy in enumerate(self.copies()):
                copy.wait_recv()
                total = total + slots[9 + p.tps + s]
            slots[7] = total
            for k in range(p.tps - 1):
                self.along(k).start()

    def total(self):
        p, slots = self.place, self.slots_ref
        value = slots[7]
        for k in range(p.tps - 1):
            self.along(k, lands=True).wait_recv()
            value = value + slots[8 + p.nth_block(k)]
        return value

    def finish(self):
        p = self.place
        self.move(0, 1, p.sibling, 1).wait_send()
        for copy in self.in_plane() + self.copies():
            copy.wait_send()
        for k in range(p.tps - 1):
            self.along(k).wait_send()


def dot_nn(left, right):
    return lax.dot_general(left, right, (((1,), (0,)), ((), ())), preferred_element_type=F32)


def dot_nt(left, right):
    return lax.dot_general(left, right, (((1,), (1,)), ((), ())), preferred_element_type=F32)


def dot_tn(left, right):
    return lax.dot_general(left, right, (((0,), (0,)), ((), ())), preferred_element_type=F32)


def column(axis, shape):
    return lax.broadcasted_iota(jnp.int32, shape, axis)


def each(count, step):

    def run(i, carry):
        step(i)
        return carry

    lax.fori_loop(0, count, run, 0)


CHUNK = 32
CUBE = 0.044715
ROOT = 0.7978845608028654


def layer_kernel(r):
    r.a2, r.a3, r.e = (r.memory.at[i] for i in range(3))
    columns = pl.ds(0, r.x.shape[1])
    r.dh, r.dm = r.before.at[:, columns], r.down.at[:, columns]
    place = Place()
    n = place.tps
    x, model = r.x, r.x.shape[1]
    owned = x.shape[0]
    sentences = owned // LEN
    local = r.c[0].shape[1]
    heads_here = local // HD
    units = r.hidden.shape[1]
    layers = r.memory.shape[0]
    weights = r.w
    lengths, sources, configs = r.lengths, r.src_lengths, r.configs
    width, heads, hidden_units, depth = (configs[0, i] for i in range(4))
    inv_width = 1.0 / jnp.full((1, 1), width.astype(F32))
    inv_depth = 1.0 / jnp.full((1, 1), depth.astype(F32))
    width_mask = (column(1, (1, model)) < width).astype(F32)

    local_sem = r.local_sems
    spots = (
        (0, 0, 3 * local), (0, 3 * local, local),
        (1, 0, local), (1, local, 2 * local), (1, 3 * local, local),
        (2, 0, weights[2].shape[1]), (3, 0, weights[3].shape[1]),
    )
    fills = [
        (g, pltpu.make_async_copy(r.shards[i], weights[g].at[place.tp, pl.ds(start, size)], local_sem.at[i]))
        for i, (g, start, size) in enumerate(spots)
    ]
    loads = [
        pltpu.make_async_copy(source, target, local_sem.at[7 + i])
        for i, (source, target) in enumerate(((r.x_in, r.x), (r.memory_in, r.memory), (r.upstream_in, r.upstream)))
    ]
    for _, copy in fills[:2]:
        copy.start()
    loads[0].start()
    for _, copy in fills[2:]:
        copy.start()
    loads[1].start()
    loads[2].start()
    r.bias[place.tp] = jnp.broadcast_to(r.bias_in[...].reshape(1, units), r.bias.shape[1:])
    place.barrier()

    gather = Gather(place, weights, r.gather_sems)
    bias = Line(place, r.bias, r.bias_sems)
    for g in range(4):
        for group, copy in fills:
            if group == g:
                copy.wait()
        gather.start(g)
        if g == 0:
            bias.start()
    order = [(g, k) for g in (0, 1) for k in range(n - 1)] + [(g, k) for k in range(n - 1) for g in (2, 3)]

    def g_tick(tick):
        for stage in range(4):
            if 0 <= tick - stage < len(order):
                gather.step(*order[tick - stage], stage)

    def block(k):
        later = (k + n - 1) // n
        return (1 - later) * place.tp + later * place.nth_block(k - 1)

    def block_last(k):
        own = k // (n - 1)
        return own * place.tp + (1 - own) * place.nth_block(k)

    def hooks(table, k, b):
        for (kk, bb), steps in table.items():

            @pl.when(jnp.logical_and(k == kk, b == bb))
            def _():
                for step in steps:
                    step()

    def chunk(i):
        return pl.ds(pl.multiple_of(i * CHUNK, CHUNK), CHUNK)

    def keep_of(i):
        per = LEN // CHUNK
        spot = column(0, (CHUNK, 1)) + (i % per) * CHUNK
        return (spot < lengths[place.tp * sentences + i // per]).astype(F32) * width_mask

    def norm_parts(rows):
        mean = jnp.sum(rows * width_mask, axis=-1, keepdims=True) * inv_width
        centred = (rows - mean) * width_mask
        spread = jnp.sum(centred * centred, axis=-1, keepdims=True) * inv_width
        rstd = lax.rsqrt(spread + EPSILON)
        return centred * rstd, rstd

    def norm(rows, which):
        hat, _ = norm_parts(rows)
        return ((hat * r.gains[which:which + 1] + r.shifts[which:which + 1]) * width_mask).astype(BF16)

    def fold(values):
        return jnp.sum(values.reshape(values.shape[0] // 8, 8, values.shape[1]), axis=0)

    def norm_backward(rows, which, upstream):
        hat, rstd = norm_parts(rows)
        upstream = upstream * width_mask
        sums = r.norm_sums
        sums[which] = sums[which] + fold(upstream * hat)
        sums[3 + which] = sums[3 + which] + fold(upstream)
        scaled = upstream * r.gains[which:which + 1]
        first = jnp.sum(scaled, axis=-1, keepdims=True) * inv_width
        second = jnp.sum(scaled * hat, axis=-1, keepdims=True) * inv_width
        return (rstd * (scaled - first - hat * second)) * width_mask

    chunks = owned // CHUNK

    def each_chunk(step):

        def two(i):
            step(2 * i)
            step(2 * i + 1)

        each(chunks // 2, two)

    acc, da, dh = r.acc, r.da, r.dh
    zeros = jnp.zeros((CHUNK, model), F32)
    r.norm_sums[...] = jnp.zeros(r.norm_sums.shape, F32)
    r.bias_sums[...] = jnp.zeros(r.bias_sums.shape, F32)

    def sentence(b):
        return pl.ds(pl.multiple_of(b * LEN, LEN), LEN)

    def head_keep(j, h):
        return jnp.where(j * heads_here + h < heads, 1.0, 0.0).astype(F32)

    def causal(b, start):
        return column(0, (LEN, 128)) <= column(1, (LEN, 128)) + start

    def crossing(b, start):
        return column(0, (LEN, 1)) < sources[place.tp * sentences + b]

    def bands(h):
        return [pl.ds(i * local + h * HD, HD) for i in range(3)]

    def lanes(b):
        return pl.ds(b * LEN, LEN)

    pairs = [(b, h) for b in range(sentences) for h in range(heads_here)]

    quarters = [(i, b, h, start) for i, (b, h) in enumerate(pairs) for start in range(0, LEN, 128)]

    def attend(k, table, g, allowed):
        w, t, c, p = weights[g], r.t[g], r.c[g], r.p[g]
        j = block(k)
        hooks(table, k, 0)
        if g == 0:
            t[j] = dot_nn(w[j, :3 * local], r.flip[0][...]).astype(BF16)
        else:
            t[j, :local] = dot_nn(w[j, :local], r.flip[0][...]).astype(BF16)
            t[j, local:] = dot_nn(w[j, local:3 * local], r.flip[1][...]).astype(BF16)
        heads_of = [[t[j, band, lanes(b)] for band in bands(h)] for b, h in pairs]
        for i, (query, keys, _) in enumerate(heads_of):
            r.scores[i] = dot_tn(keys, query)
        for i, b, h, start in quarters:
            part = pl.ds(start, 128)
            score = jnp.where(allowed(b, start), r.scores[i, :, part], NEGATIVE)
            raised = jnp.exp2((score - jnp.max(score, axis=0, keepdims=True)) * (SCALE * LOG2E))
            p[j, i, :, part] = (raised * (1.0 / jnp.sum(raised, axis=0, keepdims=True))).astype(BF16)
        for i, (b, h) in enumerate(pairs):
            c[j, pl.ds(h * HD, HD), lanes(b)] = (dot_nn(heads_of[i][2], p[j, i]) * head_keep(j, h)).astype(BF16)
        hooks(table, k, 1)
        acc[...] = acc[...] + dot_tn(c[j], w[j, 3 * local:])

    def attend_backward(k, table, g, query_rows, key_rows):
        w, t, c, p = weights[g], r.t[g], r.c[g], r.p[g]
        j = block_last(k)
        e, dt, dc = r.e, r.dt, r.dc
        dc_all = dot_nn(w[j, 3 * local:], r.flip[0][...])
        for h in range(heads_here):
            dc[h * HD:(h + 1) * HD] = (dc_all[h * HD:(h + 1) * HD] * head_keep(j, h)).astype(BF16)
        heads_of = [[t[j, band, lanes(b)] for band in bands(h)] for b, h in pairs]
        dc_of = [dc[h * HD:(h + 1) * HD, lanes(b)] for b, h in pairs]
        for i, (_, _, values) in enumerate(heads_of):
            r.scores[i] = dot_tn(values, dc_of[i])
        for i, b, h, start in quarters:
            part = pl.ds(start, 128)
            dp, wide = r.scores[i, :, part], p[j, i, :, part].astype(F32)
            r.ds[i, :, part] = (wide * (dp - jnp.sum(dp * wide, axis=0, keepdims=True))).astype(BF16)
        for i, (b, h) in enumerate(pairs):
            (query, keys, _), (dq, dk, dv) = heads_of[i], bands(h)
            dt[dv, lanes(b)] = dot_nt(dc_of[i], p[j, i]).astype(BF16)
            dt[dq, lanes(b)] = (dot_nn(keys, r.ds[i]) * SCALE).astype(BF16)
            dt[dk, lanes(b)] = (dot_nt(query, r.ds[i]) * SCALE).astype(BF16)
        hooks(table, k, 1)
        gather.drain(g, j)
        if g == 0:
            da[...] = da[...] + dot_tn(dt[...], w[j, :3 * local])
            w[j, :3 * local] = dot_nn(dt[...], query_rows[...]).astype(BF16)
        else:
            da[...] = da[...] + dot_tn(dt[:local], w[j, :local])
            r.dm[...] = r.dm[...] + dot_tn(dt[local:], w[j, local:3 * local])
            w[j, :local] = dot_nn(dt[:local], query_rows[...]).astype(BF16)
            w[j, local:3 * local] = dot_nn(dt[local:], key_rows[...]).astype(BF16)
        w[j, 3 * local:] = dot_nn(c[j], e[...]).astype(BF16)

    def feed(k, table):
        j = block(k)
        w_up, w_down = weights[2], weights[3]
        hooks(table, k, 0)
        r.before[...] = dot_nn(r.a3[...], w_up[j]) + r.bias[j, 0:1]
        r.down[...] = dot_nt(r.e[...], w_down[j])
        step_lanes = units // 2

        def bend(i):
            rows = pl.ds(pl.multiple_of(i * 16, 16), 16)
            for start in range(0, units, step_lanes):
                part = pl.ds(start, step_lanes)
                unit = column(1, (1, step_lanes)) + (j * units + start)
                kept = jnp.where(unit < hidden_units, 0.5, 0.0)
                before = r.before[rows, part]
                square = before * before
                bent = jnp.tanh(before * (ROOT + ROOT * CUBE * square))
                half = kept + kept * bent
                through = before * half
                r.hidden[rows, part] = through.astype(BF16)
                slope = half + (through - through * bent) * (ROOT + 3.0 * CUBE * ROOT * square)
                du = (r.down[rows, part] * slope).astype(BF16)
                r.dhidden[rows, part] = du
                r.bias_sums[j, :, part] = r.bias_sums[j, :, part] + fold(du.astype(F32))

        each(owned // 16, bend)
        hooks(table, k, 1)
        acc[...] = acc[...] + dot_nn(r.hidden[...], w_down[j])
        da[...] = da[...] + dot_nt(r.dhidden[...], w_up[j])
        gather.drain(2, j)
        gather.drain(3, j)
        w_down[j] = dot_tn(r.hidden[...], r.e[...]).astype(BF16)
        w_up[j] = dot_nn(r.flip[0][...], r.dhidden[...]).astype(BF16)

    loads[0].wait()

    def begin(i):
        rows = chunk(i)
        r.a1[rows] = norm(x[rows].astype(F32), 0)
        acc[rows] = zeros
        da[rows] = zeros

    each_chunk(begin)
    r.flip[0][...] = r.a1[...].T
    g_tick(0)
    loads[1].wait()

    def mix(i):
        rows = chunk(i)
        total = jnp.zeros((CHUNK, model), F32)
        for level in range(layers):
            chosen = (jnp.full((1, 1), depth) >= layers - level).astype(F32)
            total = total + chosen * r.memory[level, rows].astype(F32)
        r.m[rows] = (total * inv_depth * width_mask).astype(BF16)

    each_chunk(mix)
    r.flip[1][...] = r.m[...].T
    loads[2].wait()
    r.out_sums[...] = jnp.zeros(r.out_sums.shape, F32)

    def grad_in(i):
        rows = chunk(i)
        masked = r.upstream[rows].astype(F32) * keep_of(i)
        r.out_sums[...] = r.out_sums[...] + fold(masked)
        r.e[rows] = masked.astype(BF16)

    each_chunk(grad_in)

    def ticks(*numbers):
        return [functools.partial(g_tick, i) for i in numbers]

    others = n - 1
    assert n == 4
    table = {
        (0, 1): ticks(1),
        (1, 0): ticks(2, 3) + [functools.partial(bias.step, 0)],
        (2, 0): ticks(4) + [functools.partial(bias.step, 1)],
        (3, 0): ticks(5) + [functools.partial(bias.step, 2)],
    }
    each(n, lambda k: attend(k, table, 0, causal))

    def after_self(i):
        rows = chunk(i)
        h = x[rows].astype(F32) + acc[rows] * keep_of(i)
        r.h1[rows] = h
        r.a2[rows] = norm(h, 1)
        acc[rows] = zeros

    each_chunk(after_self)
    r.flip[0][...] = r.a2[...].T
    table2 = {(k, 0): ticks(6 + k) for k in range(n)}
    each(n, lambda k: attend(k, table2, 1, crossing))

    def after_cross(i):
        rows = chunk(i)
        h = r.h1[rows] + acc[rows] * keep_of(i)
        r.h2[rows] = h
        r.a3[rows] = norm(h, 2)
        acc[rows] = zeros

    each_chunk(after_cross)
    r.flip[0][...] = r.a3[...].T

    reduce = Reduce(
        place, weights, r.half, r.plane, r.line, r.extra, r.total, r.reduce_sems, (False, False, True, True)
    )
    plan = {}

    def add(tick, order, step, *args):
        plan.setdefault(tick, []).append((order, len(plan.get(tick, ())), functools.partial(step, *args)))

    def r_tick(tick):
        for _, _, step in sorted(plan.get(tick, ()), key=lambda entry: entry[:2]):
            step()

    def store(g):
        return pltpu.make_async_copy(r.total[g], r.blocks[g], local_sem.at[10 + g])

    feed_times = [(1, 2, 5, 9), (3, 4, 7, 11), (5, 6, 9, 13), (7, 8, 11, 15)]
    times = {
        3: (feed_times, (16, 17, 18, 19)),
        2: (feed_times, (17, 18, 19, 20)),
        1: ([(10, 11, 14), (12, 13, 16), (14, 15, 18), (16, 17, 20)], (20, 21, 22)),
        0: ([(19, 20, 22), (21, 22, 24), (23, 24, 25), (25, 26, 27)], (27, 28, 29)),
    }
    for late, g in enumerate((3, 2, 1, 0)):
        for k, stages in enumerate(times[g][0]):
            j = block(k) if g > 1 else block_last(k)
            for stage, tick in enumerate(stages):
                add(tick, stage, reduce.step, g, j, stage)
        for stage, tick in enumerate(times[g][1]):
            if stage == 0:
                add(tick, 20 - late, reduce.settle, g)
            else:
                add(tick, 30 + stage - late, reduce.share, g, stage)
        add(times[g][1][-1], 50, lambda g=g: store(g).start())

    def reduce_ticks(*numbers):
        return [functools.partial(r_tick, i) for i in numbers]

    def at_end(k, numbers):
        for kk, number in enumerate(numbers):

            @pl.when(k == kk)
            def _():
                r_tick(number)

    table3 = {(0, 0): ticks(10), (0, 1): ticks(11), (1, 1): ticks(12) + reduce_ticks(2),
              (2, 1): ticks(13) + reduce_ticks(4), (3, 0): ticks(14), (3, 1): reduce_ticks(6)}

    def feed_step(k):
        feed(k, table3)
        at_end(k, [2 * i + 1 for i in range(n)])

    each(n, feed_step)
    r_tick(8)
    out_copy = pltpu.make_async_copy(acc, r.layer_out, local_sem.at[14])

    def after_feed(i):
        rows = chunk(i)
        keep = keep_of(i)
        acc[rows] = r.h2[rows] + (acc[rows] + r.bias_out[...].reshape(1, model)) * keep
        down = r.upstream[rows].astype(F32) + norm_backward(r.h2[rows], 2, da[rows])
        dh[rows] = down
        r.e[rows] = (down * keep).astype(BF16)
        da[rows] = zeros
        r.dm[rows] = zeros

    each_chunk(after_feed)
    r.flip[0][...] = r.e[...].T
    out_copy.start()
    table4 = {(k, 1): reduce_ticks(9 + 2 * k) for k in range(n)}

    def cross_step(k):
        attend_backward(k, table4, 1, r.a2, r.m)
        at_end(k, [10 + 2 * i for i in range(n)])

    each(n, cross_step)
    memory_copy = pltpu.make_async_copy(r.dm, r.memory_out, local_sem.at[15])
    memory_copy.start()

    def before_cross(i):
        rows = chunk(i)
        down = dh[rows] + norm_backward(r.h1[rows], 1, da[rows])
        dh[rows] = down
        r.e[rows] = (down * keep_of(i)).astype(BF16)
        da[rows] = zeros

    each_chunk(before_cross)
    r.flip[0][...] = r.e[...].T
    r_tick(17)
    table5 = {(k, 1): reduce_ticks(18 + 2 * k) for k in range(n)}

    def self_step(k):
        attend_backward(k, table5, 0, r.a1, r.a1)
        at_end(k, [19 + 2 * i for i in range(n)])

    each(n, self_step)

    def before_self(i):
        rows = chunk(i)
        dh[rows] = dh[rows] + norm_backward(x[rows].astype(F32), 0, da[rows])

    each_chunk(before_self)
    grad_copy = pltpu.make_async_copy(dh, r.input_grad, local_sem.at[16])
    grad_copy.start()

    small = SumSmall(place, r.slots, r.small_sems)

    def small_start():
        own = r.slots.at[0]
        own[...] = jnp.zeros(own.shape, F32)
        for i in range(6):
            own[i:i + 1, :model] = jnp.sum(r.norm_sums[i], axis=0, keepdims=True)
        own[6:7, :model] = jnp.sum(r.out_sums[...], axis=0, keepdims=True)
        tokens = lengths[place.tp * sentences]
        for b in range(1, sentences):
            tokens = tokens + lengths[place.tp * sentences + b]
        own[7:8] = jnp.full((1, own.shape[1]), tokens.astype(F32))
        for i in range(n):
            own[8 + i:9 + i] = jnp.sum(r.bias_sums[i], axis=0, keepdims=True)
        small.start()

    add(26, 5, small_start)
    for stage in range(2):
        add(27 + stage, 5, small.exchange, stage)
    final = max(plan)
    for tick in range(26, final + 1):
        r_tick(tick)
    r.small_out[...] = small.total()
    bias.finish()
    for copy in (out_copy, memory_copy, grad_copy):
        copy.wait()
    for g in range(4):
        reduce.finish(g)
        store(g).wait()
    small.finish()


def call(kernel, name, ins, outs, scratch, spaces, **options):
    trees = (ins, outs, scratch)
    structure = jax.tree_util.tree_structure(trees)

    def body(*refs):
        groups = jax.tree_util.tree_unflatten(structure, refs)
        kernel(types.SimpleNamespace(**groups[0], **groups[1], **groups[2]))

    def specs(group):
        return [
            pl.BlockSpec(memory_space=spaces.get(key, pltpu.VMEM))
            for key in sorted(group) for _ in jax.tree_util.tree_leaves(group[key])
        ]

    leaves = jax.tree_util.tree_leaves
    values = pl.pallas_call(
        body,
        out_shape=leaves(outs),
        in_specs=specs(ins),
        out_specs=specs(outs),
        scratch_shapes=leaves(scratch),
        compiler_params=pltpu.CompilerParams(**options),
        name=name,
    )(*leaves(ins))
    return types.SimpleNamespace(**jax.tree_util.tree_unflatten(jax.tree_util.tree_structure(outs), values))


def run_layer(ins):
    n, extra = lax.axis_size("tp"), lax.axis_size("dp") // 2
    owned, model = ins["x_in"].shape
    memory, shards = ins["memory_in"], ins["shards"]
    local, units = shards[1].shape[0], ins["bias_in"].shape[0]
    small = (16, units)
    assert n <= 8 and units >= model and memory.shape[0] >= 3
    shapes = [(n, 4 * local, model)] * 2 + [(n,) + shards[5].shape, (n,) + shards[6].shape]
    small_slots = SumSmall.slots(n, extra)

    def vmem(*shape):
        return pltpu.VMEM(shape, BF16)

    def wide(*shape):
        return pltpu.VMEM(shape, F32)

    def eighths(*lead, parts=1):
        return [vmem(*lead, rows * parts // 8, columns) for _, rows, columns in shapes]

    dma = pltpu.SemaphoreType.DMA
    scratch = dict(
        w=[vmem(*shape) for shape in shapes],
        bias=wide(n, 8, units),
        x=vmem(owned, model),
        memory=vmem(*memory.shape),
        upstream=vmem(owned, model),
        a1=vmem(owned, model),
        m=vmem(owned, model),
        h1=wide(owned, model),
        h2=wide(owned, model),
        acc=wide(owned, model),
        da=wide(owned, model),
        t=[vmem(n, 3 * local, owned)] * 2,
        c=[vmem(n, local, owned)] * 2,
        p=[vmem(n, owned // LEN * (local // HD), LEN, LEN)] * 2,
        dt=vmem(3 * local, owned),
        dc=vmem(local, owned),
        flip=[vmem(model, owned)] * 2,
        scores=wide(owned // LEN * (local // HD), LEN, LEN),
        ds=vmem(owned // LEN * (local // HD), LEN, LEN),
        before=wide(owned, units),
        down=wide(owned, units),
        hidden=vmem(owned, units),
        dhidden=vmem(owned, units),
        bias_sums=wide(n, 8, units),
        norm_sums=wide(6, 8, model),
        out_sums=wide(8, model),
        half=eighths(n, parts=4),
        plane=eighths(n, 3),
        line=eighths(n),
        extra=eighths(extra),
        total=eighths(parts=8),
        slots=wide(small_slots, *small),
        gather_sems=dma((Gather.KINDS, 4, n)),
        bias_sems=dma((3, n)),
        reduce_sems=dma((Reduce.KINDS, 4, max(n, extra))),
        small_sems=dma((2, small_slots)),
        local_sems=dma((17,)),
    )
    rows = jax.ShapeDtypeStruct((owned, model), F32)
    outs = dict(
        layer_out=rows, input_grad=rows, memory_out=rows, small_out=jax.ShapeDtypeStruct(small, F32),
        blocks=[jax.ShapeDtypeStruct(shape[1:], BF16) for shape in shapes],
    )
    smem, hbm = pltpu.SMEM, pl.ANY
    spaces = dict(
        lengths=smem, src_lengths=smem, configs=smem, x_in=hbm, memory_in=hbm, upstream_in=hbm, shards=hbm,
        layer_out=hbm, input_grad=hbm, memory_out=hbm, blocks=hbm,
    )
    return call(
        layer_kernel, "layer", ins, outs, scratch, spaces,
        collective_id=1, has_side_effects=True, vmem_limit_bytes=64 * 2**20,
    )


def finish_kernel(r):
    small, configs, sems = r.small, r.configs, r.sems
    model = r.gain_grad.shape[1]
    layers = r.memory_grad.shape[0]
    place = lax.axis_index("tp")
    local = r.grads[1].shape[0]
    parts = (
        (0, 0, 3 * local), (0, 3 * local, local),
        (1, 0, local), (1, local, 2 * local), (1, 3 * local, local),
        (2, 0, r.block[2].shape[0]), (3, 0, r.block[3].shape[0]),
    )
    loads = [pltpu.make_async_copy(r.blocks[g], r.block[g], sems.at[g]) for g in range(4)]
    rows = [
        pltpu.make_async_copy(source, target, sems.at[4 + i])
        for i, (source, target) in enumerate(((r.layer_in, r.layer), (r.grad_in, r.grad), (r.source_in, r.source)))
    ]
    outs = [pltpu.make_async_copy(r.layer, r.layer_out, sems.at[7]), pltpu.make_async_copy(r.grad, r.input_grad, sems.at[8])]
    for copy in rows[2:] + loads + rows[:2]:
        copy.start()
    inverse = 1.0 / small[7:8, :1]
    r.gain_grad[...] = small[:3, :model] * inverse
    r.shift_grad[...] = small[3:6, :model] * inverse
    r.bias_out_grad[...] = (small[6:7, :model] * inverse).reshape(model)
    r.bias_in_grad[...] = (small[pl.ds(8 + place, 1)] * inverse).reshape(small.shape[1])
    width, depth = configs[0, 0], configs[0, 3]
    factor = (column(1, (1, model)) < width).astype(F32) / jnp.full((1, 1), depth.astype(F32))
    rows[2].wait()

    def spread(i):
        part = pl.ds(pl.multiple_of(i * 64, 64), 64)
        value = r.source[part] * factor
        for level in range(layers):
            chosen = (jnp.full((1, 1), depth) >= layers - level).astype(F32)
            r.memories[level, part] = value * chosen

    each(r.source.shape[0] // 64, spread)
    outs.append(pltpu.make_async_copy(r.memories, r.memory_grad, sems.at[9]))
    outs[2].start()
    for i, (g, start, count) in enumerate(parts):
        if start == 0:
            loads[g].wait()

        def scale(at):
            here = pl.ds(pl.multiple_of(at * 32, 32), 32)
            there = pl.ds(pl.multiple_of(start + at * 32, 32), 32)
            r.wide[g][there] = r.block[g][there].astype(F32) * inverse

        each(count // 32, scale)
        outs.append(pltpu.make_async_copy(r.wide[g].at[pl.ds(start, count)], r.grads[i], sems.at[10 + i]))
        outs[-1].start()
    for i in range(2):
        rows[i].wait()
        outs[i].start()
    for copy in outs:
        copy.wait()


def run_finish(ins, layers):
    blocks, small = ins["blocks"], ins["small"]
    rows = ins["layer_in"].shape
    local, units = blocks[0].shape[0] // 4, small.shape[1]

    def shape(*dims):
        return jax.ShapeDtypeStruct(dims, F32)

    counts = (3 * local, local, local, 2 * local, local)
    outs = dict(
        layer_out=shape(*rows), input_grad=shape(*rows), memory_grad=shape(layers, *rows),
        gain_grad=shape(3, rows[1]), shift_grad=shape(3, rows[1]), bias_in_grad=shape(units), bias_out_grad=shape(rows[1]),
        grads=[shape(count, rows[1]) for count in counts] + [shape(*blocks[2].shape), shape(*blocks[3].shape)],
    )
    scratch = dict(
        layer=pltpu.VMEM(rows, F32), grad=pltpu.VMEM(rows, F32), source=pltpu.VMEM(rows, F32),
        memories=pltpu.VMEM((layers,) + rows, F32),
        block=[pltpu.VMEM(block.shape, BF16) for block in blocks],
        wide=[pltpu.VMEM(block.shape, F32) for block in blocks],
        sems=pltpu.SemaphoreType.DMA((17,)),
    )
    hbm = pl.ANY
    spaces = dict(
        configs=pltpu.SMEM, layer_in=hbm, grad_in=hbm, source_in=hbm, blocks=hbm,
        layer_out=hbm, input_grad=hbm, memory_grad=hbm, grads=hbm,
    )
    return call(finish_kernel, "finish", ins, outs, scratch, spaces, vmem_limit_bytes=60 * 2**20)


def per_device(
    inputs, memory, out_grad, lengths, src_lengths, configs, norm_gain, norm_bias,
    self_qkv, self_out, cross_q, cross_kv, cross_out, ffn_in, ffn_in_bias, ffn_out, ffn_out_bias,
):
    model = inputs.shape[1]
    layers = memory.shape[0]
    local = self_out.shape[0]
    done = run_layer(dict(
        lengths=lengths, src_lengths=src_lengths, configs=configs, gains=norm_gain, shifts=norm_bias,
        bias_in=ffn_in_bias, bias_out=ffn_out_bias, x_in=inputs, memory_in=memory, upstream_in=out_grad,
        shards=[
            self_qkv.transpose(1, 2, 0).reshape(3 * local, model), self_out, cross_q.T,
            cross_kv.transpose(1, 2, 0).reshape(2 * local, model), cross_out, ffn_in, ffn_out,
        ],
    ))
    out = run_finish(dict(
        configs=configs, small=done.small_out, layer_in=done.layer_out, grad_in=done.input_grad,
        source_in=done.memory_out, blocks=done.blocks,
    ), layers)
    grads = out.grads
    return (
        out.layer_out,
        out.input_grad,
        out.memory_grad,
        out.gain_grad,
        out.shift_grad,
        grads[0].reshape(3, local, model).transpose(2, 0, 1),
        grads[1],
        grads[2].T,
        grads[3].reshape(2, local, model).transpose(2, 0, 1),
        grads[4],
        grads[5],
        out.bias_in_grad,
        grads[6],
        out.bias_out_grad,
    )


def solution(mesh):
    rows = P(("grp", "dp", "tp"), None)
    stack = P(None, ("grp", "dp", "tp"), None)
    weights = (
        P(None, None, "tp"), P("tp", None), P(None, "tp"), P(None, None, "tp"), P("tp", None),
        P(None, "tp"), P("tp"), P("tp", None), P(),
    )
    return jax.shard_map(
        per_device,
        mesh=mesh,
        in_specs=(rows, stack, rows, P(("grp", "dp")), P(("grp", "dp")), P("grp", None), P(), P()) + weights,
        out_specs=(rows, rows, stack, P(), P()) + weights,
        check_vma=False,
    )
```

```python
import functools
import types

import jax
import jax.numpy as jnp
from jax import lax
from jax.experimental import pallas as pl
from jax.experimental.pallas import tpu as pltpu
from jax.sharding import PartitionSpec as P

HD = 80
LEN = 256
EPSILON = 1e-05
NEGATIVE = -1e30
SCALE = HD ** (-0.5)
LOG2E = 1.4426950408889634
F32 = jnp.float32
BF16 = jnp.bfloat16


MESH = pl.DeviceIdType.MESH


class Place:
    def __init__(self):
        self.tps = lax.axis_size("tp")
        self.extra = lax.axis_size("dp") // 2
        assert lax.axis_size("grp") == 4 and lax.axis_size("dp") % 2 == 0
        grp, dp, tp = (lax.axis_index(name) for name in ("grp", "dp", "tp"))
        core, low, high = dp % 2, grp % 2, grp // 2
        flip_low, flip_high = grp + 1 - 2 * low, grp + 2 - 4 * high
        self.grp, self.dp, self.tp, self.core = grp, dp, tp, core
        self.first_bit = (1 - core) * low + core * high
        self.second_bit = (1 - core) * high + core * low
        self.first = ((1 - core) * flip_low + core * flip_high, dp, tp)
        self.second = ((1 - core) * flip_high + core * flip_low, dp, tp)
        self.across = (3 - grp, dp, tp)
        self.sibling = (grp, dp + 1 - 2 * core, tp)
        self.above = (grp, dp, tp + 1)
        self.below = (grp, dp, tp - 1)
        self.has_above = tp < self.tps - 1
        self.has_below = tp > 0

    def copy_of(self, step):
        return (self.grp, ((self.dp // 2 + step) % self.extra) * 2 + self.core, self.tp)

    def nth_block(self, k):
        size = self.tps
        upper = (2 * self.tp) // size
        lead = (1 - upper) * self.tp + upper * (size - 1 - self.tp)
        spot = k + (k + size - lead) // size
        return (1 - upper) * spot + upper * (size - 1 - spot)

    def along(self, tp):
        return (self.grp, self.dp, tp)

    def barrier(self):
        sem = pltpu.get_barrier_semaphore()
        partners = [self.first, self.second, self.across, self.sibling]
        partners += [self.along((self.tp + step) % self.tps) for step in range(1, self.tps)]
        partners += [self.copy_of(step) for step in range(1, self.extra)]
        for device in partners:
            pl.semaphore_signal(sem, inc=1, device_id=device, device_id_type=MESH)
        pl.semaphore_wait(sem, len(partners))


def push(src, dst, send_sem, recv_sem, device):
    return pltpu.make_async_remote_copy(
        src_ref=src, dst_ref=dst, send_sem=send_sem, recv_sem=recv_sem, device_id=device, device_id_type=MESH
    )


def rows_of(ref, lead, start, count):
    return ref.at[lead, pl.ds(pl.multiple_of(start, 16), count)]


def add_units(total, term, unit):
    def step(i, carry):
        rows = pl.ds(pl.multiple_of(i * unit, 16), unit)
        total[rows] = total[rows] + term[rows]
        return carry

    lax.fori_loop(0, total.shape[0] // unit, step, 0)


class Spread:
    KINDS = 14

    def __init__(self, place, view, unit, sems, direct=False):
        self.place, self.view, self.unit, self.sems = place, view, unit, sems
        f, s, c = place.first_bit, place.second_bit, place.core
        self.units = (f * 2 + s, f * 2 + 1 - s, (1 - f) * 2 + s, (1 - f) * 2 + 1 - s)
        self.theirs = (s * 2 + f, s * 2 + 1 - f, (1 - s) * 2 + f, (1 - s) * 2 + 1 - f)
        self.table = [
            (place.second, (c, self.units[0]), (c, self.units[1])),
            (place.first, (c, self.units[0]), (c, self.units[2])),
            (place.across if direct else place.first, (c, self.units[0 if direct else 1]), (c, self.units[3])),
        ] + [(place.sibling, (c, u), (1 - c, t)) for u, t in zip(self.units, self.theirs)]
        if direct:
            self.waits = ((), (0, 1, 2), (3, 4, 5, 6))
            self.sends = ((0, 1, 2, 3), (4, 5, 6), ())
        else:
            self.waits = ((), (0,), (1, 2), (3, 4, 5, 6))
            self.sends = ((0, 1, 3), (2, 4), (5, 6), ())

    def region(self, spot):
        half, unit = spot
        return self.view((half * 4 + unit) * self.unit, self.unit)

    def own(self):
        return self.region((self.place.core, self.units[0]))

    def copy(self, n, lands=False):
        device, leaves, landing = self.table[n]
        part = self.region(landing if lands else leaves)
        return push(part, part, self.sems(2 * n), self.sems(2 * n + 1), device)

    def step(self, stage):
        for n in self.waits[stage]:
            self.copy(n, lands=True).wait_recv()
        for n in self.sends[stage]:
            self.copy(n).start()

    def finish(self):
        for n in range(7):
            self.copy(n).wait_send()


class Gather:
    KINDS = Spread.KINDS + 3

    def __init__(self, place, buffers, sems):
        self.place, self.buffers, self.sems = place, buffers, sems
        self.unit = [ref.shape[1] // 8 for ref in buffers]
        self.others = place.tps - 1

    def spread(self, g, j):
        return Spread(
            self.place,
            lambda start, count: rows_of(self.buffers[g], j, start, count),
            self.unit[g],
            lambda kind: self.sems.at[kind, g, j],
        )

    def relays(self, g, j):
        p = self.place
        part = self.spread(g, j).own()
        sem = lambda n: self.sems.at[Spread.KINDS + n, g, j]
        return (
            (jnp.logical_and(j <= p.tp, p.has_above), push(part, part, sem(0), sem(2), p.above)),
            (jnp.logical_and(j >= p.tp, p.has_below), push(part, part, sem(1), sem(2), p.below)),
        )

    def start(self, g):
        for needed, copy in self.relays(g, self.place.tp):
            pl.when(needed)(copy.start)

    def step(self, g, k, stage):
        j = self.place.nth_block(k)
        if stage == 0:
            relays = self.relays(g, j)
            relays[0][1].wait_recv()
            for needed, copy in relays:
                pl.when(needed)(copy.start)
        self.spread(g, j).step(stage)

    def drain(self, g, j):
        for needed, copy in self.relays(g, j):
            pl.when(needed)(copy.wait_send)

        @pl.when(j != self.place.tp)
        def _():
            self.spread(g, j).finish()


class Line:
    def __init__(self, place, buffer, sems):
        self.place, self.buffer, self.sems = place, buffer, sems

    def relays(self, j):
        p = self.place
        part = self.buffer.at[j]
        return (
            (jnp.logical_and(j <= p.tp, p.has_above), push(part, part, self.sems.at[0, j], self.sems.at[2, j], p.above)),
            (jnp.logical_and(j >= p.tp, p.has_below), push(part, part, self.sems.at[1, j], self.sems.at[2, j], p.below)),
        )

    def start(self):
        for needed, copy in self.relays(self.place.tp):
            pl.when(needed)(copy.start)

    def step(self, k):
        j = self.place.nth_block(k)
        relays = self.relays(j)
        relays[0][1].wait_recv()
        for needed, copy in relays:
            pl.when(needed)(copy.start)

    def finish(self):
        for j in range(self.place.tps):
            for needed, copy in self.relays(j):
                pl.when(needed)(copy.wait_send)


class Reduce:
    KINDS = 8 + 6 + 2 + Spread.KINDS + 2

    def __init__(self, place, grads, halves, planes, lines, extras, totals, sems, halving):
        self.place, self.grads, self.totals, self.sems, self.halving = place, grads, totals, sems, halving
        self.halves, self.planes, self.lines, self.extras = halves, planes, lines, extras
        self.unit = [ref.shape[1] // 8 for ref in grads]

    def sem(self, kind, g, j):
        return self.sems.at[kind, g, j]

    def rows(self, g, j, half, unit, count=1):
        size = self.unit[g]
        return rows_of(self.grads[g], j, (half * 4 + unit) * size, count * size)

    def to_sibling(self, g, j):
        p = self.place
        return [push(self.rows(g, j, 1 - p.core, 0, 4), self.halves[g].at[j], self.sem(0, g, j), self.sem(1, g, j), p.sibling)]

    def in_plane(self, g, j):
        p = self.place
        f, s = p.first_bit, p.second_bit
        goals = ((p.second, f * 2 + 1 - s), (p.first, (1 - f) * 2 + s), (p.across, (1 - f) * 2 + 1 - s))
        return [self.plane_copy(g, j, i, device, u) for i, (device, u) in enumerate(goals)]

    def by_halves(self, g, j):
        p = self.place
        f, s = p.first_bit, p.second_bit
        goals = ((p.first, (1 - f) * 2), (p.first, (1 - f) * 2 + 1), (p.second, f * 2 + 1 - s))
        return [self.plane_copy(g, j, i, device, u) for i, (device, u) in enumerate(goals)]

    def plane_copy(self, g, j, i, device, unit):
        return push(
            self.rows(g, j, self.place.core, unit), self.planes[g].at[j, i],
            self.sem(8 + 2 * i, g, j), self.sem(9 + 2 * i, g, j), device,
        )

    def piece(self, g, j):
        p = self.place
        return self.rows(g, j, p.core, p.first_bit * 2 + p.second_bit)

    def along(self, g, j):
        p = self.place
        return push(self.piece(g, j), self.lines[g].at[p.tp], self.sem(14, g, j), self.sem(15, g, p.tp), p.along(j))

    def from_place(self, g, j):
        p = self.place
        return push(self.piece(g, j), self.lines[g].at[j], self.sem(14, g, j), self.sem(15, g, j), p.along(j))

    def step(self, g, j, stage):
        p = self.place
        if stage == 0:
            for copy in self.to_sibling(g, j):
                copy.start()
        if stage == 1:
            for copy in self.to_sibling(g, j):
                copy.wait_recv()
            add_units(self.rows(g, j, p.core, 0, 4), self.halves[g].at[j], self.unit[g])
            for copy in self.by_halves(g, j)[:2] if self.halving[g] else self.in_plane(g, j):
                copy.start()
        if stage == 2 and self.halving[g]:
            copies = self.by_halves(g, j)
            for i in range(2):
                copies[i].wait_recv()
                add_units(self.rows(g, j, p.core, p.first_bit * 2 + i), self.planes[g].at[j, i], self.unit[g])
            copies[2].start()
        elif stage == 2:
            for copy in self.in_plane(g, j):
                copy.wait_recv()
            a, b, c = (self.planes[g][j, i].astype(F32) for i in range(3))
            piece = self.piece(g, j)
            piece[...] = ((piece[...].astype(F32) + a) + (b + c)).astype(BF16)
            pl.when(j != p.tp)(self.along(g, j).start)
        if stage == 3:
            self.by_halves(g, j)[2].wait_recv()
            add_units(self.piece(g, j), self.planes[g].at[j, 2], self.unit[g])
            pl.when(j != p.tp)(self.along(g, j).start)

    def spread(self, g):
        return Spread(
            self.place,
            lambda start, count: self.totals[g].at[pl.ds(pl.multiple_of(start, 16), count)],
            self.unit[g],
            lambda kind: self.sems.at[16 + kind, g, 0],
            direct=not self.halving[g],
        )

    def copies(self, g, step):
        p = self.place
        base = self.KINDS - 2
        return push(
            self.piece(g, p.tp), self.extras[g].at[step], self.sem(base, g, step), self.sem(base + 1, g, step), p.copy_of(step)
        )

    def settle(self, g):
        p = self.place
        piece = self.piece(g, p.tp)
        total = piece[...].astype(F32)
        for k in range(p.tps - 1):
            j = p.nth_block(k)
            self.from_place(g, j).wait_recv()
            total = total + self.lines[g][j].astype(F32)
        if p.extra > 1:
            piece[...] = total.astype(BF16)
            for step in range(1, p.extra):
                self.copies(g, step).start()
            for step in range(1, p.extra):
                self.copies(g, step).wait()
                total = total + self.extras[g][step].astype(F32)
        own = self.spread(g).own()
        own[...] = total.astype(BF16)
        self.spread(g).step(0)

    def share(self, g, stage):
        self.spread(g).step(stage)

    def finish(self, g):
        p = self.place
        for j in range(p.tps):
            for copy in self.to_sibling(g, j) + (self.by_halves(g, j) if self.halving[g] else self.in_plane(g, j)):
                copy.wait_send()
            pl.when(j != p.tp)(self.along(g, j).wait_send)
        self.spread(g).finish()


class SumSmall:
    @staticmethod
    def slots(tps, extra):
        return 8 + tps + extra

    def __init__(self, place, slots, sems):
        self.place, self.slots_ref, self.sems = place, slots, sems

    def move(self, source, target, device, kind):
        slots = self.slots_ref
        return push(slots.at[source], slots.at[target], self.sems.at[0, kind], self.sems.at[1, target], device)

    def in_plane(self):
        p = self.place
        return [self.move(2, 3 + i, device, 3 + i) for i, device in enumerate((p.second, p.first, p.across))]

    def copies(self):
        p = self.place
        return [self.move(6, 8 + p.tps + s, p.copy_of(s), 8 + p.tps + s) for s in range(1, p.extra)]

    def along(self, k, lands=False):
        p = self.place
        j = p.nth_block(k)
        return self.move(7, 8 + (j if lands else p.tp), p.along(j), 8 + j)

    def start(self):
        self.move(0, 1, self.place.sibling, 1).start()

    def exchange(self, stage):
        p, slots = self.place, self.slots_ref
        if stage == 0:
            self.move(0, 1, p.sibling, 1).wait_recv()
            slots[2] = slots[0] + slots[1]
            for copy in self.in_plane():
                copy.start()
        else:
            for copy in self.in_plane():
                copy.wait_recv()
            slots[6] = (slots[2] + slots[3]) + (slots[4] + slots[5])
            for copy in self.copies():
                copy.start()
            total = slots[6]
            for s, copy in enumerate(self.copies()):
                copy.wait_recv()
                total = total + slots[9 + p.tps + s]
            slots[7] = total
            for k in range(p.tps - 1):
                self.along(k).start()

    def total(self):
        p, slots = self.place, self.slots_ref
        value = slots[7]
        for k in range(p.tps - 1):
            self.along(k, lands=True).wait_recv()
            value = value + slots[8 + p.nth_block(k)]
        return value

    def finish(self):
        p = self.place
        self.move(0, 1, p.sibling, 1).wait_send()
        for copy in self.in_plane() + self.copies():
            copy.wait_send()
        for k in range(p.tps - 1):
            self.along(k).wait_send()


def dot_nn(left, right):
    return lax.dot_general(left, right, (((1,), (0,)), ((), ())), preferred_element_type=F32)


def dot_nt(left, right):
    return lax.dot_general(left, right, (((1,), (1,)), ((), ())), preferred_element_type=F32)


def dot_tn(left, right):
    return lax.dot_general(left, right, (((0,), (0,)), ((), ())), preferred_element_type=F32)


def column(axis, shape):
    return lax.broadcasted_iota(jnp.int32, shape, axis)


def each(count, step):

    def run(i, carry):
        step(i)
        return carry

    lax.fori_loop(0, count, run, 0)


CHUNK = 32
CUBE = 0.044715
ROOT = 0.7978845608028654


def layer_kernel(r):
    r.a2, r.a3, r.e = (r.memory.at[i] for i in range(3))
    columns = pl.ds(0, r.x.shape[1])
    r.dh, r.dm = r.before.at[:, columns], r.down.at[:, columns]
    place = Place()
    n = place.tps
    x, model = r.x, r.x.shape[1]
    owned = x.shape[0]
    sentences = owned // LEN
    local = r.c[0].shape[1]
    heads_here = local // HD
    units = r.hidden.shape[1]
    layers = r.memory.shape[0]
    weights = r.w
    lengths, sources, configs = r.lengths, r.src_lengths, r.configs
    width, heads, hidden_units, depth = (configs[0, i] for i in range(4))
    inv_width = 1.0 / jnp.full((1, 1), width.astype(F32))
    inv_depth = 1.0 / jnp.full((1, 1), depth.astype(F32))
    width_mask = (column(1, (1, model)) < width).astype(F32)

    local_sem = r.local_sems
    spots = (
        (0, 0, 3 * local), (0, 3 * local, local),
        (1, 0, local), (1, local, 2 * local), (1, 3 * local, local),
        (2, 0, weights[2].shape[1]), (3, 0, weights[3].shape[1]),
    )
    fills = [
        (g, pltpu.make_async_copy(r.shards[i], weights[g].at[place.tp, pl.ds(start, size)], local_sem.at[i]))
        for i, (g, start, size) in enumerate(spots)
    ]
    loads = [
        pltpu.make_async_copy(source, target, local_sem.at[7 + i])
        for i, (source, target) in enumerate(((r.x_in, r.x), (r.memory_in, r.memory), (r.upstream_in, r.upstream)))
    ]
    for _, copy in fills[:2]:
        copy.start()
    loads[0].start()
    for _, copy in fills[2:]:
        copy.start()
    loads[1].start()
    loads[2].start()
    r.bias[place.tp] = jnp.broadcast_to(r.bias_in[...].reshape(1, units), r.bias.shape[1:])
    place.barrier()

    gather = Gather(place, weights, r.gather_sems)
    bias = Line(place, r.bias, r.bias_sems)
    for g in range(4):
        for group, copy in fills:
            if group == g:
                copy.wait()
        gather.start(g)
        if g == 0:
            bias.start()
    order = [(g, k) for g in (0, 1) for k in range(n - 1)] + [(g, k) for k in range(n - 1) for g in (2, 3)]

    def g_tick(tick):
        for stage in range(4):
            if 0 <= tick - stage < len(order):
                gather.step(*order[tick - stage], stage)

    def block(k):
        later = (k + n - 1) // n
        return (1 - later) * place.tp + later * place.nth_block(k - 1)

    def block_last(k):
        own = k // (n - 1)
        return own * place.tp + (1 - own) * place.nth_block(k)

    def hooks(table, k, b):
        for (kk, bb), steps in table.items():

            @pl.when(jnp.logical_and(k == kk, b == bb))
            def _():
                for step in steps:
                    step()

    def chunk(i):
        return pl.ds(pl.multiple_of(i * CHUNK, CHUNK), CHUNK)

    def keep_of(i):
        per = LEN // CHUNK
        spot = column(0, (CHUNK, 1)) + (i % per) * CHUNK
        return (spot < lengths[place.tp * sentences + i // per]).astype(F32) * width_mask

    def norm_parts(rows):
        mean = jnp.sum(rows * width_mask, axis=-1, keepdims=True) * inv_width
        centred = (rows - mean) * width_mask
        spread = jnp.sum(centred * centred, axis=-1, keepdims=True) * inv_width
        rstd = lax.rsqrt(spread + EPSILON)
        return centred * rstd, rstd

    def norm(rows, which):
        hat, _ = norm_parts(rows)
        return ((hat * r.gains[which:which + 1] + r.shifts[which:which + 1]) * width_mask).astype(BF16)

    def fold(values):
        return jnp.sum(values.reshape(values.shape[0] // 8, 8, values.shape[1]), axis=0)

    def norm_backward(rows, which, upstream):
        hat, rstd = norm_parts(rows)
        upstream = upstream * width_mask
        sums = r.norm_sums
        sums[which] = sums[which] + fold(upstream * hat)
        sums[3 + which] = sums[3 + which] + fold(upstream)
        scaled = upstream * r.gains[which:which + 1]
        first = jnp.sum(scaled, axis=-1, keepdims=True) * inv_width
        second = jnp.sum(scaled * hat, axis=-1, keepdims=True) * inv_width
        return (rstd * (scaled - first - hat * second)) * width_mask

    chunks = owned // CHUNK

    def each_chunk(step):

        def four(i):
            for part in range(4):
                step(4 * i + part)

        each(chunks // 4, four)

    acc, da, dh = r.acc, r.da, r.dh
    zeros = jnp.zeros((CHUNK, model), F32)
    r.norm_sums[...] = jnp.zeros(r.norm_sums.shape, F32)
    r.bias_sums[...] = jnp.zeros(r.bias_sums.shape, F32)

    def sentence(b):
        return pl.ds(pl.multiple_of(b * LEN, LEN), LEN)

    def head_keep(j, h):
        return jnp.where(j * heads_here + h < heads, 1.0, 0.0).astype(F32)

    def causal(b, start, size):
        return column(0, (size, 128)) <= column(1, (size, 128)) + start

    def crossing(b, start, size):
        return column(0, (size, 1)) < sources[place.tp * sentences + b]

    def reach(g, start):
        return start + 128 if g == 0 else LEN

    def bands(h):
        return [pl.ds(i * local + h * HD, HD) for i in range(3)]

    def lanes(b):
        return pl.ds(b * LEN, LEN)

    pairs = [(b, h) for b in range(sentences) for h in range(heads_here)]

    quarters = [(i, b, h, start) for i, (b, h) in enumerate(pairs) for start in range(0, LEN, 128)]

    def attend(k, table, g, allowed):
        w, t, c, p = weights[g], r.t[g], r.c[g], r.p[g]
        j = block(k)
        hooks(table, k, 0)
        if g == 0:
            t[j] = dot_nn(w[j, :3 * local], r.flip[0][...]).astype(BF16)
        else:
            t[j, :local] = dot_nn(w[j, :local], r.flip[0][...]).astype(BF16)
            t[j, local:] = dot_nn(w[j, local:3 * local], r.flip[1][...]).astype(BF16)
        heads_of = [[t[j, band, lanes(b)] for band in bands(h)] for b, h in pairs]
        for i, (query, keys, _) in enumerate(heads_of):
            r.scores[i] = dot_tn(keys, query)
        for i, b, h, start in quarters:
            part, size = pl.ds(start, 128), reach(g, start)
            score = jnp.where(allowed(b, start, size), r.scores[i, :size, part], NEGATIVE)
            raised = jnp.exp2((score - jnp.max(score, axis=0, keepdims=True)) * (SCALE * LOG2E))
            p[j, i, :size, part] = (raised * (1.0 / jnp.sum(raised, axis=0, keepdims=True))).astype(BF16)
            if size < LEN:
                p[j, i, size:, part] = jnp.zeros((LEN - size, 128), BF16)
        for i, (b, h) in enumerate(pairs):
            c[j, pl.ds(h * HD, HD), lanes(b)] = (dot_nn(heads_of[i][2], p[j, i]) * head_keep(j, h)).astype(BF16)
        hooks(table, k, 1)
        acc[...] = acc[...] + dot_tn(c[j], w[j, 3 * local:])

    def attend_backward(k, table, g, query_rows, key_rows):
        w, t, c, p = weights[g], r.t[g], r.c[g], r.p[g]
        j = block_last(k)
        e, dt, dc = r.e, r.dt, r.dc
        dc_all = dot_nn(w[j, 3 * local:], r.flip[0][...])
        for h in range(heads_here):
            dc[h * HD:(h + 1) * HD] = (dc_all[h * HD:(h + 1) * HD] * head_keep(j, h)).astype(BF16)
        heads_of = [[t[j, band, lanes(b)] for band in bands(h)] for b, h in pairs]
        dc_of = [dc[h * HD:(h + 1) * HD, lanes(b)] for b, h in pairs]
        for i, (_, _, values) in enumerate(heads_of):
            r.scores[i] = dot_tn(values, dc_of[i])
        for i, b, h, start in quarters:
            part, size = pl.ds(start, 128), reach(g, start)
            dp, wide = r.scores[i, :size, part], p[j, i, :size, part].astype(F32)
            r.ds[i, :size, part] = (wide * (dp - jnp.sum(dp * wide, axis=0, keepdims=True))).astype(BF16)
            if size < LEN:
                r.ds[i, size:, part] = jnp.zeros((LEN - size, 128), BF16)
        for i, (b, h) in enumerate(pairs):
            (query, keys, _), (dq, dk, dv) = heads_of[i], bands(h)
            dt[dv, lanes(b)] = dot_nt(dc_of[i], p[j, i]).astype(BF16)
            dt[dq, lanes(b)] = (dot_nn(keys, r.ds[i]) * SCALE).astype(BF16)
            dt[dk, lanes(b)] = (dot_nt(query, r.ds[i]) * SCALE).astype(BF16)
        hooks(table, k, 1)
        gather.drain(g, j)
        if g == 0:
            da[...] = da[...] + dot_tn(dt[...], w[j, :3 * local])
            w[j, :3 * local] = dot_nn(dt[...], query_rows[...]).astype(BF16)
        else:
            da[...] = da[...] + dot_tn(dt[:local], w[j, :local])
            r.dm[...] = r.dm[...] + dot_tn(dt[local:], w[j, local:3 * local])
            w[j, :local] = dot_nn(dt[:local], query_rows[...]).astype(BF16)
            w[j, local:3 * local] = dot_nn(dt[local:], key_rows[...]).astype(BF16)
        w[j, 3 * local:] = dot_nn(c[j], e[...]).astype(BF16)

    def feed(k, table):
        j = block(k)
        w_up, w_down = weights[2], weights[3]
        hooks(table, k, 0)
        r.before[...] = dot_nn(r.a3[...], w_up[j]) + r.bias[j, 0:1]
        r.down[...] = dot_nt(r.e[...], w_down[j])
        step_lanes = units // 2

        def bend(i):
            rows = pl.ds(pl.multiple_of(i * 16, 16), 16)
            for start in range(0, units, step_lanes):
                part = pl.ds(start, step_lanes)
                unit = column(1, (1, step_lanes)) + (j * units + start)
                kept = jnp.where(unit < hidden_units, 0.5, 0.0)
                before = r.before[rows, part]
                square = before * before
                bent = jnp.tanh(before * (ROOT + ROOT * CUBE * square))
                half = kept + kept * bent
                through = before * half
                r.hidden[rows, part] = through.astype(BF16)
                slope = half + (through - through * bent) * (ROOT + 3.0 * CUBE * ROOT * square)
                du = (r.down[rows, part] * slope).astype(BF16)
                r.dhidden[rows, part] = du
                r.bias_sums[j, :, part] = r.bias_sums[j, :, part] + fold(du.astype(F32))

        each(owned // 16, bend)
        hooks(table, k, 1)
        acc[...] = acc[...] + dot_nn(r.hidden[...], w_down[j])
        da[...] = da[...] + dot_nt(r.dhidden[...], w_up[j])
        gather.drain(2, j)
        gather.drain(3, j)
        w_down[j] = dot_tn(r.hidden[...], r.e[...]).astype(BF16)
        w_up[j] = dot_nn(r.flip[0][...], r.dhidden[...]).astype(BF16)

    loads[0].wait()

    def begin(i):
        rows = chunk(i)
        r.a1[rows] = norm(x[rows].astype(F32), 0)
        acc[rows] = zeros
        da[rows] = zeros

    each_chunk(begin)
    g_tick(0)
    r.flip[0][...] = r.a1[...].T
    loads[1].wait()

    def mix(i):
        rows = chunk(i)
        total = jnp.zeros((CHUNK, model), F32)
        for level in range(layers):
            chosen = (jnp.full((1, 1), depth) >= layers - level).astype(F32)
            total = total + chosen * r.memory[level, rows].astype(F32)
        r.m[rows] = (total * inv_depth * width_mask).astype(BF16)

    each_chunk(mix)
    g_tick(1)
    r.flip[1][...] = r.m[...].T
    loads[2].wait()
    r.out_sums[...] = jnp.zeros(r.out_sums.shape, F32)

    def grad_in(i):
        rows = chunk(i)
        masked = r.upstream[rows].astype(F32) * keep_of(i)
        r.out_sums[...] = r.out_sums[...] + fold(masked)
        r.e[rows] = masked.astype(BF16)

    each_chunk(grad_in)
    g_tick(2)

    def ticks(*numbers):
        return [functools.partial(g_tick, i) for i in numbers]

    others = n - 1
    assert n == 4
    table = {
        (0, 1): ticks(3),
        (1, 0): ticks(4) + [functools.partial(bias.step, 0)],
        (1, 1): ticks(5),
        (2, 0): [functools.partial(bias.step, 1)],
        (2, 1): ticks(6),
        (3, 0): [functools.partial(bias.step, 2)],
        (3, 1): ticks(7),
    }
    each(n, lambda k: attend(k, table, 0, causal))

    def after_self(i):
        rows = chunk(i)
        h = x[rows].astype(F32) + acc[rows] * keep_of(i)
        r.h1[rows] = h
        r.a2[rows] = norm(h, 1)
        acc[rows] = zeros

    each_chunk(after_self)
    r.flip[0][...] = r.a2[...].T
    table2 = {(0, 0): ticks(8), (0, 1): ticks(9), (1, 1): ticks(10), (2, 1): ticks(11), (3, 1): ticks(12)}
    each(n, lambda k: attend(k, table2, 1, crossing))

    def after_cross(i):
        rows = chunk(i)
        h = r.h1[rows] + acc[rows] * keep_of(i)
        r.h2[rows] = h
        r.a3[rows] = norm(h, 2)
        acc[rows] = zeros

    each_chunk(after_cross)
    r.flip[0][...] = r.a3[...].T

    reduce = Reduce(
        place, weights, r.half, r.plane, r.line, r.extra, r.total, r.reduce_sems, (False, False, True, True)
    )
    plan = {}

    def add(tick, order, step, *args):
        plan.setdefault(tick, []).append((order, len(plan.get(tick, ())), functools.partial(step, *args)))

    def r_tick(tick):
        for _, _, step in sorted(plan.get(tick, ()), key=lambda entry: entry[:2]):
            step()

    def store(g):
        return pltpu.make_async_copy(r.total[g], r.blocks[g], local_sem.at[10 + g])

    feed_times = [(1, 2, 5, 9), (3, 4, 7, 11), (5, 6, 9, 13), (7, 8, 11, 15)]
    times = {
        3: (feed_times, (16, 17, 18, 19)),
        2: (feed_times, (17, 18, 19, 20)),
        1: ([(10, 11, 14), (12, 13, 16), (14, 15, 18), (16, 17, 20)], (20, 21, 22)),
        0: ([(19, 20, 22), (21, 22, 24), (23, 24, 25), (25, 26, 27)], (27, 28, 29)),
    }
    for late, g in enumerate((3, 2, 1, 0)):
        for k, stages in enumerate(times[g][0]):
            j = block(k) if g > 1 else block_last(k)
            for stage, tick in enumerate(stages):
                add(tick, stage, reduce.step, g, j, stage)
        for stage, tick in enumerate(times[g][1]):
            if stage == 0:
                add(tick, 20 - late, reduce.settle, g)
            else:
                add(tick, 30 + stage - late, reduce.share, g, stage)
        add(times[g][1][-1], 50, lambda g=g: store(g).start())

    def reduce_ticks(*numbers):
        return [functools.partial(r_tick, i) for i in numbers]

    def at_end(k, numbers):
        for kk, number in enumerate(numbers):

            @pl.when(k == kk)
            def _():
                r_tick(number)

    table3 = {(0, 0): ticks(13), (0, 1): ticks(14), (1, 1): reduce_ticks(2), (2, 1): reduce_ticks(4), (3, 1): reduce_ticks(6)}

    def feed_step(k):
        feed(k, table3)
        at_end(k, [2 * i + 1 for i in range(n)])

    each(n, feed_step)
    r_tick(8)
    out_copy = pltpu.make_async_copy(acc, r.layer_out, local_sem.at[14])

    def after_feed(i):
        rows = chunk(i)
        keep = keep_of(i)
        acc[rows] = r.h2[rows] + (acc[rows] + r.bias_out[...].reshape(1, model)) * keep
        down = r.upstream[rows].astype(F32) + norm_backward(r.h2[rows], 2, da[rows])
        dh[rows] = down
        r.e[rows] = (down * keep).astype(BF16)
        da[rows] = zeros
        r.dm[rows] = zeros

    each_chunk(after_feed)
    r.flip[0][...] = r.e[...].T
    out_copy.start()
    table4 = {(k, 1): reduce_ticks(9 + 2 * k) for k in range(n)}

    def cross_step(k):
        attend_backward(k, table4, 1, r.a2, r.m)
        at_end(k, [10 + 2 * i for i in range(n)])

    each(n, cross_step)
    memory_copy = pltpu.make_async_copy(r.dm, r.memory_out, local_sem.at[15])
    memory_copy.start()

    def before_cross(i):
        rows = chunk(i)
        down = dh[rows] + norm_backward(r.h1[rows], 1, da[rows])
        dh[rows] = down
        r.e[rows] = (down * keep_of(i)).astype(BF16)
        da[rows] = zeros

    each_chunk(before_cross)
    r.flip[0][...] = r.e[...].T
    r_tick(17)
    table5 = {(k, 1): reduce_ticks(18 + 2 * k) for k in range(n)}

    def self_step(k):
        attend_backward(k, table5, 0, r.a1, r.a1)
        at_end(k, [19 + 2 * i for i in range(n)])

    each(n, self_step)

    def before_self(i):
        rows = chunk(i)
        dh[rows] = dh[rows] + norm_backward(x[rows].astype(F32), 0, da[rows])

    each_chunk(before_self)
    grad_copy = pltpu.make_async_copy(dh, r.input_grad, local_sem.at[16])
    grad_copy.start()

    small = SumSmall(place, r.slots, r.small_sems)

    def small_start():
        own = r.slots.at[0]
        own[...] = jnp.zeros(own.shape, F32)
        for i in range(6):
            own[i:i + 1, :model] = jnp.sum(r.norm_sums[i], axis=0, keepdims=True)
        own[6:7, :model] = jnp.sum(r.out_sums[...], axis=0, keepdims=True)
        tokens = lengths[place.tp * sentences]
        for b in range(1, sentences):
            tokens = tokens + lengths[place.tp * sentences + b]
        own[7:8] = jnp.full((1, own.shape[1]), tokens.astype(F32))
        for i in range(n):
            own[8 + i:9 + i] = jnp.sum(r.bias_sums[i], axis=0, keepdims=True)
        small.start()

    add(26, 5, small_start)
    for stage in range(2):
        add(27 + stage, 5, small.exchange, stage)
    final = max(plan)
    for tick in range(26, final + 1):
        r_tick(tick)
    r.small_out[...] = small.total()
    bias.finish()
    for copy in (out_copy, memory_copy, grad_copy):
        copy.wait()
    for g in range(4):
        reduce.finish(g)
        store(g).wait()
    small.finish()


def call(kernel, name, ins, outs, scratch, spaces, **options):
    trees = (ins, outs, scratch)
    structure = jax.tree_util.tree_structure(trees)

    def body(*refs):
        groups = jax.tree_util.tree_unflatten(structure, refs)
        kernel(types.SimpleNamespace(**groups[0], **groups[1], **groups[2]))

    def specs(group):
        return [
            pl.BlockSpec(memory_space=spaces.get(key, pltpu.VMEM))
            for key in sorted(group) for _ in jax.tree_util.tree_leaves(group[key])
        ]

    leaves = jax.tree_util.tree_leaves
    values = pl.pallas_call(
        body,
        out_shape=leaves(outs),
        in_specs=specs(ins),
        out_specs=specs(outs),
        scratch_shapes=leaves(scratch),
        compiler_params=pltpu.CompilerParams(**options),
        name=name,
    )(*leaves(ins))
    return types.SimpleNamespace(**jax.tree_util.tree_unflatten(jax.tree_util.tree_structure(outs), values))


def run_layer(ins):
    n, extra = lax.axis_size("tp"), lax.axis_size("dp") // 2
    owned, model = ins["x_in"].shape
    memory, shards = ins["memory_in"], ins["shards"]
    local, units = shards[1].shape[0], ins["bias_in"].shape[0]
    small = (16, units)
    assert n <= 8 and units >= model and memory.shape[0] >= 3
    shapes = [(n, 4 * local, model)] * 2 + [(n,) + shards[5].shape, (n,) + shards[6].shape]
    small_slots = SumSmall.slots(n, extra)

    def vmem(*shape):
        return pltpu.VMEM(shape, BF16)

    def wide(*shape):
        return pltpu.VMEM(shape, F32)

    def eighths(*lead, parts=1):
        return [vmem(*lead, rows * parts // 8, columns) for _, rows, columns in shapes]

    dma = pltpu.SemaphoreType.DMA
    scratch = dict(
        w=[vmem(*shape) for shape in shapes],
        bias=wide(n, 8, units),
        x=vmem(owned, model),
        memory=vmem(*memory.shape),
        upstream=vmem(owned, model),
        a1=vmem(owned, model),
        m=vmem(owned, model),
        h1=wide(owned, model),
        h2=wide(owned, model),
        acc=wide(owned, model),
        da=wide(owned, model),
        t=[vmem(n, 3 * local, owned)] * 2,
        c=[vmem(n, local, owned)] * 2,
        p=[vmem(n, owned // LEN * (local // HD), LEN, LEN)] * 2,
        dt=vmem(3 * local, owned),
        dc=vmem(local, owned),
        flip=[vmem(model, owned)] * 2,
        scores=wide(owned // LEN * (local // HD), LEN, LEN),
        ds=vmem(owned // LEN * (local // HD), LEN, LEN),
        before=wide(owned, units),
        down=wide(owned, units),
        hidden=vmem(owned, units),
        dhidden=vmem(owned, units),
        bias_sums=wide(n, 8, units),
        norm_sums=wide(6, 8, model),
        out_sums=wide(8, model),
        half=eighths(n, parts=4),
        plane=eighths(n, 3),
        line=eighths(n),
        extra=eighths(extra),
        total=eighths(parts=8),
        slots=wide(small_slots, *small),
        gather_sems=dma((Gather.KINDS, 4, n)),
        bias_sems=dma((3, n)),
        reduce_sems=dma((Reduce.KINDS, 4, max(n, extra))),
        small_sems=dma((2, small_slots)),
        local_sems=dma((17,)),
    )
    rows = jax.ShapeDtypeStruct((owned, model), F32)
    outs = dict(
        layer_out=rows, input_grad=rows, memory_out=rows, small_out=jax.ShapeDtypeStruct(small, F32),
        blocks=[jax.ShapeDtypeStruct(shape[1:], BF16) for shape in shapes],
    )
    smem, hbm = pltpu.SMEM, pl.ANY
    spaces = dict(
        lengths=smem, src_lengths=smem, configs=smem, x_in=hbm, memory_in=hbm, upstream_in=hbm, shards=hbm,
        layer_out=hbm, input_grad=hbm, memory_out=hbm, blocks=hbm,
    )
    return call(
        layer_kernel, "layer", ins, outs, scratch, spaces,
        collective_id=1, has_side_effects=True, vmem_limit_bytes=64 * 2**20,
    )


def finish_kernel(r):
    small, configs, sems = r.small, r.configs, r.sems
    model = r.gain_grad.shape[1]
    layers = r.memory_grad.shape[0]
    place = lax.axis_index("tp")
    local = r.grads[1].shape[0]
    parts = (
        (0, 0, 3 * local), (0, 3 * local, local),
        (1, 0, local), (1, local, 2 * local), (1, 3 * local, local),
        (2, 0, r.block[2].shape[0]), (3, 0, r.block[3].shape[0]),
    )
    loads = [pltpu.make_async_copy(r.blocks[g], r.block[g], sems.at[g]) for g in range(4)]
    rows = [
        pltpu.make_async_copy(source, target, sems.at[4 + i])
        for i, (source, target) in enumerate(((r.layer_in, r.layer), (r.grad_in, r.grad), (r.source_in, r.source)))
    ]
    outs = [pltpu.make_async_copy(r.layer, r.layer_out, sems.at[7]), pltpu.make_async_copy(r.grad, r.input_grad, sems.at[8])]
    for copy in rows + loads:
        copy.start()
    inverse = 1.0 / small[7:8, :1]
    r.gain_grad[...] = small[:3, :model] * inverse
    r.shift_grad[...] = small[3:6, :model] * inverse
    r.bias_out_grad[...] = (small[6:7, :model] * inverse).reshape(model)
    r.bias_in_grad[...] = (small[pl.ds(8 + place, 1)] * inverse).reshape(small.shape[1])
    width, depth = configs[0, 0], configs[0, 3]
    factor = (column(1, (1, model)) < width).astype(F32) / jnp.full((1, 1), depth.astype(F32))
    for i in range(2):
        rows[i].wait()
        outs[i].start()
    rows[2].wait()

    def spread(i):
        part = pl.ds(pl.multiple_of(i * 64, 64), 64)
        value = r.source[part] * factor
        for level in range(layers):
            chosen = (jnp.full((1, 1), depth) >= layers - level).astype(F32)
            r.memories[level, part] = value * chosen

    each(r.source.shape[0] // 64, spread)
    outs.append(pltpu.make_async_copy(r.memories, r.memory_grad, sems.at[9]))
    outs[2].start()
    for i, (g, start, count) in enumerate(parts):
        if start == 0:
            loads[g].wait()

        size = 80 if count % 80 == 0 else 96

        def scale(at):
            there = pl.ds(pl.multiple_of(start + at * size, 16), size)
            r.wide[g][there] = r.block[g][there].astype(F32) * inverse

        each(count // size, scale)
        outs.append(pltpu.make_async_copy(r.wide[g].at[pl.ds(start, count)], r.grads[i], sems.at[10 + i]))
        outs[-1].start()
    for copy in outs:
        copy.wait()


def run_finish(ins, layers):
    blocks, small = ins["blocks"], ins["small"]
    rows = ins["layer_in"].shape
    local, units = blocks[0].shape[0] // 4, small.shape[1]

    def shape(*dims):
        return jax.ShapeDtypeStruct(dims, F32)

    counts = (3 * local, local, local, 2 * local, local)
    outs = dict(
        layer_out=shape(*rows), input_grad=shape(*rows), memory_grad=shape(layers, *rows),
        gain_grad=shape(3, rows[1]), shift_grad=shape(3, rows[1]), bias_in_grad=shape(units), bias_out_grad=shape(rows[1]),
        grads=[shape(count, rows[1]) for count in counts] + [shape(*blocks[2].shape), shape(*blocks[3].shape)],
    )
    scratch = dict(
        layer=pltpu.VMEM(rows, F32), grad=pltpu.VMEM(rows, F32), source=pltpu.VMEM(rows, F32),
        memories=pltpu.VMEM((layers,) + rows, F32),
        block=[pltpu.VMEM(block.shape, BF16) for block in blocks],
        wide=[pltpu.VMEM(block.shape, F32) for block in blocks],
        sems=pltpu.SemaphoreType.DMA((17,)),
    )
    hbm = pl.ANY
    spaces = dict(
        configs=pltpu.SMEM, layer_in=hbm, grad_in=hbm, source_in=hbm, blocks=hbm,
        layer_out=hbm, input_grad=hbm, memory_grad=hbm, grads=hbm,
    )
    return call(finish_kernel, "finish", ins, outs, scratch, spaces, vmem_limit_bytes=60 * 2**20)


def per_device(
    inputs, memory, out_grad, lengths, src_lengths, configs, norm_gain, norm_bias,
    self_qkv, self_out, cross_q, cross_kv, cross_out, ffn_in, ffn_in_bias, ffn_out, ffn_out_bias,
):
    model = inputs.shape[1]
    layers = memory.shape[0]
    local = self_out.shape[0]
    done = run_layer(dict(
        lengths=lengths, src_lengths=src_lengths, configs=configs, gains=norm_gain, shifts=norm_bias,
        bias_in=ffn_in_bias, bias_out=ffn_out_bias, x_in=inputs, memory_in=memory, upstream_in=out_grad,
        shards=[
            self_qkv.transpose(1, 2, 0).reshape(3 * local, model), self_out, cross_q.T,
            cross_kv.transpose(1, 2, 0).reshape(2 * local, model), cross_out, ffn_in, ffn_out,
        ],
    ))
    out = run_finish(dict(
        configs=configs, small=done.small_out, layer_in=done.layer_out, grad_in=done.input_grad,
        source_in=done.memory_out, blocks=done.blocks,
    ), layers)
    grads = out.grads
    return (
        out.layer_out,
        out.input_grad,
        out.memory_grad,
        out.gain_grad,
        out.shift_grad,
        grads[0].reshape(3, local, model).transpose(2, 0, 1),
        grads[1],
        grads[2].T,
        grads[3].reshape(2, local, model).transpose(2, 0, 1),
        grads[4],
        grads[5],
        out.bias_in_grad,
        grads[6],
        out.bias_out_grad,
    )


def solution(mesh):
    rows = P(("grp", "dp", "tp"), None)
    stack = P(None, ("grp", "dp", "tp"), None)
    weights = (
        P(None, None, "tp"), P("tp", None), P(None, "tp"), P(None, None, "tp"), P("tp", None),
        P(None, "tp"), P("tp"), P("tp", None), P(),
    )
    return jax.shard_map(
        per_device,
        mesh=mesh,
        in_specs=(rows, stack, rows, P(("grp", "dp")), P(("grp", "dp")), P("grp", None), P(), P()) + weights,
        out_specs=(rows, rows, stack, P(), P()) + weights,
        check_vma=False,
    )
```

```python
import functools
import types

import jax
import jax.numpy as jnp
from jax import lax
from jax.experimental import pallas as pl
from jax.experimental.pallas import tpu as pltpu
from jax.sharding import PartitionSpec as P

HD = 80
LEN = 256
EPSILON = 1e-05
NEGATIVE = -1e30
SCALE = HD ** (-0.5)
LOG2E = 1.4426950408889634
F32 = jnp.float32
BF16 = jnp.bfloat16


MESH = pl.DeviceIdType.MESH


class Place:
    def __init__(self):
        self.tps = lax.axis_size("tp")
        self.extra = lax.axis_size("dp") // 2
        assert lax.axis_size("grp") == 4 and lax.axis_size("dp") % 2 == 0
        grp, dp, tp = (lax.axis_index(name) for name in ("grp", "dp", "tp"))
        core, low, high = dp % 2, grp % 2, grp // 2
        flip_low, flip_high = grp + 1 - 2 * low, grp + 2 - 4 * high
        self.grp, self.dp, self.tp, self.core = grp, dp, tp, core
        self.first_bit = (1 - core) * low + core * high
        self.second_bit = (1 - core) * high + core * low
        self.first = ((1 - core) * flip_low + core * flip_high, dp, tp)
        self.second = ((1 - core) * flip_high + core * flip_low, dp, tp)
        self.across = (3 - grp, dp, tp)
        self.sibling = (grp, dp + 1 - 2 * core, tp)
        self.above = (grp, dp, tp + 1)
        self.below = (grp, dp, tp - 1)
        self.has_above = tp < self.tps - 1
        self.has_below = tp > 0

    def copy_of(self, step):
        return (self.grp, ((self.dp // 2 + step) % self.extra) * 2 + self.core, self.tp)

    def nth_block(self, k):
        size = self.tps
        upper = (2 * self.tp) // size
        lead = (1 - upper) * self.tp + upper * (size - 1 - self.tp)
        spot = k + (k + size - lead) // size
        return (1 - upper) * spot + upper * (size - 1 - spot)

    def along(self, tp):
        return (self.grp, self.dp, tp)

    def barrier(self):
        sem = pltpu.get_barrier_semaphore()
        partners = [self.first, self.second, self.across, self.sibling]
        partners += [self.along((self.tp + step) % self.tps) for step in range(1, self.tps)]
        partners += [self.copy_of(step) for step in range(1, self.extra)]
        for device in partners:
            pl.semaphore_signal(sem, inc=1, device_id=device, device_id_type=MESH)
        pl.semaphore_wait(sem, len(partners))


def push(src, dst, send_sem, recv_sem, device):
    return pltpu.make_async_remote_copy(
        src_ref=src, dst_ref=dst, send_sem=send_sem, recv_sem=recv_sem, device_id=device, device_id_type=MESH
    )


def rows_of(ref, lead, start, count):
    return ref.at[lead, pl.ds(pl.multiple_of(start, 16), count)]


def add_units(total, term, unit):
    def step(i, carry):
        rows = pl.ds(pl.multiple_of(i * unit, 16), unit)
        total[rows] = total[rows] + term[rows]
        return carry

    lax.fori_loop(0, total.shape[0] // unit, step, 0)


class Spread:
    KINDS = 6

    def __init__(self, place, view, unit, sems):
        self.place, self.view, self.unit, self.sems = place, view, unit, sems
        f, s, c = place.first_bit, place.second_bit, place.core
        self.table = (
            (place.second, c * 4 + f * 2 + s, c * 4 + f * 2 + 1 - s, 1),
            (place.first, c * 4 + f * 2, c * 4 + 2 - f * 2, 2),
            (place.sibling, c * 4, 4 - c * 4, 4),
        )

    def region(self, start, count):
        return self.view(start * self.unit, count * self.unit)

    def own(self):
        return self.region(self.table[0][1], 1)

    def copy(self, n, lands=False):
        device, leaves, landing, count = self.table[n]
        part = self.region(landing if lands else leaves, count)
        return push(part, part, self.sems(2 * n), self.sems(2 * n + 1), device)

    def step(self, stage):
        if stage > 0:
            self.copy(stage - 1, lands=True).wait_recv()
        if stage < 3:
            self.copy(stage).start()

    def finish(self):
        for n in range(3):
            self.copy(n).wait_send()


class Gather:
    KINDS = Spread.KINDS + 3

    def __init__(self, place, buffers, sems):
        self.place, self.buffers, self.sems = place, buffers, sems
        self.unit = [ref.shape[1] // 8 for ref in buffers]
        self.others = place.tps - 1

    def spread(self, g, j):
        return Spread(
            self.place,
            lambda start, count: rows_of(self.buffers[g], j, start, count),
            self.unit[g],
            lambda kind: self.sems.at[kind, g, j],
        )

    def relays(self, g, j):
        p = self.place
        part = self.spread(g, j).own()
        sem = lambda n: self.sems.at[Spread.KINDS + n, g, j]
        return (
            (jnp.logical_and(j <= p.tp, p.has_above), push(part, part, sem(0), sem(2), p.above)),
            (jnp.logical_and(j >= p.tp, p.has_below), push(part, part, sem(1), sem(2), p.below)),
        )

    def start(self, g):
        for needed, copy in self.relays(g, self.place.tp):
            pl.when(needed)(copy.start)

    def step(self, g, k, stage):
        j = self.place.nth_block(k)
        if stage == 0:
            relays = self.relays(g, j)
            relays[0][1].wait_recv()
            for needed, copy in relays:
                pl.when(needed)(copy.start)
        self.spread(g, j).step(stage)

    def drain(self, g, j):
        for needed, copy in self.relays(g, j):
            pl.when(needed)(copy.wait_send)

        @pl.when(j != self.place.tp)
        def _():
            self.spread(g, j).finish()


class Line:
    def __init__(self, place, buffer, sems):
        self.place, self.buffer, self.sems = place, buffer, sems

    def relays(self, j):
        p = self.place
        part = self.buffer.at[j]
        return (
            (jnp.logical_and(j <= p.tp, p.has_above), push(part, part, self.sems.at[0, j], self.sems.at[2, j], p.above)),
            (jnp.logical_and(j >= p.tp, p.has_below), push(part, part, self.sems.at[1, j], self.sems.at[2, j], p.below)),
        )

    def start(self):
        for needed, copy in self.relays(self.place.tp):
            pl.when(needed)(copy.start)

    def step(self, k):
        j = self.place.nth_block(k)
        relays = self.relays(j)
        relays[0][1].wait_recv()
        for needed, copy in relays:
            pl.when(needed)(copy.start)

    def finish(self):
        for j in range(self.place.tps):
            for needed, copy in self.relays(j):
                pl.when(needed)(copy.wait_send)


class Reduce:
    KINDS = 8 + Spread.KINDS + 2

    def __init__(self, place, grads, halves, planes, lines, extras, totals, sems):
        self.place, self.grads, self.totals, self.sems = place, grads, totals, sems
        self.halves, self.planes, self.lines, self.extras = halves, planes, lines, extras
        self.unit = [ref.shape[1] // 8 for ref in grads]

    def sem(self, kind, g, j):
        return self.sems.at[kind, g, j]

    def rows(self, g, j, half, unit, count=1):
        size = self.unit[g]
        return rows_of(self.grads[g], j, (half * 4 + unit) * size, count * size)

    def move(self, g, j, stage):
        p, size = self.place, self.unit[g]
        if stage == 0:
            part, landing, device = self.rows(g, j, 1 - p.core, 0, 4), self.halves[g].at[j], p.sibling
        elif stage == 1:
            part, device = self.rows(g, j, p.core, 2 - p.first_bit * 2, 2), p.first
            landing = self.planes[g].at[j, pl.ds(0, 2 * size)]
        else:
            part, device = self.rows(g, j, p.core, p.first_bit * 2 + 1 - p.second_bit), p.second
            landing = self.planes[g].at[j, pl.ds(2 * size, size)]
        return push(part, landing, self.sem(2 * stage, g, j), self.sem(2 * stage + 1, g, j), device)

    def kept(self, g, j, stage):
        p, size = self.place, self.unit[g]
        if stage == 0:
            return self.rows(g, j, p.core, 0, 4), self.halves[g].at[j]
        if stage == 1:
            return self.rows(g, j, p.core, p.first_bit * 2, 2), self.planes[g].at[j, pl.ds(0, 2 * size)]
        return self.piece(g, j), self.planes[g].at[j, pl.ds(2 * size, size)]

    def piece(self, g, j):
        p = self.place
        return self.rows(g, j, p.core, p.first_bit * 2 + p.second_bit)

    def along(self, g, j):
        p = self.place
        return push(self.piece(g, j), self.lines[g].at[p.tp], self.sem(6, g, j), self.sem(7, g, p.tp), p.along(j))

    def from_place(self, g, j):
        p = self.place
        return push(self.piece(g, j), self.lines[g].at[j], self.sem(6, g, j), self.sem(7, g, j), p.along(j))

    def step(self, g, j, stage):
        if stage > 0:
            self.move(g, j, stage - 1).wait_recv()
            add_units(*self.kept(g, j, stage - 1), self.unit[g])
        if stage < 3:
            self.move(g, j, stage).start()
        else:
            pl.when(j != self.place.tp)(self.along(g, j).start)

    def spread(self, g):
        return Spread(
            self.place,
            lambda start, count: self.totals[g].at[pl.ds(pl.multiple_of(start, 16), count)],
            self.unit[g],
            lambda kind: self.sems.at[8 + kind, g, 0],
        )

    def copies(self, g, step):
        p = self.place
        base = self.KINDS - 2
        return push(
            self.piece(g, p.tp), self.extras[g].at[step], self.sem(base, g, step), self.sem(base + 1, g, step), p.copy_of(step)
        )

    def settle(self, g):
        p = self.place
        piece = self.piece(g, p.tp)
        total = piece[...].astype(F32)
        for k in range(p.tps - 1):
            j = p.nth_block(k)
            self.from_place(g, j).wait_recv()
            total = total + self.lines[g][j].astype(F32)
        if p.extra > 1:
            piece[...] = total.astype(BF16)
            for step in range(1, p.extra):
                self.copies(g, step).start()
            for step in range(1, p.extra):
                self.copies(g, step).wait()
                total = total + self.extras[g][step].astype(F32)
        own = self.spread(g).own()
        own[...] = total.astype(BF16)
        self.spread(g).step(0)

    def share(self, g, stage):
        self.spread(g).step(stage)

    def finish(self, g):
        p = self.place
        for j in range(p.tps):
            for stage in range(3):
                self.move(g, j, stage).wait_send()
            pl.when(j != p.tp)(self.along(g, j).wait_send)
        self.spread(g).finish()


class SumSmall:
    @staticmethod
    def slots(tps, extra):
        return 8 + tps + extra

    def __init__(self, place, slots, sems):
        self.place, self.slots_ref, self.sems = place, slots, sems

    def move(self, source, target, device, kind):
        slots = self.slots_ref
        return push(slots.at[source], slots.at[target], self.sems.at[0, kind], self.sems.at[1, target], device)

    def in_plane(self):
        p = self.place
        return [self.move(2, 3 + i, device, 3 + i) for i, device in enumerate((p.second, p.first, p.across))]

    def copies(self):
        p = self.place
        return [self.move(6, 8 + p.tps + s, p.copy_of(s), 8 + p.tps + s) for s in range(1, p.extra)]

    def along(self, k, lands=False):
        p = self.place
        j = p.nth_block(k)
        return self.move(7, 8 + (j if lands else p.tp), p.along(j), 8 + j)

    def start(self):
        self.move(0, 1, self.place.sibling, 1).start()

    def exchange(self, stage):
        p, slots = self.place, self.slots_ref
        if stage == 0:
            self.move(0, 1, p.sibling, 1).wait_recv()
            slots[2] = slots[0] + slots[1]
            for copy in self.in_plane():
                copy.start()
        else:
            for copy in self.in_plane():
                copy.wait_recv()
            slots[6] = (slots[2] + slots[3]) + (slots[4] + slots[5])
            for copy in self.copies():
                copy.start()
            total = slots[6]
            for s, copy in enumerate(self.copies()):
                copy.wait_recv()
                total = total + slots[9 + p.tps + s]
            slots[7] = total
            for k in range(p.tps - 1):
                self.along(k).start()

    def total(self):
        p, slots = self.place, self.slots_ref
        value = slots[7]
        for k in range(p.tps - 1):
            self.along(k, lands=True).wait_recv()
            value = value + slots[8 + p.nth_block(k)]
        return value

    def finish(self):
        p = self.place
        self.move(0, 1, p.sibling, 1).wait_send()
        for copy in self.in_plane() + self.copies():
            copy.wait_send()
        for k in range(p.tps - 1):
            self.along(k).wait_send()


def dot_nn(left, right):
    return lax.dot_general(left, right, (((1,), (0,)), ((), ())), preferred_element_type=F32)


def dot_nt(left, right):
    return lax.dot_general(left, right, (((1,), (1,)), ((), ())), preferred_element_type=F32)


def dot_tn(left, right):
    return lax.dot_general(left, right, (((0,), (0,)), ((), ())), preferred_element_type=F32)


def column(axis, shape):
    return lax.broadcasted_iota(jnp.int32, shape, axis)


def each(count, step):

    def run(i, carry):
        step(i)
        return carry

    lax.fori_loop(0, count, run, 0)


CHUNK = 32
CUBE = 0.044715
ROOT = 0.7978845608028654


def layer_kernel(r):
    r.a2, r.a3, r.e = (r.memory.at[i] for i in range(3))
    columns = pl.ds(0, r.x.shape[1])
    r.dh, r.dm = r.before.at[:, columns], r.down.at[:, columns]
    place = Place()
    n = place.tps
    x, model = r.x, r.x.shape[1]
    owned = x.shape[0]
    sentences = owned // LEN
    local = r.c[0].shape[1]
    heads_here = local // HD
    units = r.hidden.shape[1]
    layers = r.memory.shape[0]
    weights = r.w
    lengths, sources, configs = r.lengths, r.src_lengths, r.configs
    width, heads, hidden_units, depth = (configs[0, i] for i in range(4))
    inv_width = 1.0 / jnp.full((1, 1), width.astype(F32))
    inv_depth = 1.0 / jnp.full((1, 1), depth.astype(F32))
    width_mask = (column(1, (1, model)) < width).astype(F32)

    local_sem = r.local_sems
    spots = (
        (0, 0, 3 * local), (0, 3 * local, local),
        (1, 0, local), (1, local, 2 * local), (1, 3 * local, local),
        (2, 0, weights[2].shape[1]), (3, 0, weights[3].shape[1]),
    )
    fills = [
        (g, pltpu.make_async_copy(r.shards[i], weights[g].at[place.tp, pl.ds(start, size)], local_sem.at[i]))
        for i, (g, start, size) in enumerate(spots)
    ]
    loads = [
        pltpu.make_async_copy(source, target, local_sem.at[7 + i])
        for i, (source, target) in enumerate(((r.x_in, r.x), (r.memory_in, r.memory), (r.upstream_in, r.upstream)))
    ]
    for _, copy in fills[:2]:
        copy.start()
    loads[0].start()
    for _, copy in fills[2:]:
        copy.start()
    loads[1].start()
    loads[2].start()
    r.bias[place.tp] = jnp.broadcast_to(r.bias_in[...].reshape(1, units), r.bias.shape[1:])
    place.barrier()

    gather = Gather(place, weights, r.gather_sems)
    bias = Line(place, r.bias, r.bias_sems)
    for g in range(4):
        for group, copy in fills:
            if group == g:
                copy.wait()
        gather.start(g)
        if g == 0:
            bias.start()
    order = [(g, k) for g in (0, 1) for k in range(n - 1)] + [(g, k) for k in range(n - 1) for g in (2, 3)]

    def g_tick(tick):
        for stage in range(4):
            if 0 <= tick - stage < len(order):
                gather.step(*order[tick - stage], stage)

    def block(k):
        later = (k + n - 1) // n
        return (1 - later) * place.tp + later * place.nth_block(k - 1)

    def block_last(k):
        own = k // (n - 1)
        return own * place.tp + (1 - own) * place.nth_block(k)

    def hooks(table, k, b):
        for (kk, bb), steps in table.items():

            @pl.when(jnp.logical_and(k == kk, b == bb))
            def _():
                for step in steps:
                    step()

    def chunk(i):
        return pl.ds(pl.multiple_of(i * CHUNK, CHUNK), CHUNK)

    def keep_of(i):
        per = LEN // CHUNK
        spot = column(0, (CHUNK, 1)) + (i % per) * CHUNK
        return (spot < lengths[place.tp * sentences + i // per]).astype(F32) * width_mask

    def norm_parts(rows):
        mean = jnp.sum(rows * width_mask, axis=-1, keepdims=True) * inv_width
        centred = (rows - mean) * width_mask
        spread = jnp.sum(centred * centred, axis=-1, keepdims=True) * inv_width
        rstd = lax.rsqrt(spread + EPSILON)
        return centred * rstd, rstd

    def norm(rows, which):
        hat, _ = norm_parts(rows)
        return ((hat * r.gains[which:which + 1] + r.shifts[which:which + 1]) * width_mask).astype(BF16)

    def fold(values):
        return jnp.sum(values.reshape(values.shape[0] // 8, 8, values.shape[1]), axis=0)

    def norm_backward(rows, which, upstream):
        hat, rstd = norm_parts(rows)
        upstream = upstream * width_mask
        sums = r.norm_sums
        sums[which] = sums[which] + fold(upstream * hat)
        sums[3 + which] = sums[3 + which] + fold(upstream)
        scaled = upstream * r.gains[which:which + 1]
        first = jnp.sum(scaled, axis=-1, keepdims=True) * inv_width
        second = jnp.sum(scaled * hat, axis=-1, keepdims=True) * inv_width
        return (rstd * (scaled - first - hat * second)) * width_mask

    chunks = owned // CHUNK

    def each_chunk(step):

        def four(i):
            for part in range(4):
                step(4 * i + part)

        each(chunks // 4, four)

    acc, da, dh = r.acc, r.da, r.dh
    zeros = jnp.zeros((CHUNK, model), F32)
    r.norm_sums[...] = jnp.zeros(r.norm_sums.shape, F32)
    r.bias_sums[...] = jnp.zeros(r.bias_sums.shape, F32)

    def sentence(b):
        return pl.ds(pl.multiple_of(b * LEN, LEN), LEN)

    def head_keep(j, h):
        return jnp.where(j * heads_here + h < heads, 1.0, 0.0).astype(F32)

    def causal(b, start, size):
        return column(0, (size, 128)) <= column(1, (size, 128)) + start

    def crossing(b, start, size):
        return column(0, (size, 1)) < sources[place.tp * sentences + b]

    def reach(g, start):
        return start + 128 if g == 0 else LEN

    def bands(h):
        return [pl.ds(i * local + h * HD, HD) for i in range(3)]

    def lanes(b):
        return pl.ds(b * LEN, LEN)

    pairs = [(b, h) for b in range(sentences) for h in range(heads_here)]

    quarters = [(i, b, h, start) for i, (b, h) in enumerate(pairs) for start in range(0, LEN, 128)]

    def attend(k, table, g, allowed):
        w, t, c, p = weights[g], r.t[g], r.c[g], r.p[g]
        j = block(k)
        hooks(table, k, 0)
        if g == 0:
            t[j] = dot_nn(w[j, :3 * local], r.flip[0][...]).astype(BF16)
        else:
            t[j, :local] = dot_nn(w[j, :local], r.flip[0][...]).astype(BF16)
            t[j, local:] = dot_nn(w[j, local:3 * local], r.flip[1][...]).astype(BF16)
        heads_of = [[t[j, band, lanes(b)] for band in bands(h)] for b, h in pairs]
        for i, (query, keys, _) in enumerate(heads_of):
            r.scores[i] = dot_tn(keys, query)
        for i, b, h, start in quarters:
            part, size = pl.ds(start, 128), reach(g, start)
            score = jnp.where(allowed(b, start, size), r.scores[i, :size, part], NEGATIVE)
            raised = jnp.exp2((score - jnp.max(score, axis=0, keepdims=True)) * (SCALE * LOG2E))
            p[j, i, :size, part] = (raised * (1.0 / jnp.sum(raised, axis=0, keepdims=True))).astype(BF16)
            if size < LEN:
                p[j, i, size:, part] = jnp.zeros((LEN - size, 128), BF16)
        for i, (b, h) in enumerate(pairs):
            c[j, pl.ds(h * HD, HD), lanes(b)] = (dot_nn(heads_of[i][2], p[j, i]) * head_keep(j, h)).astype(BF16)
        hooks(table, k, 1)
        acc[...] = acc[...] + dot_tn(c[j], w[j, 3 * local:])

    def attend_backward(k, table, g, query_rows, key_rows):
        w, t, c, p = weights[g], r.t[g], r.c[g], r.p[g]
        j = block_last(k)
        e, dt, dc = r.e, r.dt, r.dc
        dc_all = dot_nn(w[j, 3 * local:], r.flip[0][...])
        for h in range(heads_here):
            dc[h * HD:(h + 1) * HD] = (dc_all[h * HD:(h + 1) * HD] * head_keep(j, h)).astype(BF16)
        heads_of = [[t[j, band, lanes(b)] for band in bands(h)] for b, h in pairs]
        dc_of = [dc[h * HD:(h + 1) * HD, lanes(b)] for b, h in pairs]
        for i, (_, _, values) in enumerate(heads_of):
            r.scores[i] = dot_tn(values, dc_of[i])
        for i, b, h, start in quarters:
            part, size = pl.ds(start, 128), reach(g, start)
            dp, wide = r.scores[i, :size, part], p[j, i, :size, part].astype(F32)
            r.ds[i, :size, part] = (wide * (dp - jnp.sum(dp * wide, axis=0, keepdims=True))).astype(BF16)
            if size < LEN:
                r.ds[i, size:, part] = jnp.zeros((LEN - size, 128), BF16)
        for i, (b, h) in enumerate(pairs):
            (query, keys, _), (dq, dk, dv) = heads_of[i], bands(h)
            dt[dv, lanes(b)] = dot_nt(dc_of[i], p[j, i]).astype(BF16)
            dt[dq, lanes(b)] = (dot_nn(keys, r.ds[i]) * SCALE).astype(BF16)
            dt[dk, lanes(b)] = (dot_nt(query, r.ds[i]) * SCALE).astype(BF16)
        hooks(table, k, 1)
        gather.drain(g, j)
        if g == 0:
            da[...] = da[...] + dot_tn(dt[...], w[j, :3 * local])
            w[j, :3 * local] = dot_nn(dt[...], query_rows[...]).astype(BF16)
        else:
            da[...] = da[...] + dot_tn(dt[:local], w[j, :local])
            r.dm[...] = r.dm[...] + dot_tn(dt[local:], w[j, local:3 * local])
            w[j, :local] = dot_nn(dt[:local], query_rows[...]).astype(BF16)
            w[j, local:3 * local] = dot_nn(dt[local:], key_rows[...]).astype(BF16)
        w[j, 3 * local:] = dot_nn(c[j], e[...]).astype(BF16)

    def feed(k, table):
        j = block(k)
        w_up, w_down = weights[2], weights[3]
        hooks(table, k, 0)
        r.before[...] = dot_nn(r.a3[...], w_up[j]) + r.bias[j, 0:1]
        r.down[...] = dot_nt(r.e[...], w_down[j])
        step_lanes = units // 2

        def bend(i):
            rows = pl.ds(pl.multiple_of(i * 16, 16), 16)
            for start in range(0, units, step_lanes):
                part = pl.ds(start, step_lanes)
                unit = column(1, (1, step_lanes)) + (j * units + start)
                kept = jnp.where(unit < hidden_units, 0.5, 0.0)
                before = r.before[rows, part]
                square = before * before
                bent = jnp.tanh(before * (ROOT + ROOT * CUBE * square))
                half = kept + kept * bent
                through = before * half
                r.hidden[rows, part] = through.astype(BF16)
                slope = half + (through - through * bent) * (ROOT + 3.0 * CUBE * ROOT * square)
                du = (r.down[rows, part] * slope).astype(BF16)
                r.dhidden[rows, part] = du
                r.bias_sums[j, :, part] = r.bias_sums[j, :, part] + fold(du.astype(F32))

        each(owned // 16, bend)
        hooks(table, k, 1)
        acc[...] = acc[...] + dot_nn(r.hidden[...], w_down[j])
        da[...] = da[...] + dot_nt(r.dhidden[...], w_up[j])
        gather.drain(2, j)
        gather.drain(3, j)
        w_down[j] = dot_tn(r.hidden[...], r.e[...]).astype(BF16)
        w_up[j] = dot_nn(r.flip[0][...], r.dhidden[...]).astype(BF16)

    loads[0].wait()

    def begin(i):
        rows = chunk(i)
        r.a1[rows] = norm(x[rows].astype(F32), 0)
        acc[rows] = zeros
        da[rows] = zeros

    each_chunk(begin)
    g_tick(0)
    r.flip[0][...] = r.a1[...].T
    loads[1].wait()

    def mix(i):
        rows = chunk(i)
        total = jnp.zeros((CHUNK, model), F32)
        for level in range(layers):
            chosen = (jnp.full((1, 1), depth) >= layers - level).astype(F32)
            total = total + chosen * r.memory[level, rows].astype(F32)
        r.m[rows] = (total * inv_depth * width_mask).astype(BF16)

    each_chunk(mix)
    g_tick(1)
    r.flip[1][...] = r.m[...].T
    loads[2].wait()
    r.out_sums[...] = jnp.zeros(r.out_sums.shape, F32)

    def grad_in(i):
        rows = chunk(i)
        masked = r.upstream[rows].astype(F32) * keep_of(i)
        r.out_sums[...] = r.out_sums[...] + fold(masked)
        r.e[rows] = masked.astype(BF16)

    each_chunk(grad_in)
    g_tick(2)

    def ticks(*numbers):
        return [functools.partial(g_tick, i) for i in numbers]

    others = n - 1
    assert n == 4
    table = {
        (0, 1): ticks(3),
        (1, 0): ticks(4) + [functools.partial(bias.step, 0)],
        (1, 1): ticks(5),
        (2, 0): [functools.partial(bias.step, 1)],
        (2, 1): ticks(6),
        (3, 0): [functools.partial(bias.step, 2)],
        (3, 1): ticks(7),
    }
    each(n, lambda k: attend(k, table, 0, causal))

    def after_self(i):
        rows = chunk(i)
        h = x[rows].astype(F32) + acc[rows] * keep_of(i)
        r.h1[rows] = h
        r.a2[rows] = norm(h, 1)
        acc[rows] = zeros

    each_chunk(after_self)
    r.flip[0][...] = r.a2[...].T
    table2 = {(0, 0): ticks(8), (0, 1): ticks(9), (1, 1): ticks(10), (2, 1): ticks(11), (3, 1): ticks(12)}
    each(n, lambda k: attend(k, table2, 1, crossing))

    def after_cross(i):
        rows = chunk(i)
        h = r.h1[rows] + acc[rows] * keep_of(i)
        r.h2[rows] = h
        r.a3[rows] = norm(h, 2)
        acc[rows] = zeros

    each_chunk(after_cross)
    r.flip[0][...] = r.a3[...].T

    reduce = Reduce(
        place, weights, r.half, r.plane, r.line, r.extra, r.total, r.reduce_sems
    )
    plan = {}

    def add(tick, order, step, *args):
        plan.setdefault(tick, []).append((order, len(plan.get(tick, ())), functools.partial(step, *args)))

    def r_tick(tick):
        for _, _, step in sorted(plan.get(tick, ()), key=lambda entry: entry[:2]):
            step()

    def store(g):
        return pltpu.make_async_copy(r.total[g], r.blocks[g], local_sem.at[10 + g])

    times = {
        3: ([(1, 2, 6, 10), (3, 4, 8, 11), (5, 6, 9, 13), (7, 9, 11, 15)], (17, 19, 21, 23)),
        2: ([(1, 3, 6, 9), (3, 6, 8, 11), (5, 8, 10, 13), (7, 9, 12, 16)], (18, 20, 22, 24)),
        1: ([(10, 11, 14, 16), (12, 14, 16, 18), (14, 15, 19, 21), (16, 17, 19, 21)], (23, 25, 27, 29)),
        0: ([(19, 20, 22, 24), (21, 22, 24, 25), (23, 24, 25, 26), (25, 26, 27, 28)], (28, 29, 30, 31)),
    }
    for late, g in enumerate((3, 2, 1, 0)):
        for k, stages in enumerate(times[g][0]):
            j = block(k) if g > 1 else block_last(k)
            for stage, tick in enumerate(stages):
                add(tick, stage, reduce.step, g, j, stage)
        for stage, tick in enumerate(times[g][1]):
            if stage == 0:
                add(tick, 20 - late, reduce.settle, g)
            else:
                add(tick, 30 + stage - late, reduce.share, g, stage)
        add(times[g][1][-1], 50, lambda g=g: store(g).start())

    def reduce_ticks(*numbers):
        return [functools.partial(r_tick, i) for i in numbers]

    def at_end(k, numbers):
        for kk, number in enumerate(numbers):

            @pl.when(k == kk)
            def _():
                r_tick(number)

    table3 = {(0, 0): ticks(13), (0, 1): ticks(14), (1, 1): reduce_ticks(2), (2, 1): reduce_ticks(4), (3, 1): reduce_ticks(6)}

    def feed_step(k):
        feed(k, table3)
        at_end(k, [2 * i + 1 for i in range(n)])

    each(n, feed_step)
    r_tick(8)
    out_copy = pltpu.make_async_copy(acc, r.layer_out, local_sem.at[14])

    def after_feed(i):
        rows = chunk(i)
        keep = keep_of(i)
        acc[rows] = r.h2[rows] + (acc[rows] + r.bias_out[...].reshape(1, model)) * keep
        down = r.upstream[rows].astype(F32) + norm_backward(r.h2[rows], 2, da[rows])
        dh[rows] = down
        r.e[rows] = (down * keep).astype(BF16)
        da[rows] = zeros
        r.dm[rows] = zeros

    each_chunk(after_feed)
    r.flip[0][...] = r.e[...].T
    out_copy.start()
    table4 = {(k, 1): reduce_ticks(9 + 2 * k) for k in range(n)}

    def cross_step(k):
        attend_backward(k, table4, 1, r.a2, r.m)
        at_end(k, [10 + 2 * i for i in range(n)])

    each(n, cross_step)
    memory_copy = pltpu.make_async_copy(r.dm, r.memory_out, local_sem.at[15])
    memory_copy.start()

    def before_cross(i):
        rows = chunk(i)
        down = dh[rows] + norm_backward(r.h1[rows], 1, da[rows])
        dh[rows] = down
        r.e[rows] = (down * keep_of(i)).astype(BF16)
        da[rows] = zeros

    each_chunk(before_cross)
    r.flip[0][...] = r.e[...].T
    r_tick(17)
    table5 = {(k, 1): reduce_ticks(18 + 2 * k) for k in range(n)}

    def self_step(k):
        attend_backward(k, table5, 0, r.a1, r.a1)
        at_end(k, [19 + 2 * i for i in range(n)])

    each(n, self_step)

    def before_self(i):
        rows = chunk(i)
        dh[rows] = dh[rows] + norm_backward(x[rows].astype(F32), 0, da[rows])

    each_chunk(before_self)
    grad_copy = pltpu.make_async_copy(dh, r.input_grad, local_sem.at[16])
    grad_copy.start()

    small = SumSmall(place, r.slots, r.small_sems)

    def small_start():
        own = r.slots.at[0]
        own[...] = jnp.zeros(own.shape, F32)
        for i in range(6):
            own[i:i + 1, :model] = jnp.sum(r.norm_sums[i], axis=0, keepdims=True)
        own[6:7, :model] = jnp.sum(r.out_sums[...], axis=0, keepdims=True)
        tokens = lengths[place.tp * sentences]
        for b in range(1, sentences):
            tokens = tokens + lengths[place.tp * sentences + b]
        own[7:8] = jnp.full((1, own.shape[1]), tokens.astype(F32))
        for i in range(n):
            own[8 + i:9 + i] = jnp.sum(r.bias_sums[i], axis=0, keepdims=True)
        small.start()

    add(26, 5, small_start)
    for stage in range(2):
        add(27 + stage, 5, small.exchange, stage)
    final = max(plan)
    for tick in range(26, final + 1):
        r_tick(tick)
    r.small_out[...] = small.total()
    bias.finish()
    for copy in (out_copy, memory_copy, grad_copy):
        copy.wait()
    for g in range(4):
        reduce.finish(g)
        store(g).wait()
    small.finish()


def call(kernel, name, ins, outs, scratch, spaces, **options):
    trees = (ins, outs, scratch)
    structure = jax.tree_util.tree_structure(trees)

    def body(*refs):
        groups = jax.tree_util.tree_unflatten(structure, refs)
        kernel(types.SimpleNamespace(**groups[0], **groups[1], **groups[2]))

    def specs(group):
        return [
            pl.BlockSpec(memory_space=spaces.get(key, pltpu.VMEM))
            for key in sorted(group) for _ in jax.tree_util.tree_leaves(group[key])
        ]

    leaves = jax.tree_util.tree_leaves
    values = pl.pallas_call(
        body,
        out_shape=leaves(outs),
        in_specs=specs(ins),
        out_specs=specs(outs),
        scratch_shapes=leaves(scratch),
        compiler_params=pltpu.CompilerParams(**options),
        name=name,
    )(*leaves(ins))
    return types.SimpleNamespace(**jax.tree_util.tree_unflatten(jax.tree_util.tree_structure(outs), values))


def run_layer(ins):
    n, extra = lax.axis_size("tp"), lax.axis_size("dp") // 2
    owned, model = ins["x_in"].shape
    memory, shards = ins["memory_in"], ins["shards"]
    local, units = shards[1].shape[0], ins["bias_in"].shape[0]
    small = (16, units)
    assert n <= 8 and units >= model and memory.shape[0] >= 3
    shapes = [(n, 4 * local, model)] * 2 + [(n,) + shards[5].shape, (n,) + shards[6].shape]
    small_slots = SumSmall.slots(n, extra)

    def vmem(*shape):
        return pltpu.VMEM(shape, BF16)

    def wide(*shape):
        return pltpu.VMEM(shape, F32)

    def eighths(*lead, parts=1):
        return [vmem(*lead, rows * parts // 8, columns) for _, rows, columns in shapes]

    dma = pltpu.SemaphoreType.DMA
    scratch = dict(
        w=[vmem(*shape) for shape in shapes],
        bias=wide(n, 8, units),
        x=vmem(owned, model),
        memory=vmem(*memory.shape),
        upstream=vmem(owned, model),
        a1=vmem(owned, model),
        m=vmem(owned, model),
        h1=wide(owned, model),
        h2=wide(owned, model),
        acc=wide(owned, model),
        da=wide(owned, model),
        t=[vmem(n, 3 * local, owned)] * 2,
        c=[vmem(n, local, owned)] * 2,
        p=[vmem(n, owned // LEN * (local // HD), LEN, LEN)] * 2,
        dt=vmem(3 * local, owned),
        dc=vmem(local, owned),
        flip=[vmem(model, owned)] * 2,
        scores=wide(owned // LEN * (local // HD), LEN, LEN),
        ds=vmem(owned // LEN * (local // HD), LEN, LEN),
        before=wide(owned, units),
        down=wide(owned, units),
        hidden=vmem(owned, units),
        dhidden=vmem(owned, units),
        bias_sums=wide(n, 8, units),
        norm_sums=wide(6, 8, model),
        out_sums=wide(8, model),
        half=eighths(n, parts=4),
        plane=eighths(n, parts=3),
        line=eighths(n),
        extra=eighths(extra),
        total=eighths(parts=8),
        slots=wide(small_slots, *small),
        gather_sems=dma((Gather.KINDS, 4, n)),
        bias_sems=dma((3, n)),
        reduce_sems=dma((Reduce.KINDS, 4, max(n, extra))),
        small_sems=dma((2, small_slots)),
        local_sems=dma((17,)),
    )
    rows = jax.ShapeDtypeStruct((owned, model), F32)
    outs = dict(
        layer_out=rows, input_grad=rows, memory_out=rows, small_out=jax.ShapeDtypeStruct(small, F32),
        blocks=[jax.ShapeDtypeStruct(shape[1:], BF16) for shape in shapes],
    )
    smem, hbm = pltpu.SMEM, pl.ANY
    spaces = dict(
        lengths=smem, src_lengths=smem, configs=smem, x_in=hbm, memory_in=hbm, upstream_in=hbm, shards=hbm,
        layer_out=hbm, input_grad=hbm, memory_out=hbm, blocks=hbm,
    )
    return call(
        layer_kernel, "layer", ins, outs, scratch, spaces,
        collective_id=1, has_side_effects=True, vmem_limit_bytes=64 * 2**20,
    )


def finish_kernel(r):
    small, configs, sems = r.small, r.configs, r.sems
    model = r.gain_grad.shape[1]
    layers = r.memory_grad.shape[0]
    place = lax.axis_index("tp")
    local = r.grads[1].shape[0]
    parts = (
        (0, 0, 3 * local), (0, 3 * local, local),
        (1, 0, local), (1, local, 2 * local), (1, 3 * local, local),
        (2, 0, r.block[2].shape[0]), (3, 0, r.block[3].shape[0]),
    )
    loads = [pltpu.make_async_copy(r.blocks[g], r.block[g], sems.at[g]) for g in range(4)]
    rows = [
        pltpu.make_async_copy(source, target, sems.at[4 + i])
        for i, (source, target) in enumerate(((r.layer_in, r.layer), (r.grad_in, r.grad), (r.source_in, r.source)))
    ]
    outs = [pltpu.make_async_copy(r.layer, r.layer_out, sems.at[7]), pltpu.make_async_copy(r.grad, r.input_grad, sems.at[8])]
    for copy in rows + loads:
        copy.start()
    inverse = 1.0 / small[7:8, :1]
    r.gain_grad[...] = small[:3, :model] * inverse
    r.shift_grad[...] = small[3:6, :model] * inverse
    r.bias_out_grad[...] = (small[6:7, :model] * inverse).reshape(model)
    r.bias_in_grad[...] = (small[pl.ds(8 + place, 1)] * inverse).reshape(small.shape[1])
    width, depth = configs[0, 0], configs[0, 3]
    factor = (column(1, (1, model)) < width).astype(F32) / jnp.full((1, 1), depth.astype(F32))
    for i in range(2):
        rows[i].wait()
        outs[i].start()
    rows[2].wait()

    def spread(i):
        part = pl.ds(pl.multiple_of(i * 64, 64), 64)
        value = r.source[part] * factor
        for level in range(layers):
            chosen = (jnp.full((1, 1), depth) >= layers - level).astype(F32)
            r.memories[level, part] = value * chosen

    each(r.source.shape[0] // 64, spread)
    outs.append(pltpu.make_async_copy(r.memories, r.memory_grad, sems.at[9]))
    outs[2].start()
    for i, (g, start, count) in enumerate(parts):
        if start == 0:
            loads[g].wait()

        size = 80 if count % 80 == 0 else 96

        def scale(at):
            there = pl.ds(pl.multiple_of(start + at * size, 16), size)
            r.wide[g][there] = r.block[g][there].astype(F32) * inverse

        each(count // size, scale)
        outs.append(pltpu.make_async_copy(r.wide[g].at[pl.ds(start, count)], r.grads[i], sems.at[10 + i]))
        outs[-1].start()
    for copy in outs:
        copy.wait()


def run_finish(ins, layers):
    blocks, small = ins["blocks"], ins["small"]
    rows = ins["layer_in"].shape
    local, units = blocks[0].shape[0] // 4, small.shape[1]

    def shape(*dims):
        return jax.ShapeDtypeStruct(dims, F32)

    counts = (3 * local, local, local, 2 * local, local)
    outs = dict(
        layer_out=shape(*rows), input_grad=shape(*rows), memory_grad=shape(layers, *rows),
        gain_grad=shape(3, rows[1]), shift_grad=shape(3, rows[1]), bias_in_grad=shape(units), bias_out_grad=shape(rows[1]),
        grads=[shape(count, rows[1]) for count in counts] + [shape(*blocks[2].shape), shape(*blocks[3].shape)],
    )
    scratch = dict(
        layer=pltpu.VMEM(rows, F32), grad=pltpu.VMEM(rows, F32), source=pltpu.VMEM(rows, F32),
        memories=pltpu.VMEM((layers,) + rows, F32),
        block=[pltpu.VMEM(block.shape, BF16) for block in blocks],
        wide=[pltpu.VMEM(block.shape, F32) for block in blocks],
        sems=pltpu.SemaphoreType.DMA((17,)),
    )
    hbm = pl.ANY
    spaces = dict(
        configs=pltpu.SMEM, layer_in=hbm, grad_in=hbm, source_in=hbm, blocks=hbm,
        layer_out=hbm, input_grad=hbm, memory_grad=hbm, grads=hbm,
    )
    return call(finish_kernel, "finish", ins, outs, scratch, spaces, vmem_limit_bytes=60 * 2**20)


def per_device(
    inputs, memory, out_grad, lengths, src_lengths, configs, norm_gain, norm_bias,
    self_qkv, self_out, cross_q, cross_kv, cross_out, ffn_in, ffn_in_bias, ffn_out, ffn_out_bias,
):
    model = inputs.shape[1]
    layers = memory.shape[0]
    local = self_out.shape[0]
    done = run_layer(dict(
        lengths=lengths, src_lengths=src_lengths, configs=configs, gains=norm_gain, shifts=norm_bias,
        bias_in=ffn_in_bias, bias_out=ffn_out_bias, x_in=inputs, memory_in=memory, upstream_in=out_grad,
        shards=[
            self_qkv.transpose(1, 2, 0).reshape(3 * local, model), self_out, cross_q.T,
            cross_kv.transpose(1, 2, 0).reshape(2 * local, model), cross_out, ffn_in, ffn_out,
        ],
    ))
    out = run_finish(dict(
        configs=configs, small=done.small_out, layer_in=done.layer_out, grad_in=done.input_grad,
        source_in=done.memory_out, blocks=done.blocks,
    ), layers)
    grads = out.grads
    return (
        out.layer_out,
        out.input_grad,
        out.memory_grad,
        out.gain_grad,
        out.shift_grad,
        grads[0].reshape(3, local, model).transpose(2, 0, 1),
        grads[1],
        grads[2].T,
        grads[3].reshape(2, local, model).transpose(2, 0, 1),
        grads[4],
        grads[5],
        out.bias_in_grad,
        grads[6],
        out.bias_out_grad,
    )


def solution(mesh):
    rows = P(("grp", "dp", "tp"), None)
    stack = P(None, ("grp", "dp", "tp"), None)
    weights = (
        P(None, None, "tp"), P("tp", None), P(None, "tp"), P(None, None, "tp"), P("tp", None),
        P(None, "tp"), P("tp"), P("tp", None), P(),
    )
    return jax.shard_map(
        per_device,
        mesh=mesh,
        in_specs=(rows, stack, rows, P(("grp", "dp")), P(("grp", "dp")), P("grp", None), P(), P()) + weights,
        out_specs=(rows, rows, stack, P(), P()) + weights,
        check_vma=False,
    )
```

```python
import functools
import types

import jax
import jax.numpy as jnp
from jax import lax
from jax.experimental import pallas as pl
from jax.experimental.pallas import tpu as pltpu
from jax.sharding import PartitionSpec as P

HD = 80
LEN = 256
EPSILON = 1e-05
NEGATIVE = -1e30
SCALE = HD ** (-0.5)
LOG2E = 1.4426950408889634
F32 = jnp.float32
BF16 = jnp.bfloat16


MESH = pl.DeviceIdType.MESH


class Place:
    def __init__(self):
        self.tps = lax.axis_size("tp")
        self.extra = lax.axis_size("dp") // 2
        assert lax.axis_size("grp") == 4 and lax.axis_size("dp") % 2 == 0
        grp, dp, tp = (lax.axis_index(name) for name in ("grp", "dp", "tp"))
        core, low, high = dp % 2, grp % 2, grp // 2
        flip_low, flip_high = grp + 1 - 2 * low, grp + 2 - 4 * high
        self.grp, self.dp, self.tp, self.core = grp, dp, tp, core
        self.first_bit = (1 - core) * low + core * high
        self.second_bit = (1 - core) * high + core * low
        self.first = ((1 - core) * flip_low + core * flip_high, dp, tp)
        self.second = ((1 - core) * flip_high + core * flip_low, dp, tp)
        self.across = (3 - grp, dp, tp)
        self.sibling = (grp, dp + 1 - 2 * core, tp)
        self.above = (grp, dp, tp + 1)
        self.below = (grp, dp, tp - 1)
        self.has_above = tp < self.tps - 1
        self.has_below = tp > 0

    def copy_of(self, step):
        return (self.grp, ((self.dp // 2 + step) % self.extra) * 2 + self.core, self.tp)

    def nth_block(self, k):
        size = self.tps
        upper = (2 * self.tp) // size
        lead = (1 - upper) * self.tp + upper * (size - 1 - self.tp)
        spot = k + (k + size - lead) // size
        return (1 - upper) * spot + upper * (size - 1 - spot)

    def along(self, tp):
        return (self.grp, self.dp, tp)

    def barrier(self):
        sem = pltpu.get_barrier_semaphore()
        partners = [self.first, self.second, self.across, self.sibling]
        partners += [self.along((self.tp + step) % self.tps) for step in range(1, self.tps)]
        partners += [self.copy_of(step) for step in range(1, self.extra)]
        for device in partners:
            pl.semaphore_signal(sem, inc=1, device_id=device, device_id_type=MESH)
        pl.semaphore_wait(sem, len(partners))


def push(src, dst, send_sem, recv_sem, device):
    return pltpu.make_async_remote_copy(
        src_ref=src, dst_ref=dst, send_sem=send_sem, recv_sem=recv_sem, device_id=device, device_id_type=MESH
    )


def rows_of(ref, lead, start, count):
    return ref.at[lead, pl.ds(pl.multiple_of(start, 16), count)]


def add_units(total, term, unit):
    def step(i, carry):
        rows = pl.ds(pl.multiple_of(i * unit, 16), unit)
        total[rows] = total[rows] + term[rows]
        return carry

    lax.fori_loop(0, total.shape[0] // unit, step, 0)


class Spread:
    KINDS = 6

    def __init__(self, place, view, unit, sems):
        self.place, self.view, self.unit, self.sems = place, view, unit, sems
        f, s, c = place.first_bit, place.second_bit, place.core
        self.table = (
            (place.second, c * 4 + f * 2 + s, c * 4 + f * 2 + 1 - s, 1),
            (place.first, c * 4 + f * 2, c * 4 + 2 - f * 2, 2),
            (place.sibling, c * 4, 4 - c * 4, 4),
        )

    def region(self, start, count):
        return self.view(start * self.unit, count * self.unit)

    def own(self):
        return self.region(self.table[0][1], 1)

    def copy(self, n, lands=False):
        device, leaves, landing, count = self.table[n]
        part = self.region(landing if lands else leaves, count)
        return push(part, part, self.sems(2 * n), self.sems(2 * n + 1), device)

    def step(self, stage):
        if stage > 0:
            self.copy(stage - 1, lands=True).wait_recv()
        if stage < 3:
            self.copy(stage).start()

    def finish(self):
        for n in range(3):
            self.copy(n).wait_send()


class Gather:
    KINDS = Spread.KINDS + 3

    def __init__(self, place, buffers, sems):
        self.place, self.buffers, self.sems = place, buffers, sems
        self.unit = [ref.shape[1] // 8 for ref in buffers]
        self.others = place.tps - 1

    def spread(self, g, j):
        return Spread(
            self.place,
            lambda start, count: rows_of(self.buffers[g], j, start, count),
            self.unit[g],
            lambda kind: self.sems.at[kind, g, j],
        )

    def relays(self, g, j):
        p = self.place
        part = self.spread(g, j).own()
        sem = lambda n: self.sems.at[Spread.KINDS + n, g, j]
        return (
            (jnp.logical_and(j <= p.tp, p.has_above), push(part, part, sem(0), sem(2), p.above)),
            (jnp.logical_and(j >= p.tp, p.has_below), push(part, part, sem(1), sem(2), p.below)),
        )

    def start(self, g):
        for needed, copy in self.relays(g, self.place.tp):
            pl.when(needed)(copy.start)

    def step(self, g, k, stage):
        j = self.place.nth_block(k)
        if stage == 0:
            relays = self.relays(g, j)
            relays[0][1].wait_recv()
            for needed, copy in relays:
                pl.when(needed)(copy.start)
        self.spread(g, j).step(stage)

    def drain(self, g, j):
        for needed, copy in self.relays(g, j):
            pl.when(needed)(copy.wait_send)

        @pl.when(j != self.place.tp)
        def _():
            self.spread(g, j).finish()


class Line:
    def __init__(self, place, buffer, sems):
        self.place, self.buffer, self.sems = place, buffer, sems

    def relays(self, j):
        p = self.place
        part = self.buffer.at[j]
        return (
            (jnp.logical_and(j <= p.tp, p.has_above), push(part, part, self.sems.at[0, j], self.sems.at[2, j], p.above)),
            (jnp.logical_and(j >= p.tp, p.has_below), push(part, part, self.sems.at[1, j], self.sems.at[2, j], p.below)),
        )

    def start(self):
        for needed, copy in self.relays(self.place.tp):
            pl.when(needed)(copy.start)

    def step(self, k):
        j = self.place.nth_block(k)
        relays = self.relays(j)
        relays[0][1].wait_recv()
        for needed, copy in relays:
            pl.when(needed)(copy.start)

    def finish(self):
        for j in range(self.place.tps):
            for needed, copy in self.relays(j):
                pl.when(needed)(copy.wait_send)


class Reduce:
    KINDS = 8 + Spread.KINDS + 2

    def __init__(self, place, grads, halves, planes, lines, extras, totals, sems):
        self.place, self.grads, self.totals, self.sems = place, grads, totals, sems
        self.halves, self.planes, self.lines, self.extras = halves, planes, lines, extras
        self.unit = [ref.shape[1] // 8 for ref in grads]

    def sem(self, kind, g, j):
        return self.sems.at[kind, g, j]

    def rows(self, g, j, half, unit, count=1):
        size = self.unit[g]
        return rows_of(self.grads[g], j, (half * 4 + unit) * size, count * size)

    def move(self, g, j, stage):
        p, size = self.place, self.unit[g]
        if stage == 0:
            part, landing, device = self.rows(g, j, 1 - p.core, 0, 4), self.halves[g].at[j], p.sibling
        elif stage == 1:
            part, device = self.rows(g, j, p.core, 2 - p.first_bit * 2, 2), p.first
            landing = self.planes[g].at[j, pl.ds(0, 2 * size)]
        else:
            part, device = self.rows(g, j, p.core, p.first_bit * 2 + 1 - p.second_bit), p.second
            landing = self.planes[g].at[j, pl.ds(2 * size, size)]
        return push(part, landing, self.sem(2 * stage, g, j), self.sem(2 * stage + 1, g, j), device)

    def kept(self, g, j, stage):
        p, size = self.place, self.unit[g]
        if stage == 0:
            return self.rows(g, j, p.core, 0, 4), self.halves[g].at[j]
        if stage == 1:
            return self.rows(g, j, p.core, p.first_bit * 2, 2), self.planes[g].at[j, pl.ds(0, 2 * size)]
        return self.piece(g, j), self.planes[g].at[j, pl.ds(2 * size, size)]

    def piece(self, g, j):
        p = self.place
        return self.rows(g, j, p.core, p.first_bit * 2 + p.second_bit)

    def along(self, g, j):
        p = self.place
        return push(self.piece(g, j), self.lines[g].at[p.tp], self.sem(6, g, j), self.sem(7, g, p.tp), p.along(j))

    def from_place(self, g, j):
        p = self.place
        return push(self.piece(g, j), self.lines[g].at[j], self.sem(6, g, j), self.sem(7, g, j), p.along(j))

    def step(self, g, j, stage):
        if stage > 0:
            self.move(g, j, stage - 1).wait_recv()
            add_units(*self.kept(g, j, stage - 1), self.unit[g])
        if stage < 3:
            self.move(g, j, stage).start()
        else:
            pl.when(j != self.place.tp)(self.along(g, j).start)

    def spread(self, g):
        return Spread(
            self.place,
            lambda start, count: self.totals[g].at[pl.ds(pl.multiple_of(start, 16), count)],
            self.unit[g],
            lambda kind: self.sems.at[8 + kind, g, 0],
        )

    def copies(self, g, step):
        p = self.place
        base = self.KINDS - 2
        return push(
            self.piece(g, p.tp), self.extras[g].at[step], self.sem(base, g, step), self.sem(base + 1, g, step), p.copy_of(step)
        )

    def settle(self, g):
        p = self.place
        piece = self.piece(g, p.tp)
        total = piece[...].astype(F32)
        for k in range(p.tps - 1):
            j = p.nth_block(k)
            self.from_place(g, j).wait_recv()
            total = total + self.lines[g][j].astype(F32)
        if p.extra > 1:
            piece[...] = total.astype(BF16)
            for step in range(1, p.extra):
                self.copies(g, step).start()
            for step in range(1, p.extra):
                self.copies(g, step).wait()
                total = total + self.extras[g][step].astype(F32)
        own = self.spread(g).own()
        own[...] = total.astype(BF16)
        self.spread(g).step(0)

    def share(self, g, stage):
        self.spread(g).step(stage)

    def finish(self, g):
        p = self.place
        for j in range(p.tps):
            for stage in range(3):
                self.move(g, j, stage).wait_send()
            pl.when(j != p.tp)(self.along(g, j).wait_send)
        self.spread(g).finish()


class SumSmall:
    @staticmethod
    def slots(tps, extra):
        return 8 + tps + extra

    def __init__(self, place, slots, sems):
        self.place, self.slots_ref, self.sems = place, slots, sems

    def move(self, source, target, device, kind):
        slots = self.slots_ref
        return push(slots.at[source], slots.at[target], self.sems.at[0, kind], self.sems.at[1, target], device)

    def in_plane(self):
        p = self.place
        return [self.move(2, 3 + i, device, 3 + i) for i, device in enumerate((p.second, p.first, p.across))]

    def copies(self):
        p = self.place
        return [self.move(6, 8 + p.tps + s, p.copy_of(s), 8 + p.tps + s) for s in range(1, p.extra)]

    def along(self, k, lands=False):
        p = self.place
        j = p.nth_block(k)
        return self.move(7, 8 + (j if lands else p.tp), p.along(j), 8 + j)

    def start(self):
        self.move(0, 1, self.place.sibling, 1).start()

    def exchange(self, stage):
        p, slots = self.place, self.slots_ref
        if stage == 0:
            self.move(0, 1, p.sibling, 1).wait_recv()
            slots[2] = slots[0] + slots[1]
            for copy in self.in_plane():
                copy.start()
        else:
            for copy in self.in_plane():
                copy.wait_recv()
            slots[6] = (slots[2] + slots[3]) + (slots[4] + slots[5])
            for copy in self.copies():
                copy.start()
            total = slots[6]
            for s, copy in enumerate(self.copies()):
                copy.wait_recv()
                total = total + slots[9 + p.tps + s]
            slots[7] = total
            for k in range(p.tps - 1):
                self.along(k).start()

    def total(self):
        p, slots = self.place, self.slots_ref
        value = slots[7]
        for k in range(p.tps - 1):
            self.along(k, lands=True).wait_recv()
            value = value + slots[8 + p.nth_block(k)]
        return value

    def finish(self):
        p = self.place
        self.move(0, 1, p.sibling, 1).wait_send()
        for copy in self.in_plane() + self.copies():
            copy.wait_send()
        for k in range(p.tps - 1):
            self.along(k).wait_send()


def dot_nn(left, right):
    return lax.dot_general(left, right, (((1,), (0,)), ((), ())), preferred_element_type=F32)


def dot_nt(left, right):
    return lax.dot_general(left, right, (((1,), (1,)), ((), ())), preferred_element_type=F32)


def dot_tn(left, right):
    return lax.dot_general(left, right, (((0,), (0,)), ((), ())), preferred_element_type=F32)


def column(axis, shape):
    return lax.broadcasted_iota(jnp.int32, shape, axis)


def each(count, step):

    def run(i, carry):
        step(i)
        return carry

    lax.fori_loop(0, count, run, 0)


CHUNK = 128
CUBE = 0.044715
ROOT = 0.7978845608028654


def layer_kernel(r):
    r.a2, r.a3, r.e = (r.memory.at[i] for i in range(3))
    columns = pl.ds(0, r.x.shape[1])
    r.dh, r.dm = r.before.at[:, columns], r.down.at[:, columns]
    place = Place()
    n = place.tps
    x, model = r.x, r.x.shape[1]
    owned = x.shape[0]
    sentences = owned // LEN
    local = r.c[0].shape[1]
    heads_here = local // HD
    units = r.hidden.shape[1]
    layers = r.memory.shape[0]
    weights = r.w
    lengths, sources, configs = r.lengths, r.src_lengths, r.configs
    width, heads, hidden_units, depth = (configs[0, i] for i in range(4))
    inv_width = 1.0 / jnp.full((1, 1), width.astype(F32))
    inv_depth = 1.0 / jnp.full((1, 1), depth.astype(F32))
    width_mask = (column(1, (1, model)) < width).astype(F32)

    local_sem = r.local_sems
    spots = (
        (0, 0, 3 * local), (0, 3 * local, local),
        (1, 0, local), (1, local, 2 * local), (1, 3 * local, local),
        (2, 0, weights[2].shape[1]), (3, 0, weights[3].shape[1]),
    )
    fills = [
        (g, pltpu.make_async_copy(r.shards[i], weights[g].at[place.tp, pl.ds(start, size)], local_sem.at[i]))
        for i, (g, start, size) in enumerate(spots)
    ]
    loads = [
        pltpu.make_async_copy(source, target, local_sem.at[7 + i])
        for i, (source, target) in enumerate(((r.x_in, r.x), (r.memory_in, r.memory), (r.upstream_in, r.upstream)))
    ]
    for _, copy in fills[:2]:
        copy.start()
    loads[0].start()
    for _, copy in fills[2:]:
        copy.start()
    loads[1].start()
    loads[2].start()
    r.bias[place.tp] = jnp.broadcast_to(r.bias_in[...].reshape(1, units), r.bias.shape[1:])
    place.barrier()

    gather = Gather(place, weights, r.gather_sems)
    bias = Line(place, r.bias, r.bias_sems)
    for g in range(4):
        for group, copy in fills:
            if group == g:
                copy.wait()
        gather.start(g)
        if g == 0:
            bias.start()
    order = [(g, k) for g in (0, 1) for k in range(n - 1)] + [(g, k) for k in range(n - 1) for g in (2, 3)]

    def g_tick(tick):
        for stage in range(4):
            if 0 <= tick - stage < len(order):
                gather.step(*order[tick - stage], stage)

    def block(k):
        later = (k + n - 1) // n
        return (1 - later) * place.tp + later * place.nth_block(k - 1)

    def block_last(k):
        own = k // (n - 1)
        return own * place.tp + (1 - own) * place.nth_block(k)

    def hooks(table, k, b):
        for (kk, bb), steps in table.items():

            @pl.when(jnp.logical_and(k == kk, b == bb))
            def _():
                for step in steps:
                    step()

    def chunk(i):
        return pl.ds(pl.multiple_of(i * CHUNK, CHUNK), CHUNK)

    def keep_of(i):
        per = LEN // CHUNK
        spot = column(0, (CHUNK, 1)) + (i % per) * CHUNK
        return (spot < lengths[place.tp * sentences + i // per]).astype(F32) * width_mask

    def norm_parts(rows):
        mean = jnp.sum(rows * width_mask, axis=-1, keepdims=True) * inv_width
        centred = (rows - mean) * width_mask
        spread = jnp.sum(centred * centred, axis=-1, keepdims=True) * inv_width
        rstd = lax.rsqrt(spread + EPSILON)
        return centred * rstd, rstd

    def norm(rows, which):
        hat, _ = norm_parts(rows)
        return ((hat * r.gains[which:which + 1] + r.shifts[which:which + 1]) * width_mask).astype(BF16)

    def fold(values):
        return jnp.sum(values.reshape(values.shape[0] // 8, 8, values.shape[1]), axis=0)

    def norm_backward(rows, which, upstream):
        hat, rstd = norm_parts(rows)
        upstream = upstream * width_mask
        sums = r.norm_sums
        sums[which] = sums[which] + fold(upstream * hat)
        sums[3 + which] = sums[3 + which] + fold(upstream)
        scaled = upstream * r.gains[which:which + 1]
        first = jnp.sum(scaled, axis=-1, keepdims=True) * inv_width
        second = jnp.sum(scaled * hat, axis=-1, keepdims=True) * inv_width
        return (rstd * (scaled - first - hat * second)) * width_mask

    chunks = owned // CHUNK

    def each_chunk(step):
        each(chunks, step)

    acc, da, dh = r.acc, r.da, r.dh
    zeros = jnp.zeros((CHUNK, model), F32)
    r.norm_sums[...] = jnp.zeros(r.norm_sums.shape, F32)
    r.bias_sums[...] = jnp.zeros(r.bias_sums.shape, F32)

    def sentence(b):
        return pl.ds(pl.multiple_of(b * LEN, LEN), LEN)

    def head_keep(j, h):
        return jnp.where(j * heads_here + h < heads, 1.0, 0.0).astype(F32)

    def causal(b, start, size):
        return column(0, (size, 128)) <= column(1, (size, 128)) + start

    def crossing(b, start, size):
        return column(0, (size, 1)) < sources[place.tp * sentences + b]

    def reach(g, start):
        return start + 128 if g == 0 else LEN

    def bands(h):
        return [pl.ds(i * local + h * HD, HD) for i in range(3)]

    def lanes(b):
        return pl.ds(b * LEN, LEN)

    pairs = [(b, h) for b in range(sentences) for h in range(heads_here)]

    quarters = [(i, b, h, start) for i, (b, h) in enumerate(pairs) for start in range(0, LEN, 128)]

    def attend(k, table, g, allowed):
        w, t, c, p = weights[g], r.t[g], r.c[g], r.p[g]
        j = block(k)
        hooks(table, k, 0)
        if g == 0:
            t[j] = dot_nt(w[j, :3 * local], r.a1[...]).astype(BF16)
        else:
            t[j, :local] = dot_nt(w[j, :local], r.a2[...]).astype(BF16)
            t[j, local:] = dot_nt(w[j, local:3 * local], r.m[...]).astype(BF16)
        heads_of = [[t[j, band, lanes(b)] for band in bands(h)] for b, h in pairs]
        for i, (query, keys, _) in enumerate(heads_of):
            r.scores[i] = dot_tn(keys, query)
        for i, b, h, start in quarters:
            part, size = pl.ds(start, 128), reach(g, start)
            score = jnp.where(allowed(b, start, size), r.scores[i, :size, part], NEGATIVE)
            raised = jnp.exp2((score - jnp.max(score, axis=0, keepdims=True)) * (SCALE * LOG2E))
            p[j, i, :size, part] = (raised * (1.0 / jnp.sum(raised, axis=0, keepdims=True))).astype(BF16)
            if size < LEN:
                p[j, i, size:, part] = jnp.zeros((LEN - size, 128), BF16)
        for i, (b, h) in enumerate(pairs):
            c[j, pl.ds(h * HD, HD), lanes(b)] = (dot_nn(heads_of[i][2], p[j, i]) * head_keep(j, h)).astype(BF16)
        hooks(table, k, 1)
        acc[...] = acc[...] + dot_tn(c[j], w[j, 3 * local:])

    def attend_backward(k, table, g, query_rows, key_rows):
        w, t, c, p = weights[g], r.t[g], r.c[g], r.p[g]
        j = block_last(k)
        e, dt, dc = r.e, r.dt, r.dc
        dc_all = dot_nt(w[j, 3 * local:], e[...])
        for h in range(heads_here):
            dc[h * HD:(h + 1) * HD] = (dc_all[h * HD:(h + 1) * HD] * head_keep(j, h)).astype(BF16)
        heads_of = [[t[j, band, lanes(b)] for band in bands(h)] for b, h in pairs]
        dc_of = [dc[h * HD:(h + 1) * HD, lanes(b)] for b, h in pairs]
        for i, (_, _, values) in enumerate(heads_of):
            r.scores[i] = dot_tn(values, dc_of[i])
        for i, b, h, start in quarters:
            part, size = pl.ds(start, 128), reach(g, start)
            dp, wide = r.scores[i, :size, part], p[j, i, :size, part].astype(F32)
            r.ds[i, :size, part] = (wide * (dp - jnp.sum(dp * wide, axis=0, keepdims=True))).astype(BF16)
            if size < LEN:
                r.ds[i, size:, part] = jnp.zeros((LEN - size, 128), BF16)
        for i, (b, h) in enumerate(pairs):
            (query, keys, _), (dq, dk, dv) = heads_of[i], bands(h)
            dt[dv, lanes(b)] = dot_nt(dc_of[i], p[j, i]).astype(BF16)
            dt[dq, lanes(b)] = (dot_nn(keys, r.ds[i]) * SCALE).astype(BF16)
            dt[dk, lanes(b)] = (dot_nt(query, r.ds[i]) * SCALE).astype(BF16)
        hooks(table, k, 1)
        gather.drain(g, j)
        if g == 0:
            da[...] = da[...] + dot_tn(dt[...], w[j, :3 * local])
            w[j, :3 * local] = dot_nn(dt[...], query_rows[...]).astype(BF16)
        else:
            da[...] = da[...] + dot_tn(dt[:local], w[j, :local])
            r.dm[...] = r.dm[...] + dot_tn(dt[local:], w[j, local:3 * local])
            w[j, :local] = dot_nn(dt[:local], query_rows[...]).astype(BF16)
            w[j, local:3 * local] = dot_nn(dt[local:], key_rows[...]).astype(BF16)
        w[j, 3 * local:] = dot_nn(c[j], e[...]).astype(BF16)

    def feed(k, table):
        j = block(k)
        w_up, w_down = weights[2], weights[3]
        hooks(table, k, 0)
        r.before[...] = dot_nn(r.a3[...], w_up[j]) + r.bias[j, 0:1]
        r.down[...] = dot_nt(r.e[...], w_down[j])
        step_lanes = units // 2

        def bend(i):
            for start in range(0, units, step_lanes):
                part = pl.ds(start, step_lanes)
                unit = column(1, (1, step_lanes)) + (j * units + start)
                kept = jnp.where(unit < hidden_units, 0.5, 0.0)
                sums = r.bias_sums[j, :, part]
                for line in range(4):
                    rows = pl.ds(pl.multiple_of(i * 64, 64) + line * 16, 16)
                    before = r.before[rows, part]
                    square = before * before
                    bent = jnp.tanh(before * (ROOT + ROOT * CUBE * square))
                    half = kept + kept * bent
                    through = before * half
                    r.hidden[rows, part] = through.astype(BF16)
                    slope = half + (through - through * bent) * (ROOT + 3.0 * CUBE * ROOT * square)
                    du = (r.down[rows, part] * slope).astype(BF16)
                    r.dhidden[rows, part] = du
                    sums = sums + fold(du.astype(F32))
                r.bias_sums[j, :, part] = sums

        each(owned // 64, bend)
        hooks(table, k, 1)
        acc[...] = acc[...] + dot_nn(r.hidden[...], w_down[j])
        da[...] = da[...] + dot_nt(r.dhidden[...], w_up[j])
        gather.drain(2, j)
        gather.drain(3, j)
        w_down[j] = dot_tn(r.hidden[...], r.e[...]).astype(BF16)
        w_up[j] = dot_nn(r.a3t[...], r.dhidden[...]).astype(BF16)

    loads[0].wait()

    def begin(i):
        rows = chunk(i)
        r.a1[rows] = norm(x[rows].astype(F32), 0)
        acc[rows] = zeros
        da[rows] = zeros

    each_chunk(begin)
    g_tick(0)
    loads[1].wait()

    def mix(i):
        rows = chunk(i)
        total = jnp.zeros((CHUNK, model), F32)
        for level in range(layers):
            chosen = (jnp.full((1, 1), depth) >= layers - level).astype(F32)
            total = total + chosen * r.memory[level, rows].astype(F32)
        r.m[rows] = (total * inv_depth * width_mask).astype(BF16)

    each_chunk(mix)
    g_tick(1)
    loads[2].wait()
    r.out_sums[...] = jnp.zeros(r.out_sums.shape, F32)

    def grad_in(i):
        rows = chunk(i)
        masked = r.upstream[rows].astype(F32) * keep_of(i)
        r.out_sums[...] = r.out_sums[...] + fold(masked)
        r.e[rows] = masked.astype(BF16)

    each_chunk(grad_in)
    g_tick(2)

    def ticks(*numbers):
        return [functools.partial(g_tick, i) for i in numbers]

    others = n - 1
    assert n == 4
    table = {
        (0, 1): ticks(3),
        (1, 0): ticks(4) + [functools.partial(bias.step, 0)],
        (1, 1): ticks(5),
        (2, 0): [functools.partial(bias.step, 1)],
        (2, 1): ticks(6),
        (3, 0): [functools.partial(bias.step, 2)],
        (3, 1): ticks(7),
    }
    each(n, lambda k: attend(k, table, 0, causal))

    def after_self(i):
        rows = chunk(i)
        h = x[rows].astype(F32) + acc[rows] * keep_of(i)
        r.h1[rows] = h
        r.a2[rows] = norm(h, 1)
        acc[rows] = zeros

    each_chunk(after_self)
    table2 = {(0, 0): ticks(8), (0, 1): ticks(9), (1, 1): ticks(10), (2, 1): ticks(11), (3, 1): ticks(12)}
    each(n, lambda k: attend(k, table2, 1, crossing))

    def after_cross(i):
        rows = chunk(i)
        h = r.h1[rows] + acc[rows] * keep_of(i)
        r.h2[rows] = h
        r.a3[rows] = norm(h, 2)
        acc[rows] = zeros

    each_chunk(after_cross)
    r.a3t[...] = r.a3[...].T

    reduce = Reduce(
        place, weights, r.half, r.plane, r.line, r.extra, r.total, r.reduce_sems
    )
    plan = {}

    def add(tick, order, step, *args):
        plan.setdefault(tick, []).append((order, len(plan.get(tick, ())), functools.partial(step, *args)))

    def r_tick(tick):
        for _, _, step in sorted(plan.get(tick, ()), key=lambda entry: entry[:2]):
            step()

    def store(g):
        return pltpu.make_async_copy(r.total[g], r.blocks[g], local_sem.at[10 + g])

    times = {
        3: ([(1, 2, 6, 10), (3, 4, 8, 11), (5, 6, 9, 13), (7, 9, 11, 15)], (17, 19, 21, 23)),
        2: ([(1, 3, 6, 9), (3, 6, 8, 11), (5, 8, 10, 13), (7, 9, 12, 16)], (18, 20, 22, 24)),
        1: ([(10, 11, 14, 16), (12, 14, 16, 18), (14, 15, 19, 21), (16, 17, 19, 21)], (23, 25, 27, 29)),
        0: ([(19, 20, 22, 24), (21, 22, 24, 25), (23, 24, 25, 26), (25, 26, 27, 28)], (28, 29, 30, 31)),
    }
    for late, g in enumerate((3, 2, 1, 0)):
        for k, stages in enumerate(times[g][0]):
            j = block(k) if g > 1 else block_last(k)
            for stage, tick in enumerate(stages):
                add(tick, stage, reduce.step, g, j, stage)
        for stage, tick in enumerate(times[g][1]):
            if stage == 0:
                add(tick, 20 - late, reduce.settle, g)
            else:
                add(tick, 30 + stage - late, reduce.share, g, stage)
        add(times[g][1][-1], 50, lambda g=g: store(g).start())

    def reduce_ticks(*numbers):
        return [functools.partial(r_tick, i) for i in numbers]

    def at_end(k, numbers):
        for kk, number in enumerate(numbers):

            @pl.when(k == kk)
            def _():
                r_tick(number)

    table3 = {(0, 0): ticks(13), (0, 1): ticks(14), (1, 1): reduce_ticks(2), (2, 1): reduce_ticks(4), (3, 1): reduce_ticks(6)}

    def feed_step(k):
        feed(k, table3)
        at_end(k, [2 * i + 1 for i in range(n)])

    each(n, feed_step)
    r_tick(8)
    out_copy = pltpu.make_async_copy(acc, r.layer_out, local_sem.at[14])

    def after_feed(i):
        rows = chunk(i)
        keep = keep_of(i)
        acc[rows] = r.h2[rows] + (acc[rows] + r.bias_out[...].reshape(1, model)) * keep
        down = r.upstream[rows].astype(F32) + norm_backward(r.h2[rows], 2, da[rows])
        dh[rows] = down
        r.e[rows] = (down * keep).astype(BF16)
        da[rows] = zeros
        r.dm[rows] = zeros

    each_chunk(after_feed)
    out_copy.start()
    table4 = {(k, 1): reduce_ticks(9 + 2 * k) for k in range(n)}

    def cross_step(k):
        attend_backward(k, table4, 1, r.a2, r.m)
        at_end(k, [10 + 2 * i for i in range(n)])

    each(n, cross_step)
    memory_copy = pltpu.make_async_copy(r.dm, r.memory_out, local_sem.at[15])
    memory_copy.start()

    def before_cross(i):
        rows = chunk(i)
        down = dh[rows] + norm_backward(r.h1[rows], 1, da[rows])
        dh[rows] = down
        r.e[rows] = (down * keep_of(i)).astype(BF16)
        da[rows] = zeros

    each_chunk(before_cross)
    r_tick(17)
    table5 = {(k, 1): reduce_ticks(18 + 2 * k) for k in range(n)}

    def self_step(k):
        attend_backward(k, table5, 0, r.a1, r.a1)
        at_end(k, [19 + 2 * i for i in range(n)])

    each(n, self_step)

    def before_self(i):
        rows = chunk(i)
        dh[rows] = dh[rows] + norm_backward(x[rows].astype(F32), 0, da[rows])

    each_chunk(before_self)
    grad_copy = pltpu.make_async_copy(dh, r.input_grad, local_sem.at[16])
    grad_copy.start()

    small = SumSmall(place, r.slots, r.small_sems)

    def small_start():
        own = r.slots.at[0]
        own[...] = jnp.zeros(own.shape, F32)
        for i in range(6):
            own[i:i + 1, :model] = jnp.sum(r.norm_sums[i], axis=0, keepdims=True)
        own[6:7, :model] = jnp.sum(r.out_sums[...], axis=0, keepdims=True)
        tokens = lengths[place.tp * sentences]
        for b in range(1, sentences):
            tokens = tokens + lengths[place.tp * sentences + b]
        own[7:8] = jnp.full((1, own.shape[1]), tokens.astype(F32))
        for i in range(n):
            own[8 + i:9 + i] = jnp.sum(r.bias_sums[i], axis=0, keepdims=True)
        small.start()

    add(26, 5, small_start)
    for stage in range(2):
        add(27 + stage, 5, small.exchange, stage)
    final = max(plan)
    for tick in range(26, final + 1):
        r_tick(tick)
    r.small_out[...] = small.total()
    bias.finish()
    for copy in (out_copy, memory_copy, grad_copy):
        copy.wait()
    for g in range(4):
        reduce.finish(g)
        store(g).wait()
    small.finish()


def call(kernel, name, ins, outs, scratch, spaces, **options):
    trees = (ins, outs, scratch)
    structure = jax.tree_util.tree_structure(trees)

    def body(*refs):
        groups = jax.tree_util.tree_unflatten(structure, refs)
        kernel(types.SimpleNamespace(**groups[0], **groups[1], **groups[2]))

    def specs(group):
        return [
            pl.BlockSpec(memory_space=spaces.get(key, pltpu.VMEM))
            for key in sorted(group) for _ in jax.tree_util.tree_leaves(group[key])
        ]

    leaves = jax.tree_util.tree_leaves
    values = pl.pallas_call(
        body,
        out_shape=leaves(outs),
        in_specs=specs(ins),
        out_specs=specs(outs),
        scratch_shapes=leaves(scratch),
        compiler_params=pltpu.CompilerParams(**options),
        name=name,
    )(*leaves(ins))
    return types.SimpleNamespace(**jax.tree_util.tree_unflatten(jax.tree_util.tree_structure(outs), values))


def run_layer(ins):
    n, extra = lax.axis_size("tp"), lax.axis_size("dp") // 2
    owned, model = ins["x_in"].shape
    memory, shards = ins["memory_in"], ins["shards"]
    local, units = shards[1].shape[0], ins["bias_in"].shape[0]
    small = (16, units)
    assert n <= 8 and units >= model and memory.shape[0] >= 3
    shapes = [(n, 4 * local, model)] * 2 + [(n,) + shards[5].shape, (n,) + shards[6].shape]
    small_slots = SumSmall.slots(n, extra)

    def vmem(*shape):
        return pltpu.VMEM(shape, BF16)

    def wide(*shape):
        return pltpu.VMEM(shape, F32)

    def eighths(*lead, parts=1):
        return [vmem(*lead, rows * parts // 8, columns) for _, rows, columns in shapes]

    dma = pltpu.SemaphoreType.DMA
    scratch = dict(
        w=[vmem(*shape) for shape in shapes],
        bias=wide(n, 8, units),
        x=vmem(owned, model),
        memory=vmem(*memory.shape),
        upstream=vmem(owned, model),
        a1=vmem(owned, model),
        m=vmem(owned, model),
        h1=wide(owned, model),
        h2=wide(owned, model),
        acc=wide(owned, model),
        da=wide(owned, model),
        t=[vmem(n, 3 * local, owned)] * 2,
        c=[vmem(n, local, owned)] * 2,
        p=[vmem(n, owned // LEN * (local // HD), LEN, LEN)] * 2,
        dt=vmem(3 * local, owned),
        dc=vmem(local, owned),
        a3t=vmem(model, owned),
        scores=wide(owned // LEN * (local // HD), LEN, LEN),
        ds=vmem(owned // LEN * (local // HD), LEN, LEN),
        before=wide(owned, units),
        down=wide(owned, units),
        hidden=vmem(owned, units),
        dhidden=vmem(owned, units),
        bias_sums=wide(n, 8, units),
        norm_sums=wide(6, 8, model),
        out_sums=wide(8, model),
        half=eighths(n, parts=4),
        plane=eighths(n, parts=3),
        line=eighths(n),
        extra=eighths(extra),
        total=eighths(parts=8),
        slots=wide(small_slots, *small),
        gather_sems=dma((Gather.KINDS, 4, n)),
        bias_sems=dma((3, n)),
        reduce_sems=dma((Reduce.KINDS, 4, max(n, extra))),
        small_sems=dma((2, small_slots)),
        local_sems=dma((17,)),
    )
    rows = jax.ShapeDtypeStruct((owned, model), F32)
    outs = dict(
        layer_out=rows, input_grad=rows, memory_out=rows, small_out=jax.ShapeDtypeStruct(small, F32),
        blocks=[jax.ShapeDtypeStruct(shape[1:], BF16) for shape in shapes],
    )
    smem, hbm = pltpu.SMEM, pl.ANY
    spaces = dict(
        lengths=smem, src_lengths=smem, configs=smem, x_in=hbm, memory_in=hbm, upstream_in=hbm, shards=hbm,
        layer_out=hbm, input_grad=hbm, memory_out=hbm, blocks=hbm,
    )
    return call(
        layer_kernel, "layer", ins, outs, scratch, spaces,
        collective_id=1, has_side_effects=True, vmem_limit_bytes=64 * 2**20,
    )


def finish_kernel(r):
    small, configs, sems = r.small, r.configs, r.sems
    model = r.gain_grad.shape[1]
    layers = r.memory_grad.shape[0]
    place = lax.axis_index("tp")
    local = r.grads[1].shape[0]
    parts = (
        (0, 0, 3 * local), (0, 3 * local, local),
        (1, 0, local), (1, local, 2 * local), (1, 3 * local, local),
        (2, 0, r.block[2].shape[0]), (3, 0, r.block[3].shape[0]),
    )
    loads = [pltpu.make_async_copy(r.blocks[g], r.block[g], sems.at[g]) for g in range(4)]
    rows = [
        pltpu.make_async_copy(source, target, sems.at[4 + i])
        for i, (source, target) in enumerate(((r.layer_in, r.layer), (r.grad_in, r.grad), (r.source_in, r.source)))
    ]
    outs = [pltpu.make_async_copy(r.layer, r.layer_out, sems.at[7]), pltpu.make_async_copy(r.grad, r.input_grad, sems.at[8])]
    for copy in rows + loads:
        copy.start()
    inverse = 1.0 / small[7:8, :1]
    r.gain_grad[...] = small[:3, :model] * inverse
    r.shift_grad[...] = small[3:6, :model] * inverse
    r.bias_out_grad[...] = (small[6:7, :model] * inverse).reshape(model)
    r.bias_in_grad[...] = (small[pl.ds(8 + place, 1)] * inverse).reshape(small.shape[1])
    width, depth = configs[0, 0], configs[0, 3]
    factor = (column(1, (1, model)) < width).astype(F32) / jnp.full((1, 1), depth.astype(F32))
    for i in range(2):
        rows[i].wait()
        outs[i].start()
    rows[2].wait()

    def spread(i):
        part = pl.ds(pl.multiple_of(i * 64, 64), 64)
        value = r.source[part] * factor
        for level in range(layers):
            chosen = (jnp.full((1, 1), depth) >= layers - level).astype(F32)
            r.memories[level, part] = value * chosen

    each(r.source.shape[0] // 64, spread)
    outs.append(pltpu.make_async_copy(r.memories, r.memory_grad, sems.at[9]))
    outs[2].start()
    for i, (g, start, count) in enumerate(parts):
        if start == 0:
            loads[g].wait()

        size = 80 if count % 80 == 0 else 96

        def scale(at):
            there = pl.ds(pl.multiple_of(start + at * size, 16), size)
            r.wide[g][there] = r.block[g][there].astype(F32) * inverse

        each(count // size, scale)
        outs.append(pltpu.make_async_copy(r.wide[g].at[pl.ds(start, count)], r.grads[i], sems.at[10 + i]))
        outs[-1].start()
    for copy in outs:
        copy.wait()


def run_finish(ins, layers):
    blocks, small = ins["blocks"], ins["small"]
    rows = ins["layer_in"].shape
    local, units = blocks[0].shape[0] // 4, small.shape[1]

    def shape(*dims):
        return jax.ShapeDtypeStruct(dims, F32)

    counts = (3 * local, local, local, 2 * local, local)
    outs = dict(
        layer_out=shape(*rows), input_grad=shape(*rows), memory_grad=shape(layers, *rows),
        gain_grad=shape(3, rows[1]), shift_grad=shape(3, rows[1]), bias_in_grad=shape(units), bias_out_grad=shape(rows[1]),
        grads=[shape(count, rows[1]) for count in counts] + [shape(*blocks[2].shape), shape(*blocks[3].shape)],
    )
    scratch = dict(
        layer=pltpu.VMEM(rows, F32), grad=pltpu.VMEM(rows, F32), source=pltpu.VMEM(rows, F32),
        memories=pltpu.VMEM((layers,) + rows, F32),
        block=[pltpu.VMEM(block.shape, BF16) for block in blocks],
        wide=[pltpu.VMEM(block.shape, F32) for block in blocks],
        sems=pltpu.SemaphoreType.DMA((17,)),
    )
    hbm = pl.ANY
    spaces = dict(
        configs=pltpu.SMEM, layer_in=hbm, grad_in=hbm, source_in=hbm, blocks=hbm,
        layer_out=hbm, input_grad=hbm, memory_grad=hbm, grads=hbm,
    )
    return call(finish_kernel, "finish", ins, outs, scratch, spaces, vmem_limit_bytes=60 * 2**20)


def per_device(
    inputs, memory, out_grad, lengths, src_lengths, configs, norm_gain, norm_bias,
    self_qkv, self_out, cross_q, cross_kv, cross_out, ffn_in, ffn_in_bias, ffn_out, ffn_out_bias,
):
    model = inputs.shape[1]
    layers = memory.shape[0]
    local = self_out.shape[0]
    done = run_layer(dict(
        lengths=lengths, src_lengths=src_lengths, configs=configs, gains=norm_gain, shifts=norm_bias,
        bias_in=ffn_in_bias, bias_out=ffn_out_bias, x_in=inputs, memory_in=memory, upstream_in=out_grad,
        shards=[
            self_qkv.transpose(1, 2, 0).reshape(3 * local, model), self_out, cross_q.T,
            cross_kv.transpose(1, 2, 0).reshape(2 * local, model), cross_out, ffn_in, ffn_out,
        ],
    ))
    out = run_finish(dict(
        configs=configs, small=done.small_out, layer_in=done.layer_out, grad_in=done.input_grad,
        source_in=done.memory_out, blocks=done.blocks,
    ), layers)
    grads = out.grads
    return (
        out.layer_out,
        out.input_grad,
        out.memory_grad,
        out.gain_grad,
        out.shift_grad,
        grads[0].reshape(3, local, model).transpose(2, 0, 1),
        grads[1],
        grads[2].T,
        grads[3].reshape(2, local, model).transpose(2, 0, 1),
        grads[4],
        grads[5],
        out.bias_in_grad,
        grads[6],
        out.bias_out_grad,
    )


def solution(mesh):
    rows = P(("grp", "dp", "tp"), None)
    stack = P(None, ("grp", "dp", "tp"), None)
    weights = (
        P(None, None, "tp"), P("tp", None), P(None, "tp"), P(None, None, "tp"), P("tp", None),
        P(None, "tp"), P("tp"), P("tp", None), P(),
    )
    return jax.shard_map(
        per_device,
        mesh=mesh,
        in_specs=(rows, stack, rows, P(("grp", "dp")), P(("grp", "dp")), P("grp", None), P(), P()) + weights,
        out_specs=(rows, rows, stack, P(), P()) + weights,
        check_vma=False,
    )
```

```python
import functools
import types

import jax
import jax.numpy as jnp
from jax import lax
from jax.experimental import pallas as pl
from jax.experimental.pallas import tpu as pltpu
from jax.sharding import PartitionSpec as P

HD = 80
LEN = 256
EPSILON = 1e-05
NEGATIVE = -1e30
SCALE = HD ** (-0.5)
LOG2E = 1.4426950408889634
F32 = jnp.float32
BF16 = jnp.bfloat16


MESH = pl.DeviceIdType.MESH


class Place:
    def __init__(self):
        self.tps = lax.axis_size("tp")
        self.extra = lax.axis_size("dp") // 2
        assert lax.axis_size("grp") == 4 and lax.axis_size("dp") % 2 == 0
        grp, dp, tp = (lax.axis_index(name) for name in ("grp", "dp", "tp"))
        core, low, high = dp % 2, grp % 2, grp // 2
        flip_low, flip_high = grp + 1 - 2 * low, grp + 2 - 4 * high
        self.grp, self.dp, self.tp, self.core = grp, dp, tp, core
        self.first_bit = (1 - core) * low + core * high
        self.second_bit = (1 - core) * high + core * low
        self.first = ((1 - core) * flip_low + core * flip_high, dp, tp)
        self.second = ((1 - core) * flip_high + core * flip_low, dp, tp)
        self.across = (3 - grp, dp, tp)
        self.sibling = (grp, dp + 1 - 2 * core, tp)
        self.above = (grp, dp, tp + 1)
        self.below = (grp, dp, tp - 1)
        self.has_above = tp < self.tps - 1
        self.has_below = tp > 0

    def copy_of(self, step):
        return (self.grp, ((self.dp // 2 + step) % self.extra) * 2 + self.core, self.tp)

    def nth_block(self, k):
        size = self.tps
        upper = (2 * self.tp) // size
        lead = (1 - upper) * self.tp + upper * (size - 1 - self.tp)
        spot = k + (k + size - lead) // size
        return (1 - upper) * spot + upper * (size - 1 - spot)

    def along(self, tp):
        return (self.grp, self.dp, tp)

    def barrier(self):
        sem = pltpu.get_barrier_semaphore()
        partners = [self.first, self.second, self.across, self.sibling]
        partners += [self.along((self.tp + step) % self.tps) for step in range(1, self.tps)]
        partners += [self.copy_of(step) for step in range(1, self.extra)]
        for device in partners:
            pl.semaphore_signal(sem, inc=1, device_id=device, device_id_type=MESH)
        pl.semaphore_wait(sem, len(partners))


def push(src, dst, send_sem, recv_sem, device):
    return pltpu.make_async_remote_copy(
        src_ref=src, dst_ref=dst, send_sem=send_sem, recv_sem=recv_sem, device_id=device, device_id_type=MESH
    )


def rows_of(ref, lead, start, count):
    return ref.at[lead, pl.ds(pl.multiple_of(start, 16), count)]


def add_units(total, term, unit):
    def step(i, carry):
        rows = pl.ds(pl.multiple_of(i * unit, 16), unit)
        total[rows] = total[rows] + term[rows]
        return carry

    lax.fori_loop(0, total.shape[0] // unit, step, 0)


class Spread:
    KINDS = 6

    def __init__(self, place, view, unit, sems):
        self.place, self.view, self.unit, self.sems = place, view, unit, sems
        f, s, c = place.first_bit, place.second_bit, place.core
        self.table = (
            (place.second, c * 4 + f * 2 + s, c * 4 + f * 2 + 1 - s, 1),
            (place.first, c * 4 + f * 2, c * 4 + 2 - f * 2, 2),
            (place.sibling, c * 4, 4 - c * 4, 4),
        )

    def region(self, start, count):
        return self.view(start * self.unit, count * self.unit)

    def own(self):
        return self.region(self.table[0][1], 1)

    def copy(self, n, lands=False):
        device, leaves, landing, count = self.table[n]
        part = self.region(landing if lands else leaves, count)
        return push(part, part, self.sems(2 * n), self.sems(2 * n + 1), device)

    def step(self, stage):
        if stage > 0:
            self.copy(stage - 1, lands=True).wait_recv()
        if stage < 3:
            self.copy(stage).start()

    def finish(self):
        for n in range(3):
            self.copy(n).wait_send()


class Gather:
    KINDS = Spread.KINDS + 3

    def __init__(self, place, buffers, sems):
        self.place, self.buffers, self.sems = place, buffers, sems
        self.unit = [ref.shape[1] // 8 for ref in buffers]
        self.others = place.tps - 1

    def spread(self, g, j):
        return Spread(
            self.place,
            lambda start, count: rows_of(self.buffers[g], j, start, count),
            self.unit[g],
            lambda kind: self.sems.at[kind, g, j],
        )

    def relays(self, g, j):
        p = self.place
        part = self.spread(g, j).own()
        sem = lambda n: self.sems.at[Spread.KINDS + n, g, j]
        return (
            (jnp.logical_and(j <= p.tp, p.has_above), push(part, part, sem(0), sem(2), p.above)),
            (jnp.logical_and(j >= p.tp, p.has_below), push(part, part, sem(1), sem(2), p.below)),
        )

    def start(self, g):
        for needed, copy in self.relays(g, self.place.tp):
            pl.when(needed)(copy.start)

    def step(self, g, k, stage):
        j = self.place.nth_block(k)
        if stage == 0:
            relays = self.relays(g, j)
            relays[0][1].wait_recv()
            for needed, copy in relays:
                pl.when(needed)(copy.start)
        self.spread(g, j).step(stage)

    def drain(self, g, j):
        for needed, copy in self.relays(g, j):
            pl.when(needed)(copy.wait_send)

        @pl.when(j != self.place.tp)
        def _():
            self.spread(g, j).finish()


class Line:
    def __init__(self, place, buffer, sems):
        self.place, self.buffer, self.sems = place, buffer, sems

    def relays(self, j):
        p = self.place
        part = self.buffer.at[j]
        return (
            (jnp.logical_and(j <= p.tp, p.has_above), push(part, part, self.sems.at[0, j], self.sems.at[2, j], p.above)),
            (jnp.logical_and(j >= p.tp, p.has_below), push(part, part, self.sems.at[1, j], self.sems.at[2, j], p.below)),
        )

    def start(self):
        for needed, copy in self.relays(self.place.tp):
            pl.when(needed)(copy.start)

    def step(self, k):
        j = self.place.nth_block(k)
        relays = self.relays(j)
        relays[0][1].wait_recv()
        for needed, copy in relays:
            pl.when(needed)(copy.start)

    def finish(self):
        for j in range(self.place.tps):
            for needed, copy in self.relays(j):
                pl.when(needed)(copy.wait_send)


class Reduce:
    KINDS = 8 + Spread.KINDS + 2

    def __init__(self, place, grads, halves, planes, lines, extras, totals, sems):
        self.place, self.grads, self.totals, self.sems = place, grads, totals, sems
        self.halves, self.planes, self.lines, self.extras = halves, planes, lines, extras
        self.unit = [ref.shape[0] // 8 for ref in totals]

    def sem(self, kind, g, j):
        return self.sems.at[kind, g, j]

    def rows(self, g, j, half, unit, count=1):
        size = self.unit[g]
        return rows_of(self.grads[g], j, (half * 4 + unit) * size, count * size)

    def move(self, g, j, stage):
        p, size = self.place, self.unit[g]
        if stage == 0:
            part, landing, device = self.rows(g, j, 1 - p.core, 0, 4), self.halves[g].at[j], p.sibling
        elif stage == 1:
            part, device = self.rows(g, j, p.core, 2 - p.first_bit * 2, 2), p.first
            landing = self.planes[g].at[j, pl.ds(0, 2 * size)]
        else:
            part, device = self.rows(g, j, p.core, p.first_bit * 2 + 1 - p.second_bit), p.second
            landing = self.planes[g].at[j, pl.ds(2 * size, size)]
        return push(part, landing, self.sem(2 * stage, g, j), self.sem(2 * stage + 1, g, j), device)

    def kept(self, g, j, stage):
        p, size = self.place, self.unit[g]
        if stage == 0:
            return self.rows(g, j, p.core, 0, 4), self.halves[g].at[j]
        if stage == 1:
            return self.rows(g, j, p.core, p.first_bit * 2, 2), self.planes[g].at[j, pl.ds(0, 2 * size)]
        return self.piece(g, j), self.planes[g].at[j, pl.ds(2 * size, size)]

    def piece(self, g, j):
        p = self.place
        return self.rows(g, j, p.core, p.first_bit * 2 + p.second_bit)

    def along(self, g, j):
        p = self.place
        return push(self.piece(g, j), self.lines[g].at[p.tp], self.sem(6, g, j), self.sem(7, g, p.tp), p.along(j))

    def from_place(self, g, j):
        p = self.place
        return push(self.piece(g, j), self.lines[g].at[j], self.sem(6, g, j), self.sem(7, g, j), p.along(j))

    def step(self, g, j, stage):
        if stage > 0:
            self.move(g, j, stage - 1).wait_recv()
            add_units(*self.kept(g, j, stage - 1), self.unit[g])
        if stage < 3:
            self.move(g, j, stage).start()
        else:
            pl.when(j != self.place.tp)(self.along(g, j).start)

    def spread(self, g):
        return Spread(
            self.place,
            lambda start, count: self.totals[g].at[pl.ds(pl.multiple_of(start, 16), count)],
            self.unit[g],
            lambda kind: self.sems.at[8 + kind, g, 0],
        )

    def copies(self, g, step):
        p = self.place
        base = self.KINDS - 2
        return push(
            self.piece(g, p.tp), self.extras[g].at[step], self.sem(base, g, step), self.sem(base + 1, g, step), p.copy_of(step)
        )

    def settle(self, g):
        p = self.place
        piece = self.piece(g, p.tp)
        total = piece[...].astype(F32)
        for k in range(p.tps - 1):
            j = p.nth_block(k)
            self.from_place(g, j).wait_recv()
            total = total + self.lines[g][j].astype(F32)
        if p.extra > 1:
            piece[...] = total.astype(BF16)
            for step in range(1, p.extra):
                self.copies(g, step).start()
            for step in range(1, p.extra):
                self.copies(g, step).wait()
                total = total + self.extras[g][step].astype(F32)
        own = self.spread(g).own()
        own[...] = total.astype(BF16)
        self.spread(g).step(0)

    def share(self, g, stage):
        self.spread(g).step(stage)

    def clear(self, g):
        p = self.place
        for j in range(p.tps):
            for stage in range(3):
                self.move(g, j, stage).wait_send()
            pl.when(j != p.tp)(self.along(g, j).wait_send)


class SumSmall:
    @staticmethod
    def slots(tps, extra):
        return 8 + tps + extra

    def __init__(self, place, slots, sems):
        self.place, self.slots_ref, self.sems = place, slots, sems

    def move(self, source, target, device, kind):
        slots = self.slots_ref
        return push(slots.at[source], slots.at[target], self.sems.at[0, kind], self.sems.at[1, target], device)

    def in_plane(self):
        p = self.place
        return [self.move(2, 3 + i, device, 3 + i) for i, device in enumerate((p.second, p.first, p.across))]

    def copies(self):
        p = self.place
        return [self.move(6, 8 + p.tps + s, p.copy_of(s), 8 + p.tps + s) for s in range(1, p.extra)]

    def along(self, k, lands=False):
        p = self.place
        j = p.nth_block(k)
        return self.move(7, 8 + (j if lands else p.tp), p.along(j), 8 + j)

    def start(self):
        self.move(0, 1, self.place.sibling, 1).start()

    def exchange(self, stage):
        p, slots = self.place, self.slots_ref
        if stage == 0:
            self.move(0, 1, p.sibling, 1).wait_recv()
            slots[2] = slots[0] + slots[1]
            for copy in self.in_plane():
                copy.start()
        else:
            for copy in self.in_plane():
                copy.wait_recv()
            slots[6] = (slots[2] + slots[3]) + (slots[4] + slots[5])
            for copy in self.copies():
                copy.start()
            total = slots[6]
            for s, copy in enumerate(self.copies()):
                copy.wait_recv()
                total = total + slots[9 + p.tps + s]
            slots[7] = total
            for k in range(p.tps - 1):
                self.along(k).start()

    def total(self):
        p, slots = self.place, self.slots_ref
        value = slots[7]
        for k in range(p.tps - 1):
            self.along(k, lands=True).wait_recv()
            value = value + slots[8 + p.nth_block(k)]
        return value

    def finish(self):
        p = self.place
        self.move(0, 1, p.sibling, 1).wait_send()
        for copy in self.in_plane() + self.copies():
            copy.wait_send()
        for k in range(p.tps - 1):
            self.along(k).wait_send()


def dot_nn(left, right):
    return lax.dot_general(left, right, (((1,), (0,)), ((), ())), preferred_element_type=F32)


def dot_nt(left, right):
    return lax.dot_general(left, right, (((1,), (1,)), ((), ())), preferred_element_type=F32)


def dot_tn(left, right):
    return lax.dot_general(left, right, (((0,), (0,)), ((), ())), preferred_element_type=F32)


def column(axis, shape):
    return lax.broadcasted_iota(jnp.int32, shape, axis)


def each(count, step):

    def run(i, carry):
        step(i)
        return carry

    lax.fori_loop(0, count, run, 0)


CHUNK = 128
CUBE = 0.044715
ROOT = 0.7978845608028654


def layer_kernel(r):
    r.a2, r.a3, r.e = (r.memory.at[i] for i in range(3))
    columns = pl.ds(0, r.x.shape[1])
    r.dh, r.dm = r.before.at[:, columns], r.down.at[:, columns]
    place = Place()
    n = place.tps
    x, model = r.x, r.x.shape[1]
    owned = x.shape[0]
    sentences = owned // LEN
    local = r.c[0].shape[1]
    heads_here = local // HD
    units = r.hidden.shape[1]
    layers = r.memory.shape[0]
    weights = r.w
    lengths, sources, configs = r.lengths, r.src_lengths, r.configs
    width, heads, hidden_units, depth = (configs[0, i] for i in range(4))
    inv_width = 1.0 / jnp.full((1, 1), width.astype(F32))
    inv_depth = 1.0 / jnp.full((1, 1), depth.astype(F32))
    width_mask = (column(1, (1, model)) < width).astype(F32)

    local_sem = r.local_sems
    spots = (
        (0, 0, 3 * local), (0, 3 * local, local),
        (1, 0, local), (1, local, 2 * local), (1, 3 * local, local),
        (2, 0, weights[2].shape[1]), (3, 0, weights[3].shape[1]),
    )
    fills = [
        (g, pltpu.make_async_copy(r.shards[i], weights[g].at[place.tp, pl.ds(start, size)], local_sem.at[i]))
        for i, (g, start, size) in enumerate(spots)
    ]
    loads = [
        pltpu.make_async_copy(source, target, local_sem.at[7 + i])
        for i, (source, target) in enumerate(((r.x_in, r.x), (r.memory_in, r.memory), (r.upstream_in, r.upstream)))
    ]
    for _, copy in fills[:2]:
        copy.start()
    loads[0].start()
    for _, copy in fills[2:]:
        copy.start()
    loads[1].start()
    loads[2].start()
    r.bias[place.tp] = jnp.broadcast_to(r.bias_in[...].reshape(1, units), r.bias.shape[1:])
    place.barrier()

    gather = Gather(place, weights, r.gather_sems)
    bias = Line(place, r.bias, r.bias_sems)
    for g in range(4):
        for group, copy in fills:
            if group == g:
                copy.wait()
        gather.start(g)
        if g == 0:
            bias.start()
    order = [(g, k) for g in (0, 1) for k in range(n - 1)] + [(g, k) for k in range(n - 1) for g in (2, 3)]

    def g_tick(tick):
        for stage in range(4):
            if 0 <= tick - stage < len(order):
                gather.step(*order[tick - stage], stage)

    def block(k):
        later = (k + n - 1) // n
        return (1 - later) * place.tp + later * place.nth_block(k - 1)

    def block_last(k):
        own = k // (n - 1)
        return own * place.tp + (1 - own) * place.nth_block(k)

    def hooks(table, k, b):
        for (kk, bb), steps in table.items():

            @pl.when(jnp.logical_and(k == kk, b == bb))
            def _():
                for step in steps:
                    step()

    def chunk(i):
        return pl.ds(pl.multiple_of(i * CHUNK, CHUNK), CHUNK)

    def keep_of(i):
        per = LEN // CHUNK
        spot = column(0, (CHUNK, 1)) + (i % per) * CHUNK
        return (spot < lengths[place.tp * sentences + i // per]).astype(F32) * width_mask

    def norm_parts(rows):
        mean = jnp.sum(rows * width_mask, axis=-1, keepdims=True) * inv_width
        centred = (rows - mean) * width_mask
        spread = jnp.sum(centred * centred, axis=-1, keepdims=True) * inv_width
        rstd = lax.rsqrt(spread + EPSILON)
        return centred * rstd, rstd

    def norm(rows, which):
        hat, _ = norm_parts(rows)
        return ((hat * r.gains[which:which + 1] + r.shifts[which:which + 1]) * width_mask).astype(BF16)

    def fold(values):
        return jnp.sum(values.reshape(values.shape[0] // 8, 8, values.shape[1]), axis=0)

    def norm_backward(rows, which, upstream):
        hat, rstd = norm_parts(rows)
        upstream = upstream * width_mask
        sums = r.norm_sums
        sums[which] = sums[which] + fold(upstream * hat)
        sums[3 + which] = sums[3 + which] + fold(upstream)
        scaled = upstream * r.gains[which:which + 1]
        first = jnp.sum(scaled, axis=-1, keepdims=True) * inv_width
        second = jnp.sum(scaled * hat, axis=-1, keepdims=True) * inv_width
        return (rstd * (scaled - first - hat * second)) * width_mask

    chunks = owned // CHUNK

    def each_chunk(step):
        each(chunks, step)

    acc, da, dh = r.acc, r.da, r.dh
    zeros = jnp.zeros((CHUNK, model), F32)
    r.norm_sums[...] = jnp.zeros(r.norm_sums.shape, F32)
    r.bias_sums[...] = jnp.zeros(r.bias_sums.shape, F32)

    def sentence(b):
        return pl.ds(pl.multiple_of(b * LEN, LEN), LEN)

    def head_keep(j, h):
        return jnp.where(j * heads_here + h < heads, 1.0, 0.0).astype(F32)

    def causal(b, start, size):
        return column(0, (size, 128)) <= column(1, (size, 128)) + start

    def crossing(b, start, size):
        return column(0, (size, 1)) < sources[place.tp * sentences + b]

    def reach(g, start):
        return start + 128 if g == 0 else LEN

    def bands(h):
        return [pl.ds(i * local + h * HD, HD) for i in range(3)]

    def lanes(b):
        return pl.ds(b * LEN, LEN)

    pairs = [(b, h) for b in range(sentences) for h in range(heads_here)]

    quarters = [(i, b, h, start) for i, (b, h) in enumerate(pairs) for start in range(0, LEN, 128)]

    def attend(k, table, g, allowed):
        w, t, c, p = weights[g], r.t[g], r.c[g], r.p[g]
        j = block(k)
        hooks(table, k, 0)
        if g == 0:
            t[j] = dot_nt(w[j, :3 * local], r.a1[...]).astype(BF16)
        else:
            t[j, :local] = dot_nt(w[j, :local], r.a2[...]).astype(BF16)
            t[j, local:] = dot_nt(w[j, local:3 * local], r.m[...]).astype(BF16)
        heads_of = [[t[j, band, lanes(b)] for band in bands(h)] for b, h in pairs]
        for i, (query, keys, _) in enumerate(heads_of):
            r.scores[i] = dot_tn(keys, query)
        for i, b, h, start in quarters:
            part, size = pl.ds(start, 128), reach(g, start)
            score = jnp.where(allowed(b, start, size), r.scores[i, :size, part], NEGATIVE)
            raised = jnp.exp2((score - jnp.max(score, axis=0, keepdims=True)) * (SCALE * LOG2E))
            p[j, i, :size, part] = (raised * (1.0 / jnp.sum(raised, axis=0, keepdims=True))).astype(BF16)
            if size < LEN:
                p[j, i, size:, part] = jnp.zeros((LEN - size, 128), BF16)
        for i, (b, h) in enumerate(pairs):
            c[j, pl.ds(h * HD, HD), lanes(b)] = (dot_nn(heads_of[i][2], p[j, i]) * head_keep(j, h)).astype(BF16)
        hooks(table, k, 1)
        acc[...] = acc[...] + dot_tn(c[j], w[j, 3 * local:])

    def attend_backward(k, table, g, query_rows, key_rows):
        w, t, c, p = weights[g], r.t[g], r.c[g], r.p[g]
        j = block_last(k)
        e, dc = r.e, r.dc
        dt, goal = (t.at[j], weights[3].at[j]) if g == 0 else (r.dt, w.at[j])
        dc_all = dot_nt(w[j, 3 * local:], e[...])
        for h in range(heads_here):
            dc[h * HD:(h + 1) * HD] = (dc_all[h * HD:(h + 1) * HD] * head_keep(j, h)).astype(BF16)
        heads_of = [[t[j, band, lanes(b)] for band in bands(h)] for b, h in pairs]
        dc_of = [dc[h * HD:(h + 1) * HD, lanes(b)] for b, h in pairs]
        for i, (_, _, values) in enumerate(heads_of):
            r.scores[i] = dot_tn(values, dc_of[i])
        for i, b, h, start in quarters:
            part, size = pl.ds(start, 128), reach(g, start)
            dp, wide = r.scores[i, :size, part], p[j, i, :size, part].astype(F32)
            r.ds[i, :size, part] = (wide * (dp - jnp.sum(dp * wide, axis=0, keepdims=True))).astype(BF16)
            if size < LEN:
                r.ds[i, size:, part] = jnp.zeros((LEN - size, 128), BF16)
        for i, (b, h) in enumerate(pairs):
            (query, keys, _), (dq, dk, dv) = heads_of[i], bands(h)
            dt[dv, lanes(b)] = dot_nt(dc_of[i], p[j, i]).astype(BF16)
            dt[dq, lanes(b)] = (dot_nn(keys, r.ds[i]) * SCALE).astype(BF16)
            dt[dk, lanes(b)] = (dot_nt(query, r.ds[i]) * SCALE).astype(BF16)
        hooks(table, k, 1)
        if g == 0:
            goal[:3 * local] = dot_nn(dt[...], query_rows[...]).astype(BF16)
        else:
            gather.drain(g, j)
            da[...] = da[...] + dot_tn(dt[:local], w[j, :local])
            r.dm[...] = r.dm[...] + dot_tn(dt[local:], w[j, local:3 * local])
            goal[:local] = dot_nn(dt[:local], query_rows[...]).astype(BF16)
            goal[local:3 * local] = dot_nn(dt[local:], key_rows[...]).astype(BF16)
        goal[3 * local:4 * local] = dot_nn(c[j], e[...]).astype(BF16)

    def feed(k, table):
        j = block(k)
        w_up, w_down = weights[2], weights[3]
        hooks(table, k, 0)
        r.before[...] = dot_nn(r.a3[...], w_up[j]) + r.bias[j, 0:1]
        r.down[...] = dot_nt(r.e[...], w_down[j])
        step_lanes = units // 2

        def bend(i):
            for start in range(0, units, step_lanes):
                part = pl.ds(start, step_lanes)
                unit = column(1, (1, step_lanes)) + (j * units + start)
                kept = jnp.where(unit < hidden_units, 0.5, 0.0)
                sums = r.bias_sums[j, :, part]
                for line in range(4):
                    rows = pl.ds(pl.multiple_of(i * 64, 64) + line * 16, 16)
                    before = r.before[rows, part]
                    square = before * before
                    bent = jnp.tanh(before * (ROOT + ROOT * CUBE * square))
                    half = kept + kept * bent
                    through = before * half
                    r.hidden[rows, part] = through.astype(BF16)
                    slope = half + (through - through * bent) * (ROOT + 3.0 * CUBE * ROOT * square)
                    du = (r.down[rows, part] * slope).astype(BF16)
                    r.dhidden[rows, part] = du
                    sums = sums + fold(du.astype(F32))
                r.bias_sums[j, :, part] = sums

        each(owned // 64, bend)
        hooks(table, k, 1)
        acc[...] = acc[...] + dot_nn(r.hidden[...], w_down[j])
        da[...] = da[...] + dot_nt(r.dhidden[...], w_up[j])
        gather.drain(2, j)
        gather.drain(3, j)
        w_down[j] = dot_tn(r.hidden[...], r.e[...]).astype(BF16)
        w_up[j] = dot_nn(r.a3t[...], r.dhidden[...]).astype(BF16)

    loads[0].wait()

    def begin(i):
        rows = chunk(i)
        r.a1[rows] = norm(x[rows].astype(F32), 0)
        acc[rows] = zeros
        da[rows] = zeros

    each_chunk(begin)
    g_tick(0)
    loads[1].wait()

    def mix(i):
        rows = chunk(i)
        total = jnp.zeros((CHUNK, model), F32)
        for level in range(layers):
            chosen = (jnp.full((1, 1), depth) >= layers - level).astype(F32)
            total = total + chosen * r.memory[level, rows].astype(F32)
        r.m[rows] = (total * inv_depth * width_mask).astype(BF16)

    each_chunk(mix)
    g_tick(1)
    loads[2].wait()
    r.out_sums[...] = jnp.zeros(r.out_sums.shape, F32)

    def grad_in(i):
        rows = chunk(i)
        masked = r.upstream[rows].astype(F32) * keep_of(i)
        r.out_sums[...] = r.out_sums[...] + fold(masked)
        r.e[rows] = masked.astype(BF16)

    each_chunk(grad_in)
    g_tick(2)

    def ticks(*numbers):
        return [functools.partial(g_tick, i) for i in numbers]

    others = n - 1
    assert n == 4
    table = {
        (0, 1): ticks(3),
        (1, 0): ticks(4) + [functools.partial(bias.step, 0)],
        (1, 1): ticks(5),
        (2, 0): [functools.partial(bias.step, 1)],
        (2, 1): ticks(6),
        (3, 0): [functools.partial(bias.step, 2)],
        (3, 1): ticks(7),
    }
    each(n, lambda k: attend(k, table, 0, causal))

    def after_self(i):
        rows = chunk(i)
        h = x[rows].astype(F32) + acc[rows] * keep_of(i)
        r.h1[rows] = h
        r.a2[rows] = norm(h, 1)
        acc[rows] = zeros

    each_chunk(after_self)
    table2 = {(0, 0): ticks(8), (0, 1): ticks(9), (1, 1): ticks(10), (2, 1): ticks(11), (3, 1): ticks(12)}
    each(n, lambda k: attend(k, table2, 1, crossing))

    def after_cross(i):
        rows = chunk(i)
        h = r.h1[rows] + acc[rows] * keep_of(i)
        r.h2[rows] = h
        r.a3[rows] = norm(h, 2)
        acc[rows] = zeros

    each_chunk(after_cross)
    r.a3t[...] = r.a3[...].T

    reduce = Reduce(
        place, weights[3:] + weights[1:], r.half, r.plane, r.line, r.extra, r.total, r.reduce_sems
    )
    plan = {}

    def add(tick, order, step, *args):
        plan.setdefault(tick, []).append((order, len(plan.get(tick, ())), functools.partial(step, *args)))

    def r_tick(tick):
        for _, _, step in sorted(plan.get(tick, ()), key=lambda entry: entry[:2]):
            step()

    def store(g):
        return pltpu.make_async_copy(r.total[g], r.blocks[g], local_sem.at[10 + g])

    times = {
        3: ([(1, 2, 6, 10), (3, 4, 8, 11), (5, 6, 9, 13), (7, 9, 11, 15)], (17, 19, 21, 23)),
        2: ([(1, 3, 6, 9), (3, 6, 8, 11), (5, 8, 10, 13), (7, 9, 12, 16)], (18, 20, 22, 24)),
        1: ([(10, 11, 14, 16), (12, 14, 16, 18), (14, 15, 19, 21), (16, 17, 19, 21)], (23, 25, 27, 29)),
        0: ([(19, 20, 22, 24), (21, 22, 24, 25), (23, 24, 25, 26), (25, 26, 27, 28)], (28, 29, 30, 31)),
    }
    for late, g in enumerate((3, 2, 1, 0)):
        for k, stages in enumerate(times[g][0]):
            j = block(k) if g > 1 else block_last(k)
            for stage, tick in enumerate(stages):
                add(tick, stage, reduce.step, g, j, stage)
        for stage, tick in enumerate(times[g][1]):
            if stage == 0:
                add(tick, 20 - late, reduce.settle, g)
            else:
                add(tick, 30 + stage - late, reduce.share, g, stage)
        add(times[g][1][-1], 50, lambda g=g: store(g).start())

    def reduce_ticks(*numbers):
        return [functools.partial(r_tick, i) for i in numbers]

    def at_end(k, numbers):
        for kk, number in enumerate(numbers):

            @pl.when(k == kk)
            def _():
                r_tick(number)

    table3 = {(0, 0): ticks(13), (0, 1): ticks(14), (1, 1): reduce_ticks(2), (2, 1): reduce_ticks(4), (3, 1): reduce_ticks(6)}

    def feed_step(k):
        feed(k, table3)
        at_end(k, [2 * i + 1 for i in range(n)])

    each(n, feed_step)
    r_tick(8)
    out_copy = pltpu.make_async_copy(acc, r.layer_out, local_sem.at[14])

    def after_feed(i):
        rows = chunk(i)
        keep = keep_of(i)
        acc[rows] = r.h2[rows] + (acc[rows] + r.bias_out[...].reshape(1, model)) * keep
        down = r.upstream[rows].astype(F32) + norm_backward(r.h2[rows], 2, da[rows])
        dh[rows] = down
        r.e[rows] = (down * keep).astype(BF16)
        da[rows] = zeros
        r.dm[rows] = zeros

    each_chunk(after_feed)
    out_copy.start()
    table4 = {(k, 1): reduce_ticks(9 + 2 * k) for k in range(n)}

    def cross_step(k):
        attend_backward(k, table4, 1, r.a2, r.m)
        at_end(k, [10 + 2 * i for i in range(n)])

    each(n, cross_step)
    memory_copy = pltpu.make_async_copy(r.dm, r.memory_out, local_sem.at[15])
    memory_copy.start()

    def before_cross(i):
        rows = chunk(i)
        down = dh[rows] + norm_backward(r.h1[rows], 1, da[rows])
        dh[rows] = down
        r.e[rows] = (down * keep_of(i)).astype(BF16)
        da[rows] = zeros

    each_chunk(before_cross)
    r_tick(17)
    reduce.clear(3)
    table5 = {(k, 1): reduce_ticks(18 + 2 * k) for k in range(n)}

    def self_step(k):
        attend_backward(k, table5, 0, r.a1, r.a1)
        at_end(k, [19 + 2 * i for i in range(n)])

    each(n, self_step)

    for j in range(n):
        da[...] = da[...] + dot_tn(r.t[0][j], weights[0][j, :3 * local])
        if j > 0:
            r_tick(25 + j)

    def before_self(i):
        rows = chunk(i)
        dh[rows] = dh[rows] + norm_backward(x[rows].astype(F32), 0, da[rows])

    each_chunk(before_self)
    grad_copy = pltpu.make_async_copy(dh, r.input_grad, local_sem.at[16])
    grad_copy.start()

    small = SumSmall(place, r.slots, r.small_sems)

    def small_start():
        own = r.slots.at[0]
        own[...] = jnp.zeros(own.shape, F32)
        for i in range(6):
            own[i:i + 1, :model] = jnp.sum(r.norm_sums[i], axis=0, keepdims=True)
        own[6:7, :model] = jnp.sum(r.out_sums[...], axis=0, keepdims=True)
        tokens = lengths[place.tp * sentences]
        for b in range(1, sentences):
            tokens = tokens + lengths[place.tp * sentences + b]
        own[7:8] = jnp.full((1, own.shape[1]), tokens.astype(F32))
        for i in range(n):
            own[8 + i:9 + i] = jnp.sum(r.bias_sums[i], axis=0, keepdims=True)
        small.start()

    small_start()
    for stage in range(2):
        add(30 + stage, 5, small.exchange, stage)
    final = max(plan)
    for tick in range(25 + n, final + 1):
        r_tick(tick)
    r.small_out[...] = small.total()
    bias.finish()
    for copy in (out_copy, memory_copy, grad_copy):
        copy.wait()
    for g in range(4):
        if g < 3:
            reduce.clear(g)
        reduce.spread(g).finish()
        store(g).wait()
    for j in range(n):
        gather.drain(0, j)
    small.finish()


def call(kernel, name, ins, outs, scratch, spaces, **options):
    trees = (ins, outs, scratch)
    structure = jax.tree_util.tree_structure(trees)

    def body(*refs):
        groups = jax.tree_util.tree_unflatten(structure, refs)
        kernel(types.SimpleNamespace(**groups[0], **groups[1], **groups[2]))

    def specs(group):
        return [
            pl.BlockSpec(memory_space=spaces.get(key, pltpu.VMEM))
            for key in sorted(group) for _ in jax.tree_util.tree_leaves(group[key])
        ]

    leaves = jax.tree_util.tree_leaves
    values = pl.pallas_call(
        body,
        out_shape=leaves(outs),
        in_specs=specs(ins),
        out_specs=specs(outs),
        scratch_shapes=leaves(scratch),
        compiler_params=pltpu.CompilerParams(**options),
        name=name,
    )(*leaves(ins))
    return types.SimpleNamespace(**jax.tree_util.tree_unflatten(jax.tree_util.tree_structure(outs), values))


def run_layer(ins):
    n, extra = lax.axis_size("tp"), lax.axis_size("dp") // 2
    owned, model = ins["x_in"].shape
    memory, shards = ins["memory_in"], ins["shards"]
    local, units = shards[1].shape[0], ins["bias_in"].shape[0]
    small = (16, units)
    assert n <= 8 and units >= model and memory.shape[0] >= 3
    shapes = [(n, 4 * local, model)] * 2 + [(n,) + shards[5].shape, (n,) + shards[6].shape]
    small_slots = SumSmall.slots(n, extra)

    def vmem(*shape):
        return pltpu.VMEM(shape, BF16)

    def wide(*shape):
        return pltpu.VMEM(shape, F32)

    def eighths(*lead, parts=1):
        return [vmem(*lead, rows * parts // 8, columns) for _, rows, columns in shapes]

    dma = pltpu.SemaphoreType.DMA
    scratch = dict(
        w=[vmem(*shape) for shape in shapes],
        bias=wide(n, 8, units),
        x=vmem(owned, model),
        memory=vmem(*memory.shape),
        upstream=vmem(owned, model),
        a1=vmem(owned, model),
        m=vmem(owned, model),
        h1=wide(owned, model),
        h2=wide(owned, model),
        acc=wide(owned, model),
        da=wide(owned, model),
        t=[vmem(n, 3 * local, owned)] * 2,
        c=[vmem(n, local, owned)] * 2,
        p=[vmem(n, owned // LEN * (local // HD), LEN, LEN)] * 2,
        dt=vmem(3 * local, owned),
        dc=vmem(local, owned),
        a3t=vmem(model, owned),
        scores=wide(owned // LEN * (local // HD), LEN, LEN),
        ds=vmem(owned // LEN * (local // HD), LEN, LEN),
        before=wide(owned, units),
        down=wide(owned, units),
        hidden=vmem(owned, units),
        dhidden=vmem(owned, units),
        bias_sums=wide(n, 8, units),
        norm_sums=wide(6, 8, model),
        out_sums=wide(8, model),
        half=eighths(n, parts=4),
        plane=eighths(n, parts=3),
        line=eighths(n),
        extra=eighths(extra),
        total=eighths(parts=8),
        slots=wide(small_slots, *small),
        gather_sems=dma((Gather.KINDS, 4, n)),
        bias_sems=dma((3, n)),
        reduce_sems=dma((Reduce.KINDS, 4, max(n, extra))),
        small_sems=dma((2, small_slots)),
        local_sems=dma((17,)),
    )
    rows = jax.ShapeDtypeStruct((owned, model), F32)
    outs = dict(
        layer_out=rows, input_grad=rows, memory_out=rows, small_out=jax.ShapeDtypeStruct(small, F32),
        blocks=[jax.ShapeDtypeStruct(shape[1:], BF16) for shape in shapes],
    )
    smem, hbm = pltpu.SMEM, pl.ANY
    spaces = dict(
        lengths=smem, src_lengths=smem, configs=smem, x_in=hbm, memory_in=hbm, upstream_in=hbm, shards=hbm,
        layer_out=hbm, input_grad=hbm, memory_out=hbm, blocks=hbm,
    )
    return call(
        layer_kernel, "layer", ins, outs, scratch, spaces,
        collective_id=1, has_side_effects=True, vmem_limit_bytes=64 * 2**20,
    )


def finish_kernel(r):
    small, configs, sems = r.small, r.configs, r.sems
    model = r.gain_grad.shape[1]
    layers = r.memory_grad.shape[0]
    place = lax.axis_index("tp")
    local = r.grads[1].shape[0]
    parts = (
        (0, 0, 3 * local), (0, 3 * local, local),
        (1, 0, local), (1, local, 2 * local), (1, 3 * local, local),
        (2, 0, r.block[2].shape[0]), (3, 0, r.block[3].shape[0]),
    )
    loads = [pltpu.make_async_copy(r.blocks[g], r.block[g], sems.at[g]) for g in range(4)]
    rows = [
        pltpu.make_async_copy(source, target, sems.at[4 + i])
        for i, (source, target) in enumerate(((r.layer_in, r.layer), (r.grad_in, r.grad), (r.source_in, r.source)))
    ]
    outs = [pltpu.make_async_copy(r.layer, r.layer_out, sems.at[7]), pltpu.make_async_copy(r.grad, r.input_grad, sems.at[8])]
    for copy in rows + loads:
        copy.start()
    inverse = 1.0 / small[7:8, :1]
    r.gain_grad[...] = small[:3, :model] * inverse
    r.shift_grad[...] = small[3:6, :model] * inverse
    r.bias_out_grad[...] = (small[6:7, :model] * inverse).reshape(model)
    r.bias_in_grad[...] = (small[pl.ds(8 + place, 1)] * inverse).reshape(small.shape[1])
    width, depth = configs[0, 0], configs[0, 3]
    factor = (column(1, (1, model)) < width).astype(F32) / jnp.full((1, 1), depth.astype(F32))
    for i in range(2):
        rows[i].wait()
        outs[i].start()
    rows[2].wait()

    def spread(i):
        part = pl.ds(pl.multiple_of(i * 64, 64), 64)
        value = r.source[part] * factor
        for level in range(layers):
            chosen = (jnp.full((1, 1), depth) >= layers - level).astype(F32)
            r.memories[level, part] = value * chosen

    each(r.source.shape[0] // 64, spread)
    outs.append(pltpu.make_async_copy(r.memories, r.memory_grad, sems.at[9]))
    outs[2].start()
    for i, (g, start, count) in enumerate(parts):
        if start == 0:
            loads[g].wait()

        size = 80 if count % 80 == 0 else 96

        def scale(at):
            there = pl.ds(pl.multiple_of(start + at * size, 16), size)
            r.wide[g][there] = r.block[g][there].astype(F32) * inverse

        each(count // size, scale)
        outs.append(pltpu.make_async_copy(r.wide[g].at[pl.ds(start, count)], r.grads[i], sems.at[10 + i]))
        outs[-1].start()
    for copy in outs:
        copy.wait()


def run_finish(ins, layers):
    blocks, small = ins["blocks"], ins["small"]
    rows = ins["layer_in"].shape
    local, units = blocks[0].shape[0] // 4, small.shape[1]

    def shape(*dims):
        return jax.ShapeDtypeStruct(dims, F32)

    counts = (3 * local, local, local, 2 * local, local)
    outs = dict(
        layer_out=shape(*rows), input_grad=shape(*rows), memory_grad=shape(layers, *rows),
        gain_grad=shape(3, rows[1]), shift_grad=shape(3, rows[1]), bias_in_grad=shape(units), bias_out_grad=shape(rows[1]),
        grads=[shape(count, rows[1]) for count in counts] + [shape(*blocks[2].shape), shape(*blocks[3].shape)],
    )
    scratch = dict(
        layer=pltpu.VMEM(rows, F32), grad=pltpu.VMEM(rows, F32), source=pltpu.VMEM(rows, F32),
        memories=pltpu.VMEM((layers,) + rows, F32),
        block=[pltpu.VMEM(block.shape, BF16) for block in blocks],
        wide=[pltpu.VMEM(block.shape, F32) for block in blocks],
        sems=pltpu.SemaphoreType.DMA((17,)),
    )
    hbm = pl.ANY
    spaces = dict(
        configs=pltpu.SMEM, layer_in=hbm, grad_in=hbm, source_in=hbm, blocks=hbm,
        layer_out=hbm, input_grad=hbm, memory_grad=hbm, grads=hbm,
    )
    return call(finish_kernel, "finish", ins, outs, scratch, spaces, vmem_limit_bytes=60 * 2**20)


def per_device(
    inputs, memory, out_grad, lengths, src_lengths, configs, norm_gain, norm_bias,
    self_qkv, self_out, cross_q, cross_kv, cross_out, ffn_in, ffn_in_bias, ffn_out, ffn_out_bias,
):
    model = inputs.shape[1]
    layers = memory.shape[0]
    local = self_out.shape[0]
    done = run_layer(dict(
        lengths=lengths, src_lengths=src_lengths, configs=configs, gains=norm_gain, shifts=norm_bias,
        bias_in=ffn_in_bias, bias_out=ffn_out_bias, x_in=inputs, memory_in=memory, upstream_in=out_grad,
        shards=[
            self_qkv.transpose(1, 2, 0).reshape(3 * local, model), self_out, cross_q.T,
            cross_kv.transpose(1, 2, 0).reshape(2 * local, model), cross_out, ffn_in, ffn_out,
        ],
    ))
    out = run_finish(dict(
        configs=configs, small=done.small_out, layer_in=done.layer_out, grad_in=done.input_grad,
        source_in=done.memory_out, blocks=done.blocks,
    ), layers)
    grads = out.grads
    return (
        out.layer_out,
        out.input_grad,
        out.memory_grad,
        out.gain_grad,
        out.shift_grad,
        grads[0].reshape(3, local, model).transpose(2, 0, 1),
        grads[1],
        grads[2].T,
        grads[3].reshape(2, local, model).transpose(2, 0, 1),
        grads[4],
        grads[5],
        out.bias_in_grad,
        grads[6],
        out.bias_out_grad,
    )


def solution(mesh):
    rows = P(("grp", "dp", "tp"), None)
    stack = P(None, ("grp", "dp", "tp"), None)
    weights = (
        P(None, None, "tp"), P("tp", None), P(None, "tp"), P(None, None, "tp"), P("tp", None),
        P(None, "tp"), P("tp"), P("tp", None), P(),
    )
    return jax.shard_map(
        per_device,
        mesh=mesh,
        in_specs=(rows, stack, rows, P(("grp", "dp")), P(("grp", "dp")), P("grp", None), P(), P()) + weights,
        out_specs=(rows, rows, stack, P(), P()) + weights,
        check_vma=False,
    )
```

```python
import functools
import types

import jax
import jax.numpy as jnp
from jax import lax
from jax.experimental import pallas as pl
from jax.experimental.pallas import tpu as pltpu
from jax.sharding import PartitionSpec as P

HD = 80
LEN = 256
EPSILON = 1e-05
NEGATIVE = -1e30
SCALE = HD ** (-0.5)
LOG2E = 1.4426950408889634
F32 = jnp.float32
BF16 = jnp.bfloat16


MESH = pl.DeviceIdType.MESH


class Place:
    def __init__(self):
        self.tps = lax.axis_size("tp")
        self.extra = lax.axis_size("dp") // 2
        assert lax.axis_size("grp") == 4 and lax.axis_size("dp") % 2 == 0
        grp, dp, tp = (lax.axis_index(name) for name in ("grp", "dp", "tp"))
        core, low, high = dp % 2, grp % 2, grp // 2
        flip_low, flip_high = grp + 1 - 2 * low, grp + 2 - 4 * high
        self.grp, self.dp, self.tp, self.core = grp, dp, tp, core
        self.first_bit = (1 - core) * low + core * high
        self.second_bit = (1 - core) * high + core * low
        self.first = ((1 - core) * flip_low + core * flip_high, dp, tp)
        self.second = ((1 - core) * flip_high + core * flip_low, dp, tp)
        self.across = (3 - grp, dp, tp)
        self.sibling = (grp, dp + 1 - 2 * core, tp)
        self.above = (grp, dp, tp + 1)
        self.below = (grp, dp, tp - 1)
        self.has_above = tp < self.tps - 1
        self.has_below = tp > 0

    def copy_of(self, step):
        return (self.grp, ((self.dp // 2 + step) % self.extra) * 2 + self.core, self.tp)

    def nth_block(self, k):
        size = self.tps
        upper = (2 * self.tp) // size
        lead = (1 - upper) * self.tp + upper * (size - 1 - self.tp)
        spot = k + (k + size - lead) // size
        return (1 - upper) * spot + upper * (size - 1 - spot)

    def along(self, tp):
        return (self.grp, self.dp, tp)

    def barrier(self):
        sem = pltpu.get_barrier_semaphore()
        partners = [self.first, self.second, self.across, self.sibling]
        partners += [self.along((self.tp + step) % self.tps) for step in range(1, self.tps)]
        partners += [self.copy_of(step) for step in range(1, self.extra)]
        for device in partners:
            pl.semaphore_signal(sem, inc=1, device_id=device, device_id_type=MESH)
        pl.semaphore_wait(sem, len(partners))


def push(src, dst, send_sem, recv_sem, device):
    return pltpu.make_async_remote_copy(
        src_ref=src, dst_ref=dst, send_sem=send_sem, recv_sem=recv_sem, device_id=device, device_id_type=MESH
    )


def rows_of(ref, lead, start, count):
    return ref.at[lead, pl.ds(pl.multiple_of(start, 16), count)]


def add_units(total, term, unit):
    def step(i, carry):
        rows = pl.ds(pl.multiple_of(i * unit, 16), unit)
        total[rows] = total[rows] + term[rows]
        return carry

    lax.fori_loop(0, total.shape[0] // unit, step, 0)


class Spread:
    KINDS = 6

    def __init__(self, place, view, unit, sems):
        self.place, self.view, self.unit, self.sems = place, view, unit, sems
        f, s, c = place.first_bit, place.second_bit, place.core
        self.table = (
            (place.second, c * 4 + f * 2 + s, c * 4 + f * 2 + 1 - s, 1),
            (place.first, c * 4 + f * 2, c * 4 + 2 - f * 2, 2),
            (place.sibling, c * 4, 4 - c * 4, 4),
        )

    def region(self, start, count):
        return self.view(start * self.unit, count * self.unit)

    def own(self):
        return self.region(self.table[0][1], 1)

    def copy(self, n, lands=False):
        device, leaves, landing, count = self.table[n]
        part = self.region(landing if lands else leaves, count)
        return push(part, part, self.sems(2 * n), self.sems(2 * n + 1), device)

    def step(self, stage):
        if stage > 0:
            self.copy(stage - 1, lands=True).wait_recv()
        if stage < 3:
            self.copy(stage).start()

    def finish(self):
        for n in range(3):
            self.copy(n).wait_send()


class Gather:
    KINDS = Spread.KINDS + 3

    def __init__(self, place, buffers, sems):
        self.place, self.buffers, self.sems = place, buffers, sems
        self.unit = [ref.shape[1] // 8 for ref in buffers]
        self.others = place.tps - 1

    def spread(self, g, j):
        return Spread(
            self.place,
            lambda start, count: rows_of(self.buffers[g], j, start, count),
            self.unit[g],
            lambda kind: self.sems.at[kind, g, j],
        )

    def relays(self, g, j):
        p = self.place
        part = self.spread(g, j).own()
        sem = lambda n: self.sems.at[Spread.KINDS + n, g, j]
        return (
            (jnp.logical_and(j <= p.tp, p.has_above), push(part, part, sem(0), sem(2), p.above)),
            (jnp.logical_and(j >= p.tp, p.has_below), push(part, part, sem(1), sem(2), p.below)),
        )

    def start(self, g):
        for needed, copy in self.relays(g, self.place.tp):
            pl.when(needed)(copy.start)

    def step(self, g, k, stage):
        j = self.place.nth_block(k)
        if stage == 0:
            relays = self.relays(g, j)
            relays[0][1].wait_recv()
            for needed, copy in relays:
                pl.when(needed)(copy.start)
        self.spread(g, j).step(stage)

    def drain(self, g, j):
        for needed, copy in self.relays(g, j):
            pl.when(needed)(copy.wait_send)

        @pl.when(j != self.place.tp)
        def _():
            self.spread(g, j).finish()


class Line:
    def __init__(self, place, buffer, sems):
        self.place, self.buffer, self.sems = place, buffer, sems

    def relays(self, j):
        p = self.place
        part = self.buffer.at[j]
        return (
            (jnp.logical_and(j <= p.tp, p.has_above), push(part, part, self.sems.at[0, j], self.sems.at[2, j], p.above)),
            (jnp.logical_and(j >= p.tp, p.has_below), push(part, part, self.sems.at[1, j], self.sems.at[2, j], p.below)),
        )

    def start(self):
        for needed, copy in self.relays(self.place.tp):
            pl.when(needed)(copy.start)

    def step(self, k):
        j = self.place.nth_block(k)
        relays = self.relays(j)
        relays[0][1].wait_recv()
        for needed, copy in relays:
            pl.when(needed)(copy.start)

    def finish(self):
        for j in range(self.place.tps):
            for needed, copy in self.relays(j):
                pl.when(needed)(copy.wait_send)


class Reduce:
    KINDS = 8 + Spread.KINDS + 2

    def __init__(self, place, grads, halves, planes, lines, extras, totals, sems):
        self.place, self.grads, self.totals, self.sems = place, grads, totals, sems
        self.halves, self.planes, self.lines, self.extras = halves, planes, lines, extras
        self.unit = [ref.shape[1] // 8 for ref in grads]

    def sem(self, kind, g, j):
        return self.sems.at[kind, g, j]

    def rows(self, g, j, half, unit, count=1):
        size = self.unit[g]
        return rows_of(self.grads[g], j, (half * 4 + unit) * size, count * size)

    def move(self, g, j, stage):
        p, size = self.place, self.unit[g]
        if stage == 0:
            part, landing, device = self.rows(g, j, 1 - p.core, 0, 4), self.halves[g].at[j], p.sibling
        elif stage == 1:
            part, device = self.rows(g, j, p.core, 2 - p.first_bit * 2, 2), p.first
            landing = self.planes[g].at[j, pl.ds(0, 2 * size)]
        else:
            part, device = self.rows(g, j, p.core, p.first_bit * 2 + 1 - p.second_bit), p.second
            landing = self.planes[g].at[j, pl.ds(2 * size, size)]
        return push(part, landing, self.sem(2 * stage, g, j), self.sem(2 * stage + 1, g, j), device)

    def kept(self, g, j, stage):
        p, size = self.place, self.unit[g]
        if stage == 0:
            return self.rows(g, j, p.core, 0, 4), self.halves[g].at[j]
        if stage == 1:
            return self.rows(g, j, p.core, p.first_bit * 2, 2), self.planes[g].at[j, pl.ds(0, 2 * size)]
        return self.piece(g, j), self.planes[g].at[j, pl.ds(2 * size, size)]

    def piece(self, g, j):
        p = self.place
        return self.rows(g, j, p.core, p.first_bit * 2 + p.second_bit)

    def along(self, g, j):
        p = self.place
        return push(self.piece(g, j), self.lines[g].at[p.tp], self.sem(6, g, j), self.sem(7, g, p.tp), p.along(j))

    def from_place(self, g, j):
        p = self.place
        return push(self.piece(g, j), self.lines[g].at[j], self.sem(6, g, j), self.sem(7, g, j), p.along(j))

    def step(self, g, j, stage):
        if stage > 0:
            self.move(g, j, stage - 1).wait_recv()
            add_units(*self.kept(g, j, stage - 1), self.unit[g])
        if stage < 3:
            self.move(g, j, stage).start()
        else:
            pl.when(j != self.place.tp)(self.along(g, j).start)

    def spread(self, g):
        return Spread(
            self.place,
            lambda start, count: self.totals[g].at[pl.ds(pl.multiple_of(start, 16), count)],
            self.unit[g],
            lambda kind: self.sems.at[8 + kind, g, 0],
        )

    def copies(self, g, step):
        p = self.place
        base = self.KINDS - 2
        return push(
            self.piece(g, p.tp), self.extras[g].at[step], self.sem(base, g, step), self.sem(base + 1, g, step), p.copy_of(step)
        )

    def settle(self, g):
        p = self.place
        piece = self.piece(g, p.tp)
        total = piece[...].astype(F32)
        for k in range(p.tps - 1):
            j = p.nth_block(k)
            self.from_place(g, j).wait_recv()
            total = total + self.lines[g][j].astype(F32)
        if p.extra > 1:
            piece[...] = total.astype(BF16)
            for step in range(1, p.extra):
                self.copies(g, step).start()
            for step in range(1, p.extra):
                self.copies(g, step).wait()
                total = total + self.extras[g][step].astype(F32)
        own = self.spread(g).own()
        own[...] = total.astype(BF16)
        self.spread(g).step(0)

    def share(self, g, stage):
        self.spread(g).step(stage)

    def finish(self, g):
        p = self.place
        for j in range(p.tps):
            for stage in range(3):
                self.move(g, j, stage).wait_send()
            pl.when(j != p.tp)(self.along(g, j).wait_send)
        self.spread(g).finish()


class SumSmall:
    @staticmethod
    def slots(tps, extra):
        return 8 + tps + extra

    def __init__(self, place, slots, sems):
        self.place, self.slots_ref, self.sems = place, slots, sems

    def move(self, source, target, device, kind):
        slots = self.slots_ref
        return push(slots.at[source], slots.at[target], self.sems.at[0, kind], self.sems.at[1, target], device)

    def in_plane(self):
        p = self.place
        return [self.move(2, 3 + i, device, 3 + i) for i, device in enumerate((p.second, p.first, p.across))]

    def copies(self):
        p = self.place
        return [self.move(6, 8 + p.tps + s, p.copy_of(s), 8 + p.tps + s) for s in range(1, p.extra)]

    def along(self, k, lands=False):
        p = self.place
        j = p.nth_block(k)
        return self.move(7, 8 + (j if lands else p.tp), p.along(j), 8 + j)

    def start(self):
        self.move(0, 1, self.place.sibling, 1).start()

    def exchange(self, stage):
        p, slots = self.place, self.slots_ref
        if stage == 0:
            self.move(0, 1, p.sibling, 1).wait_recv()
            slots[2] = slots[0] + slots[1]
            for copy in self.in_plane():
                copy.start()
        else:
            for copy in self.in_plane():
                copy.wait_recv()
            slots[6] = (slots[2] + slots[3]) + (slots[4] + slots[5])
            for copy in self.copies():
                copy.start()
            total = slots[6]
            for s, copy in enumerate(self.copies()):
                copy.wait_recv()
                total = total + slots[9 + p.tps + s]
            slots[7] = total
            for k in range(p.tps - 1):
                self.along(k).start()

    def total(self):
        p, slots = self.place, self.slots_ref
        value = slots[7]
        for k in range(p.tps - 1):
            self.along(k, lands=True).wait_recv()
            value = value + slots[8 + p.nth_block(k)]
        return value

    def finish(self):
        p = self.place
        self.move(0, 1, p.sibling, 1).wait_send()
        for copy in self.in_plane() + self.copies():
            copy.wait_send()
        for k in range(p.tps - 1):
            self.along(k).wait_send()


def dot_nn(left, right):
    return lax.dot_general(left, right, (((1,), (0,)), ((), ())), preferred_element_type=F32)


def dot_nt(left, right):
    return lax.dot_general(left, right, (((1,), (1,)), ((), ())), preferred_element_type=F32)


def dot_tn(left, right):
    return lax.dot_general(left, right, (((0,), (0,)), ((), ())), preferred_element_type=F32)


def column(axis, shape):
    return lax.broadcasted_iota(jnp.int32, shape, axis)


def each(count, step):

    def run(i, carry):
        step(i)
        return carry

    lax.fori_loop(0, count, run, 0)


CHUNK = 128
CUBE = 0.044715
ROOT = 0.7978845608028654


def layer_kernel(r):
    r.a2, r.a3, r.e = (r.memory.at[i] for i in range(3))
    columns = pl.ds(0, r.x.shape[1])
    r.dh, r.dm = r.before.at[:, columns], r.down.at[:, columns]
    place = Place()
    n = place.tps
    x, model = r.x, r.x.shape[1]
    owned = x.shape[0]
    sentences = owned // LEN
    local = r.c[0].shape[1]
    heads_here = local // HD
    units = r.hidden.shape[1]
    layers = r.memory.shape[0]
    weights = r.w
    lengths, sources, configs = r.lengths, r.src_lengths, r.configs
    width, heads, hidden_units, depth = (configs[0, i] for i in range(4))
    inv_width = 1.0 / jnp.full((1, 1), width.astype(F32))
    inv_depth = 1.0 / jnp.full((1, 1), depth.astype(F32))
    width_mask = (column(1, (1, model)) < width).astype(F32)

    local_sem = r.local_sems
    spots = (
        (0, 0, 3 * local), (0, 3 * local, local),
        (1, 0, local), (1, local, 2 * local), (1, 3 * local, local),
        (2, 0, weights[2].shape[1]), (3, 0, weights[3].shape[1]),
    )
    fills = [
        (g, pltpu.make_async_copy(r.shards[i], weights[g].at[place.tp, pl.ds(start, size)], local_sem.at[i]))
        for i, (g, start, size) in enumerate(spots)
    ]
    loads = [
        pltpu.make_async_copy(source, target, local_sem.at[7 + i])
        for i, (source, target) in enumerate(((r.x_in, r.x), (r.memory_in, r.memory), (r.upstream_in, r.upstream)))
    ]
    for _, copy in fills[:2]:
        copy.start()
    loads[0].start()
    for _, copy in fills[2:]:
        copy.start()
    loads[1].start()
    loads[2].start()
    r.bias[place.tp] = jnp.broadcast_to(r.bias_in[...].reshape(1, units), r.bias.shape[1:])
    place.barrier()

    gather = Gather(place, weights, r.gather_sems)
    bias = Line(place, r.bias, r.bias_sems)
    for g in range(4):
        for group, copy in fills:
            if group == g:
                copy.wait()
        gather.start(g)
        if g == 0:
            bias.start()
    order = [(g, k) for g in (0, 1) for k in range(n - 1)] + [(g, k) for k in range(n - 1) for g in (2, 3)]

    def g_tick(tick):
        for stage in range(4):
            if 0 <= tick - stage < len(order):
                gather.step(*order[tick - stage], stage)

    def block(k):
        later = (k + n - 1) // n
        return (1 - later) * place.tp + later * place.nth_block(k - 1)

    def block_last(k):
        own = k // (n - 1)
        return own * place.tp + (1 - own) * place.nth_block(k)

    def hooks(table, k, b):
        for (kk, bb), steps in table.items():

            @pl.when(jnp.logical_and(k == kk, b == bb))
            def _():
                for step in steps:
                    step()

    def chunk(i):
        return pl.ds(pl.multiple_of(i * CHUNK, CHUNK), CHUNK)

    def keep_of(i):
        per = LEN // CHUNK
        spot = column(0, (CHUNK, 1)) + (i % per) * CHUNK
        return (spot < lengths[place.tp * sentences + i // per]).astype(F32) * width_mask

    def norm_parts(rows):
        mean = jnp.sum(rows * width_mask, axis=-1, keepdims=True) * inv_width
        centred = (rows - mean) * width_mask
        spread = jnp.sum(centred * centred, axis=-1, keepdims=True) * inv_width
        rstd = lax.rsqrt(spread + EPSILON)
        return centred * rstd, rstd

    def norm(rows, which):
        hat, _ = norm_parts(rows)
        return ((hat * r.gains[which:which + 1] + r.shifts[which:which + 1]) * width_mask).astype(BF16)

    def fold(values):
        return jnp.sum(values.reshape(values.shape[0] // 8, 8, values.shape[1]), axis=0)

    def norm_backward(rows, which, upstream):
        hat, rstd = norm_parts(rows)
        upstream = upstream * width_mask
        sums = r.norm_sums
        sums[which] = sums[which] + fold(upstream * hat)
        sums[3 + which] = sums[3 + which] + fold(upstream)
        scaled = upstream * r.gains[which:which + 1]
        first = jnp.sum(scaled, axis=-1, keepdims=True) * inv_width
        second = jnp.sum(scaled * hat, axis=-1, keepdims=True) * inv_width
        return (rstd * (scaled - first - hat * second)) * width_mask

    chunks = owned // CHUNK

    def each_chunk(step):
        each(chunks, step)

    acc, da, dh = r.acc, r.da, r.dh
    zeros = jnp.zeros((CHUNK, model), F32)
    r.norm_sums[...] = jnp.zeros(r.norm_sums.shape, F32)
    r.bias_sums[...] = jnp.zeros(r.bias_sums.shape, F32)

    def sentence(b):
        return pl.ds(pl.multiple_of(b * LEN, LEN), LEN)

    def head_keep(j, h):
        return jnp.where(j * heads_here + h < heads, 1.0, 0.0).astype(F32)

    def causal(b, start, size):
        return column(0, (size, 128)) <= column(1, (size, 128)) + start

    def crossing(b, start, size):
        return column(0, (size, 1)) < sources[place.tp * sentences + b]

    def reach(g, start):
        return start + 128 if g == 0 else LEN

    def bands(h):
        return [pl.ds(i * local + h * HD, HD) for i in range(3)]

    def lanes(b):
        return pl.ds(b * LEN, LEN)

    pairs = [(b, h) for b in range(sentences) for h in range(heads_here)]

    quarters = [(i, b, h, start) for i, (b, h) in enumerate(pairs) for start in range(0, LEN, 128)]

    def attend(k, table, g, allowed):
        w, t, c, p = weights[g], r.t[g], r.c[g], r.p[g]
        j = block(k)
        hooks(table, k, 0)
        if g == 0:
            t[j] = dot_nt(w[j, :3 * local], r.a1[...]).astype(BF16)
        else:
            t[j, :local] = dot_nt(w[j, :local], r.a2[...]).astype(BF16)
            t[j, local:] = dot_nt(w[j, local:3 * local], r.m[...]).astype(BF16)
        heads_of = [[t[j, band, lanes(b)] for band in bands(h)] for b, h in pairs]
        for i, (query, keys, _) in enumerate(heads_of):
            r.scores[i] = dot_tn(keys, query)
        for i, b, h, start in quarters:
            part, size = pl.ds(start, 128), reach(g, start)
            score = jnp.where(allowed(b, start, size), r.scores[i, :size, part], NEGATIVE)
            raised = jnp.exp2((score - jnp.max(score, axis=0, keepdims=True)) * (SCALE * LOG2E))
            p[j, i, :size, part] = (raised * (1.0 / jnp.sum(raised, axis=0, keepdims=True))).astype(BF16)
            if size < LEN:
                p[j, i, size:, part] = jnp.zeros((LEN - size, 128), BF16)
        for i, (b, h) in enumerate(pairs):
            c[j, pl.ds(h * HD, HD), lanes(b)] = (dot_nn(heads_of[i][2], p[j, i]) * head_keep(j, h)).astype(BF16)
        hooks(table, k, 1)
        acc[...] = acc[...] + dot_tn(c[j], w[j, 3 * local:])

    def attend_backward(k, table, g, query_rows, key_rows):
        w, t, c, p = weights[g], r.t[g], r.c[g], r.p[g]
        j = block_last(k)
        e, dt, dc = r.e, r.dt, r.dc
        dc_all = dot_nt(w[j, 3 * local:], e[...])
        for h in range(heads_here):
            dc[h * HD:(h + 1) * HD] = (dc_all[h * HD:(h + 1) * HD] * head_keep(j, h)).astype(BF16)
        heads_of = [[t[j, band, lanes(b)] for band in bands(h)] for b, h in pairs]
        dc_of = [dc[h * HD:(h + 1) * HD, lanes(b)] for b, h in pairs]
        for i, (_, _, values) in enumerate(heads_of):
            r.scores[i] = dot_tn(values, dc_of[i])
        for i, b, h, start in quarters:
            part, size = pl.ds(start, 128), reach(g, start)
            dp, wide = r.scores[i, :size, part], p[j, i, :size, part].astype(F32)
            r.ds[i, :size, part] = (wide * (dp - jnp.sum(dp * wide, axis=0, keepdims=True))).astype(BF16)
            if size < LEN:
                r.ds[i, size:, part] = jnp.zeros((LEN - size, 128), BF16)
        for i, (b, h) in enumerate(pairs):
            (query, keys, _), (dq, dk, dv) = heads_of[i], bands(h)
            dt[dv, lanes(b)] = dot_nt(dc_of[i], p[j, i]).astype(BF16)
            dt[dq, lanes(b)] = (dot_nn(keys, r.ds[i]) * SCALE).astype(BF16)
            dt[dk, lanes(b)] = (dot_nt(query, r.ds[i]) * SCALE).astype(BF16)
        hooks(table, k, 1)
        gather.drain(g, j)
        if g == 0:
            da[...] = da[...] + dot_tn(dt[...], w[j, :3 * local])
            w[j, :3 * local] = dot_nn(dt[...], query_rows[...]).astype(BF16)
        else:
            da[...] = da[...] + dot_tn(dt[:local], w[j, :local])
            r.dm[...] = r.dm[...] + dot_tn(dt[local:], w[j, local:3 * local])
            w[j, :local] = dot_nn(dt[:local], query_rows[...]).astype(BF16)
            w[j, local:3 * local] = dot_nn(dt[local:], key_rows[...]).astype(BF16)
        w[j, 3 * local:] = dot_nn(c[j], e[...]).astype(BF16)

    def feed(k, table):
        j = block(k)
        w_up, w_down = weights[2], weights[3]
        hooks(table, k, 0)
        r.before[...] = dot_nn(r.a3[...], w_up[j]) + r.bias[j, 0:1]
        r.down[...] = dot_nt(r.e[...], w_down[j])
        step_lanes = units // 2

        def bend(i):
            for start in range(0, units, step_lanes):
                part = pl.ds(start, step_lanes)
                unit = column(1, (1, step_lanes)) + (j * units + start)
                kept = jnp.where(unit < hidden_units, 0.5, 0.0)
                sums = r.bias_sums[j, :, part]
                for line in range(4):
                    rows = pl.ds(pl.multiple_of(i * 64, 64) + line * 16, 16)
                    before = r.before[rows, part]
                    square = before * before
                    bent = jnp.tanh(before * (ROOT + ROOT * CUBE * square))
                    half = kept + kept * bent
                    through = before * half
                    r.hidden[rows, part] = through.astype(BF16)
                    slope = half + (through - through * bent) * (ROOT + 3.0 * CUBE * ROOT * square)
                    du = (r.down[rows, part] * slope).astype(BF16)
                    r.dhidden[rows, part] = du
                    sums = sums + fold(du.astype(F32))
                r.bias_sums[j, :, part] = sums

        each(owned // 64, bend)
        hooks(table, k, 1)
        acc[...] = acc[...] + dot_nn(r.hidden[...], w_down[j])
        da[...] = da[...] + dot_nt(r.dhidden[...], w_up[j])
        gather.drain(2, j)
        gather.drain(3, j)
        w_down[j] = dot_tn(r.hidden[...], r.e[...]).astype(BF16)
        w_up[j] = dot_nn(r.a3t[...], r.dhidden[...]).astype(BF16)

    loads[0].wait()

    def begin(i):
        rows = chunk(i)
        r.a1[rows] = norm(x[rows].astype(F32), 0)
        acc[rows] = zeros
        da[rows] = zeros

    each_chunk(begin)
    g_tick(0)
    loads[1].wait()

    def mix(i):
        rows = chunk(i)
        total = jnp.zeros((CHUNK, model), F32)
        for level in range(layers):
            chosen = (jnp.full((1, 1), depth) >= layers - level).astype(F32)
            total = total + chosen * r.memory[level, rows].astype(F32)
        r.m[rows] = (total * inv_depth * width_mask).astype(BF16)

    each_chunk(mix)
    g_tick(1)
    loads[2].wait()
    r.out_sums[...] = jnp.zeros(r.out_sums.shape, F32)

    def grad_in(i):
        rows = chunk(i)
        masked = r.upstream[rows].astype(F32) * keep_of(i)
        r.out_sums[...] = r.out_sums[...] + fold(masked)
        r.e[rows] = masked.astype(BF16)

    each_chunk(grad_in)
    g_tick(2)

    def ticks(*numbers):
        return [functools.partial(g_tick, i) for i in numbers]

    others = n - 1
    assert n == 4
    table = {
        (0, 1): ticks(3),
        (1, 0): ticks(4) + [functools.partial(bias.step, 0)],
        (1, 1): ticks(5),
        (2, 0): [functools.partial(bias.step, 1)],
        (2, 1): ticks(6),
        (3, 0): [functools.partial(bias.step, 2)],
        (3, 1): ticks(7),
    }
    each(n, lambda k: attend(k, table, 0, causal))

    def after_self(i):
        rows = chunk(i)
        h = x[rows].astype(F32) + acc[rows] * keep_of(i)
        r.h1[rows] = h
        r.a2[rows] = norm(h, 1)
        acc[rows] = zeros

    each_chunk(after_self)
    table2 = {(0, 0): ticks(8), (0, 1): ticks(9), (1, 1): ticks(10), (2, 1): ticks(11), (3, 1): ticks(12)}
    each(n, lambda k: attend(k, table2, 1, crossing))

    def after_cross(i):
        rows = chunk(i)
        h = r.h1[rows] + acc[rows] * keep_of(i)
        r.h2[rows] = h
        r.a3[rows] = norm(h, 2)
        acc[rows] = zeros

    each_chunk(after_cross)
    r.a3t[...] = r.a3[...].T

    reduce = Reduce(
        place, weights, r.half, r.plane, r.line, r.extra, r.total, r.reduce_sems
    )
    plan = {}

    def add(tick, order, step, *args):
        plan.setdefault(tick, []).append((order, len(plan.get(tick, ())), functools.partial(step, *args)))

    def r_tick(tick):
        for _, _, step in sorted(plan.get(tick, ()), key=lambda entry: entry[:2]):
            step()

    def store(g):
        return pltpu.make_async_copy(r.total[g], r.blocks[g], local_sem.at[10 + g])

    times = {
        3: ([(1, 3, 6, 10), (3, 5, 8, 12), (5, 7, 9, 14), (7, 9, 11, 15)], (17, 19, 21, 23)),
        2: ([(1, 4, 7, 10), (3, 6, 8, 12), (5, 8, 10, 14), (7, 10, 12, 16)], (18, 20, 22, 24)),
        1: ([(10, 12, 14, 16), (12, 14, 16, 18), (14, 16, 18, 20), (16, 18, 20, 22)], (23, 25, 27, 29)),
        0: ([(19, 21, 23, 25), (21, 23, 25, 26), (23, 25, 26, 27), (25, 26, 27, 28)], (28, 29, 30, 31)),
    }
    for late, g in enumerate((3, 2, 1, 0)):
        for k, stages in enumerate(times[g][0]):
            j = block(k) if g > 1 else block_last(k)
            for stage, tick in enumerate(stages):
                add(tick, stage, reduce.step, g, j, stage)
        for stage, tick in enumerate(times[g][1]):
            if stage == 0:
                add(tick, 20 - late, reduce.settle, g)
            else:
                add(tick, 30 + stage - late, reduce.share, g, stage)
        add(times[g][1][-1], 50, lambda g=g: store(g).start())

    def reduce_ticks(*numbers):
        return [functools.partial(r_tick, i) for i in numbers]

    def at_end(k, numbers):
        for kk, number in enumerate(numbers):

            @pl.when(k == kk)
            def _():
                r_tick(number)

    table3 = {(0, 0): ticks(13), (0, 1): ticks(14), (1, 1): reduce_ticks(2), (2, 1): reduce_ticks(4), (3, 1): reduce_ticks(6)}

    def feed_step(k):
        feed(k, table3)
        at_end(k, [2 * i + 1 for i in range(n)])

    each(n, feed_step)
    r_tick(8)
    out_copy = pltpu.make_async_copy(acc, r.layer_out, local_sem.at[14])

    def after_feed(i):
        rows = chunk(i)
        keep = keep_of(i)
        acc[rows] = r.h2[rows] + (acc[rows] + r.bias_out[...].reshape(1, model)) * keep
        down = r.upstream[rows].astype(F32) + norm_backward(r.h2[rows], 2, da[rows])
        dh[rows] = down
        r.e[rows] = (down * keep).astype(BF16)
        da[rows] = zeros
        r.dm[rows] = zeros

    each_chunk(after_feed)
    out_copy.start()
    table4 = {(k, 1): reduce_ticks(9 + 2 * k) for k in range(n)}

    def cross_step(k):
        attend_backward(k, table4, 1, r.a2, r.m)
        at_end(k, [10 + 2 * i for i in range(n)])

    each(n, cross_step)
    memory_copy = pltpu.make_async_copy(r.dm, r.memory_out, local_sem.at[15])
    memory_copy.start()

    def before_cross(i):
        rows = chunk(i)
        down = dh[rows] + norm_backward(r.h1[rows], 1, da[rows])
        dh[rows] = down
        r.e[rows] = (down * keep_of(i)).astype(BF16)
        da[rows] = zeros

    each_chunk(before_cross)
    r_tick(17)
    table5 = {(k, 1): reduce_ticks(18 + 2 * k) for k in range(n)}

    def self_step(k):
        attend_backward(k, table5, 0, r.a1, r.a1)
        at_end(k, [19 + 2 * i for i in range(n)])

    each(n, self_step)

    def before_self(i):
        rows = chunk(i)
        dh[rows] = dh[rows] + norm_backward(x[rows].astype(F32), 0, da[rows])

    each_chunk(before_self)
    grad_copy = pltpu.make_async_copy(dh, r.input_grad, local_sem.at[16])
    grad_copy.start()

    small = SumSmall(place, r.slots, r.small_sems)

    def small_start():
        own = r.slots.at[0]
        own[...] = jnp.zeros(own.shape, F32)
        for i in range(6):
            own[i:i + 1, :model] = jnp.sum(r.norm_sums[i], axis=0, keepdims=True)
        own[6:7, :model] = jnp.sum(r.out_sums[...], axis=0, keepdims=True)
        tokens = lengths[place.tp * sentences]
        for b in range(1, sentences):
            tokens = tokens + lengths[place.tp * sentences + b]
        own[7:8] = jnp.full((1, own.shape[1]), tokens.astype(F32))
        for i in range(n):
            own[8 + i:9 + i] = jnp.sum(r.bias_sums[i], axis=0, keepdims=True)
        small.start()

    add(26, 5, small_start)
    for stage in range(2):
        add(27 + stage, 5, small.exchange, stage)
    final = max(plan)
    for tick in range(26, final + 1):
        r_tick(tick)
    r.small_out[...] = small.total()
    bias.finish()
    for copy in (out_copy, memory_copy, grad_copy):
        copy.wait()
    for g in range(4):
        reduce.finish(g)
        store(g).wait()
    small.finish()


def call(kernel, name, ins, outs, scratch, spaces, **options):
    trees = (ins, outs, scratch)
    structure = jax.tree_util.tree_structure(trees)

    def body(*refs):
        groups = jax.tree_util.tree_unflatten(structure, refs)
        kernel(types.SimpleNamespace(**groups[0], **groups[1], **groups[2]))

    def specs(group):
        return [
            pl.BlockSpec(memory_space=spaces.get(key, pltpu.VMEM))
            for key in sorted(group) for _ in jax.tree_util.tree_leaves(group[key])
        ]

    leaves = jax.tree_util.tree_leaves
    values = pl.pallas_call(
        body,
        out_shape=leaves(outs),
        in_specs=specs(ins),
        out_specs=specs(outs),
        scratch_shapes=leaves(scratch),
        compiler_params=pltpu.CompilerParams(**options),
        name=name,
    )(*leaves(ins))
    return types.SimpleNamespace(**jax.tree_util.tree_unflatten(jax.tree_util.tree_structure(outs), values))


def run_layer(ins):
    n, extra = lax.axis_size("tp"), lax.axis_size("dp") // 2
    owned, model = ins["x_in"].shape
    memory, shards = ins["memory_in"], ins["shards"]
    local, units = shards[1].shape[0], ins["bias_in"].shape[0]
    small = (16, units)
    assert n <= 8 and units >= model and memory.shape[0] >= 3
    shapes = [(n, 4 * local, model)] * 2 + [(n,) + shards[5].shape, (n,) + shards[6].shape]
    small_slots = SumSmall.slots(n, extra)

    def vmem(*shape):
        return pltpu.VMEM(shape, BF16)

    def wide(*shape):
        return pltpu.VMEM(shape, F32)

    def eighths(*lead, parts=1):
        return [vmem(*lead, rows * parts // 8, columns) for _, rows, columns in shapes]

    dma = pltpu.SemaphoreType.DMA
    scratch = dict(
        w=[vmem(*shape) for shape in shapes],
        bias=wide(n, 8, units),
        x=vmem(owned, model),
        memory=vmem(*memory.shape),
        upstream=vmem(owned, model),
        a1=vmem(owned, model),
        m=vmem(owned, model),
        h1=wide(owned, model),
        h2=wide(owned, model),
        acc=wide(owned, model),
        da=wide(owned, model),
        t=[vmem(n, 3 * local, owned)] * 2,
        c=[vmem(n, local, owned)] * 2,
        p=[vmem(n, owned // LEN * (local // HD), LEN, LEN)] * 2,
        dt=vmem(3 * local, owned),
        dc=vmem(local, owned),
        a3t=vmem(model, owned),
        scores=wide(owned // LEN * (local // HD), LEN, LEN),
        ds=vmem(owned // LEN * (local // HD), LEN, LEN),
        before=wide(owned, units),
        down=wide(owned, units),
        hidden=vmem(owned, units),
        dhidden=vmem(owned, units),
        bias_sums=wide(n, 8, units),
        norm_sums=wide(6, 8, model),
        out_sums=wide(8, model),
        half=eighths(n, parts=4),
        plane=eighths(n, parts=3),
        line=eighths(n),
        extra=eighths(extra),
        total=eighths(parts=8),
        slots=wide(small_slots, *small),
        gather_sems=dma((Gather.KINDS, 4, n)),
        bias_sems=dma((3, n)),
        reduce_sems=dma((Reduce.KINDS, 4, max(n, extra))),
        small_sems=dma((2, small_slots)),
        local_sems=dma((17,)),
    )
    rows = jax.ShapeDtypeStruct((owned, model), F32)
    outs = dict(
        layer_out=rows, input_grad=rows, memory_out=rows, small_out=jax.ShapeDtypeStruct(small, F32),
        blocks=[jax.ShapeDtypeStruct(shape[1:], BF16) for shape in shapes],
    )
    smem, hbm = pltpu.SMEM, pl.ANY
    spaces = dict(
        lengths=smem, src_lengths=smem, configs=smem, x_in=hbm, memory_in=hbm, upstream_in=hbm, shards=hbm,
        layer_out=hbm, input_grad=hbm, memory_out=hbm, blocks=hbm,
    )
    return call(
        layer_kernel, "layer", ins, outs, scratch, spaces,
        collective_id=1, has_side_effects=True, vmem_limit_bytes=64 * 2**20,
    )


def finish_kernel(r):
    small, configs, sems = r.small, r.configs, r.sems
    model = r.gain_grad.shape[1]
    layers = r.memory_grad.shape[0]
    place = lax.axis_index("tp")
    local = r.grads[1].shape[0]
    parts = (
        (0, 0, 3 * local), (0, 3 * local, local),
        (1, 0, local), (1, local, 2 * local), (1, 3 * local, local),
        (2, 0, r.block[2].shape[0]), (3, 0, r.block[3].shape[0]),
    )
    loads = [pltpu.make_async_copy(r.blocks[g], r.block[g], sems.at[g]) for g in range(4)]
    rows = [
        pltpu.make_async_copy(source, target, sems.at[4 + i])
        for i, (source, target) in enumerate(((r.layer_in, r.layer), (r.grad_in, r.grad), (r.source_in, r.source)))
    ]
    outs = [pltpu.make_async_copy(r.layer, r.layer_out, sems.at[7]), pltpu.make_async_copy(r.grad, r.input_grad, sems.at[8])]
    for copy in rows + loads:
        copy.start()
    inverse = 1.0 / small[7:8, :1]
    r.gain_grad[...] = small[:3, :model] * inverse
    r.shift_grad[...] = small[3:6, :model] * inverse
    r.bias_out_grad[...] = (small[6:7, :model] * inverse).reshape(model)
    r.bias_in_grad[...] = (small[pl.ds(8 + place, 1)] * inverse).reshape(small.shape[1])
    width, depth = configs[0, 0], configs[0, 3]
    factor = (column(1, (1, model)) < width).astype(F32) / jnp.full((1, 1), depth.astype(F32))
    for i in range(2):
        rows[i].wait()
        outs[i].start()
    rows[2].wait()

    def spread(i):
        part = pl.ds(pl.multiple_of(i * 64, 64), 64)
        value = r.source[part] * factor
        for level in range(layers):
            chosen = (jnp.full((1, 1), depth) >= layers - level).astype(F32)
            r.memories[level, part] = value * chosen

    each(r.source.shape[0] // 64, spread)
    outs.append(pltpu.make_async_copy(r.memories, r.memory_grad, sems.at[9]))
    outs[2].start()
    for i, (g, start, count) in enumerate(parts):
        if start == 0:
            loads[g].wait()

        size = 80 if count % 80 == 0 else 96

        def scale(at):
            there = pl.ds(pl.multiple_of(start + at * size, 16), size)
            r.wide[g][there] = r.block[g][there].astype(F32) * inverse

        each(count // size, scale)
        outs.append(pltpu.make_async_copy(r.wide[g].at[pl.ds(start, count)], r.grads[i], sems.at[10 + i]))
        outs[-1].start()
    for copy in outs:
        copy.wait()


def run_finish(ins, layers):
    blocks, small = ins["blocks"], ins["small"]
    rows = ins["layer_in"].shape
    local, units = blocks[0].shape[0] // 4, small.shape[1]

    def shape(*dims):
        return jax.ShapeDtypeStruct(dims, F32)

    counts = (3 * local, local, local, 2 * local, local)
    outs = dict(
        layer_out=shape(*rows), input_grad=shape(*rows), memory_grad=shape(layers, *rows),
        gain_grad=shape(3, rows[1]), shift_grad=shape(3, rows[1]), bias_in_grad=shape(units), bias_out_grad=shape(rows[1]),
        grads=[shape(count, rows[1]) for count in counts] + [shape(*blocks[2].shape), shape(*blocks[3].shape)],
    )
    scratch = dict(
        layer=pltpu.VMEM(rows, F32), grad=pltpu.VMEM(rows, F32), source=pltpu.VMEM(rows, F32),
        memories=pltpu.VMEM((layers,) + rows, F32),
        block=[pltpu.VMEM(block.shape, BF16) for block in blocks],
        wide=[pltpu.VMEM(block.shape, F32) for block in blocks],
        sems=pltpu.SemaphoreType.DMA((17,)),
    )
    hbm = pl.ANY
    spaces = dict(
        configs=pltpu.SMEM, layer_in=hbm, grad_in=hbm, source_in=hbm, blocks=hbm,
        layer_out=hbm, input_grad=hbm, memory_grad=hbm, grads=hbm,
    )
    return call(finish_kernel, "finish", ins, outs, scratch, spaces, vmem_limit_bytes=60 * 2**20)


def per_device(
    inputs, memory, out_grad, lengths, src_lengths, configs, norm_gain, norm_bias,
    self_qkv, self_out, cross_q, cross_kv, cross_out, ffn_in, ffn_in_bias, ffn_out, ffn_out_bias,
):
    model = inputs.shape[1]
    layers = memory.shape[0]
    local = self_out.shape[0]
    done = run_layer(dict(
        lengths=lengths, src_lengths=src_lengths, configs=configs, gains=norm_gain, shifts=norm_bias,
        bias_in=ffn_in_bias, bias_out=ffn_out_bias, x_in=inputs, memory_in=memory, upstream_in=out_grad,
        shards=[
            self_qkv.transpose(1, 2, 0).reshape(3 * local, model), self_out, cross_q.T,
            cross_kv.transpose(1, 2, 0).reshape(2 * local, model), cross_out, ffn_in, ffn_out,
        ],
    ))
    out = run_finish(dict(
        configs=configs, small=done.small_out, layer_in=done.layer_out, grad_in=done.input_grad,
        source_in=done.memory_out, blocks=done.blocks,
    ), layers)
    grads = out.grads
    return (
        out.layer_out,
        out.input_grad,
        out.memory_grad,
        out.gain_grad,
        out.shift_grad,
        grads[0].reshape(3, local, model).transpose(2, 0, 1),
        grads[1],
        grads[2].T,
        grads[3].reshape(2, local, model).transpose(2, 0, 1),
        grads[4],
        grads[5],
        out.bias_in_grad,
        grads[6],
        out.bias_out_grad,
    )


def solution(mesh):
    rows = P(("grp", "dp", "tp"), None)
    stack = P(None, ("grp", "dp", "tp"), None)
    weights = (
        P(None, None, "tp"), P("tp", None), P(None, "tp"), P(None, None, "tp"), P("tp", None),
        P(None, "tp"), P("tp"), P("tp", None), P(),
    )
    return jax.shard_map(
        per_device,
        mesh=mesh,
        in_specs=(rows, stack, rows, P(("grp", "dp")), P(("grp", "dp")), P("grp", None), P(), P()) + weights,
        out_specs=(rows, rows, stack, P(), P()) + weights,
        check_vma=False,
    )
```

```python
import functools
import types

import jax
import jax.numpy as jnp
from jax import lax
from jax.experimental import pallas as pl
from jax.experimental.pallas import tpu as pltpu
from jax.sharding import PartitionSpec as P

HD = 80
LEN = 256
EPSILON = 1e-05
NEGATIVE = -1e30
SCALE = HD ** (-0.5)
LOG2E = 1.4426950408889634
F32 = jnp.float32
BF16 = jnp.bfloat16


MESH = pl.DeviceIdType.MESH


class Place:
    def __init__(self):
        self.tps = lax.axis_size("tp")
        self.extra = lax.axis_size("dp") // 2
        assert lax.axis_size("grp") == 4 and lax.axis_size("dp") % 2 == 0
        grp, dp, tp = (lax.axis_index(name) for name in ("grp", "dp", "tp"))
        core, low, high = dp % 2, grp % 2, grp // 2
        flip_low, flip_high = grp + 1 - 2 * low, grp + 2 - 4 * high
        self.grp, self.dp, self.tp, self.core = grp, dp, tp, core
        self.first_bit = (1 - core) * low + core * high
        self.second_bit = (1 - core) * high + core * low
        self.first = ((1 - core) * flip_low + core * flip_high, dp, tp)
        self.second = ((1 - core) * flip_high + core * flip_low, dp, tp)
        self.across = (3 - grp, dp, tp)
        self.sibling = (grp, dp + 1 - 2 * core, tp)
        self.above = (grp, dp, tp + 1)
        self.below = (grp, dp, tp - 1)
        self.has_above = tp < self.tps - 1
        self.has_below = tp > 0

    def copy_of(self, step):
        return (self.grp, ((self.dp // 2 + step) % self.extra) * 2 + self.core, self.tp)

    def nth_block(self, k):
        size = self.tps
        upper = (2 * self.tp) // size
        lead = (1 - upper) * self.tp + upper * (size - 1 - self.tp)
        spot = k + (k + size - lead) // size
        return (1 - upper) * spot + upper * (size - 1 - spot)

    def along(self, tp):
        return (self.grp, self.dp, tp)

    def barrier(self):
        sem = pltpu.get_barrier_semaphore()
        partners = [self.first, self.second, self.across, self.sibling]
        partners += [self.along((self.tp + step) % self.tps) for step in range(1, self.tps)]
        partners += [self.copy_of(step) for step in range(1, self.extra)]
        for device in partners:
            pl.semaphore_signal(sem, inc=1, device_id=device, device_id_type=MESH)
        pl.semaphore_wait(sem, len(partners))


def push(src, dst, send_sem, recv_sem, device):
    return pltpu.make_async_remote_copy(
        src_ref=src, dst_ref=dst, send_sem=send_sem, recv_sem=recv_sem, device_id=device, device_id_type=MESH
    )


def rows_of(ref, lead, start, count):
    return ref.at[lead, pl.ds(pl.multiple_of(start, 16), count)]


def add_units(total, term, unit):
    def step(i, carry):
        rows = pl.ds(pl.multiple_of(i * unit, 16), unit)
        total[rows] = total[rows] + term[rows]
        return carry

    lax.fori_loop(0, total.shape[0] // unit, step, 0)


class Spread:
    KINDS = 6

    def __init__(self, place, view, unit, sems):
        self.place, self.view, self.unit, self.sems = place, view, unit, sems
        f, s, c = place.first_bit, place.second_bit, place.core
        self.table = (
            (place.second, c * 4 + f * 2 + s, c * 4 + f * 2 + 1 - s, 1),
            (place.first, c * 4 + f * 2, c * 4 + 2 - f * 2, 2),
            (place.sibling, c * 4, 4 - c * 4, 4),
        )

    def region(self, start, count):
        return self.view(start * self.unit, count * self.unit)

    def own(self):
        return self.region(self.table[0][1], 1)

    def copy(self, n, lands=False):
        device, leaves, landing, count = self.table[n]
        part = self.region(landing if lands else leaves, count)
        return push(part, part, self.sems(2 * n), self.sems(2 * n + 1), device)

    def step(self, stage):
        if stage > 0:
            self.copy(stage - 1, lands=True).wait_recv()
        if stage < 3:
            self.copy(stage).start()

    def finish(self):
        for n in range(3):
            self.copy(n).wait_send()


class Gather:
    KINDS = Spread.KINDS + 3

    def __init__(self, place, buffers, sems):
        self.place, self.buffers, self.sems = place, buffers, sems
        self.unit = [ref.shape[1] // 8 for ref in buffers]
        self.others = place.tps - 1

    def spread(self, g, j):
        return Spread(
            self.place,
            lambda start, count: rows_of(self.buffers[g], j, start, count),
            self.unit[g],
            lambda kind: self.sems.at[kind, g, j],
        )

    def relays(self, g, j):
        p = self.place
        part = self.spread(g, j).own()
        sem = lambda n: self.sems.at[Spread.KINDS + n, g, j]
        return (
            (jnp.logical_and(j <= p.tp, p.has_above), push(part, part, sem(0), sem(2), p.above)),
            (jnp.logical_and(j >= p.tp, p.has_below), push(part, part, sem(1), sem(2), p.below)),
        )

    def start(self, g):
        for needed, copy in self.relays(g, self.place.tp):
            pl.when(needed)(copy.start)

    def step(self, g, k, stage):
        j = self.place.nth_block(k)
        if stage == 0:
            relays = self.relays(g, j)
            relays[0][1].wait_recv()
            for needed, copy in relays:
                pl.when(needed)(copy.start)
        self.spread(g, j).step(stage)

    def drain(self, g, j):
        for needed, copy in self.relays(g, j):
            pl.when(needed)(copy.wait_send)

        @pl.when(j != self.place.tp)
        def _():
            self.spread(g, j).finish()


class Line:
    def __init__(self, place, buffer, sems):
        self.place, self.buffer, self.sems = place, buffer, sems

    def relays(self, j):
        p = self.place
        part = self.buffer.at[j]
        return (
            (jnp.logical_and(j <= p.tp, p.has_above), push(part, part, self.sems.at[0, j], self.sems.at[2, j], p.above)),
            (jnp.logical_and(j >= p.tp, p.has_below), push(part, part, self.sems.at[1, j], self.sems.at[2, j], p.below)),
        )

    def start(self):
        for needed, copy in self.relays(self.place.tp):
            pl.when(needed)(copy.start)

    def step(self, k):
        j = self.place.nth_block(k)
        relays = self.relays(j)
        relays[0][1].wait_recv()
        for needed, copy in relays:
            pl.when(needed)(copy.start)

    def finish(self):
        for j in range(self.place.tps):
            for needed, copy in self.relays(j):
                pl.when(needed)(copy.wait_send)


class Reduce:
    KINDS = 8 + Spread.KINDS + 2

    def __init__(self, place, grads, halves, planes, lines, extras, totals, sems):
        self.place, self.grads, self.totals, self.sems = place, grads, totals, sems
        self.halves, self.planes, self.lines, self.extras = halves, planes, lines, extras
        self.unit = [ref.shape[1] // 8 for ref in grads]

    def sem(self, kind, g, j):
        return self.sems.at[kind, g, j]

    def rows(self, g, j, half, unit, count=1):
        size = self.unit[g]
        return rows_of(self.grads[g], j, (half * 4 + unit) * size, count * size)

    def move(self, g, j, stage):
        p, size = self.place, self.unit[g]
        if stage == 0:
            part, landing, device = self.rows(g, j, 1 - p.core, 0, 4), self.halves[g].at[j], p.sibling
        elif stage == 1:
            part, device = self.rows(g, j, p.core, 2 - p.first_bit * 2, 2), p.first
            landing = self.planes[g].at[j, pl.ds(0, 2 * size)]
        else:
            part, device = self.rows(g, j, p.core, p.first_bit * 2 + 1 - p.second_bit), p.second
            landing = self.planes[g].at[j, pl.ds(2 * size, size)]
        return push(part, landing, self.sem(2 * stage, g, j), self.sem(2 * stage + 1, g, j), device)

    def kept(self, g, j, stage):
        p, size = self.place, self.unit[g]
        if stage == 0:
            return self.rows(g, j, p.core, 0, 4), self.halves[g].at[j]
        if stage == 1:
            return self.rows(g, j, p.core, p.first_bit * 2, 2), self.planes[g].at[j, pl.ds(0, 2 * size)]
        return self.piece(g, j), self.planes[g].at[j, pl.ds(2 * size, size)]

    def piece(self, g, j):
        p = self.place
        return self.rows(g, j, p.core, p.first_bit * 2 + p.second_bit)

    def along(self, g, j):
        p = self.place
        return push(self.piece(g, j), self.lines[g].at[p.tp], self.sem(6, g, j), self.sem(7, g, p.tp), p.along(j))

    def from_place(self, g, j):
        p = self.place
        return push(self.piece(g, j), self.lines[g].at[j], self.sem(6, g, j), self.sem(7, g, j), p.along(j))

    def step(self, g, j, stage):
        if stage > 0:
            self.move(g, j, stage - 1).wait_recv()
            add_units(*self.kept(g, j, stage - 1), self.unit[g])
        if stage < 3:
            self.move(g, j, stage).start()
        else:
            pl.when(j != self.place.tp)(self.along(g, j).start)

    def spread(self, g):
        return Spread(
            self.place,
            lambda start, count: self.totals[g].at[pl.ds(pl.multiple_of(start, 16), count)],
            self.unit[g],
            lambda kind: self.sems.at[8 + kind, g, 0],
        )

    def copies(self, g, step):
        p = self.place
        base = self.KINDS - 2
        return push(
            self.piece(g, p.tp), self.extras[g].at[step], self.sem(base, g, step), self.sem(base + 1, g, step), p.copy_of(step)
        )

    def settle(self, g):
        p = self.place
        piece = self.piece(g, p.tp)
        total = piece[...].astype(F32)
        for k in range(p.tps - 1):
            j = p.nth_block(k)
            self.from_place(g, j).wait_recv()
            total = total + self.lines[g][j].astype(F32)
        if p.extra > 1:
            piece[...] = total.astype(BF16)
            for step in range(1, p.extra):
                self.copies(g, step).start()
            for step in range(1, p.extra):
                self.copies(g, step).wait()
                total = total + self.extras[g][step].astype(F32)
        own = self.spread(g).own()
        own[...] = total.astype(BF16)
        self.spread(g).step(0)

    def share(self, g, stage):
        self.spread(g).step(stage)

    def finish(self, g):
        p = self.place
        for j in range(p.tps):
            for stage in range(3):
                self.move(g, j, stage).wait_send()
            pl.when(j != p.tp)(self.along(g, j).wait_send)
        self.spread(g).finish()


class SumSmall:
    @staticmethod
    def slots(tps, extra):
        return 8 + tps + extra

    def __init__(self, place, slots, sems):
        self.place, self.slots_ref, self.sems = place, slots, sems

    def move(self, source, target, device, kind):
        slots = self.slots_ref
        return push(slots.at[source], slots.at[target], self.sems.at[0, kind], self.sems.at[1, target], device)

    def in_plane(self):
        p = self.place
        return [self.move(2, 3 + i, device, 3 + i) for i, device in enumerate((p.second, p.first, p.across))]

    def copies(self):
        p = self.place
        return [self.move(6, 8 + p.tps + s, p.copy_of(s), 8 + p.tps + s) for s in range(1, p.extra)]

    def along(self, k, lands=False):
        p = self.place
        j = p.nth_block(k)
        return self.move(7, 8 + (j if lands else p.tp), p.along(j), 8 + j)

    def start(self):
        self.move(0, 1, self.place.sibling, 1).start()

    def exchange(self, stage):
        p, slots = self.place, self.slots_ref
        if stage == 0:
            self.move(0, 1, p.sibling, 1).wait_recv()
            slots[2] = slots[0] + slots[1]
            for copy in self.in_plane():
                copy.start()
        else:
            for copy in self.in_plane():
                copy.wait_recv()
            slots[6] = (slots[2] + slots[3]) + (slots[4] + slots[5])
            for copy in self.copies():
                copy.start()
            total = slots[6]
            for s, copy in enumerate(self.copies()):
                copy.wait_recv()
                total = total + slots[9 + p.tps + s]
            slots[7] = total
            for k in range(p.tps - 1):
                self.along(k).start()

    def total(self):
        p, slots = self.place, self.slots_ref
        value = slots[7]
        for k in range(p.tps - 1):
            self.along(k, lands=True).wait_recv()
            value = value + slots[8 + p.nth_block(k)]
        return value

    def finish(self):
        p = self.place
        self.move(0, 1, p.sibling, 1).wait_send()
        for copy in self.in_plane() + self.copies():
            copy.wait_send()
        for k in range(p.tps - 1):
            self.along(k).wait_send()


def dot_nn(left, right):
    return lax.dot_general(left, right, (((1,), (0,)), ((), ())), preferred_element_type=F32)


def dot_nt(left, right):
    return lax.dot_general(left, right, (((1,), (1,)), ((), ())), preferred_element_type=F32)


def dot_tn(left, right):
    return lax.dot_general(left, right, (((0,), (0,)), ((), ())), preferred_element_type=F32)


def column(axis, shape):
    return lax.broadcasted_iota(jnp.int32, shape, axis)


def each(count, step):

    def run(i, carry):
        step(i)
        return carry

    lax.fori_loop(0, count, run, 0)


CHUNK = 128
CUBE = 0.044715
ROOT = 0.7978845608028654


def layer_kernel(r):
    r.a2, r.a3, r.e = (r.memory.at[i] for i in range(3))
    columns = pl.ds(0, r.x.shape[1])
    r.dh, r.dm = r.before.at[:, columns], r.down.at[:, columns]
    place = Place()
    n = place.tps
    x, model = r.x, r.x.shape[1]
    owned = x.shape[0]
    sentences = owned // LEN
    local = r.c[0].shape[1]
    heads_here = local // HD
    units = r.hidden.shape[1]
    layers = r.memory.shape[0]
    weights = r.w
    lengths, sources, configs = r.lengths, r.src_lengths, r.configs
    width, heads, hidden_units, depth = (configs[0, i] for i in range(4))
    inv_width = 1.0 / jnp.full((1, 1), width.astype(F32))
    inv_depth = 1.0 / jnp.full((1, 1), depth.astype(F32))
    width_mask = (column(1, (1, model)) < width).astype(F32)

    local_sem = r.local_sems
    spots = (
        (0, 0, 3 * local), (0, 3 * local, local),
        (1, 0, local), (1, local, 2 * local), (1, 3 * local, local),
        (2, 0, weights[2].shape[1]), (3, 0, weights[3].shape[1]),
    )
    fills = [
        (g, pltpu.make_async_copy(r.shards[i], weights[g].at[place.tp, pl.ds(start, size)], local_sem.at[i]))
        for i, (g, start, size) in enumerate(spots)
    ]
    loads = [
        pltpu.make_async_copy(source, target, local_sem.at[7 + i])
        for i, (source, target) in enumerate(((r.x_in, r.x), (r.memory_in, r.memory), (r.upstream_in, r.upstream)))
    ]
    for _, copy in fills[:2]:
        copy.start()
    loads[0].start()
    for _, copy in fills[2:]:
        copy.start()
    loads[1].start()
    loads[2].start()
    r.bias[place.tp] = jnp.broadcast_to(r.bias_in[...].reshape(1, units), r.bias.shape[1:])
    place.barrier()

    gather = Gather(place, weights, r.gather_sems)
    bias = Line(place, r.bias, r.bias_sems)
    for g in range(4):
        for group, copy in fills:
            if group == g:
                copy.wait()
        gather.start(g)
        if g == 0:
            bias.start()
    order = [(g, k) for g in (0, 1) for k in range(n - 1)] + [(g, k) for k in range(n - 1) for g in (2, 3)]

    def g_tick(tick):
        for stage in range(4):
            if 0 <= tick - stage < len(order):
                gather.step(*order[tick - stage], stage)

    def block(k):
        later = (k + n - 1) // n
        return (1 - later) * place.tp + later * place.nth_block(k - 1)

    def block_last(k):
        own = k // (n - 1)
        return own * place.tp + (1 - own) * place.nth_block((n - 2 - k) * (1 - own))

    def hooks(table, k, b):
        for (kk, bb), steps in table.items():

            @pl.when(jnp.logical_and(k == kk, b == bb))
            def _():
                for step in steps:
                    step()

    def chunk(i):
        return pl.ds(pl.multiple_of(i * CHUNK, CHUNK), CHUNK)

    def keep_of(i):
        per = LEN // CHUNK
        spot = column(0, (CHUNK, 1)) + (i % per) * CHUNK
        return (spot < lengths[place.tp * sentences + i // per]).astype(F32) * width_mask

    def norm_parts(rows):
        mean = jnp.sum(rows * width_mask, axis=-1, keepdims=True) * inv_width
        centred = (rows - mean) * width_mask
        spread = jnp.sum(centred * centred, axis=-1, keepdims=True) * inv_width
        rstd = lax.rsqrt(spread + EPSILON)
        return centred * rstd, rstd

    def norm(rows, which):
        hat, _ = norm_parts(rows)
        return ((hat * r.gains[which:which + 1] + r.shifts[which:which + 1]) * width_mask).astype(BF16)

    def fold(values):
        return jnp.sum(values.reshape(values.shape[0] // 8, 8, values.shape[1]), axis=0)

    def norm_backward(rows, which, upstream):
        hat, rstd = norm_parts(rows)
        upstream = upstream * width_mask
        sums = r.norm_sums
        sums[which] = sums[which] + fold(upstream * hat)
        sums[3 + which] = sums[3 + which] + fold(upstream)
        scaled = upstream * r.gains[which:which + 1]
        first = jnp.sum(scaled, axis=-1, keepdims=True) * inv_width
        second = jnp.sum(scaled * hat, axis=-1, keepdims=True) * inv_width
        return (rstd * (scaled - first - hat * second)) * width_mask

    chunks = owned // CHUNK

    def each_chunk(step):
        each(chunks, step)

    acc, da, dh = r.acc, r.da, r.dh
    zeros = jnp.zeros((CHUNK, model), F32)
    r.norm_sums[...] = jnp.zeros(r.norm_sums.shape, F32)
    r.bias_sums[...] = jnp.zeros(r.bias_sums.shape, F32)

    def sentence(b):
        return pl.ds(pl.multiple_of(b * LEN, LEN), LEN)

    def head_keep(j, h):
        return jnp.where(j * heads_here + h < heads, 1.0, 0.0).astype(F32)

    def causal(b, start, size):
        return column(0, (size, 128)) <= column(1, (size, 128)) + start

    def crossing(b, start, size):
        return column(0, (size, 1)) < sources[place.tp * sentences + b]

    def reach(g, start):
        return start + 128 if g == 0 else LEN

    def bands(h):
        return [pl.ds(i * local + h * HD, HD) for i in range(3)]

    def lanes(b):
        return pl.ds(b * LEN, LEN)

    pairs = [(b, h) for b in range(sentences) for h in range(heads_here)]

    quarters = [(i, b, h, start) for i, (b, h) in enumerate(pairs) for start in range(0, LEN, 128)]

    def attend(k, table, g, allowed):
        w, t, c, p = weights[g], r.t[g], r.c[g], r.p[g]
        j = block(k)
        hooks(table, k, 0)
        if g == 0:
            t[j] = dot_nt(w[j, :3 * local], r.a1[...]).astype(BF16)
        else:
            t[j, :local] = dot_nt(w[j, :local], r.a2[...]).astype(BF16)
            t[j, local:] = dot_nt(w[j, local:3 * local], r.m[...]).astype(BF16)
        heads_of = [[t[j, band, lanes(b)] for band in bands(h)] for b, h in pairs]
        for i, (query, keys, _) in enumerate(heads_of):
            r.scores[i] = dot_tn(keys, query)
        for i, b, h, start in quarters:
            part, size = pl.ds(start, 128), reach(g, start)
            score = jnp.where(allowed(b, start, size), r.scores[i, :size, part], NEGATIVE)
            raised = jnp.exp2((score - jnp.max(score, axis=0, keepdims=True)) * (SCALE * LOG2E))
            p[j, i, :size, part] = (raised * (1.0 / jnp.sum(raised, axis=0, keepdims=True))).astype(BF16)
            if size < LEN:
                p[j, i, size:, part] = jnp.zeros((LEN - size, 128), BF16)
        for i, (b, h) in enumerate(pairs):
            c[j, pl.ds(h * HD, HD), lanes(b)] = (dot_nn(heads_of[i][2], p[j, i]) * head_keep(j, h)).astype(BF16)
        hooks(table, k, 1)
        acc[...] = acc[...] + dot_tn(c[j], w[j, 3 * local:])

    def attend_backward(k, table, g, query_rows, key_rows):
        w, t, c, p = weights[g], r.t[g], r.c[g], r.p[g]
        j = block_last(k)
        e, dt, dc = r.e, r.dt, r.dc
        dc_all = dot_nt(w[j, 3 * local:], e[...])
        for h in range(heads_here):
            dc[h * HD:(h + 1) * HD] = (dc_all[h * HD:(h + 1) * HD] * head_keep(j, h)).astype(BF16)
        heads_of = [[t[j, band, lanes(b)] for band in bands(h)] for b, h in pairs]
        dc_of = [dc[h * HD:(h + 1) * HD, lanes(b)] for b, h in pairs]
        for i, (_, _, values) in enumerate(heads_of):
            r.scores[i] = dot_tn(values, dc_of[i])
        for i, b, h, start in quarters:
            part, size = pl.ds(start, 128), reach(g, start)
            dp, wide = r.scores[i, :size, part], p[j, i, :size, part].astype(F32)
            r.ds[i, :size, part] = (wide * (dp - jnp.sum(dp * wide, axis=0, keepdims=True))).astype(BF16)
            if size < LEN:
                r.ds[i, size:, part] = jnp.zeros((LEN - size, 128), BF16)
        for i, (b, h) in enumerate(pairs):
            (query, keys, _), (dq, dk, dv) = heads_of[i], bands(h)
            dt[dv, lanes(b)] = dot_nt(dc_of[i], p[j, i]).astype(BF16)
            dt[dq, lanes(b)] = (dot_nn(keys, r.ds[i]) * SCALE).astype(BF16)
            dt[dk, lanes(b)] = (dot_nt(query, r.ds[i]) * SCALE).astype(BF16)
        hooks(table, k, 1)
        gather.drain(g, j)
        if g == 0:
            da[...] = da[...] + dot_tn(dt[...], w[j, :3 * local])
            w[j, :3 * local] = dot_nn(dt[...], query_rows[...]).astype(BF16)
        else:
            da[...] = da[...] + dot_tn(dt[:local], w[j, :local])
            r.dm[...] = r.dm[...] + dot_tn(dt[local:], w[j, local:3 * local])
            w[j, :local] = dot_nn(dt[:local], query_rows[...]).astype(BF16)
            w[j, local:3 * local] = dot_nn(dt[local:], key_rows[...]).astype(BF16)
        w[j, 3 * local:] = dot_nn(c[j], e[...]).astype(BF16)

    def feed(k, table):
        j = block(k)
        w_up, w_down = weights[2], weights[3]
        hooks(table, k, 0)
        r.before[...] = dot_nn(r.a3[...], w_up[j]) + r.bias[j, 0:1]
        r.down[...] = dot_nt(r.e[...], w_down[j])
        step_lanes = units // 2

        def bend(i):
            for start in range(0, units, step_lanes):
                part = pl.ds(start, step_lanes)
                unit = column(1, (1, step_lanes)) + (j * units + start)
                kept = jnp.where(unit < hidden_units, 0.5, 0.0)
                sums = r.bias_sums[j, :, part]
                for line in range(4):
                    rows = pl.ds(pl.multiple_of(i * 64, 64) + line * 16, 16)
                    before = r.before[rows, part]
                    square = before * before
                    bent = jnp.tanh(before * (ROOT + ROOT * CUBE * square))
                    half = kept + kept * bent
                    through = before * half
                    r.hidden[rows, part] = through.astype(BF16)
                    slope = half + (through - through * bent) * (ROOT + 3.0 * CUBE * ROOT * square)
                    du = (r.down[rows, part] * slope).astype(BF16)
                    r.dhidden[rows, part] = du
                    sums = sums + fold(du.astype(F32))
                r.bias_sums[j, :, part] = sums

        each(owned // 64, bend)
        hooks(table, k, 1)
        acc[...] = acc[...] + dot_nn(r.hidden[...], w_down[j])
        da[...] = da[...] + dot_nt(r.dhidden[...], w_up[j])
        gather.drain(2, j)
        gather.drain(3, j)
        w_down[j] = dot_tn(r.hidden[...], r.e[...]).astype(BF16)
        w_up[j] = dot_nn(r.a3t[...], r.dhidden[...]).astype(BF16)

    loads[0].wait()

    def begin(i):
        rows = chunk(i)
        r.a1[rows] = norm(x[rows].astype(F32), 0)
        acc[rows] = zeros
        da[rows] = zeros

    each_chunk(begin)
    g_tick(0)
    loads[1].wait()

    def mix(i):
        rows = chunk(i)
        total = jnp.zeros((CHUNK, model), F32)
        for level in range(layers):
            chosen = (jnp.full((1, 1), depth) >= layers - level).astype(F32)
            total = total + chosen * r.memory[level, rows].astype(F32)
        r.m[rows] = (total * inv_depth * width_mask).astype(BF16)

    each_chunk(mix)
    g_tick(1)
    loads[2].wait()
    r.out_sums[...] = jnp.zeros(r.out_sums.shape, F32)

    def grad_in(i):
        rows = chunk(i)
        masked = r.upstream[rows].astype(F32) * keep_of(i)
        r.out_sums[...] = r.out_sums[...] + fold(masked)
        r.e[rows] = masked.astype(BF16)

    each_chunk(grad_in)
    g_tick(2)

    def ticks(*numbers):
        return [functools.partial(g_tick, i) for i in numbers]

    others = n - 1
    assert n == 4
    table = {
        (0, 1): ticks(3),
        (1, 0): ticks(4) + [functools.partial(bias.step, 0)],
        (1, 1): ticks(5),
        (2, 0): [functools.partial(bias.step, 1)],
        (2, 1): ticks(6),
        (3, 0): [functools.partial(bias.step, 2)],
        (3, 1): ticks(7),
    }
    each(n, lambda k: attend(k, table, 0, causal))

    def after_self(i):
        rows = chunk(i)
        h = x[rows].astype(F32) + acc[rows] * keep_of(i)
        r.h1[rows] = h
        r.a2[rows] = norm(h, 1)
        acc[rows] = zeros

    each_chunk(after_self)
    table2 = {(0, 0): ticks(8), (0, 1): ticks(9), (1, 1): ticks(10), (2, 1): ticks(11), (3, 1): ticks(12)}
    each(n, lambda k: attend(k, table2, 1, crossing))

    def after_cross(i):
        rows = chunk(i)
        h = r.h1[rows] + acc[rows] * keep_of(i)
        r.h2[rows] = h
        r.a3[rows] = norm(h, 2)
        acc[rows] = zeros

    each_chunk(after_cross)
    r.a3t[...] = r.a3[...].T

    reduce = Reduce(
        place, weights, r.half, r.plane, r.line, r.extra, r.total, r.reduce_sems
    )
    plan = {}

    def add(tick, order, step, *args):
        plan.setdefault(tick, []).append((order, len(plan.get(tick, ())), functools.partial(step, *args)))

    def r_tick(tick):
        for _, _, step in sorted(plan.get(tick, ()), key=lambda entry: entry[:2]):
            step()

    def store(g):
        return pltpu.make_async_copy(r.total[g], r.blocks[g], local_sem.at[10 + g])

    times = {
        3: ([(1, 2, 4, 7), (3, 4, 6, 9), (5, 6, 8, 10), (7, 9, 10, 12)], (14, 15, 17, 18)),
        2: ([(1, 3, 5, 8), (3, 5, 7, 9), (5, 7, 9, 11), (7, 9, 11, 13)], (15, 16, 18, 19)),
        1: ([(10, 11, 13, 15), (12, 13, 15, 17), (14, 15, 17, 19), (16, 17, 18, 20)], (21, 22, 23, 24)),
        0: ([(19, 20, 21, 23), (21, 22, 23, 24), (23, 24, 25, 26), (25, 26, 27, 28)], (28, 29, 30, 31)),
    }
    for late, g in enumerate((3, 2, 1, 0)):
        for k, stages in enumerate(times[g][0]):
            j = block(k) if g > 1 else block_last(k)
            for stage, tick in enumerate(stages):
                add(tick, stage, reduce.step, g, j, stage)
        for stage, tick in enumerate(times[g][1]):
            if stage == 0:
                add(tick, 20 - late, reduce.settle, g)
            else:
                add(tick, 30 + stage - late, reduce.share, g, stage)
        add(times[g][1][-1], 50, lambda g=g: store(g).start())

    def reduce_ticks(*numbers):
        return [functools.partial(r_tick, i) for i in numbers]

    def at_end(k, numbers):
        for kk, number in enumerate(numbers):

            @pl.when(k == kk)
            def _():
                r_tick(number)

    table3 = {(0, 0): ticks(13), (0, 1): ticks(14), (1, 1): reduce_ticks(2), (2, 1): reduce_ticks(4), (3, 1): reduce_ticks(6)}

    def feed_step(k):
        feed(k, table3)
        at_end(k, [2 * i + 1 for i in range(n)])

    each(n, feed_step)
    r_tick(8)
    out_copy = pltpu.make_async_copy(acc, r.layer_out, local_sem.at[14])

    def after_feed(i):
        rows = chunk(i)
        keep = keep_of(i)
        acc[rows] = r.h2[rows] + (acc[rows] + r.bias_out[...].reshape(1, model)) * keep
        down = r.upstream[rows].astype(F32) + norm_backward(r.h2[rows], 2, da[rows])
        dh[rows] = down
        r.e[rows] = (down * keep).astype(BF16)
        da[rows] = zeros
        r.dm[rows] = zeros

    each_chunk(after_feed)
    out_copy.start()
    table4 = {(k, 1): reduce_ticks(9 + 2 * k) for k in range(n)}

    def cross_step(k):
        attend_backward(k, table4, 1, r.a2, r.m)
        at_end(k, [10 + 2 * i for i in range(n)])

    each(n, cross_step)
    memory_copy = pltpu.make_async_copy(r.dm, r.memory_out, local_sem.at[15])
    memory_copy.start()

    def before_cross(i):
        rows = chunk(i)
        down = dh[rows] + norm_backward(r.h1[rows], 1, da[rows])
        dh[rows] = down
        r.e[rows] = (down * keep_of(i)).astype(BF16)
        da[rows] = zeros

    each_chunk(before_cross)
    r_tick(17)
    table5 = {(k, 1): reduce_ticks(18 + 2 * k) for k in range(n)}

    def self_step(k):
        attend_backward(k, table5, 0, r.a1, r.a1)
        at_end(k, [19 + 2 * i for i in range(n)])

    each(n, self_step)

    def before_self(i):
        rows = chunk(i)
        dh[rows] = dh[rows] + norm_backward(x[rows].astype(F32), 0, da[rows])

    each_chunk(before_self)
    grad_copy = pltpu.make_async_copy(dh, r.input_grad, local_sem.at[16])
    grad_copy.start()

    small = SumSmall(place, r.slots, r.small_sems)

    def small_start():
        own = r.slots.at[0]
        own[...] = jnp.zeros(own.shape, F32)
        for i in range(6):
            own[i:i + 1, :model] = jnp.sum(r.norm_sums[i], axis=0, keepdims=True)
        own[6:7, :model] = jnp.sum(r.out_sums[...], axis=0, keepdims=True)
        tokens = lengths[place.tp * sentences]
        for b in range(1, sentences):
            tokens = tokens + lengths[place.tp * sentences + b]
        own[7:8] = jnp.full((1, own.shape[1]), tokens.astype(F32))
        for i in range(n):
            own[8 + i:9 + i] = jnp.sum(r.bias_sums[i], axis=0, keepdims=True)
        small.start()

    add(26, 5, small_start)
    for stage in range(2):
        add(27 + stage, 5, small.exchange, stage)
    final = max(plan)
    for tick in range(26, final + 1):
        r_tick(tick)
    r.small_out[...] = small.total()
    bias.finish()
    for copy in (out_copy, memory_copy, grad_copy):
        copy.wait()
    for g in range(4):
        reduce.finish(g)
        store(g).wait()
    small.finish()


def call(kernel, name, ins, outs, scratch, spaces, **options):
    trees = (ins, outs, scratch)
    structure = jax.tree_util.tree_structure(trees)

    def body(*refs):
        groups = jax.tree_util.tree_unflatten(structure, refs)
        kernel(types.SimpleNamespace(**groups[0], **groups[1], **groups[2]))

    def specs(group):
        return [
            pl.BlockSpec(memory_space=spaces.get(key, pltpu.VMEM))
            for key in sorted(group) for _ in jax.tree_util.tree_leaves(group[key])
        ]

    leaves = jax.tree_util.tree_leaves
    values = pl.pallas_call(
        body,
        out_shape=leaves(outs),
        in_specs=specs(ins),
        out_specs=specs(outs),
        scratch_shapes=leaves(scratch),
        compiler_params=pltpu.CompilerParams(**options),
        name=name,
    )(*leaves(ins))
    return types.SimpleNamespace(**jax.tree_util.tree_unflatten(jax.tree_util.tree_structure(outs), values))


def run_layer(ins):
    n, extra = lax.axis_size("tp"), lax.axis_size("dp") // 2
    owned, model = ins["x_in"].shape
    memory, shards = ins["memory_in"], ins["shards"]
    local, units = shards[1].shape[0], ins["bias_in"].shape[0]
    small = (16, units)
    assert n <= 8 and units >= model and memory.shape[0] >= 3
    shapes = [(n, 4 * local, model)] * 2 + [(n,) + shards[5].shape, (n,) + shards[6].shape]
    small_slots = SumSmall.slots(n, extra)

    def vmem(*shape):
        return pltpu.VMEM(shape, BF16)

    def wide(*shape):
        return pltpu.VMEM(shape, F32)

    def eighths(*lead, parts=1):
        return [vmem(*lead, rows * parts // 8, columns) for _, rows, columns in shapes]

    dma = pltpu.SemaphoreType.DMA
    scratch = dict(
        w=[vmem(*shape) for shape in shapes],
        bias=wide(n, 8, units),
        x=vmem(owned, model),
        memory=vmem(*memory.shape),
        upstream=vmem(owned, model),
        a1=vmem(owned, model),
        m=vmem(owned, model),
        h1=wide(owned, model),
        h2=wide(owned, model),
        acc=wide(owned, model),
        da=wide(owned, model),
        t=[vmem(n, 3 * local, owned)] * 2,
        c=[vmem(n, local, owned)] * 2,
        p=[vmem(n, owned // LEN * (local // HD), LEN, LEN)] * 2,
        dt=vmem(3 * local, owned),
        dc=vmem(local, owned),
        a3t=vmem(model, owned),
        scores=wide(owned // LEN * (local // HD), LEN, LEN),
        ds=vmem(owned // LEN * (local // HD), LEN, LEN),
        before=wide(owned, units),
        down=wide(owned, units),
        hidden=vmem(owned, units),
        dhidden=vmem(owned, units),
        bias_sums=wide(n, 8, units),
        norm_sums=wide(6, 8, model),
        out_sums=wide(8, model),
        half=eighths(n, parts=4),
        plane=eighths(n, parts=3),
        line=eighths(n),
        extra=eighths(extra),
        total=eighths(parts=8),
        slots=wide(small_slots, *small),
        gather_sems=dma((Gather.KINDS, 4, n)),
        bias_sems=dma((3, n)),
        reduce_sems=dma((Reduce.KINDS, 4, max(n, extra))),
        small_sems=dma((2, small_slots)),
        local_sems=dma((17,)),
    )
    rows = jax.ShapeDtypeStruct((owned, model), F32)
    outs = dict(
        layer_out=rows, input_grad=rows, memory_out=rows, small_out=jax.ShapeDtypeStruct(small, F32),
        blocks=[jax.ShapeDtypeStruct(shape[1:], BF16) for shape in shapes],
    )
    smem, hbm = pltpu.SMEM, pl.ANY
    spaces = dict(
        lengths=smem, src_lengths=smem, configs=smem, x_in=hbm, memory_in=hbm, upstream_in=hbm, shards=hbm,
        layer_out=hbm, input_grad=hbm, memory_out=hbm, blocks=hbm,
    )
    return call(
        layer_kernel, "layer", ins, outs, scratch, spaces,
        collective_id=1, has_side_effects=True, vmem_limit_bytes=64 * 2**20,
    )


def finish_kernel(r):
    small, configs, sems = r.small, r.configs, r.sems
    model = r.gain_grad.shape[1]
    layers = r.memory_grad.shape[0]
    place = lax.axis_index("tp")
    local = r.grads[1].shape[0]
    parts = (
        (0, 0, 3 * local), (0, 3 * local, local),
        (1, 0, local), (1, local, 2 * local), (1, 3 * local, local),
        (2, 0, r.block[2].shape[0]), (3, 0, r.block[3].shape[0]),
    )
    loads = [pltpu.make_async_copy(r.blocks[g], r.block[g], sems.at[g]) for g in range(4)]
    rows = [
        pltpu.make_async_copy(source, target, sems.at[4 + i])
        for i, (source, target) in enumerate(((r.layer_in, r.layer), (r.grad_in, r.grad), (r.source_in, r.source)))
    ]
    outs = [pltpu.make_async_copy(r.layer, r.layer_out, sems.at[7]), pltpu.make_async_copy(r.grad, r.input_grad, sems.at[8])]
    for copy in rows + loads:
        copy.start()
    inverse = 1.0 / small[7:8, :1]
    r.gain_grad[...] = small[:3, :model] * inverse
    r.shift_grad[...] = small[3:6, :model] * inverse
    r.bias_out_grad[...] = (small[6:7, :model] * inverse).reshape(model)
    r.bias_in_grad[...] = (small[pl.ds(8 + place, 1)] * inverse).reshape(small.shape[1])
    width, depth = configs[0, 0], configs[0, 3]
    factor = (column(1, (1, model)) < width).astype(F32) / jnp.full((1, 1), depth.astype(F32))
    for i in range(2):
        rows[i].wait()
        outs[i].start()
    rows[2].wait()

    def spread(i):
        part = pl.ds(pl.multiple_of(i * 64, 64), 64)
        value = r.source[part] * factor
        for level in range(layers):
            chosen = (jnp.full((1, 1), depth) >= layers - level).astype(F32)
            r.memories[level, part] = value * chosen

    each(r.source.shape[0] // 64, spread)
    outs.append(pltpu.make_async_copy(r.memories, r.memory_grad, sems.at[9]))
    outs[2].start()
    for i, (g, start, count) in enumerate(parts):
        if start == 0:
            loads[g].wait()

        size = 80 if count % 80 == 0 else 96

        def scale(at):
            there = pl.ds(pl.multiple_of(start + at * size, 16), size)
            r.wide[g][there] = r.block[g][there].astype(F32) * inverse

        each(count // size, scale)
        outs.append(pltpu.make_async_copy(r.wide[g].at[pl.ds(start, count)], r.grads[i], sems.at[10 + i]))
        outs[-1].start()
    for copy in outs:
        copy.wait()


def run_finish(ins, layers):
    blocks, small = ins["blocks"], ins["small"]
    rows = ins["layer_in"].shape
    local, units = blocks[0].shape[0] // 4, small.shape[1]

    def shape(*dims):
        return jax.ShapeDtypeStruct(dims, F32)

    counts = (3 * local, local, local, 2 * local, local)
    outs = dict(
        layer_out=shape(*rows), input_grad=shape(*rows), memory_grad=shape(layers, *rows),
        gain_grad=shape(3, rows[1]), shift_grad=shape(3, rows[1]), bias_in_grad=shape(units), bias_out_grad=shape(rows[1]),
        grads=[shape(count, rows[1]) for count in counts] + [shape(*blocks[2].shape), shape(*blocks[3].shape)],
    )
    scratch = dict(
        layer=pltpu.VMEM(rows, F32), grad=pltpu.VMEM(rows, F32), source=pltpu.VMEM(rows, F32),
        memories=pltpu.VMEM((layers,) + rows, F32),
        block=[pltpu.VMEM(block.shape, BF16) for block in blocks],
        wide=[pltpu.VMEM(block.shape, F32) for block in blocks],
        sems=pltpu.SemaphoreType.DMA((17,)),
    )
    hbm = pl.ANY
    spaces = dict(
        configs=pltpu.SMEM, layer_in=hbm, grad_in=hbm, source_in=hbm, blocks=hbm,
        layer_out=hbm, input_grad=hbm, memory_grad=hbm, grads=hbm,
    )
    return call(finish_kernel, "finish", ins, outs, scratch, spaces, vmem_limit_bytes=60 * 2**20)


def per_device(
    inputs, memory, out_grad, lengths, src_lengths, configs, norm_gain, norm_bias,
    self_qkv, self_out, cross_q, cross_kv, cross_out, ffn_in, ffn_in_bias, ffn_out, ffn_out_bias,
):
    model = inputs.shape[1]
    layers = memory.shape[0]
    local = self_out.shape[0]
    done = run_layer(dict(
        lengths=lengths, src_lengths=src_lengths, configs=configs, gains=norm_gain, shifts=norm_bias,
        bias_in=ffn_in_bias, bias_out=ffn_out_bias, x_in=inputs, memory_in=memory, upstream_in=out_grad,
        shards=[
            self_qkv.transpose(1, 2, 0).reshape(3 * local, model), self_out, cross_q.T,
            cross_kv.transpose(1, 2, 0).reshape(2 * local, model), cross_out, ffn_in, ffn_out,
        ],
    ))
    out = run_finish(dict(
        configs=configs, small=done.small_out, layer_in=done.layer_out, grad_in=done.input_grad,
        source_in=done.memory_out, blocks=done.blocks,
    ), layers)
    grads = out.grads
    return (
        out.layer_out,
        out.input_grad,
        out.memory_grad,
        out.gain_grad,
        out.shift_grad,
        grads[0].reshape(3, local, model).transpose(2, 0, 1),
        grads[1],
        grads[2].T,
        grads[3].reshape(2, local, model).transpose(2, 0, 1),
        grads[4],
        grads[5],
        out.bias_in_grad,
        grads[6],
        out.bias_out_grad,
    )


def solution(mesh):
    rows = P(("grp", "dp", "tp"), None)
    stack = P(None, ("grp", "dp", "tp"), None)
    weights = (
        P(None, None, "tp"), P("tp", None), P(None, "tp"), P(None, None, "tp"), P("tp", None),
        P(None, "tp"), P("tp"), P("tp", None), P(),
    )
    return jax.shard_map(
        per_device,
        mesh=mesh,
        in_specs=(rows, stack, rows, P(("grp", "dp")), P(("grp", "dp")), P("grp", None), P(), P()) + weights,
        out_specs=(rows, rows, stack, P(), P()) + weights,
        check_vma=False,
    )
```

```python
import functools
import types

import jax
import jax.numpy as jnp
from jax import lax
from jax.experimental import pallas as pl
from jax.experimental.pallas import tpu as pltpu
from jax.sharding import PartitionSpec as P

HD = 80
LEN = 256
EPSILON = 1e-05
NEGATIVE = -1e30
SCALE = HD ** (-0.5)
LOG2E = 1.4426950408889634
F32 = jnp.float32
BF16 = jnp.bfloat16


MESH = pl.DeviceIdType.MESH


class Place:
    def __init__(self):
        self.tps = lax.axis_size("tp")
        self.extra = lax.axis_size("dp") // 2
        assert lax.axis_size("grp") == 4 and lax.axis_size("dp") % 2 == 0
        grp, dp, tp = (lax.axis_index(name) for name in ("grp", "dp", "tp"))
        core, low, high = dp % 2, grp % 2, grp // 2
        flip_low, flip_high = grp + 1 - 2 * low, grp + 2 - 4 * high
        self.grp, self.dp, self.tp, self.core = grp, dp, tp, core
        self.first_bit = (1 - core) * low + core * high
        self.second_bit = (1 - core) * high + core * low
        self.first = ((1 - core) * flip_low + core * flip_high, dp, tp)
        self.second = ((1 - core) * flip_high + core * flip_low, dp, tp)
        self.across = (3 - grp, dp, tp)
        self.sibling = (grp, dp + 1 - 2 * core, tp)
        self.above = (grp, dp, tp + 1)
        self.below = (grp, dp, tp - 1)
        self.has_above = tp < self.tps - 1
        self.has_below = tp > 0

    def copy_of(self, step):
        return (self.grp, ((self.dp // 2 + step) % self.extra) * 2 + self.core, self.tp)

    def nth_block(self, k):
        size = self.tps
        upper = (2 * self.tp) // size
        lead = (1 - upper) * self.tp + upper * (size - 1 - self.tp)
        spot = k + (k + size - lead) // size
        return (1 - upper) * spot + upper * (size - 1 - spot)

    def along(self, tp):
        return (self.grp, self.dp, tp)

    def barrier(self):
        sem = pltpu.get_barrier_semaphore()
        partners = [self.first, self.second, self.across, self.sibling]
        partners += [self.along((self.tp + step) % self.tps) for step in range(1, self.tps)]
        partners += [self.copy_of(step) for step in range(1, self.extra)]
        for device in partners:
            pl.semaphore_signal(sem, inc=1, device_id=device, device_id_type=MESH)
        pl.semaphore_wait(sem, len(partners))


def push(src, dst, send_sem, recv_sem, device):
    return pltpu.make_async_remote_copy(
        src_ref=src, dst_ref=dst, send_sem=send_sem, recv_sem=recv_sem, device_id=device, device_id_type=MESH
    )


def rows_of(ref, lead, start, count):
    return ref.at[lead, pl.ds(pl.multiple_of(start, 16), count)]


def add_units(total, term, unit):
    def step(i, carry):
        rows = pl.ds(pl.multiple_of(i * unit, 16), unit)
        total[rows] = total[rows] + term[rows]
        return carry

    lax.fori_loop(0, total.shape[0] // unit, step, 0)


class Spread:
    KINDS = 6

    def __init__(self, place, view, unit, sems):
        self.place, self.view, self.unit, self.sems = place, view, unit, sems
        f, s, c = place.first_bit, place.second_bit, place.core
        self.table = (
            (place.second, c * 4 + f * 2 + s, c * 4 + f * 2 + 1 - s, 1),
            (place.first, c * 4 + f * 2, c * 4 + 2 - f * 2, 2),
            (place.sibling, c * 4, 4 - c * 4, 4),
        )

    def region(self, start, count):
        return self.view(start * self.unit, count * self.unit)

    def own(self):
        return self.region(self.table[0][1], 1)

    def copy(self, n, lands=False):
        device, leaves, landing, count = self.table[n]
        part = self.region(landing if lands else leaves, count)
        return push(part, part, self.sems(2 * n), self.sems(2 * n + 1), device)

    def step(self, stage):
        if stage > 0:
            self.copy(stage - 1, lands=True).wait_recv()
        if stage < 3:
            self.copy(stage).start()

    def finish(self):
        for n in range(3):
            self.copy(n).wait_send()


class Gather:
    KINDS = Spread.KINDS + 3

    def __init__(self, place, buffers, sems):
        self.place, self.buffers, self.sems = place, buffers, sems
        self.unit = [ref.shape[1] // 8 for ref in buffers]
        self.others = place.tps - 1

    def spread(self, g, j):
        return Spread(
            self.place,
            lambda start, count: rows_of(self.buffers[g], j, start, count),
            self.unit[g],
            lambda kind: self.sems.at[kind, g, j],
        )

    def relays(self, g, j):
        p = self.place
        part = self.spread(g, j).own()
        sem = lambda n: self.sems.at[Spread.KINDS + n, g, j]
        return (
            (jnp.logical_and(j <= p.tp, p.has_above), push(part, part, sem(0), sem(2), p.above)),
            (jnp.logical_and(j >= p.tp, p.has_below), push(part, part, sem(1), sem(2), p.below)),
        )

    def start(self, g):
        for needed, copy in self.relays(g, self.place.tp):
            pl.when(needed)(copy.start)

    def step(self, g, k, stage):
        j = self.place.nth_block(k)
        if stage == 0:
            relays = self.relays(g, j)
            relays[0][1].wait_recv()
            for needed, copy in relays:
                pl.when(needed)(copy.start)
        self.spread(g, j).step(stage)

    def drain(self, g, j):
        for needed, copy in self.relays(g, j):
            pl.when(needed)(copy.wait_send)

        @pl.when(j != self.place.tp)
        def _():
            self.spread(g, j).finish()


class Line:
    def __init__(self, place, buffer, sems):
        self.place, self.buffer, self.sems = place, buffer, sems

    def relays(self, j):
        p = self.place
        part = self.buffer.at[j]
        return (
            (jnp.logical_and(j <= p.tp, p.has_above), push(part, part, self.sems.at[0, j], self.sems.at[2, j], p.above)),
            (jnp.logical_and(j >= p.tp, p.has_below), push(part, part, self.sems.at[1, j], self.sems.at[2, j], p.below)),
        )

    def start(self):
        for needed, copy in self.relays(self.place.tp):
            pl.when(needed)(copy.start)

    def step(self, k):
        j = self.place.nth_block(k)
        relays = self.relays(j)
        relays[0][1].wait_recv()
        for needed, copy in relays:
            pl.when(needed)(copy.start)

    def finish(self):
        for j in range(self.place.tps):
            for needed, copy in self.relays(j):
                pl.when(needed)(copy.wait_send)


class Reduce:
    KINDS = 8 + Spread.KINDS + 2

    def __init__(self, place, grads, halves, planes, lines, extras, totals, sems):
        self.place, self.grads, self.totals, self.sems = place, grads, totals, sems
        self.halves, self.planes, self.lines, self.extras = halves, planes, lines, extras
        self.unit = [ref.shape[1] // 8 for ref in grads]

    def sem(self, kind, g, j):
        return self.sems.at[kind, g, j]

    def rows(self, g, j, half, unit, count=1):
        size = self.unit[g]
        return rows_of(self.grads[g], j, (half * 4 + unit) * size, count * size)

    def move(self, g, j, stage):
        p, size = self.place, self.unit[g]
        if stage == 0:
            part, landing, device = self.rows(g, j, 1 - p.core, 0, 4), self.halves[g].at[j], p.sibling
        elif stage == 1:
            part, device = self.rows(g, j, p.core, 2 - p.first_bit * 2, 2), p.first
            landing = self.planes[g].at[j, pl.ds(0, 2 * size)]
        else:
            part, device = self.rows(g, j, p.core, p.first_bit * 2 + 1 - p.second_bit), p.second
            landing = self.planes[g].at[j, pl.ds(2 * size, size)]
        return push(part, landing, self.sem(2 * stage, g, j), self.sem(2 * stage + 1, g, j), device)

    def kept(self, g, j, stage):
        p, size = self.place, self.unit[g]
        if stage == 0:
            return self.rows(g, j, p.core, 0, 4), self.halves[g].at[j]
        if stage == 1:
            return self.rows(g, j, p.core, p.first_bit * 2, 2), self.planes[g].at[j, pl.ds(0, 2 * size)]
        return self.piece(g, j), self.planes[g].at[j, pl.ds(2 * size, size)]

    def piece(self, g, j):
        p = self.place
        return self.rows(g, j, p.core, p.first_bit * 2 + p.second_bit)

    def along(self, g, j):
        p = self.place
        return push(self.piece(g, j), self.lines[g].at[p.tp], self.sem(6, g, j), self.sem(7, g, p.tp), p.along(j))

    def from_place(self, g, j):
        p = self.place
        return push(self.piece(g, j), self.lines[g].at[j], self.sem(6, g, j), self.sem(7, g, j), p.along(j))

    def step(self, g, j, stage):
        if stage > 0:
            self.move(g, j, stage - 1).wait_recv()
            add_units(*self.kept(g, j, stage - 1), self.unit[g])
        if stage < 3:
            self.move(g, j, stage).start()
        else:
            pl.when(j != self.place.tp)(self.along(g, j).start)

    def spread(self, g):
        return Spread(
            self.place,
            lambda start, count: self.totals[g].at[pl.ds(pl.multiple_of(start, 16), count)],
            self.unit[g],
            lambda kind: self.sems.at[8 + kind, g, 0],
        )

    def copies(self, g, step):
        p = self.place
        base = self.KINDS - 2
        return push(
            self.piece(g, p.tp), self.extras[g].at[step], self.sem(base, g, step), self.sem(base + 1, g, step), p.copy_of(step)
        )

    def settle(self, g):
        p = self.place
        piece = self.piece(g, p.tp)
        total = piece[...].astype(F32)
        for k in range(p.tps - 1):
            j = p.nth_block(k)
            self.from_place(g, j).wait_recv()
            total = total + self.lines[g][j].astype(F32)
        if p.extra > 1:
            piece[...] = total.astype(BF16)
            for step in range(1, p.extra):
                self.copies(g, step).start()
            for step in range(1, p.extra):
                self.copies(g, step).wait()
                total = total + self.extras[g][step].astype(F32)
        own = self.spread(g).own()
        own[...] = total.astype(BF16)
        self.spread(g).step(0)

    def share(self, g, stage):
        self.spread(g).step(stage)

    def finish(self, g):
        p = self.place
        for j in range(p.tps):
            for stage in range(3):
                self.move(g, j, stage).wait_send()
            pl.when(j != p.tp)(self.along(g, j).wait_send)
        self.spread(g).finish()


class SumSmall:
    @staticmethod
    def slots(tps, extra):
        return 8 + tps + extra

    def __init__(self, place, slots, sems):
        self.place, self.slots_ref, self.sems = place, slots, sems

    def move(self, source, target, device, kind):
        slots = self.slots_ref
        return push(slots.at[source], slots.at[target], self.sems.at[0, kind], self.sems.at[1, target], device)

    def in_plane(self):
        p = self.place
        return [self.move(2, 3 + i, device, 3 + i) for i, device in enumerate((p.second, p.first, p.across))]

    def copies(self):
        p = self.place
        return [self.move(6, 8 + p.tps + s, p.copy_of(s), 8 + p.tps + s) for s in range(1, p.extra)]

    def along(self, k, lands=False):
        p = self.place
        j = p.nth_block(k)
        return self.move(7, 8 + (j if lands else p.tp), p.along(j), 8 + j)

    def start(self):
        self.move(0, 1, self.place.sibling, 1).start()

    def exchange(self, stage):
        p, slots = self.place, self.slots_ref
        if stage == 0:
            self.move(0, 1, p.sibling, 1).wait_recv()
            slots[2] = slots[0] + slots[1]
            for copy in self.in_plane():
                copy.start()
        else:
            for copy in self.in_plane():
                copy.wait_recv()
            slots[6] = (slots[2] + slots[3]) + (slots[4] + slots[5])
            for copy in self.copies():
                copy.start()
            total = slots[6]
            for s, copy in enumerate(self.copies()):
                copy.wait_recv()
                total = total + slots[9 + p.tps + s]
            slots[7] = total
            for k in range(p.tps - 1):
                self.along(k).start()

    def total(self):
        p, slots = self.place, self.slots_ref
        value = slots[7]
        for k in range(p.tps - 1):
            self.along(k, lands=True).wait_recv()
            value = value + slots[8 + p.nth_block(k)]
        return value

    def finish(self):
        p = self.place
        self.move(0, 1, p.sibling, 1).wait_send()
        for copy in self.in_plane() + self.copies():
            copy.wait_send()
        for k in range(p.tps - 1):
            self.along(k).wait_send()


def dot_nn(left, right):
    return lax.dot_general(left, right, (((1,), (0,)), ((), ())), preferred_element_type=F32)


def dot_nt(left, right):
    return lax.dot_general(left, right, (((1,), (1,)), ((), ())), preferred_element_type=F32)


def dot_tn(left, right):
    return lax.dot_general(left, right, (((0,), (0,)), ((), ())), preferred_element_type=F32)


def column(axis, shape):
    return lax.broadcasted_iota(jnp.int32, shape, axis)


def each(count, step):

    def run(i, carry):
        step(i)
        return carry

    lax.fori_loop(0, count, run, 0)


CHUNK = 128
CUBE = 0.044715
ROOT = 0.7978845608028654


def layer_kernel(r):
    r.a2, r.a3, r.e = (r.memory.at[i] for i in range(3))
    columns = pl.ds(0, r.x.shape[1])
    r.dh, r.dm = r.before.at[:, columns], r.down.at[:, columns]
    place = Place()
    n = place.tps
    x, model = r.x, r.x.shape[1]
    owned = x.shape[0]
    sentences = owned // LEN
    local = r.c[0].shape[1]
    heads_here = local // HD
    units = r.hidden.shape[1]
    layers = r.memory.shape[0]
    weights = r.w
    lengths, sources, configs = r.lengths, r.src_lengths, r.configs
    width, heads, hidden_units, depth = (configs[0, i] for i in range(4))
    inv_width = 1.0 / jnp.full((1, 1), width.astype(F32))
    inv_depth = 1.0 / jnp.full((1, 1), depth.astype(F32))
    width_mask = (column(1, (1, model)) < width).astype(F32)

    local_sem = r.local_sems
    spots = (
        (0, 0, 3 * local), (0, 3 * local, local),
        (1, 0, local), (1, local, 2 * local), (1, 3 * local, local),
        (2, 0, weights[2].shape[1]), (3, 0, weights[3].shape[1]),
    )
    fills = [
        (g, pltpu.make_async_copy(r.shards[i], weights[g].at[place.tp, pl.ds(start, size)], local_sem.at[i]))
        for i, (g, start, size) in enumerate(spots)
    ]
    loads = [
        pltpu.make_async_copy(source, target, local_sem.at[7 + i])
        for i, (source, target) in enumerate(((r.x_in, r.x), (r.memory_in, r.memory), (r.upstream_in, r.upstream)))
    ]
    for _, copy in fills[:2]:
        copy.start()
    loads[0].start()
    for _, copy in fills[2:]:
        copy.start()
    loads[1].start()
    loads[2].start()
    r.bias[place.tp] = jnp.broadcast_to(r.bias_in[...].reshape(1, units), r.bias.shape[1:])
    place.barrier()

    gather = Gather(place, weights, r.gather_sems)
    bias = Line(place, r.bias, r.bias_sems)
    for g in range(4):
        for group, copy in fills:
            if group == g:
                copy.wait()
        gather.start(g)
        if g == 0:
            bias.start()
    order = [(g, k) for g in (0, 1) for k in range(n - 1)] + [(g, k) for k in range(n - 1) for g in (2, 3)]

    def g_tick(tick):
        for stage in range(4):
            if 0 <= tick - stage < len(order):
                gather.step(*order[tick - stage], stage)

    def block(k):
        later = (k + n - 1) // n
        return (1 - later) * place.tp + later * place.nth_block(k - 1)

    def block_last(k):
        own = k // (n - 1)
        return own * place.tp + (1 - own) * place.nth_block(k)

    def hooks(table, k, b):
        for (kk, bb), steps in table.items():

            @pl.when(jnp.logical_and(k == kk, b == bb))
            def _():
                for step in steps:
                    step()

    def chunk(i):
        return pl.ds(pl.multiple_of(i * CHUNK, CHUNK), CHUNK)

    def keep_of(i):
        per = LEN // CHUNK
        spot = column(0, (CHUNK, 1)) + (i % per) * CHUNK
        return (spot < lengths[place.tp * sentences + i // per]).astype(F32) * width_mask

    def norm_parts(rows):
        mean = jnp.sum(rows * width_mask, axis=-1, keepdims=True) * inv_width
        centred = (rows - mean) * width_mask
        spread = jnp.sum(centred * centred, axis=-1, keepdims=True) * inv_width
        rstd = lax.rsqrt(spread + EPSILON)
        return centred * rstd, rstd

    def norm(rows, which):
        hat, _ = norm_parts(rows)
        return ((hat * r.gains[which:which + 1] + r.shifts[which:which + 1]) * width_mask).astype(BF16)

    def fold(values):
        return jnp.sum(values.reshape(values.shape[0] // 8, 8, values.shape[1]), axis=0)

    def norm_backward(rows, which, upstream):
        hat, rstd = norm_parts(rows)
        upstream = upstream * width_mask
        sums = r.norm_sums
        sums[which] = sums[which] + fold(upstream * hat)
        sums[3 + which] = sums[3 + which] + fold(upstream)
        scaled = upstream * r.gains[which:which + 1]
        first = jnp.sum(scaled, axis=-1, keepdims=True) * inv_width
        second = jnp.sum(scaled * hat, axis=-1, keepdims=True) * inv_width
        return (rstd * (scaled - first - hat * second)) * width_mask

    chunks = owned // CHUNK

    def each_chunk(step):
        each(chunks, step)

    acc, da, dh = r.acc, r.da, r.dh
    zeros = jnp.zeros((CHUNK, model), F32)
    r.norm_sums[...] = jnp.zeros(r.norm_sums.shape, F32)
    r.bias_sums[...] = jnp.zeros(r.bias_sums.shape, F32)

    def sentence(b):
        return pl.ds(pl.multiple_of(b * LEN, LEN), LEN)

    def head_keep(j, h):
        return jnp.where(j * heads_here + h < heads, 1.0, 0.0).astype(F32)

    def causal(b, start, size):
        return column(0, (size, 128)) <= column(1, (size, 128)) + start

    def crossing(b, start, size):
        return column(0, (size, 1)) < sources[place.tp * sentences + b]

    def reach(g, start):
        return start + 128 if g == 0 else LEN

    def bands(h):
        return [pl.ds(i * local + h * HD, HD) for i in range(3)]

    def lanes(b):
        return pl.ds(b * LEN, LEN)

    pairs = [(b, h) for b in range(sentences) for h in range(heads_here)]

    quarters = [(i, b, h, start) for i, (b, h) in enumerate(pairs) for start in range(0, LEN, 128)]

    def attend(k, table, g, allowed):
        w, t, c, p = weights[g], r.t[g], r.c[g], r.p[g]
        j = block(k)
        hooks(table, k, 0)
        if g == 0:
            t[j] = dot_nt(w[j, :3 * local], r.a1[...]).astype(BF16)
        else:
            t[j, :local] = dot_nt(w[j, :local], r.a2[...]).astype(BF16)
            t[j, local:] = dot_nt(w[j, local:3 * local], r.m[...]).astype(BF16)
        heads_of = [[t[j, band, lanes(b)] for band in bands(h)] for b, h in pairs]
        for i, (query, keys, _) in enumerate(heads_of):
            r.scores[i] = dot_tn(keys, query)
        for i, b, h, start in quarters:
            part, size = pl.ds(start, 128), reach(g, start)
            score = jnp.where(allowed(b, start, size), r.scores[i, :size, part], NEGATIVE)
            raised = jnp.exp2((score - jnp.max(score, axis=0, keepdims=True)) * (SCALE * LOG2E))
            p[j, i, :size, part] = (raised * (1.0 / jnp.sum(raised, axis=0, keepdims=True))).astype(BF16)
            if size < LEN:
                p[j, i, size:, part] = jnp.zeros((LEN - size, 128), BF16)
        for i, (b, h) in enumerate(pairs):
            c[j, pl.ds(h * HD, HD), lanes(b)] = (dot_nn(heads_of[i][2], p[j, i]) * head_keep(j, h)).astype(BF16)
        hooks(table, k, 1)
        acc[...] = acc[...] + dot_tn(c[j], w[j, 3 * local:])

    def attend_backward(k, table, g, query_rows, key_rows):
        w, t, c, p = weights[g], r.t[g], r.c[g], r.p[g]
        j = block_last(k)
        e, dt, dc = r.e, r.dt, r.dc
        gather.drain(g, j)
        dc_all = dot_nt(w[j, 3 * local:], e[...])
        for h in range(heads_here):
            dc[h * HD:(h + 1) * HD] = (dc_all[h * HD:(h + 1) * HD] * head_keep(j, h)).astype(BF16)
        heads_of = [[t[j, band, lanes(b)] for band in bands(h)] for b, h in pairs]
        dc_of = [dc[h * HD:(h + 1) * HD, lanes(b)] for b, h in pairs]
        for i, (_, _, values) in enumerate(heads_of):
            r.scores[i] = dot_tn(values, dc_of[i])
        for i, (b, h) in enumerate(pairs):
            dt[bands(h)[2], lanes(b)] = dot_nt(dc_of[i], p[j, i]).astype(BF16)
        w[j, 3 * local:] = dot_nn(c[j], e[...]).astype(BF16)
        for i, b, h, start in quarters:
            part, size = pl.ds(start, 128), reach(g, start)
            dp, wide = r.scores[i, :size, part], p[j, i, :size, part].astype(F32)
            r.ds[i, :size, part] = (wide * (dp - jnp.sum(dp * wide, axis=0, keepdims=True))).astype(BF16)
            if size < LEN:
                r.ds[i, size:, part] = jnp.zeros((LEN - size, 128), BF16)
        for i, (b, h) in enumerate(pairs):
            (query, keys, _), (dq, dk, _) = heads_of[i], bands(h)
            dt[dq, lanes(b)] = (dot_nn(keys, r.ds[i]) * SCALE).astype(BF16)
            dt[dk, lanes(b)] = (dot_nt(query, r.ds[i]) * SCALE).astype(BF16)
        hooks(table, k, 1)
        if g == 0:
            da[...] = da[...] + dot_tn(dt[...], w[j, :3 * local])
            w[j, :3 * local] = dot_nn(dt[...], query_rows[...]).astype(BF16)
        else:
            da[...] = da[...] + dot_tn(dt[:local], w[j, :local])
            r.dm[...] = r.dm[...] + dot_tn(dt[local:], w[j, local:3 * local])
            w[j, :local] = dot_nn(dt[:local], query_rows[...]).astype(BF16)
            w[j, local:3 * local] = dot_nn(dt[local:], key_rows[...]).astype(BF16)

    def feed(k, table):
        j = block(k)
        w_up, w_down = weights[2], weights[3]
        hooks(table, k, 0)
        unit = column(1, (1, units)) + j * units
        kept = jnp.where(unit < hidden_units, 0.5, 0.0)
        found = []
        for b in range(sentences):
            rows = sentence(b)
            found.append((dot_nn(r.a3[rows], w_up[j]) + r.bias[j, 0:1], dot_nt(r.e[rows], w_down[j])))
        for b, (before, down) in enumerate(found):
            rows = sentence(b)
            square = before * before
            bent = jnp.tanh(before * (ROOT + ROOT * CUBE * square))
            half = kept + kept * bent
            through = before * half
            r.hidden[rows] = through.astype(BF16)
            slope = half + (through - through * bent) * (ROOT + 3.0 * CUBE * ROOT * square)
            du = (down * slope).astype(BF16)
            r.dhidden[rows] = du
            r.bias_sums[j] = r.bias_sums[j] + fold(du.astype(F32))
        for b in range(sentences):
            rows = sentence(b)
            acc[rows] = acc[rows] + dot_nn(r.hidden[rows], w_down[j])
            da[rows] = da[rows] + dot_nt(r.dhidden[rows], w_up[j])
        hooks(table, k, 1)
        gather.drain(2, j)
        gather.drain(3, j)
        w_down[j] = dot_tn(r.hidden[...], r.e[...]).astype(BF16)
        w_up[j] = dot_nn(r.a3t[...], r.dhidden[...]).astype(BF16)

    loads[0].wait()

    def begin(i):
        rows = chunk(i)
        r.a1[rows] = norm(x[rows].astype(F32), 0)
        acc[rows] = zeros
        da[rows] = zeros

    each_chunk(begin)
    g_tick(0)
    loads[1].wait()

    def mix(i):
        rows = chunk(i)
        total = jnp.zeros((CHUNK, model), F32)
        for level in range(layers):
            chosen = (jnp.full((1, 1), depth) >= layers - level).astype(F32)
            total = total + chosen * r.memory[level, rows].astype(F32)
        r.m[rows] = (total * inv_depth * width_mask).astype(BF16)

    each_chunk(mix)
    g_tick(1)
    loads[2].wait()
    r.out_sums[...] = jnp.zeros(r.out_sums.shape, F32)

    def grad_in(i):
        rows = chunk(i)
        masked = r.upstream[rows].astype(F32) * keep_of(i)
        r.out_sums[...] = r.out_sums[...] + fold(masked)
        r.e[rows] = masked.astype(BF16)

    each_chunk(grad_in)
    g_tick(2)

    def ticks(*numbers):
        return [functools.partial(g_tick, i) for i in numbers]

    others = n - 1
    assert n == 4
    table = {
        (0, 1): ticks(3),
        (1, 0): ticks(4) + [functools.partial(bias.step, 0)],
        (1, 1): ticks(5),
        (2, 0): [functools.partial(bias.step, 1)],
        (2, 1): ticks(6),
        (3, 0): [functools.partial(bias.step, 2)],
        (3, 1): ticks(7),
    }
    each(n, lambda k: attend(k, table, 0, causal))

    def after_self(i):
        rows = chunk(i)
        h = x[rows].astype(F32) + acc[rows] * keep_of(i)
        r.h1[rows] = h
        r.a2[rows] = norm(h, 1)
        acc[rows] = zeros

    each_chunk(after_self)
    table2 = {(0, 0): ticks(8), (0, 1): ticks(9), (1, 1): ticks(10), (2, 1): ticks(11), (3, 1): ticks(12)}
    each(n, lambda k: attend(k, table2, 1, crossing))

    def after_cross(i):
        rows = chunk(i)
        h = r.h1[rows] + acc[rows] * keep_of(i)
        r.h2[rows] = h
        r.a3[rows] = norm(h, 2)
        acc[rows] = zeros

    each_chunk(after_cross)
    r.a3t[...] = r.a3[...].T

    reduce = Reduce(
        place, weights, r.half, r.plane, r.line, r.extra, r.total, r.reduce_sems
    )
    plan = {}

    def add(tick, order, step, *args):
        plan.setdefault(tick, []).append((order, len(plan.get(tick, ())), functools.partial(step, *args)))

    def r_tick(tick):
        for _, _, step in sorted(plan.get(tick, ()), key=lambda entry: entry[:2]):
            step()

    def store(g):
        return pltpu.make_async_copy(r.total[g], r.blocks[g], local_sem.at[10 + g])

    times = {
        3: ([(1, 2, 6, 10), (3, 4, 8, 11), (5, 6, 9, 13), (7, 9, 11, 15)], (17, 19, 21, 23)),
        2: ([(1, 3, 6, 9), (3, 6, 8, 11), (5, 8, 10, 13), (7, 9, 12, 16)], (18, 20, 22, 24)),
        1: ([(10, 11, 14, 16), (12, 14, 16, 18), (14, 15, 19, 21), (16, 17, 19, 21)], (23, 25, 27, 29)),
        0: ([(19, 20, 22, 24), (21, 22, 24, 25), (23, 24, 25, 26), (25, 26, 27, 28)], (28, 29, 30, 31)),
    }
    for late, g in enumerate((3, 2, 1, 0)):
        for k, stages in enumerate(times[g][0]):
            j = block(k) if g > 1 else block_last(k)
            for stage, tick in enumerate(stages):
                add(tick, stage, reduce.step, g, j, stage)
        for stage, tick in enumerate(times[g][1]):
            if stage == 0:
                add(tick, 20 - late, reduce.settle, g)
            else:
                add(tick, 30 + stage - late, reduce.share, g, stage)
        add(times[g][1][-1], 50, lambda g=g: store(g).start())

    def reduce_ticks(*numbers):
        return [functools.partial(r_tick, i) for i in numbers]

    def at_end(k, numbers):
        for kk, number in enumerate(numbers):

            @pl.when(k == kk)
            def _():
                r_tick(number)

    table3 = {(0, 0): ticks(13), (0, 1): ticks(14), (1, 1): reduce_ticks(2), (2, 1): reduce_ticks(4), (3, 1): reduce_ticks(6)}

    def feed_step(k):
        feed(k, table3)
        at_end(k, [2 * i + 1 for i in range(n)])

    each(n, feed_step)
    r_tick(8)
    out_copy = pltpu.make_async_copy(acc, r.layer_out, local_sem.at[14])

    def after_feed(i):
        rows = chunk(i)
        keep = keep_of(i)
        acc[rows] = r.h2[rows] + (acc[rows] + r.bias_out[...].reshape(1, model)) * keep
        down = r.upstream[rows].astype(F32) + norm_backward(r.h2[rows], 2, da[rows])
        dh[rows] = down
        r.e[rows] = (down * keep).astype(BF16)
        da[rows] = zeros
        r.dm[rows] = zeros

    each_chunk(after_feed)
    out_copy.start()
    table4 = {(k, 1): reduce_ticks(9 + 2 * k) for k in range(n)}

    def cross_step(k):
        attend_backward(k, table4, 1, r.a2, r.m)
        at_end(k, [10 + 2 * i for i in range(n)])

    each(n, cross_step)
    memory_copy = pltpu.make_async_copy(r.dm, r.memory_out, local_sem.at[15])
    memory_copy.start()

    def before_cross(i):
        rows = chunk(i)
        down = dh[rows] + norm_backward(r.h1[rows], 1, da[rows])
        dh[rows] = down
        r.e[rows] = (down * keep_of(i)).astype(BF16)
        da[rows] = zeros

    each_chunk(before_cross)
    r_tick(17)
    table5 = {(k, 1): reduce_ticks(18 + 2 * k) for k in range(n)}

    def self_step(k):
        attend_backward(k, table5, 0, r.a1, r.a1)
        at_end(k, [19 + 2 * i for i in range(n)])

    each(n, self_step)

    def before_self(i):
        rows = chunk(i)
        dh[rows] = dh[rows] + norm_backward(x[rows].astype(F32), 0, da[rows])

    each_chunk(before_self)
    grad_copy = pltpu.make_async_copy(dh, r.input_grad, local_sem.at[16])
    grad_copy.start()

    small = SumSmall(place, r.slots, r.small_sems)

    def small_start():
        own = r.slots.at[0]
        own[...] = jnp.zeros(own.shape, F32)
        for i in range(6):
            own[i:i + 1, :model] = jnp.sum(r.norm_sums[i], axis=0, keepdims=True)
        own[6:7, :model] = jnp.sum(r.out_sums[...], axis=0, keepdims=True)
        tokens = lengths[place.tp * sentences]
        for b in range(1, sentences):
            tokens = tokens + lengths[place.tp * sentences + b]
        own[7:8] = jnp.full((1, own.shape[1]), tokens.astype(F32))
        for i in range(n):
            own[8 + i:9 + i] = jnp.sum(r.bias_sums[i], axis=0, keepdims=True)
        small.start()

    add(26, 5, small_start)
    for stage in range(2):
        add(27 + stage, 5, small.exchange, stage)
    final = max(plan)
    for tick in range(26, final + 1):
        r_tick(tick)
    r.small_out[...] = small.total()
    bias.finish()
    for copy in (out_copy, memory_copy, grad_copy):
        copy.wait()
    for g in range(4):
        reduce.finish(g)
        store(g).wait()
    small.finish()


def call(kernel, name, ins, outs, scratch, spaces, **options):
    trees = (ins, outs, scratch)
    structure = jax.tree_util.tree_structure(trees)

    def body(*refs):
        groups = jax.tree_util.tree_unflatten(structure, refs)
        kernel(types.SimpleNamespace(**groups[0], **groups[1], **groups[2]))

    def specs(group):
        return [
            pl.BlockSpec(memory_space=spaces.get(key, pltpu.VMEM))
            for key in sorted(group) for _ in jax.tree_util.tree_leaves(group[key])
        ]

    leaves = jax.tree_util.tree_leaves
    values = pl.pallas_call(
        body,
        out_shape=leaves(outs),
        in_specs=specs(ins),
        out_specs=specs(outs),
        scratch_shapes=leaves(scratch),
        compiler_params=pltpu.CompilerParams(**options),
        name=name,
    )(*leaves(ins))
    return types.SimpleNamespace(**jax.tree_util.tree_unflatten(jax.tree_util.tree_structure(outs), values))


def run_layer(ins):
    n, extra = lax.axis_size("tp"), lax.axis_size("dp") // 2
    owned, model = ins["x_in"].shape
    memory, shards = ins["memory_in"], ins["shards"]
    local, units = shards[1].shape[0], ins["bias_in"].shape[0]
    small = (16, units)
    assert n <= 8 and units >= model and memory.shape[0] >= 3
    shapes = [(n, 4 * local, model)] * 2 + [(n,) + shards[5].shape, (n,) + shards[6].shape]
    small_slots = SumSmall.slots(n, extra)

    def vmem(*shape):
        return pltpu.VMEM(shape, BF16)

    def wide(*shape):
        return pltpu.VMEM(shape, F32)

    def eighths(*lead, parts=1):
        return [vmem(*lead, rows * parts // 8, columns) for _, rows, columns in shapes]

    dma = pltpu.SemaphoreType.DMA
    scratch = dict(
        w=[vmem(*shape) for shape in shapes],
        bias=wide(n, 8, units),
        x=vmem(owned, model),
        memory=vmem(*memory.shape),
        upstream=vmem(owned, model),
        a1=vmem(owned, model),
        m=vmem(owned, model),
        h1=wide(owned, model),
        h2=wide(owned, model),
        acc=wide(owned, model),
        da=wide(owned, model),
        t=[vmem(n, 3 * local, owned)] * 2,
        c=[vmem(n, local, owned)] * 2,
        p=[vmem(n, owned // LEN * (local // HD), LEN, LEN)] * 2,
        dt=vmem(3 * local, owned),
        dc=vmem(local, owned),
        a3t=vmem(model, owned),
        scores=wide(owned // LEN * (local // HD), LEN, LEN),
        ds=vmem(owned // LEN * (local // HD), LEN, LEN),
        before=wide(owned, units),
        down=wide(owned, units),
        hidden=vmem(owned, units),
        dhidden=vmem(owned, units),
        bias_sums=wide(n, 8, units),
        norm_sums=wide(6, 8, model),
        out_sums=wide(8, model),
        half=eighths(n, parts=4),
        plane=eighths(n, parts=3),
        line=eighths(n),
        extra=eighths(extra),
        total=eighths(parts=8),
        slots=wide(small_slots, *small),
        gather_sems=dma((Gather.KINDS, 4, n)),
        bias_sems=dma((3, n)),
        reduce_sems=dma((Reduce.KINDS, 4, max(n, extra))),
        small_sems=dma((2, small_slots)),
        local_sems=dma((17,)),
    )
    rows = jax.ShapeDtypeStruct((owned, model), F32)
    outs = dict(
        layer_out=rows, input_grad=rows, memory_out=rows, small_out=jax.ShapeDtypeStruct(small, F32),
        blocks=[jax.ShapeDtypeStruct(shape[1:], BF16) for shape in shapes],
    )
    smem, hbm = pltpu.SMEM, pl.ANY
    spaces = dict(
        lengths=smem, src_lengths=smem, configs=smem, x_in=hbm, memory_in=hbm, upstream_in=hbm, shards=hbm,
        layer_out=hbm, input_grad=hbm, memory_out=hbm, blocks=hbm,
    )
    return call(
        layer_kernel, "layer", ins, outs, scratch, spaces,
        collective_id=1, has_side_effects=True, vmem_limit_bytes=64 * 2**20,
    )


def finish_kernel(r):
    small, configs, sems = r.small, r.configs, r.sems
    model = r.gain_grad.shape[1]
    layers = r.memory_grad.shape[0]
    place = lax.axis_index("tp")
    local = r.grads[1].shape[0]
    parts = (
        (0, 0, 3 * local), (0, 3 * local, local),
        (1, 0, local), (1, local, 2 * local), (1, 3 * local, local),
        (2, 0, r.block[2].shape[0]), (3, 0, r.block[3].shape[0]),
    )
    loads = [pltpu.make_async_copy(r.blocks[g], r.block[g], sems.at[g]) for g in range(4)]
    rows = [
        pltpu.make_async_copy(source, target, sems.at[4 + i])
        for i, (source, target) in enumerate(((r.layer_in, r.layer), (r.grad_in, r.grad), (r.source_in, r.source)))
    ]
    outs = [pltpu.make_async_copy(r.layer, r.layer_out, sems.at[7]), pltpu.make_async_copy(r.grad, r.input_grad, sems.at[8])]
    for copy in rows + loads:
        copy.start()
    inverse = 1.0 / small[7:8, :1]
    r.gain_grad[...] = small[:3, :model] * inverse
    r.shift_grad[...] = small[3:6, :model] * inverse
    r.bias_out_grad[...] = (small[6:7, :model] * inverse).reshape(model)
    r.bias_in_grad[...] = (small[pl.ds(8 + place, 1)] * inverse).reshape(small.shape[1])
    width, depth = configs[0, 0], configs[0, 3]
    factor = (column(1, (1, model)) < width).astype(F32) / jnp.full((1, 1), depth.astype(F32))
    for i in range(2):
        rows[i].wait()
        outs[i].start()
    rows[2].wait()

    def spread(i):
        part = pl.ds(pl.multiple_of(i * 64, 64), 64)
        value = r.source[part] * factor
        for level in range(layers):
            chosen = (jnp.full((1, 1), depth) >= layers - level).astype(F32)
            r.memories[level, part] = value * chosen

    each(r.source.shape[0] // 64, spread)
    outs.append(pltpu.make_async_copy(r.memories, r.memory_grad, sems.at[9]))
    outs[2].start()
    for i, (g, start, count) in enumerate(parts):
        if start == 0:
            loads[g].wait()

        size = 80 if count % 80 == 0 else 96

        def scale(at):
            there = pl.ds(pl.multiple_of(start + at * size, 16), size)
            r.wide[g][there] = r.block[g][there].astype(F32) * inverse

        each(count // size, scale)
        outs.append(pltpu.make_async_copy(r.wide[g].at[pl.ds(start, count)], r.grads[i], sems.at[10 + i]))
        outs[-1].start()
    for copy in outs:
        copy.wait()


def run_finish(ins, layers):
    blocks, small = ins["blocks"], ins["small"]
    rows = ins["layer_in"].shape
    local, units = blocks[0].shape[0] // 4, small.shape[1]

    def shape(*dims):
        return jax.ShapeDtypeStruct(dims, F32)

    counts = (3 * local, local, local, 2 * local, local)
    outs = dict(
        layer_out=shape(*rows), input_grad=shape(*rows), memory_grad=shape(layers, *rows),
        gain_grad=shape(3, rows[1]), shift_grad=shape(3, rows[1]), bias_in_grad=shape(units), bias_out_grad=shape(rows[1]),
        grads=[shape(count, rows[1]) for count in counts] + [shape(*blocks[2].shape), shape(*blocks[3].shape)],
    )
    scratch = dict(
        layer=pltpu.VMEM(rows, F32), grad=pltpu.VMEM(rows, F32), source=pltpu.VMEM(rows, F32),
        memories=pltpu.VMEM((layers,) + rows, F32),
        block=[pltpu.VMEM(block.shape, BF16) for block in blocks],
        wide=[pltpu.VMEM(block.shape, F32) for block in blocks],
        sems=pltpu.SemaphoreType.DMA((17,)),
    )
    hbm = pl.ANY
    spaces = dict(
        configs=pltpu.SMEM, layer_in=hbm, grad_in=hbm, source_in=hbm, blocks=hbm,
        layer_out=hbm, input_grad=hbm, memory_grad=hbm, grads=hbm,
    )
    return call(finish_kernel, "finish", ins, outs, scratch, spaces, vmem_limit_bytes=60 * 2**20)


def per_device(
    inputs, memory, out_grad, lengths, src_lengths, configs, norm_gain, norm_bias,
    self_qkv, self_out, cross_q, cross_kv, cross_out, ffn_in, ffn_in_bias, ffn_out, ffn_out_bias,
):
    model = inputs.shape[1]
    layers = memory.shape[0]
    local = self_out.shape[0]
    done = run_layer(dict(
        lengths=lengths, src_lengths=src_lengths, configs=configs, gains=norm_gain, shifts=norm_bias,
        bias_in=ffn_in_bias, bias_out=ffn_out_bias, x_in=inputs, memory_in=memory, upstream_in=out_grad,
        shards=[
            self_qkv.transpose(1, 2, 0).reshape(3 * local, model), self_out, cross_q.T,
            cross_kv.transpose(1, 2, 0).reshape(2 * local, model), cross_out, ffn_in, ffn_out,
        ],
    ))
    out = run_finish(dict(
        configs=configs, small=done.small_out, layer_in=done.layer_out, grad_in=done.input_grad,
        source_in=done.memory_out, blocks=done.blocks,
    ), layers)
    grads = out.grads
    return (
        out.layer_out,
        out.input_grad,
        out.memory_grad,
        out.gain_grad,
        out.shift_grad,
        grads[0].reshape(3, local, model).transpose(2, 0, 1),
        grads[1],
        grads[2].T,
        grads[3].reshape(2, local, model).transpose(2, 0, 1),
        grads[4],
        grads[5],
        out.bias_in_grad,
        grads[6],
        out.bias_out_grad,
    )


def solution(mesh):
    rows = P(("grp", "dp", "tp"), None)
    stack = P(None, ("grp", "dp", "tp"), None)
    weights = (
        P(None, None, "tp"), P("tp", None), P(None, "tp"), P(None, None, "tp"), P("tp", None),
        P(None, "tp"), P("tp"), P("tp", None), P(),
    )
    return jax.shard_map(
        per_device,
        mesh=mesh,
        in_specs=(rows, stack, rows, P(("grp", "dp")), P(("grp", "dp")), P("grp", None), P(), P()) + weights,
        out_specs=(rows, rows, stack, P(), P()) + weights,
        check_vma=False,
    )
```

```python
import functools
import types

import jax
import jax.numpy as jnp
from jax import lax
from jax.experimental import pallas as pl
from jax.experimental.pallas import tpu as pltpu
from jax.sharding import PartitionSpec as P

HD = 80
LEN = 256
EPSILON = 1e-05
NEGATIVE = -1e30
SCALE = HD ** (-0.5)
LOG2E = 1.4426950408889634
F32 = jnp.float32
BF16 = jnp.bfloat16


MESH = pl.DeviceIdType.MESH


class Place:
    def __init__(self):
        self.tps = lax.axis_size("tp")
        self.extra = lax.axis_size("dp") // 2
        assert lax.axis_size("grp") == 4 and lax.axis_size("dp") % 2 == 0
        grp, dp, tp = (lax.axis_index(name) for name in ("grp", "dp", "tp"))
        core, low, high = dp % 2, grp % 2, grp // 2
        flip_low, flip_high = grp + 1 - 2 * low, grp + 2 - 4 * high
        self.grp, self.dp, self.tp, self.core = grp, dp, tp, core
        self.first_bit = (1 - core) * low + core * high
        self.second_bit = (1 - core) * high + core * low
        self.first = ((1 - core) * flip_low + core * flip_high, dp, tp)
        self.second = ((1 - core) * flip_high + core * flip_low, dp, tp)
        self.across = (3 - grp, dp, tp)
        self.sibling = (grp, dp + 1 - 2 * core, tp)
        self.above = (grp, dp, tp + 1)
        self.below = (grp, dp, tp - 1)
        self.has_above = tp < self.tps - 1
        self.has_below = tp > 0

    def copy_of(self, step):
        return (self.grp, ((self.dp // 2 + step) % self.extra) * 2 + self.core, self.tp)

    def nth_block(self, k):
        size = self.tps
        upper = (2 * self.tp) // size
        lead = (1 - upper) * self.tp + upper * (size - 1 - self.tp)
        spot = k + (k + size - lead) // size
        return (1 - upper) * spot + upper * (size - 1 - spot)

    def along(self, tp):
        return (self.grp, self.dp, tp)

    def barrier(self):
        sem = pltpu.get_barrier_semaphore()
        partners = [self.first, self.second, self.across, self.sibling]
        partners += [self.along((self.tp + step) % self.tps) for step in range(1, self.tps)]
        partners += [self.copy_of(step) for step in range(1, self.extra)]
        for device in partners:
            pl.semaphore_signal(sem, inc=1, device_id=device, device_id_type=MESH)
        pl.semaphore_wait(sem, len(partners))


def push(src, dst, send_sem, recv_sem, device):
    return pltpu.make_async_remote_copy(
        src_ref=src, dst_ref=dst, send_sem=send_sem, recv_sem=recv_sem, device_id=device, device_id_type=MESH
    )


def rows_of(ref, lead, start, count):
    return ref.at[lead, pl.ds(pl.multiple_of(start, 16), count)]


def add_units(total, term, unit):
    def step(i, carry):
        rows = pl.ds(pl.multiple_of(i * unit, 16), unit)
        total[rows] = total[rows] + term[rows]
        return carry

    lax.fori_loop(0, total.shape[0] // unit, step, 0)


class Spread:
    KINDS = 6

    def __init__(self, place, view, unit, sems):
        self.place, self.view, self.unit, self.sems = place, view, unit, sems
        f, s, c = place.first_bit, place.second_bit, place.core
        self.table = (
            (place.second, c * 4 + f * 2 + s, c * 4 + f * 2 + 1 - s, 1),
            (place.first, c * 4 + f * 2, c * 4 + 2 - f * 2, 2),
            (place.sibling, c * 4, 4 - c * 4, 4),
        )

    def region(self, start, count):
        return self.view(start * self.unit, count * self.unit)

    def own(self):
        return self.region(self.table[0][1], 1)

    def copy(self, n, lands=False):
        device, leaves, landing, count = self.table[n]
        part = self.region(landing if lands else leaves, count)
        return push(part, part, self.sems(2 * n), self.sems(2 * n + 1), device)

    def step(self, stage):
        if stage > 0:
            self.copy(stage - 1, lands=True).wait_recv()
        if stage < 3:
            self.copy(stage).start()

    def finish(self):
        for n in range(3):
            self.copy(n).wait_send()


class Gather:
    KINDS = Spread.KINDS + 3

    def __init__(self, place, buffers, sems):
        self.place, self.buffers, self.sems = place, buffers, sems
        self.unit = [ref.shape[1] // 8 for ref in buffers]
        self.others = place.tps - 1

    def spread(self, g, j):
        return Spread(
            self.place,
            lambda start, count: rows_of(self.buffers[g], j, start, count),
            self.unit[g],
            lambda kind: self.sems.at[kind, g, j],
        )

    def relays(self, g, j):
        p = self.place
        part = self.spread(g, j).own()
        sem = lambda n: self.sems.at[Spread.KINDS + n, g, j]
        return (
            (jnp.logical_and(j <= p.tp, p.has_above), push(part, part, sem(0), sem(2), p.above)),
            (jnp.logical_and(j >= p.tp, p.has_below), push(part, part, sem(1), sem(2), p.below)),
        )

    def start(self, g):
        for needed, copy in self.relays(g, self.place.tp):
            pl.when(needed)(copy.start)

    def step(self, g, k, stage):
        j = self.place.nth_block(k)
        if stage == 0:
            relays = self.relays(g, j)
            relays[0][1].wait_recv()
            for needed, copy in relays:
                pl.when(needed)(copy.start)
        self.spread(g, j).step(stage)

    def drain(self, g, j):
        for needed, copy in self.relays(g, j):
            pl.when(needed)(copy.wait_send)

        @pl.when(j != self.place.tp)
        def _():
            self.spread(g, j).finish()


class Line:
    def __init__(self, place, buffer, sems):
        self.place, self.buffer, self.sems = place, buffer, sems

    def relays(self, j):
        p = self.place
        part = self.buffer.at[j]
        return (
            (jnp.logical_and(j <= p.tp, p.has_above), push(part, part, self.sems.at[0, j], self.sems.at[2, j], p.above)),
            (jnp.logical_and(j >= p.tp, p.has_below), push(part, part, self.sems.at[1, j], self.sems.at[2, j], p.below)),
        )

    def start(self):
        for needed, copy in self.relays(self.place.tp):
            pl.when(needed)(copy.start)

    def step(self, k):
        j = self.place.nth_block(k)
        relays = self.relays(j)
        relays[0][1].wait_recv()
        for needed, copy in relays:
            pl.when(needed)(copy.start)

    def finish(self):
        for j in range(self.place.tps):
            for needed, copy in self.relays(j):
                pl.when(needed)(copy.wait_send)


class Reduce:
    KINDS = 8 + Spread.KINDS + 2

    def __init__(self, place, grads, halves, planes, lines, extras, totals, sems):
        self.place, self.grads, self.totals, self.sems = place, grads, totals, sems
        self.halves, self.planes, self.lines, self.extras = halves, planes, lines, extras
        self.unit = [ref.shape[1] // 8 for ref in grads]

    def sem(self, kind, g, j):
        return self.sems.at[kind, g, j]

    def rows(self, g, j, half, unit, count=1):
        size = self.unit[g]
        return rows_of(self.grads[g], j, (half * 4 + unit) * size, count * size)

    def move(self, g, j, stage):
        p, size = self.place, self.unit[g]
        if stage == 0:
            part, landing, device = self.rows(g, j, 1 - p.core, 0, 4), self.halves[g].at[j], p.sibling
        elif stage == 1:
            part, device = self.rows(g, j, p.core, 2 - p.first_bit * 2, 2), p.first
            landing = self.planes[g].at[j, pl.ds(0, 2 * size)]
        else:
            part, device = self.rows(g, j, p.core, p.first_bit * 2 + 1 - p.second_bit), p.second
            landing = self.planes[g].at[j, pl.ds(2 * size, size)]
        return push(part, landing, self.sem(2 * stage, g, j), self.sem(2 * stage + 1, g, j), device)

    def kept(self, g, j, stage):
        p, size = self.place, self.unit[g]
        if stage == 0:
            return self.rows(g, j, p.core, 0, 4), self.halves[g].at[j]
        if stage == 1:
            return self.rows(g, j, p.core, p.first_bit * 2, 2), self.planes[g].at[j, pl.ds(0, 2 * size)]
        return self.piece(g, j), self.planes[g].at[j, pl.ds(2 * size, size)]

    def piece(self, g, j):
        p = self.place
        return self.rows(g, j, p.core, p.first_bit * 2 + p.second_bit)

    def along(self, g, j):
        p = self.place
        return push(self.piece(g, j), self.lines[g].at[p.tp], self.sem(6, g, j), self.sem(7, g, p.tp), p.along(j))

    def from_place(self, g, j):
        p = self.place
        return push(self.piece(g, j), self.lines[g].at[j], self.sem(6, g, j), self.sem(7, g, j), p.along(j))

    def step(self, g, j, stage):
        if stage > 0:
            self.move(g, j, stage - 1).wait_recv()
            add_units(*self.kept(g, j, stage - 1), self.unit[g])
        if stage < 3:
            self.move(g, j, stage).start()
        else:
            pl.when(j != self.place.tp)(self.along(g, j).start)

    def spread(self, g):
        return Spread(
            self.place,
            lambda start, count: self.totals[g].at[pl.ds(pl.multiple_of(start, 16), count)],
            self.unit[g],
            lambda kind: self.sems.at[8 + kind, g, 0],
        )

    def copies(self, g, step):
        p = self.place
        base = self.KINDS - 2
        return push(
            self.piece(g, p.tp), self.extras[g].at[step], self.sem(base, g, step), self.sem(base + 1, g, step), p.copy_of(step)
        )

    def settle(self, g):
        p = self.place
        piece = self.piece(g, p.tp)
        total = piece[...].astype(F32)
        for k in range(p.tps - 1):
            j = p.nth_block(k)
            self.from_place(g, j).wait_recv()
            total = total + self.lines[g][j].astype(F32)
        if p.extra > 1:
            piece[...] = total.astype(BF16)
            for step in range(1, p.extra):
                self.copies(g, step).start()
            for step in range(1, p.extra):
                self.copies(g, step).wait()
                total = total + self.extras[g][step].astype(F32)
        own = self.spread(g).own()
        own[...] = total.astype(BF16)
        self.spread(g).step(0)

    def share(self, g, stage):
        self.spread(g).step(stage)

    def finish(self, g):
        p = self.place
        for j in range(p.tps):
            for stage in range(3):
                self.move(g, j, stage).wait_send()
            pl.when(j != p.tp)(self.along(g, j).wait_send)
        self.spread(g).finish()


class SumSmall:
    @staticmethod
    def slots(tps, extra):
        return 8 + tps + extra

    def __init__(self, place, slots, sems):
        self.place, self.slots_ref, self.sems = place, slots, sems

    def move(self, source, target, device, kind):
        slots = self.slots_ref
        return push(slots.at[source], slots.at[target], self.sems.at[0, kind], self.sems.at[1, target], device)

    def in_plane(self):
        p = self.place
        return [self.move(2, 3 + i, device, 3 + i) for i, device in enumerate((p.second, p.first, p.across))]

    def copies(self):
        p = self.place
        return [self.move(6, 8 + p.tps + s, p.copy_of(s), 8 + p.tps + s) for s in range(1, p.extra)]

    def along(self, k, lands=False):
        p = self.place
        j = p.nth_block(k)
        return self.move(7, 8 + (j if lands else p.tp), p.along(j), 8 + j)

    def start(self):
        self.move(0, 1, self.place.sibling, 1).start()

    def exchange(self, stage):
        p, slots = self.place, self.slots_ref
        if stage == 0:
            self.move(0, 1, p.sibling, 1).wait_recv()
            slots[2] = slots[0] + slots[1]
            for copy in self.in_plane():
                copy.start()
        else:
            for copy in self.in_plane():
                copy.wait_recv()
            slots[6] = (slots[2] + slots[3]) + (slots[4] + slots[5])
            for copy in self.copies():
                copy.start()
            total = slots[6]
            for s, copy in enumerate(self.copies()):
                copy.wait_recv()
                total = total + slots[9 + p.tps + s]
            slots[7] = total
            for k in range(p.tps - 1):
                self.along(k).start()

    def total(self):
        p, slots = self.place, self.slots_ref
        value = slots[7]
        for k in range(p.tps - 1):
            self.along(k, lands=True).wait_recv()
            value = value + slots[8 + p.nth_block(k)]
        return value

    def finish(self):
        p = self.place
        self.move(0, 1, p.sibling, 1).wait_send()
        for copy in self.in_plane() + self.copies():
            copy.wait_send()
        for k in range(p.tps - 1):
            self.along(k).wait_send()


def dot_nn(left, right):
    return lax.dot_general(left, right, (((1,), (0,)), ((), ())), preferred_element_type=F32)


def dot_nt(left, right):
    return lax.dot_general(left, right, (((1,), (1,)), ((), ())), preferred_element_type=F32)


def dot_tn(left, right):
    return lax.dot_general(left, right, (((0,), (0,)), ((), ())), preferred_element_type=F32)


def column(axis, shape):
    return lax.broadcasted_iota(jnp.int32, shape, axis)


def each(count, step):

    def run(i, carry):
        step(i)
        return carry

    lax.fori_loop(0, count, run, 0)


CHUNK = 128
CUBE = 0.044715
ROOT = 0.7978845608028654


def layer_kernel(r):
    r.a2, r.a3, r.e = (r.memory.at[i] for i in range(3))
    columns = pl.ds(0, r.x.shape[1])
    r.dh, r.dm = r.before.at[:, columns], r.down.at[:, columns]
    place = Place()
    n = place.tps
    x, model = r.x, r.x.shape[1]
    owned = x.shape[0]
    sentences = owned // LEN
    local = r.c[0].shape[1]
    heads_here = local // HD
    units = r.hidden.shape[1]
    layers = r.memory.shape[0]
    weights = r.w
    lengths, sources, configs = r.lengths, r.src_lengths, r.configs
    width, heads, hidden_units, depth = (configs[0, i] for i in range(4))
    inv_width = 1.0 / jnp.full((1, 1), width.astype(F32))
    inv_depth = 1.0 / jnp.full((1, 1), depth.astype(F32))
    width_mask = (column(1, (1, model)) < width).astype(F32)

    local_sem = r.local_sems
    spots = (
        (0, 0, 3 * local), (0, 3 * local, local),
        (1, 0, local), (1, local, 2 * local), (1, 3 * local, local),
        (2, 0, weights[2].shape[1]), (3, 0, weights[3].shape[1]),
    )
    fills = [
        (g, pltpu.make_async_copy(r.shards[i], weights[g].at[place.tp, pl.ds(start, size)], local_sem.at[i]))
        for i, (g, start, size) in enumerate(spots)
    ]
    loads = [
        pltpu.make_async_copy(source, target, local_sem.at[7 + i])
        for i, (source, target) in enumerate(((r.x_in, r.x), (r.memory_in, r.memory), (r.upstream_in, r.upstream)))
    ]
    for _, copy in fills[:2]:
        copy.start()
    loads[0].start()
    for _, copy in fills[2:]:
        copy.start()
    loads[1].start()
    loads[2].start()
    r.bias[place.tp] = jnp.broadcast_to(r.bias_in[...].reshape(1, units), r.bias.shape[1:])
    place.barrier()

    gather = Gather(place, weights, r.gather_sems)
    bias = Line(place, r.bias, r.bias_sems)
    for g in range(4):
        for group, copy in fills:
            if group == g:
                copy.wait()
        gather.start(g)
        if g == 0:
            bias.start()
    order = [(g, k) for g in (0, 1) for k in range(n - 1)] + [(g, k) for k in range(n - 1) for g in (2, 3)]

    places = (
        (0, 1, 2, 5), (1, 2, 4, 7), (2, 3, 6, 9), (3, 5, 7, 11), (4, 6, 9, 12), (6, 8, 10, 11),
        (7, 10, 11, 15), (9, 11, 13, 15), (11, 12, 15, 18), (12, 15, 20, 23), (13, 16, 21, 23), (15, 18, 22, 25),
    )
    assert len(places) == len(order)

    def gather_at(spot):
        found = [(stage, e) for e, stages in enumerate(places) for stage, at in enumerate(stages) if at == spot]
        for stage, e in sorted(found):
            gather.step(*order[e], stage)

    def gather_table(start):
        return {(k, b): [functools.partial(gather_at, start + 2 * k + b)] for k in range(n) for b in range(2)}

    def block(k):
        later = (k + n - 1) // n
        return (1 - later) * place.tp + later * place.nth_block(k - 1)

    def block_last(k):
        own = k // (n - 1)
        return own * place.tp + (1 - own) * place.nth_block(k)

    def hooks(table, k, b):
        for (kk, bb), steps in table.items():

            @pl.when(jnp.logical_and(k == kk, b == bb))
            def _():
                for step in steps:
                    step()

    def chunk(i):
        return pl.ds(pl.multiple_of(i * CHUNK, CHUNK), CHUNK)

    def keep_of(i):
        per = LEN // CHUNK
        spot = column(0, (CHUNK, 1)) + (i % per) * CHUNK
        return (spot < lengths[place.tp * sentences + i // per]).astype(F32) * width_mask

    def norm_parts(rows):
        mean = jnp.sum(rows * width_mask, axis=-1, keepdims=True) * inv_width
        centred = (rows - mean) * width_mask
        spread = jnp.sum(centred * centred, axis=-1, keepdims=True) * inv_width
        rstd = lax.rsqrt(spread + EPSILON)
        return centred * rstd, rstd

    def norm(rows, which):
        hat, _ = norm_parts(rows)
        return ((hat * r.gains[which:which + 1] + r.shifts[which:which + 1]) * width_mask).astype(BF16)

    def fold(values):
        return jnp.sum(values.reshape(values.shape[0] // 8, 8, values.shape[1]), axis=0)

    def norm_backward(rows, which, upstream):
        hat, rstd = norm_parts(rows)
        upstream = upstream * width_mask
        sums = r.norm_sums
        sums[which] = sums[which] + fold(upstream * hat)
        sums[3 + which] = sums[3 + which] + fold(upstream)
        scaled = upstream * r.gains[which:which + 1]
        first = jnp.sum(scaled, axis=-1, keepdims=True) * inv_width
        second = jnp.sum(scaled * hat, axis=-1, keepdims=True) * inv_width
        return (rstd * (scaled - first - hat * second)) * width_mask

    chunks = owned // CHUNK

    def each_chunk(step):
        each(chunks, step)

    acc, da, dh = r.acc, r.da, r.dh
    zeros = jnp.zeros((CHUNK, model), F32)
    r.norm_sums[...] = jnp.zeros(r.norm_sums.shape, F32)
    r.bias_sums[...] = jnp.zeros(r.bias_sums.shape, F32)

    def sentence(b):
        return pl.ds(pl.multiple_of(b * LEN, LEN), LEN)

    def head_keep(j, h):
        return jnp.where(j * heads_here + h < heads, 1.0, 0.0).astype(F32)

    def causal(b, start, size):
        return column(0, (size, 128)) <= column(1, (size, 128)) + start

    def crossing(b, start, size):
        return column(0, (size, 1)) < sources[place.tp * sentences + b]

    def reach(g, start):
        return start + 128 if g == 0 else LEN

    def bands(h):
        return [pl.ds(i * local + h * HD, HD) for i in range(3)]

    def lanes(b):
        return pl.ds(b * LEN, LEN)

    pairs = [(b, h) for b in range(sentences) for h in range(heads_here)]

    def attend(k, table, g, allowed):
        w, t, c, p = weights[g], r.t[g], r.c[g], r.p[g]
        j = block(k)
        hooks(table, k, 0)
        if g == 0:
            t[j] = dot_nt(w[j, :3 * local], r.a1[...]).astype(BF16)
        else:
            t[j, :local] = dot_nt(w[j, :local], r.a2[...]).astype(BF16)
            t[j, local:] = dot_nt(w[j, local:3 * local], r.m[...]).astype(BF16)
        heads_of = [[t[j, band, lanes(b)] for band in bands(h)] for b, h in pairs]
        for i, (query, keys, _) in enumerate(heads_of):
            r.scores[i] = dot_tn(keys, query)
        for i, (b, h) in enumerate(pairs):
            for start in range(0, LEN, 128):
                part, size = pl.ds(start, 128), reach(g, start)
                score = jnp.where(allowed(b, start, size), r.scores[i, :size, part], NEGATIVE)
                raised = jnp.exp2((score - jnp.max(score, axis=0, keepdims=True)) * (SCALE * LOG2E))
                p[j, i, :size, part] = (raised * (1.0 / jnp.sum(raised, axis=0, keepdims=True))).astype(BF16)
                if size < LEN:
                    p[j, i, size:, part] = jnp.zeros((LEN - size, 128), BF16)
            c[j, pl.ds(h * HD, HD), lanes(b)] = (dot_nn(heads_of[i][2], p[j, i]) * head_keep(j, h)).astype(BF16)
        hooks(table, k, 1)
        acc[...] = acc[...] + dot_tn(c[j], w[j, 3 * local:])

    def attend_backward(k, table, g, query_rows, key_rows):
        w, t, c, p = weights[g], r.t[g], r.c[g], r.p[g]
        j = block_last(k)
        e, dt, dc = r.e, r.dt, r.dc
        gather.drain(g, j)
        dc_all = dot_nt(w[j, 3 * local:], e[...])
        for h in range(heads_here):
            dc[h * HD:(h + 1) * HD] = (dc_all[h * HD:(h + 1) * HD] * head_keep(j, h)).astype(BF16)
        heads_of = [[t[j, band, lanes(b)] for band in bands(h)] for b, h in pairs]
        dc_of = [dc[h * HD:(h + 1) * HD, lanes(b)] for b, h in pairs]
        for i, (_, _, values) in enumerate(heads_of):
            r.scores[i] = dot_tn(values, dc_of[i])
        for i, (b, h) in enumerate(pairs):
            dt[bands(h)[2], lanes(b)] = dot_nt(dc_of[i], p[j, i]).astype(BF16)
        w[j, 3 * local:] = dot_nn(c[j], e[...]).astype(BF16)
        for i, (b, h) in enumerate(pairs):
            (query, keys, _), (dq, dk, _) = heads_of[i], bands(h)
            for start in range(0, LEN, 128):
                part, size = pl.ds(start, 128), reach(g, start)
                dp, wide = r.scores[i, :size, part], p[j, i, :size, part].astype(F32)
                r.ds[i, :size, part] = (wide * (dp - jnp.sum(dp * wide, axis=0, keepdims=True))).astype(BF16)
                if size < LEN:
                    r.ds[i, size:, part] = jnp.zeros((LEN - size, 128), BF16)
            dt[dq, lanes(b)] = (dot_nn(keys, r.ds[i]) * SCALE).astype(BF16)
            dt[dk, lanes(b)] = (dot_nt(query, r.ds[i]) * SCALE).astype(BF16)
        hooks(table, k, 1)
        if g == 0:
            da[...] = da[...] + dot_tn(dt[...], w[j, :3 * local])
            w[j, :3 * local] = dot_nn(dt[...], query_rows[...]).astype(BF16)
        else:
            da[...] = da[...] + dot_tn(dt[:local], w[j, :local])
            r.dm[...] = r.dm[...] + dot_tn(dt[local:], w[j, local:3 * local])
            w[j, :local] = dot_nn(dt[:local], query_rows[...]).astype(BF16)
            w[j, local:3 * local] = dot_nn(dt[local:], key_rows[...]).astype(BF16)

    def feed(k, table):
        j = block(k)
        w_up, w_down = weights[2], weights[3]
        hooks(table, k, 0)
        unit = column(1, (1, units)) + j * units
        kept = jnp.where(unit < hidden_units, 0.5, 0.0)
        found = []
        for b in range(sentences):
            rows = sentence(b)
            found.append((dot_nn(r.a3[rows], w_up[j]) + r.bias[j, 0:1], dot_nt(r.e[rows], w_down[j])))
        for b, (before, down) in enumerate(found):
            rows = sentence(b)
            square = before * before
            bent = jnp.tanh(before * (ROOT + ROOT * CUBE * square))
            half = kept + kept * bent
            through = before * half
            r.hidden[rows] = through.astype(BF16)
            slope = half + (through - through * bent) * (ROOT + 3.0 * CUBE * ROOT * square)
            du = (down * slope).astype(BF16)
            r.dhidden[rows] = du
            r.bias_sums[j] = r.bias_sums[j] + fold(du.astype(F32))
        for b in range(sentences):
            rows = sentence(b)
            acc[rows] = acc[rows] + dot_nn(r.hidden[rows], w_down[j])
            da[rows] = da[rows] + dot_nt(r.dhidden[rows], w_up[j])
        hooks(table, k, 1)
        gather.drain(2, j)
        gather.drain(3, j)
        w_down[j] = dot_tn(r.hidden[...], r.e[...]).astype(BF16)
        w_up[j] = dot_nn(r.a3t[...], r.dhidden[...]).astype(BF16)

    loads[0].wait()

    def begin(i):
        rows = chunk(i)
        r.a1[rows] = norm(x[rows].astype(F32), 0)
        acc[rows] = zeros
        da[rows] = zeros

    each_chunk(begin)
    gather_at(0)
    loads[1].wait()

    def mix(i):
        rows = chunk(i)
        total = jnp.zeros((CHUNK, model), F32)
        for level in range(layers):
            chosen = (jnp.full((1, 1), depth) >= layers - level).astype(F32)
            total = total + chosen * r.memory[level, rows].astype(F32)
        r.m[rows] = (total * inv_depth * width_mask).astype(BF16)

    each_chunk(mix)
    gather_at(1)
    loads[2].wait()
    r.out_sums[...] = jnp.zeros(r.out_sums.shape, F32)

    def grad_in(i):
        rows = chunk(i)
        masked = r.upstream[rows].astype(F32) * keep_of(i)
        r.out_sums[...] = r.out_sums[...] + fold(masked)
        r.e[rows] = masked.astype(BF16)

    each_chunk(grad_in)
    gather_at(2)

    others = n - 1
    assert n == 4
    table = gather_table(3)
    for k in range(others):
        table[k + 1, 0].append(functools.partial(bias.step, k))
    each(n, lambda k: attend(k, table, 0, causal))

    def after_self(i):
        rows = chunk(i)
        h = x[rows].astype(F32) + acc[rows] * keep_of(i)
        r.h1[rows] = h
        r.a2[rows] = norm(h, 1)
        acc[rows] = zeros

    each_chunk(after_self)
    table2 = gather_table(11)
    each(n, lambda k: attend(k, table2, 1, crossing))

    def after_cross(i):
        rows = chunk(i)
        h = r.h1[rows] + acc[rows] * keep_of(i)
        r.h2[rows] = h
        r.a3[rows] = norm(h, 2)
        acc[rows] = zeros

    each_chunk(after_cross)
    r.a3t[...] = r.a3[...].T

    reduce = Reduce(
        place, weights, r.half, r.plane, r.line, r.extra, r.total, r.reduce_sems
    )
    plan = {}

    def add(tick, order, step, *args):
        plan.setdefault(tick, []).append((order, len(plan.get(tick, ())), functools.partial(step, *args)))

    def r_tick(tick):
        for _, _, step in sorted(plan.get(tick, ()), key=lambda entry: entry[:2]):
            step()

    def store(g):
        return pltpu.make_async_copy(r.total[g], r.blocks[g], local_sem.at[10 + g])

    times = {
        3: ([(1, 2, 6, 10), (3, 4, 8, 11), (5, 6, 9, 13), (7, 9, 11, 15)], (17, 19, 21, 25)),
        2: ([(1, 3, 6, 9), (3, 6, 8, 11), (5, 8, 10, 13), (7, 9, 12, 16)], (19, 21, 23, 26)),
        1: ([(10, 11, 14, 16), (12, 14, 16, 18), (14, 15, 19, 21), (16, 17, 19, 21)], (24, 27, 28, 29)),
        0: ([(19, 20, 22, 24), (21, 22, 24, 25), (23, 24, 25, 26), (25, 26, 27, 28)], (28, 29, 30, 31)),
    }
    for late, g in enumerate((3, 2, 1, 0)):
        for k, stages in enumerate(times[g][0]):
            j = block(k) if g > 1 else block_last(k)
            for stage, tick in enumerate(stages):
                add(tick, stage, reduce.step, g, j, stage)
        for stage, tick in enumerate(times[g][1]):
            if stage == 0:
                add(tick, 20 - late, reduce.settle, g)
            else:
                add(tick, 30 + stage - late, reduce.share, g, stage)
        add(times[g][1][-1], 50, lambda g=g: store(g).start())

    def reduce_ticks(*numbers):
        return [functools.partial(r_tick, i) for i in numbers]

    def at_end(k, numbers):
        for kk, number in enumerate(numbers):

            @pl.when(k == kk)
            def _():
                r_tick(number)

    table3 = gather_table(19)
    for k in range(1, n):
        table3[k, 1] += reduce_ticks(2 * k)

    def feed_step(k):
        feed(k, table3)
        at_end(k, [2 * i + 1 for i in range(n)])

    each(n, feed_step)
    r_tick(8)
    out_copy = pltpu.make_async_copy(acc, r.layer_out, local_sem.at[14])

    def after_feed(i):
        rows = chunk(i)
        keep = keep_of(i)
        acc[rows] = r.h2[rows] + (acc[rows] + r.bias_out[...].reshape(1, model)) * keep
        down = r.upstream[rows].astype(F32) + norm_backward(r.h2[rows], 2, da[rows])
        dh[rows] = down
        r.e[rows] = (down * keep).astype(BF16)
        da[rows] = zeros
        r.dm[rows] = zeros

    each_chunk(after_feed)
    out_copy.start()
    table4 = {(k, 1): reduce_ticks(9 + 2 * k) for k in range(n)}

    def cross_step(k):
        attend_backward(k, table4, 1, r.a2, r.m)
        at_end(k, [10 + 2 * i for i in range(n)])

    each(n, cross_step)
    memory_copy = pltpu.make_async_copy(r.dm, r.memory_out, local_sem.at[15])
    memory_copy.start()

    def before_cross(i):
        rows = chunk(i)
        down = dh[rows] + norm_backward(r.h1[rows], 1, da[rows])
        dh[rows] = down
        r.e[rows] = (down * keep_of(i)).astype(BF16)
        da[rows] = zeros

    each_chunk(before_cross)
    r_tick(17)
    table5 = {(k, 1): reduce_ticks(18 + 2 * k) for k in range(n)}

    def self_step(k):
        attend_backward(k, table5, 0, r.a1, r.a1)
        at_end(k, [19 + 2 * i for i in range(n)])

    each(n, self_step)

    def before_self(i):
        rows = chunk(i)
        dh[rows] = dh[rows] + norm_backward(x[rows].astype(F32), 0, da[rows])

    each_chunk(before_self)
    grad_copy = pltpu.make_async_copy(dh, r.input_grad, local_sem.at[16])
    grad_copy.start()

    small = SumSmall(place, r.slots, r.small_sems)

    def small_start():
        own = r.slots.at[0]
        own[...] = jnp.zeros(own.shape, F32)
        for i in range(6):
            own[i:i + 1, :model] = jnp.sum(r.norm_sums[i], axis=0, keepdims=True)
        own[6:7, :model] = jnp.sum(r.out_sums[...], axis=0, keepdims=True)
        tokens = lengths[place.tp * sentences]
        for b in range(1, sentences):
            tokens = tokens + lengths[place.tp * sentences + b]
        own[7:8] = jnp.full((1, own.shape[1]), tokens.astype(F32))
        for i in range(n):
            own[8 + i:9 + i] = jnp.sum(r.bias_sums[i], axis=0, keepdims=True)
        small.start()

    add(26, 5, small_start)
    for stage in range(2):
        add(27 + stage, 5, small.exchange, stage)
    final = max(plan)
    for tick in range(26, final + 1):
        r_tick(tick)
    r.small_out[...] = small.total()
    bias.finish()
    for copy in (out_copy, memory_copy, grad_copy):
        copy.wait()
    for g in range(4):
        reduce.finish(g)
        store(g).wait()
    small.finish()


def call(kernel, name, ins, outs, scratch, spaces, **options):
    trees = (ins, outs, scratch)
    structure = jax.tree_util.tree_structure(trees)

    def body(*refs):
        groups = jax.tree_util.tree_unflatten(structure, refs)
        kernel(types.SimpleNamespace(**groups[0], **groups[1], **groups[2]))

    def specs(group):
        return [
            pl.BlockSpec(memory_space=spaces.get(key, pltpu.VMEM))
            for key in sorted(group) for _ in jax.tree_util.tree_leaves(group[key])
        ]

    leaves = jax.tree_util.tree_leaves
    values = pl.pallas_call(
        body,
        out_shape=leaves(outs),
        in_specs=specs(ins),
        out_specs=specs(outs),
        scratch_shapes=leaves(scratch),
        compiler_params=pltpu.CompilerParams(**options),
        name=name,
    )(*leaves(ins))
    return types.SimpleNamespace(**jax.tree_util.tree_unflatten(jax.tree_util.tree_structure(outs), values))


def run_layer(ins):
    n, extra = lax.axis_size("tp"), lax.axis_size("dp") // 2
    owned, model = ins["x_in"].shape
    memory, shards = ins["memory_in"], ins["shards"]
    local, units = shards[1].shape[0], ins["bias_in"].shape[0]
    small = (16, units)
    assert n <= 8 and units >= model and memory.shape[0] >= 3
    shapes = [(n, 4 * local, model)] * 2 + [(n,) + shards[5].shape, (n,) + shards[6].shape]
    small_slots = SumSmall.slots(n, extra)

    def vmem(*shape):
        return pltpu.VMEM(shape, BF16)

    def wide(*shape):
        return pltpu.VMEM(shape, F32)

    def eighths(*lead, parts=1):
        return [vmem(*lead, rows * parts // 8, columns) for _, rows, columns in shapes]

    dma = pltpu.SemaphoreType.DMA
    scratch = dict(
        w=[vmem(*shape) for shape in shapes],
        bias=wide(n, 8, units),
        x=vmem(owned, model),
        memory=vmem(*memory.shape),
        upstream=vmem(owned, model),
        a1=vmem(owned, model),
        m=vmem(owned, model),
        h1=wide(owned, model),
        h2=wide(owned, model),
        acc=wide(owned, model),
        da=wide(owned, model),
        t=[vmem(n, 3 * local, owned)] * 2,
        c=[vmem(n, local, owned)] * 2,
        p=[vmem(n, owned // LEN * (local // HD), LEN, LEN)] * 2,
        dt=vmem(3 * local, owned),
        dc=vmem(local, owned),
        a3t=vmem(model, owned),
        scores=wide(owned // LEN * (local // HD), LEN, LEN),
        ds=vmem(owned // LEN * (local // HD), LEN, LEN),
        before=wide(owned, units),
        down=wide(owned, units),
        hidden=vmem(owned, units),
        dhidden=vmem(owned, units),
        bias_sums=wide(n, 8, units),
        norm_sums=wide(6, 8, model),
        out_sums=wide(8, model),
        half=eighths(n, parts=4),
        plane=eighths(n, parts=3),
        line=eighths(n),
        extra=eighths(extra),
        total=eighths(parts=8),
        slots=wide(small_slots, *small),
        gather_sems=dma((Gather.KINDS, 4, n)),
        bias_sems=dma((3, n)),
        reduce_sems=dma((Reduce.KINDS, 4, max(n, extra))),
        small_sems=dma((2, small_slots)),
        local_sems=dma((17,)),
    )
    rows = jax.ShapeDtypeStruct((owned, model), F32)
    outs = dict(
        layer_out=rows, input_grad=rows, memory_out=rows, small_out=jax.ShapeDtypeStruct(small, F32),
        blocks=[jax.ShapeDtypeStruct(shape[1:], BF16) for shape in shapes],
    )
    smem, hbm = pltpu.SMEM, pl.ANY
    spaces = dict(
        lengths=smem, src_lengths=smem, configs=smem, x_in=hbm, memory_in=hbm, upstream_in=hbm, shards=hbm,
        layer_out=hbm, input_grad=hbm, memory_out=hbm, blocks=hbm,
    )
    return call(
        layer_kernel, "layer", ins, outs, scratch, spaces,
        collective_id=1, has_side_effects=True, vmem_limit_bytes=64 * 2**20,
    )


def finish_kernel(r):
    small, configs, sems = r.small, r.configs, r.sems
    model = r.gain_grad.shape[1]
    layers = r.memory_grad.shape[0]
    place = lax.axis_index("tp")
    local = r.grads[1].shape[0]
    parts = (
        (0, 0, 3 * local), (0, 3 * local, local),
        (1, 0, local), (1, local, 2 * local), (1, 3 * local, local),
        (2, 0, r.block[2].shape[0]), (3, 0, r.block[3].shape[0]),
    )
    loads = [pltpu.make_async_copy(r.blocks[g], r.block[g], sems.at[g]) for g in range(4)]
    rows = [
        pltpu.make_async_copy(source, target, sems.at[4 + i])
        for i, (source, target) in enumerate(((r.layer_in, r.layer), (r.grad_in, r.grad), (r.source_in, r.source)))
    ]
    outs = [pltpu.make_async_copy(r.layer, r.layer_out, sems.at[7]), pltpu.make_async_copy(r.grad, r.input_grad, sems.at[8])]
    for copy in rows + loads:
        copy.start()
    inverse = 1.0 / small[7:8, :1]
    r.gain_grad[...] = small[:3, :model] * inverse
    r.shift_grad[...] = small[3:6, :model] * inverse
    r.bias_out_grad[...] = (small[6:7, :model] * inverse).reshape(model)
    r.bias_in_grad[...] = (small[pl.ds(8 + place, 1)] * inverse).reshape(small.shape[1])
    width, depth = configs[0, 0], configs[0, 3]
    factor = (column(1, (1, model)) < width).astype(F32) / jnp.full((1, 1), depth.astype(F32))
    for i in range(2):
        rows[i].wait()
        outs[i].start()
    rows[2].wait()

    def spread(i):
        part = pl.ds(pl.multiple_of(i * 64, 64), 64)
        value = r.source[part] * factor
        for level in range(layers):
            chosen = (jnp.full((1, 1), depth) >= layers - level).astype(F32)
            r.memories[level, part] = value * chosen

    each(r.source.shape[0] // 64, spread)
    outs.append(pltpu.make_async_copy(r.memories, r.memory_grad, sems.at[9]))
    outs[2].start()
    for i, (g, start, count) in enumerate(parts):
        if start == 0:
            loads[g].wait()

        size = 80 if count % 80 == 0 else 96

        def scale(at):
            there = pl.ds(pl.multiple_of(start + at * size, 16), size)
            r.wide[g][there] = r.block[g][there].astype(F32) * inverse

        each(count // size, scale)
        outs.append(pltpu.make_async_copy(r.wide[g].at[pl.ds(start, count)], r.grads[i], sems.at[10 + i]))
        outs[-1].start()
    for copy in outs:
        copy.wait()


def run_finish(ins, layers):
    blocks, small = ins["blocks"], ins["small"]
    rows = ins["layer_in"].shape
    local, units = blocks[0].shape[0] // 4, small.shape[1]

    def shape(*dims):
        return jax.ShapeDtypeStruct(dims, F32)

    counts = (3 * local, local, local, 2 * local, local)
    outs = dict(
        layer_out=shape(*rows), input_grad=shape(*rows), memory_grad=shape(layers, *rows),
        gain_grad=shape(3, rows[1]), shift_grad=shape(3, rows[1]), bias_in_grad=shape(units), bias_out_grad=shape(rows[1]),
        grads=[shape(count, rows[1]) for count in counts] + [shape(*blocks[2].shape), shape(*blocks[3].shape)],
    )
    scratch = dict(
        layer=pltpu.VMEM(rows, F32), grad=pltpu.VMEM(rows, F32), source=pltpu.VMEM(rows, F32),
        memories=pltpu.VMEM((layers,) + rows, F32),
        block=[pltpu.VMEM(block.shape, BF16) for block in blocks],
        wide=[pltpu.VMEM(block.shape, F32) for block in blocks],
        sems=pltpu.SemaphoreType.DMA((17,)),
    )
    hbm = pl.ANY
    spaces = dict(
        configs=pltpu.SMEM, layer_in=hbm, grad_in=hbm, source_in=hbm, blocks=hbm,
        layer_out=hbm, input_grad=hbm, memory_grad=hbm, grads=hbm,
    )
    return call(finish_kernel, "finish", ins, outs, scratch, spaces, vmem_limit_bytes=60 * 2**20)


def per_device(
    inputs, memory, out_grad, lengths, src_lengths, configs, norm_gain, norm_bias,
    self_qkv, self_out, cross_q, cross_kv, cross_out, ffn_in, ffn_in_bias, ffn_out, ffn_out_bias,
):
    model = inputs.shape[1]
    layers = memory.shape[0]
    local = self_out.shape[0]
    done = run_layer(dict(
        lengths=lengths, src_lengths=src_lengths, configs=configs, gains=norm_gain, shifts=norm_bias,
        bias_in=ffn_in_bias, bias_out=ffn_out_bias, x_in=inputs, memory_in=memory, upstream_in=out_grad,
        shards=[
            self_qkv.transpose(1, 2, 0).reshape(3 * local, model), self_out, cross_q.T,
            cross_kv.transpose(1, 2, 0).reshape(2 * local, model), cross_out, ffn_in, ffn_out,
        ],
    ))
    out = run_finish(dict(
        configs=configs, small=done.small_out, layer_in=done.layer_out, grad_in=done.input_grad,
        source_in=done.memory_out, blocks=done.blocks,
    ), layers)
    grads = out.grads
    return (
        out.layer_out,
        out.input_grad,
        out.memory_grad,
        out.gain_grad,
        out.shift_grad,
        grads[0].reshape(3, local, model).transpose(2, 0, 1),
        grads[1],
        grads[2].T,
        grads[3].reshape(2, local, model).transpose(2, 0, 1),
        grads[4],
        grads[5],
        out.bias_in_grad,
        grads[6],
        out.bias_out_grad,
    )


def solution(mesh):
    rows = P(("grp", "dp", "tp"), None)
    stack = P(None, ("grp", "dp", "tp"), None)
    weights = (
        P(None, None, "tp"), P("tp", None), P(None, "tp"), P(None, None, "tp"), P("tp", None),
        P(None, "tp"), P("tp"), P("tp", None), P(),
    )
    return jax.shard_map(
        per_device,
        mesh=mesh,
        in_specs=(rows, stack, rows, P(("grp", "dp")), P(("grp", "dp")), P("grp", None), P(), P()) + weights,
        out_specs=(rows, rows, stack, P(), P()) + weights,
        check_vma=False,
    )
```

```python
import functools
import types

import jax
import jax.numpy as jnp
from jax import lax
from jax.experimental import pallas as pl
from jax.experimental.pallas import tpu as pltpu
from jax.sharding import PartitionSpec as P

HD = 80
LEN = 256
EPSILON = 1e-05
NEGATIVE = -1e30
SCALE = HD ** (-0.5)
LOG2E = 1.4426950408889634
F32 = jnp.float32
BF16 = jnp.bfloat16


MESH = pl.DeviceIdType.MESH


class Place:
    def __init__(self):
        self.tps = lax.axis_size("tp")
        self.extra = lax.axis_size("dp") // 2
        assert lax.axis_size("grp") == 4 and lax.axis_size("dp") % 2 == 0
        grp, dp, tp = (lax.axis_index(name) for name in ("grp", "dp", "tp"))
        core, low, high = dp % 2, grp % 2, grp // 2
        flip_low, flip_high = grp + 1 - 2 * low, grp + 2 - 4 * high
        self.grp, self.dp, self.tp, self.core = grp, dp, tp, core
        self.first_bit = (1 - core) * low + core * high
        self.second_bit = (1 - core) * high + core * low
        self.first = ((1 - core) * flip_low + core * flip_high, dp, tp)
        self.second = ((1 - core) * flip_high + core * flip_low, dp, tp)
        self.across = (3 - grp, dp, tp)
        self.sibling = (grp, dp + 1 - 2 * core, tp)
        self.above = (grp, dp, tp + 1)
        self.below = (grp, dp, tp - 1)
        self.has_above = tp < self.tps - 1
        self.has_below = tp > 0

    def copy_of(self, step):
        return (self.grp, ((self.dp // 2 + step) % self.extra) * 2 + self.core, self.tp)

    def nth_block(self, k):
        size = self.tps
        upper = (2 * self.tp) // size
        lead = (1 - upper) * self.tp + upper * (size - 1 - self.tp)
        spot = k + (k + size - lead) // size
        return (1 - upper) * spot + upper * (size - 1 - spot)

    def along(self, tp):
        return (self.grp, self.dp, tp)

    def barrier(self):
        sem = pltpu.get_barrier_semaphore()
        partners = [self.first, self.second, self.across, self.sibling]
        partners += [self.along((self.tp + step) % self.tps) for step in range(1, self.tps)]
        partners += [self.copy_of(step) for step in range(1, self.extra)]
        for device in partners:
            pl.semaphore_signal(sem, inc=1, device_id=device, device_id_type=MESH)
        pl.semaphore_wait(sem, len(partners))


def push(src, dst, send_sem, recv_sem, device):
    return pltpu.make_async_remote_copy(
        src_ref=src, dst_ref=dst, send_sem=send_sem, recv_sem=recv_sem, device_id=device, device_id_type=MESH
    )


def rows_of(ref, lead, start, count):
    return ref.at[lead, pl.ds(pl.multiple_of(start, 16), count)]


def add_units(total, term, unit):
    def step(i, carry):
        rows = pl.ds(pl.multiple_of(i * unit, 16), unit)
        total[rows] = total[rows] + term[rows]
        return carry

    lax.fori_loop(0, total.shape[0] // unit, step, 0)


class Spread:
    KINDS = 6

    def __init__(self, place, view, unit, sems):
        self.place, self.view, self.unit, self.sems = place, view, unit, sems
        f, s, c = place.first_bit, place.second_bit, place.core
        self.table = (
            (place.second, c * 4 + f * 2 + s, c * 4 + f * 2 + 1 - s, 1),
            (place.first, c * 4 + f * 2, c * 4 + 2 - f * 2, 2),
            (place.sibling, c * 4, 4 - c * 4, 4),
        )

    def region(self, start, count):
        return self.view(start * self.unit, count * self.unit)

    def own(self):
        return self.region(self.table[0][1], 1)

    def copy(self, n, lands=False):
        device, leaves, landing, count = self.table[n]
        part = self.region(landing if lands else leaves, count)
        return push(part, part, self.sems(2 * n), self.sems(2 * n + 1), device)

    def step(self, stage):
        if stage > 0:
            self.copy(stage - 1, lands=True).wait_recv()
        if stage < 3:
            self.copy(stage).start()

    def finish(self):
        for n in range(3):
            self.copy(n).wait_send()


class Gather:
    KINDS = Spread.KINDS + 3

    def __init__(self, place, buffers, sems):
        self.place, self.buffers, self.sems = place, buffers, sems
        self.unit = [ref.shape[1] // 8 for ref in buffers]
        self.others = place.tps - 1

    def spread(self, g, j):
        return Spread(
            self.place,
            lambda start, count: rows_of(self.buffers[g], j, start, count),
            self.unit[g],
            lambda kind: self.sems.at[kind, g, j],
        )

    def relays(self, g, j):
        p = self.place
        part = self.spread(g, j).own()
        sem = lambda n: self.sems.at[Spread.KINDS + n, g, j]
        return (
            (jnp.logical_and(j <= p.tp, p.has_above), push(part, part, sem(0), sem(2), p.above)),
            (jnp.logical_and(j >= p.tp, p.has_below), push(part, part, sem(1), sem(2), p.below)),
        )

    def start(self, g):
        for needed, copy in self.relays(g, self.place.tp):
            pl.when(needed)(copy.start)

    def step(self, g, k, stage):
        j = self.place.nth_block(k)
        if stage == 0:
            relays = self.relays(g, j)
            relays[0][1].wait_recv()
            for needed, copy in relays:
                pl.when(needed)(copy.start)
        self.spread(g, j).step(stage)

    def drain(self, g, j):
        for needed, copy in self.relays(g, j):
            pl.when(needed)(copy.wait_send)

        @pl.when(j != self.place.tp)
        def _():
            self.spread(g, j).finish()


class Line:
    def __init__(self, place, buffer, sems):
        self.place, self.buffer, self.sems = place, buffer, sems

    def relays(self, j):
        p = self.place
        part = self.buffer.at[j]
        return (
            (jnp.logical_and(j <= p.tp, p.has_above), push(part, part, self.sems.at[0, j], self.sems.at[2, j], p.above)),
            (jnp.logical_and(j >= p.tp, p.has_below), push(part, part, self.sems.at[1, j], self.sems.at[2, j], p.below)),
        )

    def start(self):
        for needed, copy in self.relays(self.place.tp):
            pl.when(needed)(copy.start)

    def step(self, k):
        j = self.place.nth_block(k)
        relays = self.relays(j)
        relays[0][1].wait_recv()
        for needed, copy in relays:
            pl.when(needed)(copy.start)

    def finish(self):
        for j in range(self.place.tps):
            for needed, copy in self.relays(j):
                pl.when(needed)(copy.wait_send)


class Reduce:
    KINDS = 8 + Spread.KINDS + 2

    def __init__(self, place, grads, halves, planes, lines, extras, totals, sems):
        self.place, self.grads, self.totals, self.sems = place, grads, totals, sems
        self.halves, self.planes, self.lines, self.extras = halves, planes, lines, extras
        self.unit = [ref.shape[1] // 8 for ref in grads]

    def sem(self, kind, g, j):
        return self.sems.at[kind, g, j]

    def rows(self, g, j, half, unit, count=1):
        size = self.unit[g]
        return rows_of(self.grads[g], j, (half * 4 + unit) * size, count * size)

    def move(self, g, j, stage):
        p, size = self.place, self.unit[g]
        if stage == 0:
            part, landing, device = self.rows(g, j, 1 - p.core, 0, 4), self.halves[g].at[j], p.sibling
        elif stage == 1:
            part, device = self.rows(g, j, p.core, 2 - p.first_bit * 2, 2), p.first
            landing = self.planes[g].at[j, pl.ds(0, 2 * size)]
        else:
            part, device = self.rows(g, j, p.core, p.first_bit * 2 + 1 - p.second_bit), p.second
            landing = self.planes[g].at[j, pl.ds(2 * size, size)]
        return push(part, landing, self.sem(2 * stage, g, j), self.sem(2 * stage + 1, g, j), device)

    def kept(self, g, j, stage):
        p, size = self.place, self.unit[g]
        if stage == 0:
            return self.rows(g, j, p.core, 0, 4), self.halves[g].at[j]
        if stage == 1:
            return self.rows(g, j, p.core, p.first_bit * 2, 2), self.planes[g].at[j, pl.ds(0, 2 * size)]
        return self.piece(g, j), self.planes[g].at[j, pl.ds(2 * size, size)]

    def piece(self, g, j):
        p = self.place
        return self.rows(g, j, p.core, p.first_bit * 2 + p.second_bit)

    def along(self, g, j):
        p = self.place
        return push(self.piece(g, j), self.lines[g].at[p.tp], self.sem(6, g, j), self.sem(7, g, p.tp), p.along(j))

    def from_place(self, g, j):
        p = self.place
        return push(self.piece(g, j), self.lines[g].at[j], self.sem(6, g, j), self.sem(7, g, j), p.along(j))

    def step(self, g, j, stage):
        if stage > 0:
            self.move(g, j, stage - 1).wait_recv()
            add_units(*self.kept(g, j, stage - 1), self.unit[g])
        if stage < 3:
            self.move(g, j, stage).start()
        else:
            pl.when(j != self.place.tp)(self.along(g, j).start)

    def spread(self, g):
        return Spread(
            self.place,
            lambda start, count: self.totals[g].at[pl.ds(pl.multiple_of(start, 16), count)],
            self.unit[g],
            lambda kind: self.sems.at[8 + kind, g, 0],
        )

    def copies(self, g, step):
        p = self.place
        base = self.KINDS - 2
        return push(
            self.piece(g, p.tp), self.extras[g].at[step], self.sem(base, g, step), self.sem(base + 1, g, step), p.copy_of(step)
        )

    def settle(self, g):
        p = self.place
        piece = self.piece(g, p.tp)
        total = piece[...].astype(F32)
        for k in range(p.tps - 1):
            j = p.nth_block(k)
            self.from_place(g, j).wait_recv()
            total = total + self.lines[g][j].astype(F32)
        if p.extra > 1:
            piece[...] = total.astype(BF16)
            for step in range(1, p.extra):
                self.copies(g, step).start()
            for step in range(1, p.extra):
                self.copies(g, step).wait()
                total = total + self.extras[g][step].astype(F32)
        own = self.spread(g).own()
        own[...] = total.astype(BF16)
        self.spread(g).step(0)

    def share(self, g, stage):
        self.spread(g).step(stage)

    def finish(self, g):
        p = self.place
        for j in range(p.tps):
            for stage in range(3):
                self.move(g, j, stage).wait_send()
            pl.when(j != p.tp)(self.along(g, j).wait_send)
        self.spread(g).finish()


class SumSmall:
    @staticmethod
    def slots(tps, extra):
        return 8 + tps + extra

    def __init__(self, place, slots, sems):
        self.place, self.slots_ref, self.sems = place, slots, sems

    def move(self, source, target, device, kind):
        slots = self.slots_ref
        return push(slots.at[source], slots.at[target], self.sems.at[0, kind], self.sems.at[1, target], device)

    def in_plane(self):
        p = self.place
        return [self.move(2, 3 + i, device, 3 + i) for i, device in enumerate((p.second, p.first, p.across))]

    def copies(self):
        p = self.place
        return [self.move(6, 8 + p.tps + s, p.copy_of(s), 8 + p.tps + s) for s in range(1, p.extra)]

    def along(self, k, lands=False):
        p = self.place
        j = p.nth_block(k)
        return self.move(7, 8 + (j if lands else p.tp), p.along(j), 8 + j)

    def start(self):
        self.move(0, 1, self.place.sibling, 1).start()

    def exchange(self, stage):
        p, slots = self.place, self.slots_ref
        if stage == 0:
            self.move(0, 1, p.sibling, 1).wait_recv()
            slots[2] = slots[0] + slots[1]
            for copy in self.in_plane():
                copy.start()
        else:
            for copy in self.in_plane():
                copy.wait_recv()
            slots[6] = (slots[2] + slots[3]) + (slots[4] + slots[5])
            for copy in self.copies():
                copy.start()
            total = slots[6]
            for s, copy in enumerate(self.copies()):
                copy.wait_recv()
                total = total + slots[9 + p.tps + s]
            slots[7] = total
            for k in range(p.tps - 1):
                self.along(k).start()

    def total(self):
        p, slots = self.place, self.slots_ref
        value = slots[7]
        for k in range(p.tps - 1):
            self.along(k, lands=True).wait_recv()
            value = value + slots[8 + p.nth_block(k)]
        return value

    def finish(self):
        p = self.place
        self.move(0, 1, p.sibling, 1).wait_send()
        for copy in self.in_plane() + self.copies():
            copy.wait_send()
        for k in range(p.tps - 1):
            self.along(k).wait_send()


def dot_nn(left, right):
    return lax.dot_general(left, right, (((1,), (0,)), ((), ())), preferred_element_type=F32)


def dot_nt(left, right):
    return lax.dot_general(left, right, (((1,), (1,)), ((), ())), preferred_element_type=F32)


def dot_tn(left, right):
    return lax.dot_general(left, right, (((0,), (0,)), ((), ())), preferred_element_type=F32)


def column(axis, shape):
    return lax.broadcasted_iota(jnp.int32, shape, axis)


def each(count, step):

    def run(i, carry):
        step(i)
        return carry

    lax.fori_loop(0, count, run, 0)


CHUNK = 128
CUBE = 0.044715
ROOT = 0.7978845608028654


def layer_kernel(r):
    r.a2, r.a3, r.e = (r.memory.at[i] for i in range(3))
    columns = pl.ds(0, r.x.shape[1])
    r.dh, r.dm = r.before.at[:, columns], r.down.at[:, columns]
    place = Place()
    n = place.tps
    x, model = r.x, r.x.shape[1]
    owned = x.shape[0]
    sentences = owned // LEN
    local = r.c[0].shape[1]
    heads_here = local // HD
    units = r.hidden.shape[1]
    layers = r.memory.shape[0]
    weights = r.w
    lengths, sources, configs = r.lengths, r.src_lengths, r.configs
    width, heads, hidden_units, depth = (configs[0, i] for i in range(4))
    inv_width = 1.0 / jnp.full((1, 1), width.astype(F32))
    inv_depth = 1.0 / jnp.full((1, 1), depth.astype(F32))
    width_mask = (column(1, (1, model)) < width).astype(F32)

    local_sem = r.local_sems
    spots = (
        (0, 0, 3 * local), (0, 3 * local, local),
        (1, 0, local), (1, local, 2 * local), (1, 3 * local, local),
        (2, 0, weights[2].shape[1]), (3, 0, weights[3].shape[1]),
    )
    fills = [
        (g, pltpu.make_async_copy(r.shards[i], weights[g].at[place.tp, pl.ds(start, size)], local_sem.at[i]))
        for i, (g, start, size) in enumerate(spots)
    ]
    loads = [
        pltpu.make_async_copy(source, target, local_sem.at[7 + i])
        for i, (source, target) in enumerate(((r.x_in, r.x), (r.memory_in, r.memory), (r.upstream_in, r.upstream)))
    ]
    for _, copy in fills[:2]:
        copy.start()
    loads[0].start()
    for _, copy in fills[2:]:
        copy.start()
    loads[1].start()
    loads[2].start()
    r.bias[place.tp] = jnp.broadcast_to(r.bias_in[...].reshape(1, units), r.bias.shape[1:])
    place.barrier()

    gather = Gather(place, weights, r.gather_sems)
    bias = Line(place, r.bias, r.bias_sems)
    for g in range(4):
        for group, copy in fills:
            if group == g:
                copy.wait()
        gather.start(g)
        if g == 0:
            bias.start()
    order = [(g, k) for g in (0, 1) for k in range(n - 1)] + [(g, k) for k in range(n - 1) for g in (2, 3)]

    places = (
        (0, 1, 2, 5), (1, 2, 4, 7), (2, 3, 6, 9), (3, 5, 7, 11), (4, 6, 9, 12), (6, 8, 10, 11),
        (7, 10, 11, 15), (9, 11, 13, 15), (11, 12, 15, 18), (12, 15, 20, 23), (13, 16, 21, 23), (15, 18, 22, 25),
    )
    assert len(places) == len(order)

    def gather_at(spot):
        found = [(stage, e) for e, stages in enumerate(places) for stage, at in enumerate(stages) if at == spot]
        for stage, e in sorted(found):
            gather.step(*order[e], stage)

    def gather_table(start):
        return {(k, b): [functools.partial(gather_at, start + 2 * k + b)] for k in range(n) for b in range(2)}

    def block(k):
        later = (k + n - 1) // n
        return (1 - later) * place.tp + later * place.nth_block(k - 1)

    def block_last(k):
        own = k // (n - 1)
        return own * place.tp + (1 - own) * place.nth_block((n - 2 - k) * (1 - own))

    def hooks(table, k, b):
        for (kk, bb), steps in table.items():

            @pl.when(jnp.logical_and(k == kk, b == bb))
            def _():
                for step in steps:
                    step()

    def chunk(i):
        return pl.ds(pl.multiple_of(i * CHUNK, CHUNK), CHUNK)

    def keep_of(i):
        per = LEN // CHUNK
        spot = column(0, (CHUNK, 1)) + (i % per) * CHUNK
        return (spot < lengths[place.tp * sentences + i // per]).astype(F32) * width_mask

    def norm_parts(rows):
        mean = jnp.sum(rows * width_mask, axis=-1, keepdims=True) * inv_width
        centred = (rows - mean) * width_mask
        spread = jnp.sum(centred * centred, axis=-1, keepdims=True) * inv_width
        rstd = lax.rsqrt(spread + EPSILON)
        return centred * rstd, rstd

    def norm(rows, which):
        hat, _ = norm_parts(rows)
        return ((hat * r.gains[which:which + 1] + r.shifts[which:which + 1]) * width_mask).astype(BF16)

    def fold(values):
        return jnp.sum(values.reshape(values.shape[0] // 8, 8, values.shape[1]), axis=0)

    def norm_backward(rows, which, upstream):
        hat, rstd = norm_parts(rows)
        upstream = upstream * width_mask
        sums = r.norm_sums
        sums[which] = sums[which] + fold(upstream * hat)
        sums[3 + which] = sums[3 + which] + fold(upstream)
        scaled = upstream * r.gains[which:which + 1]
        first = jnp.sum(scaled, axis=-1, keepdims=True) * inv_width
        second = jnp.sum(scaled * hat, axis=-1, keepdims=True) * inv_width
        return (rstd * (scaled - first - hat * second)) * width_mask

    chunks = owned // CHUNK

    def each_chunk(step):
        each(chunks, step)

    acc, da, dh = r.acc, r.da, r.dh
    zeros = jnp.zeros((CHUNK, model), F32)
    r.norm_sums[...] = jnp.zeros(r.norm_sums.shape, F32)
    r.bias_sums[...] = jnp.zeros(r.bias_sums.shape, F32)

    def sentence(b):
        return pl.ds(pl.multiple_of(b * LEN, LEN), LEN)

    def head_keep(j, h):
        return jnp.where(j * heads_here + h < heads, 1.0, 0.0).astype(F32)

    def causal(b, start, size):
        return column(0, (size, 128)) <= column(1, (size, 128)) + start

    def crossing(b, start, size):
        return column(0, (size, 1)) < sources[place.tp * sentences + b]

    def reach(g, start):
        return start + 128 if g == 0 else LEN

    def bands(h):
        return [pl.ds(i * local + h * HD, HD) for i in range(3)]

    def lanes(b):
        return pl.ds(b * LEN, LEN)

    pairs = [(b, h) for b in range(sentences) for h in range(heads_here)]

    def attend(k, table, g, allowed):
        w, t, c, p = weights[g], r.t[g], r.c[g], r.p[g]
        j = block(k)
        hooks(table, k, 0)
        if g == 0:
            t[j] = dot_nt(w[j, :3 * local], r.a1[...]).astype(BF16)
        else:
            t[j, :local] = dot_nt(w[j, :local], r.a2[...]).astype(BF16)
            t[j, local:] = dot_nt(w[j, local:3 * local], r.m[...]).astype(BF16)
        heads_of = [[t[j, band, lanes(b)] for band in bands(h)] for b, h in pairs]
        for i, (query, keys, _) in enumerate(heads_of):
            r.scores[i] = dot_tn(keys, query)
        for i, (b, h) in enumerate(pairs):
            for start in range(0, LEN, 128):
                part, size = pl.ds(start, 128), reach(g, start)
                score = jnp.where(allowed(b, start, size), r.scores[i, :size, part], NEGATIVE)
                raised = jnp.exp2((score - jnp.max(score, axis=0, keepdims=True)) * (SCALE * LOG2E))
                p[j, i, :size, part] = (raised * (1.0 / jnp.sum(raised, axis=0, keepdims=True))).astype(BF16)
                if size < LEN:
                    p[j, i, size:, part] = jnp.zeros((LEN - size, 128), BF16)
            c[j, pl.ds(h * HD, HD), lanes(b)] = (dot_nn(heads_of[i][2], p[j, i]) * head_keep(j, h)).astype(BF16)
        hooks(table, k, 1)
        acc[...] = acc[...] + dot_tn(c[j], w[j, 3 * local:])

    def attend_backward(k, table, g, query_rows, key_rows):
        w, t, c, p = weights[g], r.t[g], r.c[g], r.p[g]
        j = block_last(k)
        e, dt, dc = r.e, r.dt, r.dc
        gather.drain(g, j)
        dc_all = dot_nt(w[j, 3 * local:], e[...])
        for h in range(heads_here):
            dc[h * HD:(h + 1) * HD] = (dc_all[h * HD:(h + 1) * HD] * head_keep(j, h)).astype(BF16)
        heads_of = [[t[j, band, lanes(b)] for band in bands(h)] for b, h in pairs]
        dc_of = [dc[h * HD:(h + 1) * HD, lanes(b)] for b, h in pairs]
        for i, (_, _, values) in enumerate(heads_of):
            r.scores[i] = dot_tn(values, dc_of[i])
        for i, (b, h) in enumerate(pairs):
            dt[bands(h)[2], lanes(b)] = dot_nt(dc_of[i], p[j, i]).astype(BF16)
        w[j, 3 * local:] = dot_nn(c[j], e[...]).astype(BF16)
        for i, (b, h) in enumerate(pairs):
            (query, keys, _), (dq, dk, _) = heads_of[i], bands(h)
            for start in range(0, LEN, 128):
                part, size = pl.ds(start, 128), reach(g, start)
                dp, wide = r.scores[i, :size, part], p[j, i, :size, part].astype(F32)
                r.ds[i, :size, part] = (wide * (dp - jnp.sum(dp * wide, axis=0, keepdims=True))).astype(BF16)
                if size < LEN:
                    r.ds[i, size:, part] = jnp.zeros((LEN - size, 128), BF16)
            dt[dq, lanes(b)] = (dot_nn(keys, r.ds[i]) * SCALE).astype(BF16)
            dt[dk, lanes(b)] = (dot_nt(query, r.ds[i]) * SCALE).astype(BF16)
        hooks(table, k, 1)
        if g == 0:
            da[...] = da[...] + dot_tn(dt[...], w[j, :3 * local])
            w[j, :3 * local] = dot_nn(dt[...], query_rows[...]).astype(BF16)
        else:
            da[...] = da[...] + dot_tn(dt[:local], w[j, :local])
            r.dm[...] = r.dm[...] + dot_tn(dt[local:], w[j, local:3 * local])
            w[j, :local] = dot_nn(dt[:local], query_rows[...]).astype(BF16)
            w[j, local:3 * local] = dot_nn(dt[local:], key_rows[...]).astype(BF16)

    def feed(k, table):
        j = block(k)
        w_up, w_down = weights[2], weights[3]
        hooks(table, k, 0)
        unit = column(1, (1, units)) + j * units
        kept = jnp.where(unit < hidden_units, 0.5, 0.0)
        found = []
        for b in range(sentences):
            rows = sentence(b)
            found.append((dot_nn(r.a3[rows], w_up[j]) + r.bias[j, 0:1], dot_nt(r.e[rows], w_down[j])))
        for b, (before, down) in enumerate(found):
            rows = sentence(b)
            square = before * before
            bent = jnp.tanh(before * (ROOT + ROOT * CUBE * square))
            half = kept + kept * bent
            through = before * half
            r.hidden[rows] = through.astype(BF16)
            slope = half + (through - through * bent) * (ROOT + 3.0 * CUBE * ROOT * square)
            du = (down * slope).astype(BF16)
            r.dhidden[rows] = du
            r.bias_sums[j] = r.bias_sums[j] + fold(du.astype(F32))
            acc[rows] = acc[rows] + dot_nn(r.hidden[rows], w_down[j])
            da[rows] = da[rows] + dot_nt(r.dhidden[rows], w_up[j])
        hooks(table, k, 1)
        gather.drain(2, j)
        gather.drain(3, j)
        w_down[j] = dot_tn(r.hidden[...], r.e[...]).astype(BF16)
        w_up[j] = dot_nn(r.a3t[...], r.dhidden[...]).astype(BF16)

    loads[0].wait()

    def begin(i):
        rows = chunk(i)
        r.a1[rows] = norm(x[rows].astype(F32), 0)
        acc[rows] = zeros
        da[rows] = zeros

    each_chunk(begin)
    gather_at(0)
    loads[1].wait()

    def mix(i):
        rows = chunk(i)
        total = jnp.zeros((CHUNK, model), F32)
        for level in range(layers):
            chosen = (jnp.full((1, 1), depth) >= layers - level).astype(F32)
            total = total + chosen * r.memory[level, rows].astype(F32)
        r.m[rows] = (total * inv_depth * width_mask).astype(BF16)

    each_chunk(mix)
    gather_at(1)
    loads[2].wait()
    r.out_sums[...] = jnp.zeros(r.out_sums.shape, F32)

    def grad_in(i):
        rows = chunk(i)
        masked = r.upstream[rows].astype(F32) * keep_of(i)
        r.out_sums[...] = r.out_sums[...] + fold(masked)
        r.e[rows] = masked.astype(BF16)

    each_chunk(grad_in)
    gather_at(2)

    others = n - 1
    assert n == 4
    table = gather_table(3)
    for k in range(others):
        table[k + 1, 0].append(functools.partial(bias.step, k))
    each(n, lambda k: attend(k, table, 0, causal))

    def after_self(i):
        rows = chunk(i)
        h = x[rows].astype(F32) + acc[rows] * keep_of(i)
        r.h1[rows] = h
        r.a2[rows] = norm(h, 1)
        acc[rows] = zeros

    each_chunk(after_self)
    table2 = gather_table(11)
    each(n, lambda k: attend(k, table2, 1, crossing))

    def after_cross(i):
        rows = chunk(i)
        h = r.h1[rows] + acc[rows] * keep_of(i)
        r.h2[rows] = h
        r.a3[rows] = norm(h, 2)
        acc[rows] = zeros

    each_chunk(after_cross)
    r.a3t[...] = r.a3[...].T

    reduce = Reduce(
        place, weights, r.half, r.plane, r.line, r.extra, r.total, r.reduce_sems
    )
    plan = {}

    def add(tick, order, step, *args):
        plan.setdefault(tick, []).append((order, len(plan.get(tick, ())), functools.partial(step, *args)))

    def r_tick(tick):
        for _, _, step in sorted(plan.get(tick, ()), key=lambda entry: entry[:2]):
            step()

    def store(g):
        return pltpu.make_async_copy(r.total[g], r.blocks[g], local_sem.at[10 + g])

    times = {
        3: ([(1, 2, 6, 10), (3, 4, 8, 11), (5, 6, 9, 13), (7, 9, 11, 15)], (17, 19, 21, 25)),
        2: ([(1, 3, 6, 9), (3, 6, 8, 11), (5, 8, 10, 13), (7, 9, 12, 16)], (19, 21, 23, 26)),
        1: ([(10, 11, 14, 16), (12, 14, 16, 18), (14, 15, 19, 21), (16, 17, 19, 21)], (24, 27, 28, 29)),
        0: ([(19, 20, 22, 24), (21, 22, 24, 25), (23, 24, 25, 26), (25, 26, 27, 28)], (28, 29, 30, 31)),
    }
    for late, g in enumerate((3, 2, 1, 0)):
        for k, stages in enumerate(times[g][0]):
            j = block(k) if g > 1 else block_last(k)
            for stage, tick in enumerate(stages):
                add(tick, stage, reduce.step, g, j, stage)
        for stage, tick in enumerate(times[g][1]):
            if stage == 0:
                add(tick, 20 - late, reduce.settle, g)
            else:
                add(tick, 30 + stage - late, reduce.share, g, stage)
        add(times[g][1][-1], 50, lambda g=g: store(g).start())

    def reduce_ticks(*numbers):
        return [functools.partial(r_tick, i) for i in numbers]

    def at_end(k, numbers):
        for kk, number in enumerate(numbers):

            @pl.when(k == kk)
            def _():
                r_tick(number)

    table3 = gather_table(19)
    for k in range(1, n):
        table3[k, 1] += reduce_ticks(2 * k)

    def feed_step(k):
        feed(k, table3)
        at_end(k, [2 * i + 1 for i in range(n)])

    each(n, feed_step)
    r_tick(8)
    out_copy = pltpu.make_async_copy(acc, r.layer_out, local_sem.at[14])

    def after_feed(i):
        rows = chunk(i)
        keep = keep_of(i)
        acc[rows] = r.h2[rows] + (acc[rows] + r.bias_out[...].reshape(1, model)) * keep
        down = r.upstream[rows].astype(F32) + norm_backward(r.h2[rows], 2, da[rows])
        dh[rows] = down
        r.e[rows] = (down * keep).astype(BF16)
        da[rows] = zeros
        r.dm[rows] = zeros

    each_chunk(after_feed)
    out_copy.start()
    table4 = {(k, 1): reduce_ticks(9 + 2 * k) for k in range(n)}

    def cross_step(k):
        attend_backward(k, table4, 1, r.a2, r.m)
        at_end(k, [10 + 2 * i for i in range(n)])

    each(n, cross_step)
    memory_copy = pltpu.make_async_copy(r.dm, r.memory_out, local_sem.at[15])
    memory_copy.start()

    def before_cross(i):
        rows = chunk(i)
        down = dh[rows] + norm_backward(r.h1[rows], 1, da[rows])
        dh[rows] = down
        r.e[rows] = (down * keep_of(i)).astype(BF16)
        da[rows] = zeros

    each_chunk(before_cross)
    r_tick(17)
    table5 = {(k, 1): reduce_ticks(18 + 2 * k) for k in range(n)}

    def self_step(k):
        attend_backward(k, table5, 0, r.a1, r.a1)
        at_end(k, [19 + 2 * i for i in range(n)])

    each(n, self_step)

    def before_self(i):
        rows = chunk(i)
        dh[rows] = dh[rows] + norm_backward(x[rows].astype(F32), 0, da[rows])

    each_chunk(before_self)
    grad_copy = pltpu.make_async_copy(dh, r.input_grad, local_sem.at[16])
    grad_copy.start()

    small = SumSmall(place, r.slots, r.small_sems)

    def small_start():
        own = r.slots.at[0]
        own[...] = jnp.zeros(own.shape, F32)
        for i in range(6):
            own[i:i + 1, :model] = jnp.sum(r.norm_sums[i], axis=0, keepdims=True)
        own[6:7, :model] = jnp.sum(r.out_sums[...], axis=0, keepdims=True)
        tokens = lengths[place.tp * sentences]
        for b in range(1, sentences):
            tokens = tokens + lengths[place.tp * sentences + b]
        own[7:8] = jnp.full((1, own.shape[1]), tokens.astype(F32))
        for i in range(n):
            own[8 + i:9 + i] = jnp.sum(r.bias_sums[i], axis=0, keepdims=True)
        small.start()

    add(26, 5, small_start)
    for stage in range(2):
        add(27 + stage, 5, small.exchange, stage)
    final = max(plan)
    for tick in range(26, final + 1):
        r_tick(tick)
    r.small_out[...] = small.total()
    bias.finish()
    for copy in (out_copy, memory_copy, grad_copy):
        copy.wait()
    for g in range(4):
        reduce.finish(g)
        store(g).wait()
    small.finish()


def call(kernel, name, ins, outs, scratch, spaces, **options):
    trees = (ins, outs, scratch)
    structure = jax.tree_util.tree_structure(trees)

    def body(*refs):
        groups = jax.tree_util.tree_unflatten(structure, refs)
        kernel(types.SimpleNamespace(**groups[0], **groups[1], **groups[2]))

    def specs(group):
        return [
            pl.BlockSpec(memory_space=spaces.get(key, pltpu.VMEM))
            for key in sorted(group) for _ in jax.tree_util.tree_leaves(group[key])
        ]

    leaves = jax.tree_util.tree_leaves
    values = pl.pallas_call(
        body,
        out_shape=leaves(outs),
        in_specs=specs(ins),
        out_specs=specs(outs),
        scratch_shapes=leaves(scratch),
        compiler_params=pltpu.CompilerParams(**options),
        name=name,
    )(*leaves(ins))
    return types.SimpleNamespace(**jax.tree_util.tree_unflatten(jax.tree_util.tree_structure(outs), values))


def run_layer(ins):
    n, extra = lax.axis_size("tp"), lax.axis_size("dp") // 2
    owned, model = ins["x_in"].shape
    memory, shards = ins["memory_in"], ins["shards"]
    local, units = shards[1].shape[0], ins["bias_in"].shape[0]
    small = (16, units)
    assert n <= 8 and units >= model and memory.shape[0] >= 3
    shapes = [(n, 4 * local, model)] * 2 + [(n,) + shards[5].shape, (n,) + shards[6].shape]
    small_slots = SumSmall.slots(n, extra)

    def vmem(*shape):
        return pltpu.VMEM(shape, BF16)

    def wide(*shape):
        return pltpu.VMEM(shape, F32)

    def eighths(*lead, parts=1):
        return [vmem(*lead, rows * parts // 8, columns) for _, rows, columns in shapes]

    dma = pltpu.SemaphoreType.DMA
    scratch = dict(
        w=[vmem(*shape) for shape in shapes],
        bias=wide(n, 8, units),
        x=vmem(owned, model),
        memory=vmem(*memory.shape),
        upstream=vmem(owned, model),
        a1=vmem(owned, model),
        m=vmem(owned, model),
        h1=wide(owned, model),
        h2=wide(owned, model),
        acc=wide(owned, model),
        da=wide(owned, model),
        t=[vmem(n, 3 * local, owned)] * 2,
        c=[vmem(n, local, owned)] * 2,
        p=[vmem(n, owned // LEN * (local // HD), LEN, LEN)] * 2,
        dt=vmem(3 * local, owned),
        dc=vmem(local, owned),
        a3t=vmem(model, owned),
        scores=wide(owned // LEN * (local // HD), LEN, LEN),
        ds=vmem(owned // LEN * (local // HD), LEN, LEN),
        before=wide(owned, units),
        down=wide(owned, units),
        hidden=vmem(owned, units),
        dhidden=vmem(owned, units),
        bias_sums=wide(n, 8, units),
        norm_sums=wide(6, 8, model),
        out_sums=wide(8, model),
        half=eighths(n, parts=4),
        plane=eighths(n, parts=3),
        line=eighths(n),
        extra=eighths(extra),
        total=eighths(parts=8),
        slots=wide(small_slots, *small),
        gather_sems=dma((Gather.KINDS, 4, n)),
        bias_sems=dma((3, n)),
        reduce_sems=dma((Reduce.KINDS, 4, max(n, extra))),
        small_sems=dma((2, small_slots)),
        local_sems=dma((17,)),
    )
    rows = jax.ShapeDtypeStruct((owned, model), F32)
    outs = dict(
        layer_out=rows, input_grad=rows, memory_out=rows, small_out=jax.ShapeDtypeStruct(small, F32),
        blocks=[jax.ShapeDtypeStruct(shape[1:], BF16) for shape in shapes],
    )
    smem, hbm = pltpu.SMEM, pl.ANY
    spaces = dict(
        lengths=smem, src_lengths=smem, configs=smem, x_in=hbm, memory_in=hbm, upstream_in=hbm, shards=hbm,
        layer_out=hbm, input_grad=hbm, memory_out=hbm, blocks=hbm,
    )
    return call(
        layer_kernel, "layer", ins, outs, scratch, spaces,
        collective_id=1, has_side_effects=True, vmem_limit_bytes=64 * 2**20,
    )


def finish_kernel(r):
    small, configs, sems = r.small, r.configs, r.sems
    model = r.gain_grad.shape[1]
    layers = r.memory_grad.shape[0]
    place = lax.axis_index("tp")
    local = r.grads[1].shape[0]
    parts = (
        (0, 0, 3 * local), (0, 3 * local, local),
        (1, 0, local), (1, local, 2 * local), (1, 3 * local, local),
        (2, 0, r.block[2].shape[0]), (3, 0, r.block[3].shape[0]),
    )
    loads = [pltpu.make_async_copy(r.blocks[g], r.block[g], sems.at[g]) for g in range(4)]
    rows = [
        pltpu.make_async_copy(source, target, sems.at[4 + i])
        for i, (source, target) in enumerate(((r.layer_in, r.layer), (r.grad_in, r.grad), (r.source_in, r.source)))
    ]
    outs = [pltpu.make_async_copy(r.layer, r.layer_out, sems.at[7]), pltpu.make_async_copy(r.grad, r.input_grad, sems.at[8])]
    for copy in rows + loads:
        copy.start()
    inverse = 1.0 / small[7:8, :1]
    r.gain_grad[...] = small[:3, :model] * inverse
    r.shift_grad[...] = small[3:6, :model] * inverse
    r.bias_out_grad[...] = (small[6:7, :model] * inverse).reshape(model)
    r.bias_in_grad[...] = (small[pl.ds(8 + place, 1)] * inverse).reshape(small.shape[1])
    width, depth = configs[0, 0], configs[0, 3]
    factor = (column(1, (1, model)) < width).astype(F32) / jnp.full((1, 1), depth.astype(F32))
    for i in range(2):
        rows[i].wait()
        outs[i].start()
    rows[2].wait()

    def spread(i):
        part = pl.ds(pl.multiple_of(i * 64, 64), 64)
        value = r.source[part] * factor
        for level in range(layers):
            chosen = (jnp.full((1, 1), depth) >= layers - level).astype(F32)
            r.memories[level, part] = value * chosen

    each(r.source.shape[0] // 64, spread)
    outs.append(pltpu.make_async_copy(r.memories, r.memory_grad, sems.at[9]))
    outs[2].start()
    for i, (g, start, count) in enumerate(parts):
        if start == 0:
            loads[g].wait()

        size = 80 if count % 80 == 0 else 96

        def scale(at):
            there = pl.ds(pl.multiple_of(start + at * size, 16), size)
            r.wide[g][there] = r.block[g][there].astype(F32) * inverse

        each(count // size, scale)
        outs.append(pltpu.make_async_copy(r.wide[g].at[pl.ds(start, count)], r.grads[i], sems.at[10 + i]))
        outs[-1].start()
    for copy in outs:
        copy.wait()


def run_finish(ins, layers):
    blocks, small = ins["blocks"], ins["small"]
    rows = ins["layer_in"].shape
    local, units = blocks[0].shape[0] // 4, small.shape[1]

    def shape(*dims):
        return jax.ShapeDtypeStruct(dims, F32)

    counts = (3 * local, local, local, 2 * local, local)
    outs = dict(
        layer_out=shape(*rows), input_grad=shape(*rows), memory_grad=shape(layers, *rows),
        gain_grad=shape(3, rows[1]), shift_grad=shape(3, rows[1]), bias_in_grad=shape(units), bias_out_grad=shape(rows[1]),
        grads=[shape(count, rows[1]) for count in counts] + [shape(*blocks[2].shape), shape(*blocks[3].shape)],
    )
    scratch = dict(
        layer=pltpu.VMEM(rows, F32), grad=pltpu.VMEM(rows, F32), source=pltpu.VMEM(rows, F32),
        memories=pltpu.VMEM((layers,) + rows, F32),
        block=[pltpu.VMEM(block.shape, BF16) for block in blocks],
        wide=[pltpu.VMEM(block.shape, F32) for block in blocks],
        sems=pltpu.SemaphoreType.DMA((17,)),
    )
    hbm = pl.ANY
    spaces = dict(
        configs=pltpu.SMEM, layer_in=hbm, grad_in=hbm, source_in=hbm, blocks=hbm,
        layer_out=hbm, input_grad=hbm, memory_grad=hbm, grads=hbm,
    )
    return call(finish_kernel, "finish", ins, outs, scratch, spaces, vmem_limit_bytes=60 * 2**20)


def per_device(
    inputs, memory, out_grad, lengths, src_lengths, configs, norm_gain, norm_bias,
    self_qkv, self_out, cross_q, cross_kv, cross_out, ffn_in, ffn_in_bias, ffn_out, ffn_out_bias,
):
    model = inputs.shape[1]
    layers = memory.shape[0]
    local = self_out.shape[0]
    done = run_layer(dict(
        lengths=lengths, src_lengths=src_lengths, configs=configs, gains=norm_gain, shifts=norm_bias,
        bias_in=ffn_in_bias, bias_out=ffn_out_bias, x_in=inputs, memory_in=memory, upstream_in=out_grad,
        shards=[
            self_qkv.transpose(1, 2, 0).reshape(3 * local, model), self_out, cross_q.T,
            cross_kv.transpose(1, 2, 0).reshape(2 * local, model), cross_out, ffn_in, ffn_out,
        ],
    ))
    out = run_finish(dict(
        configs=configs, small=done.small_out, layer_in=done.layer_out, grad_in=done.input_grad,
        source_in=done.memory_out, blocks=done.blocks,
    ), layers)
    grads = out.grads
    return (
        out.layer_out,
        out.input_grad,
        out.memory_grad,
        out.gain_grad,
        out.shift_grad,
        grads[0].reshape(3, local, model).transpose(2, 0, 1),
        grads[1],
        grads[2].T,
        grads[3].reshape(2, local, model).transpose(2, 0, 1),
        grads[4],
        grads[5],
        out.bias_in_grad,
        grads[6],
        out.bias_out_grad,
    )


def solution(mesh):
    rows = P(("grp", "dp", "tp"), None)
    stack = P(None, ("grp", "dp", "tp"), None)
    weights = (
        P(None, None, "tp"), P("tp", None), P(None, "tp"), P(None, None, "tp"), P("tp", None),
        P(None, "tp"), P("tp"), P("tp", None), P(),
    )
    return jax.shard_map(
        per_device,
        mesh=mesh,
        in_specs=(rows, stack, rows, P(("grp", "dp")), P(("grp", "dp")), P("grp", None), P(), P()) + weights,
        out_specs=(rows, rows, stack, P(), P()) + weights,
        check_vma=False,
    )
```

```python
import functools
import types

import jax
import jax.numpy as jnp
from jax import lax
from jax.experimental import pallas as pl
from jax.experimental.pallas import tpu as pltpu
from jax.sharding import PartitionSpec as P

HD = 80
LEN = 256
EPSILON = 1e-05
NEGATIVE = -1e30
SCALE = HD ** (-0.5)
LOG2E = 1.4426950408889634
F32 = jnp.float32
BF16 = jnp.bfloat16


MESH = pl.DeviceIdType.MESH


class Place:
    def __init__(self):
        self.tps = lax.axis_size("tp")
        self.extra = lax.axis_size("dp") // 2
        assert lax.axis_size("grp") == 4 and lax.axis_size("dp") % 2 == 0
        grp, dp, tp = (lax.axis_index(name) for name in ("grp", "dp", "tp"))
        core, low, high = dp % 2, grp % 2, grp // 2
        flip_low, flip_high = grp + 1 - 2 * low, grp + 2 - 4 * high
        self.grp, self.dp, self.tp, self.core = grp, dp, tp, core
        self.first_bit = (1 - core) * low + core * high
        self.second_bit = (1 - core) * high + core * low
        self.first = ((1 - core) * flip_low + core * flip_high, dp, tp)
        self.second = ((1 - core) * flip_high + core * flip_low, dp, tp)
        self.across = (3 - grp, dp, tp)
        self.sibling = (grp, dp + 1 - 2 * core, tp)
        self.above = (grp, dp, tp + 1)
        self.below = (grp, dp, tp - 1)
        self.has_above = tp < self.tps - 1
        self.has_below = tp > 0

    def copy_of(self, step):
        return (self.grp, ((self.dp // 2 + step) % self.extra) * 2 + self.core, self.tp)

    def nth_block(self, k):
        size = self.tps
        upper = (2 * self.tp) // size
        lead = (1 - upper) * self.tp + upper * (size - 1 - self.tp)
        spot = k + (k + size - lead) // size
        return (1 - upper) * spot + upper * (size - 1 - spot)

    def along(self, tp):
        return (self.grp, self.dp, tp)

    def barrier(self):
        sem = pltpu.get_barrier_semaphore()
        partners = [self.first, self.second, self.across, self.sibling]
        partners += [self.along((self.tp + step) % self.tps) for step in range(1, self.tps)]
        partners += [self.copy_of(step) for step in range(1, self.extra)]
        for device in partners:
            pl.semaphore_signal(sem, inc=1, device_id=device, device_id_type=MESH)
        pl.semaphore_wait(sem, len(partners))


def push(src, dst, send_sem, recv_sem, device):
    return pltpu.make_async_remote_copy(
        src_ref=src, dst_ref=dst, send_sem=send_sem, recv_sem=recv_sem, device_id=device, device_id_type=MESH
    )


def rows_of(ref, lead, start, count):
    return ref.at[lead, pl.ds(pl.multiple_of(start, 16), count)]


def add_units(total, term, unit):
    def step(i, carry):
        rows = pl.ds(pl.multiple_of(i * unit, 16), unit)
        total[rows] = total[rows] + term[rows]
        return carry

    lax.fori_loop(0, total.shape[0] // unit, step, 0)


class Spread:
    KINDS = 6

    def __init__(self, place, view, unit, sems):
        self.place, self.view, self.unit, self.sems = place, view, unit, sems
        f, s, c = place.first_bit, place.second_bit, place.core
        self.table = (
            (place.second, c * 4 + f * 2 + s, c * 4 + f * 2 + 1 - s, 1),
            (place.first, c * 4 + f * 2, c * 4 + 2 - f * 2, 2),
            (place.sibling, c * 4, 4 - c * 4, 4),
        )

    def region(self, start, count):
        return self.view(start * self.unit, count * self.unit)

    def own(self):
        return self.region(self.table[0][1], 1)

    def copy(self, n, lands=False):
        device, leaves, landing, count = self.table[n]
        part = self.region(landing if lands else leaves, count)
        return push(part, part, self.sems(2 * n), self.sems(2 * n + 1), device)

    def step(self, stage):
        if stage > 0:
            self.copy(stage - 1, lands=True).wait_recv()
        if stage < 3:
            self.copy(stage).start()

    def finish(self):
        for n in range(3):
            self.copy(n).wait_send()


class Gather:
    KINDS = Spread.KINDS + 3

    def __init__(self, place, buffers, sems):
        self.place, self.buffers, self.sems = place, buffers, sems
        self.unit = [ref.shape[1] // 8 for ref in buffers]
        self.others = place.tps - 1

    def spread(self, g, j):
        return Spread(
            self.place,
            lambda start, count: rows_of(self.buffers[g], j, start, count),
            self.unit[g],
            lambda kind: self.sems.at[kind, g, j],
        )

    def relays(self, g, j):
        p = self.place
        part = self.spread(g, j).own()
        sem = lambda n: self.sems.at[Spread.KINDS + n, g, j]
        return (
            (jnp.logical_and(j <= p.tp, p.has_above), push(part, part, sem(0), sem(2), p.above)),
            (jnp.logical_and(j >= p.tp, p.has_below), push(part, part, sem(1), sem(2), p.below)),
        )

    def start(self, g):
        for needed, copy in self.relays(g, self.place.tp):
            pl.when(needed)(copy.start)

    def passes(self, j):
        p = self.place
        up = jnp.logical_and(j < p.tp, p.has_above)
        down = jnp.logical_and(j > p.tp, p.has_below)
        return jnp.logical_or(up, down)

    def relay(self, g, k):
        j = self.place.nth_block(k)

        @pl.when(self.passes(j))
        def _():
            relays = self.relays(g, j)
            relays[0][1].wait_recv()
            for needed, copy in relays:
                pl.when(needed)(copy.start)

    def step(self, g, k, stage):
        j = self.place.nth_block(k)
        if stage == 0:
            pl.when(jnp.logical_not(self.passes(j)))(self.relays(g, j)[0][1].wait_recv)
        self.spread(g, j).step(stage)

    def drain(self, g, j):
        for needed, copy in self.relays(g, j):
            pl.when(needed)(copy.wait_send)

        @pl.when(j != self.place.tp)
        def _():
            self.spread(g, j).finish()


class Line:
    def __init__(self, place, buffer, sems):
        self.place, self.buffer, self.sems = place, buffer, sems

    def relays(self, j):
        p = self.place
        part = self.buffer.at[j]
        return (
            (jnp.logical_and(j <= p.tp, p.has_above), push(part, part, self.sems.at[0, j], self.sems.at[2, j], p.above)),
            (jnp.logical_and(j >= p.tp, p.has_below), push(part, part, self.sems.at[1, j], self.sems.at[2, j], p.below)),
        )

    def start(self):
        for needed, copy in self.relays(self.place.tp):
            pl.when(needed)(copy.start)

    def step(self, k):
        j = self.place.nth_block(k)
        relays = self.relays(j)
        relays[0][1].wait_recv()
        for needed, copy in relays:
            pl.when(needed)(copy.start)

    def finish(self):
        for j in range(self.place.tps):
            for needed, copy in self.relays(j):
                pl.when(needed)(copy.wait_send)


class Reduce:
    KINDS = 8 + Spread.KINDS + 2

    def __init__(self, place, grads, halves, planes, lines, extras, totals, sems):
        self.place, self.grads, self.totals, self.sems = place, grads, totals, sems
        self.halves, self.planes, self.lines, self.extras = halves, planes, lines, extras
        self.unit = [ref.shape[1] // 8 for ref in grads]

    def sem(self, kind, g, j):
        return self.sems.at[kind, g, j]

    def rows(self, g, j, half, unit, count=1):
        size = self.unit[g]
        return rows_of(self.grads[g], j, (half * 4 + unit) * size, count * size)

    def move(self, g, j, stage):
        p, size = self.place, self.unit[g]
        if stage == 0:
            part, landing, device = self.rows(g, j, 1 - p.core, 0, 4), self.halves[g].at[j], p.sibling
        elif stage == 1:
            part, device = self.rows(g, j, p.core, 2 - p.first_bit * 2, 2), p.first
            landing = self.planes[g].at[j, pl.ds(0, 2 * size)]
        else:
            part, device = self.rows(g, j, p.core, p.first_bit * 2 + 1 - p.second_bit), p.second
            landing = self.planes[g].at[j, pl.ds(2 * size, size)]
        return push(part, landing, self.sem(2 * stage, g, j), self.sem(2 * stage + 1, g, j), device)

    def kept(self, g, j, stage):
        p, size = self.place, self.unit[g]
        if stage == 0:
            return self.rows(g, j, p.core, 0, 4), self.halves[g].at[j]
        if stage == 1:
            return self.rows(g, j, p.core, p.first_bit * 2, 2), self.planes[g].at[j, pl.ds(0, 2 * size)]
        return self.piece(g, j), self.planes[g].at[j, pl.ds(2 * size, size)]

    def piece(self, g, j):
        p = self.place
        return self.rows(g, j, p.core, p.first_bit * 2 + p.second_bit)

    def along(self, g, j):
        p = self.place
        return push(self.piece(g, j), self.lines[g].at[p.tp], self.sem(6, g, j), self.sem(7, g, p.tp), p.along(j))

    def from_place(self, g, j):
        p = self.place
        return push(self.piece(g, j), self.lines[g].at[j], self.sem(6, g, j), self.sem(7, g, j), p.along(j))

    def step(self, g, j, stage):
        if stage > 0:
            self.move(g, j, stage - 1).wait_recv()
            add_units(*self.kept(g, j, stage - 1), self.unit[g])
        if stage < 3:
            self.move(g, j, stage).start()
        else:
            pl.when(j != self.place.tp)(self.along(g, j).start)

    def spread(self, g):
        return Spread(
            self.place,
            lambda start, count: self.totals[g].at[pl.ds(pl.multiple_of(start, 16), count)],
            self.unit[g],
            lambda kind: self.sems.at[8 + kind, g, 0],
        )

    def copies(self, g, step):
        p = self.place
        base = self.KINDS - 2
        return push(
            self.piece(g, p.tp), self.extras[g].at[step], self.sem(base, g, step), self.sem(base + 1, g, step), p.copy_of(step)
        )

    def settle(self, g):
        p = self.place
        piece = self.piece(g, p.tp)
        total = piece[...].astype(F32)
        for k in range(p.tps - 1):
            j = p.nth_block(k)
            self.from_place(g, j).wait_recv()
            total = total + self.lines[g][j].astype(F32)
        if p.extra > 1:
            piece[...] = total.astype(BF16)
            for step in range(1, p.extra):
                self.copies(g, step).start()
            for step in range(1, p.extra):
                self.copies(g, step).wait()
                total = total + self.extras[g][step].astype(F32)
        own = self.spread(g).own()
        own[...] = total.astype(BF16)
        self.spread(g).step(0)

    def share(self, g, stage):
        self.spread(g).step(stage)

    def finish(self, g):
        p = self.place
        for j in range(p.tps):
            for stage in range(3):
                self.move(g, j, stage).wait_send()
            pl.when(j != p.tp)(self.along(g, j).wait_send)
        self.spread(g).finish()


class SumSmall:
    @staticmethod
    def slots(tps, extra):
        return 8 + tps + extra

    def __init__(self, place, slots, sems):
        self.place, self.slots_ref, self.sems = place, slots, sems

    def move(self, source, target, device, kind):
        slots = self.slots_ref
        return push(slots.at[source], slots.at[target], self.sems.at[0, kind], self.sems.at[1, target], device)

    def in_plane(self):
        p = self.place
        return [self.move(2, 3 + i, device, 3 + i) for i, device in enumerate((p.second, p.first, p.across))]

    def copies(self):
        p = self.place
        return [self.move(6, 8 + p.tps + s, p.copy_of(s), 8 + p.tps + s) for s in range(1, p.extra)]

    def along(self, k, lands=False):
        p = self.place
        j = p.nth_block(k)
        return self.move(7, 8 + (j if lands else p.tp), p.along(j), 8 + j)

    def start(self):
        self.move(0, 1, self.place.sibling, 1).start()

    def exchange(self, stage):
        p, slots = self.place, self.slots_ref
        if stage == 0:
            self.move(0, 1, p.sibling, 1).wait_recv()
            slots[2] = slots[0] + slots[1]
            for copy in self.in_plane():
                copy.start()
        else:
            for copy in self.in_plane():
                copy.wait_recv()
            slots[6] = (slots[2] + slots[3]) + (slots[4] + slots[5])
            for copy in self.copies():
                copy.start()
            total = slots[6]
            for s, copy in enumerate(self.copies()):
                copy.wait_recv()
                total = total + slots[9 + p.tps + s]
            slots[7] = total
            for k in range(p.tps - 1):
                self.along(k).start()

    def total(self):
        p, slots = self.place, self.slots_ref
        value = slots[7]
        for k in range(p.tps - 1):
            self.along(k, lands=True).wait_recv()
            value = value + slots[8 + p.nth_block(k)]
        return value

    def finish(self):
        p = self.place
        self.move(0, 1, p.sibling, 1).wait_send()
        for copy in self.in_plane() + self.copies():
            copy.wait_send()
        for k in range(p.tps - 1):
            self.along(k).wait_send()


def dot_nn(left, right):
    return lax.dot_general(left, right, (((1,), (0,)), ((), ())), preferred_element_type=F32)


def dot_nt(left, right):
    return lax.dot_general(left, right, (((1,), (1,)), ((), ())), preferred_element_type=F32)


def dot_tn(left, right):
    return lax.dot_general(left, right, (((0,), (0,)), ((), ())), preferred_element_type=F32)


def column(axis, shape):
    return lax.broadcasted_iota(jnp.int32, shape, axis)


def each(count, step):

    def run(i, carry):
        step(i)
        return carry

    lax.fori_loop(0, count, run, 0)


CHUNK = 128
CUBE = 0.044715
ROOT = 0.7978845608028654


def layer_kernel(r):
    r.a2, r.a3, r.e = (r.memory.at[i] for i in range(3))
    columns = pl.ds(0, r.x.shape[1])
    r.dh, r.dm = r.before.at[:, columns], r.down.at[:, columns]
    place = Place()
    n = place.tps
    x, model = r.x, r.x.shape[1]
    owned = x.shape[0]
    sentences = owned // LEN
    local = r.c[0].shape[1]
    heads_here = local // HD
    units = r.hidden.shape[1]
    layers = r.memory.shape[0]
    weights = r.w
    lengths, sources, configs = r.lengths, r.src_lengths, r.configs
    width, heads, hidden_units, depth = (configs[0, i] for i in range(4))
    inv_width = 1.0 / jnp.full((1, 1), width.astype(F32))
    inv_depth = 1.0 / jnp.full((1, 1), depth.astype(F32))
    width_mask = (column(1, (1, model)) < width).astype(F32)

    local_sem = r.local_sems
    spots = (
        (0, 0, 3 * local), (0, 3 * local, local),
        (1, 0, local), (1, local, 2 * local), (1, 3 * local, local),
        (2, 0, weights[2].shape[1]), (3, 0, weights[3].shape[1]),
    )
    fills = [
        (g, pltpu.make_async_copy(r.shards[i], weights[g].at[place.tp, pl.ds(start, size)], local_sem.at[i]))
        for i, (g, start, size) in enumerate(spots)
    ]
    loads = [
        pltpu.make_async_copy(source, target, local_sem.at[7 + i])
        for i, (source, target) in enumerate(((r.x_in, r.x), (r.memory_in, r.memory), (r.upstream_in, r.upstream)))
    ]
    for _, copy in fills[:2]:
        copy.start()
    loads[0].start()
    for _, copy in fills[2:]:
        copy.start()
    loads[1].start()
    loads[2].start()
    r.bias[place.tp] = jnp.broadcast_to(r.bias_in[...].reshape(1, units), r.bias.shape[1:])
    place.barrier()

    gather = Gather(place, weights, r.gather_sems)
    bias = Line(place, r.bias, r.bias_sems)
    for g in range(4):
        for group, copy in fills:
            if group == g:
                copy.wait()
        gather.start(g)
        if g == 0:
            bias.start()
    order = [(g, k) for g in (0, 1) for k in range(n - 1)] + [(g, k) for k in range(n - 1) for g in (2, 3)]

    places = (
        (0, 1, 2, 5), (1, 2, 4, 7), (2, 3, 6, 9), (3, 5, 7, 11), (4, 6, 9, 12), (6, 8, 10, 11),
        (7, 10, 11, 15), (9, 11, 13, 15), (11, 12, 15, 18), (12, 15, 20, 23), (13, 16, 21, 23), (15, 18, 22, 25),
    )
    assert len(places) == len(order)

    def gather_at(spot):
        found = [(stage, e) for e, stages in enumerate(places) for stage, at in enumerate(stages) if at == spot]
        for stage, e in sorted(found):
            if stage == 0 and e == 0:
                gather.relay(*order[0])
            gather.step(*order[e], stage)
            if stage == 0 and e + 1 < len(order):
                gather.relay(*order[e + 1])

    def gather_table(start):
        return {(k, b): [functools.partial(gather_at, start + 2 * k + b)] for k in range(n) for b in range(2)}

    def block(k):
        later = (k + n - 1) // n
        return (1 - later) * place.tp + later * place.nth_block(k - 1)

    def block_last(k):
        own = k // (n - 1)
        return own * place.tp + (1 - own) * place.nth_block(k)

    def hooks(table, k, b):
        for (kk, bb), steps in table.items():

            @pl.when(jnp.logical_and(k == kk, b == bb))
            def _():
                for step in steps:
                    step()

    def chunk(i):
        return pl.ds(pl.multiple_of(i * CHUNK, CHUNK), CHUNK)

    def keep_of(i):
        per = LEN // CHUNK
        spot = column(0, (CHUNK, 1)) + (i % per) * CHUNK
        return (spot < lengths[place.tp * sentences + i // per]).astype(F32) * width_mask

    def norm_parts(rows):
        mean = jnp.sum(rows * width_mask, axis=-1, keepdims=True) * inv_width
        centred = (rows - mean) * width_mask
        spread = jnp.sum(centred * centred, axis=-1, keepdims=True) * inv_width
        rstd = lax.rsqrt(spread + EPSILON)
        return centred * rstd, rstd

    def norm(rows, which):
        hat, _ = norm_parts(rows)
        return ((hat * r.gains[which:which + 1] + r.shifts[which:which + 1]) * width_mask).astype(BF16)

    def fold(values):
        return jnp.sum(values.reshape(values.shape[0] // 8, 8, values.shape[1]), axis=0)

    def norm_backward(rows, which, upstream):
        hat, rstd = norm_parts(rows)
        upstream = upstream * width_mask
        sums = r.norm_sums
        sums[which] = sums[which] + fold(upstream * hat)
        sums[3 + which] = sums[3 + which] + fold(upstream)
        scaled = upstream * r.gains[which:which + 1]
        first = jnp.sum(scaled, axis=-1, keepdims=True) * inv_width
        second = jnp.sum(scaled * hat, axis=-1, keepdims=True) * inv_width
        return (rstd * (scaled - first - hat * second)) * width_mask

    chunks = owned // CHUNK

    def each_chunk(step):
        each(chunks, step)

    acc, da, dh = r.acc, r.da, r.dh
    zeros = jnp.zeros((CHUNK, model), F32)
    r.norm_sums[...] = jnp.zeros(r.norm_sums.shape, F32)
    r.bias_sums[...] = jnp.zeros(r.bias_sums.shape, F32)

    def sentence(b):
        return pl.ds(pl.multiple_of(b * LEN, LEN), LEN)

    def head_keep(j, h):
        return jnp.where(j * heads_here + h < heads, 1.0, 0.0).astype(F32)

    def causal(b, start, size):
        return column(0, (size, 128)) <= column(1, (size, 128)) + start

    def crossing(b, start, size):
        return column(0, (size, 1)) < sources[place.tp * sentences + b]

    def reach(g, start):
        return start + 128 if g == 0 else LEN

    def bands(h):
        return [pl.ds(i * local + h * HD, HD) for i in range(3)]

    def lanes(b):
        return pl.ds(b * LEN, LEN)

    pairs = [(b, h) for b in range(sentences) for h in range(heads_here)]

    def attend(k, table, g, allowed):
        w, t, c, p = weights[g], r.t[g], r.c[g], r.p[g]
        j = block(k)
        hooks(table, k, 0)
        if g == 0:
            t[j] = dot_nt(w[j, :3 * local], r.a1[...]).astype(BF16)
        else:
            t[j, :local] = dot_nt(w[j, :local], r.a2[...]).astype(BF16)
            t[j, local:] = dot_nt(w[j, local:3 * local], r.m[...]).astype(BF16)
        heads_of = [[t[j, band, lanes(b)] for band in bands(h)] for b, h in pairs]
        for i, (query, keys, _) in enumerate(heads_of):
            r.scores[i] = dot_tn(keys, query)
        for i, (b, h) in enumerate(pairs):
            for start in range(0, LEN, 128):
                part, size = pl.ds(start, 128), reach(g, start)
                score = jnp.where(allowed(b, start, size), r.scores[i, :size, part], NEGATIVE)
                raised = jnp.exp2((score - jnp.max(score, axis=0, keepdims=True)) * (SCALE * LOG2E))
                p[j, i, :size, part] = (raised * (1.0 / jnp.sum(raised, axis=0, keepdims=True))).astype(BF16)
                if size < LEN:
                    p[j, i, size:, part] = jnp.zeros((LEN - size, 128), BF16)
            c[j, pl.ds(h * HD, HD), lanes(b)] = (dot_nn(heads_of[i][2], p[j, i]) * head_keep(j, h)).astype(BF16)
        hooks(table, k, 1)
        acc[...] = acc[...] + dot_tn(c[j], w[j, 3 * local:])

    def attend_backward(k, table, g, query_rows, key_rows):
        w, t, c, p = weights[g], r.t[g], r.c[g], r.p[g]
        j = block_last(k)
        e, dt, dc = r.e, r.dt, r.dc
        gather.drain(g, j)
        dc_all = dot_nt(w[j, 3 * local:], e[...])
        for h in range(heads_here):
            dc[h * HD:(h + 1) * HD] = (dc_all[h * HD:(h + 1) * HD] * head_keep(j, h)).astype(BF16)
        heads_of = [[t[j, band, lanes(b)] for band in bands(h)] for b, h in pairs]
        dc_of = [dc[h * HD:(h + 1) * HD, lanes(b)] for b, h in pairs]
        for i, (_, _, values) in enumerate(heads_of):
            r.scores[i] = dot_tn(values, dc_of[i])
        for i, (b, h) in enumerate(pairs):
            dt[bands(h)[2], lanes(b)] = dot_nt(dc_of[i], p[j, i]).astype(BF16)
        w[j, 3 * local:] = dot_nn(c[j], e[...]).astype(BF16)
        for i, (b, h) in enumerate(pairs):
            (query, keys, _), (dq, dk, _) = heads_of[i], bands(h)
            for start in range(0, LEN, 128):
                part, size = pl.ds(start, 128), reach(g, start)
                dp, wide = r.scores[i, :size, part], p[j, i, :size, part].astype(F32)
                r.ds[i, :size, part] = (wide * (dp - jnp.sum(dp * wide, axis=0, keepdims=True))).astype(BF16)
                if size < LEN:
                    r.ds[i, size:, part] = jnp.zeros((LEN - size, 128), BF16)
            dt[dq, lanes(b)] = (dot_nn(keys, r.ds[i]) * SCALE).astype(BF16)
            dt[dk, lanes(b)] = (dot_nt(query, r.ds[i]) * SCALE).astype(BF16)
        hooks(table, k, 1)
        if g == 0:
            da[...] = da[...] + dot_tn(dt[...], w[j, :3 * local])
            w[j, :3 * local] = dot_nn(dt[...], query_rows[...]).astype(BF16)
        else:
            da[...] = da[...] + dot_tn(dt[:local], w[j, :local])
            r.dm[...] = r.dm[...] + dot_tn(dt[local:], w[j, local:3 * local])
            w[j, :local] = dot_nn(dt[:local], query_rows[...]).astype(BF16)
            w[j, local:3 * local] = dot_nn(dt[local:], key_rows[...]).astype(BF16)

    def feed(k, table):
        j = block(k)
        w_up, w_down = weights[2], weights[3]
        hooks(table, k, 0)
        unit = column(1, (1, units)) + j * units
        kept = jnp.where(unit < hidden_units, 0.5, 0.0)
        found = []
        for b in range(sentences):
            rows = sentence(b)
            found.append((dot_nn(r.a3[rows], w_up[j]) + r.bias[j, 0:1], dot_nt(r.e[rows], w_down[j])))
        for b, (before, down) in enumerate(found):
            rows = sentence(b)
            square = before * before
            bent = jnp.tanh(before * (ROOT + ROOT * CUBE * square))
            half = kept + kept * bent
            through = before * half
            r.hidden[rows] = through.astype(BF16)
            slope = half + (through - through * bent) * (ROOT + 3.0 * CUBE * ROOT * square)
            du = (down * slope).astype(BF16)
            r.dhidden[rows] = du
            r.bias_sums[j] = r.bias_sums[j] + fold(du.astype(F32))
        for b in range(sentences):
            rows = sentence(b)
            acc[rows] = acc[rows] + dot_nn(r.hidden[rows], w_down[j])
            da[rows] = da[rows] + dot_nt(r.dhidden[rows], w_up[j])
        hooks(table, k, 1)
        gather.drain(2, j)
        gather.drain(3, j)
        w_down[j] = dot_tn(r.hidden[...], r.e[...]).astype(BF16)
        w_up[j] = dot_nn(r.a3t[...], r.dhidden[...]).astype(BF16)

    loads[0].wait()

    def begin(i):
        rows = chunk(i)
        r.a1[rows] = norm(x[rows].astype(F32), 0)
        acc[rows] = zeros
        da[rows] = zeros

    each_chunk(begin)
    gather_at(0)
    loads[1].wait()

    def mix(i):
        rows = chunk(i)
        total = jnp.zeros((CHUNK, model), F32)
        for level in range(layers):
            chosen = (jnp.full((1, 1), depth) >= layers - level).astype(F32)
            total = total + chosen * r.memory[level, rows].astype(F32)
        r.m[rows] = (total * inv_depth * width_mask).astype(BF16)

    each_chunk(mix)
    gather_at(1)
    loads[2].wait()
    r.out_sums[...] = jnp.zeros(r.out_sums.shape, F32)

    def grad_in(i):
        rows = chunk(i)
        masked = r.upstream[rows].astype(F32) * keep_of(i)
        r.out_sums[...] = r.out_sums[...] + fold(masked)
        r.e[rows] = masked.astype(BF16)

    each_chunk(grad_in)
    gather_at(2)

    others = n - 1
    assert n == 4
    table = gather_table(3)
    for k in range(others):
        table[k + 1, 0].append(functools.partial(bias.step, k))
    each(n, lambda k: attend(k, table, 0, causal))

    def after_self(i):
        rows = chunk(i)
        h = x[rows].astype(F32) + acc[rows] * keep_of(i)
        r.h1[rows] = h
        r.a2[rows] = norm(h, 1)
        acc[rows] = zeros

    each_chunk(after_self)
    table2 = gather_table(11)
    each(n, lambda k: attend(k, table2, 1, crossing))

    def after_cross(i):
        rows = chunk(i)
        h = r.h1[rows] + acc[rows] * keep_of(i)
        r.h2[rows] = h
        r.a3[rows] = norm(h, 2)
        acc[rows] = zeros

    each_chunk(after_cross)
    r.a3t[...] = r.a3[...].T

    reduce = Reduce(
        place, weights, r.half, r.plane, r.line, r.extra, r.total, r.reduce_sems
    )
    plan = {}

    def add(tick, order, step, *args):
        plan.setdefault(tick, []).append((order, len(plan.get(tick, ())), functools.partial(step, *args)))

    def r_tick(tick):
        for _, _, step in sorted(plan.get(tick, ()), key=lambda entry: entry[:2]):
            step()

    def store(g):
        return pltpu.make_async_copy(r.total[g], r.blocks[g], local_sem.at[10 + g])

    times = {
        3: ([(1, 2, 6, 10), (3, 4, 8, 11), (5, 6, 9, 13), (7, 9, 11, 15)], (17, 19, 21, 25)),
        2: ([(1, 3, 6, 9), (3, 6, 8, 11), (5, 8, 10, 13), (7, 9, 12, 16)], (19, 21, 23, 26)),
        1: ([(10, 11, 14, 16), (12, 14, 16, 18), (14, 15, 19, 21), (16, 17, 19, 21)], (24, 27, 28, 29)),
        0: ([(19, 20, 22, 24), (21, 22, 24, 25), (23, 24, 25, 26), (25, 26, 27, 28)], (28, 29, 30, 31)),
    }
    for late, g in enumerate((3, 2, 1, 0)):
        for k, stages in enumerate(times[g][0]):
            j = block(k) if g > 1 else block_last(k)
            for stage, tick in enumerate(stages):
                add(tick, stage, reduce.step, g, j, stage)
        for stage, tick in enumerate(times[g][1]):
            if stage == 0:
                add(tick, 20 - late, reduce.settle, g)
            else:
                add(tick, 30 + stage - late, reduce.share, g, stage)
        add(times[g][1][-1], 50, lambda g=g: store(g).start())

    def reduce_ticks(*numbers):
        return [functools.partial(r_tick, i) for i in numbers]

    def at_end(k, numbers):
        for kk, number in enumerate(numbers):

            @pl.when(k == kk)
            def _():
                r_tick(number)

    table3 = gather_table(19)
    for k in range(1, n):
        table3[k, 1] += reduce_ticks(2 * k)

    def feed_step(k):
        feed(k, table3)
        at_end(k, [2 * i + 1 for i in range(n)])

    each(n, feed_step)
    r_tick(8)
    out_copy = pltpu.make_async_copy(acc, r.layer_out, local_sem.at[14])

    def after_feed(i):
        rows = chunk(i)
        keep = keep_of(i)
        acc[rows] = r.h2[rows] + (acc[rows] + r.bias_out[...].reshape(1, model)) * keep
        down = r.upstream[rows].astype(F32) + norm_backward(r.h2[rows], 2, da[rows])
        dh[rows] = down
        r.e[rows] = (down * keep).astype(BF16)
        da[rows] = zeros
        r.dm[rows] = zeros

    each_chunk(after_feed)
    out_copy.start()
    table4 = {(k, 1): reduce_ticks(9 + 2 * k) for k in range(n)}

    def cross_step(k):
        attend_backward(k, table4, 1, r.a2, r.m)
        at_end(k, [10 + 2 * i for i in range(n)])

    each(n, cross_step)
    memory_copy = pltpu.make_async_copy(r.dm, r.memory_out, local_sem.at[15])
    memory_copy.start()

    def before_cross(i):
        rows = chunk(i)
        down = dh[rows] + norm_backward(r.h1[rows], 1, da[rows])
        dh[rows] = down
        r.e[rows] = (down * keep_of(i)).astype(BF16)
        da[rows] = zeros

    each_chunk(before_cross)
    r_tick(17)
    table5 = {(k, 1): reduce_ticks(18 + 2 * k) for k in range(n)}

    def self_step(k):
        attend_backward(k, table5, 0, r.a1, r.a1)
        at_end(k, [19 + 2 * i for i in range(n)])

    each(n, self_step)

    def before_self(i):
        rows = chunk(i)
        dh[rows] = dh[rows] + norm_backward(x[rows].astype(F32), 0, da[rows])

    each_chunk(before_self)
    grad_copy = pltpu.make_async_copy(dh, r.input_grad, local_sem.at[16])
    grad_copy.start()

    small = SumSmall(place, r.slots, r.small_sems)

    def small_start():
        own = r.slots.at[0]
        own[...] = jnp.zeros(own.shape, F32)
        for i in range(6):
            own[i:i + 1, :model] = jnp.sum(r.norm_sums[i], axis=0, keepdims=True)
        own[6:7, :model] = jnp.sum(r.out_sums[...], axis=0, keepdims=True)
        tokens = lengths[place.tp * sentences]
        for b in range(1, sentences):
            tokens = tokens + lengths[place.tp * sentences + b]
        own[7:8] = jnp.full((1, own.shape[1]), tokens.astype(F32))
        for i in range(n):
            own[8 + i:9 + i] = jnp.sum(r.bias_sums[i], axis=0, keepdims=True)
        small.start()

    add(26, 5, small_start)
    for stage in range(2):
        add(27 + stage, 5, small.exchange, stage)
    final = max(plan)
    for tick in range(26, final + 1):
        r_tick(tick)
    r.small_out[...] = small.total()
    bias.finish()
    for copy in (out_copy, memory_copy, grad_copy):
        copy.wait()
    for g in range(4):
        reduce.finish(g)
        store(g).wait()
    small.finish()


def call(kernel, name, ins, outs, scratch, spaces, **options):
    trees = (ins, outs, scratch)
    structure = jax.tree_util.tree_structure(trees)

    def body(*refs):
        groups = jax.tree_util.tree_unflatten(structure, refs)
        kernel(types.SimpleNamespace(**groups[0], **groups[1], **groups[2]))

    def specs(group):
        return [
            pl.BlockSpec(memory_space=spaces.get(key, pltpu.VMEM))
            for key in sorted(group) for _ in jax.tree_util.tree_leaves(group[key])
        ]

    leaves = jax.tree_util.tree_leaves
    values = pl.pallas_call(
        body,
        out_shape=leaves(outs),
        in_specs=specs(ins),
        out_specs=specs(outs),
        scratch_shapes=leaves(scratch),
        compiler_params=pltpu.CompilerParams(**options),
        name=name,
    )(*leaves(ins))
    return types.SimpleNamespace(**jax.tree_util.tree_unflatten(jax.tree_util.tree_structure(outs), values))


def run_layer(ins):
    n, extra = lax.axis_size("tp"), lax.axis_size("dp") // 2
    owned, model = ins["x_in"].shape
    memory, shards = ins["memory_in"], ins["shards"]
    local, units = shards[1].shape[0], ins["bias_in"].shape[0]
    small = (16, units)
    assert n <= 8 and units >= model and memory.shape[0] >= 3
    shapes = [(n, 4 * local, model)] * 2 + [(n,) + shards[5].shape, (n,) + shards[6].shape]
    small_slots = SumSmall.slots(n, extra)

    def vmem(*shape):
        return pltpu.VMEM(shape, BF16)

    def wide(*shape):
        return pltpu.VMEM(shape, F32)

    def eighths(*lead, parts=1):
        return [vmem(*lead, rows * parts // 8, columns) for _, rows, columns in shapes]

    dma = pltpu.SemaphoreType.DMA
    scratch = dict(
        w=[vmem(*shape) for shape in shapes],
        bias=wide(n, 8, units),
        x=vmem(owned, model),
        memory=vmem(*memory.shape),
        upstream=vmem(owned, model),
        a1=vmem(owned, model),
        m=vmem(owned, model),
        h1=wide(owned, model),
        h2=wide(owned, model),
        acc=wide(owned, model),
        da=wide(owned, model),
        t=[vmem(n, 3 * local, owned)] * 2,
        c=[vmem(n, local, owned)] * 2,
        p=[vmem(n, owned // LEN * (local // HD), LEN, LEN)] * 2,
        dt=vmem(3 * local, owned),
        dc=vmem(local, owned),
        a3t=vmem(model, owned),
        scores=wide(owned // LEN * (local // HD), LEN, LEN),
        ds=vmem(owned // LEN * (local // HD), LEN, LEN),
        before=wide(owned, units),
        down=wide(owned, units),
        hidden=vmem(owned, units),
        dhidden=vmem(owned, units),
        bias_sums=wide(n, 8, units),
        norm_sums=wide(6, 8, model),
        out_sums=wide(8, model),
        half=eighths(n, parts=4),
        plane=eighths(n, parts=3),
        line=eighths(n),
        extra=eighths(extra),
        total=eighths(parts=8),
        slots=wide(small_slots, *small),
        gather_sems=dma((Gather.KINDS, 4, n)),
        bias_sems=dma((3, n)),
        reduce_sems=dma((Reduce.KINDS, 4, max(n, extra))),
        small_sems=dma((2, small_slots)),
        local_sems=dma((17,)),
    )
    rows = jax.ShapeDtypeStruct((owned, model), F32)
    outs = dict(
        layer_out=rows, input_grad=rows, memory_out=rows, small_out=jax.ShapeDtypeStruct(small, F32),
        blocks=[jax.ShapeDtypeStruct(shape[1:], BF16) for shape in shapes],
    )
    smem, hbm = pltpu.SMEM, pl.ANY
    spaces = dict(
        lengths=smem, src_lengths=smem, configs=smem, x_in=hbm, memory_in=hbm, upstream_in=hbm, shards=hbm,
        layer_out=hbm, input_grad=hbm, memory_out=hbm, blocks=hbm,
    )
    return call(
        layer_kernel, "layer", ins, outs, scratch, spaces,
        collective_id=1, has_side_effects=True, vmem_limit_bytes=64 * 2**20,
    )


def finish_kernel(r):
    small, configs, sems = r.small, r.configs, r.sems
    model = r.gain_grad.shape[1]
    layers = r.memory_grad.shape[0]
    place = lax.axis_index("tp")
    local = r.grads[1].shape[0]
    parts = (
        (0, 0, 3 * local), (0, 3 * local, local),
        (1, 0, local), (1, local, 2 * local), (1, 3 * local, local),
        (2, 0, r.block[2].shape[0]), (3, 0, r.block[3].shape[0]),
    )
    loads = [pltpu.make_async_copy(r.blocks[g], r.block[g], sems.at[g]) for g in range(4)]
    rows = [
        pltpu.make_async_copy(source, target, sems.at[4 + i])
        for i, (source, target) in enumerate(((r.layer_in, r.layer), (r.grad_in, r.grad), (r.source_in, r.source)))
    ]
    outs = [pltpu.make_async_copy(r.layer, r.layer_out, sems.at[7]), pltpu.make_async_copy(r.grad, r.input_grad, sems.at[8])]
    for copy in rows + loads:
        copy.start()
    inverse = 1.0 / small[7:8, :1]
    r.gain_grad[...] = small[:3, :model] * inverse
    r.shift_grad[...] = small[3:6, :model] * inverse
    r.bias_out_grad[...] = (small[6:7, :model] * inverse).reshape(model)
    r.bias_in_grad[...] = (small[pl.ds(8 + place, 1)] * inverse).reshape(small.shape[1])
    width, depth = configs[0, 0], configs[0, 3]
    factor = (column(1, (1, model)) < width).astype(F32) / jnp.full((1, 1), depth.astype(F32))
    for i in range(2):
        rows[i].wait()
        outs[i].start()
    rows[2].wait()

    def spread(i):
        part = pl.ds(pl.multiple_of(i * 64, 64), 64)
        value = r.source[part] * factor
        for level in range(layers):
            chosen = (jnp.full((1, 1), depth) >= layers - level).astype(F32)
            r.memories[level, part] = value * chosen

    each(r.source.shape[0] // 64, spread)
    outs.append(pltpu.make_async_copy(r.memories, r.memory_grad, sems.at[9]))
    outs[2].start()
    for i, (g, start, count) in enumerate(parts):
        if start == 0:
            loads[g].wait()

        size = 80 if count % 80 == 0 else 96

        def scale(at):
            there = pl.ds(pl.multiple_of(start + at * size, 16), size)
            r.wide[g][there] = r.block[g][there].astype(F32) * inverse

        each(count // size, scale)
        outs.append(pltpu.make_async_copy(r.wide[g].at[pl.ds(start, count)], r.grads[i], sems.at[10 + i]))
        outs[-1].start()
    for copy in outs:
        copy.wait()


def run_finish(ins, layers):
    blocks, small = ins["blocks"], ins["small"]
    rows = ins["layer_in"].shape
    local, units = blocks[0].shape[0] // 4, small.shape[1]

    def shape(*dims):
        return jax.ShapeDtypeStruct(dims, F32)

    counts = (3 * local, local, local, 2 * local, local)
    outs = dict(
        layer_out=shape(*rows), input_grad=shape(*rows), memory_grad=shape(layers, *rows),
        gain_grad=shape(3, rows[1]), shift_grad=shape(3, rows[1]), bias_in_grad=shape(units), bias_out_grad=shape(rows[1]),
        grads=[shape(count, rows[1]) for count in counts] + [shape(*blocks[2].shape), shape(*blocks[3].shape)],
    )
    scratch = dict(
        layer=pltpu.VMEM(rows, F32), grad=pltpu.VMEM(rows, F32), source=pltpu.VMEM(rows, F32),
        memories=pltpu.VMEM((layers,) + rows, F32),
        block=[pltpu.VMEM(block.shape, BF16) for block in blocks],
        wide=[pltpu.VMEM(block.shape, F32) for block in blocks],
        sems=pltpu.SemaphoreType.DMA((17,)),
    )
    hbm = pl.ANY
    spaces = dict(
        configs=pltpu.SMEM, layer_in=hbm, grad_in=hbm, source_in=hbm, blocks=hbm,
        layer_out=hbm, input_grad=hbm, memory_grad=hbm, grads=hbm,
    )
    return call(finish_kernel, "finish", ins, outs, scratch, spaces, vmem_limit_bytes=60 * 2**20)


def per_device(
    inputs, memory, out_grad, lengths, src_lengths, configs, norm_gain, norm_bias,
    self_qkv, self_out, cross_q, cross_kv, cross_out, ffn_in, ffn_in_bias, ffn_out, ffn_out_bias,
):
    model = inputs.shape[1]
    layers = memory.shape[0]
    local = self_out.shape[0]
    done = run_layer(dict(
        lengths=lengths, src_lengths=src_lengths, configs=configs, gains=norm_gain, shifts=norm_bias,
        bias_in=ffn_in_bias, bias_out=ffn_out_bias, x_in=inputs, memory_in=memory, upstream_in=out_grad,
        shards=[
            self_qkv.transpose(1, 2, 0).reshape(3 * local, model), self_out, cross_q.T,
            cross_kv.transpose(1, 2, 0).reshape(2 * local, model), cross_out, ffn_in, ffn_out,
        ],
    ))
    out = run_finish(dict(
        configs=configs, small=done.small_out, layer_in=done.layer_out, grad_in=done.input_grad,
        source_in=done.memory_out, blocks=done.blocks,
    ), layers)
    grads = out.grads
    return (
        out.layer_out,
        out.input_grad,
        out.memory_grad,
        out.gain_grad,
        out.shift_grad,
        grads[0].reshape(3, local, model).transpose(2, 0, 1),
        grads[1],
        grads[2].T,
        grads[3].reshape(2, local, model).transpose(2, 0, 1),
        grads[4],
        grads[5],
        out.bias_in_grad,
        grads[6],
        out.bias_out_grad,
    )


def solution(mesh):
    rows = P(("grp", "dp", "tp"), None)
    stack = P(None, ("grp", "dp", "tp"), None)
    weights = (
        P(None, None, "tp"), P("tp", None), P(None, "tp"), P(None, None, "tp"), P("tp", None),
        P(None, "tp"), P("tp"), P("tp", None), P(),
    )
    return jax.shard_map(
        per_device,
        mesh=mesh,
        in_specs=(rows, stack, rows, P(("grp", "dp")), P(("grp", "dp")), P("grp", None), P(), P()) + weights,
        out_specs=(rows, rows, stack, P(), P()) + weights,
        check_vma=False,
    )
```

```python
import functools
import types

import jax
import jax.numpy as jnp
from jax import lax
from jax.experimental import pallas as pl
from jax.experimental.pallas import tpu as pltpu
from jax.sharding import PartitionSpec as P

HD = 80
LEN = 256
EPSILON = 1e-05
NEGATIVE = -1e30
SCALE = HD ** (-0.5)
LOG2E = 1.4426950408889634
F32 = jnp.float32
BF16 = jnp.bfloat16


MESH = pl.DeviceIdType.MESH


class Place:
    def __init__(self):
        self.tps = lax.axis_size("tp")
        self.extra = lax.axis_size("dp") // 2
        assert lax.axis_size("grp") == 4 and lax.axis_size("dp") % 2 == 0
        grp, dp, tp = (lax.axis_index(name) for name in ("grp", "dp", "tp"))
        core, low, high = dp % 2, grp % 2, grp // 2
        flip_low, flip_high = grp + 1 - 2 * low, grp + 2 - 4 * high
        self.grp, self.dp, self.tp, self.core = grp, dp, tp, core
        self.first_bit = (1 - core) * low + core * high
        self.second_bit = (1 - core) * high + core * low
        self.first = ((1 - core) * flip_low + core * flip_high, dp, tp)
        self.second = ((1 - core) * flip_high + core * flip_low, dp, tp)
        self.across = (3 - grp, dp, tp)
        self.sibling = (grp, dp + 1 - 2 * core, tp)
        self.above = (grp, dp, tp + 1)
        self.below = (grp, dp, tp - 1)
        self.has_above = tp < self.tps - 1
        self.has_below = tp > 0

    def copy_of(self, step):
        return (self.grp, ((self.dp // 2 + step) % self.extra) * 2 + self.core, self.tp)

    def nth_block(self, k):
        size = self.tps
        upper = (2 * self.tp) // size
        lead = (1 - upper) * self.tp + upper * (size - 1 - self.tp)
        spot = k + (k + size - lead) // size
        return (1 - upper) * spot + upper * (size - 1 - spot)

    def along(self, tp):
        return (self.grp, self.dp, tp)

    def barrier(self):
        sem = pltpu.get_barrier_semaphore()
        partners = [self.first, self.second, self.across, self.sibling]
        partners += [self.along((self.tp + step) % self.tps) for step in range(1, self.tps)]
        partners += [self.copy_of(step) for step in range(1, self.extra)]
        for device in partners:
            pl.semaphore_signal(sem, inc=1, device_id=device, device_id_type=MESH)
        pl.semaphore_wait(sem, len(partners))


def push(src, dst, send_sem, recv_sem, device):
    return pltpu.make_async_remote_copy(
        src_ref=src, dst_ref=dst, send_sem=send_sem, recv_sem=recv_sem, device_id=device, device_id_type=MESH
    )


def rows_of(ref, lead, start, count):
    return ref.at[lead, pl.ds(pl.multiple_of(start, 16), count)]


def add_units(total, term, unit):
    def step(i, carry):
        rows = pl.ds(pl.multiple_of(i * unit, 16), unit)
        total[rows] = total[rows] + term[rows]
        return carry

    lax.fori_loop(0, total.shape[0] // unit, step, 0)


class Spread:
    KINDS = 6

    def __init__(self, place, view, unit, sems):
        self.place, self.view, self.unit, self.sems = place, view, unit, sems
        f, s, c = place.first_bit, place.second_bit, place.core
        self.table = (
            (place.second, c * 4 + f * 2 + s, c * 4 + f * 2 + 1 - s, 1),
            (place.first, c * 4 + f * 2, c * 4 + 2 - f * 2, 2),
            (place.sibling, c * 4, 4 - c * 4, 4),
        )

    def region(self, start, count):
        return self.view(start * self.unit, count * self.unit)

    def own(self):
        return self.region(self.table[0][1], 1)

    def copy(self, n, lands=False):
        device, leaves, landing, count = self.table[n]
        part = self.region(landing if lands else leaves, count)
        return push(part, part, self.sems(2 * n), self.sems(2 * n + 1), device)

    def step(self, stage):
        if stage > 0:
            self.copy(stage - 1, lands=True).wait_recv()
        if stage < 3:
            self.copy(stage).start()

    def finish(self):
        for n in range(3):
            self.copy(n).wait_send()


class Gather:
    KINDS = Spread.KINDS + 3

    def __init__(self, place, buffers, sems):
        self.place, self.buffers, self.sems = place, buffers, sems
        self.unit = [ref.shape[1] // 8 for ref in buffers]
        self.others = place.tps - 1

    def spread(self, g, j):
        return Spread(
            self.place,
            lambda start, count: rows_of(self.buffers[g], j, start, count),
            self.unit[g],
            lambda kind: self.sems.at[kind, g, j],
        )

    def relays(self, g, j):
        p = self.place
        part = self.spread(g, j).own()
        sem = lambda n: self.sems.at[Spread.KINDS + n, g, j]
        return (
            (jnp.logical_and(j <= p.tp, p.has_above), push(part, part, sem(0), sem(2), p.above)),
            (jnp.logical_and(j >= p.tp, p.has_below), push(part, part, sem(1), sem(2), p.below)),
        )

    def start(self, g):
        for needed, copy in self.relays(g, self.place.tp):
            pl.when(needed)(copy.start)

    def step(self, g, k, stage):
        j = self.place.nth_block(k)
        if stage == 0:
            relays = self.relays(g, j)
            relays[0][1].wait_recv()
            for needed, copy in relays:
                pl.when(needed)(copy.start)
        self.spread(g, j).step(stage)

    def drain(self, g, j):
        for needed, copy in self.relays(g, j):
            pl.when(needed)(copy.wait_send)

        @pl.when(j != self.place.tp)
        def _():
            self.spread(g, j).finish()


class Line:
    def __init__(self, place, buffer, sems):
        self.place, self.buffer, self.sems = place, buffer, sems

    def relays(self, j):
        p = self.place
        part = self.buffer.at[j]
        return (
            (jnp.logical_and(j <= p.tp, p.has_above), push(part, part, self.sems.at[0, j], self.sems.at[2, j], p.above)),
            (jnp.logical_and(j >= p.tp, p.has_below), push(part, part, self.sems.at[1, j], self.sems.at[2, j], p.below)),
        )

    def start(self):
        for needed, copy in self.relays(self.place.tp):
            pl.when(needed)(copy.start)

    def step(self, k):
        j = self.place.nth_block(k)
        relays = self.relays(j)
        relays[0][1].wait_recv()
        for needed, copy in relays:
            pl.when(needed)(copy.start)

    def finish(self):
        for j in range(self.place.tps):
            for needed, copy in self.relays(j):
                pl.when(needed)(copy.wait_send)


class Reduce:
    KINDS = 8 + Spread.KINDS + 2

    def __init__(self, place, grads, halves, planes, lines, extras, totals, sems):
        self.place, self.grads, self.totals, self.sems = place, grads, totals, sems
        self.halves, self.planes, self.lines, self.extras = halves, planes, lines, extras
        self.unit = [ref.shape[1] // 8 for ref in grads]

    def sem(self, kind, g, j):
        return self.sems.at[kind, g, j]

    def rows(self, g, j, half, unit, count=1):
        size = self.unit[g]
        return rows_of(self.grads[g], j, (half * 4 + unit) * size, count * size)

    def move(self, g, j, stage):
        p, size = self.place, self.unit[g]
        if stage == 0:
            part, landing, device = self.rows(g, j, 1 - p.core, 0, 4), self.halves[g].at[j], p.sibling
        elif stage == 1:
            part, device = self.rows(g, j, p.core, 2 - p.first_bit * 2, 2), p.first
            landing = self.planes[g].at[j, pl.ds(0, 2 * size)]
        else:
            part, device = self.rows(g, j, p.core, p.first_bit * 2 + 1 - p.second_bit), p.second
            landing = self.planes[g].at[j, pl.ds(2 * size, size)]
        return push(part, landing, self.sem(2 * stage, g, j), self.sem(2 * stage + 1, g, j), device)

    def kept(self, g, j, stage):
        p, size = self.place, self.unit[g]
        if stage == 0:
            return self.rows(g, j, p.core, 0, 4), self.halves[g].at[j]
        if stage == 1:
            return self.rows(g, j, p.core, p.first_bit * 2, 2), self.planes[g].at[j, pl.ds(0, 2 * size)]
        return self.piece(g, j), self.planes[g].at[j, pl.ds(2 * size, size)]

    def piece(self, g, j):
        p = self.place
        return self.rows(g, j, p.core, p.first_bit * 2 + p.second_bit)

    def along(self, g, j):
        p = self.place
        return push(self.piece(g, j), self.lines[g].at[p.tp], self.sem(6, g, j), self.sem(7, g, p.tp), p.along(j))

    def from_place(self, g, j):
        p = self.place
        return push(self.piece(g, j), self.lines[g].at[j], self.sem(6, g, j), self.sem(7, g, j), p.along(j))

    def step(self, g, j, stage):
        if stage > 0:
            self.move(g, j, stage - 1).wait_recv()
            add_units(*self.kept(g, j, stage - 1), self.unit[g])
        if stage < 3:
            self.move(g, j, stage).start()
        else:
            pl.when(j != self.place.tp)(self.along(g, j).start)

    def spread(self, g):
        return Spread(
            self.place,
            lambda start, count: self.totals[g].at[pl.ds(pl.multiple_of(start, 16), count)],
            self.unit[g],
            lambda kind: self.sems.at[8 + kind, g, 0],
        )

    def copies(self, g, step):
        p = self.place
        base = self.KINDS - 2
        return push(
            self.piece(g, p.tp), self.extras[g].at[step], self.sem(base, g, step), self.sem(base + 1, g, step), p.copy_of(step)
        )

    def settle(self, g):
        p = self.place
        piece = self.piece(g, p.tp)
        total = piece[...].astype(F32)
        for k in range(p.tps - 1):
            j = p.nth_block(k)
            self.from_place(g, j).wait_recv()
            total = total + self.lines[g][j].astype(F32)
        if p.extra > 1:
            piece[...] = total.astype(BF16)
            for step in range(1, p.extra):
                self.copies(g, step).start()
            for step in range(1, p.extra):
                self.copies(g, step).wait()
                total = total + self.extras[g][step].astype(F32)
        own = self.spread(g).own()
        own[...] = total.astype(BF16)
        self.spread(g).step(0)

    def share(self, g, stage):
        self.spread(g).step(stage)

    def finish(self, g):
        p = self.place
        for j in range(p.tps):
            for stage in range(3):
                self.move(g, j, stage).wait_send()
            pl.when(j != p.tp)(self.along(g, j).wait_send)
        self.spread(g).finish()


class SumSmall:
    @staticmethod
    def slots(tps, extra):
        return 8 + tps + extra

    def __init__(self, place, slots, sems):
        self.place, self.slots_ref, self.sems = place, slots, sems

    def move(self, source, target, device, kind):
        slots = self.slots_ref
        return push(slots.at[source], slots.at[target], self.sems.at[0, kind], self.sems.at[1, target], device)

    def in_plane(self):
        p = self.place
        return [self.move(2, 3 + i, device, 3 + i) for i, device in enumerate((p.second, p.first, p.across))]

    def copies(self):
        p = self.place
        return [self.move(6, 8 + p.tps + s, p.copy_of(s), 8 + p.tps + s) for s in range(1, p.extra)]

    def along(self, k, lands=False):
        p = self.place
        j = p.nth_block(k)
        return self.move(7, 8 + (j if lands else p.tp), p.along(j), 8 + j)

    def start(self):
        self.move(0, 1, self.place.sibling, 1).start()

    def exchange(self, stage):
        p, slots = self.place, self.slots_ref
        if stage == 0:
            self.move(0, 1, p.sibling, 1).wait_recv()
            slots[2] = slots[0] + slots[1]
            for copy in self.in_plane():
                copy.start()
        else:
            for copy in self.in_plane():
                copy.wait_recv()
            slots[6] = (slots[2] + slots[3]) + (slots[4] + slots[5])
            for copy in self.copies():
                copy.start()
            total = slots[6]
            for s, copy in enumerate(self.copies()):
                copy.wait_recv()
                total = total + slots[9 + p.tps + s]
            slots[7] = total
            for k in range(p.tps - 1):
                self.along(k).start()

    def total(self):
        p, slots = self.place, self.slots_ref
        value = slots[7]
        for k in range(p.tps - 1):
            self.along(k, lands=True).wait_recv()
            value = value + slots[8 + p.nth_block(k)]
        return value

    def finish(self):
        p = self.place
        self.move(0, 1, p.sibling, 1).wait_send()
        for copy in self.in_plane() + self.copies():
            copy.wait_send()
        for k in range(p.tps - 1):
            self.along(k).wait_send()


def dot_nn(left, right):
    return lax.dot_general(left, right, (((1,), (0,)), ((), ())), preferred_element_type=F32)


def dot_nt(left, right):
    return lax.dot_general(left, right, (((1,), (1,)), ((), ())), preferred_element_type=F32)


def dot_tn(left, right):
    return lax.dot_general(left, right, (((0,), (0,)), ((), ())), preferred_element_type=F32)


def column(axis, shape):
    return lax.broadcasted_iota(jnp.int32, shape, axis)


def each(count, step):

    def run(i, carry):
        step(i)
        return carry

    lax.fori_loop(0, count, run, 0)


CHUNK = 128
CUBE = 0.044715
ROOT = 0.7978845608028654


def layer_kernel(r):
    r.a2, r.a3, r.e = (r.memory.at[i] for i in range(3))
    columns = pl.ds(0, r.x.shape[1])
    r.dh, r.dm = r.before.at[:, columns], r.down.at[:, columns]
    place = Place()
    n = place.tps
    x, model = r.x, r.x.shape[1]
    owned = x.shape[0]
    sentences = owned // LEN
    local = r.c[0].shape[1]
    heads_here = local // HD
    units = r.hidden.shape[1]
    layers = r.memory.shape[0]
    weights = r.w
    lengths, sources, configs = r.lengths, r.src_lengths, r.configs
    width, heads, hidden_units, depth = (configs[0, i] for i in range(4))
    inv_width = 1.0 / jnp.full((1, 1), width.astype(F32))
    inv_depth = 1.0 / jnp.full((1, 1), depth.astype(F32))
    width_mask = (column(1, (1, model)) < width).astype(F32)

    local_sem = r.local_sems
    spots = (
        (0, 0, 3 * local), (0, 3 * local, local),
        (1, 0, local), (1, local, 2 * local), (1, 3 * local, local),
        (2, 0, weights[2].shape[1]), (3, 0, weights[3].shape[1]),
    )
    fills = [
        (g, pltpu.make_async_copy(r.shards[i], weights[g].at[place.tp, pl.ds(start, size)], local_sem.at[i]))
        for i, (g, start, size) in enumerate(spots)
    ]
    loads = [
        pltpu.make_async_copy(source, target, local_sem.at[7 + i])
        for i, (source, target) in enumerate(((r.x_in, r.x), (r.memory_in, r.memory), (r.upstream_in, r.upstream)))
    ]
    for _, copy in fills[:2]:
        copy.start()
    loads[0].start()
    for _, copy in fills[2:]:
        copy.start()
    loads[1].start()
    loads[2].start()
    r.bias[place.tp] = jnp.broadcast_to(r.bias_in[...].reshape(1, units), r.bias.shape[1:])
    place.barrier()

    gather = Gather(place, weights, r.gather_sems)
    bias = Line(place, r.bias, r.bias_sems)
    for g in range(4):
        for group, copy in fills:
            if group == g:
                copy.wait()
        gather.start(g)
        if g == 0:
            bias.start()
    order = [(g, k) for g in (0, 1) for k in range(n - 1)] + [(g, k) for k in range(n - 1) for g in (2, 3)]

    places = (
        (0, 1, 2, 5), (1, 2, 4, 7), (2, 3, 6, 9), (3, 5, 7, 11), (4, 6, 9, 12), (6, 8, 10, 11),
        (7, 10, 11, 15), (9, 11, 13, 15), (11, 12, 15, 18), (12, 15, 20, 23), (13, 16, 21, 23), (15, 18, 22, 25),
    )
    assert len(places) == len(order)

    def gather_at(spot):
        found = [(stage, e) for e, stages in enumerate(places) for stage, at in enumerate(stages) if at == spot]
        for stage, e in sorted(found):
            gather.step(*order[e], stage)

    def gather_table(start):
        return {(k, b): [functools.partial(gather_at, start + 2 * k + b)] for k in range(n) for b in range(2)}

    def block(k):
        later = (k + n - 1) // n
        return (1 - later) * place.tp + later * place.nth_block(k - 1)

    def block_last(k):
        own = k // (n - 1)
        return own * place.tp + (1 - own) * place.nth_block(k)

    def hooks(table, k, b):
        for (kk, bb), steps in table.items():

            @pl.when(jnp.logical_and(k == kk, b == bb))
            def _():
                for step in steps:
                    step()

    def chunk(i):
        return pl.ds(pl.multiple_of(i * CHUNK, CHUNK), CHUNK)

    def keep_of(i):
        per = LEN // CHUNK
        spot = column(0, (CHUNK, 1)) + (i % per) * CHUNK
        return (spot < lengths[place.tp * sentences + i // per]).astype(F32) * width_mask

    def norm_parts(rows):
        mean = jnp.sum(rows * width_mask, axis=-1, keepdims=True) * inv_width
        centred = (rows - mean) * width_mask
        spread = jnp.sum(centred * centred, axis=-1, keepdims=True) * inv_width
        rstd = lax.rsqrt(spread + EPSILON)
        return centred * rstd, rstd

    def norm(rows, which):
        hat, _ = norm_parts(rows)
        return ((hat * r.gains[which:which + 1] + r.shifts[which:which + 1]) * width_mask).astype(BF16)

    def fold(values):
        return jnp.sum(values.reshape(values.shape[0] // 8, 8, values.shape[1]), axis=0)

    def norm_backward(rows, which, upstream):
        hat, rstd = norm_parts(rows)
        upstream = upstream * width_mask
        sums = r.norm_sums
        sums[which] = sums[which] + fold(upstream * hat)
        sums[3 + which] = sums[3 + which] + fold(upstream)
        scaled = upstream * r.gains[which:which + 1]
        first = jnp.sum(scaled, axis=-1, keepdims=True) * inv_width
        second = jnp.sum(scaled * hat, axis=-1, keepdims=True) * inv_width
        return (rstd * (scaled - first - hat * second)) * width_mask

    chunks = owned // CHUNK

    def each_chunk(step):
        each(chunks, step)

    acc, da, dh = r.acc, r.da, r.dh
    zeros = jnp.zeros((CHUNK, model), F32)
    r.norm_sums[...] = jnp.zeros(r.norm_sums.shape, F32)
    r.bias_sums[...] = jnp.zeros(r.bias_sums.shape, F32)

    def sentence(b):
        return pl.ds(pl.multiple_of(b * LEN, LEN), LEN)

    def head_keep(j, h):
        return jnp.where(j * heads_here + h < heads, 1.0, 0.0).astype(F32)

    def causal(b, start, size):
        return column(0, (size, 128)) <= column(1, (size, 128)) + start

    def crossing(b, start, size):
        return column(0, (size, 1)) < sources[place.tp * sentences + b]

    def reach(g, start):
        return start + 128 if g == 0 else LEN

    def bands(h):
        return [pl.ds(i * local + h * HD, HD) for i in range(3)]

    def lanes(b):
        return pl.ds(b * LEN, LEN)

    pairs = [(b, h) for b in range(sentences) for h in range(heads_here)]

    def attend(k, table, g, allowed):
        w, t, c, p = weights[g], r.t[g], r.c[g], r.p[g]
        j = block(k)
        hooks(table, k, 0)
        if g == 0:
            t[j] = dot_nt(w[j, :3 * local], r.a1[...]).astype(BF16)
        else:
            t[j, :local] = dot_nt(w[j, :local], r.a2[...]).astype(BF16)
            t[j, local:] = dot_nt(w[j, local:3 * local], r.m[...]).astype(BF16)
        heads_of = [[t[j, band, lanes(b)] for band in bands(h)] for b, h in pairs]
        for i, (query, keys, _) in enumerate(heads_of):
            r.scores[i] = dot_tn(keys, query)
        for i, (b, h) in enumerate(pairs):
            for start in range(0, LEN, 128):
                part, size = pl.ds(start, 128), reach(g, start)
                score = jnp.where(allowed(b, start, size), r.scores[i, :size, part], NEGATIVE)
                raised = jnp.exp2((score - jnp.max(score, axis=0, keepdims=True)) * (SCALE * LOG2E))
                p[j, i, :size, part] = (raised * (1.0 / jnp.sum(raised, axis=0, keepdims=True))).astype(BF16)
                if size < LEN:
                    p[j, i, size:, part] = jnp.zeros((LEN - size, 128), BF16)
            c[j, pl.ds(h * HD, HD), lanes(b)] = (dot_nn(heads_of[i][2], p[j, i]) * head_keep(j, h)).astype(BF16)
        hooks(table, k, 1)
        acc[...] = acc[...] + dot_tn(c[j], w[j, 3 * local:])

    def attend_backward(k, table, g, query_rows, key_rows):
        w, t, c, p = weights[g], r.t[g], r.c[g], r.p[g]
        j = block_last(k)
        e, dt, dc = r.e, r.dt, r.dc
        gather.drain(g, j)
        dc_all = dot_nt(w[j, 3 * local:], e[...])
        for h in range(heads_here):
            dc[h * HD:(h + 1) * HD] = (dc_all[h * HD:(h + 1) * HD] * head_keep(j, h)).astype(BF16)
        heads_of = [[t[j, band, lanes(b)] for band in bands(h)] for b, h in pairs]
        dc_of = [dc[h * HD:(h + 1) * HD, lanes(b)] for b, h in pairs]
        for i, (_, _, values) in enumerate(heads_of):
            r.scores[i] = dot_tn(values, dc_of[i])
        for i, (b, h) in enumerate(pairs):
            dt[bands(h)[2], lanes(b)] = dot_nt(dc_of[i], p[j, i]).astype(BF16)
        w[j, 3 * local:] = dot_nn(c[j], e[...]).astype(BF16)
        for i, (b, h) in enumerate(pairs):
            (query, keys, _), (dq, dk, _) = heads_of[i], bands(h)
            for start in range(0, LEN, 128):
                part, size = pl.ds(start, 128), reach(g, start)
                dp, wide = r.scores[i, :size, part], p[j, i, :size, part].astype(F32)
                r.ds[i, :size, part] = (wide * (dp - jnp.sum(dp * wide, axis=0, keepdims=True))).astype(BF16)
                if size < LEN:
                    r.ds[i, size:, part] = jnp.zeros((LEN - size, 128), BF16)
            dt[dq, lanes(b)] = (dot_nn(keys, r.ds[i]) * SCALE).astype(BF16)
            dt[dk, lanes(b)] = (dot_nt(query, r.ds[i]) * SCALE).astype(BF16)
        hooks(table, k, 1)
        if g == 0:
            da[...] = da[...] + dot_tn(dt[...], w[j, :3 * local])
            w[j, :3 * local] = dot_nn(dt[...], query_rows[...]).astype(BF16)
        else:
            da[...] = da[...] + dot_tn(dt[:local], w[j, :local])
            r.dm[...] = r.dm[...] + dot_tn(dt[local:], w[j, local:3 * local])
            w[j, :local] = dot_nn(dt[:local], query_rows[...]).astype(BF16)
            w[j, local:3 * local] = dot_nn(dt[local:], key_rows[...]).astype(BF16)

    def feed(k, table):
        j = block(k)
        w_up, w_down = weights[2], weights[3]
        hooks(table, k, 0)
        unit = column(1, (1, units)) + j * units
        kept = jnp.where(unit < hidden_units, 0.5, 0.0)
        found = []
        for b in range(sentences):
            rows = sentence(b)
            found.append((dot_nn(r.a3[rows], w_up[j]) + r.bias[j, 0:1], dot_nt(r.e[rows], w_down[j])))
        for b, (before, down) in enumerate(found):
            rows = sentence(b)
            square = before * before
            bent = jnp.tanh(before * (ROOT + ROOT * CUBE * square))
            half = kept + kept * bent
            through = before * half
            r.hidden[rows] = through.astype(BF16)
            slope = half + (through - through * bent) * (ROOT + 3.0 * CUBE * ROOT * square)
            du = (down * slope).astype(BF16)
            r.dhidden[rows] = du
            r.bias_sums[j] = r.bias_sums[j] + fold(du.astype(F32))
            acc[rows] = acc[rows] + dot_nn(r.hidden[rows], w_down[j])
            da[rows] = da[rows] + dot_nt(r.dhidden[rows], w_up[j])
        hooks(table, k, 1)
        gather.drain(2, j)
        gather.drain(3, j)
        w_down[j] = dot_tn(r.hidden[...], r.e[...]).astype(BF16)
        w_up[j] = dot_nn(r.a3t[...], r.dhidden[...]).astype(BF16)

    loads[0].wait()

    def begin(i):
        rows = chunk(i)
        r.a1[rows] = norm(x[rows].astype(F32), 0)
        acc[rows] = zeros
        da[rows] = zeros

    each_chunk(begin)
    gather_at(0)
    loads[1].wait()

    def mix(i):
        rows = chunk(i)
        total = jnp.zeros((CHUNK, model), F32)
        for level in range(layers):
            chosen = (jnp.full((1, 1), depth) >= layers - level).astype(F32)
            total = total + chosen * r.memory[level, rows].astype(F32)
        r.m[rows] = (total * inv_depth * width_mask).astype(BF16)

    each_chunk(mix)
    gather_at(1)
    loads[2].wait()
    r.out_sums[...] = jnp.zeros(r.out_sums.shape, F32)

    def grad_in(i):
        rows = chunk(i)
        masked = r.upstream[rows].astype(F32) * keep_of(i)
        r.out_sums[...] = r.out_sums[...] + fold(masked)
        r.e[rows] = masked.astype(BF16)

    each_chunk(grad_in)
    gather_at(2)

    others = n - 1
    assert n == 4
    table = gather_table(3)
    for k in range(others):
        table[k + 1, 0].append(functools.partial(bias.step, k))
    each(n, lambda k: attend(k, table, 0, causal))

    def after_self(i):
        rows = chunk(i)
        h = x[rows].astype(F32) + acc[rows] * keep_of(i)
        r.h1[rows] = h
        r.a2[rows] = norm(h, 1)
        acc[rows] = zeros

    each_chunk(after_self)
    table2 = gather_table(11)
    each(n, lambda k: attend(k, table2, 1, crossing))

    def after_cross(i):
        rows = chunk(i)
        h = r.h1[rows] + acc[rows] * keep_of(i)
        r.h2[rows] = h
        r.a3[rows] = norm(h, 2)
        acc[rows] = zeros

    each_chunk(after_cross)
    r.a3t[...] = r.a3[...].T

    reduce = Reduce(
        place, weights, r.half, r.plane, r.line, r.extra, r.total, r.reduce_sems
    )
    plan = {}

    def add(tick, order, step, *args):
        plan.setdefault(tick, []).append((order, len(plan.get(tick, ())), functools.partial(step, *args)))

    def r_tick(tick):
        for _, _, step in sorted(plan.get(tick, ()), key=lambda entry: entry[:2]):
            step()

    def store(g):
        return pltpu.make_async_copy(r.total[g], r.blocks[g], local_sem.at[10 + g])

    times = {
        3: ([(1, 2, 6, 10), (3, 4, 8, 11), (5, 6, 9, 13), (7, 9, 11, 15)], (17, 19, 21, 25)),
        2: ([(1, 3, 6, 9), (3, 6, 8, 11), (5, 8, 10, 13), (7, 9, 12, 16)], (19, 21, 23, 26)),
        1: ([(10, 11, 14, 16), (12, 14, 16, 18), (14, 15, 19, 21), (16, 17, 19, 21)], (24, 27, 28, 29)),
        0: ([(19, 20, 22, 24), (21, 22, 24, 25), (23, 24, 25, 26), (25, 26, 27, 28)], (28, 29, 30, 31)),
    }
    for late, g in enumerate((3, 2, 1, 0)):
        for k, stages in enumerate(times[g][0]):
            j = block(k) if g > 1 else block_last(k)
            for stage, tick in enumerate(stages):
                add(tick, stage, reduce.step, g, j, stage)
        for stage, tick in enumerate(times[g][1]):
            if stage == 0:
                add(tick, 20 - late, reduce.settle, g)
            else:
                add(tick, 30 + stage - late, reduce.share, g, stage)
        add(times[g][1][-1], 50, lambda g=g: store(g).start())

    def reduce_ticks(*numbers):
        return [functools.partial(r_tick, i) for i in numbers]

    def at_end(k, numbers):
        for kk, number in enumerate(numbers):

            @pl.when(k == kk)
            def _():
                r_tick(number)

    table3 = gather_table(19)
    for k in range(1, n):
        table3[k, 1] += reduce_ticks(2 * k)

    def feed_step(k):
        feed(k, table3)
        at_end(k, [2 * i + 1 for i in range(n)])

    each(n, feed_step)
    r_tick(8)
    out_copy = pltpu.make_async_copy(acc, r.layer_out, local_sem.at[14])

    def after_feed(i):
        rows = chunk(i)
        keep = keep_of(i)
        acc[rows] = r.h2[rows] + (acc[rows] + r.bias_out[...].reshape(1, model)) * keep
        down = r.upstream[rows].astype(F32) + norm_backward(r.h2[rows], 2, da[rows])
        dh[rows] = down
        r.e[rows] = (down * keep).astype(BF16)
        da[rows] = zeros
        r.dm[rows] = zeros

    each_chunk(after_feed)
    out_copy.start()
    table4 = {(k, 1): reduce_ticks(9 + 2 * k) for k in range(n)}

    def cross_step(k):
        attend_backward(k, table4, 1, r.a2, r.m)
        at_end(k, [10 + 2 * i for i in range(n)])

    each(n, cross_step)
    memory_copy = pltpu.make_async_copy(r.dm, r.memory_out, local_sem.at[15])
    memory_copy.start()

    def before_cross(i):
        rows = chunk(i)
        down = dh[rows] + norm_backward(r.h1[rows], 1, da[rows])
        dh[rows] = down
        r.e[rows] = (down * keep_of(i)).astype(BF16)
        da[rows] = zeros

    each_chunk(before_cross)
    r_tick(17)
    table5 = {(k, 1): reduce_ticks(18 + 2 * k) for k in range(n)}

    def self_step(k):
        attend_backward(k, table5, 0, r.a1, r.a1)
        at_end(k, [19 + 2 * i for i in range(n)])

    each(n, self_step)

    def before_self(i):
        rows = chunk(i)
        dh[rows] = dh[rows] + norm_backward(x[rows].astype(F32), 0, da[rows])

    each_chunk(before_self)
    grad_copy = pltpu.make_async_copy(dh, r.input_grad, local_sem.at[16])
    grad_copy.start()

    small = SumSmall(place, r.slots, r.small_sems)

    def small_start():
        own = r.slots.at[0]
        own[...] = jnp.zeros(own.shape, F32)
        for i in range(6):
            own[i:i + 1, :model] = jnp.sum(r.norm_sums[i], axis=0, keepdims=True)
        own[6:7, :model] = jnp.sum(r.out_sums[...], axis=0, keepdims=True)
        tokens = lengths[place.tp * sentences]
        for b in range(1, sentences):
            tokens = tokens + lengths[place.tp * sentences + b]
        own[7:8] = jnp.full((1, own.shape[1]), tokens.astype(F32))
        for i in range(n):
            own[8 + i:9 + i] = jnp.sum(r.bias_sums[i], axis=0, keepdims=True)
        small.start()

    add(26, 5, small_start)
    for stage in range(2):
        add(27 + stage, 5, small.exchange, stage)
    final = max(plan)
    for tick in range(26, final + 1):
        r_tick(tick)
    r.small_out[...] = small.total()
    bias.finish()
    for copy in (out_copy, memory_copy, grad_copy):
        copy.wait()
    for g in range(4):
        reduce.finish(g)
        store(g).wait()
    small.finish()


def call(kernel, name, ins, outs, scratch, spaces, **options):
    trees = (ins, outs, scratch)
    structure = jax.tree_util.tree_structure(trees)

    def body(*refs):
        groups = jax.tree_util.tree_unflatten(structure, refs)
        kernel(types.SimpleNamespace(**groups[0], **groups[1], **groups[2]))

    def specs(group):
        return [
            pl.BlockSpec(memory_space=spaces.get(key, pltpu.VMEM))
            for key in sorted(group) for _ in jax.tree_util.tree_leaves(group[key])
        ]

    leaves = jax.tree_util.tree_leaves
    values = pl.pallas_call(
        body,
        out_shape=leaves(outs),
        in_specs=specs(ins),
        out_specs=specs(outs),
        scratch_shapes=leaves(scratch),
        compiler_params=pltpu.CompilerParams(**options),
        name=name,
    )(*leaves(ins))
    return types.SimpleNamespace(**jax.tree_util.tree_unflatten(jax.tree_util.tree_structure(outs), values))


def run_layer(ins):
    n, extra = lax.axis_size("tp"), lax.axis_size("dp") // 2
    owned, model = ins["x_in"].shape
    memory, shards = ins["memory_in"], ins["shards"]
    local, units = shards[1].shape[0], ins["bias_in"].shape[0]
    small = (16, units)
    assert n <= 8 and units >= model and memory.shape[0] >= 3
    shapes = [(n, 4 * local, model)] * 2 + [(n,) + shards[5].shape, (n,) + shards[6].shape]
    small_slots = SumSmall.slots(n, extra)

    def vmem(*shape):
        return pltpu.VMEM(shape, BF16)

    def wide(*shape):
        return pltpu.VMEM(shape, F32)

    def eighths(*lead, parts=1):
        return [vmem(*lead, rows * parts // 8, columns) for _, rows, columns in shapes]

    dma = pltpu.SemaphoreType.DMA
    scratch = dict(
        w=[vmem(*shape) for shape in shapes],
        bias=wide(n, 8, units),
        x=vmem(owned, model),
        memory=vmem(*memory.shape),
        upstream=vmem(owned, model),
        a1=vmem(owned, model),
        m=vmem(owned, model),
        h1=wide(owned, model),
        h2=wide(owned, model),
        acc=wide(owned, model),
        da=wide(owned, model),
        t=[vmem(n, 3 * local, owned)] * 2,
        c=[vmem(n, local, owned)] * 2,
        p=[vmem(n, owned // LEN * (local // HD), LEN, LEN)] * 2,
        dt=vmem(3 * local, owned),
        dc=vmem(local, owned),
        a3t=vmem(model, owned),
        scores=wide(owned // LEN * (local // HD), LEN, LEN),
        ds=vmem(owned // LEN * (local // HD), LEN, LEN),
        before=wide(owned, units),
        down=wide(owned, units),
        hidden=vmem(owned, units),
        dhidden=vmem(owned, units),
        bias_sums=wide(n, 8, units),
        norm_sums=wide(6, 8, model),
        out_sums=wide(8, model),
        half=eighths(n, parts=4),
        plane=eighths(n, parts=3),
        line=eighths(n),
        extra=eighths(extra),
        total=eighths(parts=8),
        slots=wide(small_slots, *small),
        gather_sems=dma((Gather.KINDS, 4, n)),
        bias_sems=dma((3, n)),
        reduce_sems=dma((Reduce.KINDS, 4, max(n, extra))),
        small_sems=dma((2, small_slots)),
        local_sems=dma((17,)),
    )
    rows = jax.ShapeDtypeStruct((owned, model), F32)
    outs = dict(
        layer_out=rows, input_grad=rows, memory_out=rows, small_out=jax.ShapeDtypeStruct(small, F32),
        blocks=[jax.ShapeDtypeStruct(shape[1:], BF16) for shape in shapes],
    )
    smem, hbm = pltpu.SMEM, pl.ANY
    spaces = dict(
        lengths=smem, src_lengths=smem, configs=smem, x_in=hbm, memory_in=hbm, upstream_in=hbm, shards=hbm,
        layer_out=hbm, input_grad=hbm, memory_out=hbm, blocks=hbm,
    )
    return call(
        layer_kernel, "layer", ins, outs, scratch, spaces,
        collective_id=1, has_side_effects=True, vmem_limit_bytes=64 * 2**20,
    )


def finish_kernel(r):
    small, configs, sems = r.small, r.configs, r.sems
    model = r.gain_grad.shape[1]
    layers = r.memory_grad.shape[0]
    place = lax.axis_index("tp")
    local = r.grads[1].shape[0]
    parts = (
        (0, 0, 3 * local), (0, 3 * local, local),
        (1, 0, local), (1, local, 2 * local), (1, 3 * local, local),
        (2, 0, r.block[2].shape[0]), (3, 0, r.block[3].shape[0]),
    )
    loads = [pltpu.make_async_copy(r.blocks[g], r.block[g], sems.at[g]) for g in range(4)]
    rows = [
        pltpu.make_async_copy(source, target, sems.at[4 + i])
        for i, (source, target) in enumerate(((r.layer_in, r.layer), (r.grad_in, r.grad), (r.source_in, r.source)))
    ]
    outs = [pltpu.make_async_copy(r.layer, r.layer_out, sems.at[7]), pltpu.make_async_copy(r.grad, r.input_grad, sems.at[8])]
    for copy in rows + loads:
        copy.start()
    inverse = 1.0 / small[7:8, :1]
    r.gain_grad[...] = small[:3, :model] * inverse
    r.shift_grad[...] = small[3:6, :model] * inverse
    r.bias_out_grad[...] = (small[6:7, :model] * inverse).reshape(model)
    r.bias_in_grad[...] = (small[pl.ds(8 + place, 1)] * inverse).reshape(small.shape[1])
    width, depth = configs[0, 0], configs[0, 3]
    factor = (column(1, (1, model)) < width).astype(F32) / jnp.full((1, 1), depth.astype(F32))
    for i in range(2):
        rows[i].wait()
        outs[i].start()
    rows[2].wait()

    def spread(i):
        part = pl.ds(pl.multiple_of(i * 64, 64), 64)
        value = r.source[part] * factor
        for level in range(layers):
            chosen = (jnp.full((1, 1), depth) >= layers - level).astype(F32)
            r.memories[level, part] = value * chosen

    each(r.source.shape[0] // 64, spread)
    outs.append(pltpu.make_async_copy(r.memories, r.memory_grad, sems.at[9]))
    outs[2].start()
    for i, (g, start, count) in enumerate(parts):
        if start == 0:
            loads[g].wait()

        size = 80 if count % 80 == 0 else 96

        def scale(at):
            there = pl.ds(pl.multiple_of(start + at * size, 16), size)
            r.wide[g][there] = r.block[g][there].astype(F32) * inverse

        each(count // size, scale)
        outs.append(pltpu.make_async_copy(r.wide[g].at[pl.ds(start, count)], r.grads[i], sems.at[10 + i]))
        outs[-1].start()
    for copy in outs:
        copy.wait()


def run_finish(ins, layers):
    blocks, small = ins["blocks"], ins["small"]
    rows = ins["layer_in"].shape
    local, units = blocks[0].shape[0] // 4, small.shape[1]

    def shape(*dims):
        return jax.ShapeDtypeStruct(dims, F32)

    counts = (3 * local, local, local, 2 * local, local)
    outs = dict(
        layer_out=shape(*rows), input_grad=shape(*rows), memory_grad=shape(layers, *rows),
        gain_grad=shape(3, rows[1]), shift_grad=shape(3, rows[1]), bias_in_grad=shape(units), bias_out_grad=shape(rows[1]),
        grads=[shape(count, rows[1]) for count in counts] + [shape(*blocks[2].shape), shape(*blocks[3].shape)],
    )
    scratch = dict(
        layer=pltpu.VMEM(rows, F32), grad=pltpu.VMEM(rows, F32), source=pltpu.VMEM(rows, F32),
        memories=pltpu.VMEM((layers,) + rows, F32),
        block=[pltpu.VMEM(block.shape, BF16) for block in blocks],
        wide=[pltpu.VMEM(block.shape, F32) for block in blocks],
        sems=pltpu.SemaphoreType.DMA((17,)),
    )
    hbm = pl.ANY
    spaces = dict(
        configs=pltpu.SMEM, layer_in=hbm, grad_in=hbm, source_in=hbm, blocks=hbm,
        layer_out=hbm, input_grad=hbm, memory_grad=hbm, grads=hbm,
    )
    return call(finish_kernel, "finish", ins, outs, scratch, spaces, vmem_limit_bytes=60 * 2**20)


def per_device(
    inputs, memory, out_grad, lengths, src_lengths, configs, norm_gain, norm_bias,
    self_qkv, self_out, cross_q, cross_kv, cross_out, ffn_in, ffn_in_bias, ffn_out, ffn_out_bias,
):
    model = inputs.shape[1]
    layers = memory.shape[0]
    local = self_out.shape[0]
    done = run_layer(dict(
        lengths=lengths, src_lengths=src_lengths, configs=configs, gains=norm_gain, shifts=norm_bias,
        bias_in=ffn_in_bias, bias_out=ffn_out_bias, x_in=inputs, memory_in=memory, upstream_in=out_grad,
        shards=[
            self_qkv.transpose(1, 2, 0).reshape(3 * local, model), self_out, cross_q.T,
            cross_kv.transpose(1, 2, 0).reshape(2 * local, model), cross_out, ffn_in, ffn_out,
        ],
    ))
    out = run_finish(dict(
        configs=configs, small=done.small_out, layer_in=done.layer_out, grad_in=done.input_grad,
        source_in=done.memory_out, blocks=done.blocks,
    ), layers)
    grads = out.grads
    return (
        out.layer_out,
        out.input_grad,
        out.memory_grad,
        out.gain_grad,
        out.shift_grad,
        grads[0].reshape(3, local, model).transpose(2, 0, 1),
        grads[1],
        grads[2].T,
        grads[3].reshape(2, local, model).transpose(2, 0, 1),
        grads[4],
        grads[5],
        out.bias_in_grad,
        grads[6],
        out.bias_out_grad,
    )


def solution(mesh):
    rows = P(("grp", "dp", "tp"), None)
    stack = P(None, ("grp", "dp", "tp"), None)
    weights = (
        P(None, None, "tp"), P("tp", None), P(None, "tp"), P(None, None, "tp"), P("tp", None),
        P(None, "tp"), P("tp"), P("tp", None), P(),
    )
    return jax.shard_map(
        per_device,
        mesh=mesh,
        in_specs=(rows, stack, rows, P(("grp", "dp")), P(("grp", "dp")), P("grp", None), P(), P()) + weights,
        out_specs=(rows, rows, stack, P(), P()) + weights,
        check_vma=False,
    )
```
